32 devices in a mesh: dp: 8 (over y, x, core), tensor: 4 (over z).
Axes of the slice: x: 2, y: 2, z: 4, core: 2. Of those that a mesh axis runs over, the one named last changes fastest.
Arguments:
- tokens: bfloat16 [8192, 1024], P(('dp', 'tensor')), may hold values from -6 to 6
- query_proj: bfloat16 [1024, 512], P('dp', 'tensor'), may hold values from -0.1875 to 0.1875
- attend_out: bfloat16 [512, 1024], P('tensor', 'dp'), may hold values from -3 to 3
- inner_proj: bfloat16 [2, 1024, 1536], P(None, 'dp', 'tensor'), may hold values from -0.1875 to 0.1875
- step_proj: bfloat16 [1024, 24], P('dp', 'tensor'), may hold values from -0.1875 to 0.1875
- mamba_out: bfloat16 [1536, 1024], P('tensor', 'dp'), may hold values from -0.15625 to 0.15625
- hidden_proj: bfloat16 [2, 1024, 2048], P(None, 'dp', 'tensor'), may hold values from -0.1875 to 0.1875
- down_proj: bfloat16 [2048, 1024], P('tensor', 'dp'), may hold values from -0.125 to 0.125
- channel_taps: bfloat16 [5, 24, 64], P(None, 'tensor', 'dp'), may hold values from -3 to 3
- mixer_gain: bfloat16 [24, 64], P('tensor', 'dp'), may hold values from 0.25 to 1.75
- decay_log: bfloat16 [24], P('tensor'), may hold values from -4 to 0
- step_bias: bfloat16 [24], P('tensor'), may hold values from -6 to -2
- skip_weight: bfloat16 [24], P('tensor'), may hold values from 0.5 to 2
- shared_proj: bfloat16 [1024, 512], P(('dp', 'tensor')), may hold values from -0.1875 to 0.1875
- norm_gains: bfloat16 [2, 1024], P(None, ('dp', 'tensor')), may hold values from 0.25 to 1.75
- shared_taps: bfloat16 [5, 256], P(None, ('dp', 'tensor')), may hold values from -3 to 3
- cotangent: bfloat16 [8192, 1024], P(('dp', 'tensor')), may hold values from -6 to 6
Outputs:
- layer_out: bfloat16 [8192, 1024], P(('dp', 'tensor'))
- gradient_tokens: bfloat16 [8192, 1024], P(('dp', 'tensor'))
- gradient_query: float32 [1024, 512], P('dp', 'tensor')
- gradient_attend: float32 [512, 1024], P('tensor', 'dp')
- gradient_inner: float32 [2, 1024, 1536], P(None, 'dp', 'tensor')
- gradient_step: float32 [1024, 24], P('dp', 'tensor')
- gradient_mamba: float32 [1536, 1024], P('tensor', 'dp')
- gradient_hidden: float32 [2, 1024, 2048], P(None, 'dp', 'tensor')
- gradient_down: float32 [2048, 1024], P('tensor', 'dp')
- gradient_channel: float32 [5, 24, 64], P(None, 'tensor', 'dp')
- gradient_mixer: float32 [24, 64], P('tensor', 'dp')
- gradient_decay: float32 [24], P('tensor')
- gradient_bias: float32 [24], P('tensor')
- gradient_skip: float32 [24], P('tensor')
- gradient_shared: float32 [1024, 512], P(('dp', 'tensor'))
- gradient_norms: float32 [2, 1024], P(None, ('dp', 'tensor'))
- gradient_taps: float32 [5, 256], P(None, ('dp', 'tensor'))
The draws below stay inside these ranges and needn't reach their ends.
All inputs are finite; a program needn't handle non-finite values.
Results may differ from the reference program's by a relative error of at most 0.024.
Values may be sent and summed in bfloat16 or wider, within the bound.
A program may use at most 192 MiB of HBM per device.

```python
import math
import jax
import jax.numpy as jnp
from jax import lax

D = 1024
QHEADS = 8
KVHEADS = 2
HEAD_SIZE = 64
SSM_HEADS = 24
SSM_DIM = 64
STATE = 128
CONV = 4
FF = 2048
LEN = 1024
INNER = 1536
SEQUENCES = 8
TOKENS = 8192


def shard_levels(rng, extent, cuts, smallest, high):
    def one(dim, parts):
        draws = jax.random.uniform(jax.random.fold_in(jax.random.fold_in(rng, 6), dim), (parts,), jnp.float32, smallest / len(cuts), high / len(cuts))
        return jnp.repeat(jnp.exp(draws), extent[dim] // parts).reshape((-1,) + (1,) * (len(extent) - dim - 1))

    level = one(*cuts[0])
    for cut in cuts[1:]:
        level = level * one(*cut)
    return level


def normal_values(own_key, extent, scale, bound, cuts=(), held_as=jnp.bfloat16):
    level = shard_levels(own_key, extent, cuts, -0.22, 0.18) if cuts else 1.0
    values = jax.random.normal(own_key, extent, jnp.float32) * scale * level
    return jnp.minimum(jnp.maximum(values, -bound), bound).astype(held_as)


def setup_inputs(seed: int = 0) -> dict:
    arg_keys = jax.random.split(jax.random.key(seed), 18)
    tokens = normal_values(arg_keys[0], (TOKENS, D), 1.0, 6.0, ((0, 32),))
    query_proj = normal_values(arg_keys[1], (D, QHEADS * HEAD_SIZE), D ** -0.5, 0.1875, ((0, 8), (1, 4)))
    attend_out = normal_values(arg_keys[2], (QHEADS * HEAD_SIZE, D), (QHEADS * HEAD_SIZE // 128) ** -0.5, 3.0, ((0, 4), (1, 8)))
    inner_proj = normal_values(arg_keys[3], (2, D, INNER), D ** -0.5, 0.1875, ((1, 8), (2, 4)))
    step_proj = normal_values(arg_keys[4], (D, SSM_HEADS), D ** -0.5, 0.1875, ((0, 8), (1, 4)))
    mamba_out = normal_values(arg_keys[5], (INNER, D), INNER ** -0.5, 0.15625, ((0, 4), (1, 8)))
    hidden_proj = normal_values(arg_keys[6], (2, D, FF), D ** -0.5, 0.1875, ((1, 8), (2, 4)))
    down_proj = normal_values(arg_keys[7], (FF, D), FF ** -0.5, 0.125, ((0, 4), (1, 8)))
    channel_taps = normal_values(arg_keys[8], (CONV + 1, SSM_HEADS, SSM_DIM), CONV ** -0.5, 3.0, ((1, 4), (2, 8)))
    mixer_gain = jnp.clip(1.0 + 0.15 * jax.random.normal(arg_keys[9], (SSM_HEADS, SSM_DIM), jnp.float32), 0.25, 1.75).astype(jnp.bfloat16)
    decay_log = jnp.clip(-4.0 + 4.0 * jax.random.uniform(arg_keys[10], (SSM_HEADS,), jnp.float32) ** shard_levels(arg_keys[10], (SSM_HEADS,), ((0, 4),), -0.2, 0.2), -4.0, 0.0).astype(jnp.bfloat16)
    step_bias = jnp.clip(-6.0 + 4.0 * jax.random.uniform(arg_keys[11], (SSM_HEADS,), jnp.float32) ** shard_levels(arg_keys[11], (SSM_HEADS,), ((0, 4),), -0.2, 0.2), -6.0, -2.0).astype(jnp.bfloat16)
    skip_weight = jnp.clip(0.5 + 1.5 * jax.random.uniform(arg_keys[12], (SSM_HEADS,), jnp.float32) ** shard_levels(arg_keys[12], (SSM_HEADS,), ((0, 4),), -0.2, 0.2), 0.5, 2.0).astype(jnp.bfloat16)
    shared_proj = normal_values(arg_keys[13], (D, 2 * KVHEADS * HEAD_SIZE + 2 * STATE), D ** -0.5, 0.1875, ((0, 32),))
    norm_gains = jnp.clip(1.0 + 0.15 * jax.random.normal(arg_keys[14], (2, D), jnp.float32), 0.25, 1.75).astype(jnp.bfloat16)
    shared_taps = normal_values(arg_keys[15], (CONV + 1, 2 * STATE), CONV ** -0.5, 3.0, ((1, 32),))
    cotangent = normal_values(arg_keys[16], (TOKENS, D), 1.0, 6.0, ((0, 32),))
    return dict(tokens=tokens, query_proj=query_proj, attend_out=attend_out, inner_proj=inner_proj, step_proj=step_proj, mamba_out=mamba_out, hidden_proj=hidden_proj, down_proj=down_proj, channel_taps=channel_taps, mixer_gain=mixer_gain, decay_log=decay_log, step_bias=step_bias, skip_weight=skip_weight, shared_proj=shared_proj, norm_gains=norm_gains, shared_taps=shared_taps, cotangent=cotangent)


epsilon = 1e-05
rope_base = 100000000000.0
highest_precision = lax.Precision.HIGHEST
neg_large = -1e+30
block_len = 128

@jax.custom_vjp
def low(v):
    return lax.optimization_barrier(v.astype(jnp.bfloat16)).astype(jnp.float32)

@jax.custom_vjp
def lowered_backward(v):
    return v

def low_keep(v):
    return (low(v), None)

def low_pass(kept, grad):
    return (grad,)

def back_keep(v):
    return (v, None)

def back_low(kept, grad):
    return (low(grad),)
low.defvjp(low_keep, low_pass)
lowered_backward.defvjp(back_keep, back_low)

def norm_apply(values, gain):
    factor = lax.rsqrt(lax.optimization_barrier(jnp.mean(values * values, axis=-1, keepdims=True)) + epsilon)
    return values * factor * gain

def rope_tables(length, width):
    halfway = width // 2
    inverse = rope_base ** (-jnp.arange(halfway, dtype=jnp.float32) * (2.0 / width))
    angles = jnp.arange(length, dtype=jnp.float32)[:, None] * inverse[None, :]
    return (jnp.cos(angles), jnp.sin(angles))

def rotate(values, cosine, sine):
    halfway = values.shape[-1] // 2
    first = values[..., :halfway]
    second = values[..., halfway:]
    cos_wide = cosine[:, None, :]
    sin_wide = sine[:, None, :]
    return jnp.concatenate([first * cos_wide - second * sin_wide, second * cos_wide + first * sin_wide], axis=-1)

def causal_conv(sequences, table):
    taps = table.shape[0] - 1
    length = sequences.shape[1]
    padded = jnp.pad(sequences, ((0, 0), (taps - 1, 0), (0, 0)))
    total = table[taps] + jnp.zeros_like(sequences)
    for offset in range(taps):
        total = total + table[offset] * padded[:, offset:offset + length]
    return total

def duality_scan(inputs, step_size, decay, in_mat, out_mat):
    length, num_heads, head_width = inputs.shape
    state_width = in_mat.shape[-1]
    window = min(block_len, length)
    blocks = length // window
    x_blocks = inputs.reshape(blocks, window, num_heads, head_width)
    s_blocks = step_size.reshape(blocks, window, num_heads)
    b_blocks = in_mat.reshape(blocks, window, state_width)
    c_blocks = out_mat.reshape(blocks, window, state_width)
    cumul = jnp.cumsum(s_blocks * decay, axis=1)
    lower_mask = jnp.arange(window)[:, None] >= jnp.arange(window)[None, :]
    gap_logs = cumul[:, :, None, :] - cumul[:, None, :, :]
    fading = jnp.exp(jnp.where(lower_mask[None, :, :, None], gap_logs, -jnp.inf))
    cross_terms = jnp.einsum('cin,cjn->cij', c_blocks, b_blocks, precision=highest_precision)
    mixing = cross_terms[..., None] * fading * s_blocks[:, None, :, :]
    within = jnp.einsum('cijh,cjhp->cihp', mixing, x_blocks, precision=highest_precision)
    ending = cumul[:, -1:, :]
    carried = x_blocks * (jnp.exp(ending - cumul) * s_blocks)[..., None]
    contrib = jnp.einsum('cjn,cjhp->chnp', b_blocks, carried, precision=highest_precision)
    block_fade = jnp.exp(ending[:, 0, :])

    def advance(carry, pieces):
        fade_now, added = pieces
        return (fade_now[:, None, None] * carry + added, carry)
    start = jnp.zeros((num_heads, state_width, head_width), inputs.dtype)
    finished, entering = lax.scan(advance, start, (block_fade, contrib))
    across = jnp.einsum('cin,chnp->cihp', c_blocks, entering, precision=highest_precision) * jnp.exp(cumul)[..., None]
    return (within + across).reshape(length, num_heads, head_width)

def mixer_local(gate_raw, signal_raw, step_raw, pair_raw, inner_taps, outer_taps, decay_log, step_bias, skip_weight, num_seq):
    total_rows = gate_raw.shape[0]
    seq_len = total_rows // num_seq
    num_heads = step_raw.shape[1]
    head_width = signal_raw.shape[1] // num_heads
    signal = jax.nn.silu(causal_conv(signal_raw.reshape(num_seq, seq_len, -1), inner_taps))
    paired = jax.nn.silu(causal_conv(pair_raw.reshape(num_seq, seq_len, -1), outer_taps))
    state_width = paired.shape[-1] // 2
    in_mat = paired[..., :state_width]
    out_mat = paired[..., state_width:]
    step_size = jax.nn.softplus(step_raw.reshape(num_seq, seq_len, num_heads) + step_bias)
    decay = -jnp.exp(decay_log)
    signal_heads = signal.reshape(num_seq, seq_len, num_heads, head_width)
    scanned = jax.vmap(duality_scan, in_axes=(0, 0, None, 0, 0))(signal_heads, step_size, decay, in_mat, out_mat)
    scanned = scanned + skip_weight[:, None] * signal_heads
    return scanned.reshape(total_rows, num_heads * head_width) * jax.nn.silu(gate_raw)

def attend_ref(pieces):
    query_rows, key_repeated, value_repeated = pieces
    length = query_rows.shape[0]
    attention_scores = lowered_backward(jnp.einsum('bja,oja->jbo', query_rows, key_repeated, precision=highest_precision) * HEAD_SIZE ** (-0.5))
    causal = jnp.arange(length)[:, None] >= jnp.arange(length)[None, :]
    attention_scores = jnp.where(causal[None], attention_scores, neg_large)
    attention_probabilities = low(jax.nn.softmax(attention_scores, axis=-1))
    return jnp.einsum('rfu,urs->frs', attention_probabilities, value_repeated, precision=highest_precision)

def layer_forward(tokens, params, num_seq):
    query_proj, attend_out, inner_proj, step_proj, mamba_out, hidden_proj, down_proj, channel_taps, mixer_gain, decay_log, step_bias, skip_weight, shared_proj, norm_gains, shared_taps = params
    total_rows = tokens.shape[0]
    seq_len = total_rows // num_seq
    kv_cols = KVHEADS * HEAD_SIZE
    normed = low(norm_apply(tokens, norm_gains[0]))
    query_raw = lowered_backward(jnp.dot(normed, query_proj, precision=highest_precision))
    shared_raw = lowered_backward(jnp.dot(normed, shared_proj, precision=highest_precision))
    gate_raw = lowered_backward(jnp.dot(normed, inner_proj[0], precision=highest_precision))
    signal_raw = lowered_backward(jnp.dot(normed, inner_proj[1], precision=highest_precision))
    step_raw = lowered_backward(jnp.dot(normed, step_proj, precision=highest_precision))
    cosine, sine = rope_tables(seq_len, HEAD_SIZE)
    query_rows = low(rotate(query_raw.reshape(num_seq, seq_len, QHEADS, HEAD_SIZE), cosine, sine))
    key_all = low(rotate(shared_raw[:, :kv_cols].reshape(num_seq, seq_len, KVHEADS, HEAD_SIZE), cosine, sine))
    value_all = low(shared_raw[:, kv_cols:2 * kv_cols].reshape(num_seq, seq_len, KVHEADS, HEAD_SIZE))
    group_size = QHEADS // KVHEADS
    key_repeated = jnp.repeat(key_all, group_size, axis=2)
    value_repeated = jnp.repeat(value_all, group_size, axis=2)
    attended = lax.map(jax.checkpoint(attend_ref), (query_rows, key_repeated, value_repeated))
    attended = low(lowered_backward(attended.reshape(total_rows, QHEADS * HEAD_SIZE)))
    attn_term = jnp.dot(attended, attend_out, precision=highest_precision)
    mixed_in = mixer_local(gate_raw, signal_raw, step_raw, shared_raw[:, 2 * kv_cols:], channel_taps.reshape(CONV + 1, INNER), shared_taps, decay_log, step_bias, skip_weight, num_seq)
    inv_rms = lax.rsqrt(lax.optimization_barrier(jnp.mean(mixed_in * mixed_in, axis=-1, keepdims=True)) + epsilon)
    mamba_low = low(mixed_in * inv_rms * mixer_gain.reshape(INNER))
    mamba_term = jnp.dot(mamba_low, mamba_out, precision=highest_precision)
    hidden = tokens + lowered_backward(attn_term + mamba_term)
    normed_two = low(norm_apply(hidden, norm_gains[1]))
    gate_val = lowered_backward(jnp.dot(normed_two, hidden_proj[0], precision=highest_precision))
    up_val = lowered_backward(jnp.dot(normed_two, hidden_proj[1], precision=highest_precision))
    inner_low = low(jax.nn.silu(gate_val) * up_val)
    return hidden + jnp.dot(inner_low, down_proj, precision=highest_precision)

def reference(tokens, query_proj, attend_out, inner_proj, step_proj, mamba_out, hidden_proj, down_proj, channel_taps, mixer_gain, decay_log, step_bias, skip_weight, shared_proj, norm_gains, shared_taps, cotangent):
    params = tuple((weight.astype(jnp.float32) for weight in (query_proj, attend_out, inner_proj, step_proj, mamba_out, hidden_proj, down_proj, channel_taps, mixer_gain, decay_log, step_bias, skip_weight, shared_proj, norm_gains, shared_taps)))
    group_seq = math.gcd(4, SEQUENCES)
    num_groups = SEQUENCES // group_seq
    group_rows = group_seq * LEN
    token_groups = tokens.astype(jnp.float32).reshape(num_groups, group_rows, D)
    cot_groups = cotangent.astype(jnp.float32).reshape(num_groups, group_rows, D)

    def one_group(totals, pieces):
        token_block, cot_block = pieces

        def forward(token_arg, param_arg):
            return layer_forward(token_arg, param_arg, group_seq)
        result, pullback = jax.vjp(forward, token_block, params)
        grad_tokens, grad_params = pullback(cot_block)
        totals = jax.tree.map(jnp.add, totals, grad_params)
        return (totals, (result.astype(jnp.bfloat16), grad_tokens.astype(jnp.bfloat16)))
    initial = jax.tree.map(jnp.zeros_like, params)
    grads, (results, grad_rows) = lax.scan(one_group, initial, (token_groups, cot_groups))
    g_query, g_attend, g_inner, g_step, g_mamba, g_hidden, g_down, g_channel, g_mixer, g_decay, g_bias, g_skip, g_shared, g_norms, g_taps = grads
    return (results.reshape(TOKENS, D), grad_rows.reshape(TOKENS, D), g_query, g_attend, g_inner, g_step, g_mamba, g_hidden, g_down, g_channel, g_mixer, g_decay, g_bias, g_skip, g_shared, g_norms, g_taps)
```

```python
from functools import partial

import jax
import jax.numpy as jnp
from jax import lax
from jax.experimental import pallas as pl
from jax.experimental.pallas import tpu as pltpu
from jax.sharding import PartitionSpec as P

MESH = pl.DeviceIdType.MESH

QHEADS = 8
KVHEADS = 2
HEAD_SIZE = 64
SSM_DIM = 64
CONV = 4
SEQS_DEV = 1
INNER = 1536


epsilon = 1e-05
rope_base = 100000000000.0
highest_precision = lax.Precision.HIGHEST
neg_large = -1e30
block_len = 128


def norm_apply(values, gain):
    factor = lax.rsqrt(jnp.mean(values * values, axis=-1, keepdims=True) + epsilon)
    return values * factor * gain


def rope_tables(length, width):
    halfway = width // 2
    inverse = rope_base ** (-jnp.arange(halfway, dtype=jnp.float32) * (2.0 / width))
    angles = jnp.arange(length, dtype=jnp.float32)[:, None] * inverse[None, :]
    return (jnp.cos(angles), jnp.sin(angles))


def rotate(values, cosine, sine):
    halfway = values.shape[-1] // 2
    first = values[..., :halfway]
    second = values[..., halfway:]
    cos_wide = cosine[:, None, :]
    sin_wide = sine[:, None, :]
    return jnp.concatenate(
        [first * cos_wide - second * sin_wide, second * cos_wide + first * sin_wide], axis=-1
    )


def causal_conv(sequences, table):
    taps = table.shape[0] - 1
    length = sequences.shape[1]
    padded = jnp.pad(sequences, ((0, 0), (taps - 1, 0), (0, 0)))
    total = table[taps] + jnp.zeros_like(sequences)
    for offset in range(taps):
        total = total + table[offset] * padded[:, offset : offset + length]
    return total


def duality_scan(inputs, step_size, decay, in_mat, out_mat):
    length, num_heads, head_width = inputs.shape
    state_width = in_mat.shape[-1]
    window = min(block_len, length)
    blocks = length // window
    x_blocks = inputs.reshape(blocks, window, num_heads, head_width)
    s_blocks = step_size.reshape(blocks, window, num_heads)
    b_blocks = in_mat.reshape(blocks, window, state_width)
    c_blocks = out_mat.reshape(blocks, window, state_width)
    cumul = jnp.cumsum(s_blocks * decay, axis=1)
    lower_mask = jnp.arange(window)[:, None] >= jnp.arange(window)[None, :]
    gap_logs = cumul[:, :, None, :] - cumul[:, None, :, :]
    fading = jnp.exp(jnp.where(lower_mask[None, :, :, None], gap_logs, -jnp.inf))
    cross_terms = jnp.einsum("cin,cjn->cij", c_blocks, b_blocks, precision=highest_precision)
    mixing = cross_terms[..., None] * fading * s_blocks[:, None, :, :]
    within = jnp.einsum("cijh,cjhp->cihp", mixing, x_blocks, precision=highest_precision)
    ending = cumul[:, -1:, :]
    carried = x_blocks * (jnp.exp(ending - cumul) * s_blocks)[..., None]
    contrib = jnp.einsum("cjn,cjhp->chnp", b_blocks, carried, precision=highest_precision)
    block_fade = jnp.exp(ending[:, 0, :])

    def advance(carry, pieces):
        fade_now, added = pieces
        return (fade_now[:, None, None] * carry + added, carry)

    start = jnp.zeros((num_heads, state_width, head_width), inputs.dtype)
    finished, entering = lax.scan(advance, start, (block_fade, contrib))
    across = (
        jnp.einsum("cin,chnp->cihp", c_blocks, entering, precision=highest_precision)
        * jnp.exp(cumul)[..., None]
    )
    return (within + across).reshape(length, num_heads, head_width)


def mixer_local(
    gate_raw,
    signal_raw,
    step_raw,
    pair_raw,
    inner_taps,
    outer_taps,
    decay_log,
    step_bias,
    skip_weight,
    num_seq,
):
    total_rows = gate_raw.shape[0]
    seq_len = total_rows // num_seq
    num_heads = step_raw.shape[1]
    head_width = signal_raw.shape[1] // num_heads
    signal = jax.nn.silu(causal_conv(signal_raw.reshape(num_seq, seq_len, -1), inner_taps))
    paired = jax.nn.silu(causal_conv(pair_raw.reshape(num_seq, seq_len, -1), outer_taps))
    state_width = paired.shape[-1] // 2
    in_mat = paired[..., :state_width]
    out_mat = paired[..., state_width:]
    step_size = jax.nn.softplus(step_raw.reshape(num_seq, seq_len, num_heads) + step_bias)
    decay = -jnp.exp(decay_log)
    signal_heads = signal.reshape(num_seq, seq_len, num_heads, head_width)
    scanned = jax.vmap(duality_scan, in_axes=(0, 0, None, 0, 0))(
        signal_heads, step_size, decay, in_mat, out_mat
    )
    scanned = scanned + skip_weight[:, None] * signal_heads
    return scanned.reshape(total_rows, num_heads * head_width) * jax.nn.silu(gate_raw)


def causal_scores(query_low, key_low):
    length = query_low.shape[0]
    attention_scores = jnp.einsum(
        "lhd,md->hlm", query_low, key_low, preferred_element_type=jnp.float32
    ) * HEAD_SIZE ** (-0.5)
    causal = jnp.arange(length)[:, None] >= jnp.arange(length)[None, :]
    return jnp.where(causal[None], attention_scores, neg_large)


def attend_forward(pieces):
    query_low, key_low, value_low = pieces
    attention_scores = causal_scores(query_low, key_low)
    top_score = jnp.max(attention_scores, axis=-1, keepdims=True)
    expd = jnp.exp(attention_scores - top_score)
    total = jnp.sum(expd, axis=-1, keepdims=True)
    attention_probabilities = (expd / total).astype(jnp.bfloat16)
    result = jnp.einsum(
        "hlm,md->lhd", attention_probabilities, value_low, preferred_element_type=jnp.float32
    )
    return (result.astype(jnp.bfloat16), top_score[..., 0] + jnp.log(total[..., 0]))


def attend_backward(pieces):
    query_low, key_low, value_low, log_sums, grad_low = pieces
    attention_scores = causal_scores(query_low, key_low)
    attention_probabilities = jnp.exp(attention_scores - log_sums[..., None])
    probs_low = attention_probabilities.astype(jnp.bfloat16)
    grad_probs = jnp.einsum("lhd,md->hlm", grad_low, value_low, preferred_element_type=jnp.float32)
    centre = jnp.sum(attention_probabilities * grad_probs, axis=-1, keepdims=True)
    grad_scores = (attention_probabilities * (grad_probs - centre)).astype(jnp.bfloat16)
    query_back = jnp.einsum(
        "hlm,md->lhd", grad_scores, key_low, preferred_element_type=jnp.float32
    ) * HEAD_SIZE ** (-0.5)
    key_back = jnp.einsum(
        "hlm,lhd->md", grad_scores, query_low, preferred_element_type=jnp.float32
    ) * HEAD_SIZE ** (-0.5)
    value_back = jnp.einsum("hlm,lhd->md", probs_low, grad_low, preferred_element_type=jnp.float32)
    return (query_back, key_back, value_back)


def dp_bits(index):
    core = lax.rem(index, 2)
    xbit = lax.rem(index // 2, 2)
    ybit = lax.rem(index // 4, 2)
    return core, xbit, ybit


def gather_kernel(nt, *refs):
    (tok, que, att, inn, stp, mam, sha, sma) = refs[:8]
    (tok_f, que_f, att_f, inn_f, stp_f, mam_f, sha_f, sma_f) = refs[8:16]
    (lsem, zs_send, zs_recv, t_send, t_recv, d_send, d_recv) = refs[16:]
    d = lax.axis_index("dp")
    z = lax.axis_index("tensor")
    core, xbit, ybit = dp_bits(d)
    d_core = d + 1 - 2 * core
    d_x = d + 2 - 4 * xbit
    d_y = d + 4 - 8 * ybit
    d_xy = d_x + 4 - 8 * ybit

    barrier = pltpu.get_barrier_semaphore()
    for peer in (d_core, d_x, d_y):
        pl.semaphore_signal(barrier, inc=1, device_id=(peer, z), device_id_type=MESH)
    for k in range(1, nt):
        pl.semaphore_signal(
            barrier, inc=1, device_id=(d, lax.rem(z + k, nt)), device_id_type=MESH
        )
    pl.semaphore_wait(barrier, 3 + nt - 1)

    def remote(src, dst, send, recv, dev):
        return pltpu.make_async_remote_copy(
            src_ref=src, dst_ref=dst, send_sem=send, recv_sem=recv,
            device_id=dev, device_id_type=MESH,
        )

    small = []
    for i, (src, dst) in enumerate(((sha, sha_f), (sma, sma_f))):
        for k in range(1, nt):
            copy = remote(
                src, dst.at[d, z], zs_send.at[i, k], zs_recv.at[i, k],
                (d, lax.rem(z + k, nt)),
            )
            copy.start()
            small.append(copy)
    q_rows = que.shape[0]
    cols = att.shape[1]
    i_rows = inn.shape[1]
    s_rows = stp.shape[0]
    items = (
        (inn, lambda s: inn_f.at[:, pl.ds(s * i_rows, i_rows)]),
        (que, lambda s: que_f.at[pl.ds(s * q_rows, q_rows)]),
        (att, lambda s: att_f.at[:, pl.ds(pl.multiple_of(s * cols, cols), cols)]),
        (stp, lambda s: stp_f.at[pl.ds(s * s_rows, s_rows)]),
        (mam, lambda s: mam_f.at[:, pl.ds(pl.multiple_of(s * cols, cols), cols)]),
    )
    locals_ = []
    for i, (src, dst) in enumerate(
        [(tok, tok_f.at[z]), (sha, sha_f.at[d, z]), (sma, sma_f.at[d, z])]
        + [(src, at(d)) for src, at in items]
    ):
        copy = pltpu.make_async_copy(src, dst, lsem.at[i])
        copy.start()
        locals_.append(copy)
    sent = []

    def stage_one(i, src, at):
        for j, peer in enumerate((d_x, d_y, d_core)):
            copy = remote(src, at(d), d_send.at[i, j], d_recv.at[i, j], (peer, z))
            copy.start()
            sent.append(copy)

    for i, (src, at) in enumerate(items):
        stage_one(i, src, at)

    def tok_copy(slot, dirn, hop):
        dev = z + 1 if dirn == 0 else z - 1
        return remote(
            tok_f.at[slot], tok_f.at[slot], t_send.at[dirn, hop], t_recv.at[dirn, hop], (d, dev)
        )

    def own_copy(dirn):
        dev = z + 1 if dirn == 0 else z - 1
        return remote(tok, tok_f.at[z], t_send.at[dirn, 0], t_recv.at[dirn, 0], (d, dev))

    pl.when(z < nt - 1)(lambda: own_copy(0).start())
    pl.when(z > 0)(lambda: own_copy(1).start())

    locals_[1].wait()
    locals_[2].wait()
    for copy in small:
        copy.wait()
    n = len(items)
    shared_items = (
        (sha_f.at[d], lambda s: sha_f.at[s]),
        (sma_f.at[d], lambda s: sma_f.at[s]),
    )
    for i, (src, at) in enumerate(shared_items):
        stage_one(n + i, src, at)

    def wait_recv(i, j, at, slot):
        remote(at(slot), at(slot), d_send.at[i, j], d_recv.at[i, j], (d_core, z)).wait_recv()

    def forward(i, j, at, slot, peer):
        copy = remote(at(slot), at(slot), d_send.at[i, j], d_recv.at[i, j], (peer, z))
        copy.start()
        sent.append(copy)

    everything = [at for _, at in items] + [at for _, at in shared_items]
    via_y = (0, n + 1)

    def diagonal(i, at):
        wait_recv(i, 0, at, d_x)
        if i in via_y:
            forward(i, 3, at, d_x, d_y)
        forward(i, 4, at, d_x, d_core)
        wait_recv(i, 1, at, d_y)
        if i not in via_y:
            forward(i, 3, at, d_y, d_x)
        forward(i, 5, at, d_y, d_core)

    for i in range(n):
        diagonal(i, everything[i])

    def hop(dist):
        def from_left():
            tok_copy(z - dist, 0, dist - 1).wait_recv()

        def from_right():
            tok_copy(z + dist, 1, dist - 1).wait_recv()

        pl.when(z >= dist)(from_left)
        if dist < nt - 1:
            pl.when((z >= dist) & (z < nt - 1))(lambda: tok_copy(z - dist, 0, dist).start())
        pl.when(z + dist < nt)(from_right)
        if dist < nt - 1:
            pl.when((z + dist < nt) & (z > 0))(lambda: tok_copy(z + dist, 1, dist).start())

    hop(1)
    for i in range(n, n + 2):
        diagonal(i, everything[i])
    for i, at in enumerate(everything):
        wait_recv(i, 3, at, d_xy)
        forward(i, 6, at, d_xy, d_core)
    for dist in range(2, nt):
        hop(dist)
    for i, at in enumerate(everything):
        wait_recv(i, 2, at, d_core)
        for j in (4, 5, 6):
            wait_recv(i, j, at, d_core)
    for i, copy in enumerate(locals_):
        if i not in (1, 2):
            copy.wait()
    for copy in sent:
        copy.wait_send()
    pl.when(z < nt - 1)(lambda: own_copy(0).wait_send())
    pl.when(z > 0)(lambda: own_copy(1).wait_send())
    for dist in range(1, nt - 1):
        pl.when((z >= dist) & (z < nt - 1))(lambda: tok_copy(z - dist, 0, dist).wait_send())
        pl.when((z + dist < nt) & (z > 0))(lambda: tok_copy(z + dist, 1, dist).wait_send())


def gather_start(tok, que, att, inn, stp, mam, sha, sma, nd, nt):
    if nd != 8:
        shared = lax.all_gather(sha, ("dp", "tensor"), axis=0)
        small = lax.all_gather(sma, ("dp", "tensor"), axis=0)
        return (
            lax.all_gather(tok, "tensor", axis=0),
            lax.all_gather(que, "dp", axis=0, tiled=True),
            lax.all_gather(att, "dp", axis=1, tiled=True),
            lax.all_gather(inn, "dp", axis=1, tiled=True),
            lax.all_gather(stp, "dp", axis=0, tiled=True),
            lax.all_gather(mam, "dp", axis=1, tiled=True),
            shared.reshape((nd, nt) + sha.shape),
            small.reshape((nd, nt) + sma.shape),
        )
    bf = jnp.bfloat16
    outs = (
        (nt,) + tok.shape,
        (nd * que.shape[0], que.shape[1]),
        (att.shape[0], nd * att.shape[1]),
        (2, nd * inn.shape[1], inn.shape[2]),
        (nd * stp.shape[0], stp.shape[1]),
        (mam.shape[0], nd * mam.shape[1]),
        (nd, nt) + sha.shape,
        (nd, nt) + sma.shape,
    )
    anywhere = pl.BlockSpec(memory_space=pl.ANY)
    dma = pltpu.SemaphoreType.DMA
    return pl.pallas_call(
        partial(gather_kernel, nt),
        out_shape=[jax.ShapeDtypeStruct(s, bf) for s in outs],
        in_specs=[anywhere] * 8,
        out_specs=[anywhere] * 8,
        scratch_shapes=[
            dma((8,)), dma((2, nt)), dma((2, nt)), dma((2, nt)), dma((2, nt)),
            dma((7, 7)), dma((7, 7)),
        ],
        compiler_params=pltpu.CompilerParams(collective_id=0, has_side_effects=True),
        name="gather_start",
    )(tok, que, att, inn, stp, mam, sha, sma)


def pick(values, index, axis=0):
    return lax.dynamic_index_in_dim(values, index, axis, keepdims=False)


def add_low(left, right):
    return (left.astype(jnp.float32) + right.astype(jnp.float32)).astype(jnp.bfloat16)


def chain_gather(values, nt):
    z = lax.axis_index("tensor")
    out = jnp.zeros((nt,) + values.shape, values.dtype)
    out = lax.dynamic_update_index_in_dim(out, values, z, 0)
    right = left = values
    for dist in range(1, nt):
        right = lax.ppermute(right, "tensor", [(i, i + 1) for i in range(dist - 1, nt - 1)])
        left = lax.ppermute(left, "tensor", [(i, i - 1) for i in range(1, nt - dist + 1)])
        pieces = out
        pieces = jnp.where(
            z >= dist,
            lax.dynamic_update_index_in_dim(pieces, right, jnp.maximum(z - dist, 0), 0),
            pieces,
        )
        out = jnp.where(
            z + dist < nt,
            lax.dynamic_update_index_in_dim(pieces, left, jnp.minimum(z + dist, nt - 1), 0),
            pieces,
        )
    return out


def chain_scatter(parts, nt):
    z = lax.axis_index("tensor")
    right = left = None
    for t in range(nt - 1):
        to_right = pick(parts, jnp.clip(nt - 1 - t + z, 0, nt - 1))
        to_left = pick(parts, jnp.clip(t - (nt - 1) + z, 0, nt - 1))
        if t > 0:
            to_right = add_low(to_right, right)
            to_left = add_low(to_left, left)
        right = lax.ppermute(to_right, "tensor", [(i, i + 1) for i in range(t + 1)])
        left = lax.ppermute(
            to_left, "tensor", [(nt - 1 - i, nt - 2 - i) for i in range(t + 1)]
        )
    f32 = jnp.float32
    return pick(parts, z).astype(f32) + right.astype(f32) + left.astype(f32)


def cube_scatter(parts, nd, last=jnp.float32):
    if nd != 8:
        return lax.psum_scatter(parts, "dp", scatter_dimension=0, tiled=False).astype(last)
    d = lax.axis_index("dp")
    core, xbit, ybit = dp_bits(d)

    def swap(values, bit):
        return lax.ppermute(values, "dp", [(i, i ^ bit) for i in range(8)])

    tail = parts.shape[1:]
    cut = parts.reshape((4, 2) + tail)
    held = add_low(pick(cut, core, 1), swap(pick(cut, 1 - core, 1), 1))
    held = held.reshape((2, 2) + tail)
    half = tail[0] // 2
    one, two = held[:, :, :half], held[:, :, half:]
    one_b = add_low(pick(one, xbit, 1), swap(pick(one, 1 - xbit, 1), 2))
    two_b = add_low(pick(two, ybit, 0), swap(pick(two, 1 - ybit, 0), 4))
    f32 = jnp.float32
    one_c = pick(one_b, ybit).astype(f32) + swap(pick(one_b, 1 - ybit), 4).astype(f32)
    two_c = pick(two_b, xbit).astype(f32) + swap(pick(two_b, 1 - xbit), 2).astype(f32)
    return jnp.concatenate([one_c, two_c], axis=0).astype(last)


def tensor_total(values):
    return lax.psum(values, "tensor")


def matmul(left, right):
    return jnp.dot(left, right, preferred_element_type=jnp.float32)


def left_contract(left, right):
    return jnp.einsum("md,mk->dk", left, right, preferred_element_type=jnp.float32)


def right_contract(left, right):
    return jnp.einsum("mk,dk->md", left, right, preferred_element_type=jnp.float32)


def per_device(
    nd,
    nt,
    tokens,
    query_proj,
    attend_out,
    inner_proj,
    step_proj,
    mamba_out,
    hidden_proj,
    down_proj,
    channel_taps,
    mixer_gain,
    decay_log,
    step_bias,
    skip_weight,
    shared_proj,
    norm_gains,
    shared_taps,
    cotangent,
):
    f32, bf16 = jnp.float32, jnp.bfloat16
    tensor_index = lax.axis_index("tensor")
    local_rows, width = tokens.shape
    group_rows = local_rows * nt
    seq_count = SEQS_DEV
    seq_len = group_rows // seq_count
    kv_cols = KVHEADS * HEAD_SIZE
    local_heads = step_proj.shape[1]
    lanes = width // nd
    units = down_proj.shape[0]
    small_parts = [channel_taps, mixer_gain, norm_gains, shared_taps]
    flat = jnp.concatenate([p.reshape(-1) for p in small_parts])
    small_len = -(-flat.shape[0] // 2048) * 2048
    small = jnp.pad(flat, (0, small_len - flat.shape[0])).reshape(-1, 128)
    (tok_full, full_query, full_attend, full_inner, full_step, full_mamba, sha, sma) = gather_start(
        tokens, query_proj, attend_out, inner_proj, step_proj, mamba_out, shared_proj, small, nd, nt
    )
    hid_in, down_in, tok_full = lax.optimization_barrier((hidden_proj, down_proj, tok_full))
    full_hidden = lax.all_gather(hid_in, "tensor", axis=2, tiled=True)
    full_hidden = lax.all_gather(full_hidden, "dp", axis=1, tiled=True)
    full_down = lax.all_gather(down_in, "tensor", axis=0, tiled=True)
    full_down = lax.all_gather(full_down, "dp", axis=1, tiled=True)

    full_shared = sha.reshape(width, -1)
    sma = sma.reshape(nd, nt, small_len)

    def small_piece(index):
        start = sum(p.size for p in small_parts[:index])
        part = small_parts[index]
        return sma[:, :, start : start + part.size].reshape((nd, nt) + part.shape)

    mine_taps = pick(small_piece(0), tensor_index, 1)
    full_taps = mine_taps.transpose(1, 2, 0, 3)
    full_gain = pick(small_piece(1), tensor_index, 1).transpose(1, 0, 2)
    full_norms = small_piece(2).transpose(2, 0, 1, 3).reshape(2, width)
    full_stap = small_piece(3).transpose(2, 0, 1, 3).reshape(CONV + 1, -1)
    taps_inner = full_taps.astype(f32).reshape(CONV + 1, local_heads * SSM_DIM)
    taps_shared = full_stap.astype(f32)
    gain_mix = full_gain.astype(f32).reshape(local_heads * SSM_DIM)
    gain_first = full_norms[0].astype(f32)
    gain_second = full_norms[1].astype(f32)

    token_f32 = tokens.astype(f32)
    group_one = norm_apply(tok_full.reshape(group_rows, width).astype(f32), gain_first).astype(bf16)
    query_raw = matmul(group_one, full_query)
    shared_raw = matmul(group_one, full_shared)
    gate_raw = matmul(group_one, full_inner[0])
    signal_raw = matmul(group_one, full_inner[1])
    step_raw = matmul(group_one, full_step)
    q_heads = query_raw.shape[1] // HEAD_SIZE
    kv_head = tensor_index * q_heads // (QHEADS // KVHEADS)
    cosine, sine = rope_tables(seq_len, HEAD_SIZE)
    query_rot = rotate(
        query_raw.reshape(seq_count, seq_len, q_heads, HEAD_SIZE), cosine, sine
    ).astype(bf16)
    key_raw = lax.dynamic_slice_in_dim(shared_raw, kv_head * HEAD_SIZE, HEAD_SIZE, 1)
    value_raw = lax.dynamic_slice_in_dim(shared_raw, kv_cols + kv_head * HEAD_SIZE, HEAD_SIZE, 1)
    key_rot = rotate(key_raw.reshape(seq_count, seq_len, 1, HEAD_SIZE), cosine, sine)[
        :, :, 0
    ].astype(bf16)
    value_low = value_raw.reshape(seq_count, seq_len, HEAD_SIZE).astype(bf16)
    attended, log_sums = lax.map(attend_forward, (query_rot, key_rot, value_low))
    attended_flat = attended.reshape(group_rows, q_heads * HEAD_SIZE)
    mix_part = matmul(attended_flat, full_attend)
    mixed_in, mixer_back = jax.vjp(
        partial(mixer_local, num_seq=seq_count),
        gate_raw,
        signal_raw,
        step_raw,
        shared_raw[:, 2 * kv_cols :],
        taps_inner,
        taps_shared,
        decay_log.astype(f32),
        step_bias.astype(f32),
        skip_weight.astype(f32),
    )
    square_sum = tensor_total(jnp.sum(mixed_in * mixed_in, axis=1))
    inv_rms = lax.rsqrt(square_sum / INNER + epsilon)[:, None]
    mamba_low = (mixed_in * inv_rms * gain_mix).astype(bf16)
    mix_part = mix_part + matmul(mamba_low, full_mamba)
    hidden = token_f32 + chain_scatter(mix_part.astype(bf16).reshape(nt, local_rows, width), nt)
    normed_two, norm_two_back = jax.vjp(norm_apply, hidden, gain_second)
    local_two = normed_two.astype(bf16)
    gate_val = matmul(local_two, full_hidden[0])
    up_val = matmul(local_two, full_hidden[1])
    sigmoid_gate = jax.nn.sigmoid(gate_val)
    inner_low = (gate_val * sigmoid_gate * up_val).astype(bf16)
    hidden_out = hidden + matmul(inner_low, full_down)
    layer_out = hidden_out.astype(bf16)
    grad_inner_units = right_contract(cotangent, full_down)
    grad_up = (grad_inner_units * gate_val * sigmoid_gate).astype(bf16)
    grad_gate = (
        grad_inner_units * up_val * sigmoid_gate * (1.0 + gate_val * (1.0 - sigmoid_gate))
    ).astype(bf16)
    grad_normed_two = right_contract(grad_gate, full_hidden[0]) + right_contract(
        grad_up, full_hidden[1]
    )
    grad_from_two, grad_gain_two = norm_two_back(grad_normed_two)
    grad_resid = cotangent.astype(f32) + grad_from_two
    grad_mix = chain_gather(grad_resid.astype(bf16), nt).reshape(group_rows, width)
    grad_down = left_contract(inner_low, cotangent)
    grad_hidden = jnp.stack([left_contract(local_two, grad_gate), left_contract(local_two, grad_up)])
    hidden_rows = width // nd
    hid_pieces = (
        grad_hidden.astype(bf16)
        .reshape(2, nd, hidden_rows, nt, units)
        .transpose(1, 3, 0, 2, 4)
        .reshape(nd, nt, 2 * hidden_rows, units)
    )
    down_pieces = (
        grad_down.astype(bf16).reshape(nt, units, nd, lanes).transpose(2, 0, 1, 3)
    )
    hid_sum = cube_scatter(hid_pieces, nd, bf16)
    down_sum = cube_scatter(down_pieces, nd, bf16)
    gradient_hidden = chain_scatter(hid_sum, nt).reshape(2, hidden_rows, units)
    gradient_down = chain_scatter(down_sum, nt)

    grad_attend = left_contract(attended_flat, grad_mix)
    grad_attended = right_contract(grad_mix, full_attend).astype(bf16)
    grad_attended = grad_attended.reshape(seq_count, seq_len, q_heads, HEAD_SIZE)
    query_back, key_back, value_back = lax.map(
        attend_backward, (query_rot, key_rot, value_low, log_sums, grad_attended)
    )
    grad_query_raw = (
        rotate(query_back, cosine, -sine).reshape(group_rows, q_heads * HEAD_SIZE).astype(bf16)
    )
    grad_key_raw = rotate(key_back[:, :, None], cosine, -sine).reshape(group_rows, HEAD_SIZE)
    grad_value_raw = value_back.reshape(group_rows, HEAD_SIZE)
    grad_query = left_contract(group_one, grad_query_raw)
    part_one = right_contract(grad_query_raw, full_query)
    grad_mamba = left_contract(mamba_low, grad_mix)
    grad_normed_mix = right_contract(grad_mix, full_mamba)
    scaled_grad = grad_normed_mix * gain_mix
    grad_gain_mix = jnp.sum(grad_normed_mix * mixed_in * inv_rms, axis=0)
    inner_dot = tensor_total(jnp.sum(scaled_grad * mixed_in, axis=1))
    grad_mixed = inv_rms * scaled_grad - mixed_in * inv_rms**3 * (inner_dot / INNER)[:, None]
    (
        grad_gate_raw,
        grad_signal_raw,
        grad_step_raw,
        grad_pair_raw,
        grad_taps_inner,
        grad_taps_shared,
        grad_decay,
        grad_bias,
        grad_skip,
    ) = mixer_back(grad_mixed)
    gate_low = grad_gate_raw.astype(bf16)
    signal_low = grad_signal_raw.astype(bf16)
    step_low = grad_step_raw.astype(bf16)
    grad_gate_w = left_contract(group_one, gate_low)
    grad_signal_w = left_contract(group_one, signal_low)
    grad_step = left_contract(group_one, step_low)
    kv_grad = jnp.zeros((group_rows, 2 * kv_cols), f32)
    kv_grad = lax.dynamic_update_slice_in_dim(kv_grad, grad_key_raw, kv_head * HEAD_SIZE, 1)
    kv_grad = lax.dynamic_update_slice_in_dim(
        kv_grad, grad_value_raw, kv_cols + kv_head * HEAD_SIZE, 1
    )
    shared_low = jnp.concatenate([kv_grad, grad_pair_raw], axis=1).astype(bf16)
    grad_shared = left_contract(group_one, shared_low)
    part_one = (
        part_one
        + right_contract(gate_low, full_inner[0])
        + right_contract(signal_low, full_inner[1])
        + right_contract(step_low, full_step)
        + right_contract(shared_low, full_shared)
    )
    grad_normed_one = chain_scatter(part_one.astype(bf16).reshape(nt, local_rows, width), nt)
    _, norm_one_back = jax.vjp(norm_apply, token_f32, gain_first)
    grad_from_one, grad_gain_one = norm_one_back(grad_normed_one)
    gradient_tokens = (grad_resid + grad_from_one).astype(bf16)

    block = width // nd

    def by_rows(values):
        c = values.shape[1]
        values = values.astype(bf16).reshape(nd, block, c // 128, 128)
        return values.transpose(0, 2, 1, 3).reshape(nd, -1, 128)

    def by_lanes(values):
        r = values.shape[0]
        values = values.astype(bf16).reshape(r, nd, block).transpose(1, 0, 2)
        return values.reshape(nd, r * block // 128, 128)

    step_wide = jnp.pad(grad_step, ((0, 0), (0, 128 - local_heads)))
    pieces = [
        by_rows(grad_query),
        by_lanes(grad_attend),
        by_rows(grad_gate_w),
        by_rows(grad_signal_w),
        by_rows(step_wide),
        by_lanes(grad_mamba),
    ]
    sizes = [p.shape[1] for p in pieces]
    mixer_sum = cube_scatter(jnp.concatenate(pieces, axis=1), nd)
    cuts = [sum(sizes[:i]) for i in range(len(sizes) + 1)]
    got = [mixer_sum[cuts[i] : cuts[i + 1]] for i in range(len(sizes))]

    def back_rows(values):
        return values.reshape(-1, block, 128).transpose(1, 0, 2).reshape(block, -1)

    gradient_query = back_rows(got[0])
    gradient_attend = got[1].reshape(-1, block)
    gradient_inner = jnp.stack([back_rows(got[2]), back_rows(got[3])])
    gradient_step = back_rows(got[4])[:, :local_heads]
    gradient_mamba = got[5].reshape(-1, block)
    shared_cut = grad_shared.astype(bf16).reshape(nd, nt, -1, grad_shared.shape[1])
    gradient_shared = chain_scatter(cube_scatter(shared_cut, nd, bf16), nt)

    over_all = jnp.concatenate([grad_gain_one, grad_gain_two, grad_taps_shared.reshape(-1)])
    over_dp = jnp.concatenate(
        [grad_taps_inner.reshape(-1), grad_gain_mix, grad_decay, grad_bias, grad_skip]
    )
    n_all = over_all.shape[0]
    over_dp = lax.psum(jnp.concatenate([over_all, over_dp]), "dp")
    over_all = lax.psum(over_dp[:n_all], "tensor")
    over_dp = over_dp[n_all:]
    d = lax.axis_index("dp")
    place = d * nt + tensor_index
    norm_w = width // (nd * nt)
    gradient_norms = lax.dynamic_slice_in_dim(
        over_all[: 2 * width].reshape(2, width), place * norm_w, norm_w, 1
    )
    tap_all = over_all[2 * width :].reshape(CONV + 1, -1)
    tap_w = shared_taps.shape[1]
    gradient_taps = lax.dynamic_slice_in_dim(tap_all, place * tap_w, tap_w, 1)
    n_taps = (CONV + 1) * local_heads * SSM_DIM
    n_gain = local_heads * SSM_DIM
    chan = over_dp[:n_taps].reshape(CONV + 1, local_heads, SSM_DIM)
    gain = over_dp[n_taps : n_taps + n_gain].reshape(local_heads, SSM_DIM)
    part = mixer_gain.shape[1]
    gradient_channel = lax.dynamic_slice_in_dim(chan, d * part, part, 2)
    gradient_mixer = lax.dynamic_slice_in_dim(gain, d * part, part, 1)
    rest = over_dp[n_taps + n_gain :]
    gradient_decay = rest[:local_heads]
    gradient_bias = rest[local_heads : 2 * local_heads]
    gradient_skip = rest[2 * local_heads :]
    return (
        layer_out,
        gradient_tokens,
        gradient_query,
        gradient_attend,
        gradient_inner,
        gradient_step,
        gradient_mamba,
        gradient_hidden,
        gradient_down,
        gradient_channel,
        gradient_mixer,
        gradient_decay,
        gradient_bias,
        gradient_skip,
        gradient_shared,
        gradient_norms,
        gradient_taps,
    )


def solution(mesh):
    placed = (
        P(("dp", "tensor"), None),
        P("dp", "tensor"),
        P("tensor", "dp"),
        P(None, "dp", "tensor"),
        P("dp", "tensor"),
        P("tensor", "dp"),
        P(None, "dp", "tensor"),
        P("tensor", "dp"),
        P(None, "tensor", "dp"),
        P("tensor", "dp"),
        P("tensor"),
        P("tensor"),
        P("tensor"),
        P(("dp", "tensor"), None),
        P(None, ("dp", "tensor")),
        P(None, ("dp", "tensor")),
        P(("dp", "tensor"), None),
    )
    return jax.shard_map(
        partial(per_device, mesh.shape["dp"], mesh.shape["tensor"]),
        mesh=mesh,
        in_specs=placed,
        out_specs=(
            P(("dp", "tensor"), None),
            P(("dp", "tensor"), None),
            P("dp", "tensor"),
            P("tensor", "dp"),
            P(None, "dp", "tensor"),
            P("dp", "tensor"),
            P("tensor", "dp"),
            P(None, "dp", "tensor"),
            P("tensor", "dp"),
            P(None, "tensor", "dp"),
            P("tensor", "dp"),
            P("tensor"),
            P("tensor"),
            P("tensor"),
            P(("dp", "tensor"), None),
            P(None, ("dp", "tensor")),
            P(None, ("dp", "tensor")),
        ),
        check_vma=False,
    )
```

```python
from functools import partial

import numpy as np
import jax
import jax.numpy as jnp
from jax import lax
from jax.experimental import pallas as pl
from jax.experimental.pallas import tpu as pltpu
from jax.sharding import PartitionSpec as P

MESH = pl.DeviceIdType.MESH

QHEADS = 8
KVHEADS = 2
HEAD_SIZE = 64
SSM_DIM = 64
CONV = 4


epsilon = 1e-05
rope_base = 100000000000.0
neg_large = -1e30
block_len = 128


def norm_apply(values, gain):
    factor = lax.rsqrt(jnp.mean(values * values, axis=-1, keepdims=True) + epsilon)
    return values * factor * gain


def dp_bits(index):
    core = lax.rem(index, 2)
    xbit = lax.rem(index // 2, 2)
    ybit = lax.rem(index // 4, 2)
    return core, xbit, ybit


def gather_kernel(nt, *refs):
    (tok, que, att, inn, mam, sha, sma) = refs[:7]
    (tok_f, que_f, att_f, inn_f, mam_f, sha_f, sma_f) = refs[7:14]
    (lsem, zs_send, zs_recv, t_send, t_recv, d_send, d_recv) = refs[14:]
    d = lax.axis_index("dp")
    z = lax.axis_index("tensor")
    core, xbit, ybit = dp_bits(d)
    d_core = d + 1 - 2 * core
    d_x = d + 2 - 4 * xbit
    d_y = d + 4 - 8 * ybit
    d_xy = d_x + 4 - 8 * ybit

    barrier = pltpu.get_barrier_semaphore()
    for peer in (d_core, d_x, d_y):
        pl.semaphore_signal(barrier, inc=1, device_id=(peer, z), device_id_type=MESH)
    for k in range(1, nt):
        pl.semaphore_signal(
            barrier, inc=1, device_id=(d, lax.rem(z + k, nt)), device_id_type=MESH
        )
    pl.semaphore_wait(barrier, 3 + nt - 1)

    def remote(src, dst, send, recv, dev):
        return pltpu.make_async_remote_copy(
            src_ref=src, dst_ref=dst, send_sem=send, recv_sem=recv,
            device_id=dev, device_id_type=MESH,
        )

    small = []
    for i, (src, dst) in enumerate(((sha, sha_f), (sma, sma_f))):
        for k in range(1, nt):
            copy = remote(
                src, dst.at[d, z], zs_send.at[i, k], zs_recv.at[i, k],
                (d, lax.rem(z + k, nt)),
            )
            copy.start()
            small.append(copy)
    q_rows = que.shape[0]
    cols = att.shape[1]
    i_rows = inn.shape[1]
    items = (
        (inn, lambda s: inn_f.at[:, pl.ds(s * i_rows, i_rows)]),
        (que, lambda s: que_f.at[pl.ds(s * q_rows, q_rows)]),
        (att, lambda s: att_f.at[:, pl.ds(pl.multiple_of(s * cols, cols), cols)]),
        (mam, lambda s: mam_f.at[:, pl.ds(pl.multiple_of(s * cols, cols), cols)]),
    )
    locals_ = []
    for i, (src, dst) in enumerate(
        [(tok, tok_f.at[z]), (sha, sha_f.at[d, z]), (sma, sma_f.at[d, z])]
        + [(src, at(d)) for src, at in items]
    ):
        copy = pltpu.make_async_copy(src, dst, lsem.at[i])
        copy.start()
        locals_.append(copy)
    sent = []

    def stage_one(i, src, at):
        for j, peer in enumerate((d_x, d_y, d_core)):
            copy = remote(src, at(d), d_send.at[i, j], d_recv.at[i, j], (peer, z))
            copy.start()
            sent.append(copy)

    for i, (src, at) in enumerate(items):
        stage_one(i, src, at)

    def tok_copy(slot, dirn, hop):
        dev = z + 1 if dirn == 0 else z - 1
        return remote(
            tok_f.at[slot], tok_f.at[slot], t_send.at[dirn, hop], t_recv.at[dirn, hop], (d, dev)
        )

    def own_copy(dirn):
        dev = z + 1 if dirn == 0 else z - 1
        return remote(tok, tok_f.at[z], t_send.at[dirn, 0], t_recv.at[dirn, 0], (d, dev))

    pl.when(z < nt - 1)(lambda: own_copy(0).start())
    pl.when(z > 0)(lambda: own_copy(1).start())

    locals_[1].wait()
    locals_[2].wait()
    for copy in small:
        copy.wait()
    n = len(items)
    shared_items = (
        (sha_f.at[d], lambda s: sha_f.at[s]),
        (sma_f.at[d], lambda s: sma_f.at[s]),
    )
    for i, (src, at) in enumerate(shared_items):
        stage_one(n + i, src, at)

    def wait_recv(i, j, at, slot):
        remote(at(slot), at(slot), d_send.at[i, j], d_recv.at[i, j], (d_core, z)).wait_recv()

    def forward(i, j, at, slot, peer):
        copy = remote(at(slot), at(slot), d_send.at[i, j], d_recv.at[i, j], (peer, z))
        copy.start()
        sent.append(copy)

    everything = [at for _, at in items] + [at for _, at in shared_items]
    via_y = (0, n + 1)

    def diagonal(i, at):
        wait_recv(i, 0, at, d_x)
        if i in via_y:
            forward(i, 3, at, d_x, d_y)
        forward(i, 4, at, d_x, d_core)
        wait_recv(i, 1, at, d_y)
        if i not in via_y:
            forward(i, 3, at, d_y, d_x)
        forward(i, 5, at, d_y, d_core)

    for i in range(n):
        diagonal(i, everything[i])

    def hop(dist):
        def from_left():
            tok_copy(z - dist, 0, dist - 1).wait_recv()

        def from_right():
            tok_copy(z + dist, 1, dist - 1).wait_recv()

        pl.when(z >= dist)(from_left)
        if dist < nt - 1:
            pl.when((z >= dist) & (z < nt - 1))(lambda: tok_copy(z - dist, 0, dist).start())
        pl.when(z + dist < nt)(from_right)
        if dist < nt - 1:
            pl.when((z + dist < nt) & (z > 0))(lambda: tok_copy(z + dist, 1, dist).start())

    hop(1)
    for i in range(n, n + 2):
        diagonal(i, everything[i])
    for i, at in enumerate(everything):
        wait_recv(i, 3, at, d_xy)
        forward(i, 6, at, d_xy, d_core)
    for dist in range(2, nt):
        hop(dist)
    for i, at in enumerate(everything):
        wait_recv(i, 2, at, d_core)
        for j in (4, 5, 6):
            wait_recv(i, j, at, d_core)
    for i, copy in enumerate(locals_):
        if i not in (1, 2):
            copy.wait()
    for copy in sent:
        copy.wait_send()
    pl.when(z < nt - 1)(lambda: own_copy(0).wait_send())
    pl.when(z > 0)(lambda: own_copy(1).wait_send())
    for dist in range(1, nt - 1):
        pl.when((z >= dist) & (z < nt - 1))(lambda: tok_copy(z - dist, 0, dist).wait_send())
        pl.when((z + dist < nt) & (z > 0))(lambda: tok_copy(z + dist, 1, dist).wait_send())


def gather_start(tok, que, att, inn, mam, sha, sma, nd, nt):
    if nd != 8:
        shared = lax.all_gather(sha, ("dp", "tensor"), axis=0)
        small = lax.all_gather(sma, ("dp", "tensor"), axis=0)
        return (
            lax.all_gather(tok, "tensor", axis=0),
            lax.all_gather(que, "dp", axis=0, tiled=True),
            lax.all_gather(att, "dp", axis=1, tiled=True),
            lax.all_gather(inn, "dp", axis=1, tiled=True),
            lax.all_gather(mam, "dp", axis=1, tiled=True),
            shared.reshape((nd, nt) + sha.shape),
            small.reshape((nd, nt) + sma.shape),
        )
    bf = jnp.bfloat16
    outs = (
        (nt,) + tok.shape,
        (nd * que.shape[0], que.shape[1]),
        (att.shape[0], nd * att.shape[1]),
        (2, nd * inn.shape[1], inn.shape[2]),
        (mam.shape[0], nd * mam.shape[1]),
        (nd, nt) + sha.shape,
        (nd, nt) + sma.shape,
    )
    anywhere = pl.BlockSpec(memory_space=pl.ANY)
    dma = pltpu.SemaphoreType.DMA
    return pl.pallas_call(
        partial(gather_kernel, nt),
        out_shape=[jax.ShapeDtypeStruct(s, bf) for s in outs],
        in_specs=[anywhere] * 7,
        out_specs=[anywhere] * 7,
        scratch_shapes=[
            dma((7,)), dma((2, nt)), dma((2, nt)), dma((2, nt)), dma((2, nt)),
            dma((6, 7)), dma((6, 7)),
        ],
        compiler_params=pltpu.CompilerParams(collective_id=0, has_side_effects=True),
        name="gather_start",
    )(tok, que, att, inn, mam, sha, sma)


def pick(values, index, axis=0):
    return lax.dynamic_index_in_dim(values, index, axis, keepdims=False)


def add_low(left, right):
    return (left.astype(jnp.float32) + right.astype(jnp.float32)).astype(jnp.bfloat16)


def chain_gather(values, nt):
    z = lax.axis_index("tensor")
    out = jnp.zeros((nt,) + values.shape, values.dtype)
    out = lax.dynamic_update_index_in_dim(out, values, z, 0)
    right = left = values
    for dist in range(1, nt):
        right = lax.ppermute(right, "tensor", [(i, i + 1) for i in range(dist - 1, nt - 1)])
        left = lax.ppermute(left, "tensor", [(i, i - 1) for i in range(1, nt - dist + 1)])
        pieces = out
        pieces = jnp.where(
            z >= dist,
            lax.dynamic_update_index_in_dim(pieces, right, jnp.maximum(z - dist, 0), 0),
            pieces,
        )
        out = jnp.where(
            z + dist < nt,
            lax.dynamic_update_index_in_dim(pieces, left, jnp.minimum(z + dist, nt - 1), 0),
            pieces,
        )
    return out


def chain_scatter(parts, nt):
    z = lax.axis_index("tensor")
    right = left = None
    for t in range(nt - 1):
        to_right = pick(parts, jnp.clip(nt - 1 - t + z, 0, nt - 1))
        to_left = pick(parts, jnp.clip(t - (nt - 1) + z, 0, nt - 1))
        if t > 0:
            to_right = add_low(to_right, right)
            to_left = add_low(to_left, left)
        right = lax.ppermute(to_right, "tensor", [(i, i + 1) for i in range(t + 1)])
        left = lax.ppermute(
            to_left, "tensor", [(nt - 1 - i, nt - 2 - i) for i in range(t + 1)]
        )
    f32 = jnp.float32
    return pick(parts, z).astype(f32) + right.astype(f32) + left.astype(f32)


def cube_scatter(parts, nd, last=jnp.float32):
    if nd != 8:
        return lax.psum_scatter(parts, "dp", scatter_dimension=0, tiled=False).astype(last)
    d = lax.axis_index("dp")
    core, xbit, ybit = dp_bits(d)

    def swap(values, bit):
        return lax.ppermute(values, "dp", [(i, i ^ bit) for i in range(8)])

    tail = parts.shape[1:]
    cut = parts.reshape((4, 2) + tail)
    held = add_low(pick(cut, core, 1), swap(pick(cut, 1 - core, 1), 1))
    held = held.reshape((2, 2) + tail)
    half = tail[0] // 2
    one, two = held[:, :, :half], held[:, :, half:]
    one_b = add_low(pick(one, xbit, 1), swap(pick(one, 1 - xbit, 1), 2))
    two_b = add_low(pick(two, ybit, 0), swap(pick(two, 1 - ybit, 0), 4))
    f32 = jnp.float32
    one_c = pick(one_b, ybit).astype(f32) + swap(pick(one_b, 1 - ybit), 4).astype(f32)
    two_c = pick(two_b, xbit).astype(f32) + swap(pick(two_b, 1 - xbit), 2).astype(f32)
    return jnp.concatenate([one_c, two_c], axis=0).astype(last)


def tensor_total(values):
    return lax.psum(values, "tensor")


F32, BF16 = jnp.float32, jnp.bfloat16
VMEM_LIMIT = 56 * 1024 * 1024


def dot_nn(a, b):
    return lax.dot_general(a, b, (((1,), (0,)), ((), ())), preferred_element_type=F32)


def dot_nt(a, b):
    return lax.dot_general(a, b, (((1,), (1,)), ((), ())), preferred_element_type=F32)


def dot_tn(a, b):
    return lax.dot_general(a, b, (((0,), (0,)), ((), ())), preferred_element_type=F32)


def sigmoid(v):
    return 1.0 / (1.0 + jnp.exp(-v))


def lanes_of(shape):
    return lax.broadcasted_iota(jnp.int32, shape, len(shape) - 1)


def turn(values, cosine, sine):
    lane = lanes_of(values.shape)
    other = jnp.where(
        lax.rem(lane, HEAD_SIZE) < HEAD_SIZE // 2,
        pltpu.roll(values, 128 - HEAD_SIZE // 2, 1),
        pltpu.roll(values, HEAD_SIZE // 2, 1),
    )
    return values * cosine + other * sine


def softplus(v):
    return jnp.maximum(v, 0.0) + jnp.log1p(jnp.exp(-jnp.abs(v)))


def running_sum(rows):
    lane = lanes_of(rows.shape)
    step = 1
    while step < rows.shape[1]:
        rows = rows + jnp.where(lane >= step, pltpu.roll(rows, step, 1), 0.0)
        step *= 2
    return rows


def running_sum_back(rows):
    lane = lanes_of(rows.shape)
    width = rows.shape[1]
    step = 1
    while step < width:
        rows = rows + jnp.where(lane < width - step, pltpu.roll(rows, width - step, 1), 0.0)
        step *= 2
    return rows


def stack_columns(rows_list):
    used = sum(r.shape[0] for r in rows_list)
    filler = jnp.zeros((128 - used, 128), F32)
    return jnp.concatenate(rows_list + [filler], axis=0).T


def widen(cols, base, heads):
    low = lanes_of((cols.shape[0], 128)) < SSM_DIM
    return jnp.concatenate(
        [
            jnp.where(low, cols[:, base + 2 * p : base + 2 * p + 1],
                      cols[:, base + 2 * p + 1 : base + 2 * p + 2])
            for p in range(heads // 2)
        ],
        axis=1,
    )


def conv_rows(ref, taps, first, rows):
    total = taps[CONV : CONV + 1, :] + taps[0:1, :] * ref[pl.ds(first, rows), :]
    for j in range(1, CONV):
        total = total + taps[j : j + 1, :] * ref[pl.ds(first + j, rows), :]
    return total


def forward_kernel(
    heads, kvh, tok, gain, wq, win, stp, wsh, cosine, sine, tapx, tapb, decay, bias, skip,
    a1_o, q_o, k_o, v_o, lse_o, o_o, x_o, z_o, b_o, y_o, t_o, s_o, sq_o,
    keys, vals, xs, bs, state,
):
    step = pl.program_id(0)
    rows = tok.shape[0]
    second = kvh[0] == 1

    @pl.when(step == 0)
    def _():
        xs[0:8, :] = jnp.zeros((8, xs.shape[1]), F32)
        bs[0:8, :] = jnp.zeros((8, bs.shape[1]), F32)
        state[...] = jnp.zeros(state.shape, F32)

    t = tok[...].astype(F32)
    r = lax.rsqrt(jnp.mean(t * t, axis=1, keepdims=True) + epsilon)
    a1 = (t * r * gain[...]).astype(BF16)
    a1_o[...] = a1
    q = turn(dot_nn(a1, wq[...]), cosine[...], sine[...]).astype(BF16)
    q_o[...] = q
    s = dot_nn(a1, wsh[...])
    low = lanes_of((rows, 128)) < HEAD_SIZE
    k = turn(s[:, :128], cosine[...], sine[...])
    v = s[:, 128:256]
    pick_own = low != second
    k2 = jnp.where(pick_own, k, pltpu.roll(k, 64, 1)).astype(BF16)
    v2 = jnp.where(pick_own, v, pltpu.roll(v, 64, 1))
    k_o[...] = k2
    v_o[...] = v2.astype(BF16)
    place = pl.ds(pl.multiple_of(step * rows, rows), rows)
    keys[place, :] = k2
    vals[:, place] = v2.T.astype(BF16)

    scale = HEAD_SIZE**-0.5

    def attend(blocks):
        n = blocks * rows
        shape = (rows, rows)
        allowed = lax.broadcasted_iota(jnp.int32, shape, 0) <= lanes_of(shape)
        parts = []
        for h in range(2):
            qh = jnp.where(low == (h == 0), q, jnp.zeros_like(q))
            sc = dot_nt(keys[0:n, :], qh) * scale
            last = jnp.where(allowed, sc[n - rows :, :], neg_large)
            sc = jnp.concatenate([sc[: n - rows, :], last], axis=0) if blocks > 1 else last
            top = jnp.max(sc, axis=0, keepdims=True)
            e = jnp.exp(sc - top)
            total = jnp.sum(e, axis=0, keepdims=True)
            lse_o[h : h + 1, :] = top + jnp.log(total)
            parts.append(dot_nn(vals[:, 0:n], e.astype(BF16)) / total)
        sub = lax.broadcasted_iota(jnp.int32, parts[0].shape, 0)
        o_o[...] = jnp.where(sub < HEAD_SIZE, parts[0], parts[1]).T.astype(BF16)

    for i in range(keys.shape[0] // rows):
        pl.when(step == i)(partial(attend, i + 1))

    zr = dot_nn(a1, win[0])
    z_o[...] = zr
    xr = dot_nn(a1, win[1])
    x_o[...] = xr
    br = s[:, 256:]
    b_o[...] = br
    xs[8 : 8 + rows, :] = xr
    bs[8 : 8 + rows, :] = br
    u = conv_rows(xs, tapx, 5, rows)
    x = u * sigmoid(u)
    u = conv_rows(bs, tapb, 5, rows)
    bc = (u * sigmoid(u)).astype(BF16)
    xs[0:8, :] = xs[rows : rows + 8, :]
    bs[0:8, :] = bs[rows : rows + 8, :]
    tr = dot_nt(stp[...], a1)
    t_o[...] = tr
    n_state = bc.shape[1] // 2
    tri_shape = (block_len, block_len)
    lower = lax.broadcasted_iota(jnp.int32, tri_shape, 0) >= lanes_of(tri_shape)
    half = lanes_of(tri_shape) < SSM_DIM
    for c in range(rows // block_len):
        part = slice(c * block_len, (c + 1) * block_len)
        dt = softplus(tr[:, part] + bias[...])
        cum = running_sum(dt * decay[...])
        end = cum[:, block_len - 1 :]
        cols = stack_columns([cum, jnp.exp(cum), dt * jnp.exp(end - cum)])
        xc = x[part]
        x_low = xc.astype(BF16)
        b_low = bc[part, :n_state]
        c_low = bc[part, n_state:]
        cross = dot_nt(c_low, b_low)
        grow = widen(cols, 8, heads)
        y = dot_nn(c_low, state[...].astype(BF16)) * grow + skip[...] * xc
        inner = []
        for p in range(heads // 2):
            mats = []
            for h in (2 * p, 2 * p + 1):
                gap = jnp.where(lower, cols[:, h : h + 1] - cum[h : h + 1, :], neg_large)
                mats.append((cross * jnp.exp(gap) * dt[h : h + 1, :]).astype(BF16))
            xp = x_low[:, 128 * p : 128 * p + 128]
            zero = jnp.zeros_like(xp)
            both = jnp.concatenate([jnp.where(half, xp, zero), jnp.where(half, zero, xp)], axis=0)
            inner.append(dot_nn(jnp.concatenate(mats, axis=1), both))
        y = y + jnp.concatenate(inner, axis=1)
        y_o[part, :] = y
        s_o[c] = state[...]
        carried = (xc * widen(cols, 16, heads)).astype(BF16)
        state[...] = grow[block_len - 1 :, :] * state[...] + dot_tn(b_low, carried)
        zc = zr[part]
        w = y * (zc * sigmoid(zc))
        total = jnp.sum(w * w, axis=1, keepdims=True)
        sq_o[:, part] = jnp.broadcast_to(total, (block_len, 128)).T[0:8, :]


def mixers_forward(heads, kvh, tok, gain, wq, win, stp, wsh, cosine, sine, tapx, tapb, decay, bias, skip):
    total, width = tok.shape
    rows = 256
    inner = heads * SSM_DIM
    pair = wsh.shape[1] - 256
    state = pair // 2
    chunks = rows // block_len

    def whole(v):
        return pl.BlockSpec(v.shape, lambda i: (0,) * v.ndim)

    def tall(n):
        return pl.BlockSpec((rows, n), lambda i: (i, 0))

    wide = pl.BlockSpec((8, rows), lambda i: (0, i))
    sds = jax.ShapeDtypeStruct
    return pl.pallas_call(
        partial(forward_kernel, heads),
        grid=(total // rows,),
        in_specs=[pl.BlockSpec(memory_space=pltpu.SMEM), tall(width), whole(gain), whole(wq), whole(win),
                  whole(stp), whole(wsh), tall(128), tall(128), whole(tapx), whole(tapb),
                  whole(decay), whole(bias), whole(skip)],
        out_specs=[tall(width), tall(128), tall(128), tall(128), wide, tall(128), tall(inner),
                   tall(inner), tall(pair), tall(inner), wide,
                   pl.BlockSpec((chunks, state, inner), lambda i: (i, 0, 0)), wide],
        out_shape=[sds((total, width), BF16), sds((total, 128), BF16), sds((total, 128), BF16),
                   sds((total, 128), BF16), sds((8, total), F32), sds((total, 128), BF16),
                   sds((total, inner), F32), sds((total, inner), F32), sds((total, pair), F32),
                   sds((total, inner), F32), sds((8, total), F32),
                   sds((total // block_len, state, inner), F32), sds((8, total), F32)],
        scratch_shapes=[pltpu.VMEM((total, 128), BF16), pltpu.VMEM((128, total), BF16),
                        pltpu.VMEM((rows + 8, inner), F32), pltpu.VMEM((rows + 8, pair), F32),
                        pltpu.VMEM((state, inner), F32)],
        compiler_params=pltpu.CompilerParams(vmem_limit_bytes=VMEM_LIMIT),
        cost_estimate=pl.CostEstimate(flops=int(5e9), bytes_accessed=int(15e6), transcendentals=int(4e6)),
        name="mixers_forward",
    )(kvh, tok, gain, wq, win, stp, wsh, cosine, sine, tapx, tapb, decay, bias, skip)


def attend_back_kernel(kvh, q, k2, v2, lse, do, cosine, sine, cos_all, sin_all, dq_o, dkv_o, dk, dv):
    step = pl.program_id(0)
    rows = q.shape[0]
    steps = k2.shape[0] // rows
    scale = HEAD_SIZE**-0.5
    low = lanes_of((rows, 128)) < HEAD_SIZE

    @pl.when(step == 0)
    def _():
        dk[...] = jnp.zeros(dk.shape, F32)
        dv[...] = jnp.zeros(dv.shape, F32)

    def back(blocks):
        n = blocks * rows
        shape = (rows, rows)
        allowed = lax.broadcasted_iota(jnp.int32, shape, 0) <= lanes_of(shape)
        qs, dos, ps, dss, dqs = [], [], [], [], []
        for h in range(2):
            mine = low == (h == 0)
            qh = jnp.where(mine, q[...], jnp.zeros_like(q[...]))
            doh = jnp.where(mine, do[...], jnp.zeros_like(do[...]))
            sc = dot_nt(k2[0:n, :], qh) * scale - lse[h : h + 1, :]
            last = jnp.where(allowed, sc[n - rows :, :], neg_large)
            sc = jnp.concatenate([sc[: n - rows, :], last], axis=0) if blocks > 1 else last
            p = jnp.exp(sc)
            dp = dot_nt(v2[0:n, :], doh)
            centre = jnp.sum(p * dp, axis=0, keepdims=True)
            ds = (p * (dp - centre)).astype(BF16)
            qs.append(qh)
            dos.append(doh)
            ps.append(p.astype(BF16))
            dss.append(ds)
            dqs.append(dot_tn(ds, k2[0:n, :]) * scale)
        dk[0:n, :] += dot_nn(jnp.concatenate(dss, axis=1), jnp.concatenate(qs, axis=0)) * scale
        dv[0:n, :] += dot_nn(jnp.concatenate(ps, axis=1), jnp.concatenate(dos, axis=0))
        dq_o[...] = turn(jnp.where(low, dqs[0], dqs[1]), cosine[...], -sine[...]).astype(BF16)

    for i in range(steps):
        pl.when(step == i)(partial(back, i + 1))

    @pl.when(step == steps - 1)
    def _():
        own = (lanes_of(dk.shape) < HEAD_SIZE) != (kvh[0] == 1)
        g = dk[...]
        g = turn(g + pltpu.roll(g, 64, 1), cos_all[...], -sin_all[...])
        dkv_o[:, 0:128] = jnp.where(own, g, 0.0).astype(BF16)
        g = dv[...]
        g = g + pltpu.roll(g, 64, 1)
        dkv_o[:, 128:256] = jnp.where(own, g, 0.0).astype(BF16)


def attend_back(kvh, q, k2, v2, lse, do, cosine, sine):
    total = q.shape[0]
    rows = 256

    def whole(v):
        return pl.BlockSpec(v.shape, lambda i: (0,) * v.ndim)

    tall = pl.BlockSpec((rows, 128), lambda i: (i, 0))
    wide = pl.BlockSpec((8, rows), lambda i: (0, i))
    sds = jax.ShapeDtypeStruct
    return pl.pallas_call(
        attend_back_kernel,
        grid=(total // rows,),
        in_specs=[pl.BlockSpec(memory_space=pltpu.SMEM), tall, whole(k2), whole(v2), wide, tall, tall, tall,
                  whole(cosine), whole(sine)],
        out_specs=[tall, pl.BlockSpec((total, 256), lambda i: (0, 0))],
        out_shape=[sds((total, 128), BF16), sds((total, 256), BF16)],
        scratch_shapes=[pltpu.VMEM((total, 128), F32), pltpu.VMEM((total, 128), F32)],
        compiler_params=pltpu.CompilerParams(vmem_limit_bytes=VMEM_LIMIT),
        cost_estimate=pl.CostEstimate(flops=int(2e9), bytes_accessed=int(3e6), transcendentals=int(2e6)),
        name="attend_back",
    )(kvh, q, k2, v2, lse, do, cosine, sine, cosine, sine)


def scan_back_kernel(
    heads, channels, dm, y, zr, xr, xp, br, bp, trow, states, rsum, dots, gain, tapx, tapb, decay,
    bias, skip,
    dz_o, dx_o, db_o, dt_o, gx_o, gb_o, gm_o, gh_o,
    xs, bs, dxs, dbs, dstate,
):
    step = pl.program_id(0)
    last_step = pl.num_programs(0) - 1
    first = step == last_step
    rows = block_len
    inner = heads * SSM_DIM
    n_state = br.shape[1] // 2

    @pl.when(step == 0)
    def _():
        dxs[rows : rows + 8, :] = jnp.zeros((8, inner), F32)
        dbs[rows : rows + 8, :] = jnp.zeros((8, 2 * n_state), F32)
        dstate[...] = jnp.zeros(dstate.shape, F32)
        gx_o[...] = jnp.zeros(gx_o.shape, F32)
        gb_o[...] = jnp.zeros(gb_o.shape, F32)
        gm_o[...] = jnp.zeros(gm_o.shape, F32)
        gh_o[...] = jnp.zeros(gh_o.shape, F32)

    xs[0:8, :] = jnp.where(first, 0.0, xp[...])
    bs[0:8, :] = jnp.where(first, 0.0, bp[...])
    xs[8 : 8 + rows, :] = xr[...]
    bs[8 : 8 + rows, :] = br[...]
    ux = conv_rows(xs, tapx, 5, rows)
    sx = sigmoid(ux)
    x = ux * sx
    ub = conv_rows(bs, tapb, 5, rows)
    sb = sigmoid(ub)
    bc = (ub * sb).astype(BF16)
    b_low, c_low = bc[:, :n_state], bc[:, n_state:]

    pre = trow[...] + bias[...]
    dt = softplus(pre)
    cum = running_sum(dt * decay[...])
    end = cum[:, rows - 1 :]
    fade = jnp.exp(end - cum)
    inv = lax.rsqrt(rsum[...] / channels + epsilon)
    cols = stack_columns(
        [cum, jnp.exp(cum), dt * fade, dt, inv, inv * inv * inv * dots[...] / channels]
    )
    r = cols[:, 32:33]
    kk = cols[:, 40:41]
    z = zr[...]
    sz = sigmoid(z)
    silu_z = z * sz
    yv = y[...]
    w = yv * silu_z
    dmv = dm[...]
    dw = r * gain[...] * dmv - w * kk
    gm_o[0:1, :] += jnp.sum(dmv * w * r, axis=0, keepdims=True)
    dy = dw * silu_z
    dz_o[...] = (dw * yv * sz * (1.0 + z * (1.0 - sz))).astype(BF16)
    gm_o[1:2, :] += jnp.sum(dy * x, axis=0, keepdims=True)

    grow = widen(cols, 8, heads)
    tail = widen(cols, 16, heads)
    dt_wide = widen(cols, 24, heads)
    x_low = x.astype(BF16)
    dy_low = dy.astype(BF16)
    state = states[0]
    state_low = state.astype(BF16)
    ds = dstate[...]
    ds_low = ds.astype(BF16)
    cross = dot_nt(b_low, c_low)
    shape = (rows, rows)
    upper = lax.broadcasted_iota(jnp.int32, shape, 0) <= lanes_of(shape)
    half = lanes_of(shape) < SSM_DIM
    lane = lanes_of(shape)
    dcross = jnp.zeros(shape, F32)
    col_sums = jnp.zeros(shape, F32)
    row_sums = []
    mids = []
    for p in range(heads // 2):
        span = slice(128 * p, 128 * p + 128)
        xpair, dypair = x_low[:, span], dy_low[:, span]
        zero = jnp.zeros_like(xpair)
        dys = (jnp.where(half, dypair, zero), jnp.where(half, zero, dypair))
        mats = []
        for k in range(2):
            h = 2 * p + k
            gap = jnp.where(upper, cum[h : h + 1, :] - cols[:, h : h + 1], neg_large)
            faded = jnp.exp(gap)
            mats.append((cross * faded).astype(BF16))
            t = dot_nt(xpair, dys[k]) * faded
            dt_col = cols[:, 24 + h : 25 + h]
            td = t * dt_col
            dcross = dcross + td
            row_sums.append(jnp.sum(td * cross, axis=0, keepdims=True))
            col = jnp.sum(t * cross, axis=1, keepdims=True)
            col_sums = jnp.where(lane == h, col, col_sums)
        mids.append(dot_nn(jnp.concatenate(mats, axis=1), jnp.concatenate(dys, axis=0)))
    mid = jnp.concatenate(mids, axis=1)
    row_sums = jnp.concatenate(row_sums + [jnp.zeros((8 - heads, rows), F32)], axis=0)
    col_sums = col_sums.T[0:8, :]

    dye = dy * grow
    dye_low = dye.astype(BF16)
    xd = x * tail
    xd_low = xd.astype(BF16)
    from_b = dot_nn(b_low, ds_low)
    through = dot_nn(c_low, state_low)
    dcross_low = dcross.astype(BF16)
    db = dot_nn(dcross_low, c_low) + dot_nt(xd_low, ds_low)
    dc = dot_tn(dcross_low, b_low) + dot_nt(dye_low, state_low)

    head_of = lax.broadcasted_iota(jnp.int32, (8, inner), 0)
    chan = lanes_of((8, inner)) // SSM_DIM
    ones = jnp.where(head_of == chan, 1.0, 0.0).astype(BF16)

    def by_head(v):
        high = v.astype(BF16)
        rest = (v - high.astype(F32)).astype(BF16)
        return dot_nt(ones, high) + dot_nt(ones, rest)

    grown = by_head(dye * through)
    ended = by_head(x * from_b)
    kept = jnp.sum(ds * state, axis=0, keepdims=True) * grow[rows - 1 :, :]
    kept = jnp.where(head_of == chan, kept, 0.0).sum(axis=1, keepdims=True)
    pulled = dt * fade * ended
    lane8 = lanes_of((8, rows))
    at_end = kept + jnp.sum(pulled, axis=1, keepdims=True)
    dcum = row_sums - dt * col_sums + grown - pulled + jnp.where(lane8 == rows - 1, at_end, 0.0)
    da = running_sum_back(dcum)
    ddt = col_sums + fade * ended + decay[...] * da
    dpre = ddt * sigmoid(pre)
    dt_o[...] = dpre
    gh_o[0:8, :] += da * dt * decay[...]
    gh_o[8:16, :] += dpre

    dstate[...] = grow[rows - 1 :, :] * ds + dot_tn(c_low, dye_low)
    dx = skip[...] * dy + dt_wide * mid + tail * from_b
    dux = dx * sx * (1.0 + ux * (1.0 - sx))
    dub = jnp.concatenate([db, dc], axis=1) * sb * (1.0 + ub * (1.0 - sb))
    for taps, src, d, buf, acc, out in (
        (tapx, xs, dux, dxs, gx_o, dx_o),
        (tapb, bs, dub, dbs, gb_o, db_o),
    ):
        buf[0:rows, :] = d
        total = taps[CONV - 1 : CONV, :] * d
        for j in range(CONV - 1):
            total = total + taps[j : j + 1, :] * buf[pl.ds(CONV - 1 - j, rows), :]
        out[...] = total.astype(BF16)
        for j in range(CONV):
            acc[j : j + 1, :] += jnp.sum(d * src[pl.ds(5 + j, rows), :], axis=0, keepdims=True)
        acc[CONV : CONV + 1, :] += jnp.sum(d, axis=0, keepdims=True)
        buf[rows : rows + 8, :] = d[0:8, :]


def scan_back(heads, channels, dm, y, zr, xr, br, trow, states, rsum, dots, gain, tapx, tapb, decay, bias, skip):
    total, inner = y.shape
    pair = br.shape[1]
    rows = block_len
    steps = total // rows
    per = rows // 8

    def whole(v):
        return pl.BlockSpec(v.shape, lambda i: (0,) * v.ndim)

    def tall(n):
        return pl.BlockSpec((rows, n), lambda i: (steps - 1 - i, 0))

    def before(n):
        return pl.BlockSpec((8, n), lambda i: (jnp.maximum((steps - 1 - i) * per - 1, 0), 0))

    wide = pl.BlockSpec((8, rows), lambda i: (0, steps - 1 - i))
    sds = jax.ShapeDtypeStruct

    def fixed(*shape):
        return pl.BlockSpec(shape, lambda i: (0, 0))

    return pl.pallas_call(
        partial(scan_back_kernel, heads, channels),
        grid=(steps,),
        in_specs=[tall(inner), tall(inner), tall(inner), tall(inner), before(inner), tall(pair),
                  before(pair), wide,
                  pl.BlockSpec((1, pair // 2, inner), lambda i: (steps - 1 - i, 0, 0)), wide, wide,
                  whole(gain), whole(tapx), whole(tapb), whole(decay), whole(bias), whole(skip)],
        out_specs=[tall(inner), tall(inner), tall(pair), wide, fixed(8, inner), fixed(8, pair),
                   fixed(8, inner), fixed(16, rows)],
        out_shape=[sds((total, inner), BF16), sds((total, inner), BF16), sds((total, pair), BF16),
                   sds((8, total), F32), sds((8, inner), F32), sds((8, pair), F32),
                   sds((8, inner), F32), sds((16, rows), F32)],
        scratch_shapes=[pltpu.VMEM((rows + 8, inner), F32), pltpu.VMEM((rows + 8, pair), F32),
                        pltpu.VMEM((rows + 8, inner), F32), pltpu.VMEM((rows + 8, pair), F32),
                        pltpu.VMEM((pair // 2, inner), F32)],
        compiler_params=pltpu.CompilerParams(vmem_limit_bytes=VMEM_LIMIT),
        cost_estimate=pl.CostEstimate(flops=int(4e9), bytes_accessed=int(15e6), transcendentals=int(5e6)),
        name="scan_back",
    )(dm, y, zr, xr, xr, br, br, trow, states, rsum, dots, gain, tapx, tapb,
      decay, bias, skip)


def whole_spec(v):
    return pl.BlockSpec(v.shape, lambda i: (0,) * v.ndim)


def feed_kernel(
    hid, gain, cot, whid, wdown, out_o, dh_o, dmix_o, gg_o, ghid_o, gdown_o, a2, a2t, acc, dacc
):
    step = pl.program_id(0)
    width = hid.shape[1]
    blocks = width // 128

    @pl.when(step == 0)
    def _():
        v = hid[...]
        f = lax.rsqrt(jnp.mean(v * v, axis=1, keepdims=True) + epsilon)
        low = (v * f * gain[...]).astype(BF16)
        a2[...] = low
        a2t[...] = low.T
        acc[...] = jnp.zeros(acc.shape, F32)
        dacc[...] = jnp.zeros(dacc.shape, F32)

    units = whid.shape[4]
    w_gate = whid[:, 0, 0].reshape(width, units)
    w_up = whid[:, 0, 1].reshape(width, units)
    w_down = jnp.concatenate([wdown[k, 0] for k in range(blocks)], axis=1)
    g = dot_nn(a2[...], w_gate)
    u = dot_nn(a2[...], w_up)
    s = sigmoid(g)
    f_low = (g * s * u).astype(BF16)
    c = cot[...]
    acc[...] += dot_nn(f_low, w_down)
    df = dot_nt(c, w_down)
    du = (df * g * s).astype(BF16)
    dg = (df * u * s * (1.0 + g * (1.0 - s))).astype(BF16)
    dacc[...] += dot_nt(dg, w_gate) + dot_nt(du, w_up)
    ghid_o[:, 0, 0] = dot_nn(a2t[...], dg).astype(BF16).reshape(blocks, 128, units)
    ghid_o[:, 0, 1] = dot_nn(a2t[...], du).astype(BF16).reshape(blocks, 128, units)
    gd = dot_tn(f_low, c).astype(BF16)
    for k in range(blocks):
        gdown_o[k, 0] = gd[:, 128 * k : 128 * k + 128]

    @pl.when(step == pl.num_programs(0) - 1)
    def _():
        v = hid[...]
        out_o[...] = (v + acc[...]).astype(BF16)
        f = lax.rsqrt(jnp.mean(v * v, axis=1, keepdims=True) + epsilon)
        dy = dacc[...]
        gg_o[...] = jnp.sum(dy * v * f, axis=0, keepdims=True)
        gdy = dy * gain[...]
        lean = jnp.sum(gdy * v, axis=1, keepdims=True) * (f * f * f / width)
        dh = cot[...].astype(F32) + (f * gdy - v * lean)
        dh_o[...] = dh
        dmix_o[...] = dh.astype(BF16)


def feed_forward(hid, gain, cot, whid, wdown):
    rows, width = hid.shape
    blocks, nt, _, depth, units = whid.shape
    tile = 256
    per = units // tile
    hid_spec = pl.BlockSpec((blocks, 1, 2, depth, tile), lambda i: (0, i // per, 0, 0, lax.rem(i, per)))
    down_spec = pl.BlockSpec((blocks, 1, tile, 128), lambda i: (0, i // per, lax.rem(i, per), 0))
    sds = jax.ShapeDtypeStruct

    def fixed(*shape):
        return pl.BlockSpec(shape, lambda i: (0, 0))

    return pl.pallas_call(
        feed_kernel,
        grid=(nt * per,),
        in_specs=[fixed(rows, width), fixed(1, width), fixed(rows, width), hid_spec, down_spec],
        out_specs=[fixed(rows, width), fixed(rows, width), fixed(rows, width), fixed(1, width), hid_spec,
                   down_spec],
        out_shape=[sds((rows, width), BF16), sds((rows, width), F32), sds((rows, width), BF16),
                   sds((1, width), F32), sds(whid.shape, BF16), sds(wdown.shape, BF16)],
        scratch_shapes=[pltpu.VMEM((rows, width), BF16), pltpu.VMEM((width, rows), BF16),
                        pltpu.VMEM((rows, width), F32), pltpu.VMEM((rows, width), F32)],
        compiler_params=pltpu.CompilerParams(vmem_limit_bytes=VMEM_LIMIT),
        cost_estimate=pl.CostEstimate(flops=int(1e10), bytes_accessed=int(26e6), transcendentals=int(5e5)),
        name="feed_forward",
    )(hid, gain, cot, whid, wdown)


def row_columns(rows_list, rows):
    return jnp.concatenate(
        [stack_columns([r[:, c : c + 128] for r in rows_list]) for c in range(0, rows, 128)], axis=0
    )


def mix_kernel(channels, o, y, z, sq, gain, watt, wmam, m_o, part_o):
    rows = o.shape[0]
    r = row_columns([lax.rsqrt(sq[...] / channels + epsilon)], rows)[:, 0:1]
    zv = z[...]
    m = (y[...] * (zv * sigmoid(zv)) * r * gain[...]).astype(BF16)
    m_o[...] = m
    part_o[...] = (dot_nn(o[...], watt[...]) + dot_nn(m, wmam[...])).astype(BF16)


def mix_parts(channels, o, y, z, sq, gain, watt, wmam):
    total, inner = y.shape
    width = watt.shape[1]
    rows = 256

    def tall(n):
        return pl.BlockSpec((rows, n), lambda i: (i, 0))

    wide = pl.BlockSpec((8, rows), lambda i: (0, i))
    sds = jax.ShapeDtypeStruct
    return pl.pallas_call(
        partial(mix_kernel, channels),
        grid=(total // rows,),
        in_specs=[tall(128), tall(inner), tall(inner), wide, whole_spec(gain), whole_spec(watt),
                  whole_spec(wmam)],
        out_specs=[tall(inner), tall(width)],
        out_shape=[sds((total, inner), BF16), sds((total, width), BF16)],
        compiler_params=pltpu.CompilerParams(vmem_limit_bytes=VMEM_LIMIT),
        cost_estimate=pl.CostEstimate(flops=int(1e9), bytes_accessed=int(7e6), transcendentals=int(4e5)),
        name="mix_parts",
    )(o, y, z, sq, gain, watt, wmam)


def unmix_kernel(dmix, y, z, gain, watt, wmam, do_o, dm_o, dot_o):
    rows = dmix.shape[0]
    g = dmix[...]
    do_o[...] = dot_nt(g, watt[...]).astype(BF16)
    dm = dot_nt(g, wmam[...])
    dm_o[...] = dm
    zv = z[...]
    dots = jnp.sum(dm * gain[...] * (y[...] * (zv * sigmoid(zv))), axis=1, keepdims=True)
    for c in range(0, rows, 128):
        dot_o[:, c : c + 128] = jnp.broadcast_to(dots[c : c + 128], (128, 128)).T[0:8, :]


def unmix(dmix, y, z, gain, watt, wmam):
    total, inner = y.shape
    rows = 256

    def tall(n):
        return pl.BlockSpec((rows, n), lambda i: (i, 0))

    wide = pl.BlockSpec((8, rows), lambda i: (0, i))
    sds = jax.ShapeDtypeStruct
    return pl.pallas_call(
        unmix_kernel,
        grid=(total // rows,),
        in_specs=[tall(dmix.shape[1]), tall(inner), tall(inner), whole_spec(gain), whole_spec(watt),
                  whole_spec(wmam)],
        out_specs=[tall(128), tall(inner), wide],
        out_shape=[sds((total, 128), BF16), sds((total, inner), F32), sds((8, total), F32)],
        compiler_params=pltpu.CompilerParams(vmem_limit_bytes=VMEM_LIMIT),
        cost_estimate=pl.CostEstimate(flops=int(1e9), bytes_accessed=int(7e6), transcendentals=int(4e5)),
        name="unmix",
    )(dmix, y, z, gain, watt, wmam)


def down_kernel(dq, dz, dx, dkv, db, drow, wq, win, stp, wsh, part_o):
    total = dot_nt(dq[...], wq[...]) + dot_nt(dz[...], win[0]) + dot_nt(dx[...], win[1])
    total = total + dot_nt(dkv[...], wsh[:, 0:256]) + dot_nt(db[...], wsh[:, 256:])
    total = total + dot_tn(drow[...].astype(BF16), stp[...])
    part_o[...] = total.astype(BF16)


def down_parts(dq, dz, dx, dkv, db, drow, wq, win, stp, wsh):
    total, inner = dz.shape
    width = wq.shape[0]
    rows = 256

    def tall(v):
        return pl.BlockSpec((rows, v.shape[1]), lambda i: (i, 0))

    wide = pl.BlockSpec((8, rows), lambda i: (0, i))
    return pl.pallas_call(
        down_kernel,
        grid=(total // rows,),
        in_specs=[tall(dq), tall(dz), tall(dx), tall(dkv), tall(db), wide, whole_spec(wq), whole_spec(win),
                  whole_spec(stp), whole_spec(wsh)],
        out_specs=pl.BlockSpec((rows, width), lambda i: (i, 0)),
        out_shape=jax.ShapeDtypeStruct((total, width), BF16),
        compiler_params=pltpu.CompilerParams(vmem_limit_bytes=VMEM_LIMIT),
        cost_estimate=pl.CostEstimate(flops=int(3e9), bytes_accessed=int(8e6), transcendentals=0),
        name="down_parts",
    )(dq, dz, dx, dkv, db, drow, wq, win, stp, wsh)


def weight_kernel(a1, dq, dz, dx, dkv, db, drow, o, m, dmix, piece_o, shared_o, step_o, ot, mt):
    step = pl.program_id(0)

    @pl.when(step == 0)
    def _():
        ot[...] = o[...].T
        mt[...] = m[...].T

    a = a1[...]
    step_o[...] = dot_nn(drow[...].astype(BF16), a)
    at = a.T
    inner = dz.shape[1]

    def by_rows(values, first):
        for j in range(values.shape[1] // 128):
            piece_o[:, first + 128 * j : first + 128 * (j + 1), :] = (
                values[:, 128 * j : 128 * (j + 1)].reshape(2, 128, 128)
            )

    def by_lanes(values, first):
        n = values.shape[0]
        for k in range(2):
            piece_o[k, first : first + n, :] = values[:, 128 * k : 128 * (k + 1)]

    g = dmix[...]
    by_rows(dot_nn(at, dq[...]).astype(BF16), 0)
    by_lanes(dot_nn(ot[...], g).astype(BF16), 128)
    by_rows(dot_nn(at, dz[...]).astype(BF16), 256)
    by_rows(dot_nn(at, dx[...]).astype(BF16), 256 + inner)
    by_lanes(dot_nn(mt[...], g).astype(BF16), 256 + 2 * inner)
    shared_o[:, :, 0:256] = dot_nn(at, dkv[...]).astype(BF16).reshape(2, 128, 256)
    shared_o[:, :, 256:] = dot_nn(at, db[...]).astype(BF16).reshape(2, 128, db.shape[1])


def weight_pieces(a1, dq, dz, dx, dkv, db, drow, o, m, dmix):
    total, width = a1.shape
    inner = dz.shape[1]
    n = 256 + 3 * inner
    shared = 256 + db.shape[1]
    cols = pl.BlockSpec((total, 256), lambda i: (0, i))
    sds = jax.ShapeDtypeStruct
    args = (dq, dz, dx, dkv, db, drow, o, m)
    return pl.pallas_call(
        weight_kernel,
        grid=(width // 256,),
        in_specs=[cols] + [whole_spec(v) for v in args] + [cols],
        out_specs=[pl.BlockSpec((2, n, 128), lambda i: (i, 0, 0)),
                   pl.BlockSpec((2, 128, shared), lambda i: (i, 0, 0)),
                   pl.BlockSpec((8, 256), lambda i: (0, i))],
        out_shape=[sds((width // 128, n, 128), BF16), sds((width // 128, 128, shared), BF16),
                   sds((8, width), F32)],
        scratch_shapes=[pltpu.VMEM((128, total), BF16), pltpu.VMEM((inner, total), BF16)],
        compiler_params=pltpu.CompilerParams(vmem_limit_bytes=VMEM_LIMIT),
        cost_estimate=pl.CostEstimate(flops=int(4e9), bytes_accessed=int(12e6), transcendentals=0),
        name="weight_pieces",
    )(a1, *args, dmix)


def rope_wide(length):
    half = HEAD_SIZE // 2
    inverse = rope_base ** (-np.arange(half) * (2.0 / HEAD_SIZE))
    angles = np.arange(length)[:, None] * inverse[None, :]
    c, s = np.cos(angles), np.sin(angles)
    return (
        jnp.asarray(np.concatenate([c, c, c, c], axis=1), F32),
        jnp.asarray(np.concatenate([-s, s, -s, s], axis=1), F32),
    )


def to_blocks(full, axis, nt):
    if axis == 1:
        two, width, cols = full.shape
        return full.reshape(2, 8, width // 8, nt, cols // nt).transpose(1, 3, 0, 2, 4)
    rows, width = full.shape
    return full.reshape(nt, rows // nt, 8, width // 8).transpose(2, 0, 1, 3)


def per_device(
    nd,
    nt,
    tokens,
    query_proj,
    attend_out,
    inner_proj,
    step_proj,
    mamba_out,
    hidden_proj,
    down_proj,
    channel_taps,
    mixer_gain,
    decay_log,
    step_bias,
    skip_weight,
    shared_proj,
    norm_gains,
    shared_taps,
    cotangent,
):
    tensor_index = lax.axis_index("tensor")
    d = lax.axis_index("dp")
    local_rows, width = tokens.shape
    group_rows = local_rows * nt
    heads = step_proj.shape[1]
    inner = heads * SSM_DIM
    channels = inner * nt
    units = down_proj.shape[0]
    small_parts = [channel_taps, mixer_gain, norm_gains, shared_taps, step_proj.T]
    flat = jnp.concatenate([p.reshape(-1) for p in small_parts])
    small_len = -(-flat.shape[0] // 2048) * 2048
    small = jnp.pad(flat, (0, small_len - flat.shape[0])).reshape(-1, 128)
    (tok_full, full_query, full_attend, full_inner, full_mamba, sha, sma) = gather_start(
        tokens, query_proj, attend_out, inner_proj, mamba_out, shared_proj, small, nd, nt
    )
    hid_in, down_in = hidden_proj, down_proj
    if nd == 8:
        full_hidden = lax.all_gather(hid_in, ("dp", "tensor"), axis=0).reshape(
            (nd, nt) + hidden_proj.shape
        )
        full_down = lax.all_gather(down_in, ("dp", "tensor"), axis=0).reshape(
            (nd, nt) + down_proj.shape
        )
    else:
        full_hidden = lax.all_gather(hid_in, "tensor", axis=2, tiled=True)
        full_hidden = to_blocks(lax.all_gather(full_hidden, "dp", axis=1, tiled=True), 1, nt)
        full_down = lax.all_gather(down_in, "tensor", axis=0, tiled=True)
        full_down = to_blocks(lax.all_gather(full_down, "dp", axis=1, tiled=True), 0, nt)

    full_shared = sha.reshape(width, -1)
    sma = sma.reshape(nd, nt, small_len)

    def small_piece(index):
        start = sum(p.size for p in small_parts[:index])
        part = small_parts[index]
        return sma[:, :, start : start + part.size].reshape((nd, nt) + part.shape)

    taps_x = pick(small_piece(0), tensor_index, 1).transpose(1, 2, 0, 3).reshape(CONV + 1, inner)
    gain_mix = pick(small_piece(1), tensor_index, 1).transpose(1, 0, 2).reshape(1, inner)
    full_norms = small_piece(2).transpose(2, 0, 1, 3).reshape(2, width).astype(F32)
    taps_b = small_piece(3).transpose(2, 0, 1, 3).reshape(CONV + 1, -1)
    step_rows = pick(small_piece(4), tensor_index, 1).transpose(1, 0, 2).reshape(heads, width)
    step_rows = jnp.pad(step_rows, ((0, 8 - heads), (0, 0)))
    taps_x = jnp.pad(taps_x.astype(F32), ((0, 7 - CONV), (0, 0)))
    taps_b = jnp.pad(taps_b.astype(F32), ((0, 7 - CONV), (0, 0)))
    gain_mix = gain_mix.astype(F32)
    gain_first = full_norms[0:1]
    gain_second = full_norms[1:2]

    def head_rows(values):
        return jnp.pad(jnp.broadcast_to(values[:, None], (heads, 128)), ((0, 8 - heads), (0, 0)))

    decay = head_rows(-jnp.exp(decay_log.astype(F32)))
    bias = head_rows(step_bias.astype(F32))
    skip = jnp.repeat(skip_weight.astype(F32), SSM_DIM)[None, :]
    q_heads = query_proj.shape[1] // HEAD_SIZE
    kv_head = (tensor_index * q_heads // (QHEADS // KVHEADS)).astype(jnp.int32).reshape(1)
    cosine, sine = rope_wide(group_rows)

    (a1, q, k2, v2, lse, o, xr, zr, br, y, trow, states, squares) = mixers_forward(
        heads, kv_head, tok_full.reshape(group_rows, width), gain_first, full_query, full_inner, step_rows,
        full_shared, cosine, sine, taps_x, taps_b, decay, bias, skip,
    )
    squares = jnp.broadcast_to(tensor_total(squares[0:1]), (8, group_rows))
    m, mix_part = mix_parts(channels, o, y, zr, squares, gain_mix, full_attend, full_mamba)
    hidden = tokens.astype(F32) + chain_scatter(mix_part.reshape(nt, local_rows, width), nt)
    layer_out, dh, dmix, grad_gain_two, hid_pieces, down_pieces = feed_forward(
        hidden, gain_second, cotangent, full_hidden, full_down
    )
    grad_mix = chain_gather(dmix, nt).reshape(group_rows, width)
    if nd == 8:
        hid_sum = cube_scatter(hid_pieces, nd, BF16)
        down_sum = cube_scatter(down_pieces, nd, BF16)
        gradient_hidden = chain_scatter(hid_sum, nt)
        gradient_down = chain_scatter(down_sum, nt)
    else:
        hid_full = hid_pieces.transpose(2, 0, 3, 1, 4).reshape(2, nd, width // nd, nt, units)
        hid_sum = cube_scatter(hid_full.transpose(1, 3, 0, 2, 4), nd, BF16)
        down_full = down_pieces.transpose(1, 2, 0, 3).reshape(nt, units, nd, width // nd)
        down_sum = cube_scatter(down_full.transpose(2, 0, 1, 3), nd, BF16)
        gradient_hidden = chain_scatter(hid_sum, nt)
        gradient_down = chain_scatter(down_sum, nt)

    do, dm, dots = unmix(grad_mix, y, zr, gain_mix, full_attend, full_mamba)
    dots = jnp.broadcast_to(tensor_total(dots[0:1]), (8, group_rows))
    dq, dkv = attend_back(kv_head, q, k2, v2, lse, do, cosine, sine)
    dz, dx, db, drow, grad_tx, grad_tb, grad_rows, grad_heads = scan_back(
        heads, channels, dm, y, zr, xr, br, trow, states, squares, dots, gain_mix, taps_x, taps_b, decay, bias,
        skip,
    )
    part_one = down_parts(dq, dz, dx, dkv, db, drow, full_query, full_inner, step_rows, full_shared)
    grad_normed_one = chain_scatter(part_one.reshape(nt, local_rows, width), nt)
    token_f32 = tokens.astype(F32)
    _, norm_one_back = jax.vjp(norm_apply, token_f32, gain_first[0])
    grad_from_one, grad_gain_one = norm_one_back(grad_normed_one)
    gradient_tokens = (dh + grad_from_one).astype(BF16)

    pieces, shared_pieces, grad_step = weight_pieces(a1, dq, dz, dx, dkv, db, drow, o, m, grad_mix)
    block = width // nd
    q_cols = query_proj.shape[1]
    cuts = [0, q_cols, q_cols + attend_out.shape[0]]
    cuts += [cuts[2] + inner, cuts[2] + 2 * inner, cuts[2] + 3 * inner]

    def from_rows(values):
        return values.reshape(8, -1, 128, 128).transpose(0, 2, 1, 3).reshape(width, -1)

    def from_lanes(values):
        return values.transpose(1, 0, 2).reshape(-1, width)

    if nd == 8:
        mixer_sum = cube_scatter(pieces, nd)
        got = [mixer_sum[cuts[i] : cuts[i + 1]] for i in range(5)]

        def back_rows(values):
            return values.reshape(-1, 128, 128).transpose(1, 0, 2).reshape(128, -1)

        gradient_query = back_rows(got[0])
        gradient_attend = got[1]
        gradient_inner = jnp.stack([back_rows(got[2]), back_rows(got[3])])
        gradient_mamba = got[4]
    else:
        got = [pieces[:, cuts[i] : cuts[i + 1]] for i in range(5)]

        def over_rows(values):
            return cube_scatter(from_rows(values).reshape(nd, block, -1), nd)

        def over_lanes(values):
            return cube_scatter(from_lanes(values).reshape(-1, nd, block).transpose(1, 0, 2), nd)

        gradient_query = over_rows(got[0])
        gradient_attend = over_lanes(got[1])
        gradient_inner = jnp.stack([over_rows(got[2]), over_rows(got[3])])
        gradient_mamba = over_lanes(got[4])
    shared_cut = shared_pieces.reshape(nd, nt, width // (nd * nt), -1)
    gradient_shared = chain_scatter(cube_scatter(shared_cut, nd, BF16), nt)

    n_tap = CONV + 1
    over_all = jnp.concatenate(
        [grad_gain_one, grad_gain_two.reshape(-1), grad_tb[:n_tap].reshape(-1)]
    )
    over_dp = jnp.concatenate(
        [
            grad_tx[:n_tap].reshape(-1),
            grad_rows[0],
            grad_rows[1].reshape(heads, SSM_DIM).sum(axis=1),
            grad_heads[:heads].sum(axis=1),
            grad_heads[8 : 8 + heads].sum(axis=1),
            grad_step[:heads].reshape(-1),
        ]
    )
    n_all = over_all.shape[0]
    over_dp = lax.psum(jnp.concatenate([over_all, over_dp]), "dp")
    over_all = lax.psum(over_dp[:n_all], "tensor")
    over_dp = over_dp[n_all:]
    place = d * nt + tensor_index
    norm_w = width // (nd * nt)
    gradient_norms = lax.dynamic_slice_in_dim(
        over_all[: 2 * width].reshape(2, width), place * norm_w, norm_w, 1
    )
    tap_w = shared_taps.shape[1]
    gradient_taps = lax.dynamic_slice_in_dim(
        over_all[2 * width :].reshape(n_tap, -1), place * tap_w, tap_w, 1
    )
    part = mixer_gain.shape[1]
    n_taps = n_tap * inner
    chan = over_dp[:n_taps].reshape(n_tap, heads, SSM_DIM)
    gain = over_dp[n_taps : n_taps + inner].reshape(heads, SSM_DIM)
    gradient_channel = lax.dynamic_slice_in_dim(chan, d * part, part, 2)
    gradient_mixer = lax.dynamic_slice_in_dim(gain, d * part, part, 1)
    rest = over_dp[n_taps + inner :]
    gradient_skip = rest[:heads]
    gradient_decay = rest[heads : 2 * heads]
    gradient_bias = rest[2 * heads : 3 * heads]
    step_all = rest[3 * heads :].reshape(heads, width)
    gradient_step = lax.dynamic_slice_in_dim(step_all, d * block, block, 1).T
    return (
        layer_out,
        gradient_tokens,
        gradient_query,
        gradient_attend,
        gradient_inner,
        gradient_step,
        gradient_mamba,
        gradient_hidden,
        gradient_down,
        gradient_channel,
        gradient_mixer,
        gradient_decay,
        gradient_bias,
        gradient_skip,
        gradient_shared,
        gradient_norms,
        gradient_taps,
    )


def solution(mesh):
    placed = (
        P(("dp", "tensor"), None),
        P("dp", "tensor"),
        P("tensor", "dp"),
        P(None, "dp", "tensor"),
        P("dp", "tensor"),
        P("tensor", "dp"),
        P(None, "dp", "tensor"),
        P("tensor", "dp"),
        P(None, "tensor", "dp"),
        P("tensor", "dp"),
        P("tensor"),
        P("tensor"),
        P("tensor"),
        P(("dp", "tensor"), None),
        P(None, ("dp", "tensor")),
        P(None, ("dp", "tensor")),
        P(("dp", "tensor"), None),
    )
    return jax.shard_map(
        partial(per_device, mesh.shape["dp"], mesh.shape["tensor"]),
        mesh=mesh,
        in_specs=placed,
        out_specs=(
            P(("dp", "tensor"), None),
            P(("dp", "tensor"), None),
            P("dp", "tensor"),
            P("tensor", "dp"),
            P(None, "dp", "tensor"),
            P("dp", "tensor"),
            P("tensor", "dp"),
            P(None, "dp", "tensor"),
            P("tensor", "dp"),
            P(None, "tensor", "dp"),
            P("tensor", "dp"),
            P("tensor"),
            P("tensor"),
            P("tensor"),
            P(("dp", "tensor"), None),
            P(None, ("dp", "tensor")),
            P(None, ("dp", "tensor")),
        ),
        check_vma=False,
    )
```

```python
from functools import partial

import numpy as np
import jax
import jax.numpy as jnp
from jax import lax
from jax.experimental import pallas as pl
from jax.experimental.pallas import tpu as pltpu
from jax.sharding import PartitionSpec as P

MESH = pl.DeviceIdType.MESH

QHEADS = 8
KVHEADS = 2
HEAD_SIZE = 64
SSM_DIM = 64
CONV = 4


epsilon = 1e-05
rope_base = 100000000000.0
neg_large = -1e30
block_len = 128


def norm_apply(values, gain):
    factor = lax.rsqrt(jnp.mean(values * values, axis=-1, keepdims=True) + epsilon)
    return values * factor * gain


def dp_bits(index):
    core = lax.rem(index, 2)
    xbit = lax.rem(index // 2, 2)
    ybit = lax.rem(index // 4, 2)
    return core, xbit, ybit


def gather_kernel(nt, *refs):
    (tok, que, att, inn, mam, sha, sma) = refs[:7]
    (tok_f, que_f, att_f, inn_f, mam_f, sha_f, sma_f) = refs[7:14]
    (lsem, zs_send, zs_recv, t_send, t_recv, d_send, d_recv) = refs[14:]
    d = lax.axis_index("dp")
    z = lax.axis_index("tensor")
    core, xbit, ybit = dp_bits(d)
    d_core = d + 1 - 2 * core
    d_x = d + 2 - 4 * xbit
    d_y = d + 4 - 8 * ybit
    d_xy = d_x + 4 - 8 * ybit

    barrier = pltpu.get_barrier_semaphore()
    for peer in (d_core, d_x, d_y):
        pl.semaphore_signal(barrier, inc=1, device_id=(peer, z), device_id_type=MESH)
    for k in range(1, nt):
        pl.semaphore_signal(
            barrier, inc=1, device_id=(d, lax.rem(z + k, nt)), device_id_type=MESH
        )
    pl.semaphore_wait(barrier, 3 + nt - 1)

    def remote(src, dst, send, recv, dev):
        return pltpu.make_async_remote_copy(
            src_ref=src, dst_ref=dst, send_sem=send, recv_sem=recv,
            device_id=dev, device_id_type=MESH,
        )

    small = []
    for i, (src, dst) in enumerate(((sha, sha_f), (sma, sma_f))):
        for k in range(1, nt):
            copy = remote(
                src, dst.at[d, z], zs_send.at[i, k], zs_recv.at[i, k],
                (d, lax.rem(z + k, nt)),
            )
            copy.start()
            small.append(copy)
    q_rows = que.shape[0]
    cols = att.shape[1]
    i_rows = inn.shape[1]
    items = (
        (inn, lambda s: inn_f.at[:, pl.ds(s * i_rows, i_rows)]),
        (que, lambda s: que_f.at[pl.ds(s * q_rows, q_rows)]),
        (att, lambda s: att_f.at[:, pl.ds(pl.multiple_of(s * cols, cols), cols)]),
        (mam, lambda s: mam_f.at[:, pl.ds(pl.multiple_of(s * cols, cols), cols)]),
    )
    locals_ = []
    for i, (src, dst) in enumerate(
        [(tok, tok_f.at[z]), (sha, sha_f.at[d, z]), (sma, sma_f.at[d, z])]
        + [(src, at(d)) for src, at in items]
    ):
        copy = pltpu.make_async_copy(src, dst, lsem.at[i])
        copy.start()
        locals_.append(copy)
    sent = []

    def stage_one(i, src, at):
        for j, peer in enumerate((d_x, d_y, d_core)):
            copy = remote(src, at(d), d_send.at[i, j], d_recv.at[i, j], (peer, z))
            copy.start()
            sent.append(copy)

    for i, (src, at) in enumerate(items):
        stage_one(i, src, at)

    def tok_copy(slot, dirn, hop):
        dev = z + 1 if dirn == 0 else z - 1
        return remote(
            tok_f.at[slot], tok_f.at[slot], t_send.at[dirn, hop], t_recv.at[dirn, hop], (d, dev)
        )

    def own_copy(dirn):
        dev = z + 1 if dirn == 0 else z - 1
        return remote(tok, tok_f.at[z], t_send.at[dirn, 0], t_recv.at[dirn, 0], (d, dev))

    pl.when(z < nt - 1)(lambda: own_copy(0).start())
    pl.when(z > 0)(lambda: own_copy(1).start())

    locals_[1].wait()
    locals_[2].wait()
    for copy in small:
        copy.wait()
    n = len(items)
    shared_items = (
        (sha_f.at[d], lambda s: sha_f.at[s]),
        (sma_f.at[d], lambda s: sma_f.at[s]),
    )
    for i, (src, at) in enumerate(shared_items):
        stage_one(n + i, src, at)

    def wait_recv(i, j, at, slot):
        remote(at(slot), at(slot), d_send.at[i, j], d_recv.at[i, j], (d_core, z)).wait_recv()

    def forward(i, j, at, slot, peer):
        copy = remote(at(slot), at(slot), d_send.at[i, j], d_recv.at[i, j], (peer, z))
        copy.start()
        sent.append(copy)

    everything = [at for _, at in items] + [at for _, at in shared_items]
    via_y = (0, n + 1)

    def diagonal(i, at):
        wait_recv(i, 0, at, d_x)
        if i in via_y:
            forward(i, 3, at, d_x, d_y)
        forward(i, 4, at, d_x, d_core)
        wait_recv(i, 1, at, d_y)
        if i not in via_y:
            forward(i, 3, at, d_y, d_x)
        forward(i, 5, at, d_y, d_core)

    for i in range(n):
        diagonal(i, everything[i])

    def hop(dist):
        def from_left():
            tok_copy(z - dist, 0, dist - 1).wait_recv()

        def from_right():
            tok_copy(z + dist, 1, dist - 1).wait_recv()

        pl.when(z >= dist)(from_left)
        if dist < nt - 1:
            pl.when((z >= dist) & (z < nt - 1))(lambda: tok_copy(z - dist, 0, dist).start())
        pl.when(z + dist < nt)(from_right)
        if dist < nt - 1:
            pl.when((z + dist < nt) & (z > 0))(lambda: tok_copy(z + dist, 1, dist).start())

    hop(1)
    for i in range(n, n + 2):
        diagonal(i, everything[i])
    for i, at in enumerate(everything):
        wait_recv(i, 3, at, d_xy)
        forward(i, 6, at, d_xy, d_core)
    for dist in range(2, nt):
        hop(dist)
    for i, at in enumerate(everything):
        wait_recv(i, 2, at, d_core)
        for j in (4, 5, 6):
            wait_recv(i, j, at, d_core)
    for i, copy in enumerate(locals_):
        if i not in (1, 2):
            copy.wait()
    for copy in sent:
        copy.wait_send()
    pl.when(z < nt - 1)(lambda: own_copy(0).wait_send())
    pl.when(z > 0)(lambda: own_copy(1).wait_send())
    for dist in range(1, nt - 1):
        pl.when((z >= dist) & (z < nt - 1))(lambda: tok_copy(z - dist, 0, dist).wait_send())
        pl.when((z + dist < nt) & (z > 0))(lambda: tok_copy(z + dist, 1, dist).wait_send())


def gather_start(tok, que, att, inn, mam, sha, sma, nd, nt):
    if nd != 8:
        shared = lax.all_gather(sha, ("dp", "tensor"), axis=0)
        small = lax.all_gather(sma, ("dp", "tensor"), axis=0)
        return (
            lax.all_gather(tok, "tensor", axis=0),
            lax.all_gather(que, "dp", axis=0, tiled=True),
            lax.all_gather(att, "dp", axis=1, tiled=True),
            lax.all_gather(inn, "dp", axis=1, tiled=True),
            lax.all_gather(mam, "dp", axis=1, tiled=True),
            shared.reshape((nd, nt) + sha.shape),
            small.reshape((nd, nt) + sma.shape),
        )
    bf = jnp.bfloat16
    outs = (
        (nt,) + tok.shape,
        (nd * que.shape[0], que.shape[1]),
        (att.shape[0], nd * att.shape[1]),
        (2, nd * inn.shape[1], inn.shape[2]),
        (mam.shape[0], nd * mam.shape[1]),
        (nd, nt) + sha.shape,
        (nd, nt) + sma.shape,
    )
    anywhere = pl.BlockSpec(memory_space=pl.ANY)
    dma = pltpu.SemaphoreType.DMA
    return pl.pallas_call(
        partial(gather_kernel, nt),
        out_shape=[jax.ShapeDtypeStruct(s, bf) for s in outs],
        in_specs=[anywhere] * 7,
        out_specs=[anywhere] * 7,
        scratch_shapes=[
            dma((7,)), dma((2, nt)), dma((2, nt)), dma((2, nt)), dma((2, nt)),
            dma((6, 7)), dma((6, 7)),
        ],
        compiler_params=pltpu.CompilerParams(collective_id=0, has_side_effects=True),
        name="gather_start",
    )(tok, que, att, inn, mam, sha, sma)


def pick(values, index, axis=0):
    return lax.dynamic_index_in_dim(values, index, axis, keepdims=False)


def add_low(left, right):
    return (left.astype(jnp.float32) + right.astype(jnp.float32)).astype(jnp.bfloat16)


def chain_scatter(parts, nt):
    z = lax.axis_index("tensor")
    right = left = None
    for t in range(nt - 1):
        to_right = pick(parts, jnp.clip(nt - 1 - t + z, 0, nt - 1))
        to_left = pick(parts, jnp.clip(t - (nt - 1) + z, 0, nt - 1))
        if t > 0:
            to_right = add_low(to_right, right)
            to_left = add_low(to_left, left)
        right = lax.ppermute(to_right, "tensor", [(i, i + 1) for i in range(t + 1)])
        left = lax.ppermute(
            to_left, "tensor", [(nt - 1 - i, nt - 2 - i) for i in range(t + 1)]
        )
    f32 = jnp.float32
    return pick(parts, z).astype(f32) + right.astype(f32) + left.astype(f32)


def cube_scatter(parts, nd, last=jnp.float32):
    if nd != 8:
        return lax.psum_scatter(parts, "dp", scatter_dimension=0, tiled=False).astype(last)
    d = lax.axis_index("dp")
    core, xbit, ybit = dp_bits(d)

    def swap(values, bit):
        return lax.ppermute(values, "dp", [(i, i ^ bit) for i in range(8)])

    tail = parts.shape[1:]
    cut = parts.reshape((4, 2) + tail)
    held = add_low(pick(cut, core, 1), swap(pick(cut, 1 - core, 1), 1))
    held = held.reshape((2, 2) + tail)
    half = tail[0] // 2
    one, two = held[:, :, :half], held[:, :, half:]
    one_b = add_low(pick(one, xbit, 1), swap(pick(one, 1 - xbit, 1), 2))
    two_b = add_low(pick(two, ybit, 0), swap(pick(two, 1 - ybit, 0), 4))
    f32 = jnp.float32
    one_c = pick(one_b, ybit).astype(f32) + swap(pick(one_b, 1 - ybit), 4).astype(f32)
    two_c = pick(two_b, xbit).astype(f32) + swap(pick(two_b, 1 - xbit), 2).astype(f32)
    return jnp.concatenate([one_c, two_c], axis=0).astype(last)


F32, BF16 = jnp.float32, jnp.bfloat16
VMEM_LIMIT = 56 * 1024 * 1024


def dot_nn(a, b):
    return lax.dot_general(a, b, (((1,), (0,)), ((), ())), preferred_element_type=F32)


def dot_nt(a, b):
    return lax.dot_general(a, b, (((1,), (1,)), ((), ())), preferred_element_type=F32)


def dot_tn(a, b):
    return lax.dot_general(a, b, (((0,), (0,)), ((), ())), preferred_element_type=F32)


def sigmoid(v):
    return 1.0 / (1.0 + jnp.exp(-v))


def lanes_of(shape):
    return lax.broadcasted_iota(jnp.int32, shape, len(shape) - 1)


def turn(values, cosine, sine):
    lane = lanes_of(values.shape)
    other = jnp.where(
        lax.rem(lane, HEAD_SIZE) < HEAD_SIZE // 2,
        pltpu.roll(values, 128 - HEAD_SIZE // 2, 1),
        pltpu.roll(values, HEAD_SIZE // 2, 1),
    )
    return values * cosine + other * sine


def softplus(v):
    return jnp.maximum(v, 0.0) + jnp.log1p(jnp.exp(-jnp.abs(v)))


def running_sum(rows):
    lane = lanes_of(rows.shape)
    step = 1
    while step < rows.shape[1]:
        rows = rows + jnp.where(lane >= step, pltpu.roll(rows, step, 1), 0.0)
        step *= 2
    return rows


def running_sum_back(rows):
    lane = lanes_of(rows.shape)
    width = rows.shape[1]
    step = 1
    while step < width:
        rows = rows + jnp.where(lane < width - step, pltpu.roll(rows, width - step, 1), 0.0)
        step *= 2
    return rows


def stack_columns(rows_list):
    used = sum(r.shape[0] for r in rows_list)
    filler = jnp.zeros((128 - used, 128), F32)
    return jnp.concatenate(rows_list + [filler], axis=0).T


def widen(cols, base, heads):
    low = lanes_of((cols.shape[0], 128)) < SSM_DIM
    return jnp.concatenate(
        [
            jnp.where(low, cols[:, base + 2 * p : base + 2 * p + 1],
                      cols[:, base + 2 * p + 1 : base + 2 * p + 2])
            for p in range(heads // 2)
        ],
        axis=1,
    )


def conv_rows(ref, taps, first, rows):
    total = taps[CONV : CONV + 1, :] + taps[0:1, :] * ref[pl.ds(first, rows), :]
    for j in range(1, CONV):
        total = total + taps[j : j + 1, :] * ref[pl.ds(first + j, rows), :]
    return total


def forward_kernel(
    heads, kvh, tok, gain, wq, win, stp, wsh, cosine, sine, tapx, tapb, decay, bias, skip,
    a1_o, q_o, k_o, v_o, lse_o, o_o, x_o, z_o, b_o, y_o, t_o, s_o, sq_o,
    keys, vals, xs, bs, state,
):
    step = pl.program_id(0)
    rows = tok.shape[0]
    second = kvh[0] == 1

    @pl.when(step == 0)
    def _():
        xs[0:8, :] = jnp.zeros((8, xs.shape[1]), F32)
        bs[0:8, :] = jnp.zeros((8, bs.shape[1]), F32)
        state[...] = jnp.zeros(state.shape, F32)

    t = tok[...].astype(F32)
    r = lax.rsqrt(jnp.mean(t * t, axis=1, keepdims=True) + epsilon)
    a1 = (t * r * gain[...]).astype(BF16)
    a1_o[...] = a1
    q = turn(dot_nn(a1, wq[...]), cosine[...], sine[...]).astype(BF16)
    q_o[...] = q
    s = dot_nn(a1, wsh[...])
    low = lanes_of((rows, 128)) < HEAD_SIZE
    k = turn(s[:, :128], cosine[...], sine[...])
    v = s[:, 128:256]
    pick_own = low != second
    k2 = jnp.where(pick_own, k, pltpu.roll(k, 64, 1)).astype(BF16)
    v2 = jnp.where(pick_own, v, pltpu.roll(v, 64, 1))
    k_o[...] = k2
    v_o[...] = v2.astype(BF16)
    place = pl.ds(pl.multiple_of(step * rows, rows), rows)
    keys[place, :] = k2
    vals[:, place] = v2.T.astype(BF16)

    scale = HEAD_SIZE**-0.5

    def attend(blocks):
        n = blocks * rows
        shape = (rows, rows)
        allowed = lax.broadcasted_iota(jnp.int32, shape, 0) <= lanes_of(shape)
        parts = []
        for h in range(2):
            qh = jnp.where(low == (h == 0), q, jnp.zeros_like(q))
            sc = dot_nt(keys[0:n, :], qh) * scale
            last = jnp.where(allowed, sc[n - rows :, :], neg_large)
            sc = jnp.concatenate([sc[: n - rows, :], last], axis=0) if blocks > 1 else last
            top = jnp.max(sc, axis=0, keepdims=True)
            e = jnp.exp(sc - top)
            total = jnp.sum(e, axis=0, keepdims=True)
            lse_o[h : h + 1, :] = top + jnp.log(total)
            parts.append(dot_nn(vals[:, 0:n], e.astype(BF16)) / total)
        sub = lax.broadcasted_iota(jnp.int32, parts[0].shape, 0)
        o_o[...] = jnp.where(sub < HEAD_SIZE, parts[0], parts[1]).T.astype(BF16)

    for i in range(keys.shape[0] // rows):
        pl.when(step == i)(partial(attend, i + 1))

    zr = dot_nn(a1, win[0])
    z_o[...] = zr
    xr = dot_nn(a1, win[1])
    x_o[...] = xr
    br = s[:, 256:]
    b_o[...] = br
    xs[8 : 8 + rows, :] = xr
    bs[8 : 8 + rows, :] = br
    u = conv_rows(xs, tapx, 5, rows)
    x = u * sigmoid(u)
    u = conv_rows(bs, tapb, 5, rows)
    bc = (u * sigmoid(u)).astype(BF16)
    xs[0:8, :] = xs[rows : rows + 8, :]
    bs[0:8, :] = bs[rows : rows + 8, :]
    tr = dot_nt(stp[...], a1)
    t_o[...] = tr
    n_state = bc.shape[1] // 2
    tri_shape = (block_len, block_len)
    lower = lax.broadcasted_iota(jnp.int32, tri_shape, 0) >= lanes_of(tri_shape)
    half = lanes_of(tri_shape) < SSM_DIM
    for c in range(rows // block_len):
        part = slice(c * block_len, (c + 1) * block_len)
        dt = softplus(tr[:, part] + bias[...])
        cum = running_sum(dt * decay[...])
        end = cum[:, block_len - 1 :]
        cols = stack_columns([cum, jnp.exp(cum), dt * jnp.exp(end - cum)])
        xc = x[part]
        x_low = xc.astype(BF16)
        b_low = bc[part, :n_state]
        c_low = bc[part, n_state:]
        cross = dot_nt(c_low, b_low)
        grow = widen(cols, 8, heads)
        y = dot_nn(c_low, state[...].astype(BF16)) * grow + skip[...] * xc
        inner = []
        for p in range(heads // 2):
            mats = []
            for h in (2 * p, 2 * p + 1):
                gap = jnp.where(lower, cols[:, h : h + 1] - cum[h : h + 1, :], neg_large)
                mats.append((cross * jnp.exp(gap) * dt[h : h + 1, :]).astype(BF16))
            xp = x_low[:, 128 * p : 128 * p + 128]
            zero = jnp.zeros_like(xp)
            both = jnp.concatenate([jnp.where(half, xp, zero), jnp.where(half, zero, xp)], axis=0)
            inner.append(dot_nn(jnp.concatenate(mats, axis=1), both))
        y = y + jnp.concatenate(inner, axis=1)
        y_o[part, :] = y
        s_o[c] = state[...]
        carried = (xc * widen(cols, 16, heads)).astype(BF16)
        state[...] = grow[block_len - 1 :, :] * state[...] + dot_tn(b_low, carried)
        zc = zr[part]
        w = y * (zc * sigmoid(zc))
        total = jnp.sum(w * w, axis=1, keepdims=True)
        sq_o[:, part] = jnp.broadcast_to(total, (block_len, 128)).T[0:8, :]


def mixers_forward(heads, kvh, tok, gain, wq, win, stp, wsh, cosine, sine, tapx, tapb, decay, bias, skip):
    total, width = tok.shape
    rows = 256
    inner = heads * SSM_DIM
    pair = wsh.shape[1] - 256
    state = pair // 2
    chunks = rows // block_len

    def whole(v):
        return pl.BlockSpec(v.shape, lambda i: (0,) * v.ndim)

    def tall(n):
        return pl.BlockSpec((rows, n), lambda i: (i, 0))

    wide = pl.BlockSpec((8, rows), lambda i: (0, i))
    sds = jax.ShapeDtypeStruct
    return pl.pallas_call(
        partial(forward_kernel, heads),
        grid=(total // rows,),
        in_specs=[pl.BlockSpec(memory_space=pltpu.SMEM), tall(width), whole(gain), whole(wq), whole(win),
                  whole(stp), whole(wsh), tall(128), tall(128), whole(tapx), whole(tapb),
                  whole(decay), whole(bias), whole(skip)],
        out_specs=[tall(width), tall(128), tall(128), tall(128), wide, tall(128), tall(inner),
                   tall(inner), tall(pair), tall(inner), wide,
                   pl.BlockSpec((chunks, state, inner), lambda i: (i, 0, 0)), wide],
        out_shape=[sds((total, width), BF16), sds((total, 128), BF16), sds((total, 128), BF16),
                   sds((total, 128), BF16), sds((8, total), F32), sds((total, 128), BF16),
                   sds((total, inner), F32), sds((total, inner), F32), sds((total, pair), F32),
                   sds((total, inner), F32), sds((8, total), F32),
                   sds((total // block_len, state, inner), F32), sds((8, total), F32)],
        scratch_shapes=[pltpu.VMEM((total, 128), BF16), pltpu.VMEM((128, total), BF16),
                        pltpu.VMEM((rows + 8, inner), F32), pltpu.VMEM((rows + 8, pair), F32),
                        pltpu.VMEM((state, inner), F32)],
        compiler_params=pltpu.CompilerParams(vmem_limit_bytes=VMEM_LIMIT),
        cost_estimate=pl.CostEstimate(flops=int(5e9), bytes_accessed=int(15e6), transcendentals=int(4e6)),
        name="mixers_forward",
    )(kvh, tok, gain, wq, win, stp, wsh, cosine, sine, tapx, tapb, decay, bias, skip)


def attend_back_kernel(kvh, q, k2, v2, lse, do, cosine, sine, cos_all, sin_all, dq_o, dkv_o, dk, dv):
    step = pl.program_id(0)
    rows = q.shape[0]
    steps = k2.shape[0] // rows
    scale = HEAD_SIZE**-0.5
    low = lanes_of((rows, 128)) < HEAD_SIZE

    @pl.when(step == 0)
    def _():
        dk[...] = jnp.zeros(dk.shape, F32)
        dv[...] = jnp.zeros(dv.shape, F32)

    def back(blocks):
        n = blocks * rows
        shape = (rows, rows)
        allowed = lax.broadcasted_iota(jnp.int32, shape, 0) <= lanes_of(shape)
        qs, dos, ps, dss, dqs = [], [], [], [], []
        for h in range(2):
            mine = low == (h == 0)
            qh = jnp.where(mine, q[...], jnp.zeros_like(q[...]))
            doh = jnp.where(mine, do[...], jnp.zeros_like(do[...]))
            sc = dot_nt(k2[0:n, :], qh) * scale - lse[h : h + 1, :]
            last = jnp.where(allowed, sc[n - rows :, :], neg_large)
            sc = jnp.concatenate([sc[: n - rows, :], last], axis=0) if blocks > 1 else last
            p = jnp.exp(sc)
            dp = dot_nt(v2[0:n, :], doh)
            centre = jnp.sum(p * dp, axis=0, keepdims=True)
            ds = (p * (dp - centre)).astype(BF16)
            qs.append(qh)
            dos.append(doh)
            ps.append(p.astype(BF16))
            dss.append(ds)
            dqs.append(dot_tn(ds, k2[0:n, :]) * scale)
        dk[0:n, :] += dot_nn(jnp.concatenate(dss, axis=1), jnp.concatenate(qs, axis=0)) * scale
        dv[0:n, :] += dot_nn(jnp.concatenate(ps, axis=1), jnp.concatenate(dos, axis=0))
        dq_o[...] = turn(jnp.where(low, dqs[0], dqs[1]), cosine[...], -sine[...]).astype(BF16)

    for i in range(steps):
        pl.when(step == i)(partial(back, i + 1))

    @pl.when(step == steps - 1)
    def _():
        own = (lanes_of(dk.shape) < HEAD_SIZE) != (kvh[0] == 1)
        g = dk[...]
        g = turn(g + pltpu.roll(g, 64, 1), cos_all[...], -sin_all[...])
        dkv_o[:, 0:128] = jnp.where(own, g, 0.0).astype(BF16)
        g = dv[...]
        g = g + pltpu.roll(g, 64, 1)
        dkv_o[:, 128:256] = jnp.where(own, g, 0.0).astype(BF16)


def attend_back(kvh, q, k2, v2, lse, do, cosine, sine):
    total = q.shape[0]
    rows = 256

    def whole(v):
        return pl.BlockSpec(v.shape, lambda i: (0,) * v.ndim)

    tall = pl.BlockSpec((rows, 128), lambda i: (i, 0))
    wide = pl.BlockSpec((8, rows), lambda i: (0, i))
    sds = jax.ShapeDtypeStruct
    return pl.pallas_call(
        attend_back_kernel,
        grid=(total // rows,),
        in_specs=[pl.BlockSpec(memory_space=pltpu.SMEM), tall, whole(k2), whole(v2), wide, tall, tall, tall,
                  whole(cosine), whole(sine)],
        out_specs=[tall, pl.BlockSpec((total, 256), lambda i: (0, 0))],
        out_shape=[sds((total, 128), BF16), sds((total, 256), BF16)],
        scratch_shapes=[pltpu.VMEM((total, 128), F32), pltpu.VMEM((total, 128), F32)],
        compiler_params=pltpu.CompilerParams(vmem_limit_bytes=VMEM_LIMIT),
        cost_estimate=pl.CostEstimate(flops=int(2e9), bytes_accessed=int(3e6), transcendentals=int(2e6)),
        name="attend_back",
    )(kvh, q, k2, v2, lse, do, cosine, sine, cosine, sine)


def scan_back_kernel(
    heads, channels, dm, y, zr, xr, xp, br, bp, trow, states, rsum, dots, gain, tapx, tapb, decay,
    bias, skip,
    dz_o, dx_o, db_o, dt_o, gx_o, gb_o, gm_o, gh_o,
    xs, bs, dxs, dbs, dstate,
):
    step = pl.program_id(0)
    last_step = pl.num_programs(0) - 1
    first = step == last_step
    rows = block_len
    inner = heads * SSM_DIM
    n_state = br.shape[1] // 2

    @pl.when(step == 0)
    def _():
        dxs[rows : rows + 8, :] = jnp.zeros((8, inner), F32)
        dbs[rows : rows + 8, :] = jnp.zeros((8, 2 * n_state), F32)
        dstate[...] = jnp.zeros(dstate.shape, F32)
        gx_o[...] = jnp.zeros(gx_o.shape, F32)
        gb_o[...] = jnp.zeros(gb_o.shape, F32)
        gm_o[...] = jnp.zeros(gm_o.shape, F32)
        gh_o[...] = jnp.zeros(gh_o.shape, F32)

    xs[0:8, :] = jnp.where(first, 0.0, xp[...])
    bs[0:8, :] = jnp.where(first, 0.0, bp[...])
    xs[8 : 8 + rows, :] = xr[...]
    bs[8 : 8 + rows, :] = br[...]
    ux = conv_rows(xs, tapx, 5, rows)
    sx = sigmoid(ux)
    x = ux * sx
    ub = conv_rows(bs, tapb, 5, rows)
    sb = sigmoid(ub)
    bc = (ub * sb).astype(BF16)
    b_low, c_low = bc[:, :n_state], bc[:, n_state:]

    pre = trow[...] + bias[...]
    dt = softplus(pre)
    cum = running_sum(dt * decay[...])
    end = cum[:, rows - 1 :]
    fade = jnp.exp(end - cum)
    inv = lax.rsqrt(rsum[...] / channels + epsilon)
    cols = stack_columns(
        [cum, jnp.exp(cum), dt * fade, dt, inv, inv * inv * inv * dots[...] / channels]
    )
    r = cols[:, 32:33]
    kk = cols[:, 40:41]
    z = zr[...]
    sz = sigmoid(z)
    silu_z = z * sz
    yv = y[...]
    w = yv * silu_z
    dmv = dm[...]
    dw = r * gain[...] * dmv - w * kk
    gm_o[0:1, :] += jnp.sum(dmv * w * r, axis=0, keepdims=True)
    dy = dw * silu_z
    dz_o[...] = (dw * yv * sz * (1.0 + z * (1.0 - sz))).astype(BF16)
    gm_o[1:2, :] += jnp.sum(dy * x, axis=0, keepdims=True)

    grow = widen(cols, 8, heads)
    tail = widen(cols, 16, heads)
    dt_wide = widen(cols, 24, heads)
    x_low = x.astype(BF16)
    dy_low = dy.astype(BF16)
    state = states[0]
    state_low = state.astype(BF16)
    ds = dstate[...]
    ds_low = ds.astype(BF16)
    cross = dot_nt(b_low, c_low)
    shape = (rows, rows)
    upper = lax.broadcasted_iota(jnp.int32, shape, 0) <= lanes_of(shape)
    half = lanes_of(shape) < SSM_DIM
    lane = lanes_of(shape)
    dcross = jnp.zeros(shape, F32)
    col_sums = jnp.zeros(shape, F32)
    row_sums = []
    mids = []
    for p in range(heads // 2):
        span = slice(128 * p, 128 * p + 128)
        xpair, dypair = x_low[:, span], dy_low[:, span]
        zero = jnp.zeros_like(xpair)
        dys = (jnp.where(half, dypair, zero), jnp.where(half, zero, dypair))
        mats = []
        for k in range(2):
            h = 2 * p + k
            gap = jnp.where(upper, cum[h : h + 1, :] - cols[:, h : h + 1], neg_large)
            faded = jnp.exp(gap)
            mats.append((cross * faded).astype(BF16))
            t = dot_nt(xpair, dys[k]) * faded
            dt_col = cols[:, 24 + h : 25 + h]
            td = t * dt_col
            dcross = dcross + td
            row_sums.append(jnp.sum(td * cross, axis=0, keepdims=True))
            col = jnp.sum(t * cross, axis=1, keepdims=True)
            col_sums = jnp.where(lane == h, col, col_sums)
        mids.append(dot_nn(jnp.concatenate(mats, axis=1), jnp.concatenate(dys, axis=0)))
    mid = jnp.concatenate(mids, axis=1)
    row_sums = jnp.concatenate(row_sums + [jnp.zeros((8 - heads, rows), F32)], axis=0)
    col_sums = col_sums.T[0:8, :]

    dye = dy * grow
    dye_low = dye.astype(BF16)
    xd = x * tail
    xd_low = xd.astype(BF16)
    from_b = dot_nn(b_low, ds_low)
    through = dot_nn(c_low, state_low)
    dcross_low = dcross.astype(BF16)
    db = dot_nn(dcross_low, c_low) + dot_nt(xd_low, ds_low)
    dc = dot_tn(dcross_low, b_low) + dot_nt(dye_low, state_low)

    head_of = lax.broadcasted_iota(jnp.int32, (8, inner), 0)
    chan = lanes_of((8, inner)) // SSM_DIM
    ones = jnp.where(head_of == chan, 1.0, 0.0).astype(BF16)

    def by_head(v):
        high = v.astype(BF16)
        rest = (v - high.astype(F32)).astype(BF16)
        return dot_nt(ones, high) + dot_nt(ones, rest)

    grown = by_head(dye * through)
    ended = by_head(x * from_b)
    kept = jnp.sum(ds * state, axis=0, keepdims=True) * grow[rows - 1 :, :]
    kept = jnp.where(head_of == chan, kept, 0.0).sum(axis=1, keepdims=True)
    pulled = dt * fade * ended
    lane8 = lanes_of((8, rows))
    at_end = kept + jnp.sum(pulled, axis=1, keepdims=True)
    dcum = row_sums - dt * col_sums + grown - pulled + jnp.where(lane8 == rows - 1, at_end, 0.0)
    da = running_sum_back(dcum)
    ddt = col_sums + fade * ended + decay[...] * da
    dpre = ddt * sigmoid(pre)
    dt_o[...] = dpre
    gh_o[0:8, :] += da * dt * decay[...]
    gh_o[8:16, :] += dpre

    dstate[...] = grow[rows - 1 :, :] * ds + dot_tn(c_low, dye_low)
    dx = skip[...] * dy + dt_wide * mid + tail * from_b
    dux = dx * sx * (1.0 + ux * (1.0 - sx))
    dub = jnp.concatenate([db, dc], axis=1) * sb * (1.0 + ub * (1.0 - sb))
    for taps, src, d, buf, acc, out in (
        (tapx, xs, dux, dxs, gx_o, dx_o),
        (tapb, bs, dub, dbs, gb_o, db_o),
    ):
        buf[0:rows, :] = d
        total = taps[CONV - 1 : CONV, :] * d
        for j in range(CONV - 1):
            total = total + taps[j : j + 1, :] * buf[pl.ds(CONV - 1 - j, rows), :]
        out[...] = total.astype(BF16)
        for j in range(CONV):
            acc[j : j + 1, :] += jnp.sum(d * src[pl.ds(5 + j, rows), :], axis=0, keepdims=True)
        acc[CONV : CONV + 1, :] += jnp.sum(d, axis=0, keepdims=True)
        buf[rows : rows + 8, :] = d[0:8, :]


def scan_back(heads, channels, dm, y, zr, xr, br, trow, states, rsum, dots, gain, tapx, tapb, decay, bias, skip):
    total, inner = y.shape
    pair = br.shape[1]
    rows = block_len
    steps = total // rows
    per = rows // 8

    def whole(v):
        return pl.BlockSpec(v.shape, lambda i: (0,) * v.ndim)

    def tall(n):
        return pl.BlockSpec((rows, n), lambda i: (steps - 1 - i, 0))

    def before(n):
        return pl.BlockSpec((8, n), lambda i: (jnp.maximum((steps - 1 - i) * per - 1, 0), 0))

    wide = pl.BlockSpec((8, rows), lambda i: (0, steps - 1 - i))
    sds = jax.ShapeDtypeStruct

    def fixed(*shape):
        return pl.BlockSpec(shape, lambda i: (0, 0))

    return pl.pallas_call(
        partial(scan_back_kernel, heads, channels),
        grid=(steps,),
        in_specs=[tall(inner), tall(inner), tall(inner), tall(inner), before(inner), tall(pair),
                  before(pair), wide,
                  pl.BlockSpec((1, pair // 2, inner), lambda i: (steps - 1 - i, 0, 0)), wide, wide,
                  whole(gain), whole(tapx), whole(tapb), whole(decay), whole(bias), whole(skip)],
        out_specs=[tall(inner), tall(inner), tall(pair), wide, fixed(8, inner), fixed(8, pair),
                   fixed(8, inner), fixed(16, rows)],
        out_shape=[sds((total, inner), BF16), sds((total, inner), BF16), sds((total, pair), BF16),
                   sds((8, total), F32), sds((8, inner), F32), sds((8, pair), F32),
                   sds((8, inner), F32), sds((16, rows), F32)],
        scratch_shapes=[pltpu.VMEM((rows + 8, inner), F32), pltpu.VMEM((rows + 8, pair), F32),
                        pltpu.VMEM((rows + 8, inner), F32), pltpu.VMEM((rows + 8, pair), F32),
                        pltpu.VMEM((pair // 2, inner), F32)],
        compiler_params=pltpu.CompilerParams(vmem_limit_bytes=VMEM_LIMIT),
        cost_estimate=pl.CostEstimate(flops=int(4e9), bytes_accessed=int(15e6), transcendentals=int(5e6)),
        name="scan_back",
    )(dm, y, zr, xr, xr, br, br, trow, states, rsum, dots, gain, tapx, tapb,
      decay, bias, skip)


def whole_spec(v):
    return pl.BlockSpec(v.shape, lambda i: (0,) * v.ndim)


def feed_kernel(
    hid, gain, cot, whid, wdown, out_o, dh_o, dmix_o, gg_o, ghid_o, gdown_o, a2, a2t, acc, dacc
):
    step = pl.program_id(0)
    width = hid.shape[1]
    blocks = width // 128

    @pl.when(step == 0)
    def _():
        v = hid[...]
        f = lax.rsqrt(jnp.mean(v * v, axis=1, keepdims=True) + epsilon)
        low = (v * f * gain[...]).astype(BF16)
        a2[...] = low
        a2t[...] = low.T
        acc[...] = jnp.zeros(acc.shape, F32)
        dacc[...] = jnp.zeros(dacc.shape, F32)

    units = whid.shape[4]
    w_gate = whid[:, 0, 0].reshape(width, units)
    w_up = whid[:, 0, 1].reshape(width, units)
    w_down = jnp.concatenate([wdown[k, 0] for k in range(blocks)], axis=1)
    g = dot_nn(a2[...], w_gate)
    u = dot_nn(a2[...], w_up)
    s = sigmoid(g)
    f_low = (g * s * u).astype(BF16)
    c = cot[...]
    acc[...] += dot_nn(f_low, w_down)
    df = dot_nt(c, w_down)
    du = (df * g * s).astype(BF16)
    dg = (df * u * s * (1.0 + g * (1.0 - s))).astype(BF16)
    dacc[...] += dot_nt(dg, w_gate) + dot_nt(du, w_up)
    ghid_o[:, 0, 0] = dot_nn(a2t[...], dg).astype(BF16).reshape(blocks, 128, units)
    ghid_o[:, 0, 1] = dot_nn(a2t[...], du).astype(BF16).reshape(blocks, 128, units)
    gd = dot_tn(f_low, c).astype(BF16)
    for k in range(blocks):
        gdown_o[k, 0] = gd[:, 128 * k : 128 * k + 128]

    @pl.when(step == pl.num_programs(0) - 1)
    def _():
        v = hid[...]
        out_o[...] = (v + acc[...]).astype(BF16)
        f = lax.rsqrt(jnp.mean(v * v, axis=1, keepdims=True) + epsilon)
        dy = dacc[...]
        gg_o[...] = jnp.sum(dy * v * f, axis=0, keepdims=True)
        gdy = dy * gain[...]
        lean = jnp.sum(gdy * v, axis=1, keepdims=True) * (f * f * f / width)
        dh = cot[...].astype(F32) + (f * gdy - v * lean)
        dh_o[...] = dh
        dmix_o[...] = dh.astype(BF16)


def feed_forward(hid, gain, cot, whid, wdown):
    rows, width = hid.shape
    blocks, nt, _, depth, units = whid.shape
    tile = 256
    per = units // tile
    hid_spec = pl.BlockSpec((blocks, 1, 2, depth, tile), lambda i: (0, i // per, 0, 0, lax.rem(i, per)))
    down_spec = pl.BlockSpec((blocks, 1, tile, 128), lambda i: (0, i // per, lax.rem(i, per), 0))
    sds = jax.ShapeDtypeStruct

    def fixed(*shape):
        return pl.BlockSpec(shape, lambda i: (0, 0))

    return pl.pallas_call(
        feed_kernel,
        grid=(nt * per,),
        in_specs=[fixed(rows, width), fixed(1, width), fixed(rows, width), hid_spec, down_spec],
        out_specs=[fixed(rows, width), fixed(rows, width), fixed(rows, width), fixed(1, width), hid_spec,
                   down_spec],
        out_shape=[sds((rows, width), BF16), sds((rows, width), F32), sds((rows, width), BF16),
                   sds((1, width), F32), sds(whid.shape, BF16), sds(wdown.shape, BF16)],
        scratch_shapes=[pltpu.VMEM((rows, width), BF16), pltpu.VMEM((width, rows), BF16),
                        pltpu.VMEM((rows, width), F32), pltpu.VMEM((rows, width), F32)],
        compiler_params=pltpu.CompilerParams(vmem_limit_bytes=VMEM_LIMIT),
        cost_estimate=pl.CostEstimate(flops=int(1e10), bytes_accessed=int(26e6), transcendentals=int(5e5)),
        name="feed_forward",
    )(hid, gain, cot, whid, wdown)


def row_columns(rows_list, rows):
    return jnp.concatenate(
        [stack_columns([r[:, c : c + 128] for r in rows_list]) for c in range(0, rows, 128)], axis=0
    )


def down_kernel(dq, dz, dx, dkv, db, drow, wq, win, stp, wsh, part_o):
    total = dot_nt(dq[...], wq[...]) + dot_nt(dz[...], win[0]) + dot_nt(dx[...], win[1])
    total = total + dot_nt(dkv[...], wsh[:, 0:256]) + dot_nt(db[...], wsh[:, 256:])
    total = total + dot_tn(drow[...].astype(BF16), stp[...])
    part_o[...] = total.astype(BF16)


def down_parts(dq, dz, dx, dkv, db, drow, wq, win, stp, wsh):
    total, inner = dz.shape
    width = wq.shape[0]
    rows = 256

    def tall(v):
        return pl.BlockSpec((rows, v.shape[1]), lambda i: (i, 0))

    wide = pl.BlockSpec((8, rows), lambda i: (0, i))
    return pl.pallas_call(
        down_kernel,
        grid=(total // rows,),
        in_specs=[tall(dq), tall(dz), tall(dx), tall(dkv), tall(db), wide, whole_spec(wq), whole_spec(win),
                  whole_spec(stp), whole_spec(wsh)],
        out_specs=pl.BlockSpec((rows, width), lambda i: (i, 0)),
        out_shape=jax.ShapeDtypeStruct((total, width), BF16),
        compiler_params=pltpu.CompilerParams(vmem_limit_bytes=VMEM_LIMIT),
        cost_estimate=pl.CostEstimate(flops=int(3e9), bytes_accessed=int(8e6), transcendentals=0),
        name="down_parts",
    )(dq, dz, dx, dkv, db, drow, wq, win, stp, wsh)


def weight_kernel(a1, dq, dz, dx, dkv, db, drow, o, m, dmix, piece_o, shared_o, step_o, ot, mt):
    step = pl.program_id(0)

    @pl.when(step == 0)
    def _():
        ot[...] = o[...].T
        mt[...] = m[...].T

    a = a1[...]
    step_o[...] = dot_nn(drow[...].astype(BF16), a)
    at = a.T
    inner = dz.shape[1]

    def by_rows(values, first):
        for j in range(values.shape[1] // 128):
            piece_o[:, first + 128 * j : first + 128 * (j + 1), :] = (
                values[:, 128 * j : 128 * (j + 1)].reshape(2, 128, 128)
            )

    def by_lanes(values, first):
        n = values.shape[0]
        for k in range(2):
            piece_o[k, first : first + n, :] = values[:, 128 * k : 128 * (k + 1)]

    g = dmix[...]
    by_rows(dot_nn(at, dq[...]).astype(BF16), 0)
    by_lanes(dot_nn(ot[...], g).astype(BF16), 128)
    by_rows(dot_nn(at, dz[...]).astype(BF16), 256)
    by_rows(dot_nn(at, dx[...]).astype(BF16), 256 + inner)
    by_lanes(dot_nn(mt[...], g).astype(BF16), 256 + 2 * inner)
    shared_o[:, :, 0:256] = dot_nn(at, dkv[...]).astype(BF16).reshape(2, 128, 256)
    shared_o[:, :, 256:] = dot_nn(at, db[...]).astype(BF16).reshape(2, 128, db.shape[1])


def weight_pieces(a1, dq, dz, dx, dkv, db, drow, o, m, dmix):
    total, width = a1.shape
    inner = dz.shape[1]
    n = 256 + 3 * inner
    shared = 256 + db.shape[1]
    cols = pl.BlockSpec((total, 256), lambda i: (0, i))
    sds = jax.ShapeDtypeStruct
    args = (dq, dz, dx, dkv, db, drow, o, m)
    return pl.pallas_call(
        weight_kernel,
        grid=(width // 256,),
        in_specs=[cols] + [whole_spec(v) for v in args] + [cols],
        out_specs=[pl.BlockSpec((2, n, 128), lambda i: (i, 0, 0)),
                   pl.BlockSpec((2, 128, shared), lambda i: (i, 0, 0)),
                   pl.BlockSpec((8, 256), lambda i: (0, i))],
        out_shape=[sds((width // 128, n, 128), BF16), sds((width // 128, 128, shared), BF16),
                   sds((8, width), F32)],
        scratch_shapes=[pltpu.VMEM((128, total), BF16), pltpu.VMEM((inner, total), BF16)],
        compiler_params=pltpu.CompilerParams(vmem_limit_bytes=VMEM_LIMIT),
        cost_estimate=pl.CostEstimate(flops=int(4e9), bytes_accessed=int(12e6), transcendentals=0),
        name="weight_pieces",
    )(a1, *args, dmix)


def remote_copy(src, dst, send, recv, dev):
    return pltpu.make_async_remote_copy(
        src_ref=src, dst_ref=dst, send_sem=send, recv_sem=recv, device_id=dev, device_id_type=MESH
    )


def greet(peers):
    barrier = pltpu.get_barrier_semaphore()
    for peer in peers:
        pl.semaphore_signal(barrier, inc=1, device_id=peer, device_id_type=MESH)
    pl.semaphore_wait(barrier, len(peers))


def other_quarters(d, z, nt):
    return [(d, lax.rem(z + k, nt)) for k in range(1, nt)]


class Exchange:
    def __init__(self, own, landed, send, recv, d, z, nt):
        self.own, self.landed, self.z, self.nt = own, landed, z, nt
        self.copies = [
            remote_copy(own, landed.at[k - 1], send.at[k - 1], recv.at[k - 1], peer)
            for k, peer in enumerate(other_quarters(d, z, nt), 1)
        ]

    def start(self):
        for copy in self.copies:
            copy.start()

    def wait(self):
        for copy in self.copies:
            copy.wait()

    def total(self):
        total = None
        for q in range(self.nt):
            value = jnp.where(self.z == q, self.own[...].astype(F32), 0.0)
            for k in range(1, self.nt):
                value = value + jnp.where(
                    lax.rem(self.z - k + self.nt, self.nt) == q, self.landed[k - 1].astype(F32), 0.0
                )
            total = value if total is None else total + value
        return total


class ChainScatter:
    def __init__(self, parts, bufs, landed, send, recv, d, z, nt):
        self.parts, self.bufs, self.landed = parts, bufs, landed
        self.send, self.recv = send, recv
        self.d, self.z, self.nt = d, z, nt

    def active(self, way, t):
        z, nt = self.z, self.nt
        if way == 0:
            return (z <= t) & (z < nt - 1)
        return (nt - 1 - z <= t) & (z > 0)

    def copy(self, way, t):
        dev = (self.d, self.z + 1 if way == 0 else self.z - 1)
        return remote_copy(
            self.bufs.at[way, t], self.landed.at[way, t], self.send.at[way, t], self.recv.at[way, t], dev
        )

    def arrives(self, way, t):
        z, nt = self.z, self.nt
        if way == 0:
            return (z >= 1) & (z - 1 <= t)
        return (z < nt - 1) & (nt - 2 - z <= t)

    def step(self, t):
        z, nt = self.z, self.nt
        for way in range(2):
            q = nt - 1 - t + z if way == 0 else t - (nt - 1) + z

            def run():
                value = self.parts[q]
                if t > 0:
                    came = self.arrives(way, t - 1)

                    @pl.when(came)
                    def _():
                        self.copy(way, t - 1).wait_recv()
                        total = value.astype(F32) + self.landed[way, t - 1].astype(F32)
                        self.bufs[way, t] = total.astype(BF16)

                    @pl.when(jnp.logical_not(came))
                    def _():
                        self.bufs[way, t] = value
                else:
                    self.bufs[way, t] = value
                self.copy(way, t).start()

            pl.when(self.active(way, t))(run)

    def finish(self, out):
        out[...] = self.parts[self.z].astype(F32)
        t = self.nt - 2
        for way in range(2):

            @pl.when(self.arrives(way, t))
            def _():
                self.copy(way, t).wait_recv()
                out[...] += self.landed[way, t].astype(F32)

    def drain(self):
        for way in range(2):
            for t in range(self.nt - 1):
                pl.when(self.active(way, t))(self.copy(way, t).wait_send)


def chain_scratch(nt, rows, width):
    dma = pltpu.SemaphoreType.DMA
    return [
        pltpu.VMEM((2, nt - 1, rows, width), BF16),
        pltpu.VMEM((2, nt - 1, rows, width), BF16),
        dma((2, nt - 1)),
        dma((2, nt - 1)),
    ]


def mix_scatter_kernel(
    channels, nt, o, y, z_in, sq, gain, watt, wmam, tok,
    m_o, sq_o, hid_o,
    sq_land, sq_send, sq_recv, parts, bufs, landed, c_send, c_recv,
):
    d = lax.axis_index("dp")
    z = lax.axis_index("tensor")
    rows = tok.shape[0]
    greet(other_quarters(d, z, nt))
    squares = Exchange(sq, sq_land, sq_send, sq_recv, d, z, nt)
    squares.start()
    chain = ChainScatter(parts, bufs, landed, c_send, c_recv, d, z, nt)
    squares.wait()
    sq_o[...] = squares.total()

    def part(q):
        at = pl.ds(pl.multiple_of(q * rows, rows), rows)
        total = sq_o[:, at]
        r = row_columns([lax.rsqrt(total / channels + epsilon)], rows)[:, 0:1]
        zv = z_in[at, :]
        m = (y[at, :] * (zv * sigmoid(zv)) * r * gain[...]).astype(BF16)
        m_o[at, :] = m
        parts[q] = (dot_nn(o[at, :], watt[...]) + dot_nn(m, wmam[...])).astype(BF16)

    first = jnp.where(z < nt // 2, nt - 1, 0)
    part(first)
    chain.step(0)

    def rest(i, carry):
        part(lax.rem(first + 1 + i, nt))
        return carry

    lax.fori_loop(0, nt - 1, rest, 0)
    for t in range(1, nt - 1):
        chain.step(t)
    chain.finish(hid_o)
    hid_o[...] += tok[...].astype(F32)
    chain.drain()


def mix_scatter(channels, nt, o, y, zr, sq, gain, watt, wmam, tok):
    total, inner = y.shape
    rows, width = tok.shape
    dma = pltpu.SemaphoreType.DMA
    sds = jax.ShapeDtypeStruct
    vmem = pl.BlockSpec(memory_space=pltpu.VMEM)
    return pl.pallas_call(
        partial(mix_scatter_kernel, channels, nt),
        in_specs=[vmem] * 8,
        out_specs=[vmem] * 3,
        out_shape=[sds((total, inner), BF16), sds((8, total), F32), sds((rows, width), F32)],
        scratch_shapes=[pltpu.VMEM((nt - 1, 8, total), F32), dma((nt - 1,)), dma((nt - 1,)),
                        pltpu.VMEM((nt, rows, width), BF16)] + chain_scratch(nt, rows, width),
        compiler_params=pltpu.CompilerParams(
            vmem_limit_bytes=VMEM_LIMIT, collective_id=1, has_side_effects=True
        ),
        cost_estimate=pl.CostEstimate(flops=int(1e9), bytes_accessed=int(130e6), transcendentals=int(4e5)),
        name="mix_scatter",
    )(o, y, zr, sq, gain, watt, wmam, tok)


class ChainGather:
    def __init__(self, own, slots, send, recv, d, z, nt):
        self.own, self.slots, self.send, self.recv = own, slots, send, recv
        self.d, self.z, self.nt = d, z, nt

    def copy(self, way, dist):
        dev = (self.d, self.z + 1 if way == 0 else self.z - 1)
        slot = self.z - dist if way == 0 else self.z + dist
        src = self.own if dist == 0 else self.slots.at[slot]
        return remote_copy(src, self.slots.at[slot], self.send.at[way, dist], self.recv.at[way, dist], dev)

    def landing(self, way, dist):
        slot = self.z - dist if way == 0 else self.z + dist
        return remote_copy(
            self.slots.at[slot], self.slots.at[slot], self.send.at[way, dist - 1],
            self.recv.at[way, dist - 1], (self.d, self.z),
        )

    def has(self, way, dist):
        return self.z >= dist if way == 0 else self.z + dist < self.nt

    def goes_on(self, way):
        return self.z < self.nt - 1 if way == 0 else self.z > 0

    def start(self):
        for way in range(2):
            pl.when(self.goes_on(way))(self.copy(way, 0).start)

    def hop(self, dist):
        for way in range(2):
            pl.when(self.has(way, dist))(self.landing(way, dist).wait_recv)
            if dist < self.nt - 1:
                pl.when(self.has(way, dist) & self.goes_on(way))(self.copy(way, dist).start)

    def drain(self):
        for way in range(2):
            pl.when(self.goes_on(way))(self.copy(way, 0).wait_send)
            for dist in range(1, self.nt - 1):
                pl.when(self.has(way, dist) & self.goes_on(way))(self.copy(way, dist).wait_send)


def unmix_gather_kernel(
    nt, dmix, y, z_in, gain, watt, wmam,
    g_o, do_o, dm_o, dot_o,
    slots, g_send, g_recv, dot_own, dot_land, d_send, d_recv,
):
    d = lax.axis_index("dp")
    z = lax.axis_index("tensor")
    rows = dmix.shape[0]
    greet(other_quarters(d, z, nt))
    chain = ChainGather(dmix, slots, g_send, g_recv, d, z, nt)
    chain.start()

    def work(q, g):
        at = pl.ds(pl.multiple_of(q * rows, rows), rows)
        g_o[at, :] = g
        do_o[at, :] = dot_nt(g, watt[...]).astype(BF16)
        dm = dot_nt(g, wmam[...])
        dm_o[at, :] = dm
        zv = z_in[at, :]
        dots = jnp.sum(dm * gain[...] * (y[at, :] * (zv * sigmoid(zv))), axis=1, keepdims=True)
        turned = [jnp.broadcast_to(dots[c : c + 128], (128, 128)).T[0:8, :] for c in range(0, rows, 128)]
        dot_own[:, at] = jnp.concatenate(turned, axis=1)

    work(z, dmix[...])
    for dist in range(1, nt):
        chain.hop(dist)

        def side(way, carry):
            q = jnp.where(way == 0, z - dist, z + dist)

            @pl.when((q >= 0) & (q < nt))
            def _():
                work(q, slots[q])

            return carry

        lax.fori_loop(0, 2, side, 0)
    dots = Exchange(dot_own, dot_land, d_send, d_recv, d, z, nt)
    dots.start()
    chain.drain()
    dots.wait()
    dot_o[...] = dots.total()


def unmix_gather(nt, dmix, y, zr, gain, watt, wmam):
    total, inner = y.shape
    rows, width = dmix.shape
    dma = pltpu.SemaphoreType.DMA
    sds = jax.ShapeDtypeStruct
    vmem = pl.BlockSpec(memory_space=pltpu.VMEM)
    return pl.pallas_call(
        partial(unmix_gather_kernel, nt),
        in_specs=[vmem] * 6,
        out_specs=[vmem] * 4,
        out_shape=[sds((total, width), BF16), sds((total, 128), BF16), sds((total, inner), F32),
                   sds((8, total), F32)],
        scratch_shapes=[pltpu.VMEM((nt, rows, width), BF16), dma((2, nt - 1)), dma((2, nt - 1)),
                        pltpu.VMEM((8, total), F32), pltpu.VMEM((nt - 1, 8, total), F32),
                        dma((nt - 1,)), dma((nt - 1,))],
        compiler_params=pltpu.CompilerParams(
            vmem_limit_bytes=VMEM_LIMIT, collective_id=2, has_side_effects=True
        ),
        cost_estimate=pl.CostEstimate(flops=int(1e9), bytes_accessed=int(130e6), transcendentals=int(4e5)),
        name="unmix_gather",
    )(dmix, y, zr, gain, watt, wmam)


def add_refs(left, right):
    return left.astype(F32) + right.astype(F32)


class CubeScatter:
    def __init__(self, pieces, bufs, send, recv, peers, bits, z):
        (self.rc, self.held, self.r1, self.r2, self.ob, self.tb, self.r3, self.r4) = bufs
        self.p = pieces
        self.half = pieces.shape[3] // 2
        self.core, self.x, self.y = bits
        d_core, d_x, d_y = peers
        half = self.half
        n = pieces.shape[3]
        core, x, y = bits
        lo, hi = pl.ds(0, half), pl.ds(half, n - half)
        mk = remote_copy
        self.c0 = mk(pieces.at[:, :, 1 - core], self.rc, send.at[0], recv.at[0], (d_core, z))
        self.c1 = mk(self.held.at[:, 1 - x, lo], self.r1, send.at[1], recv.at[1], (d_x, z))
        self.c2 = mk(self.held.at[1 - y, :, hi], self.r2, send.at[2], recv.at[2], (d_y, z))
        self.c3 = mk(self.ob.at[1 - y], self.r3, send.at[3], recv.at[3], (d_y, z))
        self.c4 = mk(self.tb.at[1 - x], self.r4, send.at[4], recv.at[4], (d_x, z))

    def start(self):
        self.c0.start()

    def middle(self):
        self.c0.wait_recv()
        for i in range(2):
            for j in range(2):
                self.held[i, j] = add_refs(self.p[i, j, self.core], self.rc[i, j]).astype(BF16)
        self.c1.start()
        self.c2.start()

    def last(self):
        half = self.half
        self.c1.wait_recv()
        for i in range(2):
            self.ob[i] = add_refs(self.held[i, self.x, 0:half], self.r1[i]).astype(BF16)
        self.c3.start()
        self.c2.wait_recv()
        for i in range(2):
            self.tb[i] = add_refs(self.held[self.y, i, half:], self.r2[i]).astype(BF16)
        self.c4.start()

    def finish(self, out):
        half = self.half
        self.c3.wait_recv()
        out[0:half] = add_refs(self.ob[self.y], self.r3[...]).astype(out.dtype)
        self.c4.wait_recv()
        out[half:] = add_refs(self.tb[self.x], self.r4[...]).astype(out.dtype)

    def drain(self):
        for copy in (self.c0, self.c1, self.c2, self.c3, self.c4):
            copy.wait_send()


def cube_scratch(n, lanes):
    dma = pltpu.SemaphoreType.DMA
    half = n // 2
    return [
        pltpu.VMEM((2, 2, n, lanes), BF16),
        pltpu.VMEM((2, 2, n, lanes), BF16),
        pltpu.VMEM((2, half, lanes), BF16),
        pltpu.VMEM((2, n - half, lanes), BF16),
        pltpu.VMEM((2, half, lanes), BF16),
        pltpu.VMEM((2, n - half, lanes), BF16),
        pltpu.VMEM((half, lanes), BF16),
        pltpu.VMEM((n - half, lanes), BF16),
        dma((5,)),
        dma((5,)),
    ]


class CubeTotal:
    def __init__(self, held, landed, send, recv, peers, z):
        self.held, self.landed = held, landed
        self.copies = [
            remote_copy(held.at[i], landed.at[i], send.at[i], recv.at[i], (peer, z))
            for i, peer in enumerate(peers)
        ]

    def start(self, i):
        self.copies[i].start()

    def take(self, i):
        self.copies[i].wait_recv()
        self.held[i + 1] = self.held[i] + self.landed[i]

    def drain(self):
        for copy in self.copies:
            copy.wait_send()


def norm_back(dy, tok, gain, dh, out, ggain):
    v = tok[...].astype(F32)
    width = v.shape[1]
    f = lax.rsqrt(jnp.mean(v * v, axis=1, keepdims=True) + epsilon)
    ggain(jnp.sum(dy * v * f, axis=0, keepdims=True))
    gdy = dy * gain[...]
    lean = jnp.sum(gdy * v, axis=1, keepdims=True) * (f * f * f / width)
    out[...] = (dh[...] + (f * gdy - v * lean)).astype(BF16)


def tail_kernel(
    nt, n_all, parts, tok, gain, dh, pieces, shared, small,
    gt_o, mix_o, sh_o, small_o, norm_o,
    da, bufs, landed, c_send, c_recv, *rest,
):
    cube_a, rest = rest[:10], rest[10:]
    cube_b, rest = rest[:10], rest[10:]
    (sh_sum, sh_land, sh_send, sh_recv) = rest[:4]
    (sm_held, sm_land, sm_send, sm_recv, all_own, all_land, all_send, all_recv) = rest[4:12]
    (ng_held, ng_land, ng_send, ng_recv, ngz_land, ngz_send, ngz_recv) = rest[12:]
    d = lax.axis_index("dp")
    z = lax.axis_index("tensor")
    bits = dp_bits(d)
    core, x, y = bits
    peers = (d + 1 - 2 * core, d + 2 - 4 * x, d + 4 - 8 * y)
    greet([(p, z) for p in peers] + other_quarters(d, z, nt))
    chain = ChainScatter(parts, bufs, landed, c_send, c_recv, d, z, nt)
    chain.step(0)
    one = CubeScatter(pieces, cube_a[:8], cube_a[8], cube_a[9], peers, bits, z)
    two = CubeScatter(shared, cube_b[:8], cube_b[8], cube_b[9], peers, bits, z)
    sums = CubeTotal(sm_held, sm_land, sm_send, sm_recv, peers, z)
    sm_held[0] = small[...]
    sums.start(0)
    two.start()
    one.start()
    sums.take(0)
    sums.start(1)
    two.middle()
    one.middle()
    sums.take(1)
    sums.start(2)
    chain.step(1)
    sums.take(2)
    all_own[...] = sm_held[3, 0:n_all, :]
    over_all = Exchange(all_own, all_land, all_send, all_recv, d, z, nt)
    over_all.start()
    two.last()
    one.last()
    two.finish(sh_sum)
    per = sh_sum.shape[0] // nt
    copies = []
    for k in range(1, nt):
        q = lax.rem(z + k, nt)
        rows = pl.ds(pl.multiple_of(q * per, per), per)
        copies.append(
            remote_copy(sh_sum.at[rows], sh_land.at[k - 1], sh_send.at[k - 1], sh_recv.at[k - 1], (d, q))
        )
        copies[-1].start()
    for t in range(2, nt - 1):
        chain.step(t)
    one.finish(mix_o)
    small_o[...] = sm_held[3]
    over_all.wait()
    small_o[0:n_all, :] = over_all.total()
    for copy in copies:
        copy.wait()
    total = sh_sum[pl.ds(pl.multiple_of(z * per, per), per), :].astype(F32)
    for k in range(nt - 1):
        total = total + sh_land[k].astype(F32)
    sh_o[...] = total
    chain.finish(da)

    def keep(row):
        for k in range(8):
            ng_held[0, k : k + 1, :] = row[:, 128 * k : 128 * k + 128]

    norm_back(da[...], tok, gain, dh, gt_o, keep)
    norms = CubeTotal(ng_held, ng_land, ng_send, ng_recv, peers, z)
    for i in range(3):
        norms.start(i)
        norms.take(i)
    last = Exchange(ng_held.at[3], ngz_land, ngz_send, ngz_recv, d, z, nt)
    last.start()
    last.wait()
    norm_o[...] = last.total()
    for thing in (chain, one, two, sums, norms):
        thing.drain()


def tail(nt, n_all, parts, tok, gain, dh, pieces, shared, small):
    rows, width = tok.shape
    n, lanes = pieces.shape[1:]
    s_rows, s_lanes = shared.shape[1:]
    m_rows = small.shape[0]
    dma = pltpu.SemaphoreType.DMA
    sds = jax.ShapeDtypeStruct
    vmem = pl.BlockSpec(memory_space=pltpu.VMEM)
    pieces = pieces.reshape(2, 2, 2, n, lanes)
    shared = shared.reshape(2, 2, 2, s_rows, s_lanes)
    return pl.pallas_call(
        partial(tail_kernel, nt, n_all),
        in_specs=[vmem] * 7,
        out_specs=[vmem] * 5,
        out_shape=[sds((rows, width), BF16), sds((n, lanes), F32), sds((s_rows // nt, s_lanes), F32),
                   sds((m_rows, 128), F32), sds((8, 128), F32)],
        scratch_shapes=[pltpu.VMEM((rows, width), F32)] + chain_scratch(nt, rows, width)
        + cube_scratch(n, lanes) + cube_scratch(s_rows, s_lanes)
        + [pltpu.VMEM((s_rows, s_lanes), BF16), pltpu.VMEM((nt - 1, s_rows // nt, s_lanes), BF16),
           dma((nt - 1,)), dma((nt - 1,)),
           pltpu.VMEM((4, m_rows, 128), F32), pltpu.VMEM((3, m_rows, 128), F32), dma((3,)), dma((3,)),
           pltpu.VMEM((n_all, 128), F32), pltpu.VMEM((nt - 1, n_all, 128), F32), dma((nt - 1,)),
           dma((nt - 1,)),
           pltpu.VMEM((4, 8, 128), F32), pltpu.VMEM((3, 8, 128), F32), dma((3,)), dma((3,)),
           pltpu.VMEM((nt - 1, 8, 128), F32), dma((nt - 1,)), dma((nt - 1,))],
        compiler_params=pltpu.CompilerParams(
            vmem_limit_bytes=VMEM_LIMIT, collective_id=3, has_side_effects=True
        ),
        cost_estimate=pl.CostEstimate(flops=int(1e7), bytes_accessed=int(150e6), transcendentals=0),
        name="tail",
    )(parts, tok, gain, dh, pieces, shared, small)


def rope_wide(length):
    half = HEAD_SIZE // 2
    inverse = rope_base ** (-np.arange(half) * (2.0 / HEAD_SIZE))
    angles = np.arange(length)[:, None] * inverse[None, :]
    c, s = np.cos(angles), np.sin(angles)
    return (
        jnp.asarray(np.concatenate([c, c, c, c], axis=1), F32),
        jnp.asarray(np.concatenate([-s, s, -s, s], axis=1), F32),
    )


def to_blocks(full, axis, nt):
    if axis == 1:
        two, width, cols = full.shape
        return full.reshape(2, 8, width // 8, nt, cols // nt).transpose(1, 3, 0, 2, 4)
    rows, width = full.shape
    return full.reshape(nt, rows // nt, 8, width // 8).transpose(2, 0, 1, 3)


def per_device(
    nd,
    nt,
    tokens,
    query_proj,
    attend_out,
    inner_proj,
    step_proj,
    mamba_out,
    hidden_proj,
    down_proj,
    channel_taps,
    mixer_gain,
    decay_log,
    step_bias,
    skip_weight,
    shared_proj,
    norm_gains,
    shared_taps,
    cotangent,
):
    tensor_index = lax.axis_index("tensor")
    d = lax.axis_index("dp")
    local_rows, width = tokens.shape
    group_rows = local_rows * nt
    heads = step_proj.shape[1]
    inner = heads * SSM_DIM
    channels = inner * nt
    units = down_proj.shape[0]
    small_parts = [channel_taps, mixer_gain, norm_gains, shared_taps, step_proj.T]
    flat = jnp.concatenate([p.reshape(-1) for p in small_parts])
    small_len = -(-flat.shape[0] // 2048) * 2048
    small = jnp.pad(flat, (0, small_len - flat.shape[0])).reshape(-1, 128)
    (tok_full, full_query, full_attend, full_inner, full_mamba, sha, sma) = gather_start(
        tokens, query_proj, attend_out, inner_proj, mamba_out, shared_proj, small, nd, nt
    )
    hid_in, down_in = hidden_proj, down_proj
    if nd == 8:
        full_hidden = lax.all_gather(hid_in, ("dp", "tensor"), axis=0).reshape(
            (nd, nt) + hidden_proj.shape
        )
        full_down = lax.all_gather(down_in, ("dp", "tensor"), axis=0).reshape(
            (nd, nt) + down_proj.shape
        )
    else:
        full_hidden = lax.all_gather(hid_in, "tensor", axis=2, tiled=True)
        full_hidden = to_blocks(lax.all_gather(full_hidden, "dp", axis=1, tiled=True), 1, nt)
        full_down = lax.all_gather(down_in, "tensor", axis=0, tiled=True)
        full_down = to_blocks(lax.all_gather(full_down, "dp", axis=1, tiled=True), 0, nt)

    full_shared = sha.reshape(width, -1)
    sma = sma.reshape(nd, nt, small_len)

    def small_piece(index):
        start = sum(p.size for p in small_parts[:index])
        part = small_parts[index]
        return sma[:, :, start : start + part.size].reshape((nd, nt) + part.shape)

    taps_x = pick(small_piece(0), tensor_index, 1).transpose(1, 2, 0, 3).reshape(CONV + 1, inner)
    gain_mix = pick(small_piece(1), tensor_index, 1).transpose(1, 0, 2).reshape(1, inner)
    full_norms = small_piece(2).transpose(2, 0, 1, 3).reshape(2, width).astype(F32)
    taps_b = small_piece(3).transpose(2, 0, 1, 3).reshape(CONV + 1, -1)
    step_rows = pick(small_piece(4), tensor_index, 1).transpose(1, 0, 2).reshape(heads, width)
    step_rows = jnp.pad(step_rows, ((0, 8 - heads), (0, 0)))
    taps_x = jnp.pad(taps_x.astype(F32), ((0, 7 - CONV), (0, 0)))
    taps_b = jnp.pad(taps_b.astype(F32), ((0, 7 - CONV), (0, 0)))
    gain_mix = gain_mix.astype(F32)
    gain_first = full_norms[0:1]
    gain_second = full_norms[1:2]

    def head_rows(values):
        return jnp.pad(jnp.broadcast_to(values[:, None], (heads, 128)), ((0, 8 - heads), (0, 0)))

    decay = head_rows(-jnp.exp(decay_log.astype(F32)))
    bias = head_rows(step_bias.astype(F32))
    skip = jnp.repeat(skip_weight.astype(F32), SSM_DIM)[None, :]
    q_heads = query_proj.shape[1] // HEAD_SIZE
    kv_head = (tensor_index * q_heads // (QHEADS // KVHEADS)).astype(jnp.int32).reshape(1)
    cosine, sine = rope_wide(group_rows)

    (a1, q, k2, v2, lse, o, xr, zr, br, y, trow, states, squares) = mixers_forward(
        heads, kv_head, tok_full.reshape(group_rows, width), gain_first, full_query, full_inner, step_rows,
        full_shared, cosine, sine, taps_x, taps_b, decay, bias, skip,
    )
    m, squares, hidden = mix_scatter(
        channels, nt, o, y, zr, squares, gain_mix, full_attend, full_mamba, tokens
    )
    layer_out, dh, dmix, grad_gain_two, hid_pieces, down_pieces = feed_forward(
        hidden, gain_second, cotangent, full_hidden, full_down
    )
    grad_mix, do, dm, dots = unmix_gather(nt, dmix, y, zr, gain_mix, full_attend, full_mamba)
    if nd == 8:
        hid_sum = cube_scatter(hid_pieces, nd, BF16)
        down_sum = cube_scatter(down_pieces, nd, BF16)
        gradient_hidden = chain_scatter(hid_sum, nt)
        gradient_down = chain_scatter(down_sum, nt)
    else:
        hid_full = hid_pieces.transpose(2, 0, 3, 1, 4).reshape(2, nd, width // nd, nt, units)
        hid_sum = cube_scatter(hid_full.transpose(1, 3, 0, 2, 4), nd, BF16)
        down_full = down_pieces.transpose(1, 2, 0, 3).reshape(nt, units, nd, width // nd)
        down_sum = cube_scatter(down_full.transpose(2, 0, 1, 3), nd, BF16)
        gradient_hidden = chain_scatter(hid_sum, nt)
        gradient_down = chain_scatter(down_sum, nt)

    dq, dkv = attend_back(kv_head, q, k2, v2, lse, do, cosine, sine)
    dz, dx, db, drow, grad_tx, grad_tb, grad_rows, grad_heads = scan_back(
        heads, channels, dm, y, zr, xr, br, trow, states, squares, dots, gain_mix, taps_x, taps_b, decay, bias,
        skip,
    )
    part_one = down_parts(dq, dz, dx, dkv, db, drow, full_query, full_inner, step_rows, full_shared)
    pieces, shared_pieces, grad_step = weight_pieces(a1, dq, dz, dx, dkv, db, drow, o, m, grad_mix)
    block = width // nd
    q_cols = query_proj.shape[1]
    cuts = [0, q_cols, q_cols + attend_out.shape[0]]
    cuts += [cuts[2] + inner, cuts[2] + 2 * inner, cuts[2] + 3 * inner]

    def from_rows(values):
        return values.reshape(8, -1, 128, 128).transpose(0, 2, 1, 3).reshape(width, -1)

    def from_lanes(values):
        return values.transpose(1, 0, 2).reshape(-1, width)

    n_tap = CONV + 1
    over_all = jnp.concatenate([grad_gain_two.reshape(-1), grad_tb[:n_tap].reshape(-1)])
    over_dp = jnp.concatenate(
        [
            grad_tx[:n_tap].reshape(-1),
            grad_rows[0],
            grad_rows[1].reshape(heads, SSM_DIM).sum(axis=1),
            grad_heads[:heads].sum(axis=1),
            grad_heads[8 : 8 + heads].sum(axis=1),
            grad_step[:heads].reshape(-1),
        ]
    )

    def in_rows(values):
        return jnp.pad(values, (0, -values.shape[0] % 1024)).reshape(-1, 128)

    rows_all = in_rows(over_all)
    n_all = rows_all.shape[0]
    small_sums = jnp.concatenate([rows_all, in_rows(over_dp)], axis=0)
    parts = part_one.reshape(nt, local_rows, width)
    if nd == 8:
        gradient_tokens, mixer_sum, gradient_shared, small_sums, grad_gain_one = tail(
            nt, n_all, parts, tokens, gain_first, dh, pieces, shared_pieces, small_sums
        )
        grad_gain_one = grad_gain_one.reshape(1, width)
        got = [mixer_sum[cuts[i] : cuts[i + 1]] for i in range(5)]

        def back_rows(values):
            return values.reshape(-1, 128, 128).transpose(1, 0, 2).reshape(128, -1)

        gradient_query = back_rows(got[0])
        gradient_attend = got[1]
        gradient_inner = jnp.stack([back_rows(got[2]), back_rows(got[3])])
        gradient_mamba = got[4]
    else:
        token_f32 = tokens.astype(F32)
        _, norm_one_back = jax.vjp(norm_apply, token_f32, gain_first[0])
        grad_from_one, grad_gain_one = norm_one_back(chain_scatter(parts, nt))
        gradient_tokens = (dh + grad_from_one).astype(BF16)
        got = [pieces[:, cuts[i] : cuts[i + 1]] for i in range(5)]

        def over_rows(values):
            return cube_scatter(from_rows(values).reshape(nd, block, -1), nd)

        def over_lanes(values):
            return cube_scatter(from_lanes(values).reshape(-1, nd, block).transpose(1, 0, 2), nd)

        gradient_query = over_rows(got[0])
        gradient_attend = over_lanes(got[1])
        gradient_inner = jnp.stack([over_rows(got[2]), over_rows(got[3])])
        gradient_mamba = over_lanes(got[4])
        shared_cut = shared_pieces.reshape(nd, nt, width // (nd * nt), -1)
        gradient_shared = chain_scatter(cube_scatter(shared_cut, nd, BF16), nt)
        small_sums = lax.psum(small_sums, "dp")
        small_sums = jnp.concatenate(
            [lax.psum(small_sums[:n_all], "tensor"), small_sums[n_all:]], axis=0
        )
        grad_gain_one = lax.psum(grad_gain_one, ("dp", "tensor")).reshape(1, width)
    over_all = small_sums[:n_all].reshape(-1)
    over_dp = small_sums[n_all:].reshape(-1)
    place = d * nt + tensor_index
    norm_w = width // (nd * nt)
    both_norms = jnp.concatenate([grad_gain_one, over_all[:width].reshape(1, width)], axis=0)
    gradient_norms = lax.dynamic_slice_in_dim(both_norms, place * norm_w, norm_w, 1)
    tap_w = shared_taps.shape[1]
    tap_all = over_all[width : width + n_tap * taps_b.shape[1]].reshape(n_tap, -1)
    gradient_taps = lax.dynamic_slice_in_dim(tap_all, place * tap_w, tap_w, 1)
    part = mixer_gain.shape[1]
    n_taps = n_tap * inner
    chan = over_dp[:n_taps].reshape(n_tap, heads, SSM_DIM)
    gain = over_dp[n_taps : n_taps + inner].reshape(heads, SSM_DIM)
    gradient_channel = lax.dynamic_slice_in_dim(chan, d * part, part, 2)
    gradient_mixer = lax.dynamic_slice_in_dim(gain, d * part, part, 1)
    rest = over_dp[n_taps + inner :]
    gradient_skip = rest[:heads]
    gradient_decay = rest[heads : 2 * heads]
    gradient_bias = rest[2 * heads : 3 * heads]
    step_all = rest[3 * heads : 3 * heads + heads * width].reshape(heads, width)
    gradient_step = lax.dynamic_slice_in_dim(step_all, d * block, block, 1).T
    return (
        layer_out,
        gradient_tokens,
        gradient_query,
        gradient_attend,
        gradient_inner,
        gradient_step,
        gradient_mamba,
        gradient_hidden,
        gradient_down,
        gradient_channel,
        gradient_mixer,
        gradient_decay,
        gradient_bias,
        gradient_skip,
        gradient_shared,
        gradient_norms,
        gradient_taps,
    )


def solution(mesh):
    placed = (
        P(("dp", "tensor"), None),
        P("dp", "tensor"),
        P("tensor", "dp"),
        P(None, "dp", "tensor"),
        P("dp", "tensor"),
        P("tensor", "dp"),
        P(None, "dp", "tensor"),
        P("tensor", "dp"),
        P(None, "tensor", "dp"),
        P("tensor", "dp"),
        P("tensor"),
        P("tensor"),
        P("tensor"),
        P(("dp", "tensor"), None),
        P(None, ("dp", "tensor")),
        P(None, ("dp", "tensor")),
        P(("dp", "tensor"), None),
    )
    return jax.shard_map(
        partial(per_device, mesh.shape["dp"], mesh.shape["tensor"]),
        mesh=mesh,
        in_specs=placed,
        out_specs=(
            P(("dp", "tensor"), None),
            P(("dp", "tensor"), None),
            P("dp", "tensor"),
            P("tensor", "dp"),
            P(None, "dp", "tensor"),
            P("dp", "tensor"),
            P("tensor", "dp"),
            P(None, "dp", "tensor"),
            P("tensor", "dp"),
            P(None, "tensor", "dp"),
            P("tensor", "dp"),
            P("tensor"),
            P("tensor"),
            P("tensor"),
            P(("dp", "tensor"), None),
            P(None, ("dp", "tensor")),
            P(None, ("dp", "tensor")),
        ),
        check_vma=False,
    )
```

```python
from functools import partial

import numpy as np
import jax
import jax.numpy as jnp
from jax import lax
from jax.experimental import pallas as pl
from jax.experimental.pallas import tpu as pltpu
from jax.sharding import PartitionSpec as P

MESH = pl.DeviceIdType.MESH

QHEADS = 8
KVHEADS = 2
HEAD_SIZE = 64
SSM_DIM = 64
CONV = 4


epsilon = 1e-05
rope_base = 100000000000.0
neg_large = -1e30
block_len = 128


def norm_apply(values, gain):
    factor = lax.rsqrt(jnp.mean(values * values, axis=-1, keepdims=True) + epsilon)
    return values * factor * gain


def dp_bits(index):
    core = lax.rem(index, 2)
    xbit = lax.rem(index // 2, 2)
    ybit = lax.rem(index // 4, 2)
    return core, xbit, ybit


def remote_copy(src, dst, send, recv, dev):
    return pltpu.make_async_remote_copy(
        src_ref=src, dst_ref=dst, send_sem=send, recv_sem=recv, device_id=dev, device_id_type=MESH
    )


def greet(peers):
    barrier = pltpu.get_barrier_semaphore()
    for peer in peers:
        pl.semaphore_signal(barrier, inc=1, device_id=peer, device_id_type=MESH)
    pl.semaphore_wait(barrier, len(peers))


def other_quarters(d, z, nt):
    return [(d, lax.rem(z + k, nt)) for k in range(1, nt)]


def cube_peers(d):
    core, xbit, ybit = dp_bits(d)
    return d + 1 - 2 * core, d + 2 - 4 * xbit, d + 4 - 8 * ybit


class CubeGather:
    def __init__(self, items, via_y, send, recv, d, z):
        self.items, self.via_y, self.send, self.recv = items, via_y, send, recv
        self.d, self.z = d, z
        self.d_core, self.d_x, self.d_y = cube_peers(d)
        self.d_xy = self.d_x + self.d_y - d
        self.sent = []

    def push(self, i, j, src, dst, peer):
        copy = remote_copy(src, dst, self.send.at[i, j], self.recv.at[i, j], (peer, self.z))
        copy.start()
        self.sent.append(copy)

    def landed(self, i, j, slot):
        at = self.items[i][1]
        remote_copy(
            at(slot), at(slot), self.send.at[i, j], self.recv.at[i, j], (self.d_core, self.z)
        ).wait_recv()

    def start(self, i):
        src, at = self.items[i]
        for j, peer in enumerate((self.d_x, self.d_y, self.d_core)):
            self.push(i, j, src, at(self.d), peer)

    def near(self, i):
        at = self.items[i][1]
        d_x, d_y, d_core = self.d_x, self.d_y, self.d_core
        self.landed(i, 0, d_x)
        if i in self.via_y:
            self.push(i, 3, at(d_x), at(d_x), d_y)
        self.push(i, 4, at(d_x), at(d_x), d_core)
        self.landed(i, 1, d_y)
        if i not in self.via_y:
            self.push(i, 3, at(d_y), at(d_y), d_x)
        self.push(i, 5, at(d_y), at(d_y), d_core)

    def far(self, i):
        at = self.items[i][1]
        self.landed(i, 3, self.d_xy)
        self.push(i, 6, at(self.d_xy), at(self.d_xy), self.d_core)

    def finish(self):
        for i in range(len(self.items)):
            self.landed(i, 2, self.d_core)
            for j in (4, 5, 6):
                self.landed(i, j, self.d_core)
        for copy in self.sent:
            copy.wait_send()


def gather_kernel(nt, *refs):
    (tok, que, att, inn, mam, hid, dwn, sha, sma) = refs[:9]
    (tok_f, que_f, att_f, inn_f, mam_f, hid_f, dwn_f, sha_f, sma_f) = refs[9:18]
    (lsem, zs_send, zs_recv, t_send, t_recv, d_send, d_recv) = refs[18:]
    d = lax.axis_index("dp")
    z = lax.axis_index("tensor")
    greet([(p, z) for p in cube_peers(d)] + other_quarters(d, z, nt))

    small = []
    for i, (src, dst) in enumerate(((sha, sha_f), (sma, sma_f))):
        for k, peer in enumerate(other_quarters(d, z, nt)):
            small.append(remote_copy(src, dst.at[d, z], zs_send.at[i, k], zs_recv.at[i, k], peer))
            small[-1].start()
    q_rows = que.shape[0]
    cols = att.shape[1]
    i_rows = inn.shape[1]
    items = [
        (inn, lambda s: inn_f.at[:, pl.ds(s * i_rows, i_rows)]),
        (que, lambda s: que_f.at[pl.ds(s * q_rows, q_rows)]),
        (att, lambda s: att_f.at[:, pl.ds(pl.multiple_of(s * cols, cols), cols)]),
        (mam, lambda s: mam_f.at[:, pl.ds(pl.multiple_of(s * cols, cols), cols)]),
        (hid, lambda s: hid_f.at[s, z]),
        (dwn, lambda s: dwn_f.at[s, z]),
        (sha_f.at[d], lambda s: sha_f.at[s]),
        (sma_f.at[d], lambda s: sma_f.at[s]),
    ]
    cube = CubeGather(items, (0, 5, 7), d_send, d_recv, d, z)
    locals_ = []
    for i, (src, dst) in enumerate(
        [(sha, sha_f.at[d, z]), (sma, sma_f.at[d, z]), (tok, tok_f.at[z])]
        + [(src, at(d)) for src, at in items[:6]]
    ):
        copy = pltpu.make_async_copy(src, dst, lsem.at[i])
        copy.start()
        locals_.append(copy)
    for i in range(4):
        cube.start(i)
    chain = ChainGather(tok, tok_f, t_send, t_recv, d, z, nt)
    chain.start()
    locals_[0].wait()
    locals_[1].wait()
    for copy in small:
        copy.wait()
    cube.start(6)
    cube.start(7)
    cube.start(4)
    cube.start(5)
    for i in range(4):
        cube.near(i)
    chain.hop(1)
    for i in (6, 7, 4, 5):
        cube.near(i)
    for i in (0, 1, 2, 3, 6, 7):
        cube.far(i)
    for dist in range(2, nt - 1):
        chain.hop(dist)
    cube.far(4)
    cube.far(5)
    if nt > 2:
        chain.hop(nt - 1)
    cube.finish()
    for copy in locals_[2:]:
        copy.wait()
    chain.drain()


def gather_start(tok, que, att, inn, mam, hid, dwn, sha, sma, nd, nt):
    if nd != 8:
        shared = lax.all_gather(sha, ("dp", "tensor"), axis=0)
        small = lax.all_gather(sma, ("dp", "tensor"), axis=0)
        return (
            lax.all_gather(tok, "tensor", axis=0),
            lax.all_gather(que, "dp", axis=0, tiled=True),
            lax.all_gather(att, "dp", axis=1, tiled=True),
            lax.all_gather(inn, "dp", axis=1, tiled=True),
            lax.all_gather(mam, "dp", axis=1, tiled=True),
            None,
            None,
            shared.reshape((nd, nt) + sha.shape),
            small.reshape((nd, nt) + sma.shape),
        )
    bf = jnp.bfloat16
    outs = (
        (nt,) + tok.shape,
        (nd * que.shape[0], que.shape[1]),
        (att.shape[0], nd * att.shape[1]),
        (2, nd * inn.shape[1], inn.shape[2]),
        (mam.shape[0], nd * mam.shape[1]),
        (nd, nt) + hid.shape,
        (nd, nt) + dwn.shape,
        (nd, nt) + sha.shape,
        (nd, nt) + sma.shape,
    )
    anywhere = pl.BlockSpec(memory_space=pl.ANY)
    dma = pltpu.SemaphoreType.DMA
    return pl.pallas_call(
        partial(gather_kernel, nt),
        out_shape=[jax.ShapeDtypeStruct(s, bf) for s in outs],
        in_specs=[anywhere] * 9,
        out_specs=[anywhere] * 9,
        scratch_shapes=[
            dma((9,)), dma((2, nt)), dma((2, nt)), dma((2, nt)), dma((2, nt)),
            dma((8, 7)), dma((8, 7)),
        ],
        compiler_params=pltpu.CompilerParams(collective_id=0, has_side_effects=True),
        name="gather_start",
    )(tok, que, att, inn, mam, hid, dwn, sha, sma)


def pick(values, index, axis=0):
    return lax.dynamic_index_in_dim(values, index, axis, keepdims=False)


def add_low(left, right):
    return (left.astype(jnp.float32) + right.astype(jnp.float32)).astype(jnp.bfloat16)


def chain_scatter(parts, nt):
    z = lax.axis_index("tensor")
    right = left = None
    for t in range(nt - 1):
        to_right = pick(parts, jnp.clip(nt - 1 - t + z, 0, nt - 1))
        to_left = pick(parts, jnp.clip(t - (nt - 1) + z, 0, nt - 1))
        if t > 0:
            to_right = add_low(to_right, right)
            to_left = add_low(to_left, left)
        right = lax.ppermute(to_right, "tensor", [(i, i + 1) for i in range(t + 1)])
        left = lax.ppermute(
            to_left, "tensor", [(nt - 1 - i, nt - 2 - i) for i in range(t + 1)]
        )
    f32 = jnp.float32
    return pick(parts, z).astype(f32) + right.astype(f32) + left.astype(f32)


def cube_scatter(parts, nd, last=jnp.float32):
    return lax.psum_scatter(parts, "dp", scatter_dimension=0, tiled=False).astype(last)


F32, BF16 = jnp.float32, jnp.bfloat16
VMEM_LIMIT = 56 * 1024 * 1024


def dot_nn(a, b):
    return lax.dot_general(a, b, (((1,), (0,)), ((), ())), preferred_element_type=F32)


def dot_nt(a, b):
    return lax.dot_general(a, b, (((1,), (1,)), ((), ())), preferred_element_type=F32)


def dot_tn(a, b):
    return lax.dot_general(a, b, (((0,), (0,)), ((), ())), preferred_element_type=F32)


def sigmoid(v):
    return 1.0 / (1.0 + jnp.exp(-v))


def lanes_of(shape):
    return lax.broadcasted_iota(jnp.int32, shape, len(shape) - 1)


def turn(values, cosine, sine):
    lane = lanes_of(values.shape)
    other = jnp.where(
        lax.rem(lane, HEAD_SIZE) < HEAD_SIZE // 2,
        pltpu.roll(values, 128 - HEAD_SIZE // 2, 1),
        pltpu.roll(values, HEAD_SIZE // 2, 1),
    )
    return values * cosine + other * sine


def softplus(v):
    return jnp.maximum(v, 0.0) + jnp.log1p(jnp.exp(-jnp.abs(v)))


def running_sum(rows):
    lane = lanes_of(rows.shape)
    step = 1
    while step < rows.shape[1]:
        rows = rows + jnp.where(lane >= step, pltpu.roll(rows, step, 1), 0.0)
        step *= 2
    return rows


def running_sum_back(rows):
    lane = lanes_of(rows.shape)
    width = rows.shape[1]
    step = 1
    while step < width:
        rows = rows + jnp.where(lane < width - step, pltpu.roll(rows, width - step, 1), 0.0)
        step *= 2
    return rows


def stack_columns(rows_list):
    used = sum(r.shape[0] for r in rows_list)
    filler = jnp.zeros((128 - used, 128), F32)
    return jnp.concatenate(rows_list + [filler], axis=0).T


def widen(cols, base, heads):
    low = lanes_of((cols.shape[0], 128)) < SSM_DIM
    return jnp.concatenate(
        [
            jnp.where(low, cols[:, base + 2 * p : base + 2 * p + 1],
                      cols[:, base + 2 * p + 1 : base + 2 * p + 2])
            for p in range(heads // 2)
        ],
        axis=1,
    )


def conv_rows(ref, taps, first, rows):
    total = taps[CONV : CONV + 1, :] + taps[0:1, :] * ref[pl.ds(first, rows), :]
    for j in range(1, CONV):
        total = total + taps[j : j + 1, :] * ref[pl.ds(first + j, rows), :]
    return total


def forward_kernel(
    heads, kvh, tok, gain, wq, win, stp, wsh, cosine, sine, tapx, tapb, decay, bias, skip,
    a1_o, q_o, k_o, v_o, lse_o, o_o, x_o, z_o, b_o, y_o, t_o, s_o, sq_o,
    keys, vals, xs, bs, state,
):
    step = pl.program_id(0)
    rows = tok.shape[0]
    second = kvh[0] == 1

    @pl.when(step == 0)
    def _():
        xs[0:8, :] = jnp.zeros((8, xs.shape[1]), F32)
        bs[0:8, :] = jnp.zeros((8, bs.shape[1]), F32)
        state[...] = jnp.zeros(state.shape, F32)

    t = tok[...].astype(F32)
    r = lax.rsqrt(jnp.mean(t * t, axis=1, keepdims=True) + epsilon)
    a1 = (t * r * gain[...]).astype(BF16)
    a1_o[...] = a1
    q = turn(dot_nn(a1, wq[...]), cosine[...], sine[...]).astype(BF16)
    q_o[...] = q
    s = dot_nn(a1, wsh[...])
    low = lanes_of((rows, 128)) < HEAD_SIZE
    k = turn(s[:, :128], cosine[...], sine[...])
    v = s[:, 128:256]
    pick_own = low != second
    k2 = jnp.where(pick_own, k, pltpu.roll(k, 64, 1)).astype(BF16)
    v2 = jnp.where(pick_own, v, pltpu.roll(v, 64, 1))
    k_o[...] = k2
    v_o[...] = v2.astype(BF16)
    place = pl.ds(pl.multiple_of(step * rows, rows), rows)
    keys[place, :] = k2
    vals[:, place] = v2.T.astype(BF16)

    scale = HEAD_SIZE**-0.5

    def attend(blocks):
        n = blocks * rows
        shape = (rows, rows)
        allowed = lax.broadcasted_iota(jnp.int32, shape, 0) <= lanes_of(shape)
        parts = []
        for h in range(2):
            qh = jnp.where(low == (h == 0), q, jnp.zeros_like(q))
            sc = dot_nt(keys[0:n, :], qh) * scale
            last = jnp.where(allowed, sc[n - rows :, :], neg_large)
            sc = jnp.concatenate([sc[: n - rows, :], last], axis=0) if blocks > 1 else last
            top = jnp.max(sc, axis=0, keepdims=True)
            e = jnp.exp(sc - top)
            total = jnp.sum(e, axis=0, keepdims=True)
            lse_o[h : h + 1, :] = top + jnp.log(total)
            parts.append(dot_nn(vals[:, 0:n], e.astype(BF16)) / total)
        sub = lax.broadcasted_iota(jnp.int32, parts[0].shape, 0)
        o_o[...] = jnp.where(sub < HEAD_SIZE, parts[0], parts[1]).T.astype(BF16)

    for i in range(keys.shape[0] // rows):
        pl.when(step == i)(partial(attend, i + 1))

    zr = dot_nn(a1, win[0])
    z_o[...] = zr
    xr = dot_nn(a1, win[1])
    x_o[...] = xr
    br = s[:, 256:]
    b_o[...] = br
    xs[8 : 8 + rows, :] = xr
    bs[8 : 8 + rows, :] = br
    u = conv_rows(xs, tapx, 5, rows)
    x = u * sigmoid(u)
    u = conv_rows(bs, tapb, 5, rows)
    bc = (u * sigmoid(u)).astype(BF16)
    xs[0:8, :] = xs[rows : rows + 8, :]
    bs[0:8, :] = bs[rows : rows + 8, :]
    tr = dot_nt(stp[...], a1)
    t_o[...] = tr
    n_state = bc.shape[1] // 2
    tri_shape = (block_len, block_len)
    lower = lax.broadcasted_iota(jnp.int32, tri_shape, 0) >= lanes_of(tri_shape)
    half = lanes_of(tri_shape) < SSM_DIM
    for c in range(rows // block_len):
        part = slice(c * block_len, (c + 1) * block_len)
        dt = softplus(tr[:, part] + bias[...])
        cum = running_sum(dt * decay[...])
        end = cum[:, block_len - 1 :]
        cols = stack_columns([cum, jnp.exp(cum), dt * jnp.exp(end - cum)])
        xc = x[part]
        x_low = xc.astype(BF16)
        b_low = bc[part, :n_state]
        c_low = bc[part, n_state:]
        cross = dot_nt(c_low, b_low)
        grow = widen(cols, 8, heads)
        y = dot_nn(c_low, state[...].astype(BF16)) * grow + skip[...] * xc
        inner = []
        for p in range(heads // 2):
            mats = []
            for h in (2 * p, 2 * p + 1):
                gap = jnp.where(lower, cols[:, h : h + 1] - cum[h : h + 1, :], neg_large)
                mats.append((cross * jnp.exp(gap) * dt[h : h + 1, :]).astype(BF16))
            xp = x_low[:, 128 * p : 128 * p + 128]
            zero = jnp.zeros_like(xp)
            both = jnp.concatenate([jnp.where(half, xp, zero), jnp.where(half, zero, xp)], axis=0)
            inner.append(dot_nn(jnp.concatenate(mats, axis=1), both))
        y = y + jnp.concatenate(inner, axis=1)
        y_o[part, :] = y
        s_o[c] = state[...]
        carried = (xc * widen(cols, 16, heads)).astype(BF16)
        state[...] = grow[block_len - 1 :, :] * state[...] + dot_tn(b_low, carried)
        zc = zr[part]
        w = y * (zc * sigmoid(zc))
        total = jnp.sum(w * w, axis=1, keepdims=True)
        sq_o[:, part] = jnp.broadcast_to(total, (block_len, 128)).T[0:8, :]


def mixers_forward(heads, kvh, tok, gain, wq, win, stp, wsh, cosine, sine, tapx, tapb, decay, bias, skip):
    total, width = tok.shape
    rows = 256
    inner = heads * SSM_DIM
    pair = wsh.shape[1] - 256
    state = pair // 2
    chunks = rows // block_len

    def whole(v):
        return pl.BlockSpec(v.shape, lambda i: (0,) * v.ndim)

    def tall(n):
        return pl.BlockSpec((rows, n), lambda i: (i, 0))

    wide = pl.BlockSpec((8, rows), lambda i: (0, i))
    sds = jax.ShapeDtypeStruct
    return pl.pallas_call(
        partial(forward_kernel, heads),
        grid=(total // rows,),
        in_specs=[pl.BlockSpec(memory_space=pltpu.SMEM), tall(width), whole(gain), whole(wq), whole(win),
                  whole(stp), whole(wsh), tall(128), tall(128), whole(tapx), whole(tapb),
                  whole(decay), whole(bias), whole(skip)],
        out_specs=[tall(width), tall(128), tall(128), tall(128), wide, tall(128), tall(inner),
                   tall(inner), tall(pair), tall(inner), wide,
                   pl.BlockSpec((chunks, state, inner), lambda i: (i, 0, 0)), wide],
        out_shape=[sds((total, width), BF16), sds((total, 128), BF16), sds((total, 128), BF16),
                   sds((total, 128), BF16), sds((8, total), F32), sds((total, 128), BF16),
                   sds((total, inner), F32), sds((total, inner), F32), sds((total, pair), F32),
                   sds((total, inner), F32), sds((8, total), F32),
                   sds((total // block_len, state, inner), F32), sds((8, total), F32)],
        scratch_shapes=[pltpu.VMEM((total, 128), BF16), pltpu.VMEM((128, total), BF16),
                        pltpu.VMEM((rows + 8, inner), F32), pltpu.VMEM((rows + 8, pair), F32),
                        pltpu.VMEM((state, inner), F32)],
        compiler_params=pltpu.CompilerParams(vmem_limit_bytes=VMEM_LIMIT),
        cost_estimate=pl.CostEstimate(flops=int(5e9), bytes_accessed=int(15e6), transcendentals=int(4e6)),
        name="mixers_forward",
    )(kvh, tok, gain, wq, win, stp, wsh, cosine, sine, tapx, tapb, decay, bias, skip)


def attend_back_kernel(kvh, q, k2, v2, lse, do, cosine, sine, cos_all, sin_all, dq_o, dkv_o, dk, dv):
    step = pl.program_id(0)
    rows = q.shape[0]
    steps = k2.shape[0] // rows
    scale = HEAD_SIZE**-0.5
    low = lanes_of((rows, 128)) < HEAD_SIZE

    @pl.when(step == 0)
    def _():
        dk[...] = jnp.zeros(dk.shape, F32)
        dv[...] = jnp.zeros(dv.shape, F32)

    def back(blocks):
        n = blocks * rows
        shape = (rows, rows)
        allowed = lax.broadcasted_iota(jnp.int32, shape, 0) <= lanes_of(shape)
        qs, dos, ps, dss, dqs = [], [], [], [], []
        for h in range(2):
            mine = low == (h == 0)
            qh = jnp.where(mine, q[...], jnp.zeros_like(q[...]))
            doh = jnp.where(mine, do[...], jnp.zeros_like(do[...]))
            sc = dot_nt(k2[0:n, :], qh) * scale - lse[h : h + 1, :]
            last = jnp.where(allowed, sc[n - rows :, :], neg_large)
            sc = jnp.concatenate([sc[: n - rows, :], last], axis=0) if blocks > 1 else last
            p = jnp.exp(sc)
            dp = dot_nt(v2[0:n, :], doh)
            centre = jnp.sum(p * dp, axis=0, keepdims=True)
            ds = (p * (dp - centre)).astype(BF16)
            qs.append(qh)
            dos.append(doh)
            ps.append(p.astype(BF16))
            dss.append(ds)
            dqs.append(dot_tn(ds, k2[0:n, :]) * scale)
        dk[0:n, :] += dot_nn(jnp.concatenate(dss, axis=1), jnp.concatenate(qs, axis=0)) * scale
        dv[0:n, :] += dot_nn(jnp.concatenate(ps, axis=1), jnp.concatenate(dos, axis=0))
        dq_o[...] = turn(jnp.where(low, dqs[0], dqs[1]), cosine[...], -sine[...]).astype(BF16)

    for i in range(steps):
        pl.when(step == i)(partial(back, i + 1))

    @pl.when(step == steps - 1)
    def _():
        own = (lanes_of(dk.shape) < HEAD_SIZE) != (kvh[0] == 1)
        g = dk[...]
        g = turn(g + pltpu.roll(g, 64, 1), cos_all[...], -sin_all[...])
        dkv_o[:, 0:128] = jnp.where(own, g, 0.0).astype(BF16)
        g = dv[...]
        g = g + pltpu.roll(g, 64, 1)
        dkv_o[:, 128:256] = jnp.where(own, g, 0.0).astype(BF16)


def attend_back(kvh, q, k2, v2, lse, do, cosine, sine):
    total = q.shape[0]
    rows = 256

    def whole(v):
        return pl.BlockSpec(v.shape, lambda i: (0,) * v.ndim)

    tall = pl.BlockSpec((rows, 128), lambda i: (i, 0))
    wide = pl.BlockSpec((8, rows), lambda i: (0, i))
    sds = jax.ShapeDtypeStruct
    return pl.pallas_call(
        attend_back_kernel,
        grid=(total // rows,),
        in_specs=[pl.BlockSpec(memory_space=pltpu.SMEM), tall, whole(k2), whole(v2), wide, tall, tall, tall,
                  whole(cosine), whole(sine)],
        out_specs=[tall, pl.BlockSpec((total, 256), lambda i: (0, 0))],
        out_shape=[sds((total, 128), BF16), sds((total, 256), BF16)],
        scratch_shapes=[pltpu.VMEM((total, 128), F32), pltpu.VMEM((total, 128), F32)],
        compiler_params=pltpu.CompilerParams(vmem_limit_bytes=VMEM_LIMIT),
        cost_estimate=pl.CostEstimate(flops=int(2e9), bytes_accessed=int(3e6), transcendentals=int(2e6)),
        name="attend_back",
    )(kvh, q, k2, v2, lse, do, cosine, sine, cosine, sine)


def scan_back_kernel(
    heads, channels, dm, y, zr, xr, xp, br, bp, trow, states, rsum, dots, gain, tapx, tapb, decay,
    bias, skip,
    dz_o, dx_o, db_o, dt_o, gx_o, gb_o, gm_o, gh_o,
    xs, bs, dxs, dbs, dstate,
):
    step = pl.program_id(0)
    last_step = pl.num_programs(0) - 1
    first = step == last_step
    rows = block_len
    inner = heads * SSM_DIM
    n_state = br.shape[1] // 2

    @pl.when(step == 0)
    def _():
        dxs[rows : rows + 8, :] = jnp.zeros((8, inner), F32)
        dbs[rows : rows + 8, :] = jnp.zeros((8, 2 * n_state), F32)
        dstate[...] = jnp.zeros(dstate.shape, F32)
        gx_o[...] = jnp.zeros(gx_o.shape, F32)
        gb_o[...] = jnp.zeros(gb_o.shape, F32)
        gm_o[...] = jnp.zeros(gm_o.shape, F32)
        gh_o[...] = jnp.zeros(gh_o.shape, F32)

    xs[0:8, :] = jnp.where(first, 0.0, xp[...])
    bs[0:8, :] = jnp.where(first, 0.0, bp[...])
    xs[8 : 8 + rows, :] = xr[...]
    bs[8 : 8 + rows, :] = br[...]
    ux = conv_rows(xs, tapx, 5, rows)
    sx = sigmoid(ux)
    x = ux * sx
    ub = conv_rows(bs, tapb, 5, rows)
    sb = sigmoid(ub)
    bc = (ub * sb).astype(BF16)
    b_low, c_low = bc[:, :n_state], bc[:, n_state:]

    pre = trow[...] + bias[...]
    dt = softplus(pre)
    cum = running_sum(dt * decay[...])
    end = cum[:, rows - 1 :]
    fade = jnp.exp(end - cum)
    inv = lax.rsqrt(rsum[...] / channels + epsilon)
    cols = stack_columns(
        [cum, jnp.exp(cum), dt * fade, dt, inv, inv * inv * inv * dots[...] / channels]
    )
    r = cols[:, 32:33]
    kk = cols[:, 40:41]
    z = zr[...]
    sz = sigmoid(z)
    silu_z = z * sz
    yv = y[...]
    w = yv * silu_z
    dmv = dm[...]
    dw = r * gain[...] * dmv - w * kk
    gm_o[0:1, :] += jnp.sum(dmv * w * r, axis=0, keepdims=True)
    dy = dw * silu_z
    dz_o[...] = (dw * yv * sz * (1.0 + z * (1.0 - sz))).astype(BF16)
    gm_o[1:2, :] += jnp.sum(dy * x, axis=0, keepdims=True)

    grow = widen(cols, 8, heads)
    tail = widen(cols, 16, heads)
    dt_wide = widen(cols, 24, heads)
    x_low = x.astype(BF16)
    dy_low = dy.astype(BF16)
    state = states[0]
    state_low = state.astype(BF16)
    ds = dstate[...]
    ds_low = ds.astype(BF16)
    cross = dot_nt(b_low, c_low)
    shape = (rows, rows)
    upper = lax.broadcasted_iota(jnp.int32, shape, 0) <= lanes_of(shape)
    half = lanes_of(shape) < SSM_DIM
    lane = lanes_of(shape)
    dcross = jnp.zeros(shape, F32)
    col_sums = jnp.zeros(shape, F32)
    row_sums = []
    mids = []
    for p in range(heads // 2):
        span = slice(128 * p, 128 * p + 128)
        xpair, dypair = x_low[:, span], dy_low[:, span]
        zero = jnp.zeros_like(xpair)
        dys = (jnp.where(half, dypair, zero), jnp.where(half, zero, dypair))
        mats = []
        for k in range(2):
            h = 2 * p + k
            gap = jnp.where(upper, cum[h : h + 1, :] - cols[:, h : h + 1], neg_large)
            faded = jnp.exp(gap)
            mats.append((cross * faded).astype(BF16))
            t = dot_nt(xpair, dys[k]) * faded
            dt_col = cols[:, 24 + h : 25 + h]
            td = t * dt_col
            dcross = dcross + td
            row_sums.append(jnp.sum(td * cross, axis=0, keepdims=True))
            col = jnp.sum(t * cross, axis=1, keepdims=True)
            col_sums = jnp.where(lane == h, col, col_sums)
        mids.append(dot_nn(jnp.concatenate(mats, axis=1), jnp.concatenate(dys, axis=0)))
    mid = jnp.concatenate(mids, axis=1)
    row_sums = jnp.concatenate(row_sums + [jnp.zeros((8 - heads, rows), F32)], axis=0)
    col_sums = col_sums.T[0:8, :]

    dye = dy * grow
    dye_low = dye.astype(BF16)
    xd = x * tail
    xd_low = xd.astype(BF16)
    from_b = dot_nn(b_low, ds_low)
    through = dot_nn(c_low, state_low)
    dcross_low = dcross.astype(BF16)
    db = dot_nn(dcross_low, c_low) + dot_nt(xd_low, ds_low)
    dc = dot_tn(dcross_low, b_low) + dot_nt(dye_low, state_low)

    head_of = lax.broadcasted_iota(jnp.int32, (8, inner), 0)
    chan = lanes_of((8, inner)) // SSM_DIM
    ones = jnp.where(head_of == chan, 1.0, 0.0).astype(BF16)

    def by_head(v):
        high = v.astype(BF16)
        rest = (v - high.astype(F32)).astype(BF16)
        return dot_nt(ones, high) + dot_nt(ones, rest)

    grown = by_head(dye * through)
    ended = by_head(x * from_b)
    kept = jnp.sum(ds * state, axis=0, keepdims=True) * grow[rows - 1 :, :]
    kept = jnp.where(head_of == chan, kept, 0.0).sum(axis=1, keepdims=True)
    pulled = dt * fade * ended
    lane8 = lanes_of((8, rows))
    at_end = kept + jnp.sum(pulled, axis=1, keepdims=True)
    dcum = row_sums - dt * col_sums + grown - pulled + jnp.where(lane8 == rows - 1, at_end, 0.0)
    da = running_sum_back(dcum)
    ddt = col_sums + fade * ended + decay[...] * da
    dpre = ddt * sigmoid(pre)
    dt_o[...] = dpre
    gh_o[0:8, :] += da * dt * decay[...]
    gh_o[8:16, :] += dpre

    dstate[...] = grow[rows - 1 :, :] * ds + dot_tn(c_low, dye_low)
    dx = skip[...] * dy + dt_wide * mid + tail * from_b
    dux = dx * sx * (1.0 + ux * (1.0 - sx))
    dub = jnp.concatenate([db, dc], axis=1) * sb * (1.0 + ub * (1.0 - sb))
    for taps, src, d, buf, acc, out in (
        (tapx, xs, dux, dxs, gx_o, dx_o),
        (tapb, bs, dub, dbs, gb_o, db_o),
    ):
        buf[0:rows, :] = d
        total = taps[CONV - 1 : CONV, :] * d
        for j in range(CONV - 1):
            total = total + taps[j : j + 1, :] * buf[pl.ds(CONV - 1 - j, rows), :]
        out[...] = total.astype(BF16)
        for j in range(CONV):
            acc[j : j + 1, :] += jnp.sum(d * src[pl.ds(5 + j, rows), :], axis=0, keepdims=True)
        acc[CONV : CONV + 1, :] += jnp.sum(d, axis=0, keepdims=True)
        buf[rows : rows + 8, :] = d[0:8, :]


def scan_back(heads, channels, dm, y, zr, xr, br, trow, states, rsum, dots, gain, tapx, tapb, decay, bias, skip):
    total, inner = y.shape
    pair = br.shape[1]
    rows = block_len
    steps = total // rows
    per = rows // 8

    def whole(v):
        return pl.BlockSpec(v.shape, lambda i: (0,) * v.ndim)

    def tall(n):
        return pl.BlockSpec((rows, n), lambda i: (steps - 1 - i, 0))

    def before(n):
        return pl.BlockSpec((8, n), lambda i: (jnp.maximum((steps - 1 - i) * per - 1, 0), 0))

    wide = pl.BlockSpec((8, rows), lambda i: (0, steps - 1 - i))
    sds = jax.ShapeDtypeStruct

    def fixed(*shape):
        return pl.BlockSpec(shape, lambda i: (0, 0))

    return pl.pallas_call(
        partial(scan_back_kernel, heads, channels),
        grid=(steps,),
        in_specs=[tall(inner), tall(inner), tall(inner), tall(inner), before(inner), tall(pair),
                  before(pair), wide,
                  pl.BlockSpec((1, pair // 2, inner), lambda i: (steps - 1 - i, 0, 0)), wide, wide,
                  whole(gain), whole(tapx), whole(tapb), whole(decay), whole(bias), whole(skip)],
        out_specs=[tall(inner), tall(inner), tall(pair), wide, fixed(8, inner), fixed(8, pair),
                   fixed(8, inner), fixed(16, rows)],
        out_shape=[sds((total, inner), BF16), sds((total, inner), BF16), sds((total, pair), BF16),
                   sds((8, total), F32), sds((8, inner), F32), sds((8, pair), F32),
                   sds((8, inner), F32), sds((16, rows), F32)],
        scratch_shapes=[pltpu.VMEM((rows + 8, inner), F32), pltpu.VMEM((rows + 8, pair), F32),
                        pltpu.VMEM((rows + 8, inner), F32), pltpu.VMEM((rows + 8, pair), F32),
                        pltpu.VMEM((pair // 2, inner), F32)],
        compiler_params=pltpu.CompilerParams(vmem_limit_bytes=VMEM_LIMIT),
        cost_estimate=pl.CostEstimate(flops=int(4e9), bytes_accessed=int(15e6), transcendentals=int(5e6)),
        name="scan_back",
    )(dm, y, zr, xr, xr, br, br, trow, states, rsum, dots, gain, tapx, tapb,
      decay, bias, skip)


def whole_spec(v):
    return pl.BlockSpec(v.shape, lambda i: (0,) * v.ndim)


def feed_kernel(paired, hid, gain, cot, whid, wdown, out_o, dh_o, dmix_o, gg_o, piece_o, a2, a2t, acc, dacc, *pair):
    step = pl.program_id(0)
    tiles = pl.num_programs(0)
    width = hid.shape[1]
    blocks = width // 128
    units = whid.shape[4]
    d = lax.axis_index("dp")
    z = lax.axis_index("tensor")
    core = lax.rem(d, 2)
    if paired:
        (sent, came, send, recv) = pair
        sibling = d + 1 - 2 * core

        def swap(tile):
            return remote_copy(
                sent.at[tile], came.at[tile], send.at[tile], recv.at[tile], (sibling, z)
            )

        pl.when(step == 0)(lambda: greet([(sibling, z)]))

    @pl.when(step == 0)
    def _():
        v = hid[...]
        f = lax.rsqrt(jnp.mean(v * v, axis=1, keepdims=True) + epsilon)
        low = (v * f * gain[...]).astype(BF16)
        a2[...] = low
        a2t[...] = low.T
        acc[...] = jnp.zeros(acc.shape, F32)
        dacc[...] = jnp.zeros(dacc.shape, F32)

    w_gate = whid[:, 0, 0].reshape(width, units)
    w_up = whid[:, 0, 1].reshape(width, units)
    w_down = jnp.concatenate([wdown[k, 0] for k in range(blocks)], axis=1)
    g = dot_nn(a2[...], w_gate)
    u = dot_nn(a2[...], w_up)
    s = sigmoid(g)
    f_low = (g * s * u).astype(BF16)
    c = cot[...]
    acc[...] += dot_nn(f_low, w_down)
    df = dot_nt(c, w_down)
    du = (df * g * s).astype(BF16)
    dg = (df * u * s * (1.0 + g * (1.0 - s))).astype(BF16)
    dacc[...] += dot_nt(dg, w_gate) + dot_nt(du, w_up)

    per = units // 128
    quarter_units = (piece_o.shape[2] // 3)
    tiles_per = quarter_units // units

    def places(tile):
        part = lax.rem(tile, tiles_per)
        rows = [(k * quarter_units + part * units + cb * 128, 128) for k in range(2) for cb in range(per)]
        return tile // tiles_per, rows + [(2 * quarter_units + part * units, units)]

    quarter, rows = places(step)
    values = []
    for grad in (dg, du):
        full = dot_nn(a2t[...], grad).astype(BF16)
        for cb in range(per):
            values.append(full[:, 128 * cb : 128 * cb + 128].reshape(blocks, 128, 128))
    gd = dot_tn(f_low, c).astype(BF16)
    values.append(jnp.stack([gd[:, 128 * k : 128 * k + 128] for k in range(blocks)]))
    first = 0
    for value, (row, n) in zip(values, rows):
        at = pl.ds(pl.multiple_of(row, 128), n)
        if paired:
            value = value.reshape(blocks // 2, 2, n, 128)
            even, odd = value[:, 0], value[:, 1]
            piece_o[:, quarter, at, :] = jnp.where(core == 0, even, odd)
            sent[step, :, first : first + n, :] = jnp.where(core == 0, odd, even)
            first += n
        else:
            piece_o[:, quarter, at, :] = value

    if paired:
        swap(step).start()

        def take(tile):
            swap(tile).wait_recv()
            quarter, rows = places(tile)
            first = 0
            for row, n in rows:
                at = pl.ds(pl.multiple_of(row, 128), n)
                piece_o[:, quarter, at, :] = (
                    piece_o[:, quarter, at, :].astype(F32)
                    + came[tile, :, first : first + n, :].astype(F32)
                ).astype(BF16)
                first += n

        pl.when(step > 0)(lambda: take(step - 1))

    @pl.when(step == tiles - 1)
    def _():
        v = hid[...]
        out_o[...] = (v + acc[...]).astype(BF16)
        f = lax.rsqrt(jnp.mean(v * v, axis=1, keepdims=True) + epsilon)
        dy = dacc[...]
        gg_o[...] = jnp.sum(dy * v * f, axis=0, keepdims=True)
        gdy = dy * gain[...]
        lean = jnp.sum(gdy * v, axis=1, keepdims=True) * (f * f * f / width)
        dh = cot[...].astype(F32) + (f * gdy - v * lean)
        dh_o[...] = dh
        dmix_o[...] = dh.astype(BF16)
        if paired:
            take(tiles - 1)

            def sent_all(tile, carry):
                swap(tile).wait_send()
                return carry

            lax.fori_loop(0, tiles, sent_all, 0)


def feed_forward(paired, hid, gain, cot, whid, wdown):
    rows, width = hid.shape
    blocks, nt, _, depth, units = whid.shape
    tile = 256
    per = units // tile
    hid_spec = pl.BlockSpec((blocks, 1, 2, depth, tile), lambda i: (0, i // per, 0, 0, lax.rem(i, per)))
    down_spec = pl.BlockSpec((blocks, 1, tile, 128), lambda i: (0, i // per, lax.rem(i, per), 0))
    sds = jax.ShapeDtypeStruct
    kept = blocks // 2 if paired else blocks
    piece = (kept, nt, 3 * units, 128)
    dma = pltpu.SemaphoreType.DMA
    scratch = []
    extra = {}
    if paired:
        box = pltpu.VMEM((nt * per, kept, 3 * tile, 128), BF16)
        scratch = [box, box, dma((nt * per,)), dma((nt * per,))]
        extra = dict(collective_id=4, has_side_effects=True)

    def fixed(*shape):
        return pl.BlockSpec(shape, lambda i: (0,) * len(shape))

    return pl.pallas_call(
        partial(feed_kernel, paired),
        grid=(nt * per,),
        in_specs=[fixed(rows, width), fixed(1, width), fixed(rows, width), hid_spec, down_spec],
        out_specs=[fixed(rows, width), fixed(rows, width), fixed(rows, width), fixed(1, width),
                   fixed(*piece)],
        out_shape=[sds((rows, width), BF16), sds((rows, width), F32), sds((rows, width), BF16),
                   sds((1, width), F32), sds(piece, BF16)],
        scratch_shapes=[pltpu.VMEM((rows, width), BF16), pltpu.VMEM((width, rows), BF16),
                        pltpu.VMEM((rows, width), F32), pltpu.VMEM((rows, width), F32)] + scratch,
        compiler_params=pltpu.CompilerParams(vmem_limit_bytes=VMEM_LIMIT, **extra),
        cost_estimate=pl.CostEstimate(flops=int(1e10), bytes_accessed=int(26e6), transcendentals=int(5e5)),
        name="feed_forward",
    )(hid, gain, cot, whid, wdown)


def row_columns(rows_list, rows):
    return jnp.concatenate(
        [stack_columns([r[:, c : c + 128] for r in rows_list]) for c in range(0, rows, 128)], axis=0
    )


def down_kernel(dq, dz, dx, dkv, db, drow, wq, win, stp, wsh, part_o):
    total = dot_nt(dq[...], wq[...]) + dot_nt(dz[...], win[0]) + dot_nt(dx[...], win[1])
    total = total + dot_nt(dkv[...], wsh[:, 0:256]) + dot_nt(db[...], wsh[:, 256:])
    total = total + dot_tn(drow[...].astype(BF16), stp[...])
    part_o[...] = total.astype(BF16)


def down_parts(dq, dz, dx, dkv, db, drow, wq, win, stp, wsh):
    total, inner = dz.shape
    width = wq.shape[0]
    rows = 256

    def tall(v):
        return pl.BlockSpec((rows, v.shape[1]), lambda i: (i, 0))

    wide = pl.BlockSpec((8, rows), lambda i: (0, i))
    return pl.pallas_call(
        down_kernel,
        grid=(total // rows,),
        in_specs=[tall(dq), tall(dz), tall(dx), tall(dkv), tall(db), wide, whole_spec(wq), whole_spec(win),
                  whole_spec(stp), whole_spec(wsh)],
        out_specs=pl.BlockSpec((rows, width), lambda i: (i, 0)),
        out_shape=jax.ShapeDtypeStruct((total, width), BF16),
        compiler_params=pltpu.CompilerParams(vmem_limit_bytes=VMEM_LIMIT),
        cost_estimate=pl.CostEstimate(flops=int(3e9), bytes_accessed=int(8e6), transcendentals=0),
        name="down_parts",
    )(dq, dz, dx, dkv, db, drow, wq, win, stp, wsh)


def weight_kernel(a1, dq, dz, dx, dkv, db, drow, o, m, dmix, piece_o, shared_o, step_o, ot, mt):
    step = pl.program_id(0)

    @pl.when(step == 0)
    def _():
        ot[...] = o[...].T
        mt[...] = m[...].T

    a = a1[...]
    step_o[...] = dot_nn(drow[...].astype(BF16), a)
    at = a.T
    inner = dz.shape[1]

    def by_rows(values, first):
        for j in range(values.shape[1] // 128):
            piece_o[:, first + 128 * j : first + 128 * (j + 1), :] = (
                values[:, 128 * j : 128 * (j + 1)].reshape(2, 128, 128)
            )

    def by_lanes(values, first):
        n = values.shape[0]
        for k in range(2):
            piece_o[k, first : first + n, :] = values[:, 128 * k : 128 * (k + 1)]

    g = dmix[...]
    by_rows(dot_nn(at, dq[...]).astype(BF16), 0)
    by_lanes(dot_nn(ot[...], g).astype(BF16), 128)
    by_rows(dot_nn(at, dz[...]).astype(BF16), 256)
    by_rows(dot_nn(at, dx[...]).astype(BF16), 256 + inner)
    by_lanes(dot_nn(mt[...], g).astype(BF16), 256 + 2 * inner)
    shared_o[:, :, 0:256] = dot_nn(at, dkv[...]).astype(BF16).reshape(2, 128, 256)
    shared_o[:, :, 256:] = dot_nn(at, db[...]).astype(BF16).reshape(2, 128, db.shape[1])


def weight_pieces(a1, dq, dz, dx, dkv, db, drow, o, m, dmix):
    total, width = a1.shape
    inner = dz.shape[1]
    n = 256 + 3 * inner
    shared = 256 + db.shape[1]
    cols = pl.BlockSpec((total, 256), lambda i: (0, i))
    sds = jax.ShapeDtypeStruct
    args = (dq, dz, dx, dkv, db, drow, o, m)
    return pl.pallas_call(
        weight_kernel,
        grid=(width // 256,),
        in_specs=[cols] + [whole_spec(v) for v in args] + [cols],
        out_specs=[pl.BlockSpec((2, n, 128), lambda i: (i, 0, 0)),
                   pl.BlockSpec((2, 128, shared), lambda i: (i, 0, 0)),
                   pl.BlockSpec((8, 256), lambda i: (0, i))],
        out_shape=[sds((width // 128, n, 128), BF16), sds((width // 128, 128, shared), BF16),
                   sds((8, width), F32)],
        scratch_shapes=[pltpu.VMEM((128, total), BF16), pltpu.VMEM((inner, total), BF16)],
        compiler_params=pltpu.CompilerParams(vmem_limit_bytes=VMEM_LIMIT),
        cost_estimate=pl.CostEstimate(flops=int(4e9), bytes_accessed=int(12e6), transcendentals=0),
        name="weight_pieces",
    )(a1, *args, dmix)


class Exchange:
    def __init__(self, own, landed, send, recv, d, z, nt):
        self.own, self.landed, self.z, self.nt = own, landed, z, nt
        self.copies = [
            remote_copy(own, landed.at[k - 1], send.at[k - 1], recv.at[k - 1], peer)
            for k, peer in enumerate(other_quarters(d, z, nt), 1)
        ]

    def start(self):
        for copy in self.copies:
            copy.start()

    def wait(self):
        for copy in self.copies:
            copy.wait()

    def total(self):
        total = None
        for q in range(self.nt):
            value = jnp.where(self.z == q, self.own[...].astype(F32), 0.0)
            for k in range(1, self.nt):
                value = value + jnp.where(
                    lax.rem(self.z - k + self.nt, self.nt) == q, self.landed[k - 1].astype(F32), 0.0
                )
            total = value if total is None else total + value
        return total


class ChainScatter:
    def __init__(self, parts, bufs, landed, send, recv, d, z, nt):
        self.parts, self.bufs, self.landed = parts, bufs, landed
        self.send, self.recv = send, recv
        self.d, self.z, self.nt = d, z, nt

    def active(self, way, t):
        z, nt = self.z, self.nt
        if way == 0:
            return (z <= t) & (z < nt - 1)
        return (nt - 1 - z <= t) & (z > 0)

    def copy(self, way, t):
        dev = (self.d, self.z + 1 if way == 0 else self.z - 1)
        return remote_copy(
            self.bufs.at[way, t], self.landed.at[way, t], self.send.at[way, t], self.recv.at[way, t], dev
        )

    def arrives(self, way, t):
        z, nt = self.z, self.nt
        if way == 0:
            return (z >= 1) & (z - 1 <= t)
        return (z < nt - 1) & (nt - 2 - z <= t)

    def step(self, t):
        z, nt = self.z, self.nt
        for way in range(2):
            q = nt - 1 - t + z if way == 0 else t - (nt - 1) + z

            def run():
                value = self.parts[q]
                if t > 0:
                    came = self.arrives(way, t - 1)

                    @pl.when(came)
                    def _():
                        self.copy(way, t - 1).wait_recv()
                        total = value.astype(F32) + self.landed[way, t - 1].astype(F32)
                        self.bufs[way, t] = total.astype(BF16)

                    @pl.when(jnp.logical_not(came))
                    def _():
                        self.bufs[way, t] = value
                else:
                    self.bufs[way, t] = value
                self.copy(way, t).start()

            pl.when(self.active(way, t))(run)

    def finish(self, out):
        out[...] = self.parts[self.z].astype(F32)
        t = self.nt - 2
        for way in range(2):

            @pl.when(self.arrives(way, t))
            def _():
                self.copy(way, t).wait_recv()
                out[...] += self.landed[way, t].astype(F32)

    def drain(self):
        for way in range(2):
            for t in range(self.nt - 1):
                pl.when(self.active(way, t))(self.copy(way, t).wait_send)


def chain_scratch(nt, rows, width):
    dma = pltpu.SemaphoreType.DMA
    return [
        pltpu.VMEM((2, nt - 1, rows, width), BF16),
        pltpu.VMEM((2, nt - 1, rows, width), BF16),
        dma((2, nt - 1)),
        dma((2, nt - 1)),
    ]


def mix_scatter_kernel(channels, nt, feed, *refs):
    (o, y, z_in, sq, gain, watt, wmam, tok), refs = refs[:8], refs[8:]
    if feed:
        refs = refs[2:]
        turned, refs = refs[: 2 * (nt - 1)], refs[2 * (nt - 1) :]
        (m_o, sq_o, hid_o, hid_f, dwn_f), refs = refs[:5], refs[5:]
        (lsem, f_send, f_recv), refs = refs[:3], refs[3:]
    else:
        (m_o, sq_o, hid_o), refs = refs[:3], refs[3:]
    (sq_land, sq_send, sq_recv, parts, bufs, landed, c_send, c_recv) = refs
    d = lax.axis_index("dp")
    z = lax.axis_index("tensor")
    rows = tok.shape[0]
    peers = [(p, z) for p in cube_peers(d)] if feed else []
    greet(peers + other_quarters(d, z, nt))
    squares = Exchange(sq, sq_land, sq_send, sq_recv, d, z, nt)
    squares.start()
    n = 2 * (nt - 1)
    if feed:
        items = []
        for k in range(1, nt):
            q = lax.rem(z - k + nt, nt)
            items.append((turned[2 * k - 2], lambda s, q=q: hid_f.at[s, q]))
            items.append((turned[2 * k - 1], lambda s, q=q: dwn_f.at[s, q]))
        cube = CubeGather(items, (0, 3, 4), f_send, f_recv, d, z)
        for i in range(n):
            cube.start(i)
        locals_ = []
        for i, (src, dst) in enumerate([(src, at(d)) for src, at in items]):
            locals_.append(pltpu.make_async_copy(src, dst, lsem.at[i]))
            locals_[-1].start()
    chain = ChainScatter(parts, bufs, landed, c_send, c_recv, d, z, nt)
    squares.wait()
    sq_o[...] = squares.total()

    def part(q):
        at = pl.ds(pl.multiple_of(q * rows, rows), rows)
        total = sq_o[:, at]
        r = row_columns([lax.rsqrt(total / channels + epsilon)], rows)[:, 0:1]
        zv = z_in[at, :]
        m = (y[at, :] * (zv * sigmoid(zv)) * r * gain[...]).astype(BF16)
        m_o[at, :] = m
        parts[q] = (dot_nn(o[at, :], watt[...]) + dot_nn(m, wmam[...])).astype(BF16)

    first = jnp.where(z < nt // 2, nt - 1, 0)
    part(first)
    chain.step(0)

    def rest(i, carry):
        part(lax.rem(first + 1 + i, nt))
        return carry

    lax.fori_loop(0, nt - 1, rest, 0)
    if feed:
        cube.near(0)
        cube.near(1)
    for t in range(1, nt - 1):
        chain.step(t)
        if feed:
            cube.near(2 * t)
            cube.near(2 * t + 1)
            cube.far(2 * t - 2)
            cube.far(2 * t - 1)
    if feed:
        cube.far(n - 2)
        cube.far(n - 1)
    chain.finish(hid_o)
    hid_o[...] += tok[...].astype(F32)
    chain.drain()
    if feed:
        cube.finish()
        for copy in locals_:
            copy.wait()


def mix_scatter(channels, nt, o, y, zr, sq, gain, watt, wmam, tok, feed=()):
    total, inner = y.shape
    rows, width = tok.shape
    dma = pltpu.SemaphoreType.DMA
    sds = jax.ShapeDtypeStruct
    vmem = pl.BlockSpec(memory_space=pltpu.VMEM)
    anywhere = pl.BlockSpec(memory_space=pl.ANY)
    outs = [sds((total, inner), BF16), sds((8, total), F32), sds((rows, width), F32)]
    scratch = []
    n = 2 * (nt - 1)
    if feed:
        for v in feed[:2]:
            outs.append(sds(v.shape, BF16))
        scratch = [dma((n,)), dma((n, 7)), dma((n, 7))]
    return pl.pallas_call(
        partial(mix_scatter_kernel, channels, nt, bool(feed)),
        in_specs=[vmem] * 8 + [anywhere] * len(feed[:2]) + [vmem] * len(feed[2:]),
        out_specs=[vmem] * 3 + [anywhere] * (len(outs) - 3),
        out_shape=outs,
        input_output_aliases={8: 3, 9: 4} if feed else {},
        scratch_shapes=scratch + [pltpu.VMEM((nt - 1, 8, total), F32), dma((nt - 1,)), dma((nt - 1,)),
                        pltpu.VMEM((nt, rows, width), BF16)] + chain_scratch(nt, rows, width),
        compiler_params=pltpu.CompilerParams(
            vmem_limit_bytes=VMEM_LIMIT, collective_id=1, has_side_effects=True
        ),
        cost_estimate=pl.CostEstimate(flops=int(1e9), bytes_accessed=int(130e6), transcendentals=int(4e5)),
        name="mix_scatter",
    )(o, y, zr, sq, gain, watt, wmam, tok, *feed)


class ChainGather:
    def __init__(self, own, slots, send, recv, d, z, nt):
        self.own, self.slots, self.send, self.recv = own, slots, send, recv
        self.d, self.z, self.nt = d, z, nt

    def copy(self, way, dist):
        dev = (self.d, self.z + 1 if way == 0 else self.z - 1)
        slot = self.z - dist if way == 0 else self.z + dist
        src = self.own if dist == 0 else self.slots.at[slot]
        return remote_copy(src, self.slots.at[slot], self.send.at[way, dist], self.recv.at[way, dist], dev)

    def landing(self, way, dist):
        slot = self.z - dist if way == 0 else self.z + dist
        return remote_copy(
            self.slots.at[slot], self.slots.at[slot], self.send.at[way, dist - 1],
            self.recv.at[way, dist - 1], (self.d, self.z),
        )

    def has(self, way, dist):
        return self.z >= dist if way == 0 else self.z + dist < self.nt

    def goes_on(self, way):
        return self.z < self.nt - 1 if way == 0 else self.z > 0

    def start(self):
        for way in range(2):
            pl.when(self.goes_on(way))(self.copy(way, 0).start)

    def hop(self, dist):
        for way in range(2):
            pl.when(self.has(way, dist))(self.landing(way, dist).wait_recv)
            if dist < self.nt - 1:
                pl.when(self.has(way, dist) & self.goes_on(way))(self.copy(way, dist).start)

    def drain(self):
        for way in range(2):
            pl.when(self.goes_on(way))(self.copy(way, 0).wait_send)
            for dist in range(1, self.nt - 1):
                pl.when(self.has(way, dist) & self.goes_on(way))(self.copy(way, dist).wait_send)


def unmix_gather_kernel(nt, feed, *refs):
    (dmix, y, z_in, gain, watt, wmam), refs = refs[:6], refs[6:]
    if feed:
        pieces, refs = refs[0], refs[1:]
        (g_o, do_o, dm_o, dot_o, own_o, sum_o), refs = refs[:6], refs[6:]
        boxes, refs = refs[: 8 * (nt - 1)], refs[8 * (nt - 1) :]
    else:
        (g_o, do_o, dm_o, dot_o), refs = refs[:4], refs[4:]
    (slots, g_send, g_recv, dot_own, dot_land, d_send, d_recv) = refs
    d = lax.axis_index("dp")
    z = lax.axis_index("tensor")
    rows = dmix.shape[0]
    bits = dp_bits(d)
    peers = cube_peers(d)
    greet(([(p, z) for p in peers[1:]] if feed else []) + other_quarters(d, z, nt))
    chain = ChainGather(dmix, slots, g_send, g_recv, d, z, nt)
    chain.start()
    cubes = []
    if feed:
        for k in range(1, nt):
            q = lax.rem(z + k, nt)
            box = boxes[8 * k - 8 : 8 * k]
            cubes.append(
                SquareScatter(lambda i, j, q=q: (i, j, q), pieces, box[:6], box[6], box[7], peers, bits, z)
            )
            cubes[-1].start()

    def work(q, g):
        at = pl.ds(pl.multiple_of(q * rows, rows), rows)
        g_o[at, :] = g
        do_o[at, :] = dot_nt(g, watt[...]).astype(BF16)
        dm = dot_nt(g, wmam[...])
        dm_o[at, :] = dm
        zv = z_in[at, :]
        dots = jnp.sum(dm * gain[...] * (y[at, :] * (zv * sigmoid(zv))), axis=1, keepdims=True)
        turned = [jnp.broadcast_to(dots[c : c + 128], (128, 128)).T[0:8, :] for c in range(0, rows, 128)]
        dot_own[:, at] = jnp.concatenate(turned, axis=1)

    work(z, dmix[...])
    if feed:
        own_o[...] = pieces[:, :, z]
        cubes[0].middle()
    for dist in range(1, nt):
        chain.hop(dist)

        def side(way, carry):
            q = jnp.where(way == 0, z - dist, z + dist)

            @pl.when((q >= 0) & (q < nt))
            def _():
                work(q, slots[q])

            return carry

        lax.fori_loop(0, 2, side, 0)
        if feed:
            if dist < nt - 1:
                cubes[dist].middle()
            cubes[dist - 1].finish(sum_o.at[dist - 1])
    dots = Exchange(dot_own, dot_land, d_send, d_recv, d, z, nt)
    dots.start()
    chain.drain()
    for cube in cubes:
        cube.drain()
    dots.wait()
    dot_o[...] = dots.total()


def unmix_gather(nt, dmix, y, zr, gain, watt, wmam, pieces=None):
    total, inner = y.shape
    rows, width = dmix.shape
    dma = pltpu.SemaphoreType.DMA
    sds = jax.ShapeDtypeStruct
    vmem = pl.BlockSpec(memory_space=pltpu.VMEM)
    feed = [] if pieces is None else [pieces]
    outs = [sds((total, width), BF16), sds((total, 128), BF16), sds((total, inner), F32),
            sds((8, total), F32)]
    scratch = []
    if feed:
        n, lanes = pieces.shape[3:]
        outs += [sds((2, 2, n, lanes), BF16), sds((nt - 1, n, lanes), BF16)]
        for _ in range(nt - 1):
            scratch += square_scratch(n, lanes)
    return pl.pallas_call(
        partial(unmix_gather_kernel, nt, bool(feed)),
        in_specs=[vmem] * (6 + len(feed)),
        out_specs=[vmem] * len(outs),
        out_shape=outs,
        scratch_shapes=scratch + [pltpu.VMEM((nt, rows, width), BF16), dma((2, nt - 1)), dma((2, nt - 1)),
                        pltpu.VMEM((8, total), F32), pltpu.VMEM((nt - 1, 8, total), F32),
                        dma((nt - 1,)), dma((nt - 1,))],
        compiler_params=pltpu.CompilerParams(
            vmem_limit_bytes=VMEM_LIMIT, collective_id=2, has_side_effects=True
        ),
        cost_estimate=pl.CostEstimate(flops=int(1e9), bytes_accessed=int(130e6), transcendentals=int(4e5)),
        name="unmix_gather",
    )(dmix, y, zr, gain, watt, wmam, *feed)


def add_refs(left, right):
    return left.astype(F32) + right.astype(F32)


class SquareScatter:
    def __init__(self, place, held, bufs, send, recv, peers, bits, z):
        (self.r1, self.r2, self.ob, self.tb, self.r3, self.r4) = bufs
        self.place, self.held = place, held
        n = held.shape[-2]
        half = n // 2
        self.lo, self.hi = pl.ds(0, half), pl.ds(half, n - half)
        self.half = half
        _, self.x, self.y = bits
        x, y = self.x, self.y
        _, d_x, d_y = peers
        self.copies = []
        for i in range(2):
            self.copies.append(
                remote_copy(held.at[place(i, 1 - x) + (self.lo,)], self.r1.at[i], send.at[i], recv.at[i],
                            (d_x, z))
            )
        for j in range(2):
            self.copies.append(
                remote_copy(held.at[place(1 - y, j) + (self.hi,)], self.r2.at[j], send.at[2 + j],
                            recv.at[2 + j], (d_y, z))
            )
        self.copies.append(remote_copy(self.ob.at[1 - y], self.r3, send.at[4], recv.at[4], (d_y, z)))
        self.copies.append(remote_copy(self.tb.at[1 - x], self.r4, send.at[5], recv.at[5], (d_x, z)))

    def start(self):
        for copy in self.copies[:4]:
            copy.start()

    def middle(self):
        for i in range(2):
            self.copies[i].wait_recv()
            self.ob[i] = add_refs(self.held[self.place(i, self.x) + (self.lo,)], self.r1[i]).astype(BF16)
        self.copies[4].start()
        for j in range(2):
            self.copies[2 + j].wait_recv()
            self.tb[j] = add_refs(self.held[self.place(self.y, j) + (self.hi,)], self.r2[j]).astype(BF16)
        self.copies[5].start()

    def finish(self, out):
        self.copies[4].wait_recv()
        out[0 : self.half] = add_refs(self.ob[self.y], self.r3[...]).astype(out.dtype)
        self.copies[5].wait_recv()
        out[self.half :] = add_refs(self.tb[self.x], self.r4[...]).astype(out.dtype)

    def drain(self):
        for copy in self.copies:
            copy.wait_send()


def square_scratch(n, lanes):
    dma = pltpu.SemaphoreType.DMA
    half = n // 2
    return [
        pltpu.VMEM((2, half, lanes), BF16),
        pltpu.VMEM((2, n - half, lanes), BF16),
        pltpu.VMEM((2, half, lanes), BF16),
        pltpu.VMEM((2, n - half, lanes), BF16),
        pltpu.VMEM((half, lanes), BF16),
        pltpu.VMEM((n - half, lanes), BF16),
        dma((6,)),
        dma((6,)),
    ]


class CubeScatter:
    def __init__(self, pieces, bufs, peers, bits, z):
        (self.rc, self.held, send, recv) = bufs[:4]
        self.p = pieces
        self.core = bits[0]
        self.first = remote_copy(
            pieces.at[:, :, 1 - self.core], self.rc, send.at[0], recv.at[0], (peers[0], z)
        )
        self.square = SquareScatter(
            lambda i, j: (i, j), self.held, bufs[4:10], bufs[10], bufs[11], peers, bits, z
        )

    def start(self):
        self.first.start()

    def middle(self):
        self.first.wait_recv()
        for i in range(2):
            for j in range(2):
                self.held[i, j] = add_refs(self.p[i, j, self.core], self.rc[i, j]).astype(BF16)
        self.square.start()

    def last(self):
        self.square.middle()

    def finish(self, out):
        self.square.finish(out)

    def drain(self):
        self.first.wait_send()
        self.square.drain()


def cube_scratch(n, lanes):
    dma = pltpu.SemaphoreType.DMA
    return [
        pltpu.VMEM((2, 2, n, lanes), BF16),
        pltpu.VMEM((2, 2, n, lanes), BF16),
        dma((1,)),
        dma((1,)),
    ] + square_scratch(n, lanes)


class CubeTotal:
    def __init__(self, held, landed, send, recv, peers, z):
        self.held, self.landed = held, landed
        self.copies = [
            remote_copy(held.at[i], landed.at[i], send.at[i], recv.at[i], (peer, z))
            for i, peer in enumerate(peers)
        ]

    def start(self, i):
        self.copies[i].start()

    def take(self, i):
        self.copies[i].wait_recv()
        self.held[i + 1] = self.held[i] + self.landed[i]

    def drain(self):
        for copy in self.copies:
            copy.wait_send()


def norm_back(dy, tok, gain, dh, out, ggain):
    v = tok[...].astype(F32)
    width = v.shape[1]
    f = lax.rsqrt(jnp.mean(v * v, axis=1, keepdims=True) + epsilon)
    ggain(jnp.sum(dy * v * f, axis=0, keepdims=True))
    gdy = dy * gain[...]
    lean = jnp.sum(gdy * v, axis=1, keepdims=True) * (f * f * f / width)
    out[...] = (dh[...] + (f * gdy - v * lean)).astype(BF16)


def tail_kernel(
    nt, n_all, parts, tok, gain, dh, pieces, shared, small, feed_own, feed_rest,
    gt_o, que_o, att_o, inn_o, mam_o, hid_o, dwn_o, sh_o, small_o, norm_o,
    da, mixed, fed, bufs, landed, c_send, c_recv, *rest,
):
    cube_a, rest = rest[:12], rest[12:]
    cube_b, rest = rest[:12], rest[12:]
    square_c, rest = rest[:8], rest[8:]
    (sh_sum, sh_land, sh_send, sh_recv) = rest[:4]
    (sm_held, sm_land, sm_send, sm_recv, all_own, all_land, all_send, all_recv) = rest[4:12]
    (ng_held, ng_land, ng_send, ng_recv, ngz_land, ngz_send, ngz_recv) = rest[12:]
    d = lax.axis_index("dp")
    z = lax.axis_index("tensor")
    bits = dp_bits(d)
    peers = cube_peers(d)
    greet([(p, z) for p in peers] + other_quarters(d, z, nt))
    chain = ChainScatter(parts, bufs, landed, c_send, c_recv, d, z, nt)
    chain.step(0)
    one = CubeScatter(pieces, cube_a, peers, bits, z)
    two = CubeScatter(shared, cube_b, peers, bits, z)
    three = SquareScatter(
        lambda i, j: (i, j), feed_own, square_c[:6], square_c[6], square_c[7], peers, bits, z
    )
    sums = CubeTotal(sm_held, sm_land, sm_send, sm_recv, peers, z)
    sm_held[0] = small[...]
    sums.start(0)
    two.start()
    one.start()
    sums.take(0)
    sums.start(1)
    two.middle()
    one.middle()
    three.start()
    sums.take(1)
    sums.start(2)
    chain.step(1)
    sums.take(2)
    all_own[...] = sm_held[3, 0:n_all, :]
    over_all = Exchange(all_own, all_land, all_send, all_recv, d, z, nt)
    over_all.start()
    two.last()
    one.last()
    two.finish(sh_sum)
    per = sh_sum.shape[0] // nt
    copies = []
    for k in range(1, nt):
        q = lax.rem(z + k, nt)
        rows = pl.ds(pl.multiple_of(q * per, per), per)
        copies.append(
            remote_copy(sh_sum.at[rows], sh_land.at[k - 1], sh_send.at[k - 1], sh_recv.at[k - 1], (d, q))
        )
        copies[-1].start()
    three.middle()
    for t in range(2, nt - 1):
        chain.step(t)
    one.finish(mixed)
    block = que_o.shape[0]
    inner = mam_o.shape[0]
    first = 0
    for j in range(que_o.shape[1] // 128):
        que_o[:, 128 * j : 128 * j + 128] = mixed[first : first + block]
        first += block
    att_o[...] = mixed[first : first + att_o.shape[0]]
    first += att_o.shape[0]
    for i in range(2):
        for j in range(inner // 128):
            inn_o[i, :, 128 * j : 128 * j + 128] = mixed[first : first + block]
            first += block
    mam_o[...] = mixed[first : first + inner]
    three.finish(fed)
    for k in range(nt - 1):
        fed[...] += feed_rest[k].astype(F32)
    first = 0
    for i in range(2):
        for j in range(hid_o.shape[2] // 128):
            hid_o[i, :, 128 * j : 128 * j + 128] = fed[first : first + block]
            first += block
    dwn_o[...] = fed[first:]
    small_o[...] = sm_held[3]
    over_all.wait()
    small_o[0:n_all, :] = over_all.total()
    for copy in copies:
        copy.wait()
    total = sh_sum[pl.ds(pl.multiple_of(z * per, per), per), :].astype(F32)
    for k in range(nt - 1):
        total = total + sh_land[k].astype(F32)
    sh_o[...] = total
    chain.finish(da)

    def keep(row):
        for k in range(8):
            ng_held[0, k : k + 1, :] = row[:, 128 * k : 128 * k + 128]

    norm_back(da[...], tok, gain, dh, gt_o, keep)
    norms = CubeTotal(ng_held, ng_land, ng_send, ng_recv, peers, z)
    for i in range(3):
        norms.start(i)
        norms.take(i)
    last = Exchange(ng_held.at[3], ngz_land, ngz_send, ngz_recv, d, z, nt)
    last.start()
    last.wait()
    norm_o[...] = last.total()
    for thing in (chain, one, two, three, sums, norms):
        thing.drain()


def tail(nt, n_all, parts, tok, gain, dh, pieces, shared, small, feed_own, feed_rest, shapes):
    rows, width = tok.shape
    n, lanes = pieces.shape[1:]
    s_rows, s_lanes = shared.shape[1:]
    m_rows = small.shape[0]
    dma = pltpu.SemaphoreType.DMA
    sds = jax.ShapeDtypeStruct
    vmem = pl.BlockSpec(memory_space=pltpu.VMEM)
    pieces = pieces.reshape(2, 2, 2, n, lanes)
    shared = shared.reshape(2, 2, 2, s_rows, s_lanes)
    return pl.pallas_call(
        partial(tail_kernel, nt, n_all),
        in_specs=[vmem] * 9,
        out_specs=[vmem] * (4 + len(shapes)),
        out_shape=[sds((rows, width), BF16)] + [sds(s, F32) for s in shapes]
        + [sds((s_rows // nt, s_lanes), F32), sds((m_rows, 128), F32), sds((8, 128), F32)],
        scratch_shapes=[pltpu.VMEM((rows, width), F32), pltpu.VMEM((n, lanes), F32),
                        pltpu.VMEM(feed_own.shape[2:], F32)] + chain_scratch(nt, rows, width)
        + cube_scratch(n, lanes) + cube_scratch(s_rows, s_lanes) + square_scratch(*feed_own.shape[2:])
        + [pltpu.VMEM((s_rows, s_lanes), BF16), pltpu.VMEM((nt - 1, s_rows // nt, s_lanes), BF16),
           dma((nt - 1,)), dma((nt - 1,)),
           pltpu.VMEM((4, m_rows, 128), F32), pltpu.VMEM((3, m_rows, 128), F32), dma((3,)), dma((3,)),
           pltpu.VMEM((n_all, 128), F32), pltpu.VMEM((nt - 1, n_all, 128), F32), dma((nt - 1,)),
           dma((nt - 1,)),
           pltpu.VMEM((4, 8, 128), F32), pltpu.VMEM((3, 8, 128), F32), dma((3,)), dma((3,)),
           pltpu.VMEM((nt - 1, 8, 128), F32), dma((nt - 1,)), dma((nt - 1,))],
        compiler_params=pltpu.CompilerParams(
            vmem_limit_bytes=VMEM_LIMIT, collective_id=3, has_side_effects=True
        ),
        cost_estimate=pl.CostEstimate(flops=int(1e7), bytes_accessed=int(150e6), transcendentals=0),
        name="tail",
    )(parts, tok, gain, dh, pieces, shared, small, feed_own, feed_rest)


def rope_wide(length):
    half = HEAD_SIZE // 2
    inverse = rope_base ** (-np.arange(half) * (2.0 / HEAD_SIZE))
    angles = np.arange(length)[:, None] * inverse[None, :]
    c, s = np.cos(angles), np.sin(angles)
    return (
        jnp.asarray(np.concatenate([c, c, c, c], axis=1), F32),
        jnp.asarray(np.concatenate([-s, s, -s, s], axis=1), F32),
    )


def to_blocks(full, axis, nt):
    if axis == 1:
        two, width, cols = full.shape
        return full.reshape(2, 8, width // 8, nt, cols // nt).transpose(1, 3, 0, 2, 4)
    rows, width = full.shape
    return full.reshape(nt, rows // nt, 8, width // 8).transpose(2, 0, 1, 3)


def per_device(
    nd,
    nt,
    tokens,
    query_proj,
    attend_out,
    inner_proj,
    step_proj,
    mamba_out,
    hidden_proj,
    down_proj,
    channel_taps,
    mixer_gain,
    decay_log,
    step_bias,
    skip_weight,
    shared_proj,
    norm_gains,
    shared_taps,
    cotangent,
):
    tensor_index = lax.axis_index("tensor")
    d = lax.axis_index("dp")
    local_rows, width = tokens.shape
    group_rows = local_rows * nt
    heads = step_proj.shape[1]
    inner = heads * SSM_DIM
    channels = inner * nt
    units = down_proj.shape[0]
    small_parts = [channel_taps, mixer_gain, norm_gains, shared_taps, step_proj.T]
    flat = jnp.concatenate([p.reshape(-1) for p in small_parts])
    small_len = -(-flat.shape[0] // 2048) * 2048
    small = jnp.pad(flat, (0, small_len - flat.shape[0])).reshape(-1, 128)
    (tok_full, full_query, full_attend, full_inner, full_mamba, hid_own, down_own, sha, sma) = gather_start(
        tokens, query_proj, attend_out, inner_proj, mamba_out, hidden_proj, down_proj, shared_proj, small,
        nd, nt,
    )
    feed = ()
    if nd == 8:
        hid_in, down_in, tok_full = lax.optimization_barrier((hidden_proj, down_proj, tok_full))
        feed = [hid_own, down_own]
        for k in range(1, nt):
            ring = [(i, (i + k) % nt) for i in range(nt)]
            feed += [lax.ppermute(hid_in, "tensor", ring), lax.ppermute(down_in, "tensor", ring)]
    else:
        full_hidden = lax.all_gather(hidden_proj, "tensor", axis=2, tiled=True)
        full_hidden = to_blocks(lax.all_gather(full_hidden, "dp", axis=1, tiled=True), 1, nt)
        full_down = lax.all_gather(down_proj, "tensor", axis=0, tiled=True)
        full_down = to_blocks(lax.all_gather(full_down, "dp", axis=1, tiled=True), 0, nt)

    full_shared = sha.reshape(width, -1)
    sma = sma.reshape(nd, nt, small_len)

    def small_piece(index):
        start = sum(p.size for p in small_parts[:index])
        part = small_parts[index]
        return sma[:, :, start : start + part.size].reshape((nd, nt) + part.shape)

    taps_x = pick(small_piece(0), tensor_index, 1).transpose(1, 2, 0, 3).reshape(CONV + 1, inner)
    gain_mix = pick(small_piece(1), tensor_index, 1).transpose(1, 0, 2).reshape(1, inner)
    full_norms = small_piece(2).transpose(2, 0, 1, 3).reshape(2, width).astype(F32)
    taps_b = small_piece(3).transpose(2, 0, 1, 3).reshape(CONV + 1, -1)
    step_rows = pick(small_piece(4), tensor_index, 1).transpose(1, 0, 2).reshape(heads, width)
    step_rows = jnp.pad(step_rows, ((0, 8 - heads), (0, 0)))
    taps_x = jnp.pad(taps_x.astype(F32), ((0, 7 - CONV), (0, 0)))
    taps_b = jnp.pad(taps_b.astype(F32), ((0, 7 - CONV), (0, 0)))
    gain_mix = gain_mix.astype(F32)
    gain_first = full_norms[0:1]
    gain_second = full_norms[1:2]

    def head_rows(values):
        return jnp.pad(jnp.broadcast_to(values[:, None], (heads, 128)), ((0, 8 - heads), (0, 0)))

    decay = head_rows(-jnp.exp(decay_log.astype(F32)))
    bias = head_rows(step_bias.astype(F32))
    skip = jnp.repeat(skip_weight.astype(F32), SSM_DIM)[None, :]
    q_heads = query_proj.shape[1] // HEAD_SIZE
    kv_head = (tensor_index * q_heads // (QHEADS // KVHEADS)).astype(jnp.int32).reshape(1)
    cosine, sine = rope_wide(group_rows)

    (a1, q, k2, v2, lse, o, xr, zr, br, y, trow, states, squares) = mixers_forward(
        heads, kv_head, tok_full.reshape(group_rows, width), gain_first, full_query, full_inner, step_rows,
        full_shared, cosine, sine, taps_x, taps_b, decay, bias, skip,
    )
    mixed = mix_scatter(
        channels, nt, o, y, zr, squares, gain_mix, full_attend, full_mamba, tokens, tuple(feed)
    )
    m, squares, hidden = mixed[:3]
    if nd == 8:
        full_hidden, full_down = mixed[3:]
    layer_out, dh, dmix, grad_gain_two, feed_pieces = feed_forward(
        nd == 8, hidden, gain_second, cotangent, full_hidden, full_down
    )
    if nd == 8:
        feed_pieces = feed_pieces.reshape((2, 2) + feed_pieces.shape[1:])
        grad_mix, do, dm, dots, feed_own, feed_sums = unmix_gather(
            nt, dmix, y, zr, gain_mix, full_attend, full_mamba, feed_pieces
        )
        feed_rest = jnp.stack(
            [
                lax.ppermute(feed_sums[k - 1], "tensor", [(i, (i + k) % nt) for i in range(nt)])
                for k in range(1, nt)
            ]
        )
    else:
        grad_mix, do, dm, dots = unmix_gather(nt, dmix, y, zr, gain_mix, full_attend, full_mamba)
        hid_full = feed_pieces[:, :, : 2 * units].reshape(8, nt, 2, units // 128, width // 8, 128)
        hid_full = hid_full.transpose(2, 0, 4, 1, 3, 5).reshape(2, nd, width // nd, nt, units)
        hid_sum = cube_scatter(hid_full.transpose(1, 3, 0, 2, 4), nd, BF16)
        down_full = feed_pieces[:, :, 2 * units :].transpose(1, 2, 0, 3)
        down_full = down_full.reshape(nt, units, nd, width // nd)
        down_sum = cube_scatter(down_full.transpose(2, 0, 1, 3), nd, BF16)
        gradient_hidden = chain_scatter(hid_sum, nt)
        gradient_down = chain_scatter(down_sum, nt)

    dq, dkv = attend_back(kv_head, q, k2, v2, lse, do, cosine, sine)
    dz, dx, db, drow, grad_tx, grad_tb, grad_rows, grad_heads = scan_back(
        heads, channels, dm, y, zr, xr, br, trow, states, squares, dots, gain_mix, taps_x, taps_b, decay, bias,
        skip,
    )
    part_one = down_parts(dq, dz, dx, dkv, db, drow, full_query, full_inner, step_rows, full_shared)
    pieces, shared_pieces, grad_step = weight_pieces(a1, dq, dz, dx, dkv, db, drow, o, m, grad_mix)
    block = width // nd
    q_cols = query_proj.shape[1]
    cuts = [0, q_cols, q_cols + attend_out.shape[0]]
    cuts += [cuts[2] + inner, cuts[2] + 2 * inner, cuts[2] + 3 * inner]

    def from_rows(values):
        return values.reshape(8, -1, 128, 128).transpose(0, 2, 1, 3).reshape(width, -1)

    def from_lanes(values):
        return values.transpose(1, 0, 2).reshape(-1, width)

    n_tap = CONV + 1
    over_all = jnp.concatenate([grad_gain_two.reshape(-1), grad_tb[:n_tap].reshape(-1)])
    over_dp = jnp.concatenate(
        [
            grad_tx[:n_tap].reshape(-1),
            grad_rows[0],
            grad_rows[1].reshape(heads, SSM_DIM).sum(axis=1),
            grad_heads[:heads].sum(axis=1),
            grad_heads[8 : 8 + heads].sum(axis=1),
            grad_step[:heads].reshape(-1),
        ]
    )

    def in_rows(values):
        return jnp.pad(values, (0, -values.shape[0] % 1024)).reshape(-1, 128)

    rows_all = in_rows(over_all)
    n_all = rows_all.shape[0]
    small_sums = jnp.concatenate([rows_all, in_rows(over_dp)], axis=0)
    parts = part_one.reshape(nt, local_rows, width)
    if nd == 8:
        shapes = [
            query_proj.shape, attend_out.shape, inner_proj.shape, mamba_out.shape, hidden_proj.shape,
            down_proj.shape,
        ]
        (
            gradient_tokens,
            gradient_query,
            gradient_attend,
            gradient_inner,
            gradient_mamba,
            gradient_hidden,
            gradient_down,
            gradient_shared,
            small_sums,
            grad_gain_one,
        ) = tail(
            nt, n_all, parts, tokens, gain_first, dh, pieces, shared_pieces, small_sums, feed_own, feed_rest,
            shapes,
        )
        grad_gain_one = grad_gain_one.reshape(1, width)
    else:
        token_f32 = tokens.astype(F32)
        _, norm_one_back = jax.vjp(norm_apply, token_f32, gain_first[0])
        grad_from_one, grad_gain_one = norm_one_back(chain_scatter(parts, nt))
        gradient_tokens = (dh + grad_from_one).astype(BF16)
        got = [pieces[:, cuts[i] : cuts[i + 1]] for i in range(5)]

        def over_rows(values):
            return cube_scatter(from_rows(values).reshape(nd, block, -1), nd)

        def over_lanes(values):
            return cube_scatter(from_lanes(values).reshape(-1, nd, block).transpose(1, 0, 2), nd)

        gradient_query = over_rows(got[0])
        gradient_attend = over_lanes(got[1])
        gradient_inner = jnp.stack([over_rows(got[2]), over_rows(got[3])])
        gradient_mamba = over_lanes(got[4])
        shared_cut = shared_pieces.reshape(nd, nt, width // (nd * nt), -1)
        gradient_shared = chain_scatter(cube_scatter(shared_cut, nd, BF16), nt)
        small_sums = lax.psum(small_sums, "dp")
        small_sums = jnp.concatenate(
            [lax.psum(small_sums[:n_all], "tensor"), small_sums[n_all:]], axis=0
        )
        grad_gain_one = lax.psum(grad_gain_one, ("dp", "tensor")).reshape(1, width)
    over_all = small_sums[:n_all].reshape(-1)
    over_dp = small_sums[n_all:].reshape(-1)
    place = d * nt + tensor_index
    norm_w = width // (nd * nt)
    both_norms = jnp.concatenate([grad_gain_one, over_all[:width].reshape(1, width)], axis=0)
    gradient_norms = lax.dynamic_slice_in_dim(both_norms, place * norm_w, norm_w, 1)
    tap_w = shared_taps.shape[1]
    tap_all = over_all[width : width + n_tap * taps_b.shape[1]].reshape(n_tap, -1)
    gradient_taps = lax.dynamic_slice_in_dim(tap_all, place * tap_w, tap_w, 1)
    part = mixer_gain.shape[1]
    n_taps = n_tap * inner
    chan = over_dp[:n_taps].reshape(n_tap, heads, SSM_DIM)
    gain = over_dp[n_taps : n_taps + inner].reshape(heads, SSM_DIM)
    gradient_channel = lax.dynamic_slice_in_dim(chan, d * part, part, 2)
    gradient_mixer = lax.dynamic_slice_in_dim(gain, d * part, part, 1)
    rest = over_dp[n_taps + inner :]
    gradient_skip = rest[:heads]
    gradient_decay = rest[heads : 2 * heads]
    gradient_bias = rest[2 * heads : 3 * heads]
    step_all = rest[3 * heads : 3 * heads + heads * width].reshape(heads, width)
    gradient_step = lax.dynamic_slice_in_dim(step_all, d * block, block, 1).T
    return (
        layer_out,
        gradient_tokens,
        gradient_query,
        gradient_attend,
        gradient_inner,
        gradient_step,
        gradient_mamba,
        gradient_hidden,
        gradient_down,
        gradient_channel,
        gradient_mixer,
        gradient_decay,
        gradient_bias,
        gradient_skip,
        gradient_shared,
        gradient_norms,
        gradient_taps,
    )


def solution(mesh):
    placed = (
        P(("dp", "tensor"), None),
        P("dp", "tensor"),
        P("tensor", "dp"),
        P(None, "dp", "tensor"),
        P("dp", "tensor"),
        P("tensor", "dp"),
        P(None, "dp", "tensor"),
        P("tensor", "dp"),
        P(None, "tensor", "dp"),
        P("tensor", "dp"),
        P("tensor"),
        P("tensor"),
        P("tensor"),
        P(("dp", "tensor"), None),
        P(None, ("dp", "tensor")),
        P(None, ("dp", "tensor")),
        P(("dp", "tensor"), None),
    )
    return jax.shard_map(
        partial(per_device, mesh.shape["dp"], mesh.shape["tensor"]),
        mesh=mesh,
        in_specs=placed,
        out_specs=(
            P(("dp", "tensor"), None),
            P(("dp", "tensor"), None),
            P("dp", "tensor"),
            P("tensor", "dp"),
            P(None, "dp", "tensor"),
            P("dp", "tensor"),
            P("tensor", "dp"),
            P(None, "dp", "tensor"),
            P("tensor", "dp"),
            P(None, "tensor", "dp"),
            P("tensor", "dp"),
            P("tensor"),
            P("tensor"),
            P("tensor"),
            P(("dp", "tensor"), None),
            P(None, ("dp", "tensor")),
            P(None, ("dp", "tensor")),
        ),
        check_vma=False,
    )
```

```python
from functools import partial

import numpy as np
import jax
import jax.numpy as jnp
from jax import lax
from jax.experimental import pallas as pl
from jax.experimental.pallas import tpu as pltpu
from jax.sharding import PartitionSpec as P

MESH = pl.DeviceIdType.MESH

QHEADS = 8
KVHEADS = 2
HEAD_SIZE = 64
SSM_DIM = 64
CONV = 4


epsilon = 1e-05
rope_base = 100000000000.0
neg_large = -1e30
block_len = 128


def norm_apply(values, gain):
    factor = lax.rsqrt(jnp.mean(values * values, axis=-1, keepdims=True) + epsilon)
    return values * factor * gain


def dp_bits(index):
    core = lax.rem(index, 2)
    xbit = lax.rem(index // 2, 2)
    ybit = lax.rem(index // 4, 2)
    return core, xbit, ybit


def remote_copy(src, dst, send, recv, dev):
    return pltpu.make_async_remote_copy(
        src_ref=src, dst_ref=dst, send_sem=send, recv_sem=recv, device_id=dev, device_id_type=MESH
    )


def greet(peers):
    barrier = pltpu.get_barrier_semaphore()
    for peer in peers:
        pl.semaphore_signal(barrier, inc=1, device_id=peer, device_id_type=MESH)
    pl.semaphore_wait(barrier, len(peers))


def other_quarters(d, z, nt):
    return [(d, lax.rem(z + k, nt)) for k in range(1, nt)]


def cube_peers(d):
    core, xbit, ybit = dp_bits(d)
    return d + 1 - 2 * core, d + 2 - 4 * xbit, d + 4 - 8 * ybit


class CubeGather:
    def __init__(self, items, via_y, send, recv, d, z):
        self.items, self.via_y, self.send, self.recv = items, via_y, send, recv
        self.d, self.z = d, z
        self.d_core, self.d_x, self.d_y = cube_peers(d)
        self.d_xy = self.d_x + self.d_y - d
        self.sent = []

    def push(self, i, j, src, dst, peer):
        copy = remote_copy(src, dst, self.send.at[i, j], self.recv.at[i, j], (peer, self.z))
        copy.start()
        self.sent.append(copy)

    def landed(self, i, j, slot):
        at = self.items[i][1]
        remote_copy(
            at(slot), at(slot), self.send.at[i, j], self.recv.at[i, j], (self.d_core, self.z)
        ).wait_recv()

    def start(self, i):
        src, at = self.items[i]
        for j, peer in enumerate((self.d_x, self.d_y, self.d_core)):
            self.push(i, j, src, at(self.d), peer)

    def near(self, i):
        at = self.items[i][1]
        d_x, d_y, d_core = self.d_x, self.d_y, self.d_core
        self.landed(i, 0, d_x)
        if i in self.via_y:
            self.push(i, 3, at(d_x), at(d_x), d_y)
        self.push(i, 4, at(d_x), at(d_x), d_core)
        self.landed(i, 1, d_y)
        if i not in self.via_y:
            self.push(i, 3, at(d_y), at(d_y), d_x)
        self.push(i, 5, at(d_y), at(d_y), d_core)

    def far(self, i):
        at = self.items[i][1]
        self.landed(i, 3, self.d_xy)
        self.push(i, 6, at(self.d_xy), at(self.d_xy), self.d_core)

    def finish(self):
        for i in range(len(self.items)):
            self.landed(i, 2, self.d_core)
            for j in (4, 5, 6):
                self.landed(i, j, self.d_core)
        for copy in self.sent:
            copy.wait_send()


def gather_kernel(nt, *refs):
    (tok, que, att, inn, mam, hid, dwn, sha, sma) = refs[:9]
    (tok_f, que_f, att_f, inn_f, mam_f, hid_f, dwn_f, sha_f, sma_f) = refs[9:18]
    (lsem, zs_send, zs_recv, t_send, t_recv, d_send, d_recv) = refs[18:]
    d = lax.axis_index("dp")
    z = lax.axis_index("tensor")
    greet([(p, z) for p in cube_peers(d)] + other_quarters(d, z, nt))

    small = []
    for i, (src, dst) in enumerate(((sha, sha_f), (sma, sma_f))):
        for k, peer in enumerate(other_quarters(d, z, nt)):
            small.append(remote_copy(src, dst.at[d, z], zs_send.at[i, k], zs_recv.at[i, k], peer))
            small[-1].start()
    q_rows = que.shape[0]
    cols = att.shape[1]
    i_rows = inn.shape[1]
    items = [
        (inn, lambda s: inn_f.at[:, pl.ds(s * i_rows, i_rows)]),
        (que, lambda s: que_f.at[pl.ds(s * q_rows, q_rows)]),
        (att, lambda s: att_f.at[:, pl.ds(pl.multiple_of(s * cols, cols), cols)]),
        (mam, lambda s: mam_f.at[:, pl.ds(pl.multiple_of(s * cols, cols), cols)]),
        (hid, lambda s: hid_f.at[s, z]),
        (dwn, lambda s: dwn_f.at[s, z]),
        (sha_f.at[d], lambda s: sha_f.at[s]),
        (sma_f.at[d], lambda s: sma_f.at[s]),
    ]
    cube = CubeGather(items, (0, 5, 7), d_send, d_recv, d, z)
    locals_ = []
    for i, (src, dst) in enumerate(
        [(sha, sha_f.at[d, z]), (sma, sma_f.at[d, z]), (tok, tok_f.at[z])]
        + [(src, at(d)) for src, at in items[:6]]
    ):
        copy = pltpu.make_async_copy(src, dst, lsem.at[i])
        copy.start()
        locals_.append(copy)
    for i in range(4):
        cube.start(i)
    chain = ChainGather(tok, tok_f, t_send, t_recv, d, z, nt)
    chain.start()
    locals_[0].wait()
    locals_[1].wait()
    for copy in small:
        copy.wait()
    cube.start(6)
    cube.start(7)
    cube.start(4)
    cube.start(5)
    for i in range(4):
        cube.near(i)
    chain.hop(1)
    for i in (6, 7, 4, 5):
        cube.near(i)
    for i in (0, 1, 2, 3, 6, 7):
        cube.far(i)
    for dist in range(2, nt - 1):
        chain.hop(dist)
    cube.far(4)
    cube.far(5)
    if nt > 2:
        chain.hop(nt - 1)
    cube.finish()
    for copy in locals_[2:]:
        copy.wait()
    chain.drain()


def gather_start(tok, que, att, inn, mam, hid, dwn, sha, sma, nd, nt):
    if nd != 8:
        shared = lax.all_gather(sha, ("dp", "tensor"), axis=0)
        small = lax.all_gather(sma, ("dp", "tensor"), axis=0)
        return (
            lax.all_gather(tok, "tensor", axis=0),
            lax.all_gather(que, "dp", axis=0, tiled=True),
            lax.all_gather(att, "dp", axis=1, tiled=True),
            lax.all_gather(inn, "dp", axis=1, tiled=True),
            lax.all_gather(mam, "dp", axis=1, tiled=True),
            None,
            None,
            shared.reshape((nd, nt) + sha.shape),
            small.reshape((nd, nt) + sma.shape),
        )
    bf = jnp.bfloat16
    outs = (
        (nt,) + tok.shape,
        (nd * que.shape[0], que.shape[1]),
        (att.shape[0], nd * att.shape[1]),
        (2, nd * inn.shape[1], inn.shape[2]),
        (mam.shape[0], nd * mam.shape[1]),
        (nd, nt) + hid.shape,
        (nd, nt) + dwn.shape,
        (nd, nt) + sha.shape,
        (nd, nt) + sma.shape,
    )
    anywhere = pl.BlockSpec(memory_space=pl.ANY)
    dma = pltpu.SemaphoreType.DMA
    return pl.pallas_call(
        partial(gather_kernel, nt),
        out_shape=[jax.ShapeDtypeStruct(s, bf) for s in outs],
        in_specs=[anywhere] * 9,
        out_specs=[anywhere] * 9,
        scratch_shapes=[
            dma((9,)), dma((2, nt)), dma((2, nt)), dma((2, nt)), dma((2, nt)),
            dma((8, 7)), dma((8, 7)),
        ],
        compiler_params=pltpu.CompilerParams(collective_id=0, has_side_effects=True),
        name="gather_start",
    )(tok, que, att, inn, mam, hid, dwn, sha, sma)


def pick(values, index, axis=0):
    return lax.dynamic_index_in_dim(values, index, axis, keepdims=False)


def add_low(left, right):
    return (left.astype(jnp.float32) + right.astype(jnp.float32)).astype(jnp.bfloat16)


def chain_scatter(parts, nt):
    z = lax.axis_index("tensor")
    right = left = None
    for t in range(nt - 1):
        to_right = pick(parts, jnp.clip(nt - 1 - t + z, 0, nt - 1))
        to_left = pick(parts, jnp.clip(t - (nt - 1) + z, 0, nt - 1))
        if t > 0:
            to_right = add_low(to_right, right)
            to_left = add_low(to_left, left)
        right = lax.ppermute(to_right, "tensor", [(i, i + 1) for i in range(t + 1)])
        left = lax.ppermute(
            to_left, "tensor", [(nt - 1 - i, nt - 2 - i) for i in range(t + 1)]
        )
    f32 = jnp.float32
    return pick(parts, z).astype(f32) + right.astype(f32) + left.astype(f32)


def cube_scatter(parts, nd, last=jnp.float32):
    return lax.psum_scatter(parts, "dp", scatter_dimension=0, tiled=False).astype(last)


F32, BF16 = jnp.float32, jnp.bfloat16
VMEM_LIMIT = 56 * 1024 * 1024


def dot_nn(a, b):
    return lax.dot_general(a, b, (((1,), (0,)), ((), ())), preferred_element_type=F32)


def dot_nt(a, b):
    return lax.dot_general(a, b, (((1,), (1,)), ((), ())), preferred_element_type=F32)


def dot_tn(a, b):
    return lax.dot_general(a, b, (((0,), (0,)), ((), ())), preferred_element_type=F32)


def sigmoid(v):
    return 1.0 / (1.0 + jnp.exp(-v))


def lanes_of(shape):
    return lax.broadcasted_iota(jnp.int32, shape, len(shape) - 1)


def turn(values, cosine, sine):
    lane = lanes_of(values.shape)
    other = jnp.where(
        lax.rem(lane, HEAD_SIZE) < HEAD_SIZE // 2,
        pltpu.roll(values, 128 - HEAD_SIZE // 2, 1),
        pltpu.roll(values, HEAD_SIZE // 2, 1),
    )
    return values * cosine + other * sine


def softplus(v):
    return jnp.maximum(v, 0.0) + jnp.log1p(jnp.exp(-jnp.abs(v)))


def running_sum(rows):
    lane = lanes_of(rows.shape)
    step = 1
    while step < rows.shape[1]:
        rows = rows + jnp.where(lane >= step, pltpu.roll(rows, step, 1), 0.0)
        step *= 2
    return rows


def running_sum_back(rows):
    lane = lanes_of(rows.shape)
    width = rows.shape[1]
    step = 1
    while step < width:
        rows = rows + jnp.where(lane < width - step, pltpu.roll(rows, width - step, 1), 0.0)
        step *= 2
    return rows


def stack_columns(rows_list):
    used = sum(r.shape[0] for r in rows_list)
    filler = jnp.zeros((128 - used, 128), F32)
    return jnp.concatenate(rows_list + [filler], axis=0).T


def widen(cols, base, heads):
    low = lanes_of((cols.shape[0], 128)) < SSM_DIM
    return jnp.concatenate(
        [
            jnp.where(low, cols[:, base + 2 * p : base + 2 * p + 1],
                      cols[:, base + 2 * p + 1 : base + 2 * p + 2])
            for p in range(heads // 2)
        ],
        axis=1,
    )


def conv_rows(ref, taps, first, rows):
    total = taps[CONV : CONV + 1, :] + taps[0:1, :] * ref[pl.ds(first, rows), :]
    for j in range(1, CONV):
        total = total + taps[j : j + 1, :] * ref[pl.ds(first + j, rows), :]
    return total


def forward_kernel(
    heads, kvh, tok, gain, wq, win, stp, wsh, cosine, sine, tapx, tapb, decay, bias, skip,
    a1_o, q_o, k_o, v_o, lse_o, o_o, x_o, z_o, b_o, y_o, t_o, s_o, sq_o,
    keys, vals, xs, bs, state,
):
    step = pl.program_id(0)
    rows = tok.shape[0]
    second = kvh[0] == 1

    @pl.when(step == 0)
    def _():
        xs[0:8, :] = jnp.zeros((8, xs.shape[1]), F32)
        bs[0:8, :] = jnp.zeros((8, bs.shape[1]), F32)
        state[...] = jnp.zeros(state.shape, F32)

    t = tok[...].astype(F32)
    r = lax.rsqrt(jnp.mean(t * t, axis=1, keepdims=True) + epsilon)
    a1 = (t * r * gain[...]).astype(BF16)
    a1_o[...] = a1
    q = turn(dot_nn(a1, wq[...]), cosine[...], sine[...]).astype(BF16)
    q_o[...] = q
    s = dot_nn(a1, wsh[...])
    low = lanes_of((rows, 128)) < HEAD_SIZE
    k = turn(s[:, :128], cosine[...], sine[...])
    v = s[:, 128:256]
    pick_own = low != second
    k2 = jnp.where(pick_own, k, pltpu.roll(k, 64, 1)).astype(BF16)
    v2 = jnp.where(pick_own, v, pltpu.roll(v, 64, 1))
    k_o[...] = k2
    v_o[...] = v2.astype(BF16)
    place = pl.ds(pl.multiple_of(step * rows, rows), rows)
    keys[place, :] = k2
    vals[:, place] = v2.T.astype(BF16)

    scale = HEAD_SIZE**-0.5

    def attend(blocks):
        n = blocks * rows
        shape = (rows, rows)
        allowed = lax.broadcasted_iota(jnp.int32, shape, 0) <= lanes_of(shape)
        parts = []
        for h in range(2):
            qh = jnp.where(low == (h == 0), q, jnp.zeros_like(q))
            sc = dot_nt(keys[0:n, :], qh) * scale
            last = jnp.where(allowed, sc[n - rows :, :], neg_large)
            sc = jnp.concatenate([sc[: n - rows, :], last], axis=0) if blocks > 1 else last
            top = jnp.max(sc, axis=0, keepdims=True)
            e = jnp.exp(sc - top)
            total = jnp.sum(e, axis=0, keepdims=True)
            lse_o[h : h + 1, :] = top + jnp.log(total)
            parts.append(dot_nn(vals[:, 0:n], e.astype(BF16)) / total)
        sub = lax.broadcasted_iota(jnp.int32, parts[0].shape, 0)
        o_o[...] = jnp.where(sub < HEAD_SIZE, parts[0], parts[1]).T.astype(BF16)

    for i in range(keys.shape[0] // rows):
        pl.when(step == i)(partial(attend, i + 1))

    zr = dot_nn(a1, win[0])
    z_o[...] = zr
    xr = dot_nn(a1, win[1])
    x_o[...] = xr
    br = s[:, 256:]
    b_o[...] = br
    xs[8 : 8 + rows, :] = xr
    bs[8 : 8 + rows, :] = br
    u = conv_rows(xs, tapx, 5, rows)
    x = u * sigmoid(u)
    u = conv_rows(bs, tapb, 5, rows)
    bc = (u * sigmoid(u)).astype(BF16)
    xs[0:8, :] = xs[rows : rows + 8, :]
    bs[0:8, :] = bs[rows : rows + 8, :]
    tr = dot_nt(stp[...], a1)
    t_o[...] = tr
    n_state = bc.shape[1] // 2
    tri_shape = (block_len, block_len)
    lower = lax.broadcasted_iota(jnp.int32, tri_shape, 0) >= lanes_of(tri_shape)
    half = lanes_of(tri_shape) < SSM_DIM
    for c in range(rows // block_len):
        part = slice(c * block_len, (c + 1) * block_len)
        dt = softplus(tr[:, part] + bias[...])
        cum = running_sum(dt * decay[...])
        end = cum[:, block_len - 1 :]
        cols = stack_columns([cum, jnp.exp(cum), dt * jnp.exp(end - cum)])
        xc = x[part]
        x_low = xc.astype(BF16)
        b_low = bc[part, :n_state]
        c_low = bc[part, n_state:]
        cross = dot_nt(c_low, b_low)
        grow = widen(cols, 8, heads)
        y = dot_nn(c_low, state[...].astype(BF16)) * grow + skip[...] * xc
        inner = []
        for p in range(heads // 2):
            mats = []
            for h in (2 * p, 2 * p + 1):
                gap = jnp.where(lower, cols[:, h : h + 1] - cum[h : h + 1, :], neg_large)
                mats.append((cross * jnp.exp(gap) * dt[h : h + 1, :]).astype(BF16))
            xp = x_low[:, 128 * p : 128 * p + 128]
            zero = jnp.zeros_like(xp)
            both = jnp.concatenate([jnp.where(half, xp, zero), jnp.where(half, zero, xp)], axis=0)
            inner.append(dot_nn(jnp.concatenate(mats, axis=1), both))
        y = y + jnp.concatenate(inner, axis=1)
        y_o[part, :] = y
        s_o[c] = state[...]
        carried = (xc * widen(cols, 16, heads)).astype(BF16)
        state[...] = grow[block_len - 1 :, :] * state[...] + dot_tn(b_low, carried)
        zc = zr[part]
        w = y * (zc * sigmoid(zc))
        total = jnp.sum(w * w, axis=1, keepdims=True)
        sq_o[:, part] = jnp.broadcast_to(total, (block_len, 128)).T[0:8, :]


def mixers_forward(heads, kvh, tok, gain, wq, win, stp, wsh, cosine, sine, tapx, tapb, decay, bias, skip):
    total, width = tok.shape
    rows = 256
    inner = heads * SSM_DIM
    pair = wsh.shape[1] - 256
    state = pair // 2
    chunks = rows // block_len

    def whole(v):
        return pl.BlockSpec(v.shape, lambda i: (0,) * v.ndim)

    def tall(n):
        return pl.BlockSpec((rows, n), lambda i: (i, 0))

    wide = pl.BlockSpec((8, rows), lambda i: (0, i))
    sds = jax.ShapeDtypeStruct
    return pl.pallas_call(
        partial(forward_kernel, heads),
        grid=(total // rows,),
        in_specs=[pl.BlockSpec(memory_space=pltpu.SMEM), tall(width), whole(gain), whole(wq), whole(win),
                  whole(stp), whole(wsh), tall(128), tall(128), whole(tapx), whole(tapb),
                  whole(decay), whole(bias), whole(skip)],
        out_specs=[tall(width), tall(128), tall(128), tall(128), wide, tall(128), tall(inner),
                   tall(inner), tall(pair), tall(inner), wide,
                   pl.BlockSpec((chunks, state, inner), lambda i: (i, 0, 0)), wide],
        out_shape=[sds((total, width), BF16), sds((total, 128), BF16), sds((total, 128), BF16),
                   sds((total, 128), BF16), sds((8, total), F32), sds((total, 128), BF16),
                   sds((total, inner), F32), sds((total, inner), F32), sds((total, pair), F32),
                   sds((total, inner), F32), sds((8, total), F32),
                   sds((total // block_len, state, inner), F32), sds((8, total), F32)],
        scratch_shapes=[pltpu.VMEM((total, 128), BF16), pltpu.VMEM((128, total), BF16),
                        pltpu.VMEM((rows + 8, inner), F32), pltpu.VMEM((rows + 8, pair), F32),
                        pltpu.VMEM((state, inner), F32)],
        compiler_params=pltpu.CompilerParams(vmem_limit_bytes=VMEM_LIMIT),
        cost_estimate=pl.CostEstimate(flops=int(5e9), bytes_accessed=int(15e6), transcendentals=int(4e6)),
        name="mixers_forward",
    )(kvh, tok, gain, wq, win, stp, wsh, cosine, sine, tapx, tapb, decay, bias, skip)


def attend_back(step, kvh, q, k2, v2, lse, do, cosine, sine, cos_all, sin_all, dq_o, dkv_o, dk, dv):
    rows = q.shape[0]
    steps = k2.shape[0] // rows
    scale = HEAD_SIZE**-0.5
    low = lanes_of((rows, 128)) < HEAD_SIZE

    @pl.when(step == 0)
    def _():
        dk[...] = jnp.zeros(dk.shape, F32)
        dv[...] = jnp.zeros(dv.shape, F32)

    def back(blocks):
        n = blocks * rows
        shape = (rows, rows)
        allowed = lax.broadcasted_iota(jnp.int32, shape, 0) <= lanes_of(shape)
        qs, dos, ps, dss, dqs = [], [], [], [], []
        for h in range(2):
            mine = low == (h == 0)
            qh = jnp.where(mine, q[...], jnp.zeros_like(q[...]))
            doh = jnp.where(mine, do[...], jnp.zeros_like(do[...]))
            sc = dot_nt(k2[0:n, :], qh) * scale - lse[h : h + 1, :]
            last = jnp.where(allowed, sc[n - rows :, :], neg_large)
            sc = jnp.concatenate([sc[: n - rows, :], last], axis=0) if blocks > 1 else last
            p = jnp.exp(sc)
            dp = dot_nt(v2[0:n, :], doh)
            centre = jnp.sum(p * dp, axis=0, keepdims=True)
            ds = (p * (dp - centre)).astype(BF16)
            qs.append(qh)
            dos.append(doh)
            ps.append(p.astype(BF16))
            dss.append(ds)
            dqs.append(dot_tn(ds, k2[0:n, :]) * scale)
        dk[0:n, :] += dot_nn(jnp.concatenate(dss, axis=1), jnp.concatenate(qs, axis=0)) * scale
        dv[0:n, :] += dot_nn(jnp.concatenate(ps, axis=1), jnp.concatenate(dos, axis=0))
        dq_o[...] = turn(jnp.where(low, dqs[0], dqs[1]), cosine[...], -sine[...]).astype(BF16)

    for i in range(steps):
        pl.when(step == 2 * i)(partial(back, i + 1))

    @pl.when(step == 2 * steps - 1)
    def _():
        own = (lanes_of(dk.shape) < HEAD_SIZE) != (kvh[0] == 1)
        g = dk[...]
        g = turn(g + pltpu.roll(g, 64, 1), cos_all[...], -sin_all[...])
        dkv_o[:, 0:128] = jnp.where(own, g, 0.0).astype(BF16)
        g = dv[...]
        g = g + pltpu.roll(g, 64, 1)
        dkv_o[:, 128:256] = jnp.where(own, g, 0.0).astype(BF16)


def back_kernel(heads, channels, nt, feed, *refs):
    step = pl.program_id(0)
    if feed:
        d = lax.axis_index("dp")
        z = lax.axis_index("tensor")
        feed_in, feed_o, came, f_send, f_recv = refs[0], refs[38], refs[46], refs[47], refs[48]
        copies = [
            remote_copy(feed_in.at[k], came.at[k], f_send.at[k], f_recv.at[k], peer)
            for k, peer in enumerate(other_quarters(d, z, nt))
        ]

        @pl.when(step == 0)
        def _():
            greet(other_quarters(d, z, nt))
            for copy in copies:
                copy.start()

        refs = refs[1:38] + refs[39:46]
    attend_back(step, *refs[:10], *refs[27:29], *refs[37:39])
    scan_back(heads, channels, step, *refs[10:27], *refs[29:37], *refs[39:44])
    if feed:

        @pl.when(step == pl.num_programs(0) - 1)
        def _():
            total = None
            for k, copy in enumerate(copies):
                copy.wait()
                value = came[k].astype(F32)
                total = value if total is None else total + value
            feed_o[...] = total


def scan_back(
    heads, channels, step, dm, y, zr, xr, xp, br, bp, trow, states, rsum, dots, gain, tapx, tapb, decay,
    bias, skip,
    dz_o, dx_o, db_o, dt_o, gx_o, gb_o, gm_o, gh_o,
    xs, bs, dxs, dbs, dstate,
):
    last_step = pl.num_programs(0) - 1
    first = step == last_step
    rows = block_len
    inner = heads * SSM_DIM
    n_state = br.shape[1] // 2

    @pl.when(step == 0)
    def _():
        dxs[rows : rows + 8, :] = jnp.zeros((8, inner), F32)
        dbs[rows : rows + 8, :] = jnp.zeros((8, 2 * n_state), F32)
        dstate[...] = jnp.zeros(dstate.shape, F32)
        gx_o[...] = jnp.zeros(gx_o.shape, F32)
        gb_o[...] = jnp.zeros(gb_o.shape, F32)
        gm_o[...] = jnp.zeros(gm_o.shape, F32)
        gh_o[...] = jnp.zeros(gh_o.shape, F32)

    xs[0:8, :] = jnp.where(first, 0.0, xp[...])
    bs[0:8, :] = jnp.where(first, 0.0, bp[...])
    xs[8 : 8 + rows, :] = xr[...]
    bs[8 : 8 + rows, :] = br[...]
    ux = conv_rows(xs, tapx, 5, rows)
    sx = sigmoid(ux)
    x = ux * sx
    ub = conv_rows(bs, tapb, 5, rows)
    sb = sigmoid(ub)
    bc = (ub * sb).astype(BF16)
    b_low, c_low = bc[:, :n_state], bc[:, n_state:]

    pre = trow[...] + bias[...]
    dt = softplus(pre)
    cum = running_sum(dt * decay[...])
    end = cum[:, rows - 1 :]
    fade = jnp.exp(end - cum)
    inv = lax.rsqrt(rsum[...] / channels + epsilon)
    cols = stack_columns(
        [cum, jnp.exp(cum), dt * fade, dt, inv, inv * inv * inv * dots[...] / channels]
    )
    r = cols[:, 32:33]
    kk = cols[:, 40:41]
    z = zr[...]
    sz = sigmoid(z)
    silu_z = z * sz
    yv = y[...]
    w = yv * silu_z
    dmv = dm[...]
    dw = r * gain[...] * dmv - w * kk
    gm_o[0:1, :] += jnp.sum(dmv * w * r, axis=0, keepdims=True)
    dy = dw * silu_z
    dz_o[...] = (dw * yv * sz * (1.0 + z * (1.0 - sz))).astype(BF16)
    gm_o[1:2, :] += jnp.sum(dy * x, axis=0, keepdims=True)

    grow = widen(cols, 8, heads)
    tail = widen(cols, 16, heads)
    dt_wide = widen(cols, 24, heads)
    x_low = x.astype(BF16)
    dy_low = dy.astype(BF16)
    state = states[0]
    state_low = state.astype(BF16)
    ds = dstate[...]
    ds_low = ds.astype(BF16)
    cross = dot_nt(b_low, c_low)
    shape = (rows, rows)
    upper = lax.broadcasted_iota(jnp.int32, shape, 0) <= lanes_of(shape)
    half = lanes_of(shape) < SSM_DIM
    lane = lanes_of(shape)
    dcross = jnp.zeros(shape, F32)
    col_sums = jnp.zeros(shape, F32)
    row_sums = []
    mids = []
    for p in range(heads // 2):
        span = slice(128 * p, 128 * p + 128)
        xpair, dypair = x_low[:, span], dy_low[:, span]
        zero = jnp.zeros_like(xpair)
        dys = (jnp.where(half, dypair, zero), jnp.where(half, zero, dypair))
        mats = []
        for k in range(2):
            h = 2 * p + k
            gap = jnp.where(upper, cum[h : h + 1, :] - cols[:, h : h + 1], neg_large)
            faded = jnp.exp(gap)
            mats.append((cross * faded).astype(BF16))
            t = dot_nt(xpair, dys[k]) * faded
            dt_col = cols[:, 24 + h : 25 + h]
            td = t * dt_col
            dcross = dcross + td
            row_sums.append(jnp.sum(td * cross, axis=0, keepdims=True))
            col = jnp.sum(t * cross, axis=1, keepdims=True)
            col_sums = jnp.where(lane == h, col, col_sums)
        mids.append(dot_nn(jnp.concatenate(mats, axis=1), jnp.concatenate(dys, axis=0)))
    mid = jnp.concatenate(mids, axis=1)
    row_sums = jnp.concatenate(row_sums + [jnp.zeros((8 - heads, rows), F32)], axis=0)
    col_sums = col_sums.T[0:8, :]

    dye = dy * grow
    dye_low = dye.astype(BF16)
    xd = x * tail
    xd_low = xd.astype(BF16)
    from_b = dot_nn(b_low, ds_low)
    through = dot_nn(c_low, state_low)
    dcross_low = dcross.astype(BF16)
    db = dot_nn(dcross_low, c_low) + dot_nt(xd_low, ds_low)
    dc = dot_tn(dcross_low, b_low) + dot_nt(dye_low, state_low)

    head_of = lax.broadcasted_iota(jnp.int32, (8, inner), 0)
    chan = lanes_of((8, inner)) // SSM_DIM
    ones = jnp.where(head_of == chan, 1.0, 0.0).astype(BF16)

    def by_head(v):
        high = v.astype(BF16)
        rest = (v - high.astype(F32)).astype(BF16)
        return dot_nt(ones, high) + dot_nt(ones, rest)

    grown = by_head(dye * through)
    ended = by_head(x * from_b)
    kept = jnp.sum(ds * state, axis=0, keepdims=True) * grow[rows - 1 :, :]
    kept = jnp.where(head_of == chan, kept, 0.0).sum(axis=1, keepdims=True)
    pulled = dt * fade * ended
    lane8 = lanes_of((8, rows))
    at_end = kept + jnp.sum(pulled, axis=1, keepdims=True)
    dcum = row_sums - dt * col_sums + grown - pulled + jnp.where(lane8 == rows - 1, at_end, 0.0)
    da = running_sum_back(dcum)
    ddt = col_sums + fade * ended + decay[...] * da
    dpre = ddt * sigmoid(pre)
    dt_o[...] = dpre
    gh_o[0:8, :] += da * dt * decay[...]
    gh_o[8:16, :] += dpre

    dstate[...] = grow[rows - 1 :, :] * ds + dot_tn(c_low, dye_low)
    dx = skip[...] * dy + dt_wide * mid + tail * from_b
    dux = dx * sx * (1.0 + ux * (1.0 - sx))
    dub = jnp.concatenate([db, dc], axis=1) * sb * (1.0 + ub * (1.0 - sb))
    for taps, src, d, buf, acc, out in (
        (tapx, xs, dux, dxs, gx_o, dx_o),
        (tapb, bs, dub, dbs, gb_o, db_o),
    ):
        buf[0:rows, :] = d
        total = taps[CONV - 1 : CONV, :] * d
        for j in range(CONV - 1):
            total = total + taps[j : j + 1, :] * buf[pl.ds(CONV - 1 - j, rows), :]
        out[...] = total.astype(BF16)
        for j in range(CONV):
            acc[j : j + 1, :] += jnp.sum(d * src[pl.ds(5 + j, rows), :], axis=0, keepdims=True)
        acc[CONV : CONV + 1, :] += jnp.sum(d, axis=0, keepdims=True)
        buf[rows : rows + 8, :] = d[0:8, :]


def mixers_back(
    heads, channels, nt, kvh, q, k2, v2, lse, do, cosine, sine, dm, y, zr, xr, br, trow, states, rsum, dots,
    gain, tapx, tapb, decay, bias, skip, feed=None,
):
    total, inner = y.shape
    pair = br.shape[1]
    rows = block_len
    steps = total // rows
    per = rows // 8
    q_rows = 2 * rows

    def whole(v):
        return pl.BlockSpec(v.shape, lambda i: (0,) * v.ndim)

    def tall(n):
        return pl.BlockSpec((rows, n), lambda i: (steps - 1 - i, 0))

    def before(n):
        return pl.BlockSpec((8, n), lambda i: (jnp.maximum((steps - 1 - i) * per - 1, 0), 0))

    wide = pl.BlockSpec((8, rows), lambda i: (0, steps - 1 - i))
    ask = pl.BlockSpec((q_rows, 128), lambda i: (i // 2, 0))
    sds = jax.ShapeDtypeStruct

    def fixed(*shape):
        return pl.BlockSpec(shape, lambda i: (0,) * len(shape))

    in_specs = [pl.BlockSpec(memory_space=pltpu.SMEM), ask, whole(k2), whole(v2),
                pl.BlockSpec((8, q_rows), lambda i: (0, i // 2)), ask, ask, ask, whole(cosine), whole(sine),
                tall(inner), tall(inner), tall(inner), tall(inner), before(inner), tall(pair),
                before(pair), wide, pl.BlockSpec((1, pair // 2, inner), lambda i: (steps - 1 - i, 0, 0)),
                wide, wide, whole(gain), whole(tapx), whole(tapb), whole(decay), whole(bias), whole(skip)]
    out_specs = [ask, fixed(total, 256), tall(inner), tall(inner), tall(pair), wide, fixed(8, inner),
                 fixed(8, pair), fixed(8, inner), fixed(16, rows)]
    out_shape = [sds((total, 128), BF16), sds((total, 256), BF16), sds((total, inner), BF16),
                 sds((total, inner), BF16), sds((total, pair), BF16), sds((8, total), F32),
                 sds((8, inner), F32), sds((8, pair), F32), sds((8, inner), F32), sds((16, rows), F32)]
    scratch = [pltpu.VMEM((total, 128), F32), pltpu.VMEM((total, 128), F32),
               pltpu.VMEM((rows + 8, inner), F32), pltpu.VMEM((rows + 8, pair), F32),
               pltpu.VMEM((rows + 8, inner), F32), pltpu.VMEM((rows + 8, pair), F32),
               pltpu.VMEM((pair // 2, inner), F32)]
    args = [kvh, q, k2, v2, lse, do, cosine, sine, cosine, sine, dm, y, zr, xr, xr, br, br, trow, states,
            rsum, dots, gain, tapx, tapb, decay, bias, skip]
    extra = {}
    if feed is not None:
        dma = pltpu.SemaphoreType.DMA
        args = [feed] + args
        in_specs = [whole(feed)] + in_specs
        out_specs = out_specs + [fixed(*feed.shape[1:])]
        out_shape = out_shape + [sds(feed.shape[1:], F32)]
        scratch = scratch + [pltpu.VMEM(feed.shape, BF16), dma((nt - 1,)), dma((nt - 1,))]
        extra = dict(collective_id=5, has_side_effects=True)
    return pl.pallas_call(
        partial(back_kernel, heads, channels, nt, feed is not None),
        grid=(steps,),
        in_specs=in_specs,
        out_specs=out_specs,
        out_shape=out_shape,
        scratch_shapes=scratch,
        compiler_params=pltpu.CompilerParams(vmem_limit_bytes=VMEM_LIMIT, **extra),
        cost_estimate=pl.CostEstimate(flops=int(6e9), bytes_accessed=int(18e6), transcendentals=int(7e6)),
        name="mixers_back",
    )(*args)


def whole_spec(v):
    return pl.BlockSpec(v.shape, lambda i: (0,) * v.ndim)


def feed_kernel(paired, hid, gain, cot, whid, wdown, out_o, dh_o, dmix_o, gg_o, piece_o, a2, a2t, acc, dacc, *pair):
    step = pl.program_id(0)
    tiles = pl.num_programs(0)
    width = hid.shape[1]
    blocks = width // 128
    units = whid.shape[4]
    d = lax.axis_index("dp")
    z = lax.axis_index("tensor")
    core = lax.rem(d, 2)
    if paired:
        (sent, came, send, recv) = pair
        sibling = d + 1 - 2 * core

        def swap(tile):
            return remote_copy(
                sent.at[tile], came.at[tile], send.at[tile], recv.at[tile], (sibling, z)
            )

        pl.when(step == 0)(lambda: greet([(sibling, z)]))

    @pl.when(step == 0)
    def _():
        v = hid[...]
        f = lax.rsqrt(jnp.mean(v * v, axis=1, keepdims=True) + epsilon)
        low = (v * f * gain[...]).astype(BF16)
        a2[...] = low
        a2t[...] = low.T
        acc[...] = jnp.zeros(acc.shape, F32)
        dacc[...] = jnp.zeros(dacc.shape, F32)

    w_gate = whid[:, 0, 0].reshape(width, units)
    w_up = whid[:, 0, 1].reshape(width, units)
    w_down = jnp.concatenate([wdown[k, 0] for k in range(blocks)], axis=1)
    g = dot_nn(a2[...], w_gate)
    u = dot_nn(a2[...], w_up)
    s = sigmoid(g)
    f_low = (g * s * u).astype(BF16)
    c = cot[...]
    acc[...] += dot_nn(f_low, w_down)
    df = dot_nt(c, w_down)
    du = (df * g * s).astype(BF16)
    dg = (df * u * s * (1.0 + g * (1.0 - s))).astype(BF16)
    dacc[...] += dot_nt(dg, w_gate) + dot_nt(du, w_up)

    per = units // 128
    quarter_units = (piece_o.shape[2] // 3)
    tiles_per = quarter_units // units

    def places(tile):
        part = lax.rem(tile, tiles_per)
        rows = [(k * quarter_units + part * units + cb * 128, 128) for k in range(2) for cb in range(per)]
        return tile // tiles_per, rows + [(2 * quarter_units + part * units, units)]

    quarter, rows = places(step)
    values = []
    for grad in (dg, du):
        full = dot_nn(a2t[...], grad).astype(BF16)
        for cb in range(per):
            values.append(full[:, 128 * cb : 128 * cb + 128].reshape(blocks, 128, 128))
    gd = dot_tn(f_low, c).astype(BF16)
    values.append(jnp.stack([gd[:, 128 * k : 128 * k + 128] for k in range(blocks)]))
    first = 0
    for value, (row, n) in zip(values, rows):
        at = pl.ds(pl.multiple_of(row, 128), n)
        if paired:
            value = value.reshape(blocks // 2, 2, n, 128)
            even, odd = value[:, 0], value[:, 1]
            piece_o[:, quarter, at, :] = jnp.where(core == 0, even, odd)
            sent[step, :, first : first + n, :] = jnp.where(core == 0, odd, even)
            first += n
        else:
            piece_o[:, quarter, at, :] = value

    if paired:
        swap(step).start()

        def take(tile):
            swap(tile).wait_recv()
            quarter, rows = places(tile)
            first = 0
            for row, n in rows:
                at = pl.ds(pl.multiple_of(row, 128), n)
                piece_o[:, quarter, at, :] = (
                    piece_o[:, quarter, at, :].astype(F32)
                    + came[tile, :, first : first + n, :].astype(F32)
                ).astype(BF16)
                first += n

        pl.when(step > 0)(lambda: take(step - 1))

    @pl.when(step == tiles - 1)
    def _():
        v = hid[...]
        out_o[...] = (v + acc[...]).astype(BF16)
        f = lax.rsqrt(jnp.mean(v * v, axis=1, keepdims=True) + epsilon)
        dy = dacc[...]
        gg_o[...] = jnp.sum(dy * v * f, axis=0, keepdims=True)
        gdy = dy * gain[...]
        lean = jnp.sum(gdy * v, axis=1, keepdims=True) * (f * f * f / width)
        dh = cot[...].astype(F32) + (f * gdy - v * lean)
        dh_o[...] = dh
        dmix_o[...] = dh.astype(BF16)
        if paired:
            take(tiles - 1)

            def sent_all(tile, carry):
                swap(tile).wait_send()
                return carry

            lax.fori_loop(0, tiles, sent_all, 0)


def feed_forward(paired, hid, gain, cot, whid, wdown):
    rows, width = hid.shape
    blocks, nt, _, depth, units = whid.shape
    tile = 256
    per = units // tile
    hid_spec = pl.BlockSpec((blocks, 1, 2, depth, tile), lambda i: (0, i // per, 0, 0, lax.rem(i, per)))
    down_spec = pl.BlockSpec((blocks, 1, tile, 128), lambda i: (0, i // per, lax.rem(i, per), 0))
    sds = jax.ShapeDtypeStruct
    kept = blocks // 2 if paired else blocks
    piece = (kept, nt, 3 * units, 128)
    dma = pltpu.SemaphoreType.DMA
    scratch = []
    extra = {}
    if paired:
        box = pltpu.VMEM((nt * per, kept, 3 * tile, 128), BF16)
        scratch = [box, box, dma((nt * per,)), dma((nt * per,))]
        extra = dict(collective_id=4, has_side_effects=True)

    def fixed(*shape):
        return pl.BlockSpec(shape, lambda i: (0,) * len(shape))

    return pl.pallas_call(
        partial(feed_kernel, paired),
        grid=(nt * per,),
        in_specs=[fixed(rows, width), fixed(1, width), fixed(rows, width), hid_spec, down_spec],
        out_specs=[fixed(rows, width), fixed(rows, width), fixed(rows, width), fixed(1, width),
                   fixed(*piece)],
        out_shape=[sds((rows, width), BF16), sds((rows, width), F32), sds((rows, width), BF16),
                   sds((1, width), F32), sds(piece, BF16)],
        scratch_shapes=[pltpu.VMEM((rows, width), BF16), pltpu.VMEM((width, rows), BF16),
                        pltpu.VMEM((rows, width), F32), pltpu.VMEM((rows, width), F32)] + scratch,
        compiler_params=pltpu.CompilerParams(vmem_limit_bytes=VMEM_LIMIT, **extra),
        cost_estimate=pl.CostEstimate(flops=int(1e10), bytes_accessed=int(26e6), transcendentals=int(5e5)),
        name="feed_forward",
    )(hid, gain, cot, whid, wdown)


def row_columns(rows_list, rows):
    return jnp.concatenate(
        [stack_columns([r[:, c : c + 128] for r in rows_list]) for c in range(0, rows, 128)], axis=0
    )


def down_rows(at, dq, dz, dx, dkv, db, drow, wq, win, stp, wsh):
    total = dot_nt(dq[at, :], wq[...]) + dot_nt(dz[at, :], win[0]) + dot_nt(dx[at, :], win[1])
    total = total + dot_nt(dkv[at, :], wsh[:, 0:256]) + dot_nt(db[at, :], wsh[:, 256:])
    return total + dot_tn(drow[:, at].astype(BF16), stp[...])


def down_kernel(dq, dz, dx, dkv, db, drow, wq, win, stp, wsh, part_o):
    every = slice(None)
    part_o[...] = down_rows(every, dq, dz, dx, dkv, db, drow, wq, win, stp, wsh).astype(BF16)


def down_parts(dq, dz, dx, dkv, db, drow, wq, win, stp, wsh):
    total, inner = dz.shape
    width = wq.shape[0]
    rows = 256

    def tall(v):
        return pl.BlockSpec((rows, v.shape[1]), lambda i: (i, 0))

    wide = pl.BlockSpec((8, rows), lambda i: (0, i))
    return pl.pallas_call(
        down_kernel,
        grid=(total // rows,),
        in_specs=[tall(dq), tall(dz), tall(dx), tall(dkv), tall(db), wide, whole_spec(wq), whole_spec(win),
                  whole_spec(stp), whole_spec(wsh)],
        out_specs=pl.BlockSpec((rows, width), lambda i: (i, 0)),
        out_shape=jax.ShapeDtypeStruct((total, width), BF16),
        compiler_params=pltpu.CompilerParams(vmem_limit_bytes=VMEM_LIMIT),
        cost_estimate=pl.CostEstimate(flops=int(3e9), bytes_accessed=int(8e6), transcendentals=0),
        name="down_parts",
    )(dq, dz, dx, dkv, db, drow, wq, win, stp, wsh)


def weight_columns(a, g, dq, dz, dx, dkv, db, ot, mt, put, put_shared):
    at = a.T
    inner = dz.shape[1]

    def by_rows(values, first):
        for j in range(values.shape[1] // 128):
            for k in range(2):
                put(k, first + 128 * j, values[128 * k : 128 * (k + 1), 128 * j : 128 * (j + 1)])

    def by_lanes(values, first):
        for k in range(2):
            put(k, first, values[:, 128 * k : 128 * (k + 1)])

    by_rows(dot_nn(at, dq[...]).astype(BF16), 0)
    by_lanes(dot_nn(ot[...], g).astype(BF16), 128)
    by_rows(dot_nn(at, dz[...]).astype(BF16), 256)
    by_rows(dot_nn(at, dx[...]).astype(BF16), 256 + inner)
    by_lanes(dot_nn(mt[...], g).astype(BF16), 256 + 2 * inner)
    for first, values in ((0, dot_nn(at, dkv[...]).astype(BF16)), (256, dot_nn(at, db[...]).astype(BF16))):
        for k in range(2):
            put_shared(k, first, values[128 * k : 128 * (k + 1)])


def weight_kernel(a1, dq, dz, dx, dkv, db, drow, o, m, dmix, piece_o, shared_o, step_o, ot, mt):
    @pl.when(pl.program_id(0) == 0)
    def _():
        ot[...] = o[...].T
        mt[...] = m[...].T

    step_o[...] = dot_nn(drow[...].astype(BF16), a1[...])

    def put(k, first, values):
        piece_o[k, first : first + values.shape[0], :] = values

    def put_shared(k, first, values):
        shared_o[k, :, first : first + values.shape[1]] = values

    weight_columns(a1[...], dmix[...], dq, dz, dx, dkv, db, ot, mt, put, put_shared)


def weight_pieces(a1, dq, dz, dx, dkv, db, drow, o, m, dmix):
    total, width = a1.shape
    inner = dz.shape[1]
    n = 256 + 3 * inner
    shared = 256 + db.shape[1]
    cols = pl.BlockSpec((total, 256), lambda i: (0, i))
    sds = jax.ShapeDtypeStruct
    args = (dq, dz, dx, dkv, db, drow, o, m)
    return pl.pallas_call(
        weight_kernel,
        grid=(width // 256,),
        in_specs=[cols] + [whole_spec(v) for v in args] + [cols],
        out_specs=[pl.BlockSpec((2, n, 128), lambda i: (i, 0, 0)),
                   pl.BlockSpec((2, 128, shared), lambda i: (i, 0, 0)),
                   pl.BlockSpec((8, 256), lambda i: (0, i))],
        out_shape=[sds((width // 128, n, 128), BF16), sds((width // 128, 128, shared), BF16),
                   sds((8, width), F32)],
        scratch_shapes=[pltpu.VMEM((128, total), BF16), pltpu.VMEM((inner, total), BF16)],
        compiler_params=pltpu.CompilerParams(vmem_limit_bytes=VMEM_LIMIT),
        cost_estimate=pl.CostEstimate(flops=int(4e9), bytes_accessed=int(12e6), transcendentals=0),
        name="weight_pieces",
    )(a1, *args, dmix)


class Exchange:
    def __init__(self, own, landed, send, recv, d, z, nt):
        self.own, self.landed, self.z, self.nt = own, landed, z, nt
        self.copies = [
            remote_copy(own, landed.at[k - 1], send.at[k - 1], recv.at[k - 1], peer)
            for k, peer in enumerate(other_quarters(d, z, nt), 1)
        ]

    def start(self):
        for copy in self.copies:
            copy.start()

    def wait(self):
        for copy in self.copies:
            copy.wait()

    def total(self):
        total = None
        for q in range(self.nt):
            value = jnp.where(self.z == q, self.own[...].astype(F32), 0.0)
            for k in range(1, self.nt):
                value = value + jnp.where(
                    lax.rem(self.z - k + self.nt, self.nt) == q, self.landed[k - 1].astype(F32), 0.0
                )
            total = value if total is None else total + value
        return total


class ChainScatter:
    def __init__(self, parts, bufs, landed, send, recv, d, z, nt):
        self.parts, self.bufs, self.landed = parts, bufs, landed
        self.send, self.recv = send, recv
        self.d, self.z, self.nt = d, z, nt

    def active(self, way, t):
        z, nt = self.z, self.nt
        if way == 0:
            return (z <= t) & (z < nt - 1)
        return (nt - 1 - z <= t) & (z > 0)

    def copy(self, way, t):
        dev = (self.d, self.z + 1 if way == 0 else self.z - 1)
        return remote_copy(
            self.bufs.at[way, t], self.landed.at[way, t], self.send.at[way, t], self.recv.at[way, t], dev
        )

    def arrives(self, way, t):
        z, nt = self.z, self.nt
        if way == 0:
            return (z >= 1) & (z - 1 <= t)
        return (z < nt - 1) & (nt - 2 - z <= t)

    def step(self, t):
        z, nt = self.z, self.nt
        for way in range(2):
            q = nt - 1 - t + z if way == 0 else t - (nt - 1) + z

            def run():
                value = self.parts[q]
                if t > 0:
                    came = self.arrives(way, t - 1)

                    @pl.when(came)
                    def _():
                        self.copy(way, t - 1).wait_recv()
                        total = value.astype(F32) + self.landed[way, t - 1].astype(F32)
                        self.bufs[way, t] = total.astype(BF16)

                    @pl.when(jnp.logical_not(came))
                    def _():
                        self.bufs[way, t] = value
                else:
                    self.bufs[way, t] = value
                self.copy(way, t).start()

            pl.when(self.active(way, t))(run)

    def finish(self, out):
        out[...] = self.parts[self.z].astype(F32)
        t = self.nt - 2
        for way in range(2):

            @pl.when(self.arrives(way, t))
            def _():
                self.copy(way, t).wait_recv()
                out[...] += self.landed[way, t].astype(F32)

    def drain(self):
        for way in range(2):
            for t in range(self.nt - 1):
                pl.when(self.active(way, t))(self.copy(way, t).wait_send)


def chain_scratch(nt, rows, width):
    dma = pltpu.SemaphoreType.DMA
    return [
        pltpu.VMEM((2, nt - 1, rows, width), BF16),
        pltpu.VMEM((2, nt - 1, rows, width), BF16),
        dma((2, nt - 1)),
        dma((2, nt - 1)),
    ]


def mix_scatter_kernel(channels, nt, feed, *refs):
    (o, y, z_in, sq, gain, watt, wmam, tok), refs = refs[:8], refs[8:]
    if feed:
        refs = refs[2:]
        turned, refs = refs[: 2 * (nt - 1)], refs[2 * (nt - 1) :]
        (m_o, sq_o, hid_o, hid_f, dwn_f), refs = refs[:5], refs[5:]
        (lsem, f_send, f_recv), refs = refs[:3], refs[3:]
    else:
        (m_o, sq_o, hid_o), refs = refs[:3], refs[3:]
    (sq_land, sq_send, sq_recv, parts, bufs, landed, c_send, c_recv) = refs
    d = lax.axis_index("dp")
    z = lax.axis_index("tensor")
    rows = tok.shape[0]
    peers = [(p, z) for p in cube_peers(d)] if feed else []
    greet(peers + other_quarters(d, z, nt))
    squares = Exchange(sq, sq_land, sq_send, sq_recv, d, z, nt)
    squares.start()
    n = 2 * (nt - 1)
    if feed:
        items = []
        for k in range(1, nt):
            q = lax.rem(z - k + nt, nt)
            items.append((turned[2 * k - 2], lambda s, q=q: hid_f.at[s, q]))
            items.append((turned[2 * k - 1], lambda s, q=q: dwn_f.at[s, q]))
        cube = CubeGather(items, (0, 3, 4), f_send, f_recv, d, z)
        for i in range(n):
            cube.start(i)
        locals_ = []
        for i, (src, dst) in enumerate([(src, at(d)) for src, at in items]):
            locals_.append(pltpu.make_async_copy(src, dst, lsem.at[i]))
            locals_[-1].start()
    chain = ChainScatter(parts, bufs, landed, c_send, c_recv, d, z, nt)
    squares.wait()
    sq_o[...] = squares.total()

    def part(q):
        at = pl.ds(pl.multiple_of(q * rows, rows), rows)
        total = sq_o[:, at]
        r = row_columns([lax.rsqrt(total / channels + epsilon)], rows)[:, 0:1]
        zv = z_in[at, :]
        m = (y[at, :] * (zv * sigmoid(zv)) * r * gain[...]).astype(BF16)
        m_o[at, :] = m
        parts[q] = (dot_nn(o[at, :], watt[...]) + dot_nn(m, wmam[...])).astype(BF16)

    first = jnp.where(z < nt // 2, nt - 1, 0)
    part(first)
    chain.step(0)

    def rest(i, carry):
        part(lax.rem(first + 1 + i, nt))
        return carry

    lax.fori_loop(0, nt - 1, rest, 0)
    if feed:
        cube.near(0)
        cube.near(1)
    for t in range(1, nt - 1):
        chain.step(t)
        if feed:
            cube.near(2 * t)
            cube.near(2 * t + 1)
            cube.far(2 * t - 2)
            cube.far(2 * t - 1)
    if feed:
        cube.far(n - 2)
        cube.far(n - 1)
    chain.finish(hid_o)
    hid_o[...] += tok[...].astype(F32)
    chain.drain()
    if feed:
        cube.finish()
        for copy in locals_:
            copy.wait()


def mix_scatter(channels, nt, o, y, zr, sq, gain, watt, wmam, tok, feed=()):
    total, inner = y.shape
    rows, width = tok.shape
    dma = pltpu.SemaphoreType.DMA
    sds = jax.ShapeDtypeStruct
    vmem = pl.BlockSpec(memory_space=pltpu.VMEM)
    anywhere = pl.BlockSpec(memory_space=pl.ANY)
    outs = [sds((total, inner), BF16), sds((8, total), F32), sds((rows, width), F32)]
    scratch = []
    n = 2 * (nt - 1)
    if feed:
        for v in feed[:2]:
            outs.append(sds(v.shape, BF16))
        scratch = [dma((n,)), dma((n, 7)), dma((n, 7))]
    return pl.pallas_call(
        partial(mix_scatter_kernel, channels, nt, bool(feed)),
        in_specs=[vmem] * 8 + [anywhere] * len(feed[:2]) + [vmem] * len(feed[2:]),
        out_specs=[vmem] * 3 + [anywhere] * (len(outs) - 3),
        out_shape=outs,
        input_output_aliases={8: 3, 9: 4} if feed else {},
        scratch_shapes=scratch + [pltpu.VMEM((nt - 1, 8, total), F32), dma((nt - 1,)), dma((nt - 1,)),
                        pltpu.VMEM((nt, rows, width), BF16)] + chain_scratch(nt, rows, width),
        compiler_params=pltpu.CompilerParams(
            vmem_limit_bytes=VMEM_LIMIT, collective_id=1, has_side_effects=True
        ),
        cost_estimate=pl.CostEstimate(flops=int(1e9), bytes_accessed=int(130e6), transcendentals=int(4e5)),
        name="mix_scatter",
    )(o, y, zr, sq, gain, watt, wmam, tok, *feed)


class ChainGather:
    def __init__(self, own, slots, send, recv, d, z, nt):
        self.own, self.slots, self.send, self.recv = own, slots, send, recv
        self.d, self.z, self.nt = d, z, nt

    def copy(self, way, dist):
        dev = (self.d, self.z + 1 if way == 0 else self.z - 1)
        slot = self.z - dist if way == 0 else self.z + dist
        src = self.own if dist == 0 else self.slots.at[slot]
        return remote_copy(src, self.slots.at[slot], self.send.at[way, dist], self.recv.at[way, dist], dev)

    def landing(self, way, dist):
        slot = self.z - dist if way == 0 else self.z + dist
        return remote_copy(
            self.slots.at[slot], self.slots.at[slot], self.send.at[way, dist - 1],
            self.recv.at[way, dist - 1], (self.d, self.z),
        )

    def has(self, way, dist):
        return self.z >= dist if way == 0 else self.z + dist < self.nt

    def goes_on(self, way):
        return self.z < self.nt - 1 if way == 0 else self.z > 0

    def start(self):
        for way in range(2):
            pl.when(self.goes_on(way))(self.copy(way, 0).start)

    def hop(self, dist):
        for way in range(2):
            pl.when(self.has(way, dist))(self.landing(way, dist).wait_recv)
            if dist < self.nt - 1:
                pl.when(self.has(way, dist) & self.goes_on(way))(self.copy(way, dist).start)

    def drain(self):
        for way in range(2):
            pl.when(self.goes_on(way))(self.copy(way, 0).wait_send)
            for dist in range(1, self.nt - 1):
                pl.when(self.has(way, dist) & self.goes_on(way))(self.copy(way, dist).wait_send)


def unmix_gather_kernel(nt, feed, *refs):
    (dmix, y, z_in, gain, watt, wmam), refs = refs[:6], refs[6:]
    if feed:
        pieces, refs = refs[0], refs[1:]
        (g_o, do_o, dm_o, dot_o, own_o, sum_o), refs = refs[:6], refs[6:]
        boxes, refs = refs[: 8 * (nt - 1)], refs[8 * (nt - 1) :]
    else:
        (g_o, do_o, dm_o, dot_o), refs = refs[:4], refs[4:]
    (slots, g_send, g_recv, dot_own, dot_land, d_send, d_recv) = refs
    d = lax.axis_index("dp")
    z = lax.axis_index("tensor")
    rows = dmix.shape[0]
    bits = dp_bits(d)
    peers = cube_peers(d)
    greet(([(p, z) for p in peers[1:]] if feed else []) + other_quarters(d, z, nt))
    chain = ChainGather(dmix, slots, g_send, g_recv, d, z, nt)
    chain.start()
    cubes = []
    if feed:
        for k in range(1, nt):
            q = lax.rem(z + k, nt)
            box = boxes[8 * k - 8 : 8 * k]
            cubes.append(
                SquareScatter(lambda i, j, q=q: (i, j, q), pieces, box[:6], box[6], box[7], peers, bits, z)
            )
            cubes[-1].start()

    def work(q, g):
        at = pl.ds(pl.multiple_of(q * rows, rows), rows)
        g_o[at, :] = g
        do_o[at, :] = dot_nt(g, watt[...]).astype(BF16)
        dm = dot_nt(g, wmam[...])
        dm_o[at, :] = dm
        zv = z_in[at, :]
        dots = jnp.sum(dm * gain[...] * (y[at, :] * (zv * sigmoid(zv))), axis=1, keepdims=True)
        turned = [jnp.broadcast_to(dots[c : c + 128], (128, 128)).T[0:8, :] for c in range(0, rows, 128)]
        dot_own[:, at] = jnp.concatenate(turned, axis=1)

    work(z, dmix[...])
    if feed:
        own_o[...] = pieces[:, :, z]
        cubes[0].middle()
    for dist in range(1, nt):
        chain.hop(dist)

        def side(way, carry):
            q = jnp.where(way == 0, z - dist, z + dist)

            @pl.when((q >= 0) & (q < nt))
            def _():
                work(q, slots[q])

            return carry

        lax.fori_loop(0, 2, side, 0)
        if feed:
            if dist < nt - 1:
                cubes[dist].middle()
            cubes[dist - 1].finish(sum_o.at[dist - 1])
    dots = Exchange(dot_own, dot_land, d_send, d_recv, d, z, nt)
    dots.start()
    chain.drain()
    for cube in cubes:
        cube.drain()
    dots.wait()
    dot_o[...] = dots.total()


def unmix_gather(nt, dmix, y, zr, gain, watt, wmam, pieces=None):
    total, inner = y.shape
    rows, width = dmix.shape
    dma = pltpu.SemaphoreType.DMA
    sds = jax.ShapeDtypeStruct
    vmem = pl.BlockSpec(memory_space=pltpu.VMEM)
    feed = [] if pieces is None else [pieces]
    outs = [sds((total, width), BF16), sds((total, 128), BF16), sds((total, inner), F32),
            sds((8, total), F32)]
    scratch = []
    if feed:
        n, lanes = pieces.shape[3:]
        outs += [sds((2, 2, n, lanes), BF16), sds((nt - 1, n, lanes), BF16)]
        for _ in range(nt - 1):
            scratch += square_scratch(n, lanes)
    return pl.pallas_call(
        partial(unmix_gather_kernel, nt, bool(feed)),
        in_specs=[vmem] * (6 + len(feed)),
        out_specs=[vmem] * len(outs),
        out_shape=outs,
        scratch_shapes=scratch + [pltpu.VMEM((nt, rows, width), BF16), dma((2, nt - 1)), dma((2, nt - 1)),
                        pltpu.VMEM((8, total), F32), pltpu.VMEM((nt - 1, 8, total), F32),
                        dma((nt - 1,)), dma((nt - 1,))],
        compiler_params=pltpu.CompilerParams(
            vmem_limit_bytes=VMEM_LIMIT, collective_id=2, has_side_effects=True
        ),
        cost_estimate=pl.CostEstimate(flops=int(1e9), bytes_accessed=int(130e6), transcendentals=int(4e5)),
        name="unmix_gather",
    )(dmix, y, zr, gain, watt, wmam, *feed)


def add_refs(left, right):
    return left.astype(F32) + right.astype(F32)


class SquareScatter:
    def __init__(self, place, held, bufs, send, recv, peers, bits, z):
        (self.r1, self.r2, self.ob, self.tb, self.r3, self.r4) = bufs
        self.place, self.held = place, held
        n = held.shape[-2]
        half = n // 2
        self.lo, self.hi = pl.ds(0, half), pl.ds(half, n - half)
        self.half = half
        _, self.x, self.y = bits
        x, y = self.x, self.y
        _, d_x, d_y = peers
        self.copies = []
        for i in range(2):
            self.copies.append(
                remote_copy(held.at[place(i, 1 - x) + (self.lo,)], self.r1.at[i], send.at[i], recv.at[i],
                            (d_x, z))
            )
        for j in range(2):
            self.copies.append(
                remote_copy(held.at[place(1 - y, j) + (self.hi,)], self.r2.at[j], send.at[2 + j],
                            recv.at[2 + j], (d_y, z))
            )
        self.copies.append(remote_copy(self.ob.at[1 - y], self.r3, send.at[4], recv.at[4], (d_y, z)))
        self.copies.append(remote_copy(self.tb.at[1 - x], self.r4, send.at[5], recv.at[5], (d_x, z)))

    def start(self):
        for copy in self.copies[:4]:
            copy.start()

    def middle(self):
        for i in range(2):
            self.copies[i].wait_recv()
            self.ob[i] = add_refs(self.held[self.place(i, self.x) + (self.lo,)], self.r1[i]).astype(BF16)
        self.copies[4].start()
        for j in range(2):
            self.copies[2 + j].wait_recv()
            self.tb[j] = add_refs(self.held[self.place(self.y, j) + (self.hi,)], self.r2[j]).astype(BF16)
        self.copies[5].start()

    def finish(self, out):
        self.copies[4].wait_recv()
        out[0 : self.half] = add_refs(self.ob[self.y], self.r3[...]).astype(out.dtype)
        self.copies[5].wait_recv()
        out[self.half :] = add_refs(self.tb[self.x], self.r4[...]).astype(out.dtype)

    def drain(self):
        for copy in self.copies:
            copy.wait_send()


def square_scratch(n, lanes):
    dma = pltpu.SemaphoreType.DMA
    half = n // 2
    return [
        pltpu.VMEM((2, half, lanes), BF16),
        pltpu.VMEM((2, n - half, lanes), BF16),
        pltpu.VMEM((2, half, lanes), BF16),
        pltpu.VMEM((2, n - half, lanes), BF16),
        pltpu.VMEM((half, lanes), BF16),
        pltpu.VMEM((n - half, lanes), BF16),
        dma((6,)),
        dma((6,)),
    ]


class CubeScatter:
    def __init__(self, pieces, bufs, peers, bits, z):
        (self.rc, self.held, send, recv) = bufs[:4]
        self.p = pieces
        self.core = bits[0]
        self.first = remote_copy(
            pieces.at[:, 1 - self.core], self.rc, send.at[0], recv.at[0], (peers[0], z)
        )
        self.square = SquareScatter(
            lambda i, j: (2 * i + j,), self.held, bufs[4:10], bufs[10], bufs[11], peers, bits, z
        )

    def start(self):
        self.first.start()

    def middle(self):
        self.first.wait_recv()
        for i in range(4):
            self.held[i] = add_refs(self.p[i, self.core], self.rc[i]).astype(BF16)
        self.square.start()

    def last(self):
        self.square.middle()

    def finish(self, out):
        self.square.finish(out)

    def drain(self):
        self.first.wait_send()
        self.square.drain()


def cube_scratch(n, lanes):
    dma = pltpu.SemaphoreType.DMA
    return [
        pltpu.VMEM((4, n, lanes), BF16),
        pltpu.VMEM((4, n, lanes), BF16),
        dma((1,)),
        dma((1,)),
    ] + square_scratch(n, lanes)


class CubeTotal:
    def __init__(self, held, landed, send, recv, peers, z):
        self.held, self.landed = held, landed
        self.copies = [
            remote_copy(held.at[i], landed.at[i], send.at[i], recv.at[i], (peer, z))
            for i, peer in enumerate(peers)
        ]

    def start(self, i):
        self.copies[i].start()

    def take(self, i):
        self.copies[i].wait_recv()
        self.held[i + 1] = self.held[i] + self.landed[i]

    def drain(self):
        for copy in self.copies:
            copy.wait_send()


def norm_back(dy, tok, gain, dh, out, ggain):
    v = tok[...].astype(F32)
    width = v.shape[1]
    f = lax.rsqrt(jnp.mean(v * v, axis=1, keepdims=True) + epsilon)
    ggain(jnp.sum(dy * v * f, axis=0, keepdims=True))
    gdy = dy * gain[...]
    lean = jnp.sum(gdy * v, axis=1, keepdims=True) * (f * f * f / width)
    out[...] = (dh[...] + (f * gdy - v * lean)).astype(BF16)


SMALL_ALL = 24
SMALL_ROWS = 152


def tail_kernel(
    nt, tok, gain, dh, a1, dmix, o, m, dq, dz, dx, dkv, db, drow, wq, win, stp, wsh,
    gg, gtb, gtx, grows, gheads, feed_own, feed_rest,
    gt_o, mixed_o, fed_o, sh_o, small_o, norm_o,
    da, parts, pieces, shared, ot, mt, bufs, landed, c_send, c_recv, *rest,
):
    cube_a, rest = rest[:12], rest[12:]
    cube_b, rest = rest[:12], rest[12:]
    square_c, rest = rest[:8], rest[8:]
    (sh_sum, sh_land, sh_send, sh_recv) = rest[:4]
    (sm_held, sm_land, sm_send, sm_recv, all_own, all_land, all_send, all_recv) = rest[4:12]
    (ng_held, ng_land, ng_send, ng_recv, ngz_land, ngz_send, ngz_recv) = rest[12:]
    d = lax.axis_index("dp")
    z = lax.axis_index("tensor")
    bits = dp_bits(d)
    peers = cube_peers(d)
    rows = tok.shape[0]
    greet([(p, z) for p in peers] + other_quarters(d, z, nt))
    three = SquareScatter(
        lambda i, j: (i, j), feed_own, square_c[:6], square_c[6], square_c[7], peers, bits, z
    )
    three.start()
    chain = ChainScatter(parts, bufs, landed, c_send, c_recv, d, z, nt)

    def part(q):
        at = pl.ds(pl.multiple_of(q * rows, rows), rows)
        parts[q] = down_rows(at, dq, dz, dx, dkv, db, drow, wq, win, stp, wsh).astype(BF16)

    first = jnp.where(z < nt // 2, nt - 1, 0)
    part(first)
    chain.step(0)

    def others(i, carry):
        part(lax.rem(first + 1 + i, nt))
        return carry

    lax.fori_loop(0, nt - 1, others, 0)
    ot[...] = o[...].T
    mt[...] = m[...].T

    def columns(i, carry):
        at = pl.ds(pl.multiple_of(i * 256, 256), 256)

        def put(k, first, values):
            pieces[i, k, first : first + values.shape[0], :] = values

        def put_shared(k, first, values):
            shared[i, k, :, first : first + values.shape[1]] = values

        weight_columns(a1[:, at], dmix[:, at], dq, dz, dx, dkv, db, ot, mt, put, put_shared)
        return carry

    lax.fori_loop(0, 2, columns, 0)
    chain.step(1)
    lax.fori_loop(2, 4, columns, 0)
    one = CubeScatter(pieces, cube_a, peers, bits, z)
    two = CubeScatter(shared, cube_b, peers, bits, z)
    sums = CubeTotal(sm_held, sm_land, sm_send, sm_recv, peers, z)
    for k in range(8):
        sm_held[0, k : k + 1, :] = gg[:, 128 * k : 128 * k + 128]
    for first_row, ref in ((8, gtb), (SMALL_ALL, gtx), (48, grows)):
        for k in range(ref.shape[1] // 128):
            sm_held[0, first_row + 8 * k : first_row + 8 * k + 8, :] = ref[:, 128 * k : 128 * k + 128]
    sm_held[0, 72:88, :] = gheads[...]
    steps = dot_nn(drow[...].astype(BF16), a1[...])
    for k in range(8):
        sm_held[0, 88 + 8 * k : 96 + 8 * k, :] = steps[:, 128 * k : 128 * k + 128]
    sums.start(0)
    two.start()
    one.start()
    three.middle()
    sums.take(0)
    sums.start(1)
    two.middle()
    one.middle()
    sums.take(1)
    sums.start(2)
    for t in range(2, nt - 1):
        chain.step(t)
    sums.take(2)
    all_own[...] = sm_held[3, 0:SMALL_ALL, :]
    over_all = Exchange(all_own, all_land, all_send, all_recv, d, z, nt)
    over_all.start()
    three.finish(fed_o)
    fed_o[...] += feed_rest[...]
    two.last()
    one.last()
    two.finish(sh_sum)
    per = sh_sum.shape[0] // nt
    copies = []
    for k in range(1, nt):
        q = lax.rem(z + k, nt)
        at = pl.ds(pl.multiple_of(q * per, per), per)
        copies.append(
            remote_copy(sh_sum.at[at], sh_land.at[k - 1], sh_send.at[k - 1], sh_recv.at[k - 1], (d, q))
        )
        copies[-1].start()
    one.finish(mixed_o)
    chain.finish(da)

    def keep(row):
        for k in range(8):
            ng_held[0, k : k + 1, :] = row[:, 128 * k : 128 * k + 128]

    norm_back(da[...], tok, gain, dh, gt_o, keep)
    norms = CubeTotal(ng_held, ng_land, ng_send, ng_recv, peers, z)
    norms.start(0)
    small_o[...] = sm_held[3]
    over_all.wait()
    small_o[0:SMALL_ALL, :] = over_all.total()
    norms.take(0)
    norms.start(1)
    for copy in copies:
        copy.wait()
    total = sh_sum[pl.ds(pl.multiple_of(z * per, per), per), :].astype(F32)
    for k in range(nt - 1):
        total = total + sh_land[k].astype(F32)
    sh_o[...] = total
    norms.take(1)
    norms.start(2)
    norms.take(2)
    last = Exchange(ng_held.at[3], ngz_land, ngz_send, ngz_recv, d, z, nt)
    last.start()
    last.wait()
    norm_o[...] = last.total()
    for thing in (chain, one, two, three, sums, norms):
        thing.drain()


def tail(nt, *args):
    tok, a1, dz = args[0], args[3], args[8]
    feed_own = args[-2]
    rows, width = tok.shape
    total = a1.shape[0]
    inner = dz.shape[1]
    n, lanes = 256 + 3 * inner, 128
    s_rows, s_lanes = 128, args[16].shape[1]
    f_rows = feed_own.shape[2]
    dma = pltpu.SemaphoreType.DMA
    sds = jax.ShapeDtypeStruct
    vmem = pl.BlockSpec(memory_space=pltpu.VMEM)
    return pl.pallas_call(
        partial(tail_kernel, nt),
        in_specs=[vmem] * len(args),
        out_specs=[vmem] * 6,
        out_shape=[sds((rows, width), BF16), sds((n, lanes), F32), sds((f_rows, 128), F32),
                   sds((s_rows // nt, s_lanes), F32), sds((SMALL_ROWS, 128), F32), sds((8, 128), F32)],
        scratch_shapes=[pltpu.VMEM((rows, width), F32), pltpu.VMEM((nt, rows, width), BF16),
                        pltpu.VMEM((4, 2, n, lanes), BF16), pltpu.VMEM((4, 2, s_rows, s_lanes), BF16),
                        pltpu.VMEM((128, total), BF16), pltpu.VMEM((inner, total), BF16)]
        + chain_scratch(nt, rows, width)
        + cube_scratch(n, lanes) + cube_scratch(s_rows, s_lanes) + square_scratch(f_rows, 128)
        + [pltpu.VMEM((s_rows, s_lanes), BF16), pltpu.VMEM((nt - 1, s_rows // nt, s_lanes), BF16),
           dma((nt - 1,)), dma((nt - 1,)),
           pltpu.VMEM((4, SMALL_ROWS, 128), F32), pltpu.VMEM((3, SMALL_ROWS, 128), F32), dma((3,)), dma((3,)),
           pltpu.VMEM((SMALL_ALL, 128), F32), pltpu.VMEM((nt - 1, SMALL_ALL, 128), F32), dma((nt - 1,)),
           dma((nt - 1,)),
           pltpu.VMEM((4, 8, 128), F32), pltpu.VMEM((3, 8, 128), F32), dma((3,)), dma((3,)),
           pltpu.VMEM((nt - 1, 8, 128), F32), dma((nt - 1,)), dma((nt - 1,))],
        compiler_params=pltpu.CompilerParams(
            vmem_limit_bytes=VMEM_LIMIT, collective_id=3, has_side_effects=True
        ),
        cost_estimate=pl.CostEstimate(flops=int(7e9), bytes_accessed=int(150e6), transcendentals=0),
        name="tail",
    )(*args)


def finish_kernel(
    heads, place, mixed, fed, small, norm,
    que_o, att_o, inn_o, mam_o, hid_o, dwn_o, norms_o, taps_o, chan_o, gain_o, step_o, heads_o,
):
    d, p = place[0], place[1]
    block = que_o.shape[0]
    inner = mam_o.shape[0]
    first = 0
    for j in range(que_o.shape[1] // 128):
        que_o[:, 128 * j : 128 * j + 128] = mixed[first : first + block]
        first += block
    att_o[...] = mixed[first : first + att_o.shape[0]]
    first += att_o.shape[0]
    for i in range(2):
        for j in range(inner // 128):
            inn_o[i, :, 128 * j : 128 * j + 128] = mixed[first : first + block]
            first += block
    mam_o[...] = mixed[first : first + inner]
    first = 0
    for i in range(2):
        for j in range(hid_o.shape[2] // 128):
            hid_o[i, :, 128 * j : 128 * j + 128] = fed[first : first + block]
            first += block
    dwn_o[...] = fed[first:]

    def lanes_from(values, lane):
        return pltpu.roll(values, lax.rem(128 - lane, 128), 1)

    width = norms_o.shape[1]
    per = 128 // width
    for i, ref in enumerate((norm, small)):
        row = lanes_from(jnp.broadcast_to(ref[pl.ds(p // per, 1), :], (8, 128)), lax.rem(p, per) * width)
        norms_o[i : i + 1, :] = row[0:1, 0:width]
    width = taps_o.shape[1]
    per = 128 // width
    row = small[pl.ds(pl.multiple_of(8 + 8 * (p // per), 8), 8), :]
    taps_o[...] = lanes_from(row, lax.rem(p, per) * width)[0 : CONV + 1, 0:width]
    width = gain_o.shape[1]
    sums = jnp.zeros((8, 128), F32)
    lane = lanes_of(sums.shape)
    sub = lax.broadcasted_iota(jnp.int32, sums.shape, 0)
    for b in range(heads // 2):
        rows = lanes_from(small[SMALL_ALL + 8 * b : SMALL_ALL + 8 * b + 8, :], d * width)
        raw = small[48 + 8 * b : 56 + 8 * b, :]
        gains = lanes_from(raw, d * width)
        for k in range(2):
            h = 2 * b + k
            at = slice(64 * k, 64 * k + width)
            chan_o[:, h, :] = rows[0 : CONV + 1, at]
            gain_o[h : h + 1, :] = gains[0:1, at]
            skip = jnp.sum(jnp.where(lane // SSM_DIM == k, raw[1:2, :], 0.0), axis=1, keepdims=True)
            sums = jnp.where((sub == h) & (lane == 2), skip, sums)
    for k in range(2):
        total = jnp.sum(small[72 + 8 * k : 80 + 8 * k, :], axis=1, keepdims=True)
        sums = jnp.where(lane == k, total, sums)
    heads_o[...] = sums
    steps = small[pl.ds(pl.multiple_of(88 + 8 * d, 8), 8), :]
    steps = jnp.concatenate([steps, jnp.zeros((120, 128), F32)], axis=0).T
    step_o[...] = steps[:, 0:heads]


def finish(heads, place, mixed, fed, small, norm, shapes):
    vmem = pl.BlockSpec(memory_space=pltpu.VMEM)
    sds = jax.ShapeDtypeStruct
    return pl.pallas_call(
        partial(finish_kernel, heads),
        in_specs=[pl.BlockSpec(memory_space=pltpu.SMEM)] + [vmem] * 4,
        out_specs=[vmem] * (len(shapes) + 1),
        out_shape=[sds(s, F32) for s in shapes] + [sds((8, 128), F32)],
        compiler_params=pltpu.CompilerParams(vmem_limit_bytes=VMEM_LIMIT),
        name="finish",
    )(place, mixed, fed, small, norm)


def rope_wide(length):
    half = HEAD_SIZE // 2
    inverse = rope_base ** (-np.arange(half) * (2.0 / HEAD_SIZE))
    angles = np.arange(length)[:, None] * inverse[None, :]
    c, s = np.cos(angles), np.sin(angles)
    return (
        jnp.asarray(np.concatenate([c, c, c, c], axis=1), F32),
        jnp.asarray(np.concatenate([-s, s, -s, s], axis=1), F32),
    )


def to_blocks(full, axis, nt):
    if axis == 1:
        two, width, cols = full.shape
        return full.reshape(2, 8, width // 8, nt, cols // nt).transpose(1, 3, 0, 2, 4)
    rows, width = full.shape
    return full.reshape(nt, rows // nt, 8, width // 8).transpose(2, 0, 1, 3)


def per_device(
    nd,
    nt,
    tokens,
    query_proj,
    attend_out,
    inner_proj,
    step_proj,
    mamba_out,
    hidden_proj,
    down_proj,
    channel_taps,
    mixer_gain,
    decay_log,
    step_bias,
    skip_weight,
    shared_proj,
    norm_gains,
    shared_taps,
    cotangent,
):
    tensor_index = lax.axis_index("tensor")
    d = lax.axis_index("dp")
    local_rows, width = tokens.shape
    group_rows = local_rows * nt
    heads = step_proj.shape[1]
    inner = heads * SSM_DIM
    channels = inner * nt
    units = down_proj.shape[0]
    small_parts = [channel_taps, mixer_gain, norm_gains, shared_taps, step_proj.T]
    flat = jnp.concatenate([p.reshape(-1) for p in small_parts])
    small_len = -(-flat.shape[0] // 2048) * 2048
    small = jnp.pad(flat, (0, small_len - flat.shape[0])).reshape(-1, 128)
    (tok_full, full_query, full_attend, full_inner, full_mamba, hid_own, down_own, sha, sma) = gather_start(
        tokens, query_proj, attend_out, inner_proj, mamba_out, hidden_proj, down_proj, shared_proj, small,
        nd, nt,
    )
    feed = ()
    if nd == 8:
        hid_in, down_in, tok_full = lax.optimization_barrier((hidden_proj, down_proj, tok_full))
        feed = [hid_own, down_own]
        for k in range(1, nt):
            ring = [(i, (i + k) % nt) for i in range(nt)]
            feed += [lax.ppermute(hid_in, "tensor", ring), lax.ppermute(down_in, "tensor", ring)]
    else:
        full_hidden = lax.all_gather(hidden_proj, "tensor", axis=2, tiled=True)
        full_hidden = to_blocks(lax.all_gather(full_hidden, "dp", axis=1, tiled=True), 1, nt)
        full_down = lax.all_gather(down_proj, "tensor", axis=0, tiled=True)
        full_down = to_blocks(lax.all_gather(full_down, "dp", axis=1, tiled=True), 0, nt)

    full_shared = sha.reshape(width, -1)
    sma = sma.reshape(nd, nt, small_len)

    def small_piece(index):
        start = sum(p.size for p in small_parts[:index])
        part = small_parts[index]
        return sma[:, :, start : start + part.size].reshape((nd, nt) + part.shape)

    taps_x = pick(small_piece(0), tensor_index, 1).transpose(1, 2, 0, 3).reshape(CONV + 1, inner)
    gain_mix = pick(small_piece(1), tensor_index, 1).transpose(1, 0, 2).reshape(1, inner)
    full_norms = small_piece(2).transpose(2, 0, 1, 3).reshape(2, width).astype(F32)
    taps_b = small_piece(3).transpose(2, 0, 1, 3).reshape(CONV + 1, -1)
    step_rows = pick(small_piece(4), tensor_index, 1).transpose(1, 0, 2).reshape(heads, width)
    step_rows = jnp.pad(step_rows, ((0, 8 - heads), (0, 0)))
    taps_x = jnp.pad(taps_x.astype(F32), ((0, 7 - CONV), (0, 0)))
    taps_b = jnp.pad(taps_b.astype(F32), ((0, 7 - CONV), (0, 0)))
    gain_mix = gain_mix.astype(F32)
    gain_first = full_norms[0:1]
    gain_second = full_norms[1:2]

    def head_rows(values):
        return jnp.pad(jnp.broadcast_to(values[:, None], (heads, 128)), ((0, 8 - heads), (0, 0)))

    decay = head_rows(-jnp.exp(decay_log.astype(F32)))
    bias = head_rows(step_bias.astype(F32))
    skip = jnp.repeat(skip_weight.astype(F32), SSM_DIM)[None, :]
    q_heads = query_proj.shape[1] // HEAD_SIZE
    kv_head = (tensor_index * q_heads // (QHEADS // KVHEADS)).astype(jnp.int32).reshape(1)
    cosine, sine = rope_wide(group_rows)

    (a1, q, k2, v2, lse, o, xr, zr, br, y, trow, states, squares) = mixers_forward(
        heads, kv_head, tok_full.reshape(group_rows, width), gain_first, full_query, full_inner, step_rows,
        full_shared, cosine, sine, taps_x, taps_b, decay, bias, skip,
    )
    mixed = mix_scatter(
        channels, nt, o, y, zr, squares, gain_mix, full_attend, full_mamba, tokens, tuple(feed)
    )
    m, squares, hidden = mixed[:3]
    if nd == 8:
        full_hidden, full_down = mixed[3:]
    layer_out, dh, dmix, grad_gain_two, feed_pieces = feed_forward(
        nd == 8, hidden, gain_second, cotangent, full_hidden, full_down
    )
    if nd == 8:
        feed_pieces = feed_pieces.reshape((2, 2) + feed_pieces.shape[1:])
        grad_mix, do, dm, dots, feed_own, feed_sums = unmix_gather(
            nt, dmix, y, zr, gain_mix, full_attend, full_mamba, feed_pieces
        )
    else:
        grad_mix, do, dm, dots = unmix_gather(nt, dmix, y, zr, gain_mix, full_attend, full_mamba)
        hid_full = feed_pieces[:, :, : 2 * units].reshape(8, nt, 2, units // 128, width // 8, 128)
        hid_full = hid_full.transpose(2, 0, 4, 1, 3, 5).reshape(2, nd, width // nd, nt, units)
        hid_sum = cube_scatter(hid_full.transpose(1, 3, 0, 2, 4), nd, BF16)
        down_full = feed_pieces[:, :, 2 * units :].transpose(1, 2, 0, 3)
        down_full = down_full.reshape(nt, units, nd, width // nd)
        down_sum = cube_scatter(down_full.transpose(2, 0, 1, 3), nd, BF16)
        gradient_hidden = chain_scatter(hid_sum, nt)
        gradient_down = chain_scatter(down_sum, nt)

    back = mixers_back(
        heads, channels, nt, kv_head, q, k2, v2, lse, do, cosine, sine, dm, y, zr, xr, br, trow, states,
        squares, dots, gain_mix, taps_x, taps_b, decay, bias, skip, feed_sums if nd == 8 else None,
    )
    dq, dkv, dz, dx, db, drow, grad_tx, grad_tb, grad_rows, grad_heads = back[:10]
    if nd == 8:
        sums = tail(
            nt, tokens, gain_first, dh, a1, grad_mix, o, m, dq, dz, dx, dkv, db, drow, full_query, full_inner,
            step_rows, full_shared, grad_gain_two, grad_tb, grad_tx, grad_rows, grad_heads, feed_own, back[10],
        )
        gradient_tokens, mixed, fed, gradient_shared, small_sums, grad_gain_one = sums
        place = jnp.stack([d, d * nt + tensor_index]).astype(jnp.int32)
        shapes = [
            query_proj.shape, attend_out.shape, inner_proj.shape, mamba_out.shape, hidden_proj.shape,
            down_proj.shape, norm_gains.shape, shared_taps.shape, channel_taps.shape, mixer_gain.shape,
            step_proj.shape,
        ]
        (
            gradient_query,
            gradient_attend,
            gradient_inner,
            gradient_mamba,
            gradient_hidden,
            gradient_down,
            gradient_norms,
            gradient_taps,
            gradient_channel,
            gradient_mixer,
            gradient_step,
            head_sums,
        ) = finish(heads, place, mixed, fed, small_sums, grad_gain_one, shapes)
        return (
            layer_out,
            gradient_tokens,
            gradient_query,
            gradient_attend,
            gradient_inner,
            gradient_step,
            gradient_mamba,
            gradient_hidden,
            gradient_down,
            gradient_channel,
            gradient_mixer,
            head_sums[:heads, 0],
            head_sums[:heads, 1],
            head_sums[:heads, 2],
            gradient_shared,
            gradient_norms,
            gradient_taps,
        )

    part_one = down_parts(dq, dz, dx, dkv, db, drow, full_query, full_inner, step_rows, full_shared)
    pieces, shared_pieces, grad_step = weight_pieces(a1, dq, dz, dx, dkv, db, drow, o, m, grad_mix)
    block = width // nd
    q_cols = query_proj.shape[1]
    cuts = [0, q_cols, q_cols + attend_out.shape[0]]
    cuts += [cuts[2] + inner, cuts[2] + 2 * inner, cuts[2] + 3 * inner]

    def from_rows(values):
        return values.reshape(8, -1, 128, 128).transpose(0, 2, 1, 3).reshape(width, -1)

    def from_lanes(values):
        return values.transpose(1, 0, 2).reshape(-1, width)

    n_tap = CONV + 1
    over_all = jnp.concatenate([grad_gain_two.reshape(-1), grad_tb[:n_tap].reshape(-1)])
    over_dp = jnp.concatenate(
        [
            grad_tx[:n_tap].reshape(-1),
            grad_rows[0],
            grad_rows[1].reshape(heads, SSM_DIM).sum(axis=1),
            grad_heads[:heads].sum(axis=1),
            grad_heads[8 : 8 + heads].sum(axis=1),
            grad_step[:heads].reshape(-1),
        ]
    )

    def in_rows(values):
        return jnp.pad(values, (0, -values.shape[0] % 1024)).reshape(-1, 128)

    rows_all = in_rows(over_all)
    n_all = rows_all.shape[0]
    small_sums = jnp.concatenate([rows_all, in_rows(over_dp)], axis=0)
    parts = part_one.reshape(nt, local_rows, width)
    token_f32 = tokens.astype(F32)
    _, norm_one_back = jax.vjp(norm_apply, token_f32, gain_first[0])
    grad_from_one, grad_gain_one = norm_one_back(chain_scatter(parts, nt))
    gradient_tokens = (dh + grad_from_one).astype(BF16)
    got = [pieces[:, cuts[i] : cuts[i + 1]] for i in range(5)]

    def over_rows(values):
        return cube_scatter(from_rows(values).reshape(nd, block, -1), nd)

    def over_lanes(values):
        return cube_scatter(from_lanes(values).reshape(-1, nd, block).transpose(1, 0, 2), nd)

    gradient_query = over_rows(got[0])
    gradient_attend = over_lanes(got[1])
    gradient_inner = jnp.stack([over_rows(got[2]), over_rows(got[3])])
    gradient_mamba = over_lanes(got[4])
    shared_cut = shared_pieces.reshape(nd, nt, width // (nd * nt), -1)
    gradient_shared = chain_scatter(cube_scatter(shared_cut, nd, BF16), nt)
    small_sums = lax.psum(small_sums, "dp")
    small_sums = jnp.concatenate(
        [lax.psum(small_sums[:n_all], "tensor"), small_sums[n_all:]], axis=0
    )
    grad_gain_one = lax.psum(grad_gain_one, ("dp", "tensor")).reshape(1, width)
    over_all = small_sums[:n_all].reshape(-1)
    over_dp = small_sums[n_all:].reshape(-1)
    place = d * nt + tensor_index
    norm_w = width // (nd * nt)
    both_norms = jnp.concatenate([grad_gain_one, over_all[:width].reshape(1, width)], axis=0)
    gradient_norms = lax.dynamic_slice_in_dim(both_norms, place * norm_w, norm_w, 1)
    tap_w = shared_taps.shape[1]
    tap_all = over_all[width : width + n_tap * taps_b.shape[1]].reshape(n_tap, -1)
    gradient_taps = lax.dynamic_slice_in_dim(tap_all, place * tap_w, tap_w, 1)
    part = mixer_gain.shape[1]
    n_taps = n_tap * inner
    chan = over_dp[:n_taps].reshape(n_tap, heads, SSM_DIM)
    gain = over_dp[n_taps : n_taps + inner].reshape(heads, SSM_DIM)
    gradient_channel = lax.dynamic_slice_in_dim(chan, d * part, part, 2)
    gradient_mixer = lax.dynamic_slice_in_dim(gain, d * part, part, 1)
    rest = over_dp[n_taps + inner :]
    gradient_skip = rest[:heads]
    gradient_decay = rest[heads : 2 * heads]
    gradient_bias = rest[2 * heads : 3 * heads]
    step_all = rest[3 * heads : 3 * heads + heads * width].reshape(heads, width)
    gradient_step = lax.dynamic_slice_in_dim(step_all, d * block, block, 1).T
    return (
        layer_out,
        gradient_tokens,
        gradient_query,
        gradient_attend,
        gradient_inner,
        gradient_step,
        gradient_mamba,
        gradient_hidden,
        gradient_down,
        gradient_channel,
        gradient_mixer,
        gradient_decay,
        gradient_bias,
        gradient_skip,
        gradient_shared,
        gradient_norms,
        gradient_taps,
    )


def solution(mesh):
    placed = (
        P(("dp", "tensor"), None),
        P("dp", "tensor"),
        P("tensor", "dp"),
        P(None, "dp", "tensor"),
        P("dp", "tensor"),
        P("tensor", "dp"),
        P(None, "dp", "tensor"),
        P("tensor", "dp"),
        P(None, "tensor", "dp"),
        P("tensor", "dp"),
        P("tensor"),
        P("tensor"),
        P("tensor"),
        P(("dp", "tensor"), None),
        P(None, ("dp", "tensor")),
        P(None, ("dp", "tensor")),
        P(("dp", "tensor"), None),
    )
    return jax.shard_map(
        partial(per_device, mesh.shape["dp"], mesh.shape["tensor"]),
        mesh=mesh,
        in_specs=placed,
        out_specs=(
            P(("dp", "tensor"), None),
            P(("dp", "tensor"), None),
            P("dp", "tensor"),
            P("tensor", "dp"),
            P(None, "dp", "tensor"),
            P("dp", "tensor"),
            P("tensor", "dp"),
            P(None, "dp", "tensor"),
            P("tensor", "dp"),
            P(None, "tensor", "dp"),
            P("tensor", "dp"),
            P("tensor"),
            P("tensor"),
            P("tensor"),
            P(("dp", "tensor"), None),
            P(None, ("dp", "tensor")),
            P(None, ("dp", "tensor")),
        ),
        check_vma=False,
    )
```

```python
from functools import partial

import numpy as np
import jax
import jax.numpy as jnp
from jax import lax
from jax.experimental import pallas as pl
from jax.experimental.pallas import tpu as pltpu
from jax.sharding import PartitionSpec as P

MESH = pl.DeviceIdType.MESH

QHEADS = 8
KVHEADS = 2
HEAD_SIZE = 64
SSM_DIM = 64
CONV = 4


epsilon = 1e-05
rope_base = 100000000000.0
neg_large = -1e30
block_len = 128


def norm_apply(values, gain):
    factor = lax.rsqrt(jnp.mean(values * values, axis=-1, keepdims=True) + epsilon)
    return values * factor * gain


def dp_bits(index):
    core = lax.rem(index, 2)
    xbit = lax.rem(index // 2, 2)
    ybit = lax.rem(index // 4, 2)
    return core, xbit, ybit


def remote_copy(src, dst, send, recv, dev):
    return pltpu.make_async_remote_copy(
        src_ref=src, dst_ref=dst, send_sem=send, recv_sem=recv, device_id=dev, device_id_type=MESH
    )


def greet(peers):
    barrier = pltpu.get_barrier_semaphore()
    for peer in peers:
        pl.semaphore_signal(barrier, inc=1, device_id=peer, device_id_type=MESH)
    pl.semaphore_wait(barrier, len(peers))


def other_quarters(d, z, nt):
    return [(d, lax.rem(z + k, nt)) for k in range(1, nt)]


def cube_peers(d):
    core, xbit, ybit = dp_bits(d)
    return d + 1 - 2 * core, d + 2 - 4 * xbit, d + 4 - 8 * ybit


class CubeGather:
    def __init__(self, items, via_y, send, recv, d, z):
        self.items, self.via_y, self.send, self.recv = items, via_y, send, recv
        self.d, self.z = d, z
        self.d_core, self.d_x, self.d_y = cube_peers(d)
        self.d_xy = self.d_x + self.d_y - d
        self.sent = []

    def push(self, i, j, src, dst, peer):
        def make():
            return remote_copy(src(), dst(), self.send.at[i, j], self.recv.at[i, j], (peer, self.z))

        make().start()
        self.sent.append(make)

    def landed(self, i, j, slot):
        at = self.items[i][1]
        remote_copy(
            at(slot), at(slot), self.send.at[i, j], self.recv.at[i, j], (self.d_core, self.z)
        ).wait_recv()

    def start(self, i):
        src, at = self.items[i]
        for j, peer in enumerate((self.d_x, self.d_y, self.d_core)):
            self.push(i, j, lambda: src, lambda: at(self.d), peer)

    def near(self, i):
        d_x, d_y, d_core = self.d_x, self.d_y, self.d_core
        self.landed(i, 0, d_x)
        if i in self.via_y:
            self.hand_on(i, 3, d_x, d_y)
        self.hand_on(i, 4, d_x, d_core)
        self.landed(i, 1, d_y)
        if i not in self.via_y:
            self.hand_on(i, 3, d_y, d_x)
        self.hand_on(i, 5, d_y, d_core)

    def hand_on(self, i, j, slot, peer):
        at = self.items[i][1]
        self.push(i, j, lambda: at(slot), lambda: at(slot), peer)

    def far(self, i):
        self.landed(i, 3, self.d_xy)
        self.hand_on(i, 6, self.d_xy, self.d_core)

    def finish(self):
        for i in range(len(self.items)):
            self.landed(i, 2, self.d_core)
            for j in (4, 5, 6):
                self.landed(i, j, self.d_core)
        for make in self.sent:
            make().wait_send()


def gather_kernel(nt, *refs):
    (tok, que, att, inn, mam, sha, sma) = refs[:7]
    (tok_f, que_f, att_f, inn_f, mam_f, sha_f, sma_f) = refs[7:14]
    (lsem, zs_send, zs_recv, t_send, t_recv, d_send, d_recv) = refs[14:]
    d = lax.axis_index("dp")
    z = lax.axis_index("tensor")
    greet([(p, z) for p in cube_peers(d)] + other_quarters(d, z, nt))

    small = []
    for i, (src, dst) in enumerate(((sha, sha_f), (sma, sma_f))):
        for k, peer in enumerate(other_quarters(d, z, nt)):
            small.append(remote_copy(src, dst.at[d, z], zs_send.at[i, k], zs_recv.at[i, k], peer))
            small[-1].start()
    q_rows = que.shape[0]
    cols = att.shape[1]
    i_rows = inn.shape[1]
    items = [
        (inn, lambda s: inn_f.at[:, pl.ds(s * i_rows, i_rows)]),
        (que, lambda s: que_f.at[pl.ds(s * q_rows, q_rows)]),
        (att, lambda s: att_f.at[:, pl.ds(pl.multiple_of(s * cols, cols), cols)]),
        (mam, lambda s: mam_f.at[:, pl.ds(pl.multiple_of(s * cols, cols), cols)]),
        (sha_f.at[d], lambda s: sha_f.at[s]),
        (sma_f.at[d], lambda s: sma_f.at[s]),
    ]
    cube = CubeGather(items, (0, 5), d_send, d_recv, d, z)
    locals_ = []
    for i, (src, dst) in enumerate(
        [(sha, sha_f.at[d, z]), (sma, sma_f.at[d, z]), (tok, tok_f.at[z])]
        + [(src, at(d)) for src, at in items[:4]]
    ):
        copy = pltpu.make_async_copy(src, dst, lsem.at[i])
        copy.start()
        locals_.append(copy)
    for i in range(4):
        cube.start(i)
    chain = ChainGather(tok, tok_f, t_send, t_recv, d, z, nt)
    chain.start()
    locals_[0].wait()
    locals_[1].wait()
    for copy in small:
        copy.wait()
    cube.start(4)
    cube.start(5)
    for i in range(4):
        cube.near(i)
    chain.hop(1)
    for i in (4, 5):
        cube.near(i)
    for i in range(6):
        cube.far(i)
    for dist in range(2, nt):
        chain.hop(dist)
    cube.finish()
    for copy in locals_[2:]:
        copy.wait()
    chain.drain()


def gather_start(tok, que, att, inn, mam, sha, sma, nd, nt):
    if nd != 8:
        shared = lax.all_gather(sha, ("dp", "tensor"), axis=0)
        small = lax.all_gather(sma, ("dp", "tensor"), axis=0)
        return (
            lax.all_gather(tok, "tensor", axis=0),
            lax.all_gather(que, "dp", axis=0, tiled=True),
            lax.all_gather(att, "dp", axis=1, tiled=True),
            lax.all_gather(inn, "dp", axis=1, tiled=True),
            lax.all_gather(mam, "dp", axis=1, tiled=True),
            shared.reshape((nd, nt) + sha.shape),
            small.reshape((nd, nt) + sma.shape),
        )
    bf = jnp.bfloat16
    outs = (
        (nt,) + tok.shape,
        (nd * que.shape[0], que.shape[1]),
        (att.shape[0], nd * att.shape[1]),
        (2, nd * inn.shape[1], inn.shape[2]),
        (mam.shape[0], nd * mam.shape[1]),
        (nd, nt) + sha.shape,
        (nd, nt) + sma.shape,
    )
    anywhere = pl.BlockSpec(memory_space=pl.ANY)
    dma = pltpu.SemaphoreType.DMA
    return pl.pallas_call(
        partial(gather_kernel, nt),
        out_shape=[jax.ShapeDtypeStruct(s, bf) for s in outs],
        in_specs=[pl.BlockSpec(memory_space=pltpu.VMEM)] * 7,
        out_specs=[anywhere] * 7,
        scratch_shapes=[
            dma((7,)), dma((2, nt)), dma((2, nt)), dma((2, nt)), dma((2, nt)),
            dma((6, 7)), dma((6, 7)),
        ],
        compiler_params=pltpu.CompilerParams(collective_id=0, has_side_effects=True),
        name="gather_start",
    )(tok, que, att, inn, mam, sha, sma)


def pack_kernel(taps, gain, norms, staps, step, out, rows):
    heads = step.shape[1]
    f32 = jnp.float32
    rows[...] = jnp.zeros(rows.shape, f32)
    rows[0:2, 0:32] = norms[...].astype(f32)
    rows[0 : CONV + 1, 32:40] = staps[...].astype(f32)
    rows[0:heads, 40:48] = gain[...].astype(f32)
    for j in range(CONV + 1):
        rows[0:heads, 48 + 8 * j : 56 + 8 * j] = taps[j].astype(f32)
    wide = jnp.concatenate([step[...].astype(f32), jnp.zeros((128, 128 - heads), f32)], axis=1)
    rows[8:16, :] = wide.T[0:8, :]
    out[...] = rows[...].astype(jnp.bfloat16)


def pack_small(taps, gain, norms, staps, step):
    vmem = pl.BlockSpec(memory_space=pltpu.VMEM)
    return pl.pallas_call(
        pack_kernel,
        in_specs=[vmem] * 5,
        out_specs=vmem,
        out_shape=jax.ShapeDtypeStruct((16, 128), jnp.bfloat16),
        scratch_shapes=[pltpu.VMEM((16, 128), jnp.float32)],
        name="pack_small",
    )(taps, gain, norms, staps, step)


def unpack_kernel(
    heads, where, scal, packed, first_o, second_o, gain_o, tapx_o, tapb_o, step_o, decay_o, bias_o, skip_o
):
    z = where[0]
    f32 = jnp.float32
    nd, nt = packed.shape[:2]
    tiles = [[packed[k, q].astype(f32) for q in range(nt)] for k in range(nd)]
    for k in range(nd):
        both = jnp.concatenate([tiles[k][q][0:8, 0:32] for q in range(nt)], axis=1)
        first_o[:, 128 * k : 128 * k + 128] = both[0:1]
        second_o[:, 128 * k : 128 * k + 128] = both[1:2]
        step_o[:, 128 * k : 128 * k + 128] = packed[k, z].astype(f32)[8:16, :].astype(jnp.bfloat16)
    half = nd // 2
    for k in range(2):
        tapb_o[:, 128 * k : 128 * k + 128] = jnp.concatenate(
            [tiles[half * k + i][q][0:8, 32:40] for i in range(half) for q in range(nt)], axis=1
        )
    own = [packed[k, z].astype(f32) for k in range(nd)]

    def by_head(lane):
        wide = jnp.concatenate([own[k][0:8, lane : lane + 8] for k in range(nd)], axis=1)
        return jnp.concatenate([wide[h : h + 1, :] for h in range(heads)], axis=1)

    gain_o[...] = by_head(40)
    tapx_o[...] = jnp.zeros(tapx_o.shape, f32)
    tapb_o[CONV + 1 :, :] = jnp.zeros((7 - CONV, tapb_o.shape[1]), f32)
    for j in range(CONV + 1):
        tapx_o[j : j + 1, :] = by_head(48 + 8 * j)
    sub = lax.broadcasted_iota(jnp.int32, (8, 128), 0)
    decay = jnp.zeros((8, 128), f32)
    bias = jnp.zeros((8, 128), f32)
    for h in range(heads):
        decay = jnp.where(sub == h, scal[0, h], decay)
        bias = jnp.where(sub == h, scal[1, h], bias)
        skip_o[:, SSM_DIM * h : SSM_DIM * (h + 1)] = jnp.full((1, SSM_DIM), scal[2, h], f32)
    decay_o[...] = jnp.where(sub < heads, -jnp.exp(decay), 0.0)
    bias_o[...] = bias


def unpack_small(heads, where, scal, packed, width):
    inner = heads * SSM_DIM
    vmem = pl.BlockSpec(memory_space=pltpu.VMEM)
    smem = pl.BlockSpec(memory_space=pltpu.SMEM)
    sds = jax.ShapeDtypeStruct
    f32 = jnp.float32
    shapes = [(1, width), (1, width), (1, inner), (8, inner), (8, 256)]
    return pl.pallas_call(
        partial(unpack_kernel, heads),
        in_specs=[smem, smem, vmem],
        out_specs=[vmem] * 9,
        out_shape=[sds(s, f32) for s in shapes]
        + [sds((8, width), jnp.bfloat16), sds((8, 128), f32), sds((8, 128), f32), sds((1, inner), f32)],
        name="unpack_small",
    )(where, scal, packed)


def pick(values, index, axis=0):
    return lax.dynamic_index_in_dim(values, index, axis, keepdims=False)


def add_low(left, right):
    return (left.astype(jnp.float32) + right.astype(jnp.float32)).astype(jnp.bfloat16)


def chain_scatter(parts, nt):
    z = lax.axis_index("tensor")
    right = left = None
    for t in range(nt - 1):
        to_right = pick(parts, jnp.clip(nt - 1 - t + z, 0, nt - 1))
        to_left = pick(parts, jnp.clip(t - (nt - 1) + z, 0, nt - 1))
        if t > 0:
            to_right = add_low(to_right, right)
            to_left = add_low(to_left, left)
        right = lax.ppermute(to_right, "tensor", [(i, i + 1) for i in range(t + 1)])
        left = lax.ppermute(
            to_left, "tensor", [(nt - 1 - i, nt - 2 - i) for i in range(t + 1)]
        )
    f32 = jnp.float32
    return pick(parts, z).astype(f32) + right.astype(f32) + left.astype(f32)


def cube_scatter(parts, nd, last=jnp.float32):
    return lax.psum_scatter(parts, "dp", scatter_dimension=0, tiled=False).astype(last)


F32, BF16 = jnp.float32, jnp.bfloat16
VMEM_LIMIT = 56 * 1024 * 1024


def dot_nn(a, b):
    return lax.dot_general(a, b, (((1,), (0,)), ((), ())), preferred_element_type=F32)


def dot_nt(a, b):
    return lax.dot_general(a, b, (((1,), (1,)), ((), ())), preferred_element_type=F32)


def dot_tn(a, b):
    return lax.dot_general(a, b, (((0,), (0,)), ((), ())), preferred_element_type=F32)


def sigmoid(v):
    return 1.0 / (1.0 + jnp.exp(-v))


def lanes_of(shape):
    return lax.broadcasted_iota(jnp.int32, shape, len(shape) - 1)


def turn(values, cosine, sine):
    lane = lanes_of(values.shape)
    other = jnp.where(
        lax.rem(lane, HEAD_SIZE) < HEAD_SIZE // 2,
        pltpu.roll(values, 128 - HEAD_SIZE // 2, 1),
        pltpu.roll(values, HEAD_SIZE // 2, 1),
    )
    return values * cosine + other * sine


def softplus(v):
    return jnp.maximum(v, 0.0) + jnp.log1p(jnp.exp(-jnp.abs(v)))


def running_sum(rows):
    lane = lanes_of(rows.shape)
    step = 1
    while step < rows.shape[1]:
        rows = rows + jnp.where(lane >= step, pltpu.roll(rows, step, 1), 0.0)
        step *= 2
    return rows


def running_sum_back(rows):
    lane = lanes_of(rows.shape)
    width = rows.shape[1]
    step = 1
    while step < width:
        rows = rows + jnp.where(lane < width - step, pltpu.roll(rows, width - step, 1), 0.0)
        step *= 2
    return rows


def stack_columns(rows_list):
    used = sum(r.shape[0] for r in rows_list)
    filler = jnp.zeros((128 - used, 128), F32)
    return jnp.concatenate(rows_list + [filler], axis=0).T


def widen(cols, base, heads):
    low = lanes_of((cols.shape[0], 128)) < SSM_DIM
    return jnp.concatenate(
        [
            jnp.where(low, cols[:, base + 2 * p : base + 2 * p + 1],
                      cols[:, base + 2 * p + 1 : base + 2 * p + 2])
            for p in range(heads // 2)
        ],
        axis=1,
    )


def conv_rows(ref, taps, first, rows):
    total = taps[CONV : CONV + 1, :] + taps[0:1, :] * ref[pl.ds(first, rows), :]
    for j in range(1, CONV):
        total = total + taps[j : j + 1, :] * ref[pl.ds(first + j, rows), :]
    return total


class FeedGather:
    def __init__(self, step, nt, hid, dwn, hid_f, dwn_f, hid_z, dwn_z, lsem, sems):
        self.step, self.nt = step, nt
        d = lax.axis_index("dp")
        z = lax.axis_index("tensor")
        self.d, self.z = d, z
        self.cube = CubeGather(
            [(hid, lambda s: hid_f.at[s, z]), (dwn, lambda s: dwn_f.at[s, z])], (0,), sems[0], sems[1], d, z
        )
        self.chains = [
            ChainGather(hid, hid_z, sems[2], sems[3], d, z, nt),
            ChainGather(dwn, dwn_z, sems[4], sems[5], d, z, nt),
        ]
        self.own = lambda: [
            pltpu.make_async_copy(hid, hid_f.at[d, z], lsem.at[0]),
            pltpu.make_async_copy(dwn, dwn_f.at[d, z], lsem.at[1]),
        ]

    def at(self, step, act):
        pl.when(self.step == step)(act)

    def begin(self):
        def act():
            greet([(p, self.z) for p in cube_peers(self.d)] + other_quarters(self.d, self.z, self.nt))
            for chain in self.chains:
                chain.start()
            for i in range(2):
                self.cube.start(i)
            for copy in self.own():
                copy.start()

        self.at(0, act)
        def late():
            for chain in self.chains:
                chain.hop(2)

        self.at(3, late)

    def middle(self):
        def near():
            for chain in self.chains:
                chain.hop(1)
            for i in range(2):
                self.cube.near(i)

        def far():
            for i in range(2):
                self.cube.far(i)

        self.at(1, near)
        self.at(2, far)

    def end(self):
        def act():
            for chain in self.chains:
                chain.hop(3)
            self.cube.finish()
            for copy in self.own():
                copy.wait()
            for chain in self.chains:
                chain.drain()

        self.at(3, act)


def forward_kernel(heads, nt, feed, *refs):
    if feed:
        beside = FeedGather(
            pl.program_id(0), nt, *refs[14:16], *refs[29:33], refs[38], refs[39:45]
        )
        refs = refs[:14] + refs[16:29] + refs[33:38]
        beside.begin()
        forward_step(heads, beside.middle, *refs)
        beside.end()
    else:
        forward_step(heads, lambda: None, *refs)


def forward_step(
    heads, middle, kvh, tok, gain, wq, win, stp, wsh, cosine, sine, tapx, tapb, decay, bias, skip,
    a1_o, q_o, k_o, v_o, lse_o, o_o, x_o, z_o, b_o, y_o, t_o, s_o, sq_o,
    keys, vals, xs, bs, state,
):
    step = pl.program_id(0)
    rows = tok.shape[0]
    second = kvh[0] == 1

    @pl.when(step == 0)
    def _():
        xs[0:8, :] = jnp.zeros((8, xs.shape[1]), F32)
        bs[0:8, :] = jnp.zeros((8, bs.shape[1]), F32)
        state[...] = jnp.zeros(state.shape, F32)

    t = tok[...].astype(F32)
    r = lax.rsqrt(jnp.mean(t * t, axis=1, keepdims=True) + epsilon)
    a1 = (t * r * gain[...]).astype(BF16)
    a1_o[...] = a1
    q = turn(dot_nn(a1, wq[...]), cosine[...], sine[...]).astype(BF16)
    q_o[...] = q
    s = dot_nn(a1, wsh[...])
    low = lanes_of((rows, 128)) < HEAD_SIZE
    k = turn(s[:, :128], cosine[...], sine[...])
    v = s[:, 128:256]
    pick_own = low != second
    k2 = jnp.where(pick_own, k, pltpu.roll(k, 64, 1)).astype(BF16)
    v2 = jnp.where(pick_own, v, pltpu.roll(v, 64, 1))
    k_o[...] = k2
    v_o[...] = v2.astype(BF16)
    place = pl.ds(pl.multiple_of(step * rows, rows), rows)
    keys[place, :] = k2
    vals[:, place] = v2.T.astype(BF16)

    scale = HEAD_SIZE**-0.5

    def attend(blocks):
        n = blocks * rows
        shape = (rows, rows)
        allowed = lax.broadcasted_iota(jnp.int32, shape, 0) <= lanes_of(shape)
        parts = []
        for h in range(2):
            qh = jnp.where(low == (h == 0), q, jnp.zeros_like(q))
            sc = dot_nt(keys[0:n, :], qh) * scale
            last = jnp.where(allowed, sc[n - rows :, :], neg_large)
            sc = jnp.concatenate([sc[: n - rows, :], last], axis=0) if blocks > 1 else last
            top = jnp.max(sc, axis=0, keepdims=True)
            e = jnp.exp(sc - top)
            total = jnp.sum(e, axis=0, keepdims=True)
            lse_o[h : h + 1, :] = top + jnp.log(total)
            parts.append(dot_nn(vals[:, 0:n], e.astype(BF16)) / total)
        sub = lax.broadcasted_iota(jnp.int32, parts[0].shape, 0)
        o_o[...] = jnp.where(sub < HEAD_SIZE, parts[0], parts[1]).T.astype(BF16)

    for i in range(keys.shape[0] // rows):
        pl.when(step == i)(partial(attend, i + 1))

    middle()
    zr = dot_nn(a1, win[0])
    z_o[...] = zr
    xr = dot_nn(a1, win[1])
    x_o[...] = xr
    br = s[:, 256:]
    b_o[...] = br
    xs[8 : 8 + rows, :] = xr
    bs[8 : 8 + rows, :] = br
    u = conv_rows(xs, tapx, 5, rows)
    x = u * sigmoid(u)
    u = conv_rows(bs, tapb, 5, rows)
    bc = (u * sigmoid(u)).astype(BF16)
    xs[0:8, :] = xs[rows : rows + 8, :]
    bs[0:8, :] = bs[rows : rows + 8, :]
    tr = dot_nt(stp[...], a1)
    t_o[...] = tr
    n_state = bc.shape[1] // 2
    tri_shape = (block_len, block_len)
    lower = lax.broadcasted_iota(jnp.int32, tri_shape, 0) >= lanes_of(tri_shape)
    half = lanes_of(tri_shape) < SSM_DIM
    for c in range(rows // block_len):
        part = slice(c * block_len, (c + 1) * block_len)
        dt = softplus(tr[:, part] + bias[...])
        cum = running_sum(dt * decay[...])
        end = cum[:, block_len - 1 :]
        cols = stack_columns([cum, jnp.exp(cum), dt * jnp.exp(end - cum)])
        xc = x[part]
        x_low = xc.astype(BF16)
        b_low = bc[part, :n_state]
        c_low = bc[part, n_state:]
        cross = dot_nt(c_low, b_low)
        grow = widen(cols, 8, heads)
        y = dot_nn(c_low, state[...].astype(BF16)) * grow + skip[...] * xc
        inner = []
        for p in range(heads // 2):
            mats = []
            for h in (2 * p, 2 * p + 1):
                gap = jnp.where(lower, cols[:, h : h + 1] - cum[h : h + 1, :], neg_large)
                mats.append((cross * jnp.exp(gap) * dt[h : h + 1, :]).astype(BF16))
            xp = x_low[:, 128 * p : 128 * p + 128]
            zero = jnp.zeros_like(xp)
            both = jnp.concatenate([jnp.where(half, xp, zero), jnp.where(half, zero, xp)], axis=0)
            inner.append(dot_nn(jnp.concatenate(mats, axis=1), both))
        y = y + jnp.concatenate(inner, axis=1)
        y_o[part, :] = y
        s_o[c] = state[...]
        carried = (xc * widen(cols, 16, heads)).astype(BF16)
        state[...] = grow[block_len - 1 :, :] * state[...] + dot_tn(b_low, carried)
        zc = zr[part]
        w = y * (zc * sigmoid(zc))
        total = jnp.sum(w * w, axis=1, keepdims=True)
        sq_o[:, part] = jnp.broadcast_to(total, (block_len, 128)).T[0:8, :]


def mixers_forward(
    heads, nt, kvh, tok, gain, wq, win, stp, wsh, cosine, sine, tapx, tapb, decay, bias, skip, feed=()
):
    total, width = tok.shape
    rows = 256
    inner = heads * SSM_DIM
    pair = wsh.shape[1] - 256
    state = pair // 2
    chunks = rows // block_len

    def whole(v):
        return pl.BlockSpec(v.shape, lambda i: (0,) * v.ndim)

    def tall(n):
        return pl.BlockSpec((rows, n), lambda i: (i, 0))

    wide = pl.BlockSpec((8, rows), lambda i: (0, i))
    sds = jax.ShapeDtypeStruct
    more_in, more_out, more_shape, more_scratch, extra = [], [], [], [], {}
    if feed:
        nd = 8
        dma = pltpu.SemaphoreType.DMA
        more_in = [whole(v) for v in feed]
        more_out = [pl.BlockSpec(memory_space=pl.ANY)] * 4
        more_shape = [sds((nd, nt) + v.shape, BF16) for v in feed] + [sds((nt,) + v.shape, BF16) for v in feed]
        more_scratch = [dma((2,)), dma((2, 7)), dma((2, 7))] + [dma((2, nt - 1))] * 4
        extra = dict(collective_id=6, has_side_effects=True)
    return pl.pallas_call(
        partial(forward_kernel, heads, nt, bool(feed)),
        grid=(total // rows,),
        in_specs=[pl.BlockSpec(memory_space=pltpu.SMEM), tall(width), whole(gain), whole(wq), whole(win),
                  whole(stp), whole(wsh), tall(128), tall(128), whole(tapx), whole(tapb),
                  whole(decay), whole(bias), whole(skip)] + more_in,
        out_specs=[tall(width), tall(128), tall(128), tall(128), wide, tall(128), tall(inner),
                   tall(inner), tall(pair), tall(inner), wide,
                   pl.BlockSpec((chunks, state, inner), lambda i: (i, 0, 0)), wide] + more_out,
        out_shape=[sds((total, width), BF16), sds((total, 128), BF16), sds((total, 128), BF16),
                   sds((total, 128), BF16), sds((8, total), F32), sds((total, 128), BF16),
                   sds((total, inner), F32), sds((total, inner), F32), sds((total, pair), F32),
                   sds((total, inner), F32), sds((8, total), F32),
                   sds((total // block_len, state, inner), F32), sds((8, total), F32)] + more_shape,
        scratch_shapes=[pltpu.VMEM((total, 128), BF16), pltpu.VMEM((128, total), BF16),
                        pltpu.VMEM((rows + 8, inner), F32), pltpu.VMEM((rows + 8, pair), F32),
                        pltpu.VMEM((state, inner), F32)] + more_scratch,
        compiler_params=pltpu.CompilerParams(vmem_limit_bytes=VMEM_LIMIT, **extra),
        cost_estimate=pl.CostEstimate(flops=int(5e9), bytes_accessed=int(15e6), transcendentals=int(4e6)),
        name="mixers_forward",
    )(kvh, tok, gain, wq, win, stp, wsh, cosine, sine, tapx, tapb, decay, bias, skip, *feed)


def attend_back(step, kvh, q, k2, v2, lse, do, cosine, sine, cos_all, sin_all, dq_o, dkv_o, dk, dv):
    rows = q.shape[0]
    steps = k2.shape[0] // rows
    scale = HEAD_SIZE**-0.5
    low = lanes_of((rows, 128)) < HEAD_SIZE

    @pl.when(step == 0)
    def _():
        dk[...] = jnp.zeros(dk.shape, F32)
        dv[...] = jnp.zeros(dv.shape, F32)

    def back(blocks):
        n = blocks * rows
        shape = (rows, rows)
        allowed = lax.broadcasted_iota(jnp.int32, shape, 0) <= lanes_of(shape)
        qs, dos, ps, dss, dqs = [], [], [], [], []
        for h in range(2):
            mine = low == (h == 0)
            qh = jnp.where(mine, q[...], jnp.zeros_like(q[...]))
            doh = jnp.where(mine, do[...], jnp.zeros_like(do[...]))
            sc = dot_nt(k2[0:n, :], qh) * scale - lse[h : h + 1, :]
            last = jnp.where(allowed, sc[n - rows :, :], neg_large)
            sc = jnp.concatenate([sc[: n - rows, :], last], axis=0) if blocks > 1 else last
            p = jnp.exp(sc)
            dp = dot_nt(v2[0:n, :], doh)
            centre = jnp.sum(p * dp, axis=0, keepdims=True)
            ds = (p * (dp - centre)).astype(BF16)
            qs.append(qh)
            dos.append(doh)
            ps.append(p.astype(BF16))
            dss.append(ds)
            dqs.append(dot_tn(ds, k2[0:n, :]) * scale)
        dk[0:n, :] += dot_nn(jnp.concatenate(dss, axis=1), jnp.concatenate(qs, axis=0)) * scale
        dv[0:n, :] += dot_nn(jnp.concatenate(ps, axis=1), jnp.concatenate(dos, axis=0))
        dq_o[...] = turn(jnp.where(low, dqs[0], dqs[1]), cosine[...], -sine[...]).astype(BF16)

    for i in range(steps):
        pl.when(step == 2 * i)(partial(back, i + 1))

    @pl.when(step == 2 * steps - 1)
    def _():
        own = (lanes_of(dk.shape) < HEAD_SIZE) != (kvh[0] == 1)
        g = dk[...]
        g = turn(g + pltpu.roll(g, 64, 1), cos_all[...], -sin_all[...])
        dkv_o[:, 0:128] = jnp.where(own, g, 0.0).astype(BF16)
        g = dv[...]
        g = g + pltpu.roll(g, 64, 1)
        dkv_o[:, 128:256] = jnp.where(own, g, 0.0).astype(BF16)


def back_kernel(heads, channels, nt, feed, *refs):
    step = pl.program_id(0)
    if feed:
        d = lax.axis_index("dp")
        z = lax.axis_index("tensor")
        feed_in, feed_o, came, f_send, f_recv = refs[0], refs[38], refs[46], refs[47], refs[48]
        copies = [
            remote_copy(feed_in.at[k], came.at[k], f_send.at[k], f_recv.at[k], peer)
            for k, peer in enumerate(other_quarters(d, z, nt))
        ]

        @pl.when(step == 0)
        def _():
            greet(other_quarters(d, z, nt))
            for copy in copies:
                copy.start()

        refs = refs[1:38] + refs[39:46]
    attend_back(step, *refs[:10], *refs[27:29], *refs[37:39])
    scan_back(heads, channels, step, *refs[10:27], *refs[29:37], *refs[39:44])
    if feed:

        @pl.when(step == pl.num_programs(0) - 1)
        def _():
            total = None
            for k, copy in enumerate(copies):
                copy.wait()
                value = came[k].astype(F32)
                total = value if total is None else total + value
            feed_o[...] = total


def scan_back(
    heads, channels, step, dm, y, zr, xr, xp, br, bp, trow, states, rsum, dots, gain, tapx, tapb, decay,
    bias, skip,
    dz_o, dx_o, db_o, dt_o, gx_o, gb_o, gm_o, gh_o,
    xs, bs, dxs, dbs, dstate,
):
    last_step = pl.num_programs(0) - 1
    first = step == last_step
    rows = block_len
    inner = heads * SSM_DIM
    n_state = br.shape[1] // 2

    @pl.when(step == 0)
    def _():
        dxs[rows : rows + 8, :] = jnp.zeros((8, inner), F32)
        dbs[rows : rows + 8, :] = jnp.zeros((8, 2 * n_state), F32)
        dstate[...] = jnp.zeros(dstate.shape, F32)
        gx_o[...] = jnp.zeros(gx_o.shape, F32)
        gb_o[...] = jnp.zeros(gb_o.shape, F32)
        gm_o[...] = jnp.zeros(gm_o.shape, F32)
        gh_o[...] = jnp.zeros(gh_o.shape, F32)

    xs[0:8, :] = jnp.where(first, 0.0, xp[...])
    bs[0:8, :] = jnp.where(first, 0.0, bp[...])
    xs[8 : 8 + rows, :] = xr[...]
    bs[8 : 8 + rows, :] = br[...]
    ux = conv_rows(xs, tapx, 5, rows)
    sx = sigmoid(ux)
    x = ux * sx
    ub = conv_rows(bs, tapb, 5, rows)
    sb = sigmoid(ub)
    bc = (ub * sb).astype(BF16)
    b_low, c_low = bc[:, :n_state], bc[:, n_state:]

    pre = trow[...] + bias[...]
    dt = softplus(pre)
    cum = running_sum(dt * decay[...])
    end = cum[:, rows - 1 :]
    fade = jnp.exp(end - cum)
    inv = lax.rsqrt(rsum[...] / channels + epsilon)
    cols = stack_columns(
        [cum, jnp.exp(cum), dt * fade, dt, inv, inv * inv * inv * dots[...] / channels]
    )
    r = cols[:, 32:33]
    kk = cols[:, 40:41]
    z = zr[...]
    sz = sigmoid(z)
    silu_z = z * sz
    yv = y[...]
    w = yv * silu_z
    dmv = dm[...]
    dw = r * gain[...] * dmv - w * kk
    gm_o[0:1, :] += jnp.sum(dmv * w * r, axis=0, keepdims=True)
    dy = dw * silu_z
    dz_o[...] = (dw * yv * sz * (1.0 + z * (1.0 - sz))).astype(BF16)
    gm_o[1:2, :] += jnp.sum(dy * x, axis=0, keepdims=True)

    grow = widen(cols, 8, heads)
    tail = widen(cols, 16, heads)
    dt_wide = widen(cols, 24, heads)
    x_low = x.astype(BF16)
    dy_low = dy.astype(BF16)
    state = states[0]
    state_low = state.astype(BF16)
    ds = dstate[...]
    ds_low = ds.astype(BF16)
    cross = dot_nt(b_low, c_low)
    shape = (rows, rows)
    upper = lax.broadcasted_iota(jnp.int32, shape, 0) <= lanes_of(shape)
    half = lanes_of(shape) < SSM_DIM
    lane = lanes_of(shape)
    dcross = jnp.zeros(shape, F32)
    col_sums = jnp.zeros(shape, F32)
    row_sums = []
    mids = []
    for p in range(heads // 2):
        span = slice(128 * p, 128 * p + 128)
        xpair, dypair = x_low[:, span], dy_low[:, span]
        zero = jnp.zeros_like(xpair)
        dys = (jnp.where(half, dypair, zero), jnp.where(half, zero, dypair))
        mats = []
        for k in range(2):
            h = 2 * p + k
            gap = jnp.where(upper, cum[h : h + 1, :] - cols[:, h : h + 1], neg_large)
            faded = jnp.exp(gap)
            mats.append((cross * faded).astype(BF16))
            t = dot_nt(xpair, dys[k]) * faded
            dt_col = cols[:, 24 + h : 25 + h]
            td = t * dt_col
            dcross = dcross + td
            row_sums.append(jnp.sum(td * cross, axis=0, keepdims=True))
            col = jnp.sum(t * cross, axis=1, keepdims=True)
            col_sums = jnp.where(lane == h, col, col_sums)
        mids.append(dot_nn(jnp.concatenate(mats, axis=1), jnp.concatenate(dys, axis=0)))
    mid = jnp.concatenate(mids, axis=1)
    row_sums = jnp.concatenate(row_sums + [jnp.zeros((8 - heads, rows), F32)], axis=0)
    col_sums = col_sums.T[0:8, :]

    dye = dy * grow
    dye_low = dye.astype(BF16)
    xd = x * tail
    xd_low = xd.astype(BF16)
    from_b = dot_nn(b_low, ds_low)
    through = dot_nn(c_low, state_low)
    dcross_low = dcross.astype(BF16)
    db = dot_nn(dcross_low, c_low) + dot_nt(xd_low, ds_low)
    dc = dot_tn(dcross_low, b_low) + dot_nt(dye_low, state_low)

    head_of = lax.broadcasted_iota(jnp.int32, (8, inner), 0)
    chan = lanes_of((8, inner)) // SSM_DIM
    ones = jnp.where(head_of == chan, 1.0, 0.0).astype(BF16)

    def by_head(v):
        high = v.astype(BF16)
        rest = (v - high.astype(F32)).astype(BF16)
        return dot_nt(ones, high) + dot_nt(ones, rest)

    grown = by_head(dye * through)
    ended = by_head(x * from_b)
    kept = jnp.sum(ds * state, axis=0, keepdims=True) * grow[rows - 1 :, :]
    kept = jnp.where(head_of == chan, kept, 0.0).sum(axis=1, keepdims=True)
    pulled = dt * fade * ended
    lane8 = lanes_of((8, rows))
    at_end = kept + jnp.sum(pulled, axis=1, keepdims=True)
    dcum = row_sums - dt * col_sums + grown - pulled + jnp.where(lane8 == rows - 1, at_end, 0.0)
    da = running_sum_back(dcum)
    ddt = col_sums + fade * ended + decay[...] * da
    dpre = ddt * sigmoid(pre)
    dt_o[...] = dpre
    gh_o[0:8, :] += da * dt * decay[...]
    gh_o[8:16, :] += dpre

    dstate[...] = grow[rows - 1 :, :] * ds + dot_tn(c_low, dye_low)
    dx = skip[...] * dy + dt_wide * mid + tail * from_b
    dux = dx * sx * (1.0 + ux * (1.0 - sx))
    dub = jnp.concatenate([db, dc], axis=1) * sb * (1.0 + ub * (1.0 - sb))
    for taps, src, d, buf, acc, out in (
        (tapx, xs, dux, dxs, gx_o, dx_o),
        (tapb, bs, dub, dbs, gb_o, db_o),
    ):
        buf[0:rows, :] = d
        total = taps[CONV - 1 : CONV, :] * d
        for j in range(CONV - 1):
            total = total + taps[j : j + 1, :] * buf[pl.ds(CONV - 1 - j, rows), :]
        out[...] = total.astype(BF16)
        for j in range(CONV):
            acc[j : j + 1, :] += jnp.sum(d * src[pl.ds(5 + j, rows), :], axis=0, keepdims=True)
        acc[CONV : CONV + 1, :] += jnp.sum(d, axis=0, keepdims=True)
        buf[rows : rows + 8, :] = d[0:8, :]


def mixers_back(
    heads, channels, nt, kvh, q, k2, v2, lse, do, cosine, sine, dm, y, zr, xr, br, trow, states, rsum, dots,
    gain, tapx, tapb, decay, bias, skip, feed=None,
):
    total, inner = y.shape
    pair = br.shape[1]
    rows = block_len
    steps = total // rows
    per = rows // 8
    q_rows = 2 * rows

    def whole(v):
        return pl.BlockSpec(v.shape, lambda i: (0,) * v.ndim)

    def tall(n):
        return pl.BlockSpec((rows, n), lambda i: (steps - 1 - i, 0))

    def before(n):
        return pl.BlockSpec((8, n), lambda i: (jnp.maximum((steps - 1 - i) * per - 1, 0), 0))

    wide = pl.BlockSpec((8, rows), lambda i: (0, steps - 1 - i))
    ask = pl.BlockSpec((q_rows, 128), lambda i: (i // 2, 0))
    sds = jax.ShapeDtypeStruct

    def fixed(*shape):
        return pl.BlockSpec(shape, lambda i: (0,) * len(shape))

    in_specs = [pl.BlockSpec(memory_space=pltpu.SMEM), ask, whole(k2), whole(v2),
                pl.BlockSpec((8, q_rows), lambda i: (0, i // 2)), ask, ask, ask, whole(cosine), whole(sine),
                tall(inner), tall(inner), tall(inner), tall(inner), before(inner), tall(pair),
                before(pair), wide, pl.BlockSpec((1, pair // 2, inner), lambda i: (steps - 1 - i, 0, 0)),
                wide, wide, whole(gain), whole(tapx), whole(tapb), whole(decay), whole(bias), whole(skip)]
    out_specs = [ask, fixed(total, 256), tall(inner), tall(inner), tall(pair), wide, fixed(8, inner),
                 fixed(8, pair), fixed(8, inner), fixed(16, rows)]
    out_shape = [sds((total, 128), BF16), sds((total, 256), BF16), sds((total, inner), BF16),
                 sds((total, inner), BF16), sds((total, pair), BF16), sds((8, total), F32),
                 sds((8, inner), F32), sds((8, pair), F32), sds((8, inner), F32), sds((16, rows), F32)]
    scratch = [pltpu.VMEM((total, 128), F32), pltpu.VMEM((total, 128), F32),
               pltpu.VMEM((rows + 8, inner), F32), pltpu.VMEM((rows + 8, pair), F32),
               pltpu.VMEM((rows + 8, inner), F32), pltpu.VMEM((rows + 8, pair), F32),
               pltpu.VMEM((pair // 2, inner), F32)]
    args = [kvh, q, k2, v2, lse, do, cosine, sine, cosine, sine, dm, y, zr, xr, xr, br, br, trow, states,
            rsum, dots, gain, tapx, tapb, decay, bias, skip]
    extra = {}
    if feed is not None:
        dma = pltpu.SemaphoreType.DMA
        args = [feed] + args
        in_specs = [whole(feed)] + in_specs
        out_specs = out_specs + [fixed(*feed.shape[1:])]
        out_shape = out_shape + [sds(feed.shape[1:], F32)]
        scratch = scratch + [pltpu.VMEM(feed.shape, BF16), dma((nt - 1,)), dma((nt - 1,))]
        extra = dict(collective_id=5, has_side_effects=True)
    return pl.pallas_call(
        partial(back_kernel, heads, channels, nt, feed is not None),
        grid=(steps,),
        in_specs=in_specs,
        out_specs=out_specs,
        out_shape=out_shape,
        scratch_shapes=scratch,
        compiler_params=pltpu.CompilerParams(vmem_limit_bytes=VMEM_LIMIT, **extra),
        cost_estimate=pl.CostEstimate(flops=int(6e9), bytes_accessed=int(18e6), transcendentals=int(7e6)),
        name="mixers_back",
    )(*args)


def whole_spec(v):
    return pl.BlockSpec(v.shape, lambda i: (0,) * v.ndim)


def feed_open(hid, gain, a2, a2t, acc, dacc):
    v = hid[...]
    f = lax.rsqrt(jnp.mean(v * v, axis=1, keepdims=True) + epsilon)
    low = (v * f * gain[...]).astype(BF16)
    a2[...] = low
    a2t[...] = low.T
    acc[...] = jnp.zeros(acc.shape, F32)
    dacc[...] = jnp.zeros(dacc.shape, F32)


def feed_tile(a2, cot, whid, wdown, acc, dacc):
    width = a2.shape[1]
    units = whid.shape[4]
    w_gate = whid[:, 0, 0].reshape(width, units)
    w_up = whid[:, 0, 1].reshape(width, units)
    w_down = jnp.concatenate([wdown[k, 0] for k in range(width // 128)], axis=1)
    g = dot_nn(a2[...], w_gate)
    u = dot_nn(a2[...], w_up)
    s = sigmoid(g)
    f_low = (g * s * u).astype(BF16)
    acc[...] += dot_nn(f_low, w_down)
    df = dot_nt(cot[...], w_down)
    du = (df * g * s).astype(BF16)
    dg = (df * u * s * (1.0 + g * (1.0 - s))).astype(BF16)
    dacc[...] += dot_nt(dg, w_gate) + dot_nt(du, w_up)
    return f_low, dg, du


def feed_close(hid, gain, cot, acc, dacc, out_o, dh_o, gg_o):
    v = hid[...]
    out_o[...] = (v + acc[...]).astype(BF16)
    f = lax.rsqrt(jnp.mean(v * v, axis=1, keepdims=True) + epsilon)
    dy = dacc[...]
    gg_o[...] = jnp.sum(dy * v * f, axis=0, keepdims=True)
    gdy = dy * gain[...]
    lean = jnp.sum(gdy * v, axis=1, keepdims=True) * (f * f * f / v.shape[1])
    dh = cot[...].astype(F32) + (f * gdy - v * lean)
    dh_o[...] = dh
    return dh.astype(BF16)


def feed_grads(a2t, cot, f_low, dg, du):
    blocks = a2t.shape[0] // 128
    values = []
    for grad in (dg, du):
        full = dot_nn(a2t[...], grad).astype(BF16)
        for cb in range(grad.shape[1] // 128):
            values.append(full[:, 128 * cb : 128 * cb + 128].reshape(blocks, 128, 128))
    full = dot_tn(f_low, cot[...]).astype(BF16)
    values.append(jnp.stack([full[:, 128 * k : 128 * k + 128] for k in range(blocks)]))
    return values


def piece_rows(part, units, quarter_units):
    rows = [
        (k * quarter_units + part * units + cb * 128, 128) for k in range(2) for cb in range(units // 128)
    ]
    return rows + [(2 * quarter_units + part * units, units)]


def feed_kernel(hid, gain, cot, whid, wdown, out_o, dh_o, dmix_o, gg_o, piece_o, a2, a2t, acc, dacc):
    step = pl.program_id(0)
    pl.when(step == 0)(lambda: feed_open(hid, gain, a2, a2t, acc, dacc))
    values = feed_grads(a2t, cot, *feed_tile(a2, cot, whid, wdown, acc, dacc))
    units = whid.shape[4]
    quarter_units = piece_o.shape[2] // 3
    tiles_per = quarter_units // units
    rows = piece_rows(lax.rem(step, tiles_per), units, quarter_units)
    for value, (row, n) in zip(values, rows):
        piece_o[:, step // tiles_per, pl.ds(pl.multiple_of(row, 128), n), :] = value

    @pl.when(step == pl.num_programs(0) - 1)
    def _():
        dmix_o[...] = feed_close(hid, gain, cot, acc, dacc, out_o, dh_o, gg_o)


def feed_forward(hid, gain, cot, whid, wdown):
    rows, width = hid.shape
    blocks, nt, _, depth, units = whid.shape
    tile = 256
    per = units // tile
    hid_spec = pl.BlockSpec((blocks, 1, 2, depth, tile), lambda i: (0, i // per, 0, 0, lax.rem(i, per)))
    down_spec = pl.BlockSpec((blocks, 1, tile, 128), lambda i: (0, i // per, lax.rem(i, per), 0))
    sds = jax.ShapeDtypeStruct
    piece = (blocks, nt, 3 * units, 128)

    def fixed(*shape):
        return pl.BlockSpec(shape, lambda i: (0,) * len(shape))

    return pl.pallas_call(
        feed_kernel,
        grid=(nt * per,),
        in_specs=[fixed(rows, width), fixed(1, width), fixed(rows, width), hid_spec, down_spec],
        out_specs=[fixed(rows, width), fixed(rows, width), fixed(rows, width), fixed(1, width),
                   fixed(*piece)],
        out_shape=[sds((rows, width), BF16), sds((rows, width), F32), sds((rows, width), BF16),
                   sds((1, width), F32), sds(piece, BF16)],
        scratch_shapes=[pltpu.VMEM((rows, width), BF16), pltpu.VMEM((width, rows), BF16),
                        pltpu.VMEM((rows, width), F32), pltpu.VMEM((rows, width), F32)],
        compiler_params=pltpu.CompilerParams(vmem_limit_bytes=VMEM_LIMIT),
        name="feed_forward",
    )(hid, gain, cot, whid, wdown)


def row_columns(rows_list, rows):
    return jnp.concatenate(
        [stack_columns([r[:, c : c + 128] for r in rows_list]) for c in range(0, rows, 128)], axis=0
    )


def down_rows(at, dq, dz, dx, dkv, db, drow, wq, win, stp, wsh):
    total = dot_nt(dq[at, :], wq[...]) + dot_nt(dz[at, :], win[0]) + dot_nt(dx[at, :], win[1])
    total = total + dot_nt(dkv[at, :], wsh[:, 0:256]) + dot_nt(db[at, :], wsh[:, 256:])
    return total + dot_tn(drow[:, at].astype(BF16), stp[...])


def down_kernel(dq, dz, dx, dkv, db, drow, wq, win, stp, wsh, part_o):
    every = slice(None)
    part_o[...] = down_rows(every, dq, dz, dx, dkv, db, drow, wq, win, stp, wsh).astype(BF16)


def down_parts(dq, dz, dx, dkv, db, drow, wq, win, stp, wsh):
    total, inner = dz.shape
    width = wq.shape[0]
    rows = 256

    def tall(v):
        return pl.BlockSpec((rows, v.shape[1]), lambda i: (i, 0))

    wide = pl.BlockSpec((8, rows), lambda i: (0, i))
    return pl.pallas_call(
        down_kernel,
        grid=(total // rows,),
        in_specs=[tall(dq), tall(dz), tall(dx), tall(dkv), tall(db), wide, whole_spec(wq), whole_spec(win),
                  whole_spec(stp), whole_spec(wsh)],
        out_specs=pl.BlockSpec((rows, width), lambda i: (i, 0)),
        out_shape=jax.ShapeDtypeStruct((total, width), BF16),
        compiler_params=pltpu.CompilerParams(vmem_limit_bytes=VMEM_LIMIT),
        cost_estimate=pl.CostEstimate(flops=int(3e9), bytes_accessed=int(8e6), transcendentals=0),
        name="down_parts",
    )(dq, dz, dx, dkv, db, drow, wq, win, stp, wsh)


def weight_columns(a, g, dq, dz, dx, dkv, db, ot, mt, put, put_shared):
    at = a.T
    inner = dz.shape[1]

    def by_rows(values, first):
        for j in range(values.shape[1] // 128):
            for k in range(2):
                put(k, first + 128 * j, values[128 * k : 128 * (k + 1), 128 * j : 128 * (j + 1)])

    def by_lanes(values, first):
        for k in range(2):
            put(k, first, values[:, 128 * k : 128 * (k + 1)])

    by_rows(dot_nn(at, dq[...]).astype(BF16), 0)
    by_lanes(dot_nn(ot[...], g).astype(BF16), 128)
    by_rows(dot_nn(at, dz[...]).astype(BF16), 256)
    by_rows(dot_nn(at, dx[...]).astype(BF16), 256 + inner)
    by_lanes(dot_nn(mt[...], g).astype(BF16), 256 + 2 * inner)
    for first, values in ((0, dot_nn(at, dkv[...]).astype(BF16)), (256, dot_nn(at, db[...]).astype(BF16))):
        for k in range(2):
            put_shared(k, first, values[128 * k : 128 * (k + 1)])


def weight_kernel(a1, dq, dz, dx, dkv, db, drow, o, m, dmix, piece_o, shared_o, step_o, ot, mt):
    @pl.when(pl.program_id(0) == 0)
    def _():
        ot[...] = o[...].T
        mt[...] = m[...].T

    step_o[...] = dot_nn(drow[...].astype(BF16), a1[...])

    def put(k, first, values):
        piece_o[k, first : first + values.shape[0], :] = values

    def put_shared(k, first, values):
        shared_o[k, :, first : first + values.shape[1]] = values

    weight_columns(a1[...], dmix[...], dq, dz, dx, dkv, db, ot, mt, put, put_shared)


def weight_pieces(a1, dq, dz, dx, dkv, db, drow, o, m, dmix):
    total, width = a1.shape
    inner = dz.shape[1]
    n = 256 + 3 * inner
    shared = 256 + db.shape[1]
    cols = pl.BlockSpec((total, 256), lambda i: (0, i))
    sds = jax.ShapeDtypeStruct
    args = (dq, dz, dx, dkv, db, drow, o, m)
    return pl.pallas_call(
        weight_kernel,
        grid=(width // 256,),
        in_specs=[cols] + [whole_spec(v) for v in args] + [cols],
        out_specs=[pl.BlockSpec((2, n, 128), lambda i: (i, 0, 0)),
                   pl.BlockSpec((2, 128, shared), lambda i: (i, 0, 0)),
                   pl.BlockSpec((8, 256), lambda i: (0, i))],
        out_shape=[sds((width // 128, n, 128), BF16), sds((width // 128, 128, shared), BF16),
                   sds((8, width), F32)],
        scratch_shapes=[pltpu.VMEM((128, total), BF16), pltpu.VMEM((inner, total), BF16)],
        compiler_params=pltpu.CompilerParams(vmem_limit_bytes=VMEM_LIMIT),
        cost_estimate=pl.CostEstimate(flops=int(4e9), bytes_accessed=int(12e6), transcendentals=0),
        name="weight_pieces",
    )(a1, *args, dmix)


class Exchange:
    def __init__(self, own, landed, send, recv, d, z, nt):
        self.own, self.landed, self.z, self.nt = own, landed, z, nt
        self.copies = [
            remote_copy(own, landed.at[k - 1], send.at[k - 1], recv.at[k - 1], peer)
            for k, peer in enumerate(other_quarters(d, z, nt), 1)
        ]

    def start(self):
        for copy in self.copies:
            copy.start()

    def wait(self):
        for copy in self.copies:
            copy.wait()

    def total(self):
        total = None
        for q in range(self.nt):
            value = jnp.where(self.z == q, self.own[...].astype(F32), 0.0)
            for k in range(1, self.nt):
                value = value + jnp.where(
                    lax.rem(self.z - k + self.nt, self.nt) == q, self.landed[k - 1].astype(F32), 0.0
                )
            total = value if total is None else total + value
        return total


class ChainScatter:
    def __init__(self, parts, bufs, landed, send, recv, d, z, nt):
        self.parts, self.bufs, self.landed = parts, bufs, landed
        self.send, self.recv = send, recv
        self.d, self.z, self.nt = d, z, nt

    def active(self, way, t):
        z, nt = self.z, self.nt
        if way == 0:
            return (z <= t) & (z < nt - 1)
        return (nt - 1 - z <= t) & (z > 0)

    def copy(self, way, t):
        dev = (self.d, self.z + 1 if way == 0 else self.z - 1)
        return remote_copy(
            self.bufs.at[way, t], self.landed.at[way, t], self.send.at[way, t], self.recv.at[way, t], dev
        )

    def arrives(self, way, t):
        z, nt = self.z, self.nt
        if way == 0:
            return (z >= 1) & (z - 1 <= t)
        return (z < nt - 1) & (nt - 2 - z <= t)

    def step(self, t):
        z, nt = self.z, self.nt
        for way in range(2):
            q = nt - 1 - t + z if way == 0 else t - (nt - 1) + z

            def run():
                value = self.parts[q]
                if t > 0:
                    came = self.arrives(way, t - 1)

                    @pl.when(came)
                    def _():
                        self.copy(way, t - 1).wait_recv()
                        total = value.astype(F32) + self.landed[way, t - 1].astype(F32)
                        self.bufs[way, t] = total.astype(BF16)

                    @pl.when(jnp.logical_not(came))
                    def _():
                        self.bufs[way, t] = value
                else:
                    self.bufs[way, t] = value
                self.copy(way, t).start()

            pl.when(self.active(way, t))(run)

    def finish(self, out):
        out[...] = self.parts[self.z].astype(F32)
        t = self.nt - 2
        for way in range(2):

            @pl.when(self.arrives(way, t))
            def _():
                self.copy(way, t).wait_recv()
                out[...] += self.landed[way, t].astype(F32)

    def drain(self):
        for way in range(2):
            for t in range(self.nt - 1):
                pl.when(self.active(way, t))(self.copy(way, t).wait_send)


def chain_scratch(nt, rows, width):
    dma = pltpu.SemaphoreType.DMA
    return [
        pltpu.VMEM((2, nt - 1, rows, width), BF16),
        pltpu.VMEM((2, nt - 1, rows, width), BF16),
        dma((2, nt - 1)),
        dma((2, nt - 1)),
    ]


def mix_scatter_kernel(channels, nt, feed, *refs):
    (o, y, z_in, sq, gain, watt, wmam, tok), refs = refs[:8], refs[8:]
    if feed:
        (hid_z, dwn_z), refs = refs[2:4], refs[4:]
        (m_o, sq_o, hid_o, hid_f, dwn_f), refs = refs[:5], refs[5:]
        (lsem, f_send, f_recv), refs = refs[:3], refs[3:]
    else:
        (m_o, sq_o, hid_o), refs = refs[:3], refs[3:]
    (sq_land, sq_send, sq_recv, parts, bufs, landed, c_send, c_recv) = refs
    d = lax.axis_index("dp")
    z = lax.axis_index("tensor")
    rows = tok.shape[0]
    peers = [(p, z) for p in cube_peers(d)] if feed else []
    greet(peers + other_quarters(d, z, nt))
    squares = Exchange(sq, sq_land, sq_send, sq_recv, d, z, nt)
    squares.start()
    n = 2 * (nt - 1)
    if feed:
        items = []
        for k in range(1, nt):
            q = lax.rem(z - k + nt, nt)
            items.append((hid_z.at[q], lambda s, q=q: hid_f.at[s, q]))
            items.append((dwn_z.at[q], lambda s, q=q: dwn_f.at[s, q]))
        cube = CubeGather(items, (0, 3, 4), f_send, f_recv, d, z)
        for i in range(n):
            cube.start(i)
        locals_ = []
        for i, (src, dst) in enumerate([(src, at(d)) for src, at in items]):
            locals_.append(pltpu.make_async_copy(src, dst, lsem.at[i]))
            locals_[-1].start()
    chain = ChainScatter(parts, bufs, landed, c_send, c_recv, d, z, nt)
    squares.wait()
    sq_o[...] = squares.total()

    def part(q):
        at = pl.ds(pl.multiple_of(q * rows, rows), rows)
        total = sq_o[:, at]
        r = row_columns([lax.rsqrt(total / channels + epsilon)], rows)[:, 0:1]
        zv = z_in[at, :]
        m = (y[at, :] * (zv * sigmoid(zv)) * r * gain[...]).astype(BF16)
        m_o[at, :] = m
        parts[q] = (dot_nn(o[at, :], watt[...]) + dot_nn(m, wmam[...])).astype(BF16)

    first = jnp.where(z < nt // 2, nt - 1, 0)
    part(first)
    chain.step(0)

    def rest(i, carry):
        part(lax.rem(first + 1 + i, nt))
        return carry

    lax.fori_loop(0, nt - 1, rest, 0)
    if feed:
        cube.near(0)
        cube.near(1)
    for t in range(1, nt - 1):
        chain.step(t)
        if feed:
            cube.near(2 * t)
            cube.near(2 * t + 1)
            cube.far(2 * t - 2)
            cube.far(2 * t - 1)
    if feed:
        cube.far(n - 2)
        cube.far(n - 1)
    chain.finish(hid_o)
    hid_o[...] += tok[...].astype(F32)
    chain.drain()
    if feed:
        cube.finish()
        for copy in locals_:
            copy.wait()


def mix_scatter(channels, nt, o, y, zr, sq, gain, watt, wmam, tok, feed=()):
    total, inner = y.shape
    rows, width = tok.shape
    dma = pltpu.SemaphoreType.DMA
    sds = jax.ShapeDtypeStruct
    vmem = pl.BlockSpec(memory_space=pltpu.VMEM)
    anywhere = pl.BlockSpec(memory_space=pl.ANY)
    outs = [sds((total, inner), BF16), sds((8, total), F32), sds((rows, width), F32)]
    scratch = []
    n = 2 * (nt - 1)
    if feed:
        for v in feed[:2]:
            outs.append(sds(v.shape, BF16))
        scratch = [dma((n,)), dma((n, 7)), dma((n, 7))]
    return pl.pallas_call(
        partial(mix_scatter_kernel, channels, nt, bool(feed)),
        in_specs=[vmem] * 8 + [anywhere] * len(feed[:2]) + [vmem] * len(feed[2:]),
        out_specs=[vmem] * 3 + [anywhere] * (len(outs) - 3),
        out_shape=outs,
        input_output_aliases={8: 3, 9: 4} if feed else {},
        scratch_shapes=scratch + [pltpu.VMEM((nt - 1, 8, total), F32), dma((nt - 1,)), dma((nt - 1,)),
                        pltpu.VMEM((nt, rows, width), BF16)] + chain_scratch(nt, rows, width),
        compiler_params=pltpu.CompilerParams(
            vmem_limit_bytes=VMEM_LIMIT, collective_id=1, has_side_effects=True
        ),
        cost_estimate=pl.CostEstimate(flops=int(1e9), bytes_accessed=int(130e6), transcendentals=int(4e5)),
        name="mix_scatter",
    )(o, y, zr, sq, gain, watt, wmam, tok, *feed)


class ChainGather:
    def __init__(self, own, slots, send, recv, d, z, nt):
        self.own, self.slots, self.send, self.recv = own, slots, send, recv
        self.d, self.z, self.nt = d, z, nt

    def copy(self, way, dist):
        dev = (self.d, self.z + 1 if way == 0 else self.z - 1)
        slot = self.z - dist if way == 0 else self.z + dist
        src = self.own if dist == 0 else self.slots.at[slot]
        return remote_copy(src, self.slots.at[slot], self.send.at[way, dist], self.recv.at[way, dist], dev)

    def landing(self, way, dist):
        slot = self.z - dist if way == 0 else self.z + dist
        return remote_copy(
            self.slots.at[slot], self.slots.at[slot], self.send.at[way, dist - 1],
            self.recv.at[way, dist - 1], (self.d, self.z),
        )

    def has(self, way, dist):
        return self.z >= dist if way == 0 else self.z + dist < self.nt

    def goes_on(self, way):
        return self.z < self.nt - 1 if way == 0 else self.z > 0

    def start(self):
        for way in range(2):
            pl.when(self.goes_on(way))(self.copy(way, 0).start)

    def hop(self, dist):
        for way in range(2):
            pl.when(self.has(way, dist))(self.landing(way, dist).wait_recv)
            if dist < self.nt - 1:
                pl.when(self.has(way, dist) & self.goes_on(way))(self.copy(way, dist).start)

    def drain(self):
        for way in range(2):
            pl.when(self.goes_on(way))(self.copy(way, 0).wait_send)
            for dist in range(1, self.nt - 1):
                pl.when(self.has(way, dist) & self.goes_on(way))(self.copy(way, dist).wait_send)


class Unmix:
    def __init__(self, y, z_in, gain, watt, wmam, g_o, do_o, dm_o, dots, rows):
        self.ins = (y, z_in, gain, watt, wmam)
        self.outs = (g_o, do_o, dm_o, dots)
        self.rows = rows

    def __call__(self, q, g):
        y, z_in, gain, watt, wmam = self.ins
        g_o, do_o, dm_o, dots_o = self.outs
        rows = self.rows
        at = pl.ds(pl.multiple_of(q * rows, rows), rows)
        g_o[at, :] = g
        do_o[at, :] = dot_nt(g, watt[...]).astype(BF16)
        dm = dot_nt(g, wmam[...])
        dm_o[at, :] = dm
        zv = z_in[at, :]
        dots = jnp.sum(dm * gain[...] * (y[at, :] * (zv * sigmoid(zv))), axis=1, keepdims=True)
        turned = [jnp.broadcast_to(dots[c : c + 128], (128, 128)).T[0:8, :] for c in range(0, rows, 128)]
        dots_o[:, at] = jnp.concatenate(turned, axis=1)

    def around(self, z, dist, nt, slots):
        def side(way, carry):
            q = jnp.where(way == 0, z - dist, z + dist)

            @pl.when((q >= 0) & (q < nt))
            def _():
                self(q, slots[q])

            return carry

        lax.fori_loop(0, 2, side, 0)


def unmix_gather_kernel(nt, *refs):
    (dmix, y, z_in, gain, watt, wmam), refs = refs[:6], refs[6:]
    (g_o, do_o, dm_o, dot_o), refs = refs[:4], refs[4:]
    (slots, g_send, g_recv, dot_own, dot_land, d_send, d_recv) = refs
    d = lax.axis_index("dp")
    z = lax.axis_index("tensor")
    greet(other_quarters(d, z, nt))
    chain = ChainGather(dmix, slots, g_send, g_recv, d, z, nt)
    chain.start()
    work = Unmix(y, z_in, gain, watt, wmam, g_o, do_o, dm_o, dot_own, dmix.shape[0])
    work(z, dmix[...])
    for dist in range(1, nt):
        chain.hop(dist)
        work.around(z, dist, nt, slots)
    dots = Exchange(dot_own, dot_land, d_send, d_recv, d, z, nt)
    dots.start()
    chain.drain()
    dots.wait()
    dot_o[...] = dots.total()


def unmix_shapes(total, width, inner):
    sds = jax.ShapeDtypeStruct
    return [sds((total, width), BF16), sds((total, 128), BF16), sds((total, inner), F32),
            sds((8, total), F32)]


def unmix_scratch(nt, rows, width, total):
    dma = pltpu.SemaphoreType.DMA
    return [pltpu.VMEM((nt, rows, width), BF16), dma((2, nt - 1)), dma((2, nt - 1)),
            pltpu.VMEM((8, total), F32), pltpu.VMEM((nt - 1, 8, total), F32), dma((nt - 1,)), dma((nt - 1,))]


def unmix_gather(nt, dmix, y, zr, gain, watt, wmam):
    total, inner = y.shape
    rows, width = dmix.shape
    vmem = pl.BlockSpec(memory_space=pltpu.VMEM)
    return pl.pallas_call(
        partial(unmix_gather_kernel, nt),
        in_specs=[vmem] * 6,
        out_specs=[vmem] * 4,
        out_shape=unmix_shapes(total, width, inner),
        scratch_shapes=unmix_scratch(nt, rows, width, total),
        compiler_params=pltpu.CompilerParams(
            vmem_limit_bytes=VMEM_LIMIT, collective_id=2, has_side_effects=True
        ),
        name="unmix_gather",
    )(dmix, y, zr, gain, watt, wmam)


BOXES = 4


def feed_unmix_kernel(nt, *refs):
    (hid, gain, cot, whid, wdown, y, z_in, mgain, watt, wmam), refs = refs[:10], refs[10:]
    (out_o, dh_o, gg_o, g_o, do_o, dm_o, dot_o, own_o, sum_o), refs = refs[:9], refs[9:]
    (a2, a2t, acc, dacc, fs, dgs, dus, dmix, piece, sent, came, b_send, b_recv), refs = refs[:13], refs[13:]
    boxes, refs = refs[: 8 * (nt - 1)], refs[8 * (nt - 1) :]
    (slots, g_send, g_recv, dot_own, dot_land, d_send, d_recv) = refs
    step = pl.program_id(0)
    tiles = pl.num_programs(0) // 2
    d = lax.axis_index("dp")
    z = lax.axis_index("tensor")
    core = lax.rem(d, 2)
    bits = dp_bits(d)
    peers = cube_peers(d)
    chain = ChainGather(dmix, slots, g_send, g_recv, d, z, nt)
    cubes = []
    for k in range(1, nt):
        q = lax.rem(z + k, nt)
        box = boxes[8 * k - 8 : 8 * k]
        cubes.append(
            SquareScatter(lambda i, j, q=q: (2 * i + j, q), piece, box[:6], box[6], box[7], peers, bits, z)
        )

    @pl.when(step == 0)
    def _():
        greet([(p, z) for p in peers] + other_quarters(d, z, nt))
        feed_open(hid, gain, a2, a2t, acc, dacc)

    @pl.when(step < tiles)
    def _():
        fs[step], dgs[step], dus[step] = feed_tile(a2, cot, whid, wdown, acc, dacc)

    @pl.when(step == tiles - 1)
    def _():
        dmix[...] = feed_close(hid, gain, cot, acc, dacc, out_o, dh_o, gg_o)
        chain.start()

    units = whid.shape[4]
    quarter_units = piece.shape[2] // 3
    tiles_per = quarter_units // units

    def swap(turn_):
        box = lax.rem(turn_, BOXES)
        return remote_copy(
            sent.at[box], came.at[box], b_send.at[box], b_recv.at[box], (peers[0], z)
        )

    def places(turn_):
        quarter = lax.rem(z + 1 + turn_ // tiles_per, nt)
        part = lax.rem(turn_, tiles_per)
        return quarter, part, piece_rows(part, units, quarter_units)

    def take(turn_):
        swap(turn_).wait_recv()
        quarter, _, rows = places(turn_)
        box = lax.rem(turn_, BOXES)
        first = 0
        for row, n in rows:
            at = pl.ds(pl.multiple_of(row, 128), n)
            piece[:, quarter, at, :] = add_refs(
                piece[:, quarter, at, :], came[box, :, first : first + n, :]
            ).astype(BF16)
            first += n

    @pl.when(step >= tiles)
    def _():
        turn_ = step - tiles
        quarter, part, rows = places(turn_)
        tile = quarter * tiles_per + part
        box = lax.rem(turn_, BOXES)
        pl.when(turn_ >= BOXES)(lambda: swap(turn_ - BOXES).wait_send())
        first = 0
        for value, (row, n) in zip(feed_grads(a2t, cot, fs[tile], dgs[tile], dus[tile]), rows):
            at = pl.ds(pl.multiple_of(row, 128), n)
            value = value.reshape(value.shape[0] // 2, 2, n, 128)
            even, odd = value[:, 0], value[:, 1]
            piece[:, quarter, at, :] = jnp.where(core == 0, even, odd)
            sent[box, :, first : first + n, :] = jnp.where(core == 0, odd, even)
            first += n
        swap(turn_).start()
        pl.when(turn_ >= 1)(lambda: take(turn_ - 1))
        for k in range(1, nt):
            pl.when(turn_ == k * tiles_per)(cubes[k - 1].start)

    @pl.when(step == 2 * tiles - 1)
    def _():
        take(tiles - 1)
        for i in range(BOXES):
            swap(tiles - BOXES + i).wait_send()
        own_o[...] = piece[:, z]
        work = Unmix(y, z_in, mgain, watt, wmam, g_o, do_o, dm_o, dot_own, hid.shape[0])
        work(z, dmix[...])
        for dist in range(1, nt):
            chain.hop(dist)
            work.around(z, dist, nt, slots)
            if dist == 1:
                cubes[0].middle()
            if dist < nt - 1:
                cubes[dist].middle()
            elif dist == nt - 1:
                dots = Exchange(dot_own, dot_land, d_send, d_recv, d, z, nt)
                dots.start()
        for k, cube in enumerate(cubes):
            cube.finish(sum_o.at[k])
        chain.drain()
        for cube in cubes:
            cube.drain()
        dots.wait()
        dot_o[...] = dots.total()


def feed_unmix(nt, hid, gain, cot, whid, wdown, y, zr, mgain, watt, wmam):
    rows, width = hid.shape
    total, inner = y.shape
    blocks, _, _, depth, units = whid.shape
    tile = 256
    per = units // tile
    tiles = nt * per
    kept = blocks // 2
    n = 3 * units
    dma = pltpu.SemaphoreType.DMA
    sds = jax.ShapeDtypeStruct

    def fixed(v):
        return pl.BlockSpec(v.shape, lambda i: (0,) * len(v.shape), pipeline_mode=pl.Buffered(1))

    def at_tile(i):
        return jnp.minimum(i, tiles - 1)

    hid_spec = pl.BlockSpec(
        (blocks, 1, 2, depth, tile), lambda i: (0, at_tile(i) // per, 0, 0, lax.rem(at_tile(i), per))
    )
    down_spec = pl.BlockSpec(
        (blocks, 1, tile, 128), lambda i: (0, at_tile(i) // per, lax.rem(at_tile(i), per), 0)
    )
    out_shape = [sds((rows, width), BF16), sds((rows, width), F32), sds((1, width), F32)]
    out_shape += unmix_shapes(total, width, inner)
    out_shape += [sds((kept, n, 128), BF16), sds((nt - 1, n, 128), BF16)]
    box = pltpu.VMEM((BOXES, kept, 3 * tile, 128), BF16)
    kept_tile = pltpu.VMEM((tiles, rows, tile), BF16)
    scratch = [pltpu.VMEM((rows, width), BF16), pltpu.VMEM((width, rows), BF16),
               pltpu.VMEM((rows, width), F32), pltpu.VMEM((rows, width), F32), kept_tile, kept_tile, kept_tile,
               pltpu.VMEM((rows, width), BF16), pltpu.VMEM((kept, nt, n, 128), BF16), box, box, dma((BOXES,)),
               dma((BOXES,))]
    for _ in range(nt - 1):
        scratch += square_scratch(n, 128)
    return pl.pallas_call(
        partial(feed_unmix_kernel, nt),
        grid=(2 * tiles,),
        in_specs=[fixed(hid), fixed(gain), fixed(cot), hid_spec, down_spec, fixed(y), fixed(zr), fixed(mgain),
                  fixed(watt), fixed(wmam)],
        out_specs=[fixed(v) for v in out_shape],
        out_shape=out_shape,
        scratch_shapes=scratch + unmix_scratch(nt, rows, width, total),
        compiler_params=pltpu.CompilerParams(
            vmem_limit_bytes=60 * 1024 * 1024, collective_id=4, has_side_effects=True
        ),
        cost_estimate=pl.CostEstimate(flops=int(1e10), bytes_accessed=int(150e6), transcendentals=int(9e5)),
        name="feed_unmix",
    )(hid, gain, cot, whid, wdown, y, zr, mgain, watt, wmam)


def add_refs(left, right):
    return left.astype(F32) + right.astype(F32)


class SquareScatter:
    def __init__(self, place, held, bufs, send, recv, peers, bits, z):
        (self.r1, self.r2, self.ob, self.tb, self.r3, self.r4) = bufs
        self.place, self.held = place, held
        n = held.shape[-2]
        half = n // 2
        self.lo, self.hi = pl.ds(0, half), pl.ds(half, n - half)
        self.half = half
        _, self.x, self.y = bits
        x, y = self.x, self.y
        _, d_x, d_y = peers
        self.copies = []
        for i in range(2):
            self.copies.append(
                remote_copy(held.at[place(i, 1 - x) + (self.lo,)], self.r1.at[i], send.at[i], recv.at[i],
                            (d_x, z))
            )
        for j in range(2):
            self.copies.append(
                remote_copy(held.at[place(1 - y, j) + (self.hi,)], self.r2.at[j], send.at[2 + j],
                            recv.at[2 + j], (d_y, z))
            )
        self.copies.append(remote_copy(self.ob.at[1 - y], self.r3, send.at[4], recv.at[4], (d_y, z)))
        self.copies.append(remote_copy(self.tb.at[1 - x], self.r4, send.at[5], recv.at[5], (d_x, z)))

    def start(self):
        for copy in self.copies[:4]:
            copy.start()

    def middle(self):
        for i in range(2):
            self.copies[i].wait_recv()
            self.ob[i] = add_refs(self.held[self.place(i, self.x) + (self.lo,)], self.r1[i]).astype(BF16)
        self.copies[4].start()
        for j in range(2):
            self.copies[2 + j].wait_recv()
            self.tb[j] = add_refs(self.held[self.place(self.y, j) + (self.hi,)], self.r2[j]).astype(BF16)
        self.copies[5].start()

    def finish(self, out):
        self.copies[4].wait_recv()
        out[0 : self.half] = add_refs(self.ob[self.y], self.r3[...]).astype(out.dtype)
        self.copies[5].wait_recv()
        out[self.half :] = add_refs(self.tb[self.x], self.r4[...]).astype(out.dtype)

    def drain(self):
        for copy in self.copies:
            copy.wait_send()


def square_scratch(n, lanes):
    dma = pltpu.SemaphoreType.DMA
    half = n // 2
    return [
        pltpu.VMEM((2, half, lanes), BF16),
        pltpu.VMEM((2, n - half, lanes), BF16),
        pltpu.VMEM((2, half, lanes), BF16),
        pltpu.VMEM((2, n - half, lanes), BF16),
        pltpu.VMEM((half, lanes), BF16),
        pltpu.VMEM((n - half, lanes), BF16),
        dma((6,)),
        dma((6,)),
    ]


class CubeScatter:
    def __init__(self, pieces, bufs, peers, bits, z):
        (self.rc, self.held, send, recv) = bufs[:4]
        self.p = pieces
        self.core = bits[0]
        self.first = remote_copy(
            pieces.at[:, 1 - self.core], self.rc, send.at[0], recv.at[0], (peers[0], z)
        )
        self.square = SquareScatter(
            lambda i, j: (2 * i + j,), self.held, bufs[4:10], bufs[10], bufs[11], peers, bits, z
        )

    def start(self):
        self.first.start()

    def middle(self):
        self.first.wait_recv()
        for i in range(4):
            self.held[i] = add_refs(self.p[i, self.core], self.rc[i]).astype(BF16)
        self.square.start()

    def last(self):
        self.square.middle()

    def finish(self, out):
        self.square.finish(out)

    def drain(self):
        self.first.wait_send()
        self.square.drain()


def cube_scratch(n, lanes):
    dma = pltpu.SemaphoreType.DMA
    return [
        pltpu.VMEM((4, n, lanes), BF16),
        pltpu.VMEM((4, n, lanes), BF16),
        dma((1,)),
        dma((1,)),
    ] + square_scratch(n, lanes)


class CubeTotal:
    def __init__(self, held, landed, send, recv, peers, z):
        self.held, self.landed = held, landed
        self.copies = [
            remote_copy(held.at[i], landed.at[i], send.at[i], recv.at[i], (peer, z))
            for i, peer in enumerate(peers)
        ]

    def start(self, i):
        self.copies[i].start()

    def take(self, i):
        self.copies[i].wait_recv()
        self.held[i + 1] = self.held[i] + self.landed[i]

    def drain(self):
        for copy in self.copies:
            copy.wait_send()


def norm_back(dy, tok, gain, dh, out, ggain):
    v = tok[...].astype(F32)
    width = v.shape[1]
    f = lax.rsqrt(jnp.mean(v * v, axis=1, keepdims=True) + epsilon)
    ggain(jnp.sum(dy * v * f, axis=0, keepdims=True))
    gdy = dy * gain[...]
    lean = jnp.sum(gdy * v, axis=1, keepdims=True) * (f * f * f / width)
    out[...] = (dh[...] + (f * gdy - v * lean)).astype(BF16)


SMALL_ALL = 24
SMALL_ROWS = 152


def tail_kernel(
    nt, tok, gain, dh, a1, dmix, o, m, dq, dz, dx, dkv, db, drow, wq, win, stp, wsh,
    gg, gtb, gtx, grows, gheads, feed_own, feed_rest,
    gt_o, mixed_o, fed_o, sh_o, small_o, norm_o,
    da, parts, pieces, shared, ot, mt, bufs, landed, c_send, c_recv, *rest,
):
    cube_a, rest = rest[:12], rest[12:]
    cube_b, rest = rest[:12], rest[12:]
    square_c, rest = rest[:8], rest[8:]
    (sh_sum, sh_land, sh_send, sh_recv) = rest[:4]
    (sm_held, sm_land, sm_send, sm_recv, all_own, all_land, all_send, all_recv) = rest[4:12]
    (ng_held, ng_land, ng_send, ng_recv, ngz_land, ngz_send, ngz_recv) = rest[12:]
    d = lax.axis_index("dp")
    z = lax.axis_index("tensor")
    bits = dp_bits(d)
    peers = cube_peers(d)
    rows = tok.shape[0]
    greet([(p, z) for p in peers] + other_quarters(d, z, nt))
    three = SquareScatter(
        lambda i, j: (i, j), feed_own, square_c[:6], square_c[6], square_c[7], peers, bits, z
    )
    three.start()
    chain = ChainScatter(parts, bufs, landed, c_send, c_recv, d, z, nt)

    def part(q):
        at = pl.ds(pl.multiple_of(q * rows, rows), rows)
        parts[q] = down_rows(at, dq, dz, dx, dkv, db, drow, wq, win, stp, wsh).astype(BF16)

    first = jnp.where(z < nt // 2, nt - 1, 0)
    part(first)
    chain.step(0)

    def others(i, carry):
        part(lax.rem(first + 1 + i, nt))
        return carry

    lax.fori_loop(0, nt - 1, others, 0)
    ot[...] = o[...].T
    mt[...] = m[...].T

    def columns(i, carry):
        at = pl.ds(pl.multiple_of(i * 256, 256), 256)

        def put(k, first, values):
            pieces[i, k, first : first + values.shape[0], :] = values

        def put_shared(k, first, values):
            shared[i, k, :, first : first + values.shape[1]] = values

        weight_columns(a1[:, at], dmix[:, at], dq, dz, dx, dkv, db, ot, mt, put, put_shared)
        return carry

    lax.fori_loop(0, 2, columns, 0)
    chain.step(1)
    lax.fori_loop(2, 4, columns, 0)
    one = CubeScatter(pieces, cube_a, peers, bits, z)
    two = CubeScatter(shared, cube_b, peers, bits, z)
    sums = CubeTotal(sm_held, sm_land, sm_send, sm_recv, peers, z)
    for k in range(8):
        sm_held[0, k : k + 1, :] = gg[:, 128 * k : 128 * k + 128]
    for first_row, ref in ((8, gtb), (SMALL_ALL, gtx), (48, grows)):
        for k in range(ref.shape[1] // 128):
            sm_held[0, first_row + 8 * k : first_row + 8 * k + 8, :] = ref[:, 128 * k : 128 * k + 128]
    sm_held[0, 72:88, :] = gheads[...]
    steps = dot_nn(drow[...].astype(BF16), a1[...])
    for k in range(8):
        sm_held[0, 88 + 8 * k : 96 + 8 * k, :] = steps[:, 128 * k : 128 * k + 128]
    sums.start(0)
    two.start()
    one.start()
    three.middle()
    sums.take(0)
    sums.start(1)
    two.middle()
    one.middle()
    sums.take(1)
    sums.start(2)
    for t in range(2, nt - 1):
        chain.step(t)
    sums.take(2)
    all_own[...] = sm_held[3, 0:SMALL_ALL, :]
    over_all = Exchange(all_own, all_land, all_send, all_recv, d, z, nt)
    over_all.start()
    three.finish(fed_o)
    fed_o[...] += feed_rest[...]
    two.last()
    one.last()
    two.finish(sh_sum)
    per = sh_sum.shape[0] // nt
    copies = []
    for k in range(1, nt):
        q = lax.rem(z + k, nt)
        at = pl.ds(pl.multiple_of(q * per, per), per)
        copies.append(
            remote_copy(sh_sum.at[at], sh_land.at[k - 1], sh_send.at[k - 1], sh_recv.at[k - 1], (d, q))
        )
        copies[-1].start()
    one.finish(mixed_o)
    chain.finish(da)

    def keep(row):
        for k in range(8):
            ng_held[0, k : k + 1, :] = row[:, 128 * k : 128 * k + 128]

    norm_back(da[...], tok, gain, dh, gt_o, keep)
    norms = CubeTotal(ng_held, ng_land, ng_send, ng_recv, peers, z)
    norms.start(0)
    small_o[...] = sm_held[3]
    over_all.wait()
    small_o[0:SMALL_ALL, :] = over_all.total()
    norms.take(0)
    norms.start(1)
    for copy in copies:
        copy.wait()
    total = sh_sum[pl.ds(pl.multiple_of(z * per, per), per), :].astype(F32)
    for k in range(nt - 1):
        total = total + sh_land[k].astype(F32)
    sh_o[...] = total
    norms.take(1)
    norms.start(2)
    norms.take(2)
    last = Exchange(ng_held.at[3], ngz_land, ngz_send, ngz_recv, d, z, nt)
    last.start()
    last.wait()
    norm_o[...] = last.total()
    for thing in (chain, one, two, three, sums, norms):
        thing.drain()


def tail(nt, *args):
    tok, a1, dz = args[0], args[3], args[8]
    feed_own = args[-2]
    rows, width = tok.shape
    total = a1.shape[0]
    inner = dz.shape[1]
    n, lanes = 256 + 3 * inner, 128
    s_rows, s_lanes = 128, args[16].shape[1]
    f_rows = feed_own.shape[2]
    dma = pltpu.SemaphoreType.DMA
    sds = jax.ShapeDtypeStruct
    vmem = pl.BlockSpec(memory_space=pltpu.VMEM)
    return pl.pallas_call(
        partial(tail_kernel, nt),
        in_specs=[vmem] * len(args),
        out_specs=[vmem] * 6,
        out_shape=[sds((rows, width), BF16), sds((n, lanes), F32), sds((f_rows, 128), F32),
                   sds((s_rows // nt, s_lanes), F32), sds((SMALL_ROWS, 128), F32), sds((8, 128), F32)],
        scratch_shapes=[pltpu.VMEM((rows, width), F32), pltpu.VMEM((nt, rows, width), BF16),
                        pltpu.VMEM((4, 2, n, lanes), BF16), pltpu.VMEM((4, 2, s_rows, s_lanes), BF16),
                        pltpu.VMEM((128, total), BF16), pltpu.VMEM((inner, total), BF16)]
        + chain_scratch(nt, rows, width)
        + cube_scratch(n, lanes) + cube_scratch(s_rows, s_lanes) + square_scratch(f_rows, 128)
        + [pltpu.VMEM((s_rows, s_lanes), BF16), pltpu.VMEM((nt - 1, s_rows // nt, s_lanes), BF16),
           dma((nt - 1,)), dma((nt - 1,)),
           pltpu.VMEM((4, SMALL_ROWS, 128), F32), pltpu.VMEM((3, SMALL_ROWS, 128), F32), dma((3,)), dma((3,)),
           pltpu.VMEM((SMALL_ALL, 128), F32), pltpu.VMEM((nt - 1, SMALL_ALL, 128), F32), dma((nt - 1,)),
           dma((nt - 1,)),
           pltpu.VMEM((4, 8, 128), F32), pltpu.VMEM((3, 8, 128), F32), dma((3,)), dma((3,)),
           pltpu.VMEM((nt - 1, 8, 128), F32), dma((nt - 1,)), dma((nt - 1,))],
        compiler_params=pltpu.CompilerParams(
            vmem_limit_bytes=VMEM_LIMIT, collective_id=3, has_side_effects=True
        ),
        cost_estimate=pl.CostEstimate(flops=int(7e9), bytes_accessed=int(150e6), transcendentals=0),
        name="tail",
    )(*args)


def finish_kernel(
    heads, place, mixed, fed, small, norm,
    que_o, att_o, inn_o, mam_o, hid_o, dwn_o, norms_o, taps_o, chan_o, gain_o, step_o, heads_o,
):
    d, p = place[0], place[1]
    block = que_o.shape[0]
    inner = mam_o.shape[0]
    first = 0
    for j in range(que_o.shape[1] // 128):
        que_o[:, 128 * j : 128 * j + 128] = mixed[first : first + block]
        first += block
    att_o[...] = mixed[first : first + att_o.shape[0]]
    first += att_o.shape[0]
    for i in range(2):
        for j in range(inner // 128):
            inn_o[i, :, 128 * j : 128 * j + 128] = mixed[first : first + block]
            first += block
    mam_o[...] = mixed[first : first + inner]
    first = 0
    for i in range(2):
        for j in range(hid_o.shape[2] // 128):
            hid_o[i, :, 128 * j : 128 * j + 128] = fed[first : first + block]
            first += block
    dwn_o[...] = fed[first:]

    def lanes_from(values, lane):
        return pltpu.roll(values, lax.rem(128 - lane, 128), 1)

    width = norms_o.shape[1]
    per = 128 // width
    for i, ref in enumerate((norm, small)):
        row = lanes_from(jnp.broadcast_to(ref[pl.ds(p // per, 1), :], (8, 128)), lax.rem(p, per) * width)
        norms_o[i : i + 1, :] = row[0:1, 0:width]
    width = taps_o.shape[1]
    per = 128 // width
    row = small[pl.ds(pl.multiple_of(8 + 8 * (p // per), 8), 8), :]
    taps_o[...] = lanes_from(row, lax.rem(p, per) * width)[0 : CONV + 1, 0:width]
    width = gain_o.shape[1]
    sums = jnp.zeros((8, 128), F32)
    lane = lanes_of(sums.shape)
    sub = lax.broadcasted_iota(jnp.int32, sums.shape, 0)
    for b in range(heads // 2):
        rows = lanes_from(small[SMALL_ALL + 8 * b : SMALL_ALL + 8 * b + 8, :], d * width)
        raw = small[48 + 8 * b : 56 + 8 * b, :]
        gains = lanes_from(raw, d * width)
        for k in range(2):
            h = 2 * b + k
            at = slice(64 * k, 64 * k + width)
            chan_o[:, h, :] = rows[0 : CONV + 1, at]
            gain_o[h : h + 1, :] = gains[0:1, at]
            skip = jnp.sum(jnp.where(lane // SSM_DIM == k, raw[1:2, :], 0.0), axis=1, keepdims=True)
            sums = jnp.where((sub == h) & (lane == 2), skip, sums)
    for k in range(2):
        total = jnp.sum(small[72 + 8 * k : 80 + 8 * k, :], axis=1, keepdims=True)
        sums = jnp.where(lane == k, total, sums)
    heads_o[...] = sums
    steps = small[pl.ds(pl.multiple_of(88 + 8 * d, 8), 8), :]
    steps = jnp.concatenate([steps, jnp.zeros((120, 128), F32)], axis=0).T
    step_o[...] = steps[:, 0:heads]


def finish(heads, place, mixed, fed, small, norm, shapes):
    vmem = pl.BlockSpec(memory_space=pltpu.VMEM)
    sds = jax.ShapeDtypeStruct
    return pl.pallas_call(
        partial(finish_kernel, heads),
        in_specs=[pl.BlockSpec(memory_space=pltpu.SMEM)] + [vmem] * 4,
        out_specs=[vmem] * (len(shapes) + 1),
        out_shape=[sds(s, F32) for s in shapes] + [sds((8, 128), F32)],
        compiler_params=pltpu.CompilerParams(vmem_limit_bytes=VMEM_LIMIT),
        name="finish",
    )(place, mixed, fed, small, norm)


def rope_wide(length):
    half = HEAD_SIZE // 2
    inverse = rope_base ** (-np.arange(half) * (2.0 / HEAD_SIZE))
    angles = np.arange(length)[:, None] * inverse[None, :]
    c, s = np.cos(angles), np.sin(angles)
    return (
        jnp.asarray(np.concatenate([c, c, c, c], axis=1), F32),
        jnp.asarray(np.concatenate([-s, s, -s, s], axis=1), F32),
    )


def to_blocks(full, axis, nt):
    if axis == 1:
        two, width, cols = full.shape
        return full.reshape(2, 8, width // 8, nt, cols // nt).transpose(1, 3, 0, 2, 4)
    rows, width = full.shape
    return full.reshape(nt, rows // nt, 8, width // 8).transpose(2, 0, 1, 3)


def per_device(
    nd,
    nt,
    tokens,
    query_proj,
    attend_out,
    inner_proj,
    step_proj,
    mamba_out,
    hidden_proj,
    down_proj,
    channel_taps,
    mixer_gain,
    decay_log,
    step_bias,
    skip_weight,
    shared_proj,
    norm_gains,
    shared_taps,
    cotangent,
):
    tensor_index = lax.axis_index("tensor")
    d = lax.axis_index("dp")
    local_rows, width = tokens.shape
    group_rows = local_rows * nt
    heads = step_proj.shape[1]
    inner = heads * SSM_DIM
    channels = inner * nt
    units = down_proj.shape[0]
    feed = ()
    if nd == 8:
        small = pack_small(channel_taps, mixer_gain, norm_gains, shared_taps, step_proj)
        (tok_full, full_query, full_attend, full_inner, full_mamba, sha, sma) = gather_start(
            tokens, query_proj, attend_out, inner_proj, mamba_out, shared_proj, small, nd, nt
        )
        scal = jnp.stack([decay_log, step_bias, skip_weight]).astype(F32)
        where = tensor_index.astype(jnp.int32).reshape(1)
        (
            gain_first, gain_second, gain_mix, taps_x, taps_b, step_rows, decay, bias, skip,
        ) = unpack_small(heads, where, scal, sma, width)
        full_shared = sha.reshape(width, -1)
        feed = (hidden_proj, down_proj)
    else:
        small_parts = [channel_taps, mixer_gain, norm_gains, shared_taps, step_proj.T]
        flat = jnp.concatenate([p.reshape(-1) for p in small_parts])
        small_len = -(-flat.shape[0] // 2048) * 2048
        small = jnp.pad(flat, (0, small_len - flat.shape[0])).reshape(-1, 128)
        (tok_full, full_query, full_attend, full_inner, full_mamba, sha, sma) = gather_start(
            tokens, query_proj, attend_out, inner_proj, mamba_out, shared_proj, small, nd, nt
        )
        full_hidden = lax.all_gather(hidden_proj, "tensor", axis=2, tiled=True)
        full_hidden = to_blocks(lax.all_gather(full_hidden, "dp", axis=1, tiled=True), 1, nt)
        full_down = lax.all_gather(down_proj, "tensor", axis=0, tiled=True)
        full_down = to_blocks(lax.all_gather(full_down, "dp", axis=1, tiled=True), 0, nt)

        full_shared = sha.reshape(width, -1)
        sma = sma.reshape(nd, nt, small_len)

        def small_piece(index):
            start = sum(p.size for p in small_parts[:index])
            part = small_parts[index]
            return sma[:, :, start : start + part.size].reshape((nd, nt) + part.shape)

        taps_x = pick(small_piece(0), tensor_index, 1).transpose(1, 2, 0, 3).reshape(CONV + 1, inner)
        gain_mix = pick(small_piece(1), tensor_index, 1).transpose(1, 0, 2).reshape(1, inner)
        full_norms = small_piece(2).transpose(2, 0, 1, 3).reshape(2, width).astype(F32)
        taps_b = small_piece(3).transpose(2, 0, 1, 3).reshape(CONV + 1, -1)
        step_rows = pick(small_piece(4), tensor_index, 1).transpose(1, 0, 2).reshape(heads, width)
        step_rows = jnp.pad(step_rows, ((0, 8 - heads), (0, 0)))
        taps_x = jnp.pad(taps_x.astype(F32), ((0, 7 - CONV), (0, 0)))
        taps_b = jnp.pad(taps_b.astype(F32), ((0, 7 - CONV), (0, 0)))
        gain_mix = gain_mix.astype(F32)
        gain_first = full_norms[0:1]
        gain_second = full_norms[1:2]

        def head_rows(values):
            return jnp.pad(jnp.broadcast_to(values[:, None], (heads, 128)), ((0, 8 - heads), (0, 0)))

        decay = head_rows(-jnp.exp(decay_log.astype(F32)))
        bias = head_rows(step_bias.astype(F32))
        skip = jnp.repeat(skip_weight.astype(F32), SSM_DIM)[None, :]
    q_heads = query_proj.shape[1] // HEAD_SIZE
    kv_head = (tensor_index * q_heads // (QHEADS // KVHEADS)).astype(jnp.int32).reshape(1)
    cosine, sine = rope_wide(group_rows)

    (a1, q, k2, v2, lse, o, xr, zr, br, y, trow, states, squares, *feed) = mixers_forward(
        heads, nt, kv_head, tok_full.reshape(group_rows, width), gain_first, full_query, full_inner, step_rows,
        full_shared, cosine, sine, taps_x, taps_b, decay, bias, skip, feed,
    )
    mixed = mix_scatter(
        channels, nt, o, y, zr, squares, gain_mix, full_attend, full_mamba, tokens, tuple(feed)
    )
    m, squares, hidden = mixed[:3]
    if nd == 8:
        full_hidden, full_down = mixed[3:]
    if nd == 8:
        layer_out, dh, grad_gain_two, grad_mix, do, dm, dots, feed_own, feed_sums = feed_unmix(
            nt, hidden, gain_second, cotangent, full_hidden, full_down, y, zr, gain_mix, full_attend, full_mamba
        )
        feed_own = feed_own.reshape((2, 2) + feed_own.shape[1:])
    else:
        layer_out, dh, dmix, grad_gain_two, feed_pieces = feed_forward(
            hidden, gain_second, cotangent, full_hidden, full_down
        )
        grad_mix, do, dm, dots = unmix_gather(nt, dmix, y, zr, gain_mix, full_attend, full_mamba)
        hid_full = feed_pieces[:, :, : 2 * units].reshape(8, nt, 2, units // 128, width // 8, 128)
        hid_full = hid_full.transpose(2, 0, 4, 1, 3, 5).reshape(2, nd, width // nd, nt, units)
        hid_sum = cube_scatter(hid_full.transpose(1, 3, 0, 2, 4), nd, BF16)
        down_full = feed_pieces[:, :, 2 * units :].transpose(1, 2, 0, 3)
        down_full = down_full.reshape(nt, units, nd, width // nd)
        down_sum = cube_scatter(down_full.transpose(2, 0, 1, 3), nd, BF16)
        gradient_hidden = chain_scatter(hid_sum, nt)
        gradient_down = chain_scatter(down_sum, nt)

    back = mixers_back(
        heads, channels, nt, kv_head, q, k2, v2, lse, do, cosine, sine, dm, y, zr, xr, br, trow, states,
        squares, dots, gain_mix, taps_x, taps_b, decay, bias, skip, feed_sums if nd == 8 else None,
    )
    dq, dkv, dz, dx, db, drow, grad_tx, grad_tb, grad_rows, grad_heads = back[:10]
    if nd == 8:
        sums = tail(
            nt, tokens, gain_first, dh, a1, grad_mix, o, m, dq, dz, dx, dkv, db, drow, full_query, full_inner,
            step_rows, full_shared, grad_gain_two, grad_tb, grad_tx, grad_rows, grad_heads, feed_own, back[10],
        )
        gradient_tokens, mixed, fed, gradient_shared, small_sums, grad_gain_one = sums
        place = jnp.stack([d, d * nt + tensor_index]).astype(jnp.int32)
        shapes = [
            query_proj.shape, attend_out.shape, inner_proj.shape, mamba_out.shape, hidden_proj.shape,
            down_proj.shape, norm_gains.shape, shared_taps.shape, channel_taps.shape, mixer_gain.shape,
            step_proj.shape,
        ]
        (
            gradient_query,
            gradient_attend,
            gradient_inner,
            gradient_mamba,
            gradient_hidden,
            gradient_down,
            gradient_norms,
            gradient_taps,
            gradient_channel,
            gradient_mixer,
            gradient_step,
            head_sums,
        ) = finish(heads, place, mixed, fed, small_sums, grad_gain_one, shapes)
        return (
            layer_out,
            gradient_tokens,
            gradient_query,
            gradient_attend,
            gradient_inner,
            gradient_step,
            gradient_mamba,
            gradient_hidden,
            gradient_down,
            gradient_channel,
            gradient_mixer,
            head_sums[:heads, 0],
            head_sums[:heads, 1],
            head_sums[:heads, 2],
            gradient_shared,
            gradient_norms,
            gradient_taps,
        )

    part_one = down_parts(dq, dz, dx, dkv, db, drow, full_query, full_inner, step_rows, full_shared)
    pieces, shared_pieces, grad_step = weight_pieces(a1, dq, dz, dx, dkv, db, drow, o, m, grad_mix)
    block = width // nd
    q_cols = query_proj.shape[1]
    cuts = [0, q_cols, q_cols + attend_out.shape[0]]
    cuts += [cuts[2] + inner, cuts[2] + 2 * inner, cuts[2] + 3 * inner]

    def from_rows(values):
        return values.reshape(8, -1, 128, 128).transpose(0, 2, 1, 3).reshape(width, -1)

    def from_lanes(values):
        return values.transpose(1, 0, 2).reshape(-1, width)

    n_tap = CONV + 1
    over_all = jnp.concatenate([grad_gain_two.reshape(-1), grad_tb[:n_tap].reshape(-1)])
    over_dp = jnp.concatenate(
        [
            grad_tx[:n_tap].reshape(-1),
            grad_rows[0],
            grad_rows[1].reshape(heads, SSM_DIM).sum(axis=1),
            grad_heads[:heads].sum(axis=1),
            grad_heads[8 : 8 + heads].sum(axis=1),
            grad_step[:heads].reshape(-1),
        ]
    )

    def in_rows(values):
        return jnp.pad(values, (0, -values.shape[0] % 1024)).reshape(-1, 128)

    rows_all = in_rows(over_all)
    n_all = rows_all.shape[0]
    small_sums = jnp.concatenate([rows_all, in_rows(over_dp)], axis=0)
    parts = part_one.reshape(nt, local_rows, width)
    token_f32 = tokens.astype(F32)
    _, norm_one_back = jax.vjp(norm_apply, token_f32, gain_first[0])
    grad_from_one, grad_gain_one = norm_one_back(chain_scatter(parts, nt))
    gradient_tokens = (dh + grad_from_one).astype(BF16)
    got = [pieces[:, cuts[i] : cuts[i + 1]] for i in range(5)]

    def over_rows(values):
        return cube_scatter(from_rows(values).reshape(nd, block, -1), nd)

    def over_lanes(values):
        return cube_scatter(from_lanes(values).reshape(-1, nd, block).transpose(1, 0, 2), nd)

    gradient_query = over_rows(got[0])
    gradient_attend = over_lanes(got[1])
    gradient_inner = jnp.stack([over_rows(got[2]), over_rows(got[3])])
    gradient_mamba = over_lanes(got[4])
    shared_cut = shared_pieces.reshape(nd, nt, width // (nd * nt), -1)
    gradient_shared = chain_scatter(cube_scatter(shared_cut, nd, BF16), nt)
    small_sums = lax.psum(small_sums, "dp")
    small_sums = jnp.concatenate(
        [lax.psum(small_sums[:n_all], "tensor"), small_sums[n_all:]], axis=0
    )
    grad_gain_one = lax.psum(grad_gain_one, ("dp", "tensor")).reshape(1, width)
    over_all = small_sums[:n_all].reshape(-1)
    over_dp = small_sums[n_all:].reshape(-1)
    place = d * nt + tensor_index
    norm_w = width // (nd * nt)
    both_norms = jnp.concatenate([grad_gain_one, over_all[:width].reshape(1, width)], axis=0)
    gradient_norms = lax.dynamic_slice_in_dim(both_norms, place * norm_w, norm_w, 1)
    tap_w = shared_taps.shape[1]
    tap_all = over_all[width : width + n_tap * taps_b.shape[1]].reshape(n_tap, -1)
    gradient_taps = lax.dynamic_slice_in_dim(tap_all, place * tap_w, tap_w, 1)
    part = mixer_gain.shape[1]
    n_taps = n_tap * inner
    chan = over_dp[:n_taps].reshape(n_tap, heads, SSM_DIM)
    gain = over_dp[n_taps : n_taps + inner].reshape(heads, SSM_DIM)
    gradient_channel = lax.dynamic_slice_in_dim(chan, d * part, part, 2)
    gradient_mixer = lax.dynamic_slice_in_dim(gain, d * part, part, 1)
    rest = over_dp[n_taps + inner :]
    gradient_skip = rest[:heads]
    gradient_decay = rest[heads : 2 * heads]
    gradient_bias = rest[2 * heads : 3 * heads]
    step_all = rest[3 * heads : 3 * heads + heads * width].reshape(heads, width)
    gradient_step = lax.dynamic_slice_in_dim(step_all, d * block, block, 1).T
    return (
        layer_out,
        gradient_tokens,
        gradient_query,
        gradient_attend,
        gradient_inner,
        gradient_step,
        gradient_mamba,
        gradient_hidden,
        gradient_down,
        gradient_channel,
        gradient_mixer,
        gradient_decay,
        gradient_bias,
        gradient_skip,
        gradient_shared,
        gradient_norms,
        gradient_taps,
    )


def solution(mesh):
    placed = (
        P(("dp", "tensor"), None),
        P("dp", "tensor"),
        P("tensor", "dp"),
        P(None, "dp", "tensor"),
        P("dp", "tensor"),
        P("tensor", "dp"),
        P(None, "dp", "tensor"),
        P("tensor", "dp"),
        P(None, "tensor", "dp"),
        P("tensor", "dp"),
        P("tensor"),
        P("tensor"),
        P("tensor"),
        P(("dp", "tensor"), None),
        P(None, ("dp", "tensor")),
        P(None, ("dp", "tensor")),
        P(("dp", "tensor"), None),
    )
    return jax.shard_map(
        partial(per_device, mesh.shape["dp"], mesh.shape["tensor"]),
        mesh=mesh,
        in_specs=placed,
        out_specs=(
            P(("dp", "tensor"), None),
            P(("dp", "tensor"), None),
            P("dp", "tensor"),
            P("tensor", "dp"),
            P(None, "dp", "tensor"),
            P("dp", "tensor"),
            P("tensor", "dp"),
            P(None, "dp", "tensor"),
            P("tensor", "dp"),
            P(None, "tensor", "dp"),
            P("tensor", "dp"),
            P("tensor"),
            P("tensor"),
            P("tensor"),
            P(("dp", "tensor"), None),
            P(None, ("dp", "tensor")),
            P(None, ("dp", "tensor")),
        ),
        check_vma=False,
    )
```

```python
from functools import partial

import numpy as np
import jax
import jax.numpy as jnp
from jax import lax
from jax.experimental import pallas as pl
from jax.experimental.pallas import tpu as pltpu
from jax.sharding import PartitionSpec as P

MESH = pl.DeviceIdType.MESH

QHEADS = 8
KVHEADS = 2
HEAD_SIZE = 64
SSM_DIM = 64
CONV = 4


epsilon = 1e-05
rope_base = 100000000000.0
neg_large = -1e30
block_len = 128


def norm_apply(values, gain):
    factor = lax.rsqrt(jnp.mean(values * values, axis=-1, keepdims=True) + epsilon)
    return values * factor * gain


def dp_bits(index):
    core = lax.rem(index, 2)
    xbit = lax.rem(index // 2, 2)
    ybit = lax.rem(index // 4, 2)
    return core, xbit, ybit


def remote_copy(src, dst, send, recv, dev):
    return pltpu.make_async_remote_copy(
        src_ref=src, dst_ref=dst, send_sem=send, recv_sem=recv, device_id=dev, device_id_type=MESH
    )


def greet(peers):
    barrier = pltpu.get_barrier_semaphore()
    for peer in peers:
        pl.semaphore_signal(barrier, inc=1, device_id=peer, device_id_type=MESH)
    pl.semaphore_wait(barrier, len(peers))


def other_quarters(d, z, nt):
    return [(d, lax.rem(z + k, nt)) for k in range(1, nt)]


def cube_peers(d):
    core, xbit, ybit = dp_bits(d)
    return d + 1 - 2 * core, d + 2 - 4 * xbit, d + 4 - 8 * ybit


class CubeGather:
    def __init__(self, items, via_y, send, recv, d, z):
        self.items, self.via_y, self.send, self.recv = items, via_y, send, recv
        self.d, self.z = d, z
        self.d_core, self.d_x, self.d_y = cube_peers(d)
        self.d_xy = self.d_x + self.d_y - d
        self.sent = []

    def push(self, i, j, src, dst, peer):
        def make():
            return remote_copy(src(), dst(), self.send.at[i, j], self.recv.at[i, j], (peer, self.z))

        make().start()
        self.sent.append(make)

    def landed(self, i, j, slot):
        at = self.items[i][1]
        remote_copy(
            at(slot), at(slot), self.send.at[i, j], self.recv.at[i, j], (self.d_core, self.z)
        ).wait_recv()

    def start(self, i):
        src, at = self.items[i]
        for j, peer in enumerate((self.d_x, self.d_y, self.d_core)):
            self.push(i, j, lambda: src, lambda: at(self.d), peer)

    def near(self, i):
        d_x, d_y, d_core = self.d_x, self.d_y, self.d_core
        self.landed(i, 0, d_x)
        if i in self.via_y:
            self.hand_on(i, 3, d_x, d_y)
        self.hand_on(i, 4, d_x, d_core)
        self.landed(i, 1, d_y)
        if i not in self.via_y:
            self.hand_on(i, 3, d_y, d_x)
        self.hand_on(i, 5, d_y, d_core)

    def hand_on(self, i, j, slot, peer):
        at = self.items[i][1]
        self.push(i, j, lambda: at(slot), lambda: at(slot), peer)

    def far(self, i):
        self.landed(i, 3, self.d_xy)
        self.hand_on(i, 6, self.d_xy, self.d_core)

    def finish(self):
        for i in range(len(self.items)):
            self.landed(i, 2, self.d_core)
            for j in (4, 5, 6):
                self.landed(i, j, self.d_core)
        for make in self.sent:
            make().wait_send()


def gather_kernel(nt, *refs):
    (tok, que, att, inn, mam, sha, sma) = refs[:7]
    (tok_f, que_f, att_f, inn_f, mam_f, sha_f, sma_f) = refs[7:14]
    (lsem, zs_send, zs_recv, t_send, t_recv, d_send, d_recv) = refs[14:]
    d = lax.axis_index("dp")
    z = lax.axis_index("tensor")
    greet([(p, z) for p in cube_peers(d)] + other_quarters(d, z, nt))

    small = []
    for i, (src, dst) in enumerate(((sha, sha_f), (sma, sma_f))):
        for k, peer in enumerate(other_quarters(d, z, nt)):
            small.append(remote_copy(src, dst.at[d, z], zs_send.at[i, k], zs_recv.at[i, k], peer))
            small[-1].start()
    q_rows = que.shape[0]
    cols = att.shape[1]
    i_rows = inn.shape[1]
    items = [
        (inn, lambda s: inn_f.at[:, pl.ds(s * i_rows, i_rows)]),
        (que, lambda s: que_f.at[pl.ds(s * q_rows, q_rows)]),
        (att, lambda s: att_f.at[:, pl.ds(pl.multiple_of(s * cols, cols), cols)]),
        (mam, lambda s: mam_f.at[:, pl.ds(pl.multiple_of(s * cols, cols), cols)]),
        (sha_f.at[d], lambda s: sha_f.at[s]),
        (sma_f.at[d], lambda s: sma_f.at[s]),
    ]
    cube = CubeGather(items, (0, 5), d_send, d_recv, d, z)
    locals_ = []
    for i, (src, dst) in enumerate(
        [(sha, sha_f.at[d, z]), (sma, sma_f.at[d, z]), (tok, tok_f.at[z])]
        + [(src, at(d)) for src, at in items[:4]]
    ):
        copy = pltpu.make_async_copy(src, dst, lsem.at[i])
        copy.start()
        locals_.append(copy)
    for i in range(4):
        cube.start(i)
    chain = ChainGather(tok, tok_f, t_send, t_recv, d, z, nt)
    chain.start()
    locals_[0].wait()
    locals_[1].wait()
    for copy in small:
        copy.wait()
    cube.start(4)
    cube.start(5)
    for i in range(4):
        cube.near(i)
    chain.hop(1)
    for i in (4, 5):
        cube.near(i)
    for i in range(6):
        cube.far(i)
    for dist in range(2, nt):
        chain.hop(dist)
    cube.finish()
    for copy in locals_[2:]:
        copy.wait()
    chain.drain()


def gather_start(tok, que, att, inn, mam, sha, sma, nd, nt):
    if nd != 8:
        shared = lax.all_gather(sha, ("dp", "tensor"), axis=0)
        small = lax.all_gather(sma, ("dp", "tensor"), axis=0)
        return (
            lax.all_gather(tok, "tensor", axis=0),
            lax.all_gather(que, "dp", axis=0, tiled=True),
            lax.all_gather(att, "dp", axis=1, tiled=True),
            lax.all_gather(inn, "dp", axis=1, tiled=True),
            lax.all_gather(mam, "dp", axis=1, tiled=True),
            shared.reshape((nd, nt) + sha.shape),
            small.reshape((nd, nt) + sma.shape),
        )
    bf = jnp.bfloat16
    outs = (
        (nt,) + tok.shape,
        (nd * que.shape[0], que.shape[1]),
        (att.shape[0], nd * att.shape[1]),
        (2, nd * inn.shape[1], inn.shape[2]),
        (mam.shape[0], nd * mam.shape[1]),
        (nd, nt) + sha.shape,
        (nd, nt) + sma.shape,
    )
    anywhere = pl.BlockSpec(memory_space=pl.ANY)
    dma = pltpu.SemaphoreType.DMA
    return pl.pallas_call(
        partial(gather_kernel, nt),
        out_shape=[jax.ShapeDtypeStruct(s, bf) for s in outs],
        in_specs=[pl.BlockSpec(memory_space=pltpu.VMEM)] * 7,
        out_specs=[anywhere] * 7,
        scratch_shapes=[
            dma((7,)), dma((2, nt)), dma((2, nt)), dma((2, nt)), dma((2, nt)),
            dma((6, 7)), dma((6, 7)),
        ],
        compiler_params=pltpu.CompilerParams(collective_id=0, has_side_effects=True),
        name="gather_start",
    )(tok, que, att, inn, mam, sha, sma)


def pack_kernel(taps, gain, norms, staps, step, out, rows):
    heads = step.shape[0]
    f32 = jnp.float32
    rows[...] = jnp.zeros(rows.shape, f32)
    rows[0:2, 0:32] = norms[...].astype(f32)
    rows[0 : CONV + 1, 32:40] = staps[...].astype(f32)
    rows[0:heads, 40:48] = gain[...].astype(f32)
    for j in range(CONV + 1):
        rows[0:heads, 48 + 8 * j : 56 + 8 * j] = taps[j].astype(f32)
    rows[8 : 8 + heads, :] = step[...].astype(f32)
    out[...] = rows[...].astype(jnp.bfloat16)


def pack_small(taps, gain, norms, staps, step):
    vmem = pl.BlockSpec(memory_space=pltpu.VMEM)
    return pl.pallas_call(
        pack_kernel,
        in_specs=[vmem] * 5,
        out_specs=vmem,
        out_shape=jax.ShapeDtypeStruct((16, 128), jnp.bfloat16),
        scratch_shapes=[pltpu.VMEM((16, 128), jnp.float32)],
        name="pack_small",
    )(taps, gain, norms, staps, step)


def unpack_kernel(
    heads, where, scal, packed, first_o, second_o, gain_o, tapx_o, tapb_o, step_o, decay_o, bias_o, skip_o
):
    z = where[0]
    f32 = jnp.float32
    nd, nt = packed.shape[:2]
    tiles = [[packed[k, q].astype(f32) for q in range(nt)] for k in range(nd)]
    for k in range(nd):
        both = jnp.concatenate([tiles[k][q][0:8, 0:32] for q in range(nt)], axis=1)
        first_o[:, 128 * k : 128 * k + 128] = both[0:1]
        second_o[:, 128 * k : 128 * k + 128] = both[1:2]
        step_o[:, 128 * k : 128 * k + 128] = packed[k, z].astype(f32)[8:16, :].astype(jnp.bfloat16)
    half = nd // 2
    for k in range(2):
        tapb_o[:, 128 * k : 128 * k + 128] = jnp.concatenate(
            [tiles[half * k + i][q][0:8, 32:40] for i in range(half) for q in range(nt)], axis=1
        )
    own = [packed[k, z].astype(f32) for k in range(nd)]

    def by_head(lane):
        wide = jnp.concatenate([own[k][0:8, lane : lane + 8] for k in range(nd)], axis=1)
        return jnp.concatenate([wide[h : h + 1, :] for h in range(heads)], axis=1)

    gain_o[...] = by_head(40)
    tapx_o[...] = jnp.zeros(tapx_o.shape, f32)
    tapb_o[CONV + 1 :, :] = jnp.zeros((7 - CONV, tapb_o.shape[1]), f32)
    for j in range(CONV + 1):
        tapx_o[j : j + 1, :] = by_head(48 + 8 * j)
    sub = lax.broadcasted_iota(jnp.int32, (8, 128), 0)
    decay = jnp.zeros((8, 128), f32)
    bias = jnp.zeros((8, 128), f32)
    for h in range(heads):
        decay = jnp.where(sub == h, scal[0, h], decay)
        bias = jnp.where(sub == h, scal[1, h], bias)
        skip_o[:, SSM_DIM * h : SSM_DIM * (h + 1)] = jnp.full((1, SSM_DIM), scal[2, h], f32)
    decay_o[...] = jnp.where(sub < heads, -jnp.exp(decay), 0.0)
    bias_o[...] = bias


def unpack_small(heads, where, scal, packed, width):
    inner = heads * SSM_DIM
    vmem = pl.BlockSpec(memory_space=pltpu.VMEM)
    smem = pl.BlockSpec(memory_space=pltpu.SMEM)
    sds = jax.ShapeDtypeStruct
    f32 = jnp.float32
    shapes = [(1, width), (1, width), (1, inner), (8, inner), (8, 256)]
    return pl.pallas_call(
        partial(unpack_kernel, heads),
        in_specs=[smem, smem, vmem],
        out_specs=[vmem] * 9,
        out_shape=[sds(s, f32) for s in shapes]
        + [sds((8, width), jnp.bfloat16), sds((8, 128), f32), sds((8, 128), f32), sds((1, inner), f32)],
        name="unpack_small",
    )(where, scal, packed)


def pick(values, index, axis=0):
    return lax.dynamic_index_in_dim(values, index, axis, keepdims=False)


def add_low(left, right):
    return (left.astype(jnp.float32) + right.astype(jnp.float32)).astype(jnp.bfloat16)


def chain_scatter(parts, nt):
    z = lax.axis_index("tensor")
    right = left = None
    for t in range(nt - 1):
        to_right = pick(parts, jnp.clip(nt - 1 - t + z, 0, nt - 1))
        to_left = pick(parts, jnp.clip(t - (nt - 1) + z, 0, nt - 1))
        if t > 0:
            to_right = add_low(to_right, right)
            to_left = add_low(to_left, left)
        right = lax.ppermute(to_right, "tensor", [(i, i + 1) for i in range(t + 1)])
        left = lax.ppermute(
            to_left, "tensor", [(nt - 1 - i, nt - 2 - i) for i in range(t + 1)]
        )
    f32 = jnp.float32
    return pick(parts, z).astype(f32) + right.astype(f32) + left.astype(f32)


def cube_scatter(parts, nd, last=jnp.float32):
    return lax.psum_scatter(parts, "dp", scatter_dimension=0, tiled=False).astype(last)


F32, BF16 = jnp.float32, jnp.bfloat16
VMEM_LIMIT = 56 * 1024 * 1024


def dot_nn(a, b):
    return lax.dot_general(a, b, (((1,), (0,)), ((), ())), preferred_element_type=F32)


def dot_nt(a, b):
    return lax.dot_general(a, b, (((1,), (1,)), ((), ())), preferred_element_type=F32)


def dot_tn(a, b):
    return lax.dot_general(a, b, (((0,), (0,)), ((), ())), preferred_element_type=F32)


def sigmoid(v):
    return 1.0 / (1.0 + jnp.exp(-v))


def lanes_of(shape):
    return lax.broadcasted_iota(jnp.int32, shape, len(shape) - 1)


def turn(values, cosine, sine):
    lane = lanes_of(values.shape)
    other = jnp.where(
        lax.rem(lane, HEAD_SIZE) < HEAD_SIZE // 2,
        pltpu.roll(values, 128 - HEAD_SIZE // 2, 1),
        pltpu.roll(values, HEAD_SIZE // 2, 1),
    )
    return values * cosine + other * sine


def softplus(v):
    return jnp.maximum(v, 0.0) + jnp.log1p(jnp.exp(-jnp.abs(v)))


def running_sum(rows):
    lane = lanes_of(rows.shape)
    step = 1
    while step < rows.shape[1]:
        rows = rows + jnp.where(lane >= step, pltpu.roll(rows, step, 1), 0.0)
        step *= 2
    return rows


def running_sum_back(rows):
    lane = lanes_of(rows.shape)
    width = rows.shape[1]
    step = 1
    while step < width:
        rows = rows + jnp.where(lane < width - step, pltpu.roll(rows, width - step, 1), 0.0)
        step *= 2
    return rows


def stack_columns(rows_list):
    used = sum(r.shape[0] for r in rows_list)
    filler = jnp.zeros((128 - used, 128), F32)
    return jnp.concatenate(rows_list + [filler], axis=0).T


def widen(cols, base, heads):
    low = lanes_of((cols.shape[0], 128)) < SSM_DIM
    return jnp.concatenate(
        [
            jnp.where(low, cols[:, base + 2 * p : base + 2 * p + 1],
                      cols[:, base + 2 * p + 1 : base + 2 * p + 2])
            for p in range(heads // 2)
        ],
        axis=1,
    )


def conv_rows(ref, taps, first, rows):
    total = taps[CONV : CONV + 1, :] + taps[0:1, :] * ref[pl.ds(first, rows), :]
    for j in range(1, CONV):
        total = total + taps[j : j + 1, :] * ref[pl.ds(first + j, rows), :]
    return total


class FeedGather:
    def __init__(self, step, nt, hid, dwn, hid_f, dwn_f, hid_z, dwn_z, lsem, sems):
        self.step, self.nt = step, nt
        d = lax.axis_index("dp")
        z = lax.axis_index("tensor")
        self.d, self.z = d, z
        self.cube = CubeGather(
            [(hid, lambda s: hid_f.at[s, z]), (dwn, lambda s: dwn_f.at[s, z])], (0,), sems[0], sems[1], d, z
        )
        self.chains = [
            ChainGather(hid, hid_z, sems[2], sems[3], d, z, nt),
            ChainGather(dwn, dwn_z, sems[4], sems[5], d, z, nt),
        ]
        self.own = lambda: [
            pltpu.make_async_copy(hid, hid_f.at[d, z], lsem.at[0]),
            pltpu.make_async_copy(dwn, dwn_f.at[d, z], lsem.at[1]),
        ]

    def at(self, step, act):
        pl.when(self.step == step)(act)

    def begin(self):
        def act():
            greet([(p, self.z) for p in cube_peers(self.d)] + other_quarters(self.d, self.z, self.nt))
            for chain in self.chains:
                chain.start()
            for i in range(2):
                self.cube.start(i)
            for copy in self.own():
                copy.start()

        self.at(0, act)
    def middle(self):
        def near():
            for chain in self.chains:
                chain.hop(1)
            for i in range(2):
                self.cube.near(i)

        def far():
            for chain in self.chains:
                chain.hop(2)
            for i in range(2):
                self.cube.far(i)

        self.at(1, near)
        self.at(2, far)

    def end(self):
        def act():
            for chain in self.chains:
                chain.hop(3)
            self.cube.finish()
            for copy in self.own():
                copy.wait()
            for chain in self.chains:
                chain.drain()

        self.at(3, act)


def forward_kernel(heads, nt, feed, *refs):
    if feed:
        beside = FeedGather(
            pl.program_id(0), nt, *refs[14:16], *refs[29:33], refs[38], refs[39:45]
        )
        refs = refs[:14] + refs[16:29] + refs[33:38]
        beside.begin()
        forward_step(heads, beside.middle, *refs)
        beside.end()
    else:
        forward_step(heads, lambda: None, *refs)


def forward_step(
    heads, middle, kvh, tok, gain, wq, win, stp, wsh, cosine, sine, tapx, tapb, decay, bias, skip,
    a1_o, q_o, k_o, v_o, lse_o, o_o, x_o, z_o, b_o, y_o, t_o, s_o, sq_o,
    keys, vals, xs, bs, state,
):
    step = pl.program_id(0)
    rows = tok.shape[0]
    second = kvh[0] == 1

    @pl.when(step == 0)
    def _():
        xs[0:8, :] = jnp.zeros((8, xs.shape[1]), F32)
        bs[0:8, :] = jnp.zeros((8, bs.shape[1]), F32)
        state[...] = jnp.zeros(state.shape, F32)

    t = tok[...].astype(F32)
    r = lax.rsqrt(jnp.mean(t * t, axis=1, keepdims=True) + epsilon)
    a1 = (t * r * gain[...]).astype(BF16)
    a1_o[...] = a1
    q = turn(dot_nn(a1, wq[...]), cosine[...], sine[...]).astype(BF16)
    q_o[...] = q
    s = dot_nn(a1, wsh[...])
    low = lanes_of((rows, 128)) < HEAD_SIZE
    k = turn(s[:, :128], cosine[...], sine[...])
    v = s[:, 128:256]
    pick_own = low != second
    k2 = jnp.where(pick_own, k, pltpu.roll(k, 64, 1)).astype(BF16)
    v2 = jnp.where(pick_own, v, pltpu.roll(v, 64, 1))
    k_o[...] = k2
    v_o[...] = v2.astype(BF16)
    place = pl.ds(pl.multiple_of(step * rows, rows), rows)
    keys[place, :] = k2
    vals[:, place] = v2.T.astype(BF16)

    scale = HEAD_SIZE**-0.5

    def attend(blocks):
        n = blocks * rows
        shape = (rows, rows)
        allowed = lax.broadcasted_iota(jnp.int32, shape, 0) <= lanes_of(shape)
        parts = []
        for h in range(2):
            qh = jnp.where(low == (h == 0), q, jnp.zeros_like(q))
            sc = dot_nt(keys[0:n, :], qh) * scale
            last = jnp.where(allowed, sc[n - rows :, :], neg_large)
            sc = jnp.concatenate([sc[: n - rows, :], last], axis=0) if blocks > 1 else last
            top = jnp.max(sc, axis=0, keepdims=True)
            e = jnp.exp(sc - top)
            total = jnp.sum(e, axis=0, keepdims=True)
            lse_o[h : h + 1, :] = top + jnp.log(total)
            parts.append(dot_nn(vals[:, 0:n], e.astype(BF16)) / total)
        sub = lax.broadcasted_iota(jnp.int32, parts[0].shape, 0)
        o_o[...] = jnp.where(sub < HEAD_SIZE, parts[0], parts[1]).T.astype(BF16)

    for i in range(keys.shape[0] // rows):
        pl.when(step == i)(partial(attend, i + 1))

    middle()
    zr = dot_nn(a1, win[0])
    z_o[...] = zr
    xr = dot_nn(a1, win[1])
    x_o[...] = xr
    br = s[:, 256:]
    b_o[...] = br
    xs[8 : 8 + rows, :] = xr
    bs[8 : 8 + rows, :] = br
    u = conv_rows(xs, tapx, 5, rows)
    x = u * sigmoid(u)
    u = conv_rows(bs, tapb, 5, rows)
    bc = (u * sigmoid(u)).astype(BF16)
    xs[0:8, :] = xs[rows : rows + 8, :]
    bs[0:8, :] = bs[rows : rows + 8, :]
    tr = dot_nt(stp[...], a1)
    t_o[...] = tr
    n_state = bc.shape[1] // 2
    tri_shape = (block_len, block_len)
    lower = lax.broadcasted_iota(jnp.int32, tri_shape, 0) >= lanes_of(tri_shape)
    half = lanes_of(tri_shape) < SSM_DIM
    for c in range(rows // block_len):
        part = slice(c * block_len, (c + 1) * block_len)
        dt = softplus(tr[:, part] + bias[...])
        cum = running_sum(dt * decay[...])
        end = cum[:, block_len - 1 :]
        cols = stack_columns([cum, jnp.exp(cum), dt * jnp.exp(end - cum)])
        xc = x[part]
        x_low = xc.astype(BF16)
        b_low = bc[part, :n_state]
        c_low = bc[part, n_state:]
        cross = dot_nt(c_low, b_low)
        grow = widen(cols, 8, heads)
        y = dot_nn(c_low, state[...].astype(BF16)) * grow + skip[...] * xc
        inner = []
        for p in range(heads // 2):
            mats = []
            for h in (2 * p, 2 * p + 1):
                gap = jnp.where(lower, cols[:, h : h + 1] - cum[h : h + 1, :], neg_large)
                mats.append((cross * jnp.exp(gap) * dt[h : h + 1, :]).astype(BF16))
            xp = x_low[:, 128 * p : 128 * p + 128]
            zero = jnp.zeros_like(xp)
            both = jnp.concatenate([jnp.where(half, xp, zero), jnp.where(half, zero, xp)], axis=0)
            inner.append(dot_nn(jnp.concatenate(mats, axis=1), both))
        y = y + jnp.concatenate(inner, axis=1)
        y_o[part, :] = y
        s_o[c] = state[...]
        carried = (xc * widen(cols, 16, heads)).astype(BF16)
        state[...] = grow[block_len - 1 :, :] * state[...] + dot_tn(b_low, carried)
        zc = zr[part]
        w = y * (zc * sigmoid(zc))
        total = jnp.sum(w * w, axis=1, keepdims=True)
        sq_o[:, part] = jnp.broadcast_to(total, (block_len, 128)).T[0:8, :]


def mixers_forward(
    heads, nt, kvh, tok, gain, wq, win, stp, wsh, cosine, sine, tapx, tapb, decay, bias, skip, feed=()
):
    total, width = tok.shape
    rows = 256
    inner = heads * SSM_DIM
    pair = wsh.shape[1] - 256
    state = pair // 2
    chunks = rows // block_len

    def whole(v):
        return pl.BlockSpec(v.shape, lambda i: (0,) * v.ndim)

    def tall(n):
        return pl.BlockSpec((rows, n), lambda i: (i, 0))

    wide = pl.BlockSpec((8, rows), lambda i: (0, i))
    sds = jax.ShapeDtypeStruct
    more_in, more_out, more_shape, more_scratch, extra = [], [], [], [], {}
    if feed:
        nd = 8
        dma = pltpu.SemaphoreType.DMA
        more_in = [whole(v) for v in feed]
        more_out = [pl.BlockSpec(memory_space=pl.ANY)] * 4
        more_shape = [sds((nd, nt) + v.shape, BF16) for v in feed] + [sds((nt,) + v.shape, BF16) for v in feed]
        more_scratch = [dma((2,)), dma((2, 7)), dma((2, 7))] + [dma((2, nt - 1))] * 4
        extra = dict(collective_id=6, has_side_effects=True)
    return pl.pallas_call(
        partial(forward_kernel, heads, nt, bool(feed)),
        grid=(total // rows,),
        in_specs=[pl.BlockSpec(memory_space=pltpu.SMEM), tall(width), whole(gain), whole(wq), whole(win),
                  whole(stp), whole(wsh), tall(128), tall(128), whole(tapx), whole(tapb),
                  whole(decay), whole(bias), whole(skip)] + more_in,
        out_specs=[tall(width), tall(128), tall(128), tall(128), wide, tall(128), tall(inner),
                   tall(inner), tall(pair), tall(inner), wide,
                   pl.BlockSpec((chunks, state, inner), lambda i: (i, 0, 0)), wide] + more_out,
        out_shape=[sds((total, width), BF16), sds((total, 128), BF16), sds((total, 128), BF16),
                   sds((total, 128), BF16), sds((8, total), F32), sds((total, 128), BF16),
                   sds((total, inner), F32), sds((total, inner), F32), sds((total, pair), F32),
                   sds((total, inner), F32), sds((8, total), F32),
                   sds((total // block_len, state, inner), F32), sds((8, total), F32)] + more_shape,
        scratch_shapes=[pltpu.VMEM((total, 128), BF16), pltpu.VMEM((128, total), BF16),
                        pltpu.VMEM((rows + 8, inner), F32), pltpu.VMEM((rows + 8, pair), F32),
                        pltpu.VMEM((state, inner), F32)] + more_scratch,
        compiler_params=pltpu.CompilerParams(vmem_limit_bytes=VMEM_LIMIT, **extra),
        cost_estimate=pl.CostEstimate(flops=int(5e9), bytes_accessed=int(15e6), transcendentals=int(4e6)),
        name="mixers_forward",
    )(kvh, tok, gain, wq, win, stp, wsh, cosine, sine, tapx, tapb, decay, bias, skip, *feed)


def attend_back(step, kvh, q, k2, v2, lse, do, cosine, sine, cos_all, sin_all, dq_o, dkv_o, dk, dv):
    rows = q.shape[0]
    steps = k2.shape[0] // rows
    scale = HEAD_SIZE**-0.5
    low = lanes_of((rows, 128)) < HEAD_SIZE

    @pl.when(step == 0)
    def _():
        dk[...] = jnp.zeros(dk.shape, F32)
        dv[...] = jnp.zeros(dv.shape, F32)

    def back(blocks):
        n = blocks * rows
        shape = (rows, rows)
        allowed = lax.broadcasted_iota(jnp.int32, shape, 0) <= lanes_of(shape)
        qs, dos, ps, dss, dqs = [], [], [], [], []
        for h in range(2):
            mine = low == (h == 0)
            qh = jnp.where(mine, q[...], jnp.zeros_like(q[...]))
            doh = jnp.where(mine, do[...], jnp.zeros_like(do[...]))
            sc = dot_nt(k2[0:n, :], qh) * scale - lse[h : h + 1, :]
            last = jnp.where(allowed, sc[n - rows :, :], neg_large)
            sc = jnp.concatenate([sc[: n - rows, :], last], axis=0) if blocks > 1 else last
            p = jnp.exp(sc)
            dp = dot_nt(v2[0:n, :], doh)
            centre = jnp.sum(p * dp, axis=0, keepdims=True)
            ds = (p * (dp - centre)).astype(BF16)
            qs.append(qh)
            dos.append(doh)
            ps.append(p.astype(BF16))
            dss.append(ds)
            dqs.append(dot_tn(ds, k2[0:n, :]) * scale)
        dk[0:n, :] += dot_nn(jnp.concatenate(dss, axis=1), jnp.concatenate(qs, axis=0)) * scale
        dv[0:n, :] += dot_nn(jnp.concatenate(ps, axis=1), jnp.concatenate(dos, axis=0))
        dq_o[...] = turn(jnp.where(low, dqs[0], dqs[1]), cosine[...], -sine[...]).astype(BF16)

    for i in range(steps):
        pl.when(step == 2 * i)(partial(back, i + 1))

    @pl.when(step == 2 * steps - 1)
    def _():
        own = (lanes_of(dk.shape) < HEAD_SIZE) != (kvh[0] == 1)
        g = dk[...]
        g = turn(g + pltpu.roll(g, 64, 1), cos_all[...], -sin_all[...])
        dkv_o[:, 0:128] = jnp.where(own, g, 0.0).astype(BF16)
        g = dv[...]
        g = g + pltpu.roll(g, 64, 1)
        dkv_o[:, 128:256] = jnp.where(own, g, 0.0).astype(BF16)


def back_kernel(heads, channels, nt, feed, *refs):
    step = pl.program_id(0)
    if feed:
        d = lax.axis_index("dp")
        z = lax.axis_index("tensor")
        sums, raw, refs = refs[0], refs[1], refs[2:]
        feed_o, refs = refs[37], refs[:37] + refs[38:]
        (came, f_send, f_recv, held), box, refs = refs[44:48], refs[48:56], refs[:44]
        peers = cube_peers(d)
        square = SquareScatter(
            lambda i, j: (2 * i + j,), raw, box[:6], box[6], box[7], peers, dp_bits(d), z
        )
        sources = [sums.at[k] for k in range(nt - 2)] + [held]
        copies = [
            remote_copy(sources[k], came.at[k], f_send.at[k], f_recv.at[k], peer)
            for k, peer in enumerate(other_quarters(d, z, nt))
        ]

        @pl.when(step == 0)
        def _():
            greet([(p, z) for p in peers[1:]] + other_quarters(d, z, nt))
            for copy in copies[:-1]:
                copy.start()
            square.start()

        pl.when(step == 3)(square.middle)

        @pl.when(step == 4)
        def _():
            square.finish(held)
            copies[-1].start()

    attend_back(step, *refs[:10], *refs[27:29], *refs[37:39])
    scan_back(heads, channels, step, *refs[10:27], *refs[29:37], *refs[39:44])
    if feed:

        @pl.when(step == pl.num_programs(0) - 1)
        def _():
            total = None
            for k, copy in enumerate(copies):
                copy.wait()
                value = came[k].astype(F32)
                total = value if total is None else total + value
            feed_o[...] = total
            square.drain()


def scan_back(
    heads, channels, step, dm, y, zr, xr, xp, br, bp, trow, states, rsum, dots, gain, tapx, tapb, decay,
    bias, skip,
    dz_o, dx_o, db_o, dt_o, gx_o, gb_o, gm_o, gh_o,
    xs, bs, dxs, dbs, dstate,
):
    last_step = pl.num_programs(0) - 1
    first = step == last_step
    rows = block_len
    inner = heads * SSM_DIM
    n_state = br.shape[1] // 2

    @pl.when(step == 0)
    def _():
        dxs[rows : rows + 8, :] = jnp.zeros((8, inner), F32)
        dbs[rows : rows + 8, :] = jnp.zeros((8, 2 * n_state), F32)
        dstate[...] = jnp.zeros(dstate.shape, F32)
        gx_o[...] = jnp.zeros(gx_o.shape, F32)
        gb_o[...] = jnp.zeros(gb_o.shape, F32)
        gm_o[...] = jnp.zeros(gm_o.shape, F32)
        gh_o[...] = jnp.zeros(gh_o.shape, F32)

    xs[0:8, :] = jnp.where(first, 0.0, xp[...])
    bs[0:8, :] = jnp.where(first, 0.0, bp[...])
    xs[8 : 8 + rows, :] = xr[...]
    bs[8 : 8 + rows, :] = br[...]
    ux = conv_rows(xs, tapx, 5, rows)
    sx = sigmoid(ux)
    x = ux * sx
    ub = conv_rows(bs, tapb, 5, rows)
    sb = sigmoid(ub)
    bc = (ub * sb).astype(BF16)
    b_low, c_low = bc[:, :n_state], bc[:, n_state:]

    pre = trow[...] + bias[...]
    dt = softplus(pre)
    cum = running_sum(dt * decay[...])
    end = cum[:, rows - 1 :]
    fade = jnp.exp(end - cum)
    inv = lax.rsqrt(rsum[...] / channels + epsilon)
    cols = stack_columns(
        [cum, jnp.exp(cum), dt * fade, dt, inv, inv * inv * inv * dots[...] / channels]
    )
    r = cols[:, 32:33]
    kk = cols[:, 40:41]
    z = zr[...]
    sz = sigmoid(z)
    silu_z = z * sz
    yv = y[...]
    w = yv * silu_z
    dmv = dm[...]
    dw = r * gain[...] * dmv - w * kk
    gm_o[0:1, :] += jnp.sum(dmv * w * r, axis=0, keepdims=True)
    dy = dw * silu_z
    dz_o[...] = (dw * yv * sz * (1.0 + z * (1.0 - sz))).astype(BF16)
    gm_o[1:2, :] += jnp.sum(dy * x, axis=0, keepdims=True)

    grow = widen(cols, 8, heads)
    tail = widen(cols, 16, heads)
    dt_wide = widen(cols, 24, heads)
    x_low = x.astype(BF16)
    dy_low = dy.astype(BF16)
    state = states[0]
    state_low = state.astype(BF16)
    ds = dstate[...]
    ds_low = ds.astype(BF16)
    cross = dot_nt(b_low, c_low)
    shape = (rows, rows)
    upper = lax.broadcasted_iota(jnp.int32, shape, 0) <= lanes_of(shape)
    half = lanes_of(shape) < SSM_DIM
    lane = lanes_of(shape)
    dcross = jnp.zeros(shape, F32)
    col_sums = jnp.zeros(shape, F32)
    row_sums = []
    mids = []
    for p in range(heads // 2):
        span = slice(128 * p, 128 * p + 128)
        xpair, dypair = x_low[:, span], dy_low[:, span]
        zero = jnp.zeros_like(xpair)
        dys = (jnp.where(half, dypair, zero), jnp.where(half, zero, dypair))
        mats = []
        for k in range(2):
            h = 2 * p + k
            gap = jnp.where(upper, cum[h : h + 1, :] - cols[:, h : h + 1], neg_large)
            faded = jnp.exp(gap)
            mats.append((cross * faded).astype(BF16))
            t = dot_nt(xpair, dys[k]) * faded
            dt_col = cols[:, 24 + h : 25 + h]
            td = t * dt_col
            dcross = dcross + td
            row_sums.append(jnp.sum(td * cross, axis=0, keepdims=True))
            col = jnp.sum(t * cross, axis=1, keepdims=True)
            col_sums = jnp.where(lane == h, col, col_sums)
        mids.append(dot_nn(jnp.concatenate(mats, axis=1), jnp.concatenate(dys, axis=0)))
    mid = jnp.concatenate(mids, axis=1)
    row_sums = jnp.concatenate(row_sums + [jnp.zeros((8 - heads, rows), F32)], axis=0)
    col_sums = col_sums.T[0:8, :]

    dye = dy * grow
    dye_low = dye.astype(BF16)
    xd = x * tail
    xd_low = xd.astype(BF16)
    from_b = dot_nn(b_low, ds_low)
    through = dot_nn(c_low, state_low)
    dcross_low = dcross.astype(BF16)
    db = dot_nn(dcross_low, c_low) + dot_nt(xd_low, ds_low)
    dc = dot_tn(dcross_low, b_low) + dot_nt(dye_low, state_low)

    head_of = lax.broadcasted_iota(jnp.int32, (8, inner), 0)
    chan = lanes_of((8, inner)) // SSM_DIM
    ones = jnp.where(head_of == chan, 1.0, 0.0).astype(BF16)

    def by_head(v):
        high = v.astype(BF16)
        rest = (v - high.astype(F32)).astype(BF16)
        return dot_nt(ones, high) + dot_nt(ones, rest)

    grown = by_head(dye * through)
    ended = by_head(x * from_b)
    kept = jnp.sum(ds * state, axis=0, keepdims=True) * grow[rows - 1 :, :]
    kept = jnp.where(head_of == chan, kept, 0.0).sum(axis=1, keepdims=True)
    pulled = dt * fade * ended
    lane8 = lanes_of((8, rows))
    at_end = kept + jnp.sum(pulled, axis=1, keepdims=True)
    dcum = row_sums - dt * col_sums + grown - pulled + jnp.where(lane8 == rows - 1, at_end, 0.0)
    da = running_sum_back(dcum)
    ddt = col_sums + fade * ended + decay[...] * da
    dpre = ddt * sigmoid(pre)
    dt_o[...] = dpre
    gh_o[0:8, :] += da * dt * decay[...]
    gh_o[8:16, :] += dpre

    dstate[...] = grow[rows - 1 :, :] * ds + dot_tn(c_low, dye_low)
    dx = skip[...] * dy + dt_wide * mid + tail * from_b
    dux = dx * sx * (1.0 + ux * (1.0 - sx))
    dub = jnp.concatenate([db, dc], axis=1) * sb * (1.0 + ub * (1.0 - sb))
    for taps, src, d, buf, acc, out in (
        (tapx, xs, dux, dxs, gx_o, dx_o),
        (tapb, bs, dub, dbs, gb_o, db_o),
    ):
        buf[0:rows, :] = d
        total = taps[CONV - 1 : CONV, :] * d
        for j in range(CONV - 1):
            total = total + taps[j : j + 1, :] * buf[pl.ds(CONV - 1 - j, rows), :]
        out[...] = total.astype(BF16)
        for j in range(CONV):
            acc[j : j + 1, :] += jnp.sum(d * src[pl.ds(5 + j, rows), :], axis=0, keepdims=True)
        acc[CONV : CONV + 1, :] += jnp.sum(d, axis=0, keepdims=True)
        buf[rows : rows + 8, :] = d[0:8, :]


def mixers_back(
    heads, channels, nt, kvh, q, k2, v2, lse, do, cosine, sine, dm, y, zr, xr, br, trow, states, rsum, dots,
    gain, tapx, tapb, decay, bias, skip, feed=None,
):
    total, inner = y.shape
    pair = br.shape[1]
    rows = block_len
    steps = total // rows
    per = rows // 8
    q_rows = 2 * rows

    def whole(v):
        return pl.BlockSpec(v.shape, lambda i: (0,) * v.ndim)

    def tall(n):
        return pl.BlockSpec((rows, n), lambda i: (steps - 1 - i, 0))

    def before(n):
        return pl.BlockSpec((8, n), lambda i: (jnp.maximum((steps - 1 - i) * per - 1, 0), 0))

    wide = pl.BlockSpec((8, rows), lambda i: (0, steps - 1 - i))
    ask = pl.BlockSpec((q_rows, 128), lambda i: (i // 2, 0))
    sds = jax.ShapeDtypeStruct

    def fixed(*shape):
        return pl.BlockSpec(shape, lambda i: (0,) * len(shape))

    in_specs = [pl.BlockSpec(memory_space=pltpu.SMEM), ask, whole(k2), whole(v2),
                pl.BlockSpec((8, q_rows), lambda i: (0, i // 2)), ask, ask, ask, whole(cosine), whole(sine),
                tall(inner), tall(inner), tall(inner), tall(inner), before(inner), tall(pair),
                before(pair), wide, pl.BlockSpec((1, pair // 2, inner), lambda i: (steps - 1 - i, 0, 0)),
                wide, wide, whole(gain), whole(tapx), whole(tapb), whole(decay), whole(bias), whole(skip)]
    out_specs = [ask, fixed(total, 256), tall(inner), tall(inner), tall(pair), wide, fixed(8, inner),
                 fixed(8, pair), fixed(8, inner), fixed(16, rows)]
    out_shape = [sds((total, 128), BF16), sds((total, 256), BF16), sds((total, inner), BF16),
                 sds((total, inner), BF16), sds((total, pair), BF16), sds((8, total), F32),
                 sds((8, inner), F32), sds((8, pair), F32), sds((8, inner), F32), sds((16, rows), F32)]
    scratch = [pltpu.VMEM((total, 128), F32), pltpu.VMEM((total, 128), F32),
               pltpu.VMEM((rows + 8, inner), F32), pltpu.VMEM((rows + 8, pair), F32),
               pltpu.VMEM((rows + 8, inner), F32), pltpu.VMEM((rows + 8, pair), F32),
               pltpu.VMEM((pair // 2, inner), F32)]
    args = [kvh, q, k2, v2, lse, do, cosine, sine, cosine, sine, dm, y, zr, xr, xr, br, br, trow, states,
            rsum, dots, gain, tapx, tapb, decay, bias, skip]
    extra = {}
    if feed is not None:
        dma = pltpu.SemaphoreType.DMA
        piece = feed[0].shape[1:]
        args = list(feed) + args
        in_specs = [whole(v) for v in feed] + in_specs
        out_specs = out_specs + [fixed(*piece)]
        out_shape = out_shape + [sds(piece, F32)]
        scratch = scratch + [pltpu.VMEM((nt - 1,) + piece, BF16), dma((nt - 1,)), dma((nt - 1,)),
                             pltpu.VMEM(piece, BF16)] + square_scratch(*piece)
        extra = dict(collective_id=5, has_side_effects=True)
    return pl.pallas_call(
        partial(back_kernel, heads, channels, nt, feed is not None),
        grid=(steps,),
        in_specs=in_specs,
        out_specs=out_specs,
        out_shape=out_shape,
        scratch_shapes=scratch,
        compiler_params=pltpu.CompilerParams(vmem_limit_bytes=VMEM_LIMIT, **extra),
        cost_estimate=pl.CostEstimate(flops=int(6e9), bytes_accessed=int(18e6), transcendentals=int(7e6)),
        name="mixers_back",
    )(*args)


def whole_spec(v):
    return pl.BlockSpec(v.shape, lambda i: (0,) * v.ndim)


def feed_open(hid, gain, a2, a2t, acc, dacc):
    v = hid[...]
    f = lax.rsqrt(jnp.mean(v * v, axis=1, keepdims=True) + epsilon)
    low = (v * f * gain[...]).astype(BF16)
    a2[...] = low
    a2t[...] = low.T
    acc[...] = jnp.zeros(acc.shape, F32)
    dacc[...] = jnp.zeros(dacc.shape, F32)


def feed_tile(a2, cot, whid, wdown, acc, dacc):
    width = a2.shape[1]
    units = whid.shape[4]
    w_gate = whid[:, 0, 0].reshape(width, units)
    w_up = whid[:, 0, 1].reshape(width, units)
    w_down = jnp.concatenate([wdown[k, 0] for k in range(width // 128)], axis=1)
    g = dot_nn(a2[...], w_gate)
    u = dot_nn(a2[...], w_up)
    s = sigmoid(g)
    f_low = (g * s * u).astype(BF16)
    acc[...] += dot_nn(f_low, w_down)
    df = dot_nt(cot[...], w_down)
    du = (df * g * s).astype(BF16)
    dg = (df * u * s * (1.0 + g * (1.0 - s))).astype(BF16)
    dacc[...] += dot_nt(dg, w_gate) + dot_nt(du, w_up)
    return f_low, dg, du


def feed_close(hid, gain, cot, acc, dacc, out_o, dh_o, gg_o):
    v = hid[...]
    out_o[...] = (v + acc[...]).astype(BF16)
    f = lax.rsqrt(jnp.mean(v * v, axis=1, keepdims=True) + epsilon)
    dy = dacc[...]
    gg_o[...] = jnp.sum(dy * v * f, axis=0, keepdims=True)
    gdy = dy * gain[...]
    lean = jnp.sum(gdy * v, axis=1, keepdims=True) * (f * f * f / v.shape[1])
    dh = cot[...].astype(F32) + (f * gdy - v * lean)
    dh_o[...] = dh
    return dh.astype(BF16)


def feed_grads(a2t, cot, f_low, dg, du):
    blocks = a2t.shape[0] // 128
    values = []
    for grad in (dg, du):
        full = dot_nn(a2t[...], grad).astype(BF16)
        for cb in range(grad.shape[1] // 128):
            values.append(full[:, 128 * cb : 128 * cb + 128].reshape(blocks, 128, 128))
    full = dot_tn(f_low, cot[...]).astype(BF16)
    values.append(jnp.stack([full[:, 128 * k : 128 * k + 128] for k in range(blocks)]))
    return values


def piece_rows(part, units, quarter_units):
    rows = [
        (k * quarter_units + part * units + cb * 128, 128) for k in range(2) for cb in range(units // 128)
    ]
    return rows + [(2 * quarter_units + part * units, units)]


def feed_kernel(hid, gain, cot, whid, wdown, out_o, dh_o, dmix_o, gg_o, piece_o, a2, a2t, acc, dacc):
    step = pl.program_id(0)
    pl.when(step == 0)(lambda: feed_open(hid, gain, a2, a2t, acc, dacc))
    values = feed_grads(a2t, cot, *feed_tile(a2, cot, whid, wdown, acc, dacc))
    units = whid.shape[4]
    quarter_units = piece_o.shape[2] // 3
    tiles_per = quarter_units // units
    rows = piece_rows(lax.rem(step, tiles_per), units, quarter_units)
    for value, (row, n) in zip(values, rows):
        piece_o[:, step // tiles_per, pl.ds(pl.multiple_of(row, 128), n), :] = value

    @pl.when(step == pl.num_programs(0) - 1)
    def _():
        dmix_o[...] = feed_close(hid, gain, cot, acc, dacc, out_o, dh_o, gg_o)


def feed_forward(hid, gain, cot, whid, wdown):
    rows, width = hid.shape
    blocks, nt, _, depth, units = whid.shape
    tile = 256
    per = units // tile
    hid_spec = pl.BlockSpec((blocks, 1, 2, depth, tile), lambda i: (0, i // per, 0, 0, lax.rem(i, per)))
    down_spec = pl.BlockSpec((blocks, 1, tile, 128), lambda i: (0, i // per, lax.rem(i, per), 0))
    sds = jax.ShapeDtypeStruct
    piece = (blocks, nt, 3 * units, 128)

    def fixed(*shape):
        return pl.BlockSpec(shape, lambda i: (0,) * len(shape))

    return pl.pallas_call(
        feed_kernel,
        grid=(nt * per,),
        in_specs=[fixed(rows, width), fixed(1, width), fixed(rows, width), hid_spec, down_spec],
        out_specs=[fixed(rows, width), fixed(rows, width), fixed(rows, width), fixed(1, width),
                   fixed(*piece)],
        out_shape=[sds((rows, width), BF16), sds((rows, width), F32), sds((rows, width), BF16),
                   sds((1, width), F32), sds(piece, BF16)],
        scratch_shapes=[pltpu.VMEM((rows, width), BF16), pltpu.VMEM((width, rows), BF16),
                        pltpu.VMEM((rows, width), F32), pltpu.VMEM((rows, width), F32)],
        compiler_params=pltpu.CompilerParams(vmem_limit_bytes=VMEM_LIMIT),
        name="feed_forward",
    )(hid, gain, cot, whid, wdown)


def row_columns(rows_list, rows):
    return jnp.concatenate(
        [stack_columns([r[:, c : c + 128] for r in rows_list]) for c in range(0, rows, 128)], axis=0
    )


def down_rows(at, dq, dz, dx, dkv, db, drow, wq, win, stp, wsh):
    total = dot_nt(dq[at, :], wq[...]) + dot_nt(dz[at, :], win[0]) + dot_nt(dx[at, :], win[1])
    total = total + dot_nt(dkv[at, :], wsh[:, 0:256]) + dot_nt(db[at, :], wsh[:, 256:])
    return total + dot_tn(drow[:, at].astype(BF16), stp[...])


def down_kernel(dq, dz, dx, dkv, db, drow, wq, win, stp, wsh, part_o):
    every = slice(None)
    part_o[...] = down_rows(every, dq, dz, dx, dkv, db, drow, wq, win, stp, wsh).astype(BF16)


def down_parts(dq, dz, dx, dkv, db, drow, wq, win, stp, wsh):
    total, inner = dz.shape
    width = wq.shape[0]
    rows = 256

    def tall(v):
        return pl.BlockSpec((rows, v.shape[1]), lambda i: (i, 0))

    wide = pl.BlockSpec((8, rows), lambda i: (0, i))
    return pl.pallas_call(
        down_kernel,
        grid=(total // rows,),
        in_specs=[tall(dq), tall(dz), tall(dx), tall(dkv), tall(db), wide, whole_spec(wq), whole_spec(win),
                  whole_spec(stp), whole_spec(wsh)],
        out_specs=pl.BlockSpec((rows, width), lambda i: (i, 0)),
        out_shape=jax.ShapeDtypeStruct((total, width), BF16),
        compiler_params=pltpu.CompilerParams(vmem_limit_bytes=VMEM_LIMIT),
        cost_estimate=pl.CostEstimate(flops=int(3e9), bytes_accessed=int(8e6), transcendentals=0),
        name="down_parts",
    )(dq, dz, dx, dkv, db, drow, wq, win, stp, wsh)


def weight_columns(a, g, dq, dz, dx, dkv, db, ot, mt, put, put_shared):
    at = a.T
    inner = dz.shape[1]

    def by_rows(values, first):
        for j in range(values.shape[1] // 128):
            for k in range(2):
                put(k, first + 128 * j, values[128 * k : 128 * (k + 1), 128 * j : 128 * (j + 1)])

    def by_lanes(values, first):
        for k in range(2):
            put(k, first, values[:, 128 * k : 128 * (k + 1)])

    by_rows(dot_nn(at, dq[...]).astype(BF16), 0)
    by_lanes(dot_nn(ot[...], g).astype(BF16), 128)
    by_rows(dot_nn(at, dz[...]).astype(BF16), 256)
    by_rows(dot_nn(at, dx[...]).astype(BF16), 256 + inner)
    by_lanes(dot_nn(mt[...], g).astype(BF16), 256 + 2 * inner)
    for first, values in ((0, dot_nn(at, dkv[...]).astype(BF16)), (256, dot_nn(at, db[...]).astype(BF16))):
        for k in range(2):
            put_shared(k, first, values[128 * k : 128 * (k + 1)])


def weight_kernel(a1, dq, dz, dx, dkv, db, drow, o, m, dmix, piece_o, shared_o, step_o, ot, mt):
    @pl.when(pl.program_id(0) == 0)
    def _():
        ot[...] = o[...].T
        mt[...] = m[...].T

    step_o[...] = dot_nn(drow[...].astype(BF16), a1[...])

    def put(k, first, values):
        piece_o[k, first : first + values.shape[0], :] = values

    def put_shared(k, first, values):
        shared_o[k, :, first : first + values.shape[1]] = values

    weight_columns(a1[...], dmix[...], dq, dz, dx, dkv, db, ot, mt, put, put_shared)


def weight_pieces(a1, dq, dz, dx, dkv, db, drow, o, m, dmix):
    total, width = a1.shape
    inner = dz.shape[1]
    n = 256 + 3 * inner
    shared = 256 + db.shape[1]
    cols = pl.BlockSpec((total, 256), lambda i: (0, i))
    sds = jax.ShapeDtypeStruct
    args = (dq, dz, dx, dkv, db, drow, o, m)
    return pl.pallas_call(
        weight_kernel,
        grid=(width // 256,),
        in_specs=[cols] + [whole_spec(v) for v in args] + [cols],
        out_specs=[pl.BlockSpec((2, n, 128), lambda i: (i, 0, 0)),
                   pl.BlockSpec((2, 128, shared), lambda i: (i, 0, 0)),
                   pl.BlockSpec((8, 256), lambda i: (0, i))],
        out_shape=[sds((width // 128, n, 128), BF16), sds((width // 128, 128, shared), BF16),
                   sds((8, width), F32)],
        scratch_shapes=[pltpu.VMEM((128, total), BF16), pltpu.VMEM((inner, total), BF16)],
        compiler_params=pltpu.CompilerParams(vmem_limit_bytes=VMEM_LIMIT),
        cost_estimate=pl.CostEstimate(flops=int(4e9), bytes_accessed=int(12e6), transcendentals=0),
        name="weight_pieces",
    )(a1, *args, dmix)


class Exchange:
    def __init__(self, own, landed, send, recv, d, z, nt):
        self.own, self.landed, self.z, self.nt = own, landed, z, nt
        self.copies = [
            remote_copy(own, landed.at[k - 1], send.at[k - 1], recv.at[k - 1], peer)
            for k, peer in enumerate(other_quarters(d, z, nt), 1)
        ]

    def start(self):
        for copy in self.copies:
            copy.start()

    def wait(self):
        for copy in self.copies:
            copy.wait()

    def total(self):
        total = None
        for q in range(self.nt):
            value = jnp.where(self.z == q, self.own[...].astype(F32), 0.0)
            for k in range(1, self.nt):
                value = value + jnp.where(
                    lax.rem(self.z - k + self.nt, self.nt) == q, self.landed[k - 1].astype(F32), 0.0
                )
            total = value if total is None else total + value
        return total


class ChainScatter:
    def __init__(self, parts, bufs, landed, send, recv, d, z, nt):
        self.parts, self.bufs, self.landed = parts, bufs, landed
        self.send, self.recv = send, recv
        self.d, self.z, self.nt = d, z, nt

    def active(self, way, t):
        z, nt = self.z, self.nt
        if way == 0:
            return (z <= t) & (z < nt - 1)
        return (nt - 1 - z <= t) & (z > 0)

    def copy(self, way, t):
        dev = (self.d, self.z + 1 if way == 0 else self.z - 1)
        return remote_copy(
            self.bufs.at[way, t], self.landed.at[way, t], self.send.at[way, t], self.recv.at[way, t], dev
        )

    def arrives(self, way, t):
        z, nt = self.z, self.nt
        if way == 0:
            return (z >= 1) & (z - 1 <= t)
        return (z < nt - 1) & (nt - 2 - z <= t)

    def step(self, t):
        z, nt = self.z, self.nt
        for way in range(2):
            q = nt - 1 - t + z if way == 0 else t - (nt - 1) + z

            def run():
                value = self.parts[q]
                if t > 0:
                    came = self.arrives(way, t - 1)

                    @pl.when(came)
                    def _():
                        self.copy(way, t - 1).wait_recv()
                        total = value.astype(F32) + self.landed[way, t - 1].astype(F32)
                        self.bufs[way, t] = total.astype(BF16)

                    @pl.when(jnp.logical_not(came))
                    def _():
                        self.bufs[way, t] = value
                else:
                    self.bufs[way, t] = value
                self.copy(way, t).start()

            pl.when(self.active(way, t))(run)

    def finish(self, out):
        out[...] = self.parts[self.z].astype(F32)
        t = self.nt - 2
        for way in range(2):

            @pl.when(self.arrives(way, t))
            def _():
                self.copy(way, t).wait_recv()
                out[...] += self.landed[way, t].astype(F32)

    def drain(self):
        for way in range(2):
            for t in range(self.nt - 1):
                pl.when(self.active(way, t))(self.copy(way, t).wait_send)


def chain_scratch(nt, rows, width):
    dma = pltpu.SemaphoreType.DMA
    return [
        pltpu.VMEM((2, nt - 1, rows, width), BF16),
        pltpu.VMEM((2, nt - 1, rows, width), BF16),
        dma((2, nt - 1)),
        dma((2, nt - 1)),
    ]


def mix_scatter_kernel(channels, nt, feed, *refs):
    (o, y_in, gate_in, sq, gain, watt, wmam, tok), refs = refs[:8], refs[8:]
    if feed:
        (hid_z, dwn_z), refs = refs[2:4], refs[4:]
        (m_o, sq_o, hid_o, hid_f, dwn_f), refs = refs[:5], refs[5:]
        (lsem, f_send, f_recv), refs = refs[:3], refs[3:]
    else:
        (m_o, sq_o, hid_o), refs = refs[:3], refs[3:]
    (y, z_in, in_sem, sq_land, sq_send, sq_recv, parts, bufs, landed, c_send, c_recv) = refs
    d = lax.axis_index("dp")
    z = lax.axis_index("tensor")
    rows = tok.shape[0]

    def rows_of(q):
        return pl.ds(pl.multiple_of(q * rows, rows), rows)

    def load(q):
        at = rows_of(q)
        return [
            pltpu.make_async_copy(y_in.at[at], y.at[at], in_sem.at[0, q]),
            pltpu.make_async_copy(gate_in.at[at], z_in.at[at], in_sem.at[1, q]),
        ]

    first = jnp.where(z < nt // 2, nt - 1, 0)
    for k in range(nt):
        for copy in load(lax.rem(first + k, nt)):
            copy.start()
    peers = [(p, z) for p in cube_peers(d)] if feed else []
    greet(peers + other_quarters(d, z, nt))
    squares = Exchange(sq, sq_land, sq_send, sq_recv, d, z, nt)
    squares.start()
    n = 2 * (nt - 1)
    if feed:
        items = []
        for k in range(1, nt):
            q = lax.rem(z - k + nt, nt)
            items.append((hid_z.at[q], lambda s, q=q: hid_f.at[s, q]))
            items.append((dwn_z.at[q], lambda s, q=q: dwn_f.at[s, q]))
        cube = CubeGather(items, (0, 3, 4), f_send, f_recv, d, z)
        for i in range(n):
            cube.start(i)
        locals_ = []
        for i, (src, dst) in enumerate([(src, at(d)) for src, at in items]):
            locals_.append(pltpu.make_async_copy(src, dst, lsem.at[i]))
            locals_[-1].start()
    chain = ChainScatter(parts, bufs, landed, c_send, c_recv, d, z, nt)
    squares.wait()
    sq_o[...] = squares.total()

    def part(q):
        at = rows_of(q)
        for copy in load(q):
            copy.wait()
        total = sq_o[:, at]
        r = row_columns([lax.rsqrt(total / channels + epsilon)], rows)[:, 0:1]
        zv = z_in[at, :]
        m = (y[at, :] * (zv * sigmoid(zv)) * r * gain[...]).astype(BF16)
        m_o[at, :] = m
        parts[q] = (dot_nn(o[at, :], watt[...]) + dot_nn(m, wmam[...])).astype(BF16)

    part(first)
    chain.step(0)

    def rest(i, carry):
        part(lax.rem(first + 1 + i, nt))
        return carry

    lax.fori_loop(0, nt - 1, rest, 0)
    for t in range(1, nt - 1):
        chain.step(t)
        if feed and t == 1:
            for i in range(n):
                cube.near(i)
    if feed:
        for i in range(n):
            cube.far(i)
    chain.finish(hid_o)
    hid_o[...] += tok[...].astype(F32)
    chain.drain()
    if feed:
        cube.finish()
        for copy in locals_:
            copy.wait()


def mix_scatter(channels, nt, o, y, zr, sq, gain, watt, wmam, tok, feed=()):
    total, inner = y.shape
    rows, width = tok.shape
    dma = pltpu.SemaphoreType.DMA
    sds = jax.ShapeDtypeStruct
    vmem = pl.BlockSpec(memory_space=pltpu.VMEM)
    anywhere = pl.BlockSpec(memory_space=pl.ANY)
    outs = [sds((total, inner), BF16), sds((8, total), F32), sds((rows, width), F32)]
    scratch = []
    n = 2 * (nt - 1)
    if feed:
        for v in feed[:2]:
            outs.append(sds(v.shape, BF16))
        scratch = [dma((n,)), dma((n, 7)), dma((n, 7))]
    return pl.pallas_call(
        partial(mix_scatter_kernel, channels, nt, bool(feed)),
        in_specs=[vmem, anywhere, anywhere] + [vmem] * 5 + [anywhere] * len(feed[:2]) + [vmem] * len(feed[2:]),
        out_specs=[vmem] * 3 + [anywhere] * (len(outs) - 3),
        out_shape=outs,
        input_output_aliases={8: 3, 9: 4} if feed else {},
        scratch_shapes=scratch + [pltpu.VMEM((total, inner), F32), pltpu.VMEM((total, inner), F32),
                                  dma((2, nt)), pltpu.VMEM((nt - 1, 8, total), F32), dma((nt - 1,)), dma((nt - 1,)),
                        pltpu.VMEM((nt, rows, width), BF16)] + chain_scratch(nt, rows, width),
        compiler_params=pltpu.CompilerParams(
            vmem_limit_bytes=VMEM_LIMIT, collective_id=1, has_side_effects=True
        ),
        cost_estimate=pl.CostEstimate(flops=int(1e9), bytes_accessed=int(130e6), transcendentals=int(4e5)),
        name="mix_scatter",
    )(o, y, zr, sq, gain, watt, wmam, tok, *feed)


class ChainGather:
    def __init__(self, own, slots, send, recv, d, z, nt):
        self.own, self.slots, self.send, self.recv = own, slots, send, recv
        self.d, self.z, self.nt = d, z, nt

    def copy(self, way, dist):
        dev = (self.d, self.z + 1 if way == 0 else self.z - 1)
        slot = self.z - dist if way == 0 else self.z + dist
        src = self.own if dist == 0 else self.slots.at[slot]
        return remote_copy(src, self.slots.at[slot], self.send.at[way, dist], self.recv.at[way, dist], dev)

    def landing(self, way, dist):
        slot = self.z - dist if way == 0 else self.z + dist
        return remote_copy(
            self.slots.at[slot], self.slots.at[slot], self.send.at[way, dist - 1],
            self.recv.at[way, dist - 1], (self.d, self.z),
        )

    def has(self, way, dist):
        return self.z >= dist if way == 0 else self.z + dist < self.nt

    def goes_on(self, way):
        return self.z < self.nt - 1 if way == 0 else self.z > 0

    def start(self):
        for way in range(2):
            pl.when(self.goes_on(way))(self.copy(way, 0).start)

    def hop(self, dist):
        for way in range(2):
            pl.when(self.has(way, dist))(self.landing(way, dist).wait_recv)
            if dist < self.nt - 1:
                pl.when(self.has(way, dist) & self.goes_on(way))(self.copy(way, dist).start)

    def drain(self):
        for way in range(2):
            pl.when(self.goes_on(way))(self.copy(way, 0).wait_send)
            for dist in range(1, self.nt - 1):
                pl.when(self.has(way, dist) & self.goes_on(way))(self.copy(way, dist).wait_send)


class Unmix:
    def __init__(self, y, z_in, gain, watt, wmam, g_o, do_o, dm_o, dots, rows):
        self.ins = (y, z_in, gain, watt, wmam)
        self.outs = (g_o, do_o, dm_o, dots)
        self.rows = rows

    def __call__(self, q, g):
        y, z_in, gain, watt, wmam = self.ins
        g_o, do_o, dm_o, dots_o = self.outs
        rows = self.rows
        at = pl.ds(pl.multiple_of(q * rows, rows), rows)
        if g_o is not None:
            g_o[at, :] = g
        do_o[at, :] = dot_nt(g, watt[...]).astype(BF16)
        dm = dot_nt(g, wmam[...])
        dm_o[at, :] = dm
        zv = z_in[at, :]
        dots = jnp.sum(dm * gain[...] * (y[at, :] * (zv * sigmoid(zv))), axis=1, keepdims=True)
        turned = [jnp.broadcast_to(dots[c : c + 128], (128, 128)).T[0:8, :] for c in range(0, rows, 128)]
        dots_o[:, at] = jnp.concatenate(turned, axis=1)

    def around(self, z, dist, nt, slots, after=lambda q: None):
        def side(way, carry):
            q = jnp.where(way == 0, z - dist, z + dist)

            @pl.when((q >= 0) & (q < nt))
            def _():
                self(q, slots[q])
                after(q)

            return carry

        lax.fori_loop(0, 2, side, 0)


def unmix_gather_kernel(nt, *refs):
    (dmix, y, z_in, gain, watt, wmam), refs = refs[:6], refs[6:]
    (g_o, do_o, dm_o, dot_o), refs = refs[:4], refs[4:]
    (slots, g_send, g_recv, dot_own, dot_land, d_send, d_recv) = refs
    d = lax.axis_index("dp")
    z = lax.axis_index("tensor")
    greet(other_quarters(d, z, nt))
    chain = ChainGather(dmix, slots, g_send, g_recv, d, z, nt)
    chain.start()
    work = Unmix(y, z_in, gain, watt, wmam, g_o, do_o, dm_o, dot_own, dmix.shape[0])
    work(z, dmix[...])
    for dist in range(1, nt):
        chain.hop(dist)
        work.around(z, dist, nt, slots)
    dots = Exchange(dot_own, dot_land, d_send, d_recv, d, z, nt)
    dots.start()
    chain.drain()
    dots.wait()
    dot_o[...] = dots.total()


def unmix_shapes(total, width, inner):
    sds = jax.ShapeDtypeStruct
    return [sds((total, width), BF16), sds((total, 128), BF16), sds((total, inner), F32),
            sds((8, total), F32)]


def unmix_scratch(nt, rows, width, total):
    dma = pltpu.SemaphoreType.DMA
    return [pltpu.VMEM((nt, rows, width), BF16), dma((2, nt - 1)), dma((2, nt - 1)),
            pltpu.VMEM((8, total), F32), pltpu.VMEM((nt - 1, 8, total), F32), dma((nt - 1,)), dma((nt - 1,))]


def unmix_gather(nt, dmix, y, zr, gain, watt, wmam):
    total, inner = y.shape
    rows, width = dmix.shape
    vmem = pl.BlockSpec(memory_space=pltpu.VMEM)
    return pl.pallas_call(
        partial(unmix_gather_kernel, nt),
        in_specs=[vmem] * 6,
        out_specs=[vmem] * 4,
        out_shape=unmix_shapes(total, width, inner),
        scratch_shapes=unmix_scratch(nt, rows, width, total),
        compiler_params=pltpu.CompilerParams(
            vmem_limit_bytes=VMEM_LIMIT, collective_id=2, has_side_effects=True
        ),
        name="unmix_gather",
    )(dmix, y, zr, gain, watt, wmam)


BOXES = 4


def feed_unmix_kernel(nt, *refs):
    (hid, gain, cot, whid, wdown, y_in, gate_in, mgain, watt_in, wmam_in), refs = refs[:10], refs[10:]
    (out_o, dh_o, gg_o, g_o, do_o, dm_o, dot_o, own_o, raw_o, sum_o), refs = refs[:10], refs[10:]
    (y, z_in, watt, wmam, out, dh, dm, in_sem, out_sem, g_sem, dm_sem), refs = refs[:11], refs[11:]
    (a2, a2t, acc, dacc, fs, dgs, dus, dmix, piece, sent, came, b_send, b_recv), refs = refs[:13], refs[13:]
    boxes, refs = refs[: 8 * (nt - 2)], refs[8 * (nt - 2) :]
    (slots, g_send, g_recv, dot_own, dot_land, d_send, d_recv) = refs
    step = pl.program_id(0)
    tiles = pl.num_programs(0) // 2
    d = lax.axis_index("dp")
    z = lax.axis_index("tensor")
    core = lax.rem(d, 2)
    bits = dp_bits(d)
    peers = cube_peers(d)
    chain = ChainGather(dmix, slots, g_send, g_recv, d, z, nt)
    cubes = []
    for k in range(1, nt - 1):
        q = lax.rem(z + k, nt)
        box = boxes[8 * k - 8 : 8 * k]
        cubes.append(
            SquareScatter(lambda i, j, q=q: (2 * i + j, q), piece, box[:6], box[6], box[7], peers, bits, z)
        )

    rows = hid.shape[0]
    late = [
        pltpu.make_async_copy(src, dst, in_sem.at[i])
        for i, (src, dst) in enumerate(((y_in, y), (gate_in, z_in), (watt_in, watt), (wmam_in, wmam)))
    ]

    def rows_of(q):
        return pl.ds(pl.multiple_of(q * rows, rows), rows)

    def store_g(q):
        return pltpu.make_async_copy(slots.at[q], g_o.at[rows_of(q)], g_sem.at[q])

    def store_dm(q):
        return pltpu.make_async_copy(dm.at[rows_of(q)], dm_o.at[rows_of(q)], dm_sem.at[q])

    ready = [
        pltpu.make_async_copy(src, dst, out_sem.at[i])
        for i, (src, dst) in enumerate(
            (
                (out, out_o),
                (dh, dh_o),
                (dmix, g_o.at[rows_of(z)]),
                (piece.at[:, z], own_o),
                (piece.at[:, lax.rem(z + nt - 1, nt)], raw_o),
            )
        )
    ]

    @pl.when(step == 0)
    def _():
        for copy in late:
            copy.start()
        greet([(p, z) for p in peers] + other_quarters(d, z, nt))
        feed_open(hid, gain, a2, a2t, acc, dacc)

    @pl.when(step < tiles)
    def _():
        fs[step], dgs[step], dus[step] = feed_tile(a2, cot, whid, wdown, acc, dacc)

    @pl.when(step == tiles - 1)
    def _():
        dmix[...] = feed_close(hid, gain, cot, acc, dacc, out, dh, gg_o)
        chain.start()
        for copy in ready[:3]:
            copy.start()

    units = whid.shape[4]
    quarter_units = piece.shape[2] // 3
    tiles_per = quarter_units // units

    def swap(turn_):
        box = lax.rem(turn_, BOXES)
        return remote_copy(
            sent.at[box], came.at[box], b_send.at[box], b_recv.at[box], (peers[0], z)
        )

    def places(turn_):
        quarter = lax.rem(z + 1 + turn_ // tiles_per, nt)
        part = lax.rem(turn_, tiles_per)
        return quarter, part, piece_rows(part, units, quarter_units)

    def take(turn_):
        swap(turn_).wait_recv()
        quarter, _, rows = places(turn_)
        box = lax.rem(turn_, BOXES)
        first = 0
        for row, n in rows:
            at = pl.ds(pl.multiple_of(row, 128), n)
            piece[:, quarter, at, :] = add_refs(
                piece[:, quarter, at, :], came[box, :, first : first + n, :]
            ).astype(BF16)
            first += n

    @pl.when(step >= tiles)
    def _():
        turn_ = step - tiles
        quarter, part, rows = places(turn_)
        tile = quarter * tiles_per + part
        box = lax.rem(turn_, BOXES)
        pl.when(turn_ >= BOXES)(lambda: swap(turn_ - BOXES).wait_send())
        first = 0
        for value, (row, n) in zip(feed_grads(a2t, cot, fs[tile], dgs[tile], dus[tile]), rows):
            at = pl.ds(pl.multiple_of(row, 128), n)
            value = value.reshape(value.shape[0] // 2, 2, n, 128)
            even, odd = value[:, 0], value[:, 1]
            piece[:, quarter, at, :] = jnp.where(core == 0, even, odd)
            sent[box, :, first : first + n, :] = jnp.where(core == 0, odd, even)
            first += n
        swap(turn_).start()
        pl.when(turn_ >= 1)(lambda: take(turn_ - 1))
        for k in range(1, nt - 1):
            pl.when(turn_ == k * tiles_per)(cubes[k - 1].start)

    @pl.when(step == 2 * tiles - 1)
    def _():
        take(tiles - 1)
        for i in range(BOXES):
            swap(tiles - BOXES + i).wait_send()
        for copy in ready[3:]:
            copy.start()
        for copy in late:
            copy.wait()
        work = Unmix(y, z_in, mgain, watt, wmam, None, do_o, dm, dot_own, rows)
        work(z, dmix[...])
        store_dm(z).start()

        def after(q):
            store_g(q).start()
            store_dm(q).start()

        for dist in range(1, nt):
            chain.hop(dist)
            work.around(z, dist, nt, slots, after)
            if dist == 1:
                cubes[0].middle()
            if dist < nt - 2:
                cubes[dist].middle()
            elif dist == nt - 1:
                dots = Exchange(dot_own, dot_land, d_send, d_recv, d, z, nt)
                dots.start()
        for k, cube in enumerate(cubes):
            cube.finish(sum_o.at[k])
        chain.drain()
        for cube in cubes:
            cube.drain()
        dots.wait()
        dot_o[...] = dots.total()
        for copy in ready:
            copy.wait()
        for q in range(nt):
            store_dm(q).wait()
            pl.when(z != q)(store_g(q).wait)


def feed_unmix(nt, hid, gain, cot, whid, wdown, y, zr, mgain, watt, wmam):
    rows, width = hid.shape
    total, inner = y.shape
    blocks, _, _, depth, units = whid.shape
    tile = 256
    per = units // tile
    tiles = nt * per
    kept = blocks // 2
    n = 3 * units
    dma = pltpu.SemaphoreType.DMA
    sds = jax.ShapeDtypeStruct

    def fixed(v):
        return pl.BlockSpec(v.shape, lambda i: (0,) * len(v.shape), pipeline_mode=pl.Buffered(1))

    def at_tile(i):
        return jnp.minimum(i, tiles - 1)

    hid_spec = pl.BlockSpec(
        (blocks, 1, 2, depth, tile), lambda i: (0, at_tile(i) // per, 0, 0, lax.rem(at_tile(i), per))
    )
    down_spec = pl.BlockSpec(
        (blocks, 1, tile, 128), lambda i: (0, at_tile(i) // per, lax.rem(at_tile(i), per), 0)
    )
    out_shape = [sds((rows, width), BF16), sds((rows, width), F32), sds((1, width), F32)]
    out_shape += unmix_shapes(total, width, inner)
    out_shape += [sds((kept, n, 128), BF16), sds((kept, n, 128), BF16), sds((nt - 2, n, 128), BF16)]
    anywhere = pl.BlockSpec(memory_space=pl.ANY)
    late = [pltpu.VMEM(v.shape, v.dtype) for v in (y, zr, watt, wmam) + tuple(out_shape[:2])]
    late += [pltpu.VMEM((total, inner), F32), dma((4,)), dma((5,)), dma((nt,)), dma((nt,))]
    box = pltpu.VMEM((BOXES, kept, 3 * tile, 128), BF16)
    kept_tile = pltpu.VMEM((tiles, rows, tile), BF16)
    scratch = [pltpu.VMEM((rows, width), BF16), pltpu.VMEM((width, rows), BF16),
               pltpu.VMEM((rows, width), F32), pltpu.VMEM((rows, width), F32), kept_tile, kept_tile, kept_tile,
               pltpu.VMEM((rows, width), BF16), pltpu.VMEM((kept, nt, n, 128), BF16), box, box, dma((BOXES,)),
               dma((BOXES,))]
    for _ in range(nt - 2):
        scratch += square_scratch(n, 128)
    return pl.pallas_call(
        partial(feed_unmix_kernel, nt),
        grid=(2 * tiles,),
        in_specs=[fixed(hid), fixed(gain), fixed(cot), hid_spec, down_spec, anywhere, anywhere, fixed(mgain),
                  anywhere, anywhere],
        out_specs=[anywhere if i in (0, 1, 3, 5, 7, 8) else fixed(v) for i, v in enumerate(out_shape)],
        out_shape=out_shape,
        scratch_shapes=late + scratch + unmix_scratch(nt, rows, width, total),
        compiler_params=pltpu.CompilerParams(
            vmem_limit_bytes=60 * 1024 * 1024, collective_id=4, has_side_effects=True
        ),
        cost_estimate=pl.CostEstimate(flops=int(1e10), bytes_accessed=int(150e6), transcendentals=int(9e5)),
        name="feed_unmix",
    )(hid, gain, cot, whid, wdown, y, zr, mgain, watt, wmam)


def add_refs(left, right):
    return left.astype(F32) + right.astype(F32)


class SquareScatter:
    def __init__(self, place, held, bufs, send, recv, peers, bits, z):
        (self.r1, self.r2, self.ob, self.tb, self.r3, self.r4) = bufs
        self.place, self.held = place, held
        n = held.shape[-2]
        half = n // 2
        self.lo, self.hi = pl.ds(0, half), pl.ds(half, n - half)
        self.half = half
        _, self.x, self.y = bits
        x, y = self.x, self.y
        _, d_x, d_y = peers
        self.copies = []
        for i in range(2):
            self.copies.append(
                remote_copy(held.at[place(i, 1 - x) + (self.lo,)], self.r1.at[i], send.at[i], recv.at[i],
                            (d_x, z))
            )
        for j in range(2):
            self.copies.append(
                remote_copy(held.at[place(1 - y, j) + (self.hi,)], self.r2.at[j], send.at[2 + j],
                            recv.at[2 + j], (d_y, z))
            )
        self.copies.append(remote_copy(self.ob.at[1 - y], self.r3, send.at[4], recv.at[4], (d_y, z)))
        self.copies.append(remote_copy(self.tb.at[1 - x], self.r4, send.at[5], recv.at[5], (d_x, z)))

    def start(self):
        for copy in self.copies[:4]:
            copy.start()

    def middle(self):
        for i in range(2):
            self.copies[i].wait_recv()
            self.ob[i] = add_refs(self.held[self.place(i, self.x) + (self.lo,)], self.r1[i]).astype(BF16)
        self.copies[4].start()
        for j in range(2):
            self.copies[2 + j].wait_recv()
            self.tb[j] = add_refs(self.held[self.place(self.y, j) + (self.hi,)], self.r2[j]).astype(BF16)
        self.copies[5].start()

    def finish(self, out):
        self.copies[4].wait_recv()
        out[0 : self.half] = add_refs(self.ob[self.y], self.r3[...]).astype(out.dtype)
        self.copies[5].wait_recv()
        out[self.half :] = add_refs(self.tb[self.x], self.r4[...]).astype(out.dtype)

    def drain(self):
        for copy in self.copies:
            copy.wait_send()


def square_scratch(n, lanes):
    dma = pltpu.SemaphoreType.DMA
    half = n // 2
    return [
        pltpu.VMEM((2, half, lanes), BF16),
        pltpu.VMEM((2, n - half, lanes), BF16),
        pltpu.VMEM((2, half, lanes), BF16),
        pltpu.VMEM((2, n - half, lanes), BF16),
        pltpu.VMEM((half, lanes), BF16),
        pltpu.VMEM((n - half, lanes), BF16),
        dma((6,)),
        dma((6,)),
    ]


class CubeScatter:
    def __init__(self, pieces, bufs, peers, bits, z):
        (self.rc, self.held, send, recv) = bufs[:4]
        self.p = pieces
        self.core = bits[0]
        self.first = remote_copy(
            pieces.at[:, 1 - self.core], self.rc, send.at[0], recv.at[0], (peers[0], z)
        )
        self.square = SquareScatter(
            lambda i, j: (2 * i + j,), self.held, bufs[4:10], bufs[10], bufs[11], peers, bits, z
        )

    def start(self):
        self.first.start()

    def middle(self):
        self.first.wait_recv()
        for i in range(4):
            self.held[i] = add_refs(self.p[i, self.core], self.rc[i]).astype(BF16)
        self.square.start()

    def last(self):
        self.square.middle()

    def finish(self, out):
        self.square.finish(out)

    def drain(self):
        self.first.wait_send()
        self.square.drain()


def cube_scratch(n, lanes):
    dma = pltpu.SemaphoreType.DMA
    return [
        pltpu.VMEM((4, n, lanes), BF16),
        pltpu.VMEM((4, n, lanes), BF16),
        dma((1,)),
        dma((1,)),
    ] + square_scratch(n, lanes)


class CubeTotal:
    def __init__(self, held, landed, send, recv, peers, z):
        self.held, self.landed = held, landed
        self.copies = [
            remote_copy(held.at[i], landed.at[i], send.at[i], recv.at[i], (peer, z))
            for i, peer in enumerate(peers)
        ]

    def start(self, i):
        self.copies[i].start()

    def take(self, i):
        self.copies[i].wait_recv()
        self.held[i + 1] = self.held[i] + self.landed[i]

    def drain(self):
        for copy in self.copies:
            copy.wait_send()


def norm_back(dy, v, gain, dh):
    f = lax.rsqrt(jnp.mean(v * v, axis=1, keepdims=True) + epsilon)
    gdy = dy * gain
    lean = jnp.sum(gdy * v, axis=1, keepdims=True) * (f * f * f / v.shape[1])
    return dh + (f * gdy - v * lean)


SMALL_ALL = 32
SMALL_ROWS = 160


def tail_kernel(
    nt, tok_in, gain, dh_in, a1_in, dmix_in, o_in, m_in, dq, dz, dx, dkv, db, drow, wq, win, stp, wsh,
    gg, gtb, gtx, grows, gheads, own_in, rest_in,
    gt_o, mixed_o, fed_o, sh_o, small_o,
    feed_own, a1, o, m, dmix, feed_rest, tok, dh, lsem,
    da, gone, parts, pieces, shared, ot, mt, bufs, landed, c_send, c_recv, *rest,
):
    cube_a, rest = rest[:12], rest[12:]
    cube_b, rest = rest[:12], rest[12:]
    square_c, rest = rest[:8], rest[8:]
    (sh_sum, sh_land, sh_send, sh_recv) = rest[:4]
    (sm_held, sm_land, sm_send, sm_recv, all_own, all_land, all_send, all_recv) = rest[4:]
    d = lax.axis_index("dp")
    z = lax.axis_index("tensor")
    bits = dp_bits(d)
    peers = cube_peers(d)
    rows = tok.shape[0]
    late = [
        pltpu.make_async_copy(src, dst, lsem.at[i])
        for i, (src, dst) in enumerate(
            [(own_in, feed_own), (a1_in, a1), (o_in, o), (m_in, m), (dmix_in, dmix), (rest_in, feed_rest),
             (tok_in, tok), (dh_in, dh)]
        )
    ]
    for copy in late:
        copy.start()
    greet([(p, z) for p in peers] + other_quarters(d, z, nt))
    three = SquareScatter(
        lambda i, j: (i, j), feed_own, square_c[:6], square_c[6], square_c[7], peers, bits, z
    )
    chain = ChainScatter(parts, bufs, landed, c_send, c_recv, d, z, nt)

    def part(q):
        at = pl.ds(pl.multiple_of(q * rows, rows), rows)
        parts[q] = down_rows(at, dq, dz, dx, dkv, db, drow, wq, win, stp, wsh).astype(BF16)

    first = jnp.where(z < nt // 2, nt - 1, 0)
    part(first)
    chain.step(0)

    def others(i, carry):
        part(lax.rem(first + 1 + i, nt))
        return carry

    late[0].wait()
    three.start()
    lax.fori_loop(0, nt - 1, others, 0)
    for copy in late[1:5]:
        copy.wait()
    ot[...] = o[...].T
    mt[...] = m[...].T

    def columns(i, carry):
        at = pl.ds(pl.multiple_of(i * 256, 256), 256)

        def put(k, first, values):
            pieces[i, k, first : first + values.shape[0], :] = values

        def put_shared(k, first, values):
            shared[i, k, :, first : first + values.shape[1]] = values

        weight_columns(a1[:, at], dmix[:, at], dq, dz, dx, dkv, db, ot, mt, put, put_shared)
        return carry

    lax.fori_loop(0, 2, columns, 0)
    chain.step(1)
    lax.fori_loop(2, 4, columns, 0)
    gone[...] = jnp.zeros(gone.shape, F32)

    def gain_sums(q, carry):
        at = pl.ds(pl.multiple_of(q * rows, rows), rows)
        gone[...] += jnp.sum(parts[q].astype(F32) * a1[at, :].astype(F32), axis=0, keepdims=True)
        return carry

    lax.fori_loop(0, nt, gain_sums, 0)
    gone[...] = gone[...] / gain[...]
    one = CubeScatter(pieces, cube_a, peers, bits, z)
    two = CubeScatter(shared, cube_b, peers, bits, z)
    sums = CubeTotal(sm_held, sm_land, sm_send, sm_recv, peers, z)
    for k in range(8):
        sm_held[0, k : k + 1, :] = gg[:, 128 * k : 128 * k + 128]
        sm_held[0, 24 + k : 25 + k, :] = gone[:, 128 * k : 128 * k + 128]
    for first_row, ref in ((8, gtb), (SMALL_ALL, gtx), (56, grows)):
        for k in range(ref.shape[1] // 128):
            sm_held[0, first_row + 8 * k : first_row + 8 * k + 8, :] = ref[:, 128 * k : 128 * k + 128]
    sm_held[0, 80:96, :] = gheads[...]
    steps = dot_nn(drow[...].astype(BF16), a1[...])
    for k in range(8):
        sm_held[0, 96 + 8 * k : 104 + 8 * k, :] = steps[:, 128 * k : 128 * k + 128]
    sums.start(0)
    two.start()
    one.start()
    three.middle()
    sums.take(0)
    sums.start(1)
    two.middle()
    one.middle()
    sums.take(1)
    sums.start(2)
    for t in range(2, nt - 1):
        chain.step(t)
    sums.take(2)
    all_own[...] = sm_held[3, 0:SMALL_ALL, :]
    over_all = Exchange(all_own, all_land, all_send, all_recv, d, z, nt)
    over_all.start()
    three.finish(fed_o)
    for copy in late[5:]:
        copy.wait()
    fed_o[...] += feed_rest[...]
    two.last()
    one.last()
    two.finish(sh_sum)
    per = sh_sum.shape[0] // nt
    copies = []
    for k in range(1, nt):
        q = lax.rem(z + k, nt)
        at = pl.ds(pl.multiple_of(q * per, per), per)
        copies.append(
            remote_copy(sh_sum.at[at], sh_land.at[k - 1], sh_send.at[k - 1], sh_recv.at[k - 1], (d, q))
        )
        copies[-1].start()
    one.finish(mixed_o)
    small_o[...] = sm_held[3]
    over_all.wait()
    small_o[0:SMALL_ALL, :] = over_all.total()
    for copy in copies:
        copy.wait()
    total = sh_sum[pl.ds(pl.multiple_of(z * per, per), per), :].astype(F32)
    for k in range(nt - 1):
        total = total + sh_land[k].astype(F32)
    sh_o[...] = total
    chain.finish(da)
    gt_o[...] = norm_back(da[...], tok[...].astype(F32), gain[...], dh[...]).astype(BF16)
    for thing in (chain, one, two, three, sums):
        thing.drain()


def tail(nt, *args):
    tok, a1, dz = args[0], args[3], args[8]
    feed_own = args[-2]
    rows, width = tok.shape
    total = a1.shape[0]
    inner = dz.shape[1]
    n, lanes = 256 + 3 * inner, 128
    s_rows, s_lanes = 128, args[16].shape[1]
    f_rows = feed_own.shape[2]
    late = (len(args) - 2, 3, 5, 6, 4, len(args) - 1, 0, 2)
    dma = pltpu.SemaphoreType.DMA
    sds = jax.ShapeDtypeStruct
    vmem = pl.BlockSpec(memory_space=pltpu.VMEM)
    return pl.pallas_call(
        partial(tail_kernel, nt),
        in_specs=[pl.BlockSpec(memory_space=pl.ANY) if i in late else vmem for i in range(len(args))],
        out_specs=[vmem] * 5,
        out_shape=[sds((rows, width), BF16), sds((n, lanes), F32), sds((f_rows, 128), F32),
                   sds((s_rows // nt, s_lanes), F32), sds((SMALL_ROWS, 128), F32)],
        scratch_shapes=[pltpu.VMEM(args[i].shape, args[i].dtype) for i in late] + [dma((len(late),))]
        + [pltpu.VMEM((rows, width), F32), pltpu.VMEM((1, width), F32), pltpu.VMEM((nt, rows, width), BF16),
                        pltpu.VMEM((4, 2, n, lanes), BF16), pltpu.VMEM((4, 2, s_rows, s_lanes), BF16),
                        pltpu.VMEM((128, total), BF16), pltpu.VMEM((inner, total), BF16)]
        + chain_scratch(nt, rows, width)
        + cube_scratch(n, lanes) + cube_scratch(s_rows, s_lanes) + square_scratch(f_rows, 128)
        + [pltpu.VMEM((s_rows, s_lanes), BF16), pltpu.VMEM((nt - 1, s_rows // nt, s_lanes), BF16),
           dma((nt - 1,)), dma((nt - 1,)),
           pltpu.VMEM((4, SMALL_ROWS, 128), F32), pltpu.VMEM((3, SMALL_ROWS, 128), F32), dma((3,)), dma((3,)),
           pltpu.VMEM((SMALL_ALL, 128), F32), pltpu.VMEM((nt - 1, SMALL_ALL, 128), F32), dma((nt - 1,)),
           dma((nt - 1,))],
        compiler_params=pltpu.CompilerParams(
            vmem_limit_bytes=VMEM_LIMIT, collective_id=3, has_side_effects=True
        ),
        cost_estimate=pl.CostEstimate(flops=int(7e9), bytes_accessed=int(150e6), transcendentals=0),
        name="tail",
    )(*args)


def finish_kernel(
    heads, place, mixed, fed, small, *refs
):
    (que_o, att_o, inn_o, mam_o, hid_o, dwn_o, norms_o, taps_o, chan_o, gain_o, step_o) = refs[-17:-6]
    heads_o = refs[-6:-3]
    for src, dst in zip(refs[:3], refs[-3:]):
        dst[...] = src[...]
    d, p = place[0], place[1]
    block = que_o.shape[0]
    inner = mam_o.shape[0]
    first = 0
    for j in range(que_o.shape[1] // 128):
        que_o[:, 128 * j : 128 * j + 128] = mixed[first : first + block]
        first += block
    att_o[...] = mixed[first : first + att_o.shape[0]]
    first += att_o.shape[0]
    for i in range(2):
        for j in range(inner // 128):
            inn_o[i, :, 128 * j : 128 * j + 128] = mixed[first : first + block]
            first += block
    mam_o[...] = mixed[first : first + inner]
    first = 0
    for i in range(2):
        for j in range(hid_o.shape[2] // 128):
            hid_o[i, :, 128 * j : 128 * j + 128] = fed[first : first + block]
            first += block
    dwn_o[...] = fed[first:]

    def lanes_from(values, lane):
        return pltpu.roll(values, lax.rem(128 - lane, 128), 1)

    width = norms_o.shape[1]
    per = 128 // width
    for i, base in enumerate((24, 0)):
        row = jnp.broadcast_to(small[pl.ds(base + p // per, 1), :], (8, 128))
        row = lanes_from(row, lax.rem(p, per) * width)
        norms_o[i : i + 1, :] = row[0:1, 0:width]
    width = taps_o.shape[1]
    per = 128 // width
    row = small[pl.ds(pl.multiple_of(8 + 8 * (p // per), 8), 8), :]
    taps_o[...] = lanes_from(row, lax.rem(p, per) * width)[0 : CONV + 1, 0:width]
    width = gain_o.shape[1]
    sums = jnp.zeros((8, 128), F32)
    lane = lanes_of(sums.shape)
    sub = lax.broadcasted_iota(jnp.int32, sums.shape, 0)
    for b in range(heads // 2):
        rows = lanes_from(small[SMALL_ALL + 8 * b : SMALL_ALL + 8 * b + 8, :], d * width)
        raw = small[56 + 8 * b : 64 + 8 * b, :]
        gains = lanes_from(raw, d * width)
        for k in range(2):
            h = 2 * b + k
            at = slice(64 * k, 64 * k + width)
            chan_o[:, h, :] = rows[0 : CONV + 1, at]
            gain_o[h : h + 1, :] = gains[0:1, at]
            skip = jnp.sum(jnp.where(lane // SSM_DIM == k, raw[1:2, :], 0.0), axis=1, keepdims=True)
            sums = jnp.where((sub == h) & (lane == 2), skip, sums)
    for k in range(2):
        total = jnp.sum(small[80 + 8 * k : 88 + 8 * k, :], axis=1, keepdims=True)
        sums = jnp.where(lane == k, total, sums)
    sums = jnp.concatenate([sums, jnp.zeros((120, 128), F32)], axis=0).T
    for k in range(3):
        heads_o[k][...] = sums[k : k + 1, 0:heads]
    steps = small[pl.ds(pl.multiple_of(96 + 8 * d, 8), 8), :]
    step_o[...] = steps[0:heads, :]


def finish(heads, place, mixed, fed, small, shapes, passed):
    vmem = pl.BlockSpec(memory_space=pltpu.VMEM)
    sds = jax.ShapeDtypeStruct
    return pl.pallas_call(
        partial(finish_kernel, heads),
        in_specs=[pl.BlockSpec(memory_space=pltpu.SMEM)] + [vmem] * 6,
        out_specs=[vmem] * (len(shapes) + 6),
        out_shape=[sds(s, F32) for s in shapes] + [sds((1, heads), F32)] * 3
        + [sds(v.shape, v.dtype) for v in passed],
        compiler_params=pltpu.CompilerParams(vmem_limit_bytes=VMEM_LIMIT),
        name="finish",
    )(place, mixed, fed, small, *passed)


def rope_wide(length):
    half = HEAD_SIZE // 2
    inverse = rope_base ** (-np.arange(half) * (2.0 / HEAD_SIZE))
    angles = np.arange(length)[:, None] * inverse[None, :]
    c, s = np.cos(angles), np.sin(angles)
    return (
        jnp.asarray(np.concatenate([c, c, c, c], axis=1), F32),
        jnp.asarray(np.concatenate([-s, s, -s, s], axis=1), F32),
    )


def to_blocks(full, axis, nt):
    if axis == 1:
        two, width, cols = full.shape
        return full.reshape(2, 8, width // 8, nt, cols // nt).transpose(1, 3, 0, 2, 4)
    rows, width = full.shape
    return full.reshape(nt, rows // nt, 8, width // 8).transpose(2, 0, 1, 3)


def per_device(
    nd,
    nt,
    tokens,
    query_proj,
    attend_out,
    inner_proj,
    step_proj,
    mamba_out,
    hidden_proj,
    down_proj,
    channel_taps,
    mixer_gain,
    decay_log,
    step_bias,
    skip_weight,
    shared_proj,
    norm_gains,
    shared_taps,
    cotangent,
):
    tensor_index = lax.axis_index("tensor")
    d = lax.axis_index("dp")
    local_rows, width = tokens.shape
    group_rows = local_rows * nt
    heads = step_proj.shape[1]
    inner = heads * SSM_DIM
    channels = inner * nt
    units = down_proj.shape[0]
    feed = ()
    if nd == 8:
        small = pack_small(channel_taps, mixer_gain, norm_gains, shared_taps, step_proj.T)
        (tok_full, full_query, full_attend, full_inner, full_mamba, sha, sma) = gather_start(
            tokens, query_proj, attend_out, inner_proj, mamba_out, shared_proj, small, nd, nt
        )
        scal = jnp.stack([decay_log, step_bias, skip_weight]).astype(F32)
        where = tensor_index.astype(jnp.int32).reshape(1)
        (
            gain_first, gain_second, gain_mix, taps_x, taps_b, step_rows, decay, bias, skip,
        ) = unpack_small(heads, where, scal, sma, width)
        full_shared = sha.reshape(width, -1)
        feed = (hidden_proj, down_proj)
    else:
        small_parts = [channel_taps, mixer_gain, norm_gains, shared_taps, step_proj.T]
        flat = jnp.concatenate([p.reshape(-1) for p in small_parts])
        small_len = -(-flat.shape[0] // 2048) * 2048
        small = jnp.pad(flat, (0, small_len - flat.shape[0])).reshape(-1, 128)
        (tok_full, full_query, full_attend, full_inner, full_mamba, sha, sma) = gather_start(
            tokens, query_proj, attend_out, inner_proj, mamba_out, shared_proj, small, nd, nt
        )
        full_hidden = lax.all_gather(hidden_proj, "tensor", axis=2, tiled=True)
        full_hidden = to_blocks(lax.all_gather(full_hidden, "dp", axis=1, tiled=True), 1, nt)
        full_down = lax.all_gather(down_proj, "tensor", axis=0, tiled=True)
        full_down = to_blocks(lax.all_gather(full_down, "dp", axis=1, tiled=True), 0, nt)

        full_shared = sha.reshape(width, -1)
        sma = sma.reshape(nd, nt, small_len)

        def small_piece(index):
            start = sum(p.size for p in small_parts[:index])
            part = small_parts[index]
            return sma[:, :, start : start + part.size].reshape((nd, nt) + part.shape)

        taps_x = pick(small_piece(0), tensor_index, 1).transpose(1, 2, 0, 3).reshape(CONV + 1, inner)
        gain_mix = pick(small_piece(1), tensor_index, 1).transpose(1, 0, 2).reshape(1, inner)
        full_norms = small_piece(2).transpose(2, 0, 1, 3).reshape(2, width).astype(F32)
        taps_b = small_piece(3).transpose(2, 0, 1, 3).reshape(CONV + 1, -1)
        step_rows = pick(small_piece(4), tensor_index, 1).transpose(1, 0, 2).reshape(heads, width)
        step_rows = jnp.pad(step_rows, ((0, 8 - heads), (0, 0)))
        taps_x = jnp.pad(taps_x.astype(F32), ((0, 7 - CONV), (0, 0)))
        taps_b = jnp.pad(taps_b.astype(F32), ((0, 7 - CONV), (0, 0)))
        gain_mix = gain_mix.astype(F32)
        gain_first = full_norms[0:1]
        gain_second = full_norms[1:2]

        def head_rows(values):
            return jnp.pad(jnp.broadcast_to(values[:, None], (heads, 128)), ((0, 8 - heads), (0, 0)))

        decay = head_rows(-jnp.exp(decay_log.astype(F32)))
        bias = head_rows(step_bias.astype(F32))
        skip = jnp.repeat(skip_weight.astype(F32), SSM_DIM)[None, :]
    q_heads = query_proj.shape[1] // HEAD_SIZE
    kv_head = (tensor_index * q_heads // (QHEADS // KVHEADS)).astype(jnp.int32).reshape(1)
    cosine, sine = rope_wide(group_rows)

    (a1, q, k2, v2, lse, o, xr, zr, br, y, trow, states, squares, *feed) = mixers_forward(
        heads, nt, kv_head, tok_full.reshape(group_rows, width), gain_first, full_query, full_inner, step_rows,
        full_shared, cosine, sine, taps_x, taps_b, decay, bias, skip, feed,
    )
    mixed = mix_scatter(
        channels, nt, o, y, zr, squares, gain_mix, full_attend, full_mamba, tokens, tuple(feed)
    )
    m, squares, hidden = mixed[:3]
    if nd == 8:
        full_hidden, full_down = mixed[3:]
    if nd == 8:
        layer_out, dh, grad_gain_two, grad_mix, do, dm, dots, feed_own, feed_raw, feed_sums = feed_unmix(
            nt, hidden, gain_second, cotangent, full_hidden, full_down, y, zr, gain_mix, full_attend, full_mamba
        )
        feed_own = feed_own.reshape((2, 2) + feed_own.shape[1:])
    else:
        layer_out, dh, dmix, grad_gain_two, feed_pieces = feed_forward(
            hidden, gain_second, cotangent, full_hidden, full_down
        )
        grad_mix, do, dm, dots = unmix_gather(nt, dmix, y, zr, gain_mix, full_attend, full_mamba)
        hid_full = feed_pieces[:, :, : 2 * units].reshape(8, nt, 2, units // 128, width // 8, 128)
        hid_full = hid_full.transpose(2, 0, 4, 1, 3, 5).reshape(2, nd, width // nd, nt, units)
        hid_sum = cube_scatter(hid_full.transpose(1, 3, 0, 2, 4), nd, BF16)
        down_full = feed_pieces[:, :, 2 * units :].transpose(1, 2, 0, 3)
        down_full = down_full.reshape(nt, units, nd, width // nd)
        down_sum = cube_scatter(down_full.transpose(2, 0, 1, 3), nd, BF16)
        gradient_hidden = chain_scatter(hid_sum, nt)
        gradient_down = chain_scatter(down_sum, nt)

    back = mixers_back(
        heads, channels, nt, kv_head, q, k2, v2, lse, do, cosine, sine, dm, y, zr, xr, br, trow, states,
        squares, dots, gain_mix, taps_x, taps_b, decay, bias, skip,
        (feed_sums, feed_raw) if nd == 8 else None,
    )
    dq, dkv, dz, dx, db, drow, grad_tx, grad_tb, grad_rows, grad_heads = back[:10]
    if nd == 8:
        sums = tail(
            nt, tokens, gain_first, dh, a1, grad_mix, o, m, dq, dz, dx, dkv, db, drow, full_query, full_inner,
            step_rows, full_shared, grad_gain_two, grad_tb, grad_tx, grad_rows, grad_heads, feed_own, back[10],
        )
        gradient_tokens, mixed, fed, gradient_shared, small_sums = sums
        place = jnp.stack([d, d * nt + tensor_index]).astype(jnp.int32)
        shapes = [
            query_proj.shape, attend_out.shape, inner_proj.shape, mamba_out.shape, hidden_proj.shape,
            down_proj.shape, norm_gains.shape, shared_taps.shape, channel_taps.shape, mixer_gain.shape,
            step_proj.T.shape,
        ]
        (
            gradient_query,
            gradient_attend,
            gradient_inner,
            gradient_mamba,
            gradient_hidden,
            gradient_down,
            gradient_norms,
            gradient_taps,
            gradient_channel,
            gradient_mixer,
            gradient_step,
            gradient_decay,
            gradient_bias,
            gradient_skip,
            layer_out,
            gradient_tokens,
            gradient_shared,
        ) = finish(
            heads, place, mixed, fed, small_sums, shapes, (layer_out, gradient_tokens, gradient_shared)
        )
        return (
            layer_out,
            gradient_tokens,
            gradient_query,
            gradient_attend,
            gradient_inner,
            gradient_step.T,
            gradient_mamba,
            gradient_hidden,
            gradient_down,
            gradient_channel,
            gradient_mixer,
            gradient_decay.reshape(heads),
            gradient_bias.reshape(heads),
            gradient_skip.reshape(heads),
            gradient_shared,
            gradient_norms,
            gradient_taps,
        )

    part_one = down_parts(dq, dz, dx, dkv, db, drow, full_query, full_inner, step_rows, full_shared)
    pieces, shared_pieces, grad_step = weight_pieces(a1, dq, dz, dx, dkv, db, drow, o, m, grad_mix)
    block = width // nd
    q_cols = query_proj.shape[1]
    cuts = [0, q_cols, q_cols + attend_out.shape[0]]
    cuts += [cuts[2] + inner, cuts[2] + 2 * inner, cuts[2] + 3 * inner]

    def from_rows(values):
        return values.reshape(8, -1, 128, 128).transpose(0, 2, 1, 3).reshape(width, -1)

    def from_lanes(values):
        return values.transpose(1, 0, 2).reshape(-1, width)

    n_tap = CONV + 1
    over_all = jnp.concatenate([grad_gain_two.reshape(-1), grad_tb[:n_tap].reshape(-1)])
    over_dp = jnp.concatenate(
        [
            grad_tx[:n_tap].reshape(-1),
            grad_rows[0],
            grad_rows[1].reshape(heads, SSM_DIM).sum(axis=1),
            grad_heads[:heads].sum(axis=1),
            grad_heads[8 : 8 + heads].sum(axis=1),
            grad_step[:heads].reshape(-1),
        ]
    )

    def in_rows(values):
        return jnp.pad(values, (0, -values.shape[0] % 1024)).reshape(-1, 128)

    rows_all = in_rows(over_all)
    n_all = rows_all.shape[0]
    small_sums = jnp.concatenate([rows_all, in_rows(over_dp)], axis=0)
    parts = part_one.reshape(nt, local_rows, width)
    token_f32 = tokens.astype(F32)
    _, norm_one_back = jax.vjp(norm_apply, token_f32, gain_first[0])
    grad_from_one, grad_gain_one = norm_one_back(chain_scatter(parts, nt))
    gradient_tokens = (dh + grad_from_one).astype(BF16)
    got = [pieces[:, cuts[i] : cuts[i + 1]] for i in range(5)]

    def over_rows(values):
        return cube_scatter(from_rows(values).reshape(nd, block, -1), nd)

    def over_lanes(values):
        return cube_scatter(from_lanes(values).reshape(-1, nd, block).transpose(1, 0, 2), nd)

    gradient_query = over_rows(got[0])
    gradient_attend = over_lanes(got[1])
    gradient_inner = jnp.stack([over_rows(got[2]), over_rows(got[3])])
    gradient_mamba = over_lanes(got[4])
    shared_cut = shared_pieces.reshape(nd, nt, width // (nd * nt), -1)
    gradient_shared = chain_scatter(cube_scatter(shared_cut, nd, BF16), nt)
    small_sums = lax.psum(small_sums, "dp")
    small_sums = jnp.concatenate(
        [lax.psum(small_sums[:n_all], "tensor"), small_sums[n_all:]], axis=0
    )
    grad_gain_one = lax.psum(grad_gain_one, ("dp", "tensor")).reshape(1, width)
    over_all = small_sums[:n_all].reshape(-1)
    over_dp = small_sums[n_all:].reshape(-1)
    place = d * nt + tensor_index
    norm_w = width // (nd * nt)
    both_norms = jnp.concatenate([grad_gain_one, over_all[:width].reshape(1, width)], axis=0)
    gradient_norms = lax.dynamic_slice_in_dim(both_norms, place * norm_w, norm_w, 1)
    tap_w = shared_taps.shape[1]
    tap_all = over_all[width : width + n_tap * taps_b.shape[1]].reshape(n_tap, -1)
    gradient_taps = lax.dynamic_slice_in_dim(tap_all, place * tap_w, tap_w, 1)
    part = mixer_gain.shape[1]
    n_taps = n_tap * inner
    chan = over_dp[:n_taps].reshape(n_tap, heads, SSM_DIM)
    gain = over_dp[n_taps : n_taps + inner].reshape(heads, SSM_DIM)
    gradient_channel = lax.dynamic_slice_in_dim(chan, d * part, part, 2)
    gradient_mixer = lax.dynamic_slice_in_dim(gain, d * part, part, 1)
    rest = over_dp[n_taps + inner :]
    gradient_skip = rest[:heads]
    gradient_decay = rest[heads : 2 * heads]
    gradient_bias = rest[2 * heads : 3 * heads]
    step_all = rest[3 * heads : 3 * heads + heads * width].reshape(heads, width)
    gradient_step = lax.dynamic_slice_in_dim(step_all, d * block, block, 1).T
    return (
        layer_out,
        gradient_tokens,
        gradient_query,
        gradient_attend,
        gradient_inner,
        gradient_step,
        gradient_mamba,
        gradient_hidden,
        gradient_down,
        gradient_channel,
        gradient_mixer,
        gradient_decay,
        gradient_bias,
        gradient_skip,
        gradient_shared,
        gradient_norms,
        gradient_taps,
    )


def solution(mesh):
    placed = (
        P(("dp", "tensor"), None),
        P("dp", "tensor"),
        P("tensor", "dp"),
        P(None, "dp", "tensor"),
        P("dp", "tensor"),
        P("tensor", "dp"),
        P(None, "dp", "tensor"),
        P("tensor", "dp"),
        P(None, "tensor", "dp"),
        P("tensor", "dp"),
        P("tensor"),
        P("tensor"),
        P("tensor"),
        P(("dp", "tensor"), None),
        P(None, ("dp", "tensor")),
        P(None, ("dp", "tensor")),
        P(("dp", "tensor"), None),
    )
    return jax.shard_map(
        partial(per_device, mesh.shape["dp"], mesh.shape["tensor"]),
        mesh=mesh,
        in_specs=placed,
        out_specs=(
            P(("dp", "tensor"), None),
            P(("dp", "tensor"), None),
            P("dp", "tensor"),
            P("tensor", "dp"),
            P(None, "dp", "tensor"),
            P("dp", "tensor"),
            P("tensor", "dp"),
            P(None, "dp", "tensor"),
            P("tensor", "dp"),
            P(None, "tensor", "dp"),
            P("tensor", "dp"),
            P("tensor"),
            P("tensor"),
            P("tensor"),
            P(("dp", "tensor"), None),
            P(None, ("dp", "tensor")),
            P(None, ("dp", "tensor")),
        ),
        check_vma=False,
    )
```

```python
from functools import partial

import numpy as np
import jax
import jax.numpy as jnp
from jax import lax
from jax.experimental import pallas as pl
from jax.experimental.pallas import tpu as pltpu
from jax.sharding import PartitionSpec as P

MESH = pl.DeviceIdType.MESH

QHEADS = 8
KVHEADS = 2
HEAD_SIZE = 64
SSM_DIM = 64
CONV = 4


epsilon = 1e-05
rope_base = 100000000000.0
neg_large = -1e30
block_len = 128


def norm_apply(values, gain):
    factor = lax.rsqrt(jnp.mean(values * values, axis=-1, keepdims=True) + epsilon)
    return values * factor * gain


def dp_bits(index):
    core = lax.rem(index, 2)
    xbit = lax.rem(index // 2, 2)
    ybit = lax.rem(index // 4, 2)
    return core, xbit, ybit


def remote_copy(src, dst, send, recv, dev):
    return pltpu.make_async_remote_copy(
        src_ref=src, dst_ref=dst, send_sem=send, recv_sem=recv, device_id=dev, device_id_type=MESH
    )


def greet(peers):
    barrier = pltpu.get_barrier_semaphore()
    for peer in peers:
        pl.semaphore_signal(barrier, inc=1, device_id=peer, device_id_type=MESH)
    pl.semaphore_wait(barrier, len(peers))


def other_quarters(d, z, nt):
    return [(d, lax.rem(z + k, nt)) for k in range(1, nt)]


def cube_peers(d):
    core, xbit, ybit = dp_bits(d)
    return d + 1 - 2 * core, d + 2 - 4 * xbit, d + 4 - 8 * ybit


class CubeGather:
    def __init__(self, items, via_y, send, recv, d, z):
        self.items, self.via_y, self.send, self.recv = items, via_y, send, recv
        self.d, self.z = d, z
        self.d_core, self.d_x, self.d_y = cube_peers(d)
        self.d_xy = self.d_x + self.d_y - d
        self.sent = []

    def push(self, i, j, src, dst, peer):
        def make():
            return remote_copy(src(), dst(), self.send.at[i, j], self.recv.at[i, j], (peer, self.z))

        make().start()
        self.sent.append(make)

    def landed(self, i, j, slot):
        at = self.items[i][1]
        remote_copy(
            at(slot), at(slot), self.send.at[i, j], self.recv.at[i, j], (self.d_core, self.z)
        ).wait_recv()

    def start(self, i):
        src, at = self.items[i]
        for j, peer in enumerate((self.d_x, self.d_y, self.d_core)):
            self.push(i, j, lambda: src, lambda: at(self.d), peer)

    def near(self, i):
        d_x, d_y, d_core = self.d_x, self.d_y, self.d_core
        self.landed(i, 0, d_x)
        if i in self.via_y:
            self.hand_on(i, 3, d_x, d_y)
        self.hand_on(i, 4, d_x, d_core)
        self.landed(i, 1, d_y)
        if i not in self.via_y:
            self.hand_on(i, 3, d_y, d_x)
        self.hand_on(i, 5, d_y, d_core)

    def hand_on(self, i, j, slot, peer):
        at = self.items[i][1]
        self.push(i, j, lambda: at(slot), lambda: at(slot), peer)

    def far(self, i):
        self.landed(i, 3, self.d_xy)
        self.hand_on(i, 6, self.d_xy, self.d_core)

    def finish(self):
        for i in range(len(self.items)):
            self.landed(i, 2, self.d_core)
            for j in (4, 5, 6):
                self.landed(i, j, self.d_core)
        for make in self.sent:
            make().wait_send()


def gather_kernel(nt, *refs):
    (tok, que, att, inn, mam, sha, sma) = refs[:7]
    (tok_f, que_f, att_f, inn_f, mam_f, sha_f, sma_f) = refs[7:14]
    (lsem, zs_send, zs_recv, t_send, t_recv, d_send, d_recv) = refs[14:]
    d = lax.axis_index("dp")
    z = lax.axis_index("tensor")
    greet([(p, z) for p in cube_peers(d)] + other_quarters(d, z, nt))

    small = []
    for i, (src, dst) in enumerate(((sha, sha_f), (sma, sma_f))):
        for k, peer in enumerate(other_quarters(d, z, nt)):
            small.append(remote_copy(src, dst.at[d, z], zs_send.at[i, k], zs_recv.at[i, k], peer))
            small[-1].start()
    q_rows = que.shape[0]
    cols = att.shape[1]
    i_rows = inn.shape[1]
    items = [
        (inn, lambda s: inn_f.at[:, pl.ds(s * i_rows, i_rows)]),
        (que, lambda s: que_f.at[pl.ds(s * q_rows, q_rows)]),
        (att, lambda s: att_f.at[:, pl.ds(pl.multiple_of(s * cols, cols), cols)]),
        (mam, lambda s: mam_f.at[:, pl.ds(pl.multiple_of(s * cols, cols), cols)]),
        (sha_f.at[d], lambda s: sha_f.at[s]),
        (sma_f.at[d], lambda s: sma_f.at[s]),
    ]
    cube = CubeGather(items, (0, 5), d_send, d_recv, d, z)
    locals_ = []
    for i, (src, dst) in enumerate(
        [(sha, sha_f.at[d, z]), (sma, sma_f.at[d, z]), (tok, tok_f.at[z])]
        + [(src, at(d)) for src, at in items[:4]]
    ):
        copy = pltpu.make_async_copy(src, dst, lsem.at[i])
        copy.start()
        locals_.append(copy)
    for i in range(4):
        cube.start(i)
    chain = ChainGather(tok, tok_f, t_send, t_recv, d, z, nt)
    chain.start()
    locals_[0].wait()
    locals_[1].wait()
    for copy in small:
        copy.wait()
    cube.start(4)
    cube.start(5)
    for i in range(4):
        cube.near(i)
    chain.hop(1)
    for i in (4, 5):
        cube.near(i)
    for i in range(6):
        cube.far(i)
    for dist in range(2, nt):
        chain.hop(dist)
    cube.finish()
    for copy in locals_[2:]:
        copy.wait()
    chain.drain()


def gather_start(tok, que, att, inn, mam, sha, sma, nd, nt):
    if nd != 8:
        shared = lax.all_gather(sha, ("dp", "tensor"), axis=0)
        small = lax.all_gather(sma, ("dp", "tensor"), axis=0)
        return (
            lax.all_gather(tok, "tensor", axis=0),
            lax.all_gather(que, "dp", axis=0, tiled=True),
            lax.all_gather(att, "dp", axis=1, tiled=True),
            lax.all_gather(inn, "dp", axis=1, tiled=True),
            lax.all_gather(mam, "dp", axis=1, tiled=True),
            shared.reshape((nd, nt) + sha.shape),
            small.reshape((nd, nt) + sma.shape),
        )
    bf = jnp.bfloat16
    outs = (
        (nt,) + tok.shape,
        (nd * que.shape[0], que.shape[1]),
        (att.shape[0], nd * att.shape[1]),
        (2, nd * inn.shape[1], inn.shape[2]),
        (mam.shape[0], nd * mam.shape[1]),
        (nd, nt) + sha.shape,
        (nd, nt) + sma.shape,
    )
    anywhere = pl.BlockSpec(memory_space=pl.ANY)
    dma = pltpu.SemaphoreType.DMA
    return pl.pallas_call(
        partial(gather_kernel, nt),
        out_shape=[jax.ShapeDtypeStruct(s, bf) for s in outs],
        in_specs=[pl.BlockSpec(memory_space=pltpu.VMEM)] * 7,
        out_specs=[anywhere] * 7,
        scratch_shapes=[
            dma((7,)), dma((2, nt)), dma((2, nt)), dma((2, nt)), dma((2, nt)),
            dma((6, 7)), dma((6, 7)),
        ],
        compiler_params=pltpu.CompilerParams(collective_id=0, has_side_effects=True),
        name="gather_start",
    )(tok, que, att, inn, mam, sha, sma)


def pack_kernel(taps, gain, norms, staps, step, out, rows):
    heads = step.shape[0]
    f32 = jnp.float32
    rows[...] = jnp.zeros(rows.shape, f32)
    rows[0:2, 0:32] = norms[...].astype(f32)
    rows[0 : CONV + 1, 32:40] = staps[...].astype(f32)
    rows[0:heads, 40:48] = gain[...].astype(f32)
    for j in range(CONV + 1):
        rows[0:heads, 48 + 8 * j : 56 + 8 * j] = taps[j].astype(f32)
    rows[8 : 8 + heads, :] = step[...].astype(f32)
    out[...] = rows[...].astype(jnp.bfloat16)


def pack_small(taps, gain, norms, staps, step):
    vmem = pl.BlockSpec(memory_space=pltpu.VMEM)
    return pl.pallas_call(
        pack_kernel,
        in_specs=[vmem] * 5,
        out_specs=vmem,
        out_shape=jax.ShapeDtypeStruct((16, 128), jnp.bfloat16),
        scratch_shapes=[pltpu.VMEM((16, 128), jnp.float32)],
        name="pack_small",
    )(taps, gain, norms, staps, step)


def unpack_kernel(
    heads, where, scal, packed, first_o, second_o, gain_o, tapx_o, tapb_o, step_o, decay_o, bias_o, skip_o
):
    z = where[0]
    f32 = jnp.float32
    nd, nt = packed.shape[:2]
    tiles = [[packed[k, q].astype(f32) for q in range(nt)] for k in range(nd)]
    for k in range(nd):
        both = jnp.concatenate([tiles[k][q][0:8, 0:32] for q in range(nt)], axis=1)
        first_o[:, 128 * k : 128 * k + 128] = both[0:1]
        second_o[:, 128 * k : 128 * k + 128] = both[1:2]
        step_o[:, 128 * k : 128 * k + 128] = packed[k, z].astype(f32)[8:16, :].astype(jnp.bfloat16)
    half = nd // 2
    for k in range(2):
        tapb_o[:, 128 * k : 128 * k + 128] = jnp.concatenate(
            [tiles[half * k + i][q][0:8, 32:40] for i in range(half) for q in range(nt)], axis=1
        )
    own = [packed[k, z].astype(f32) for k in range(nd)]

    def by_head(lane):
        wide = jnp.concatenate([own[k][0:8, lane : lane + 8] for k in range(nd)], axis=1)
        return jnp.concatenate([wide[h : h + 1, :] for h in range(heads)], axis=1)

    gain_o[...] = by_head(40)
    tapx_o[...] = jnp.zeros(tapx_o.shape, f32)
    tapb_o[CONV + 1 :, :] = jnp.zeros((7 - CONV, tapb_o.shape[1]), f32)
    for j in range(CONV + 1):
        tapx_o[j : j + 1, :] = by_head(48 + 8 * j)
    sub = lax.broadcasted_iota(jnp.int32, (8, 128), 0)
    decay = jnp.zeros((8, 128), f32)
    bias = jnp.zeros((8, 128), f32)
    for h in range(heads):
        decay = jnp.where(sub == h, scal[0, h], decay)
        bias = jnp.where(sub == h, scal[1, h], bias)
        skip_o[:, SSM_DIM * h : SSM_DIM * (h + 1)] = jnp.full((1, SSM_DIM), scal[2, h], f32)
    decay_o[...] = jnp.where(sub < heads, -jnp.exp(decay), 0.0)
    bias_o[...] = bias


def unpack_small(heads, where, scal, packed, width):
    inner = heads * SSM_DIM
    vmem = pl.BlockSpec(memory_space=pltpu.VMEM)
    smem = pl.BlockSpec(memory_space=pltpu.SMEM)
    sds = jax.ShapeDtypeStruct
    f32 = jnp.float32
    shapes = [(1, width), (1, width), (1, inner), (8, inner), (8, 256)]
    return pl.pallas_call(
        partial(unpack_kernel, heads),
        in_specs=[smem, smem, vmem],
        out_specs=[vmem] * 9,
        out_shape=[sds(s, f32) for s in shapes]
        + [sds((8, width), jnp.bfloat16), sds((8, 128), f32), sds((8, 128), f32), sds((1, inner), f32)],
        name="unpack_small",
    )(where, scal, packed)


def pick(values, index, axis=0):
    return lax.dynamic_index_in_dim(values, index, axis, keepdims=False)


def add_low(left, right):
    return (left.astype(jnp.float32) + right.astype(jnp.float32)).astype(jnp.bfloat16)


def chain_scatter(parts, nt):
    z = lax.axis_index("tensor")
    right = left = None
    for t in range(nt - 1):
        to_right = pick(parts, jnp.clip(nt - 1 - t + z, 0, nt - 1))
        to_left = pick(parts, jnp.clip(t - (nt - 1) + z, 0, nt - 1))
        if t > 0:
            to_right = add_low(to_right, right)
            to_left = add_low(to_left, left)
        right = lax.ppermute(to_right, "tensor", [(i, i + 1) for i in range(t + 1)])
        left = lax.ppermute(
            to_left, "tensor", [(nt - 1 - i, nt - 2 - i) for i in range(t + 1)]
        )
    f32 = jnp.float32
    return pick(parts, z).astype(f32) + right.astype(f32) + left.astype(f32)


def cube_scatter(parts, nd, last=jnp.float32):
    return lax.psum_scatter(parts, "dp", scatter_dimension=0, tiled=False).astype(last)


F32, BF16 = jnp.float32, jnp.bfloat16
VMEM_LIMIT = 56 * 1024 * 1024


def dot_nn(a, b):
    return lax.dot_general(a, b, (((1,), (0,)), ((), ())), preferred_element_type=F32)


def dot_nt(a, b):
    return lax.dot_general(a, b, (((1,), (1,)), ((), ())), preferred_element_type=F32)


def dot_tn(a, b):
    return lax.dot_general(a, b, (((0,), (0,)), ((), ())), preferred_element_type=F32)


def sigmoid(v):
    return 1.0 / (1.0 + jnp.exp(-v))


def lanes_of(shape):
    return lax.broadcasted_iota(jnp.int32, shape, len(shape) - 1)


def turn(values, cosine, sine):
    lane = lanes_of(values.shape)
    other = jnp.where(
        lax.rem(lane, HEAD_SIZE) < HEAD_SIZE // 2,
        pltpu.roll(values, 128 - HEAD_SIZE // 2, 1),
        pltpu.roll(values, HEAD_SIZE // 2, 1),
    )
    return values * cosine + other * sine


def softplus(v):
    return jnp.maximum(v, 0.0) + jnp.log1p(jnp.exp(-jnp.abs(v)))


def running_sum(rows):
    lane = lanes_of(rows.shape)
    step = 1
    while step < rows.shape[1]:
        rows = rows + jnp.where(lane >= step, pltpu.roll(rows, step, 1), 0.0)
        step *= 2
    return rows


def running_sum_back(rows):
    lane = lanes_of(rows.shape)
    width = rows.shape[1]
    step = 1
    while step < width:
        rows = rows + jnp.where(lane < width - step, pltpu.roll(rows, width - step, 1), 0.0)
        step *= 2
    return rows


def stack_columns(rows_list):
    used = sum(r.shape[0] for r in rows_list)
    filler = jnp.zeros((128 - used, 128), F32)
    return jnp.concatenate(rows_list + [filler], axis=0).T


def widen(cols, base, heads):
    low = lanes_of((cols.shape[0], 128)) < SSM_DIM
    return jnp.concatenate(
        [
            jnp.where(low, cols[:, base + 2 * p : base + 2 * p + 1],
                      cols[:, base + 2 * p + 1 : base + 2 * p + 2])
            for p in range(heads // 2)
        ],
        axis=1,
    )


def conv_rows(ref, taps, first, rows):
    total = taps[CONV : CONV + 1, :] + taps[0:1, :] * ref[pl.ds(first, rows), :]
    for j in range(1, CONV):
        total = total + taps[j : j + 1, :] * ref[pl.ds(first + j, rows), :]
    return total


def quarter_at(i, z, nt):
    near = jnp.where(z < nt - 1, z + 1, z - 1)
    far = jnp.where(z < nt - 1, lax.rem(z + 3, nt), lax.rem(z + 1, nt))
    order = jnp.where(i == 0, lax.rem(z + 2, nt), far)
    return jnp.where(i == 2, near, jnp.where(i == 3, z, order))


class FeedGather:
    def __init__(self, step, nt, hid, dwn, hid_f, dwn_f, hid_z, dwn_z, lsem, sems):
        self.step, self.nt = step, nt
        d = lax.axis_index("dp")
        z = lax.axis_index("tensor")
        self.d, self.z = d, z
        self.cube = CubeGather(
            [(hid, lambda s: hid_f.at[s, z]), (dwn, lambda s: dwn_f.at[s, z])], (0,), sems[0], sems[1], d, z
        )
        self.chains = [
            ChainGather(hid, hid_z, sems[2], sems[3], d, z, nt),
            ChainGather(dwn, dwn_z, sems[4], sems[5], d, z, nt),
        ]
        self.own = lambda: [
            pltpu.make_async_copy(hid, hid_f.at[d, z], lsem.at[0]),
            pltpu.make_async_copy(dwn, dwn_f.at[d, z], lsem.at[1]),
        ]

    def at(self, step, act):
        pl.when(self.step == step)(act)

    def begin(self):
        def act():
            greet([(p, self.z) for p in cube_peers(self.d)] + other_quarters(self.d, self.z, self.nt))
            for chain in self.chains:
                chain.start()
            for i in range(2):
                self.cube.start(i)
            for copy in self.own():
                copy.start()

        self.at(0, act)
    def middle(self):
        def near():
            for chain in self.chains:
                chain.hop(1)
            for i in range(2):
                self.cube.near(i)

        def far():
            for chain in self.chains:
                chain.hop(2)
            for i in range(2):
                self.cube.far(i)

        self.at(1, near)
        self.at(2, far)

    def end(self):
        def act():
            for chain in self.chains:
                chain.hop(3)
            self.cube.finish()
            for copy in self.own():
                copy.wait()
            for chain in self.chains:
                chain.drain()

        self.at(3, act)


def forward_kernel(heads, nt, feed, *refs):
    if feed:
        beside = FeedGather(
            pl.program_id(0), nt, *refs[14:16], *refs[29:33], refs[38], refs[39:45]
        )
        refs = refs[:14] + refs[16:29] + refs[33:38]
        beside.begin()
        forward_step(heads, beside.middle, *refs)
        beside.end()
    else:
        forward_step(heads, lambda: None, *refs)


def forward_step(
    heads, middle, kvh, tok, gain, wq, win, stp, wsh, cosine, sine, tapx, tapb, decay, bias, skip,
    a1_o, q_o, k_o, v_o, lse_o, o_o, x_o, z_o, b_o, y_o, t_o, s_o, sq_o,
    keys, vals, xs, bs, state,
):
    step = pl.program_id(0)
    rows = tok.shape[0]
    second = kvh[0] == 1

    @pl.when(step == 0)
    def _():
        xs[0:8, :] = jnp.zeros((8, xs.shape[1]), F32)
        bs[0:8, :] = jnp.zeros((8, bs.shape[1]), F32)
        state[...] = jnp.zeros(state.shape, F32)

    t = tok[...].astype(F32)
    r = lax.rsqrt(jnp.mean(t * t, axis=1, keepdims=True) + epsilon)
    a1 = (t * r * gain[...]).astype(BF16)
    a1_o[...] = a1
    q = turn(dot_nn(a1, wq[...]), cosine[...], sine[...]).astype(BF16)
    q_o[...] = q
    s = dot_nn(a1, wsh[...])
    low = lanes_of((rows, 128)) < HEAD_SIZE
    k = turn(s[:, :128], cosine[...], sine[...])
    v = s[:, 128:256]
    pick_own = low != second
    k2 = jnp.where(pick_own, k, pltpu.roll(k, 64, 1)).astype(BF16)
    v2 = jnp.where(pick_own, v, pltpu.roll(v, 64, 1))
    k_o[...] = k2
    v_o[...] = v2.astype(BF16)
    place = pl.ds(pl.multiple_of(step * rows, rows), rows)
    keys[place, :] = k2
    vals[:, place] = v2.T.astype(BF16)

    scale = HEAD_SIZE**-0.5

    def attend(blocks):
        n = blocks * rows
        shape = (rows, rows)
        allowed = lax.broadcasted_iota(jnp.int32, shape, 0) <= lanes_of(shape)
        parts = []
        for h in range(2):
            qh = jnp.where(low == (h == 0), q, jnp.zeros_like(q))
            sc = dot_nt(keys[0:n, :], qh) * scale
            last = jnp.where(allowed, sc[n - rows :, :], neg_large)
            sc = jnp.concatenate([sc[: n - rows, :], last], axis=0) if blocks > 1 else last
            top = jnp.max(sc, axis=0, keepdims=True)
            e = jnp.exp(sc - top)
            total = jnp.sum(e, axis=0, keepdims=True)
            lse_o[h : h + 1, :] = top + jnp.log(total)
            parts.append(dot_nn(vals[:, 0:n], e.astype(BF16)) / total)
        sub = lax.broadcasted_iota(jnp.int32, parts[0].shape, 0)
        o_o[...] = jnp.where(sub < HEAD_SIZE, parts[0], parts[1]).T.astype(BF16)

    for i in range(keys.shape[0] // rows):
        pl.when(step == i)(partial(attend, i + 1))

    middle()
    zr = dot_nn(a1, win[0])
    z_o[...] = zr
    xr = dot_nn(a1, win[1])
    x_o[...] = xr
    br = s[:, 256:]
    b_o[...] = br
    xs[8 : 8 + rows, :] = xr
    bs[8 : 8 + rows, :] = br
    u = conv_rows(xs, tapx, 5, rows)
    x = u * sigmoid(u)
    u = conv_rows(bs, tapb, 5, rows)
    bc = (u * sigmoid(u)).astype(BF16)
    xs[0:8, :] = xs[rows : rows + 8, :]
    bs[0:8, :] = bs[rows : rows + 8, :]
    tr = dot_nt(stp[...], a1)
    t_o[...] = tr
    n_state = bc.shape[1] // 2
    tri_shape = (block_len, block_len)
    lower = lax.broadcasted_iota(jnp.int32, tri_shape, 0) >= lanes_of(tri_shape)
    half = lanes_of(tri_shape) < SSM_DIM
    for c in range(rows // block_len):
        part = slice(c * block_len, (c + 1) * block_len)
        dt = softplus(tr[:, part] + bias[...])
        cum = running_sum(dt * decay[...])
        end = cum[:, block_len - 1 :]
        cols = stack_columns([cum, jnp.exp(cum), dt * jnp.exp(end - cum)])
        xc = x[part]
        x_low = xc.astype(BF16)
        b_low = bc[part, :n_state]
        c_low = bc[part, n_state:]
        cross = dot_nt(c_low, b_low)
        grow = widen(cols, 8, heads)
        y = dot_nn(c_low, state[...].astype(BF16)) * grow + skip[...] * xc
        inner = []
        for p in range(heads // 2):
            mats = []
            for h in (2 * p, 2 * p + 1):
                gap = jnp.where(lower, cols[:, h : h + 1] - cum[h : h + 1, :], neg_large)
                mats.append((cross * jnp.exp(gap) * dt[h : h + 1, :]).astype(BF16))
            xp = x_low[:, 128 * p : 128 * p + 128]
            zero = jnp.zeros_like(xp)
            both = jnp.concatenate([jnp.where(half, xp, zero), jnp.where(half, zero, xp)], axis=0)
            inner.append(dot_nn(jnp.concatenate(mats, axis=1), both))
        y = y + jnp.concatenate(inner, axis=1)
        y_o[part, :] = y
        s_o[c] = state[...]
        carried = (xc * widen(cols, 16, heads)).astype(BF16)
        state[...] = grow[block_len - 1 :, :] * state[...] + dot_tn(b_low, carried)
        zc = zr[part]
        w = y * (zc * sigmoid(zc))
        total = jnp.sum(w * w, axis=1, keepdims=True)
        sq_o[:, part] = jnp.broadcast_to(total, (block_len, 128)).T[0:8, :]


def mixers_forward(
    heads, nt, kvh, tok, gain, wq, win, stp, wsh, cosine, sine, tapx, tapb, decay, bias, skip, feed=()
):
    total, width = tok.shape
    rows = 256
    inner = heads * SSM_DIM
    pair = wsh.shape[1] - 256
    state = pair // 2
    chunks = rows // block_len

    def whole(v):
        return pl.BlockSpec(v.shape, lambda i: (0,) * v.ndim)

    def tall(n):
        return pl.BlockSpec((rows, n), lambda i: (i, 0))

    wide = pl.BlockSpec((8, rows), lambda i: (0, i))
    sds = jax.ShapeDtypeStruct
    more_in, more_out, more_shape, more_scratch, extra = [], [], [], [], {}
    if feed:
        nd = 8
        dma = pltpu.SemaphoreType.DMA
        more_in = [whole(v) for v in feed]
        more_out = [pl.BlockSpec(memory_space=pl.ANY)] * 4
        more_shape = [sds((nd, nt) + v.shape, BF16) for v in feed] + [sds((nt,) + v.shape, BF16) for v in feed]
        more_scratch = [dma((2,)), dma((2, 7)), dma((2, 7))] + [dma((2, nt - 1))] * 4
        extra = dict(collective_id=6, has_side_effects=True)
    return pl.pallas_call(
        partial(forward_kernel, heads, nt, bool(feed)),
        grid=(total // rows,),
        in_specs=[pl.BlockSpec(memory_space=pltpu.SMEM), tall(width), whole(gain), whole(wq), whole(win),
                  whole(stp), whole(wsh), tall(128), tall(128), whole(tapx), whole(tapb),
                  whole(decay), whole(bias), whole(skip)] + more_in,
        out_specs=[tall(width), tall(128), tall(128), tall(128), wide, tall(128), tall(inner),
                   tall(inner), tall(pair), tall(inner), wide,
                   pl.BlockSpec((chunks, state, inner), lambda i: (i, 0, 0)), wide] + more_out,
        out_shape=[sds((total, width), BF16), sds((total, 128), BF16), sds((total, 128), BF16),
                   sds((total, 128), BF16), sds((8, total), F32), sds((total, 128), BF16),
                   sds((total, inner), F32), sds((total, inner), F32), sds((total, pair), F32),
                   sds((total, inner), F32), sds((8, total), F32),
                   sds((total // block_len, state, inner), F32), sds((8, total), F32)] + more_shape,
        scratch_shapes=[pltpu.VMEM((total, 128), BF16), pltpu.VMEM((128, total), BF16),
                        pltpu.VMEM((rows + 8, inner), F32), pltpu.VMEM((rows + 8, pair), F32),
                        pltpu.VMEM((state, inner), F32)] + more_scratch,
        compiler_params=pltpu.CompilerParams(vmem_limit_bytes=VMEM_LIMIT, **extra),
        cost_estimate=pl.CostEstimate(flops=int(5e9), bytes_accessed=int(15e6), transcendentals=int(4e6)),
        name="mixers_forward",
    )(kvh, tok, gain, wq, win, stp, wsh, cosine, sine, tapx, tapb, decay, bias, skip, *feed)


def attend_back(step, kvh, q, k2, v2, lse, do, cosine, sine, cos_all, sin_all, dq_o, dkv_o, dk, dv):
    rows = q.shape[0]
    steps = k2.shape[0] // rows
    scale = HEAD_SIZE**-0.5
    low = lanes_of((rows, 128)) < HEAD_SIZE

    @pl.when(step == 0)
    def _():
        dk[...] = jnp.zeros(dk.shape, F32)
        dv[...] = jnp.zeros(dv.shape, F32)

    def back(blocks):
        n = blocks * rows
        shape = (rows, rows)
        allowed = lax.broadcasted_iota(jnp.int32, shape, 0) <= lanes_of(shape)
        qs, dos, ps, dss, dqs = [], [], [], [], []
        for h in range(2):
            mine = low == (h == 0)
            qh = jnp.where(mine, q[...], jnp.zeros_like(q[...]))
            doh = jnp.where(mine, do[...], jnp.zeros_like(do[...]))
            sc = dot_nt(k2[0:n, :], qh) * scale - lse[h : h + 1, :]
            last = jnp.where(allowed, sc[n - rows :, :], neg_large)
            sc = jnp.concatenate([sc[: n - rows, :], last], axis=0) if blocks > 1 else last
            p = jnp.exp(sc)
            dp = dot_nt(v2[0:n, :], doh)
            centre = jnp.sum(p * dp, axis=0, keepdims=True)
            ds = (p * (dp - centre)).astype(BF16)
            qs.append(qh)
            dos.append(doh)
            ps.append(p.astype(BF16))
            dss.append(ds)
            dqs.append(dot_tn(ds, k2[0:n, :]) * scale)
        dk[0:n, :] += dot_nn(jnp.concatenate(dss, axis=1), jnp.concatenate(qs, axis=0)) * scale
        dv[0:n, :] += dot_nn(jnp.concatenate(ps, axis=1), jnp.concatenate(dos, axis=0))
        dq_o[...] = turn(jnp.where(low, dqs[0], dqs[1]), cosine[...], -sine[...]).astype(BF16)

    for i in range(steps):
        pl.when(step == 2 * i)(partial(back, i + 1))

    @pl.when(step == 2 * steps - 1)
    def _():
        own = (lanes_of(dk.shape) < HEAD_SIZE) != (kvh[0] == 1)
        g = dk[...]
        g = turn(g + pltpu.roll(g, 64, 1), cos_all[...], -sin_all[...])
        dkv_o[:, 0:128] = jnp.where(own, g, 0.0).astype(BF16)
        g = dv[...]
        g = g + pltpu.roll(g, 64, 1)
        dkv_o[:, 128:256] = jnp.where(own, g, 0.0).astype(BF16)


def back_kernel(heads, channels, nt, feed, *refs):
    step = pl.program_id(0)
    if feed:
        d = lax.axis_index("dp")
        z = lax.axis_index("tensor")
        sums, raw, refs = refs[0], refs[1], refs[2:]
        feed_o, refs = refs[37], refs[:37] + refs[38:]
        parts, chain_boxes, box, refs = refs[44], refs[45:49], refs[49:57], refs[:44]
        peers = cube_peers(d)
        square = SquareScatter(
            lambda i, j: (2 * i + j,), raw, box[:6], box[6], box[7], peers, dp_bits(d), z
        )
        chain = ChainScatter(parts, *chain_boxes, d, z, nt)

        @pl.when(step == 0)
        def _():
            greet([(p, z) for p in peers[1:]] + other_quarters(d, z, nt))
            for k in range(nt - 2):
                parts[quarter_at(k, z, nt)] = sums[k]
            parts[z] = jnp.zeros(parts.shape[1:], BF16)
            chain.step(0)
            square.start()

        pl.when(step == 3)(lambda: chain.step(1))
        pl.when(step == 3)(square.middle)

        @pl.when(step == 5)
        def _():
            square.finish(parts.at[quarter_at(nt - 2, z, nt)])
            chain.step(2)

    attend_back(step, *refs[:10], *refs[27:29], *refs[37:39])
    scan_back(heads, channels, step, *refs[10:27], *refs[29:37], *refs[39:44])
    if feed:

        @pl.when(step == pl.num_programs(0) - 1)
        def _():
            chain.finish(feed_o)
            chain.drain()
            square.drain()


def scan_back(
    heads, channels, step, dm, y, zr, xr, xp, br, bp, trow, states, rsum, dots, gain, tapx, tapb, decay,
    bias, skip,
    dz_o, dx_o, db_o, dt_o, gx_o, gb_o, gm_o, gh_o,
    xs, bs, dxs, dbs, dstate,
):
    last_step = pl.num_programs(0) - 1
    first = step == last_step
    rows = block_len
    inner = heads * SSM_DIM
    n_state = br.shape[1] // 2

    @pl.when(step == 0)
    def _():
        dxs[rows : rows + 8, :] = jnp.zeros((8, inner), F32)
        dbs[rows : rows + 8, :] = jnp.zeros((8, 2 * n_state), F32)
        dstate[...] = jnp.zeros(dstate.shape, F32)
        gx_o[...] = jnp.zeros(gx_o.shape, F32)
        gb_o[...] = jnp.zeros(gb_o.shape, F32)
        gm_o[...] = jnp.zeros(gm_o.shape, F32)
        gh_o[...] = jnp.zeros(gh_o.shape, F32)

    xs[0:8, :] = jnp.where(first, 0.0, xp[...])
    bs[0:8, :] = jnp.where(first, 0.0, bp[...])
    xs[8 : 8 + rows, :] = xr[...]
    bs[8 : 8 + rows, :] = br[...]
    ux = conv_rows(xs, tapx, 5, rows)
    sx = sigmoid(ux)
    x = ux * sx
    ub = conv_rows(bs, tapb, 5, rows)
    sb = sigmoid(ub)
    bc = (ub * sb).astype(BF16)
    b_low, c_low = bc[:, :n_state], bc[:, n_state:]

    pre = trow[...] + bias[...]
    dt = softplus(pre)
    cum = running_sum(dt * decay[...])
    end = cum[:, rows - 1 :]
    fade = jnp.exp(end - cum)
    inv = lax.rsqrt(rsum[...] / channels + epsilon)
    cols = stack_columns(
        [cum, jnp.exp(cum), dt * fade, dt, inv, inv * inv * inv * dots[...] / channels]
    )
    r = cols[:, 32:33]
    kk = cols[:, 40:41]
    z = zr[...]
    sz = sigmoid(z)
    silu_z = z * sz
    yv = y[...]
    w = yv * silu_z
    dmv = dm[...]
    dw = r * gain[...] * dmv - w * kk
    gm_o[0:1, :] += jnp.sum(dmv * w * r, axis=0, keepdims=True)
    dy = dw * silu_z
    dz_o[...] = (dw * yv * sz * (1.0 + z * (1.0 - sz))).astype(BF16)
    gm_o[1:2, :] += jnp.sum(dy * x, axis=0, keepdims=True)

    grow = widen(cols, 8, heads)
    tail = widen(cols, 16, heads)
    dt_wide = widen(cols, 24, heads)
    x_low = x.astype(BF16)
    dy_low = dy.astype(BF16)
    state = states[0]
    state_low = state.astype(BF16)
    ds = dstate[...]
    ds_low = ds.astype(BF16)
    cross = dot_nt(b_low, c_low)
    shape = (rows, rows)
    upper = lax.broadcasted_iota(jnp.int32, shape, 0) <= lanes_of(shape)
    half = lanes_of(shape) < SSM_DIM
    lane = lanes_of(shape)
    dcross = jnp.zeros(shape, F32)
    col_sums = jnp.zeros(shape, F32)
    row_sums = []
    mids = []
    for p in range(heads // 2):
        span = slice(128 * p, 128 * p + 128)
        xpair, dypair = x_low[:, span], dy_low[:, span]
        zero = jnp.zeros_like(xpair)
        dys = (jnp.where(half, dypair, zero), jnp.where(half, zero, dypair))
        mats = []
        for k in range(2):
            h = 2 * p + k
            gap = jnp.where(upper, cum[h : h + 1, :] - cols[:, h : h + 1], neg_large)
            faded = jnp.exp(gap)
            mats.append((cross * faded).astype(BF16))
            t = dot_nt(xpair, dys[k]) * faded
            dt_col = cols[:, 24 + h : 25 + h]
            td = t * dt_col
            dcross = dcross + td
            row_sums.append(jnp.sum(td * cross, axis=0, keepdims=True))
            col = jnp.sum(t * cross, axis=1, keepdims=True)
            col_sums = jnp.where(lane == h, col, col_sums)
        mids.append(dot_nn(jnp.concatenate(mats, axis=1), jnp.concatenate(dys, axis=0)))
    mid = jnp.concatenate(mids, axis=1)
    row_sums = jnp.concatenate(row_sums + [jnp.zeros((8 - heads, rows), F32)], axis=0)
    col_sums = col_sums.T[0:8, :]

    dye = dy * grow
    dye_low = dye.astype(BF16)
    xd = x * tail
    xd_low = xd.astype(BF16)
    from_b = dot_nn(b_low, ds_low)
    through = dot_nn(c_low, state_low)
    dcross_low = dcross.astype(BF16)
    db = dot_nn(dcross_low, c_low) + dot_nt(xd_low, ds_low)
    dc = dot_tn(dcross_low, b_low) + dot_nt(dye_low, state_low)

    head_of = lax.broadcasted_iota(jnp.int32, (8, inner), 0)
    chan = lanes_of((8, inner)) // SSM_DIM
    ones = jnp.where(head_of == chan, 1.0, 0.0).astype(BF16)

    def by_head(v):
        high = v.astype(BF16)
        rest = (v - high.astype(F32)).astype(BF16)
        return dot_nt(ones, high) + dot_nt(ones, rest)

    grown = by_head(dye * through)
    ended = by_head(x * from_b)
    kept = jnp.sum(ds * state, axis=0, keepdims=True) * grow[rows - 1 :, :]
    kept = jnp.where(head_of == chan, kept, 0.0).sum(axis=1, keepdims=True)
    pulled = dt * fade * ended
    lane8 = lanes_of((8, rows))
    at_end = kept + jnp.sum(pulled, axis=1, keepdims=True)
    dcum = row_sums - dt * col_sums + grown - pulled + jnp.where(lane8 == rows - 1, at_end, 0.0)
    da = running_sum_back(dcum)
    ddt = col_sums + fade * ended + decay[...] * da
    dpre = ddt * sigmoid(pre)
    dt_o[...] = dpre
    gh_o[0:8, :] += da * dt * decay[...]
    gh_o[8:16, :] += dpre

    dstate[...] = grow[rows - 1 :, :] * ds + dot_tn(c_low, dye_low)
    dx = skip[...] * dy + dt_wide * mid + tail * from_b
    dux = dx * sx * (1.0 + ux * (1.0 - sx))
    dub = jnp.concatenate([db, dc], axis=1) * sb * (1.0 + ub * (1.0 - sb))
    for taps, src, d, buf, acc, out in (
        (tapx, xs, dux, dxs, gx_o, dx_o),
        (tapb, bs, dub, dbs, gb_o, db_o),
    ):
        buf[0:rows, :] = d
        total = taps[CONV - 1 : CONV, :] * d
        for j in range(CONV - 1):
            total = total + taps[j : j + 1, :] * buf[pl.ds(CONV - 1 - j, rows), :]
        out[...] = total.astype(BF16)
        for j in range(CONV):
            acc[j : j + 1, :] += jnp.sum(d * src[pl.ds(5 + j, rows), :], axis=0, keepdims=True)
        acc[CONV : CONV + 1, :] += jnp.sum(d, axis=0, keepdims=True)
        buf[rows : rows + 8, :] = d[0:8, :]


def mixers_back(
    heads, channels, nt, kvh, q, k2, v2, lse, do, cosine, sine, dm, y, zr, xr, br, trow, states, rsum, dots,
    gain, tapx, tapb, decay, bias, skip, feed=None,
):
    total, inner = y.shape
    pair = br.shape[1]
    rows = block_len
    steps = total // rows
    per = rows // 8
    q_rows = 2 * rows

    def whole(v):
        return pl.BlockSpec(v.shape, lambda i: (0,) * v.ndim)

    def tall(n):
        return pl.BlockSpec((rows, n), lambda i: (steps - 1 - i, 0))

    def before(n):
        return pl.BlockSpec((8, n), lambda i: (jnp.maximum((steps - 1 - i) * per - 1, 0), 0))

    wide = pl.BlockSpec((8, rows), lambda i: (0, steps - 1 - i))
    ask = pl.BlockSpec((q_rows, 128), lambda i: (i // 2, 0))
    sds = jax.ShapeDtypeStruct

    def fixed(*shape):
        return pl.BlockSpec(shape, lambda i: (0,) * len(shape))

    in_specs = [pl.BlockSpec(memory_space=pltpu.SMEM), ask, whole(k2), whole(v2),
                pl.BlockSpec((8, q_rows), lambda i: (0, i // 2)), ask, ask, ask, whole(cosine), whole(sine),
                tall(inner), tall(inner), tall(inner), tall(inner), before(inner), tall(pair),
                before(pair), wide, pl.BlockSpec((1, pair // 2, inner), lambda i: (steps - 1 - i, 0, 0)),
                wide, wide, whole(gain), whole(tapx), whole(tapb), whole(decay), whole(bias), whole(skip)]
    out_specs = [ask, fixed(total, 256), tall(inner), tall(inner), tall(pair), wide, fixed(8, inner),
                 fixed(8, pair), fixed(8, inner), fixed(16, rows)]
    out_shape = [sds((total, 128), BF16), sds((total, 256), BF16), sds((total, inner), BF16),
                 sds((total, inner), BF16), sds((total, pair), BF16), sds((8, total), F32),
                 sds((8, inner), F32), sds((8, pair), F32), sds((8, inner), F32), sds((16, rows), F32)]
    scratch = [pltpu.VMEM((total, 128), F32), pltpu.VMEM((total, 128), F32),
               pltpu.VMEM((rows + 8, inner), F32), pltpu.VMEM((rows + 8, pair), F32),
               pltpu.VMEM((rows + 8, inner), F32), pltpu.VMEM((rows + 8, pair), F32),
               pltpu.VMEM((pair // 2, inner), F32)]
    args = [kvh, q, k2, v2, lse, do, cosine, sine, cosine, sine, dm, y, zr, xr, xr, br, br, trow, states,
            rsum, dots, gain, tapx, tapb, decay, bias, skip]
    extra = {}
    if feed is not None:
        piece = feed[0].shape[1:]
        args = list(feed) + args
        in_specs = [whole(v) for v in feed] + in_specs
        out_specs = out_specs + [fixed(*piece)]
        out_shape = out_shape + [sds(piece, F32)]
        scratch = scratch + [pltpu.VMEM((nt,) + piece, BF16)] + chain_scratch(nt, *piece)
        scratch = scratch + square_scratch(*piece)
        extra = dict(collective_id=5, has_side_effects=True)
    return pl.pallas_call(
        partial(back_kernel, heads, channels, nt, feed is not None),
        grid=(steps,),
        in_specs=in_specs,
        out_specs=out_specs,
        out_shape=out_shape,
        scratch_shapes=scratch,
        compiler_params=pltpu.CompilerParams(vmem_limit_bytes=VMEM_LIMIT, **extra),
        cost_estimate=pl.CostEstimate(flops=int(6e9), bytes_accessed=int(18e6), transcendentals=int(7e6)),
        name="mixers_back",
    )(*args)


def whole_spec(v):
    return pl.BlockSpec(v.shape, lambda i: (0,) * v.ndim)


def feed_open(hid, gain, a2, a2t, acc, dacc):
    v = hid[...]
    f = lax.rsqrt(jnp.mean(v * v, axis=1, keepdims=True) + epsilon)
    low = (v * f * gain[...]).astype(BF16)
    a2[...] = low
    a2t[...] = low.T
    acc[...] = jnp.zeros(acc.shape, F32)
    dacc[...] = jnp.zeros(dacc.shape, F32)


def feed_tile(a2, cot, whid, wdown, acc, dacc):
    width = a2.shape[1]
    units = whid.shape[4]
    w_gate = whid[:, 0, 0].reshape(width, units)
    w_up = whid[:, 0, 1].reshape(width, units)
    w_down = jnp.concatenate([wdown[k, 0] for k in range(width // 128)], axis=1)
    g = dot_nn(a2[...], w_gate)
    u = dot_nn(a2[...], w_up)
    s = sigmoid(g)
    f_low = (g * s * u).astype(BF16)
    acc[...] += dot_nn(f_low, w_down)
    df = dot_nt(cot[...], w_down)
    du = (df * g * s).astype(BF16)
    dg = (df * u * s * (1.0 + g * (1.0 - s))).astype(BF16)
    dacc[...] += dot_nt(dg, w_gate) + dot_nt(du, w_up)
    return f_low, dg, du


def feed_close(hid, gain, cot, acc, dacc, out_o, dh_o, gg_o):
    v = hid[...]
    out_o[...] = (v + acc[...]).astype(BF16)
    f = lax.rsqrt(jnp.mean(v * v, axis=1, keepdims=True) + epsilon)
    dy = dacc[...]
    gg_o[...] = jnp.sum(dy * v * f, axis=0, keepdims=True)
    gdy = dy * gain[...]
    lean = jnp.sum(gdy * v, axis=1, keepdims=True) * (f * f * f / v.shape[1])
    dh = cot[...].astype(F32) + (f * gdy - v * lean)
    dh_o[...] = dh
    return dh.astype(BF16)


def feed_grads(a2t, cot, f_low, dg, du):
    blocks = a2t.shape[0] // 128
    values = []
    for grad in (dg, du):
        full = dot_nn(a2t[...], grad).astype(BF16)
        for cb in range(grad.shape[1] // 128):
            values.append(full[:, 128 * cb : 128 * cb + 128].reshape(blocks, 128, 128))
    full = dot_tn(f_low, cot[...]).astype(BF16)
    values.append(jnp.stack([full[:, 128 * k : 128 * k + 128] for k in range(blocks)]))
    return values


def piece_rows(part, units, quarter_units):
    rows = [
        (k * quarter_units + part * units + cb * 128, 128) for k in range(2) for cb in range(units // 128)
    ]
    return rows + [(2 * quarter_units + part * units, units)]


def feed_kernel(hid, gain, cot, whid, wdown, out_o, dh_o, dmix_o, gg_o, piece_o, a2, a2t, acc, dacc):
    step = pl.program_id(0)
    pl.when(step == 0)(lambda: feed_open(hid, gain, a2, a2t, acc, dacc))
    values = feed_grads(a2t, cot, *feed_tile(a2, cot, whid, wdown, acc, dacc))
    units = whid.shape[4]
    quarter_units = piece_o.shape[2] // 3
    tiles_per = quarter_units // units
    rows = piece_rows(lax.rem(step, tiles_per), units, quarter_units)
    for value, (row, n) in zip(values, rows):
        piece_o[:, step // tiles_per, pl.ds(pl.multiple_of(row, 128), n), :] = value

    @pl.when(step == pl.num_programs(0) - 1)
    def _():
        dmix_o[...] = feed_close(hid, gain, cot, acc, dacc, out_o, dh_o, gg_o)


def feed_forward(hid, gain, cot, whid, wdown):
    rows, width = hid.shape
    blocks, nt, _, depth, units = whid.shape
    tile = 256
    per = units // tile
    hid_spec = pl.BlockSpec((blocks, 1, 2, depth, tile), lambda i: (0, i // per, 0, 0, lax.rem(i, per)))
    down_spec = pl.BlockSpec((blocks, 1, tile, 128), lambda i: (0, i // per, lax.rem(i, per), 0))
    sds = jax.ShapeDtypeStruct
    piece = (blocks, nt, 3 * units, 128)

    def fixed(*shape):
        return pl.BlockSpec(shape, lambda i: (0,) * len(shape))

    return pl.pallas_call(
        feed_kernel,
        grid=(nt * per,),
        in_specs=[fixed(rows, width), fixed(1, width), fixed(rows, width), hid_spec, down_spec],
        out_specs=[fixed(rows, width), fixed(rows, width), fixed(rows, width), fixed(1, width),
                   fixed(*piece)],
        out_shape=[sds((rows, width), BF16), sds((rows, width), F32), sds((rows, width), BF16),
                   sds((1, width), F32), sds(piece, BF16)],
        scratch_shapes=[pltpu.VMEM((rows, width), BF16), pltpu.VMEM((width, rows), BF16),
                        pltpu.VMEM((rows, width), F32), pltpu.VMEM((rows, width), F32)],
        compiler_params=pltpu.CompilerParams(vmem_limit_bytes=VMEM_LIMIT),
        name="feed_forward",
    )(hid, gain, cot, whid, wdown)


def row_columns(rows_list, rows):
    return jnp.concatenate(
        [stack_columns([r[:, c : c + 128] for r in rows_list]) for c in range(0, rows, 128)], axis=0
    )


def down_rows(at, dq, dz, dx, dkv, db, drow, wq, win, stp, wsh):
    total = dot_nt(dq[at, :], wq[...]) + dot_nt(dz[at, :], win[0]) + dot_nt(dx[at, :], win[1])
    total = total + dot_nt(dkv[at, :], wsh[:, 0:256]) + dot_nt(db[at, :], wsh[:, 256:])
    return total + dot_tn(drow[:, at].astype(BF16), stp[...])


def down_kernel(dq, dz, dx, dkv, db, drow, wq, win, stp, wsh, part_o):
    every = slice(None)
    part_o[...] = down_rows(every, dq, dz, dx, dkv, db, drow, wq, win, stp, wsh).astype(BF16)


def down_parts(dq, dz, dx, dkv, db, drow, wq, win, stp, wsh):
    total, inner = dz.shape
    width = wq.shape[0]
    rows = 256

    def tall(v):
        return pl.BlockSpec((rows, v.shape[1]), lambda i: (i, 0))

    wide = pl.BlockSpec((8, rows), lambda i: (0, i))
    return pl.pallas_call(
        down_kernel,
        grid=(total // rows,),
        in_specs=[tall(dq), tall(dz), tall(dx), tall(dkv), tall(db), wide, whole_spec(wq), whole_spec(win),
                  whole_spec(stp), whole_spec(wsh)],
        out_specs=pl.BlockSpec((rows, width), lambda i: (i, 0)),
        out_shape=jax.ShapeDtypeStruct((total, width), BF16),
        compiler_params=pltpu.CompilerParams(vmem_limit_bytes=VMEM_LIMIT),
        cost_estimate=pl.CostEstimate(flops=int(3e9), bytes_accessed=int(8e6), transcendentals=0),
        name="down_parts",
    )(dq, dz, dx, dkv, db, drow, wq, win, stp, wsh)


def weight_columns(a, g, dq, dz, dx, dkv, db, ot, mt, put, put_shared):
    at = a.T
    inner = dz.shape[1]

    def by_rows(values, first):
        for j in range(values.shape[1] // 128):
            for k in range(2):
                put(k, first + 128 * j, values[128 * k : 128 * (k + 1), 128 * j : 128 * (j + 1)])

    def by_lanes(values, first):
        for k in range(2):
            put(k, first, values[:, 128 * k : 128 * (k + 1)])

    by_rows(dot_nn(at, dq[...]).astype(BF16), 0)
    by_lanes(dot_nn(ot[...], g).astype(BF16), 128)
    by_rows(dot_nn(at, dz[...]).astype(BF16), 256)
    by_rows(dot_nn(at, dx[...]).astype(BF16), 256 + inner)
    by_lanes(dot_nn(mt[...], g).astype(BF16), 256 + 2 * inner)
    for first, values in ((0, dot_nn(at, dkv[...]).astype(BF16)), (256, dot_nn(at, db[...]).astype(BF16))):
        for k in range(2):
            put_shared(k, first, values[128 * k : 128 * (k + 1)])


def weight_kernel(a1, dq, dz, dx, dkv, db, drow, o, m, dmix, piece_o, shared_o, step_o, ot, mt):
    @pl.when(pl.program_id(0) == 0)
    def _():
        ot[...] = o[...].T
        mt[...] = m[...].T

    step_o[...] = dot_nn(drow[...].astype(BF16), a1[...])

    def put(k, first, values):
        piece_o[k, first : first + values.shape[0], :] = values

    def put_shared(k, first, values):
        shared_o[k, :, first : first + values.shape[1]] = values

    weight_columns(a1[...], dmix[...], dq, dz, dx, dkv, db, ot, mt, put, put_shared)


def weight_pieces(a1, dq, dz, dx, dkv, db, drow, o, m, dmix):
    total, width = a1.shape
    inner = dz.shape[1]
    n = 256 + 3 * inner
    shared = 256 + db.shape[1]
    cols = pl.BlockSpec((total, 256), lambda i: (0, i))
    sds = jax.ShapeDtypeStruct
    args = (dq, dz, dx, dkv, db, drow, o, m)
    return pl.pallas_call(
        weight_kernel,
        grid=(width // 256,),
        in_specs=[cols] + [whole_spec(v) for v in args] + [cols],
        out_specs=[pl.BlockSpec((2, n, 128), lambda i: (i, 0, 0)),
                   pl.BlockSpec((2, 128, shared), lambda i: (i, 0, 0)),
                   pl.BlockSpec((8, 256), lambda i: (0, i))],
        out_shape=[sds((width // 128, n, 128), BF16), sds((width // 128, 128, shared), BF16),
                   sds((8, width), F32)],
        scratch_shapes=[pltpu.VMEM((128, total), BF16), pltpu.VMEM((inner, total), BF16)],
        compiler_params=pltpu.CompilerParams(vmem_limit_bytes=VMEM_LIMIT),
        cost_estimate=pl.CostEstimate(flops=int(4e9), bytes_accessed=int(12e6), transcendentals=0),
        name="weight_pieces",
    )(a1, *args, dmix)


class Exchange:
    def __init__(self, own, landed, send, recv, d, z, nt):
        self.own, self.landed, self.z, self.nt = own, landed, z, nt
        self.copies = [
            remote_copy(own, landed.at[k - 1], send.at[k - 1], recv.at[k - 1], peer)
            for k, peer in enumerate(other_quarters(d, z, nt), 1)
        ]

    def start(self):
        for copy in self.copies:
            copy.start()

    def wait(self):
        for copy in self.copies:
            copy.wait()

    def total(self):
        total = None
        for q in range(self.nt):
            value = jnp.where(self.z == q, self.own[...].astype(F32), 0.0)
            for k in range(1, self.nt):
                value = value + jnp.where(
                    lax.rem(self.z - k + self.nt, self.nt) == q, self.landed[k - 1].astype(F32), 0.0
                )
            total = value if total is None else total + value
        return total


class ChainScatter:
    def __init__(self, parts, bufs, landed, send, recv, d, z, nt):
        self.parts, self.bufs, self.landed = parts, bufs, landed
        self.send, self.recv = send, recv
        self.d, self.z, self.nt = d, z, nt

    def active(self, way, t):
        z, nt = self.z, self.nt
        if way == 0:
            return (z <= t) & (z < nt - 1)
        return (nt - 1 - z <= t) & (z > 0)

    def copy(self, way, t):
        dev = (self.d, self.z + 1 if way == 0 else self.z - 1)
        return remote_copy(
            self.bufs.at[way, t], self.landed.at[way, t], self.send.at[way, t], self.recv.at[way, t], dev
        )

    def arrives(self, way, t):
        z, nt = self.z, self.nt
        if way == 0:
            return (z >= 1) & (z - 1 <= t)
        return (z < nt - 1) & (nt - 2 - z <= t)

    def step(self, t):
        z, nt = self.z, self.nt
        for way in range(2):
            q = nt - 1 - t + z if way == 0 else t - (nt - 1) + z

            def run():
                value = self.parts[q]
                if t > 0:
                    came = self.arrives(way, t - 1)

                    @pl.when(came)
                    def _():
                        self.copy(way, t - 1).wait_recv()
                        total = value.astype(F32) + self.landed[way, t - 1].astype(F32)
                        self.bufs[way, t] = total.astype(BF16)

                    @pl.when(jnp.logical_not(came))
                    def _():
                        self.bufs[way, t] = value
                else:
                    self.bufs[way, t] = value
                self.copy(way, t).start()

            pl.when(self.active(way, t))(run)

    def finish(self, out):
        out[...] = self.parts[self.z].astype(F32)
        t = self.nt - 2
        for way in range(2):

            @pl.when(self.arrives(way, t))
            def _():
                self.copy(way, t).wait_recv()
                out[...] += self.landed[way, t].astype(F32)

    def drain(self):
        for way in range(2):
            for t in range(self.nt - 1):
                pl.when(self.active(way, t))(self.copy(way, t).wait_send)


def chain_scratch(nt, rows, width):
    dma = pltpu.SemaphoreType.DMA
    return [
        pltpu.VMEM((2, nt - 1, rows, width), BF16),
        pltpu.VMEM((2, nt - 1, rows, width), BF16),
        dma((2, nt - 1)),
        dma((2, nt - 1)),
    ]


def mix_scatter_kernel(channels, nt, feed, *refs):
    (o, y_in, gate_in, sq, gain, watt, wmam, tok), refs = refs[:8], refs[8:]
    if feed:
        (hid_z, dwn_z), refs = refs[2:4], refs[4:]
        (m_o, sq_o, hid_o, hid_f, dwn_f), refs = refs[:5], refs[5:]
        (lsem, f_send, f_recv), refs = refs[:3], refs[3:]
    else:
        (m_o, sq_o, hid_o), refs = refs[:3], refs[3:]
    (y, z_in, in_sem, sq_land, sq_send, sq_recv, parts, bufs, landed, c_send, c_recv) = refs
    d = lax.axis_index("dp")
    z = lax.axis_index("tensor")
    rows = tok.shape[0]

    def rows_of(q):
        return pl.ds(pl.multiple_of(q * rows, rows), rows)

    def load(q):
        at = rows_of(q)
        return [
            pltpu.make_async_copy(y_in.at[at], y.at[at], in_sem.at[0, q]),
            pltpu.make_async_copy(gate_in.at[at], z_in.at[at], in_sem.at[1, q]),
        ]

    first = jnp.where(z < nt // 2, nt - 1, 0)
    for k in range(nt):
        for copy in load(lax.rem(first + k, nt)):
            copy.start()
    peers = [(p, z) for p in cube_peers(d)] if feed else []
    greet(peers + other_quarters(d, z, nt))
    squares = Exchange(sq, sq_land, sq_send, sq_recv, d, z, nt)
    squares.start()
    n = 2 * (nt - 1)
    if feed:
        items = []
        for k in range(1, nt):
            q = lax.rem(z - k + nt, nt)
            items.append((hid_z.at[q], lambda s, q=q: hid_f.at[s, q]))
            items.append((dwn_z.at[q], lambda s, q=q: dwn_f.at[s, q]))
        cube = CubeGather(items, (0, 3, 4), f_send, f_recv, d, z)
        for i in range(n):
            cube.start(i)
        locals_ = []
        for i, (src, dst) in enumerate([(src, at(d)) for src, at in items]):
            locals_.append(pltpu.make_async_copy(src, dst, lsem.at[i]))
            locals_[-1].start()
    chain = ChainScatter(parts, bufs, landed, c_send, c_recv, d, z, nt)
    squares.wait()
    sq_o[...] = squares.total()

    def part(q):
        at = rows_of(q)
        for copy in load(q):
            copy.wait()
        total = sq_o[:, at]
        r = row_columns([lax.rsqrt(total / channels + epsilon)], rows)[:, 0:1]
        zv = z_in[at, :]
        m = (y[at, :] * (zv * sigmoid(zv)) * r * gain[...]).astype(BF16)
        m_o[at, :] = m
        parts[q] = (dot_nn(o[at, :], watt[...]) + dot_nn(m, wmam[...])).astype(BF16)

    part(first)
    chain.step(0)

    def rest(i, carry):
        part(lax.rem(first + 1 + i, nt))
        return carry

    lax.fori_loop(0, nt - 1, rest, 0)
    for t in range(1, nt - 1):
        chain.step(t)
        if feed and t == 1:
            for i in range(n):
                cube.near(i)
    if feed:
        for i in range(n):
            cube.far(i)
    chain.finish(hid_o)
    hid_o[...] += tok[...].astype(F32)
    chain.drain()
    if feed:
        cube.finish()
        for copy in locals_:
            copy.wait()


def mix_scatter(channels, nt, o, y, zr, sq, gain, watt, wmam, tok, feed=()):
    total, inner = y.shape
    rows, width = tok.shape
    dma = pltpu.SemaphoreType.DMA
    sds = jax.ShapeDtypeStruct
    vmem = pl.BlockSpec(memory_space=pltpu.VMEM)
    anywhere = pl.BlockSpec(memory_space=pl.ANY)
    outs = [sds((total, inner), BF16), sds((8, total), F32), sds((rows, width), F32)]
    scratch = []
    n = 2 * (nt - 1)
    if feed:
        for v in feed[:2]:
            outs.append(sds(v.shape, BF16))
        scratch = [dma((n,)), dma((n, 7)), dma((n, 7))]
    return pl.pallas_call(
        partial(mix_scatter_kernel, channels, nt, bool(feed)),
        in_specs=[vmem, anywhere, anywhere] + [vmem] * 5 + [anywhere] * len(feed[:2]) + [vmem] * len(feed[2:]),
        out_specs=[vmem] * 3 + [anywhere] * (len(outs) - 3),
        out_shape=outs,
        input_output_aliases={8: 3, 9: 4} if feed else {},
        scratch_shapes=scratch + [pltpu.VMEM((total, inner), F32), pltpu.VMEM((total, inner), F32),
                                  dma((2, nt)), pltpu.VMEM((nt - 1, 8, total), F32), dma((nt - 1,)), dma((nt - 1,)),
                        pltpu.VMEM((nt, rows, width), BF16)] + chain_scratch(nt, rows, width),
        compiler_params=pltpu.CompilerParams(
            vmem_limit_bytes=VMEM_LIMIT, collective_id=1, has_side_effects=True
        ),
        cost_estimate=pl.CostEstimate(flops=int(1e9), bytes_accessed=int(130e6), transcendentals=int(4e5)),
        name="mix_scatter",
    )(o, y, zr, sq, gain, watt, wmam, tok, *feed)


class ChainGather:
    def __init__(self, own, slots, send, recv, d, z, nt):
        self.own, self.slots, self.send, self.recv = own, slots, send, recv
        self.d, self.z, self.nt = d, z, nt

    def copy(self, way, dist):
        dev = (self.d, self.z + 1 if way == 0 else self.z - 1)
        slot = self.z - dist if way == 0 else self.z + dist
        src = self.own if dist == 0 else self.slots.at[slot]
        return remote_copy(src, self.slots.at[slot], self.send.at[way, dist], self.recv.at[way, dist], dev)

    def landing(self, way, dist):
        slot = self.z - dist if way == 0 else self.z + dist
        return remote_copy(
            self.slots.at[slot], self.slots.at[slot], self.send.at[way, dist - 1],
            self.recv.at[way, dist - 1], (self.d, self.z),
        )

    def has(self, way, dist):
        return self.z >= dist if way == 0 else self.z + dist < self.nt

    def goes_on(self, way):
        return self.z < self.nt - 1 if way == 0 else self.z > 0

    def start(self):
        for way in range(2):
            pl.when(self.goes_on(way))(self.copy(way, 0).start)

    def hop(self, dist):
        for way in range(2):
            pl.when(self.has(way, dist))(self.landing(way, dist).wait_recv)
            if dist < self.nt - 1:
                pl.when(self.has(way, dist) & self.goes_on(way))(self.copy(way, dist).start)

    def drain(self):
        for way in range(2):
            pl.when(self.goes_on(way))(self.copy(way, 0).wait_send)
            for dist in range(1, self.nt - 1):
                pl.when(self.has(way, dist) & self.goes_on(way))(self.copy(way, dist).wait_send)


class Unmix:
    def __init__(self, y, z_in, gain, watt, wmam, g_o, do_o, dm_o, dots, rows):
        self.ins = (y, z_in, gain, watt, wmam)
        self.outs = (g_o, do_o, dm_o, dots)
        self.rows = rows

    def __call__(self, q, g):
        y, z_in, gain, watt, wmam = self.ins
        g_o, do_o, dm_o, dots_o = self.outs
        rows = self.rows
        at = pl.ds(pl.multiple_of(q * rows, rows), rows)
        if g_o is not None:
            g_o[at, :] = g
        do_o[at, :] = dot_nt(g, watt[...]).astype(BF16)
        dm = dot_nt(g, wmam[...])
        dm_o[at, :] = dm
        zv = z_in[at, :]
        dots = jnp.sum(dm * gain[...] * (y[at, :] * (zv * sigmoid(zv))), axis=1, keepdims=True)
        turned = [jnp.broadcast_to(dots[c : c + 128], (128, 128)).T[0:8, :] for c in range(0, rows, 128)]
        dots_o[:, at] = jnp.concatenate(turned, axis=1)

    def around(self, z, dist, nt, slots, after=lambda q: None):
        def side(way, carry):
            q = jnp.where(way == 0, z - dist, z + dist)

            @pl.when((q >= 0) & (q < nt))
            def _():
                self(q, slots[q])
                after(q)

            return carry

        lax.fori_loop(0, 2, side, 0)


def unmix_gather_kernel(nt, *refs):
    (dmix, y, z_in, gain, watt, wmam), refs = refs[:6], refs[6:]
    (g_o, do_o, dm_o, dot_o), refs = refs[:4], refs[4:]
    (slots, g_send, g_recv, dot_own, dot_land, d_send, d_recv) = refs
    d = lax.axis_index("dp")
    z = lax.axis_index("tensor")
    greet(other_quarters(d, z, nt))
    chain = ChainGather(dmix, slots, g_send, g_recv, d, z, nt)
    chain.start()
    work = Unmix(y, z_in, gain, watt, wmam, g_o, do_o, dm_o, dot_own, dmix.shape[0])
    work(z, dmix[...])
    for dist in range(1, nt):
        chain.hop(dist)
        work.around(z, dist, nt, slots)
    dots = Exchange(dot_own, dot_land, d_send, d_recv, d, z, nt)
    dots.start()
    chain.drain()
    dots.wait()
    dot_o[...] = dots.total()


def unmix_shapes(total, width, inner):
    sds = jax.ShapeDtypeStruct
    return [sds((total, width), BF16), sds((total, 128), BF16), sds((total, inner), F32),
            sds((8, total), F32)]


def unmix_scratch(nt, rows, width, total):
    dma = pltpu.SemaphoreType.DMA
    return [pltpu.VMEM((nt, rows, width), BF16), dma((2, nt - 1)), dma((2, nt - 1)),
            pltpu.VMEM((8, total), F32), pltpu.VMEM((nt - 1, 8, total), F32), dma((nt - 1,)), dma((nt - 1,))]


def unmix_gather(nt, dmix, y, zr, gain, watt, wmam):
    total, inner = y.shape
    rows, width = dmix.shape
    vmem = pl.BlockSpec(memory_space=pltpu.VMEM)
    return pl.pallas_call(
        partial(unmix_gather_kernel, nt),
        in_specs=[vmem] * 6,
        out_specs=[vmem] * 4,
        out_shape=unmix_shapes(total, width, inner),
        scratch_shapes=unmix_scratch(nt, rows, width, total),
        compiler_params=pltpu.CompilerParams(
            vmem_limit_bytes=VMEM_LIMIT, collective_id=2, has_side_effects=True
        ),
        name="unmix_gather",
    )(dmix, y, zr, gain, watt, wmam)


BOXES = 4


def feed_unmix_kernel(nt, *refs):
    (hid, gain, cot, whid, wdown, y_in, gate_in, mgain, watt_in, wmam_in), refs = refs[:10], refs[10:]
    (out_o, dh_o, gg_o, g_o, do_o, dm_o, dot_o, own_o, raw_o, sum_o), refs = refs[:10], refs[10:]
    (y, z_in, watt, wmam, out, dh, dm, in_sem, out_sem, g_sem, dm_sem), refs = refs[:11], refs[11:]
    (a2, a2t, acc, dacc, fs, dgs, dus, dmix, piece, sent, came, b_send, b_recv), refs = refs[:13], refs[13:]
    boxes, refs = refs[: 8 * (nt - 2)], refs[8 * (nt - 2) :]
    (slots, g_send, g_recv, dot_own, dot_land, d_send, d_recv) = refs
    step = pl.program_id(0)
    tiles = pl.num_programs(0) // 2
    d = lax.axis_index("dp")
    z = lax.axis_index("tensor")
    core = lax.rem(d, 2)
    bits = dp_bits(d)
    peers = cube_peers(d)
    chain = ChainGather(dmix, slots, g_send, g_recv, d, z, nt)
    cubes = []
    for k in range(1, nt - 1):
        q = quarter_at(k - 1, z, nt)
        box = boxes[8 * k - 8 : 8 * k]
        cubes.append(
            SquareScatter(lambda i, j, q=q: (2 * i + j, q), piece, box[:6], box[6], box[7], peers, bits, z)
        )

    rows = hid.shape[0]
    late = [
        pltpu.make_async_copy(src, dst, in_sem.at[i])
        for i, (src, dst) in enumerate(((y_in, y), (gate_in, z_in), (watt_in, watt), (wmam_in, wmam)))
    ]

    def rows_of(q):
        return pl.ds(pl.multiple_of(q * rows, rows), rows)

    def store_g(q):
        return pltpu.make_async_copy(slots.at[q], g_o.at[rows_of(q)], g_sem.at[q])

    def store_dm(q):
        return pltpu.make_async_copy(dm.at[rows_of(q)], dm_o.at[rows_of(q)], dm_sem.at[q])

    ready = [
        pltpu.make_async_copy(src, dst, out_sem.at[i])
        for i, (src, dst) in enumerate(
            (
                (out, out_o),
                (dh, dh_o),
                (dmix, g_o.at[rows_of(z)]),
                (piece.at[:, z], own_o),
                (piece.at[:, quarter_at(2, z, nt)], raw_o),
            )
        )
    ]

    @pl.when(step == 0)
    def _():
        for copy in late:
            copy.start()
        greet([(p, z) for p in peers] + other_quarters(d, z, nt))
        feed_open(hid, gain, a2, a2t, acc, dacc)

    @pl.when(step < tiles)
    def _():
        fs[step], dgs[step], dus[step] = feed_tile(a2, cot, whid, wdown, acc, dacc)

    @pl.when(step == tiles - 1)
    def _():
        dmix[...] = feed_close(hid, gain, cot, acc, dacc, out, dh, gg_o)
        chain.start()
        for copy in ready[:3]:
            copy.start()

    units = whid.shape[4]
    quarter_units = piece.shape[2] // 3
    tiles_per = quarter_units // units

    def swap(turn_):
        box = lax.rem(turn_, BOXES)
        return remote_copy(
            sent.at[box], came.at[box], b_send.at[box], b_recv.at[box], (peers[0], z)
        )

    def places(turn_):
        quarter = quarter_at(turn_ // tiles_per, z, nt)
        part = lax.rem(turn_, tiles_per)
        return quarter, part, piece_rows(part, units, quarter_units)

    def take(turn_):
        swap(turn_).wait_recv()
        quarter, _, rows = places(turn_)
        box = lax.rem(turn_, BOXES)
        first = 0
        for row, n in rows:
            at = pl.ds(pl.multiple_of(row, 128), n)
            piece[:, quarter, at, :] = add_refs(
                piece[:, quarter, at, :], came[box, :, first : first + n, :]
            ).astype(BF16)
            first += n

    @pl.when(step >= tiles)
    def _():
        turn_ = step - tiles
        quarter, part, rows = places(turn_)
        tile = quarter * tiles_per + part
        box = lax.rem(turn_, BOXES)
        pl.when(turn_ >= BOXES)(lambda: swap(turn_ - BOXES).wait_send())
        first = 0
        for value, (row, n) in zip(feed_grads(a2t, cot, fs[tile], dgs[tile], dus[tile]), rows):
            at = pl.ds(pl.multiple_of(row, 128), n)
            value = value.reshape(value.shape[0] // 2, 2, n, 128)
            even, odd = value[:, 0], value[:, 1]
            piece[:, quarter, at, :] = jnp.where(core == 0, even, odd)
            sent[box, :, first : first + n, :] = jnp.where(core == 0, odd, even)
            first += n
        swap(turn_).start()
        pl.when(turn_ == tiles - 1)(lambda: chain.hop(1))
        pl.when(turn_ >= 1)(lambda: take(turn_ - 1))
        for k in range(1, nt - 1):
            pl.when(turn_ == k * tiles_per)(cubes[k - 1].start)

    @pl.when(step == 2 * tiles - 1)
    def _():
        take(tiles - 1)
        for i in range(BOXES):
            swap(tiles - BOXES + i).wait_send()
        for copy in ready[3:]:
            copy.start()
        for copy in late:
            copy.wait()
        work = Unmix(y, z_in, mgain, watt, wmam, None, do_o, dm, dot_own, rows)
        work(z, dmix[...])
        store_dm(z).start()

        def after(q):
            store_g(q).start()
            store_dm(q).start()

        for dist in range(1, nt):
            if dist > 1:
                chain.hop(dist)
            work.around(z, dist, nt, slots, after)
            if dist == 1:
                cubes[0].middle()
            if dist < nt - 2:
                cubes[dist].middle()
            elif dist == nt - 1:
                dots = Exchange(dot_own, dot_land, d_send, d_recv, d, z, nt)
                dots.start()
        for k, cube in enumerate(cubes):
            cube.finish(sum_o.at[k])
        chain.drain()
        for cube in cubes:
            cube.drain()
        dots.wait()
        dot_o[...] = dots.total()
        for copy in ready:
            copy.wait()
        for q in range(nt):
            store_dm(q).wait()
            pl.when(z != q)(store_g(q).wait)


def feed_unmix(nt, hid, gain, cot, whid, wdown, y, zr, mgain, watt, wmam):
    rows, width = hid.shape
    total, inner = y.shape
    blocks, _, _, depth, units = whid.shape
    tile = 256
    per = units // tile
    tiles = nt * per
    kept = blocks // 2
    n = 3 * units
    dma = pltpu.SemaphoreType.DMA
    sds = jax.ShapeDtypeStruct

    def fixed(v):
        return pl.BlockSpec(v.shape, lambda i: (0,) * len(v.shape), pipeline_mode=pl.Buffered(1))

    def at_tile(i):
        return jnp.minimum(i, tiles - 1)

    hid_spec = pl.BlockSpec(
        (blocks, 1, 2, depth, tile), lambda i: (0, at_tile(i) // per, 0, 0, lax.rem(at_tile(i), per))
    )
    down_spec = pl.BlockSpec(
        (blocks, 1, tile, 128), lambda i: (0, at_tile(i) // per, lax.rem(at_tile(i), per), 0)
    )
    out_shape = [sds((rows, width), BF16), sds((rows, width), F32), sds((1, width), F32)]
    out_shape += unmix_shapes(total, width, inner)
    out_shape += [sds((kept, n, 128), BF16), sds((kept, n, 128), BF16), sds((nt - 2, n, 128), BF16)]
    anywhere = pl.BlockSpec(memory_space=pl.ANY)
    late = [pltpu.VMEM(v.shape, v.dtype) for v in (y, zr, watt, wmam) + tuple(out_shape[:2])]
    late += [pltpu.VMEM((total, inner), F32), dma((4,)), dma((5,)), dma((nt,)), dma((nt,))]
    box = pltpu.VMEM((BOXES, kept, 3 * tile, 128), BF16)
    kept_tile = pltpu.VMEM((tiles, rows, tile), BF16)
    scratch = [pltpu.VMEM((rows, width), BF16), pltpu.VMEM((width, rows), BF16),
               pltpu.VMEM((rows, width), F32), pltpu.VMEM((rows, width), F32), kept_tile, kept_tile, kept_tile,
               pltpu.VMEM((rows, width), BF16), pltpu.VMEM((kept, nt, n, 128), BF16), box, box, dma((BOXES,)),
               dma((BOXES,))]
    for _ in range(nt - 2):
        scratch += square_scratch(n, 128)
    return pl.pallas_call(
        partial(feed_unmix_kernel, nt),
        grid=(2 * tiles,),
        in_specs=[fixed(hid), fixed(gain), fixed(cot), hid_spec, down_spec, anywhere, anywhere, fixed(mgain),
                  anywhere, anywhere],
        out_specs=[anywhere if i in (0, 1, 3, 5, 7, 8) else fixed(v) for i, v in enumerate(out_shape)],
        out_shape=out_shape,
        scratch_shapes=late + scratch + unmix_scratch(nt, rows, width, total),
        compiler_params=pltpu.CompilerParams(
            vmem_limit_bytes=60 * 1024 * 1024, collective_id=4, has_side_effects=True
        ),
        cost_estimate=pl.CostEstimate(flops=int(1e10), bytes_accessed=int(150e6), transcendentals=int(9e5)),
        name="feed_unmix",
    )(hid, gain, cot, whid, wdown, y, zr, mgain, watt, wmam)


def add_refs(left, right):
    return left.astype(F32) + right.astype(F32)


class SquareScatter:
    def __init__(self, place, held, bufs, send, recv, peers, bits, z):
        (self.r1, self.r2, self.ob, self.tb, self.r3, self.r4) = bufs
        self.place, self.held = place, held
        n = held.shape[-2]
        half = n // 2
        self.lo, self.hi = pl.ds(0, half), pl.ds(half, n - half)
        self.half = half
        _, self.x, self.y = bits
        x, y = self.x, self.y
        _, d_x, d_y = peers
        self.copies = []
        for i in range(2):
            self.copies.append(
                remote_copy(held.at[place(i, 1 - x) + (self.lo,)], self.r1.at[i], send.at[i], recv.at[i],
                            (d_x, z))
            )
        for j in range(2):
            self.copies.append(
                remote_copy(held.at[place(1 - y, j) + (self.hi,)], self.r2.at[j], send.at[2 + j],
                            recv.at[2 + j], (d_y, z))
            )
        self.copies.append(remote_copy(self.ob.at[1 - y], self.r3, send.at[4], recv.at[4], (d_y, z)))
        self.copies.append(remote_copy(self.tb.at[1 - x], self.r4, send.at[5], recv.at[5], (d_x, z)))

    def start(self):
        for copy in self.copies[:4]:
            copy.start()

    def middle(self):
        for i in range(2):
            self.copies[i].wait_recv()
            self.ob[i] = add_refs(self.held[self.place(i, self.x) + (self.lo,)], self.r1[i]).astype(BF16)
        self.copies[4].start()
        for j in range(2):
            self.copies[2 + j].wait_recv()
            self.tb[j] = add_refs(self.held[self.place(self.y, j) + (self.hi,)], self.r2[j]).astype(BF16)
        self.copies[5].start()

    def finish(self, out):
        self.copies[4].wait_recv()
        out[0 : self.half] = add_refs(self.ob[self.y], self.r3[...]).astype(out.dtype)
        self.copies[5].wait_recv()
        out[self.half :] = add_refs(self.tb[self.x], self.r4[...]).astype(out.dtype)

    def drain(self):
        for copy in self.copies:
            copy.wait_send()


def square_scratch(n, lanes):
    dma = pltpu.SemaphoreType.DMA
    half = n // 2
    return [
        pltpu.VMEM((2, half, lanes), BF16),
        pltpu.VMEM((2, n - half, lanes), BF16),
        pltpu.VMEM((2, half, lanes), BF16),
        pltpu.VMEM((2, n - half, lanes), BF16),
        pltpu.VMEM((half, lanes), BF16),
        pltpu.VMEM((n - half, lanes), BF16),
        dma((6,)),
        dma((6,)),
    ]


class CubeScatter:
    def __init__(self, pieces, bufs, peers, bits, z):
        (self.rc, self.held, self.send, self.recv) = bufs[:4]
        self.p = pieces
        self.core = bits[0]
        self.peer = (peers[0], z)
        self.square = SquareScatter(
            lambda i, j: (2 * i + j,), self.held, bufs[4:10], bufs[10], bufs[11], peers, bits, z
        )

    def swap(self, i):
        return remote_copy(
            self.p.at[i, 1 - self.core], self.rc.at[i], self.send.at[i], self.recv.at[i], self.peer
        )

    def middle(self):
        for i in range(4):
            self.swap(i).wait_recv()
            self.held[i] = add_refs(self.p[i, self.core], self.rc[i]).astype(BF16)
        self.square.start()

    def last(self):
        self.square.middle()

    def finish(self, out):
        self.square.finish(out)

    def drain(self):
        for i in range(4):
            self.swap(i).wait_send()
        self.square.drain()


def cube_scratch(n, lanes):
    dma = pltpu.SemaphoreType.DMA
    return [
        pltpu.VMEM((4, n, lanes), BF16),
        pltpu.VMEM((4, n, lanes), BF16),
        dma((4,)),
        dma((4,)),
    ] + square_scratch(n, lanes)


class CubeTotal:
    def __init__(self, held, landed, send, recv, peers, z):
        self.held, self.landed = held, landed
        self.copies = [
            remote_copy(held.at[i], landed.at[i], send.at[i], recv.at[i], (peer, z))
            for i, peer in enumerate(peers)
        ]

    def start(self, i):
        self.copies[i].start()

    def take(self, i):
        self.copies[i].wait_recv()
        self.held[i + 1] = self.held[i] + self.landed[i]

    def drain(self):
        for copy in self.copies:
            copy.wait_send()


def norm_back(dy, v, gain, dh):
    f = lax.rsqrt(jnp.mean(v * v, axis=1, keepdims=True) + epsilon)
    gdy = dy * gain
    lean = jnp.sum(gdy * v, axis=1, keepdims=True) * (f * f * f / v.shape[1])
    return dh + (f * gdy - v * lean)


SMALL_ALL = 32
SMALL_ROWS = 160


def tail_kernel(
    nt, tok_in, gain, dh_in, a1_in, dmix_in, o_in, m_in, dq, dz, dx, dkv, db, drow, wq, win, stp, wsh,
    gg, gtb, gtx, grows, gheads, own_in, rest_in,
    gt_o, mixed_o, fed_o, sh_o, small_o,
    feed_own, a1, o, m, dmix, feed_rest, tok, dh, lsem,
    da, gone, parts, pieces, shared, ot, mt, bufs, landed, c_send, c_recv, *rest,
):
    cube_a, rest = rest[:12], rest[12:]
    cube_b, rest = rest[:12], rest[12:]
    square_c, rest = rest[:8], rest[8:]
    (sh_sum, sh_land, sh_send, sh_recv) = rest[:4]
    (sm_held, sm_land, sm_send, sm_recv, all_own, all_land, all_send, all_recv) = rest[4:]
    d = lax.axis_index("dp")
    z = lax.axis_index("tensor")
    bits = dp_bits(d)
    peers = cube_peers(d)
    rows = tok.shape[0]
    late = [
        pltpu.make_async_copy(src, dst, lsem.at[i])
        for i, (src, dst) in enumerate(
            [(own_in, feed_own), (a1_in, a1), (o_in, o), (m_in, m), (dmix_in, dmix), (rest_in, feed_rest),
             (tok_in, tok), (dh_in, dh)]
        )
    ]
    for copy in late:
        copy.start()
    greet([(p, z) for p in peers] + other_quarters(d, z, nt))
    three = SquareScatter(
        lambda i, j: (i, j), feed_own, square_c[:6], square_c[6], square_c[7], peers, bits, z
    )
    chain = ChainScatter(parts, bufs, landed, c_send, c_recv, d, z, nt)

    def part(q):
        at = pl.ds(pl.multiple_of(q * rows, rows), rows)
        parts[q] = down_rows(at, dq, dz, dx, dkv, db, drow, wq, win, stp, wsh).astype(BF16)

    first = jnp.where(z < nt // 2, nt - 1, 0)
    part(first)
    chain.step(0)

    def others(i, carry):
        part(lax.rem(first + 1 + i, nt))
        return carry

    late[0].wait()
    three.start()
    lax.fori_loop(0, nt - 1, others, 0)
    for copy in late[1:5]:
        copy.wait()
    gone[...] = jnp.zeros(gone.shape, F32)

    def gain_sums(q, carry):
        at = pl.ds(pl.multiple_of(q * rows, rows), rows)
        gone[...] += jnp.sum(parts[q].astype(F32) * a1[at, :].astype(F32), axis=0, keepdims=True)
        return carry

    lax.fori_loop(0, nt, gain_sums, 0)
    gone[...] = gone[...] / gain[...]
    sums = CubeTotal(sm_held, sm_land, sm_send, sm_recv, peers, z)
    for k in range(8):
        sm_held[0, k : k + 1, :] = gg[:, 128 * k : 128 * k + 128]
        sm_held[0, 24 + k : 25 + k, :] = gone[:, 128 * k : 128 * k + 128]
    for first_row, ref in ((8, gtb), (SMALL_ALL, gtx), (56, grows)):
        for k in range(ref.shape[1] // 128):
            sm_held[0, first_row + 8 * k : first_row + 8 * k + 8, :] = ref[:, 128 * k : 128 * k + 128]
    sm_held[0, 80:96, :] = gheads[...]
    steps = dot_nn(drow[...].astype(BF16), a1[...])
    for k in range(8):
        sm_held[0, 96 + 8 * k : 104 + 8 * k, :] = steps[:, 128 * k : 128 * k + 128]
    sums.start(0)
    ot[...] = o[...].T
    mt[...] = m[...].T

    def columns(i, carry):
        at = pl.ds(pl.multiple_of(i * 256, 256), 256)

        def put(k, first, values):
            pieces[i, k, first : first + values.shape[0], :] = values

        def put_shared(k, first, values):
            shared[i, k, :, first : first + values.shape[1]] = values

        weight_columns(a1[:, at], dmix[:, at], dq, dz, dx, dkv, db, ot, mt, put, put_shared)
        two.swap(i).start()
        one.swap(i).start()
        return carry

    one = CubeScatter(pieces, cube_a, peers, bits, z)
    two = CubeScatter(shared, cube_b, peers, bits, z)
    lax.fori_loop(0, 1, columns, 0)
    chain.step(1)
    three.middle()
    sums.take(0)
    sums.start(1)
    lax.fori_loop(1, 4, columns, 0)
    sums.take(1)
    sums.start(2)
    two.middle()
    one.middle()
    for t in range(2, nt - 1):
        chain.step(t)
    two.last()
    one.last()
    sums.take(2)
    all_own[...] = sm_held[3, 0:SMALL_ALL, :]
    over_all = Exchange(all_own, all_land, all_send, all_recv, d, z, nt)
    over_all.start()
    three.finish(fed_o)
    for copy in late[5:]:
        copy.wait()
    fed_o[...] += feed_rest[...]
    two.finish(sh_sum)
    per = sh_sum.shape[0] // nt
    copies = []
    for k in range(1, nt):
        q = lax.rem(z + k, nt)
        at = pl.ds(pl.multiple_of(q * per, per), per)
        copies.append(
            remote_copy(sh_sum.at[at], sh_land.at[k - 1], sh_send.at[k - 1], sh_recv.at[k - 1], (d, q))
        )
        copies[-1].start()
    one.finish(mixed_o)
    small_o[...] = sm_held[3]
    over_all.wait()
    small_o[0:SMALL_ALL, :] = over_all.total()
    for copy in copies:
        copy.wait()
    total = sh_sum[pl.ds(pl.multiple_of(z * per, per), per), :].astype(F32)
    for k in range(nt - 1):
        total = total + sh_land[k].astype(F32)
    sh_o[...] = total
    chain.finish(da)
    gt_o[...] = norm_back(da[...], tok[...].astype(F32), gain[...], dh[...]).astype(BF16)
    for thing in (chain, one, two, three, sums):
        thing.drain()


def tail(nt, *args):
    tok, a1, dz = args[0], args[3], args[8]
    feed_own = args[-2]
    rows, width = tok.shape
    total = a1.shape[0]
    inner = dz.shape[1]
    n, lanes = 256 + 3 * inner, 128
    s_rows, s_lanes = 128, args[16].shape[1]
    f_rows = feed_own.shape[2]
    late = (len(args) - 2, 3, 5, 6, 4, len(args) - 1, 0, 2)
    dma = pltpu.SemaphoreType.DMA
    sds = jax.ShapeDtypeStruct
    vmem = pl.BlockSpec(memory_space=pltpu.VMEM)
    return pl.pallas_call(
        partial(tail_kernel, nt),
        in_specs=[pl.BlockSpec(memory_space=pl.ANY) if i in late else vmem for i in range(len(args))],
        out_specs=[vmem] * 5,
        out_shape=[sds((rows, width), BF16), sds((n, lanes), F32), sds((f_rows, 128), F32),
                   sds((s_rows // nt, s_lanes), F32), sds((SMALL_ROWS, 128), F32)],
        scratch_shapes=[pltpu.VMEM(args[i].shape, args[i].dtype) for i in late] + [dma((len(late),))]
        + [pltpu.VMEM((rows, width), F32), pltpu.VMEM((1, width), F32), pltpu.VMEM((nt, rows, width), BF16),
                        pltpu.VMEM((4, 2, n, lanes), BF16), pltpu.VMEM((4, 2, s_rows, s_lanes), BF16),
                        pltpu.VMEM((128, total), BF16), pltpu.VMEM((inner, total), BF16)]
        + chain_scratch(nt, rows, width)
        + cube_scratch(n, lanes) + cube_scratch(s_rows, s_lanes) + square_scratch(f_rows, 128)
        + [pltpu.VMEM((s_rows, s_lanes), BF16), pltpu.VMEM((nt - 1, s_rows // nt, s_lanes), BF16),
           dma((nt - 1,)), dma((nt - 1,)),
           pltpu.VMEM((4, SMALL_ROWS, 128), F32), pltpu.VMEM((3, SMALL_ROWS, 128), F32), dma((3,)), dma((3,)),
           pltpu.VMEM((SMALL_ALL, 128), F32), pltpu.VMEM((nt - 1, SMALL_ALL, 128), F32), dma((nt - 1,)),
           dma((nt - 1,))],
        compiler_params=pltpu.CompilerParams(
            vmem_limit_bytes=VMEM_LIMIT, collective_id=3, has_side_effects=True
        ),
        cost_estimate=pl.CostEstimate(flops=int(7e9), bytes_accessed=int(150e6), transcendentals=0),
        name="tail",
    )(*args)


def finish_kernel(
    heads, place, mixed, fed, small, *refs
):
    (que_o, att_o, inn_o, mam_o, hid_o, dwn_o, norms_o, taps_o, chan_o, gain_o, step_o) = refs[-17:-6]
    heads_o = refs[-6:-3]
    for src, dst in zip(refs[:3], refs[-3:]):
        dst[...] = src[...]
    d, p = place[0], place[1]
    block = que_o.shape[0]
    inner = mam_o.shape[0]
    first = 0
    for j in range(que_o.shape[1] // 128):
        que_o[:, 128 * j : 128 * j + 128] = mixed[first : first + block]
        first += block
    att_o[...] = mixed[first : first + att_o.shape[0]]
    first += att_o.shape[0]
    for i in range(2):
        for j in range(inner // 128):
            inn_o[i, :, 128 * j : 128 * j + 128] = mixed[first : first + block]
            first += block
    mam_o[...] = mixed[first : first + inner]
    first = 0
    for i in range(2):
        for j in range(hid_o.shape[2] // 128):
            hid_o[i, :, 128 * j : 128 * j + 128] = fed[first : first + block]
            first += block
    dwn_o[...] = fed[first:]

    def lanes_from(values, lane):
        return pltpu.roll(values, lax.rem(128 - lane, 128), 1)

    width = norms_o.shape[1]
    per = 128 // width
    for i, base in enumerate((24, 0)):
        row = jnp.broadcast_to(small[pl.ds(base + p // per, 1), :], (8, 128))
        row = lanes_from(row, lax.rem(p, per) * width)
        norms_o[i : i + 1, :] = row[0:1, 0:width]
    width = taps_o.shape[1]
    per = 128 // width
    row = small[pl.ds(pl.multiple_of(8 + 8 * (p // per), 8), 8), :]
    taps_o[...] = lanes_from(row, lax.rem(p, per) * width)[0 : CONV + 1, 0:width]
    width = gain_o.shape[1]
    sums = jnp.zeros((8, 128), F32)
    lane = lanes_of(sums.shape)
    sub = lax.broadcasted_iota(jnp.int32, sums.shape, 0)
    for b in range(heads // 2):
        rows = lanes_from(small[SMALL_ALL + 8 * b : SMALL_ALL + 8 * b + 8, :], d * width)
        raw = small[56 + 8 * b : 64 + 8 * b, :]
        gains = lanes_from(raw, d * width)
        for k in range(2):
            h = 2 * b + k
            at = slice(64 * k, 64 * k + width)
            chan_o[:, h, :] = rows[0 : CONV + 1, at]
            gain_o[h : h + 1, :] = gains[0:1, at]
            skip = jnp.sum(jnp.where(lane // SSM_DIM == k, raw[1:2, :], 0.0), axis=1, keepdims=True)
            sums = jnp.where((sub == h) & (lane == 2), skip, sums)
    for k in range(2):
        total = jnp.sum(small[80 + 8 * k : 88 + 8 * k, :], axis=1, keepdims=True)
        sums = jnp.where(lane == k, total, sums)
    sums = jnp.concatenate([sums, jnp.zeros((120, 128), F32)], axis=0).T
    for k in range(3):
        heads_o[k][...] = sums[k : k + 1, 0:heads]
    steps = small[pl.ds(pl.multiple_of(96 + 8 * d, 8), 8), :]
    step_o[...] = steps[0:heads, :]


def finish(heads, place, mixed, fed, small, shapes, passed):
    vmem = pl.BlockSpec(memory_space=pltpu.VMEM)
    sds = jax.ShapeDtypeStruct
    return pl.pallas_call(
        partial(finish_kernel, heads),
        in_specs=[pl.BlockSpec(memory_space=pltpu.SMEM)] + [vmem] * 6,
        out_specs=[vmem] * (len(shapes) + 6),
        out_shape=[sds(s, F32) for s in shapes] + [sds((1, heads), F32)] * 3
        + [sds(v.shape, v.dtype) for v in passed],
        compiler_params=pltpu.CompilerParams(vmem_limit_bytes=VMEM_LIMIT),
        name="finish",
    )(place, mixed, fed, small, *passed)


def rope_wide(length):
    half = HEAD_SIZE // 2
    inverse = rope_base ** (-np.arange(half) * (2.0 / HEAD_SIZE))
    angles = np.arange(length)[:, None] * inverse[None, :]
    c, s = np.cos(angles), np.sin(angles)
    return (
        jnp.asarray(np.concatenate([c, c, c, c], axis=1), F32),
        jnp.asarray(np.concatenate([-s, s, -s, s], axis=1), F32),
    )


def to_blocks(full, axis, nt):
    if axis == 1:
        two, width, cols = full.shape
        return full.reshape(2, 8, width // 8, nt, cols // nt).transpose(1, 3, 0, 2, 4)
    rows, width = full.shape
    return full.reshape(nt, rows // nt, 8, width // 8).transpose(2, 0, 1, 3)


def per_device(
    nd,
    nt,
    tokens,
    query_proj,
    attend_out,
    inner_proj,
    step_proj,
    mamba_out,
    hidden_proj,
    down_proj,
    channel_taps,
    mixer_gain,
    decay_log,
    step_bias,
    skip_weight,
    shared_proj,
    norm_gains,
    shared_taps,
    cotangent,
):
    tensor_index = lax.axis_index("tensor")
    d = lax.axis_index("dp")
    local_rows, width = tokens.shape
    group_rows = local_rows * nt
    heads = step_proj.shape[1]
    inner = heads * SSM_DIM
    channels = inner * nt
    units = down_proj.shape[0]
    feed = ()
    if nd == 8:
        small = pack_small(channel_taps, mixer_gain, norm_gains, shared_taps, step_proj.T)
        (tok_full, full_query, full_attend, full_inner, full_mamba, sha, sma) = gather_start(
            tokens, query_proj, attend_out, inner_proj, mamba_out, shared_proj, small, nd, nt
        )
        scal = jnp.stack([decay_log, step_bias, skip_weight]).astype(F32)
        where = tensor_index.astype(jnp.int32).reshape(1)
        (
            gain_first, gain_second, gain_mix, taps_x, taps_b, step_rows, decay, bias, skip,
        ) = unpack_small(heads, where, scal, sma, width)
        full_shared = sha.reshape(width, -1)
        feed = (hidden_proj, down_proj)
    else:
        small_parts = [channel_taps, mixer_gain, norm_gains, shared_taps, step_proj.T]
        flat = jnp.concatenate([p.reshape(-1) for p in small_parts])
        small_len = -(-flat.shape[0] // 2048) * 2048
        small = jnp.pad(flat, (0, small_len - flat.shape[0])).reshape(-1, 128)
        (tok_full, full_query, full_attend, full_inner, full_mamba, sha, sma) = gather_start(
            tokens, query_proj, attend_out, inner_proj, mamba_out, shared_proj, small, nd, nt
        )
        full_hidden = lax.all_gather(hidden_proj, "tensor", axis=2, tiled=True)
        full_hidden = to_blocks(lax.all_gather(full_hidden, "dp", axis=1, tiled=True), 1, nt)
        full_down = lax.all_gather(down_proj, "tensor", axis=0, tiled=True)
        full_down = to_blocks(lax.all_gather(full_down, "dp", axis=1, tiled=True), 0, nt)

        full_shared = sha.reshape(width, -1)
        sma = sma.reshape(nd, nt, small_len)

        def small_piece(index):
            start = sum(p.size for p in small_parts[:index])
            part = small_parts[index]
            return sma[:, :, start : start + part.size].reshape((nd, nt) + part.shape)

        taps_x = pick(small_piece(0), tensor_index, 1).transpose(1, 2, 0, 3).reshape(CONV + 1, inner)
        gain_mix = pick(small_piece(1), tensor_index, 1).transpose(1, 0, 2).reshape(1, inner)
        full_norms = small_piece(2).transpose(2, 0, 1, 3).reshape(2, width).astype(F32)
        taps_b = small_piece(3).transpose(2, 0, 1, 3).reshape(CONV + 1, -1)
        step_rows = pick(small_piece(4), tensor_index, 1).transpose(1, 0, 2).reshape(heads, width)
        step_rows = jnp.pad(step_rows, ((0, 8 - heads), (0, 0)))
        taps_x = jnp.pad(taps_x.astype(F32), ((0, 7 - CONV), (0, 0)))
        taps_b = jnp.pad(taps_b.astype(F32), ((0, 7 - CONV), (0, 0)))
        gain_mix = gain_mix.astype(F32)
        gain_first = full_norms[0:1]
        gain_second = full_norms[1:2]

        def head_rows(values):
            return jnp.pad(jnp.broadcast_to(values[:, None], (heads, 128)), ((0, 8 - heads), (0, 0)))

        decay = head_rows(-jnp.exp(decay_log.astype(F32)))
        bias = head_rows(step_bias.astype(F32))
        skip = jnp.repeat(skip_weight.astype(F32), SSM_DIM)[None, :]
    q_heads = query_proj.shape[1] // HEAD_SIZE
    kv_head = (tensor_index * q_heads // (QHEADS // KVHEADS)).astype(jnp.int32).reshape(1)
    cosine, sine = rope_wide(group_rows)

    (a1, q, k2, v2, lse, o, xr, zr, br, y, trow, states, squares, *feed) = mixers_forward(
        heads, nt, kv_head, tok_full.reshape(group_rows, width), gain_first, full_query, full_inner, step_rows,
        full_shared, cosine, sine, taps_x, taps_b, decay, bias, skip, feed,
    )
    mixed = mix_scatter(
        channels, nt, o, y, zr, squares, gain_mix, full_attend, full_mamba, tokens, tuple(feed)
    )
    m, squares, hidden = mixed[:3]
    if nd == 8:
        full_hidden, full_down = mixed[3:]
    if nd == 8:
        layer_out, dh, grad_gain_two, grad_mix, do, dm, dots, feed_own, feed_raw, feed_sums = feed_unmix(
            nt, hidden, gain_second, cotangent, full_hidden, full_down, y, zr, gain_mix, full_attend, full_mamba
        )
        feed_own = feed_own.reshape((2, 2) + feed_own.shape[1:])
    else:
        layer_out, dh, dmix, grad_gain_two, feed_pieces = feed_forward(
            hidden, gain_second, cotangent, full_hidden, full_down
        )
        grad_mix, do, dm, dots = unmix_gather(nt, dmix, y, zr, gain_mix, full_attend, full_mamba)
        hid_full = feed_pieces[:, :, : 2 * units].reshape(8, nt, 2, units // 128, width // 8, 128)
        hid_full = hid_full.transpose(2, 0, 4, 1, 3, 5).reshape(2, nd, width // nd, nt, units)
        hid_sum = cube_scatter(hid_full.transpose(1, 3, 0, 2, 4), nd, BF16)
        down_full = feed_pieces[:, :, 2 * units :].transpose(1, 2, 0, 3)
        down_full = down_full.reshape(nt, units, nd, width // nd)
        down_sum = cube_scatter(down_full.transpose(2, 0, 1, 3), nd, BF16)
        gradient_hidden = chain_scatter(hid_sum, nt)
        gradient_down = chain_scatter(down_sum, nt)

    back = mixers_back(
        heads, channels, nt, kv_head, q, k2, v2, lse, do, cosine, sine, dm, y, zr, xr, br, trow, states,
        squares, dots, gain_mix, taps_x, taps_b, decay, bias, skip,
        (feed_sums, feed_raw) if nd == 8 else None,
    )
    dq, dkv, dz, dx, db, drow, grad_tx, grad_tb, grad_rows, grad_heads = back[:10]
    if nd == 8:
        sums = tail(
            nt, tokens, gain_first, dh, a1, grad_mix, o, m, dq, dz, dx, dkv, db, drow, full_query, full_inner,
            step_rows, full_shared, grad_gain_two, grad_tb, grad_tx, grad_rows, grad_heads, feed_own, back[10],
        )
        gradient_tokens, mixed, fed, gradient_shared, small_sums = sums
        place = jnp.stack([d, d * nt + tensor_index]).astype(jnp.int32)
        shapes = [
            query_proj.shape, attend_out.shape, inner_proj.shape, mamba_out.shape, hidden_proj.shape,
            down_proj.shape, norm_gains.shape, shared_taps.shape, channel_taps.shape, mixer_gain.shape,
            step_proj.T.shape,
        ]
        (
            gradient_query,
            gradient_attend,
            gradient_inner,
            gradient_mamba,
            gradient_hidden,
            gradient_down,
            gradient_norms,
            gradient_taps,
            gradient_channel,
            gradient_mixer,
            gradient_step,
            gradient_decay,
            gradient_bias,
            gradient_skip,
            layer_out,
            gradient_tokens,
            gradient_shared,
        ) = finish(
            heads, place, mixed, fed, small_sums, shapes, (layer_out, gradient_tokens, gradient_shared)
        )
        return (
            layer_out,
            gradient_tokens,
            gradient_query,
            gradient_attend,
            gradient_inner,
            gradient_step.T,
            gradient_mamba,
            gradient_hidden,
            gradient_down,
            gradient_channel,
            gradient_mixer,
            gradient_decay.reshape(heads),
            gradient_bias.reshape(heads),
            gradient_skip.reshape(heads),
            gradient_shared,
            gradient_norms,
            gradient_taps,
        )

    part_one = down_parts(dq, dz, dx, dkv, db, drow, full_query, full_inner, step_rows, full_shared)
    pieces, shared_pieces, grad_step = weight_pieces(a1, dq, dz, dx, dkv, db, drow, o, m, grad_mix)
    block = width // nd
    q_cols = query_proj.shape[1]
    cuts = [0, q_cols, q_cols + attend_out.shape[0]]
    cuts += [cuts[2] + inner, cuts[2] + 2 * inner, cuts[2] + 3 * inner]

    def from_rows(values):
        return values.reshape(8, -1, 128, 128).transpose(0, 2, 1, 3).reshape(width, -1)

    def from_lanes(values):
        return values.transpose(1, 0, 2).reshape(-1, width)

    n_tap = CONV + 1
    over_all = jnp.concatenate([grad_gain_two.reshape(-1), grad_tb[:n_tap].reshape(-1)])
    over_dp = jnp.concatenate(
        [
            grad_tx[:n_tap].reshape(-1),
            grad_rows[0],
            grad_rows[1].reshape(heads, SSM_DIM).sum(axis=1),
            grad_heads[:heads].sum(axis=1),
            grad_heads[8 : 8 + heads].sum(axis=1),
            grad_step[:heads].reshape(-1),
        ]
    )

    def in_rows(values):
        return jnp.pad(values, (0, -values.shape[0] % 1024)).reshape(-1, 128)

    rows_all = in_rows(over_all)
    n_all = rows_all.shape[0]
    small_sums = jnp.concatenate([rows_all, in_rows(over_dp)], axis=0)
    parts = part_one.reshape(nt, local_rows, width)
    token_f32 = tokens.astype(F32)
    _, norm_one_back = jax.vjp(norm_apply, token_f32, gain_first[0])
    grad_from_one, grad_gain_one = norm_one_back(chain_scatter(parts, nt))
    gradient_tokens = (dh + grad_from_one).astype(BF16)
    got = [pieces[:, cuts[i] : cuts[i + 1]] for i in range(5)]

    def over_rows(values):
        return cube_scatter(from_rows(values).reshape(nd, block, -1), nd)

    def over_lanes(values):
        return cube_scatter(from_lanes(values).reshape(-1, nd, block).transpose(1, 0, 2), nd)

    gradient_query = over_rows(got[0])
    gradient_attend = over_lanes(got[1])
    gradient_inner = jnp.stack([over_rows(got[2]), over_rows(got[3])])
    gradient_mamba = over_lanes(got[4])
    shared_cut = shared_pieces.reshape(nd, nt, width // (nd * nt), -1)
    gradient_shared = chain_scatter(cube_scatter(shared_cut, nd, BF16), nt)
    small_sums = lax.psum(small_sums, "dp")
    small_sums = jnp.concatenate(
        [lax.psum(small_sums[:n_all], "tensor"), small_sums[n_all:]], axis=0
    )
    grad_gain_one = lax.psum(grad_gain_one, ("dp", "tensor")).reshape(1, width)
    over_all = small_sums[:n_all].reshape(-1)
    over_dp = small_sums[n_all:].reshape(-1)
    place = d * nt + tensor_index
    norm_w = width // (nd * nt)
    both_norms = jnp.concatenate([grad_gain_one, over_all[:width].reshape(1, width)], axis=0)
    gradient_norms = lax.dynamic_slice_in_dim(both_norms, place * norm_w, norm_w, 1)
    tap_w = shared_taps.shape[1]
    tap_all = over_all[width : width + n_tap * taps_b.shape[1]].reshape(n_tap, -1)
    gradient_taps = lax.dynamic_slice_in_dim(tap_all, place * tap_w, tap_w, 1)
    part = mixer_gain.shape[1]
    n_taps = n_tap * inner
    chan = over_dp[:n_taps].reshape(n_tap, heads, SSM_DIM)
    gain = over_dp[n_taps : n_taps + inner].reshape(heads, SSM_DIM)
    gradient_channel = lax.dynamic_slice_in_dim(chan, d * part, part, 2)
    gradient_mixer = lax.dynamic_slice_in_dim(gain, d * part, part, 1)
    rest = over_dp[n_taps + inner :]
    gradient_skip = rest[:heads]
    gradient_decay = rest[heads : 2 * heads]
    gradient_bias = rest[2 * heads : 3 * heads]
    step_all = rest[3 * heads : 3 * heads + heads * width].reshape(heads, width)
    gradient_step = lax.dynamic_slice_in_dim(step_all, d * block, block, 1).T
    return (
        layer_out,
        gradient_tokens,
        gradient_query,
        gradient_attend,
        gradient_inner,
        gradient_step,
        gradient_mamba,
        gradient_hidden,
        gradient_down,
        gradient_channel,
        gradient_mixer,
        gradient_decay,
        gradient_bias,
        gradient_skip,
        gradient_shared,
        gradient_norms,
        gradient_taps,
    )


def solution(mesh):
    placed = (
        P(("dp", "tensor"), None),
        P("dp", "tensor"),
        P("tensor", "dp"),
        P(None, "dp", "tensor"),
        P("dp", "tensor"),
        P("tensor", "dp"),
        P(None, "dp", "tensor"),
        P("tensor", "dp"),
        P(None, "tensor", "dp"),
        P("tensor", "dp"),
        P("tensor"),
        P("tensor"),
        P("tensor"),
        P(("dp", "tensor"), None),
        P(None, ("dp", "tensor")),
        P(None, ("dp", "tensor")),
        P(("dp", "tensor"), None),
    )
    return jax.shard_map(
        partial(per_device, mesh.shape["dp"], mesh.shape["tensor"]),
        mesh=mesh,
        in_specs=placed,
        out_specs=(
            P(("dp", "tensor"), None),
            P(("dp", "tensor"), None),
            P("dp", "tensor"),
            P("tensor", "dp"),
            P(None, "dp", "tensor"),
            P("dp", "tensor"),
            P("tensor", "dp"),
            P(None, "dp", "tensor"),
            P("tensor", "dp"),
            P(None, "tensor", "dp"),
            P("tensor", "dp"),
            P("tensor"),
            P("tensor"),
            P("tensor"),
            P(("dp", "tensor"), None),
            P(None, ("dp", "tensor")),
            P(None, ("dp", "tensor")),
        ),
        check_vma=False,
    )
```

```python
from functools import partial

import numpy as np
import jax
import jax.numpy as jnp
from jax import lax
from jax.experimental import pallas as pl
from jax.experimental.pallas import tpu as pltpu
from jax.sharding import PartitionSpec as P

MESH = pl.DeviceIdType.MESH

QHEADS = 8
KVHEADS = 2
HEAD_SIZE = 64
SSM_DIM = 64
CONV = 4


epsilon = 1e-05
rope_base = 100000000000.0
neg_large = -1e30
block_len = 128


def norm_apply(values, gain):
    factor = lax.rsqrt(jnp.mean(values * values, axis=-1, keepdims=True) + epsilon)
    return values * factor * gain


def dp_bits(index):
    core = lax.rem(index, 2)
    xbit = lax.rem(index // 2, 2)
    ybit = lax.rem(index // 4, 2)
    return core, xbit, ybit


def remote_copy(src, dst, send, recv, dev):
    return pltpu.make_async_remote_copy(
        src_ref=src, dst_ref=dst, send_sem=send, recv_sem=recv, device_id=dev, device_id_type=MESH
    )


def greet(peers):
    barrier = pltpu.get_barrier_semaphore()
    for peer in peers:
        pl.semaphore_signal(barrier, inc=1, device_id=peer, device_id_type=MESH)
    pl.semaphore_wait(barrier, len(peers))


def other_quarters(d, z, nt):
    return [(d, lax.rem(z + k, nt)) for k in range(1, nt)]


def cube_peers(d):
    core, xbit, ybit = dp_bits(d)
    return d + 1 - 2 * core, d + 2 - 4 * xbit, d + 4 - 8 * ybit


class CubeGather:
    def __init__(self, items, via_y, send, recv, d, z):
        self.items, self.via_y, self.send, self.recv = items, via_y, send, recv
        self.d, self.z = d, z
        self.d_core, self.d_x, self.d_y = cube_peers(d)
        self.d_xy = self.d_x + self.d_y - d
        self.sent = []

    def push(self, i, j, src, dst, peer):
        def make():
            return remote_copy(src(), dst(), self.send.at[i, j], self.recv.at[i, j], (peer, self.z))

        make().start()
        self.sent.append(make)

    def landed(self, i, j, slot):
        at = self.items[i][1]
        remote_copy(
            at(slot), at(slot), self.send.at[i, j], self.recv.at[i, j], (self.d_core, self.z)
        ).wait_recv()

    def start(self, i):
        src, at = self.items[i]
        for j, peer in enumerate((self.d_x, self.d_y, self.d_core)):
            self.push(i, j, lambda: src, lambda: at(self.d), peer)

    def near(self, i):
        d_x, d_y, d_core = self.d_x, self.d_y, self.d_core
        self.landed(i, 0, d_x)
        if i in self.via_y:
            self.hand_on(i, 3, d_x, d_y)
        self.hand_on(i, 4, d_x, d_core)
        self.landed(i, 1, d_y)
        if i not in self.via_y:
            self.hand_on(i, 3, d_y, d_x)
        self.hand_on(i, 5, d_y, d_core)

    def hand_on(self, i, j, slot, peer):
        at = self.items[i][1]
        self.push(i, j, lambda: at(slot), lambda: at(slot), peer)

    def far(self, i):
        self.landed(i, 3, self.d_xy)
        self.hand_on(i, 6, self.d_xy, self.d_core)

    def finish(self):
        for i in range(len(self.items)):
            self.landed(i, 2, self.d_core)
            for j in (4, 5, 6):
                self.landed(i, j, self.d_core)
        for make in self.sent:
            make().wait_send()


def gather_kernel(nt, *refs):
    (tok, que, att, inn, mam, sha, sma) = refs[:7]
    (tok_f, que_f, att_f, inn_f, mam_f, sha_f, sma_f) = refs[7:14]
    (lsem, zs_send, zs_recv, t_send, t_recv, d_send, d_recv) = refs[14:]
    d = lax.axis_index("dp")
    z = lax.axis_index("tensor")
    greet([(p, z) for p in cube_peers(d)] + other_quarters(d, z, nt))

    small = []
    for i, (src, dst) in enumerate(((sha, sha_f), (sma, sma_f))):
        for k, peer in enumerate(other_quarters(d, z, nt)):
            small.append(remote_copy(src, dst.at[d, z], zs_send.at[i, k], zs_recv.at[i, k], peer))
            small[-1].start()
    q_rows = que.shape[0]
    cols = att.shape[1]
    i_rows = inn.shape[1]
    items = [
        (inn, lambda s: inn_f.at[:, pl.ds(s * i_rows, i_rows)]),
        (que, lambda s: que_f.at[pl.ds(s * q_rows, q_rows)]),
        (att, lambda s: att_f.at[:, pl.ds(pl.multiple_of(s * cols, cols), cols)]),
        (mam, lambda s: mam_f.at[:, pl.ds(pl.multiple_of(s * cols, cols), cols)]),
        (sha_f.at[d], lambda s: sha_f.at[s]),
        (sma_f.at[d], lambda s: sma_f.at[s]),
    ]
    cube = CubeGather(items, (0, 5), d_send, d_recv, d, z)
    locals_ = []
    for i, (src, dst) in enumerate(
        [(sha, sha_f.at[d, z]), (sma, sma_f.at[d, z]), (tok, tok_f.at[z])]
        + [(src, at(d)) for src, at in items[:4]]
    ):
        copy = pltpu.make_async_copy(src, dst, lsem.at[i])
        copy.start()
        locals_.append(copy)
    for i in range(4):
        cube.start(i)
    chain = ChainGather(tok, tok_f, t_send, t_recv, d, z, nt)
    chain.start()
    locals_[0].wait()
    locals_[1].wait()
    for copy in small:
        copy.wait()
    cube.start(4)
    cube.start(5)
    for i in range(4):
        cube.near(i)
    chain.hop(1)
    for i in (4, 5):
        cube.near(i)
    for i in range(6):
        cube.far(i)
    for dist in range(2, nt):
        chain.hop(dist)
    cube.finish()
    for copy in locals_[2:]:
        copy.wait()
    chain.drain()


def gather_start(tok, que, att, inn, mam, sha, sma, nd, nt):
    if nd != 8:
        shared = lax.all_gather(sha, ("dp", "tensor"), axis=0)
        small = lax.all_gather(sma, ("dp", "tensor"), axis=0)
        return (
            lax.all_gather(tok, "tensor", axis=0),
            lax.all_gather(que, "dp", axis=0, tiled=True),
            lax.all_gather(att, "dp", axis=1, tiled=True),
            lax.all_gather(inn, "dp", axis=1, tiled=True),
            lax.all_gather(mam, "dp", axis=1, tiled=True),
            shared.reshape((nd, nt) + sha.shape),
            small.reshape((nd, nt) + sma.shape),
        )
    bf = jnp.bfloat16
    outs = (
        (nt,) + tok.shape,
        (nd * que.shape[0], que.shape[1]),
        (att.shape[0], nd * att.shape[1]),
        (2, nd * inn.shape[1], inn.shape[2]),
        (mam.shape[0], nd * mam.shape[1]),
        (nd, nt) + sha.shape,
        (nd, nt) + sma.shape,
    )
    anywhere = pl.BlockSpec(memory_space=pl.ANY)
    dma = pltpu.SemaphoreType.DMA
    return pl.pallas_call(
        partial(gather_kernel, nt),
        out_shape=[jax.ShapeDtypeStruct(s, bf) for s in outs],
        in_specs=[pl.BlockSpec(memory_space=pltpu.VMEM)] * 7,
        out_specs=[anywhere] * 7,
        scratch_shapes=[
            dma((7,)), dma((2, nt)), dma((2, nt)), dma((2, nt)), dma((2, nt)),
            dma((6, 7)), dma((6, 7)),
        ],
        compiler_params=pltpu.CompilerParams(collective_id=0, has_side_effects=True),
        name="gather_start",
    )(tok, que, att, inn, mam, sha, sma)


def pack_kernel(taps, gain, norms, staps, step, out, rows):
    heads = step.shape[0]
    f32 = jnp.float32
    rows[...] = jnp.zeros(rows.shape, f32)
    rows[0:2, 0:32] = norms[...].astype(f32)
    rows[0 : CONV + 1, 32:40] = staps[...].astype(f32)
    rows[0:heads, 40:48] = gain[...].astype(f32)
    for j in range(CONV + 1):
        rows[0:heads, 48 + 8 * j : 56 + 8 * j] = taps[j].astype(f32)
    rows[8 : 8 + heads, :] = step[...].astype(f32)
    out[...] = rows[...].astype(jnp.bfloat16)


def pack_small(taps, gain, norms, staps, step):
    vmem = pl.BlockSpec(memory_space=pltpu.VMEM)
    return pl.pallas_call(
        pack_kernel,
        in_specs=[vmem] * 5,
        out_specs=vmem,
        out_shape=jax.ShapeDtypeStruct((16, 128), jnp.bfloat16),
        scratch_shapes=[pltpu.VMEM((16, 128), jnp.float32)],
        name="pack_small",
    )(taps, gain, norms, staps, step)


def unpack_kernel(
    heads, where, scal, packed, first_o, second_o, gain_o, tapx_o, tapb_o, step_o, decay_o, bias_o, skip_o
):
    z = where[0]
    f32 = jnp.float32
    nd, nt = packed.shape[:2]
    tiles = [[packed[k, q].astype(f32) for q in range(nt)] for k in range(nd)]
    for k in range(nd):
        both = jnp.concatenate([tiles[k][q][0:8, 0:32] for q in range(nt)], axis=1)
        first_o[:, 128 * k : 128 * k + 128] = both[0:1]
        second_o[:, 128 * k : 128 * k + 128] = both[1:2]
        step_o[:, 128 * k : 128 * k + 128] = packed[k, z].astype(f32)[8:16, :].astype(jnp.bfloat16)
    half = nd // 2
    for k in range(2):
        tapb_o[:, 128 * k : 128 * k + 128] = jnp.concatenate(
            [tiles[half * k + i][q][0:8, 32:40] for i in range(half) for q in range(nt)], axis=1
        )
    own = [packed[k, z].astype(f32) for k in range(nd)]

    def by_head(lane):
        wide = jnp.concatenate([own[k][0:8, lane : lane + 8] for k in range(nd)], axis=1)
        return jnp.concatenate([wide[h : h + 1, :] for h in range(heads)], axis=1)

    gain_o[...] = by_head(40)
    tapx_o[...] = jnp.zeros(tapx_o.shape, f32)
    tapb_o[CONV + 1 :, :] = jnp.zeros((7 - CONV, tapb_o.shape[1]), f32)
    for j in range(CONV + 1):
        tapx_o[j : j + 1, :] = by_head(48 + 8 * j)
    sub = lax.broadcasted_iota(jnp.int32, (8, 128), 0)
    decay = jnp.zeros((8, 128), f32)
    bias = jnp.zeros((8, 128), f32)
    for h in range(heads):
        decay = jnp.where(sub == h, scal[0, h], decay)
        bias = jnp.where(sub == h, scal[1, h], bias)
        skip_o[:, SSM_DIM * h : SSM_DIM * (h + 1)] = jnp.full((1, SSM_DIM), scal[2, h], f32)
    decay_o[...] = jnp.where(sub < heads, -jnp.exp(decay), 0.0)
    bias_o[...] = bias


def unpack_small(heads, where, scal, packed, width):
    inner = heads * SSM_DIM
    vmem = pl.BlockSpec(memory_space=pltpu.VMEM)
    smem = pl.BlockSpec(memory_space=pltpu.SMEM)
    sds = jax.ShapeDtypeStruct
    f32 = jnp.float32
    shapes = [(1, width), (1, width), (1, inner), (8, inner), (8, 256)]
    return pl.pallas_call(
        partial(unpack_kernel, heads),
        in_specs=[smem, smem, vmem],
        out_specs=[vmem] * 9,
        out_shape=[sds(s, f32) for s in shapes]
        + [sds((8, width), jnp.bfloat16), sds((8, 128), f32), sds((8, 128), f32), sds((1, inner), f32)],
        name="unpack_small",
    )(where, scal, packed)


def pick(values, index, axis=0):
    return lax.dynamic_index_in_dim(values, index, axis, keepdims=False)


def add_low(left, right):
    return (left.astype(jnp.float32) + right.astype(jnp.float32)).astype(jnp.bfloat16)


def chain_scatter(parts, nt):
    z = lax.axis_index("tensor")
    right = left = None
    for t in range(nt - 1):
        to_right = pick(parts, jnp.clip(nt - 1 - t + z, 0, nt - 1))
        to_left = pick(parts, jnp.clip(t - (nt - 1) + z, 0, nt - 1))
        if t > 0:
            to_right = add_low(to_right, right)
            to_left = add_low(to_left, left)
        right = lax.ppermute(to_right, "tensor", [(i, i + 1) for i in range(t + 1)])
        left = lax.ppermute(
            to_left, "tensor", [(nt - 1 - i, nt - 2 - i) for i in range(t + 1)]
        )
    f32 = jnp.float32
    return pick(parts, z).astype(f32) + right.astype(f32) + left.astype(f32)


def cube_scatter(parts, nd, last=jnp.float32):
    return lax.psum_scatter(parts, "dp", scatter_dimension=0, tiled=False).astype(last)


F32, BF16 = jnp.float32, jnp.bfloat16
VMEM_LIMIT = 56 * 1024 * 1024


def dot_nn(a, b):
    return lax.dot_general(a, b, (((1,), (0,)), ((), ())), preferred_element_type=F32)


def dot_nt(a, b):
    return lax.dot_general(a, b, (((1,), (1,)), ((), ())), preferred_element_type=F32)


def dot_tn(a, b):
    return lax.dot_general(a, b, (((0,), (0,)), ((), ())), preferred_element_type=F32)


def sigmoid(v):
    return 1.0 / (1.0 + jnp.exp(-v))


def lanes_of(shape):
    return lax.broadcasted_iota(jnp.int32, shape, len(shape) - 1)


def turn(values, cosine, sine):
    lane = lanes_of(values.shape)
    other = jnp.where(
        lax.rem(lane, HEAD_SIZE) < HEAD_SIZE // 2,
        pltpu.roll(values, 128 - HEAD_SIZE // 2, 1),
        pltpu.roll(values, HEAD_SIZE // 2, 1),
    )
    return values * cosine + other * sine


def softplus(v):
    return jnp.maximum(v, 0.0) + jnp.log1p(jnp.exp(-jnp.abs(v)))


def running_sum(rows):
    lane = lanes_of(rows.shape)
    step = 1
    while step < rows.shape[1]:
        rows = rows + jnp.where(lane >= step, pltpu.roll(rows, step, 1), 0.0)
        step *= 2
    return rows


def running_sum_back(rows):
    lane = lanes_of(rows.shape)
    width = rows.shape[1]
    step = 1
    while step < width:
        rows = rows + jnp.where(lane < width - step, pltpu.roll(rows, width - step, 1), 0.0)
        step *= 2
    return rows


def stack_columns(rows_list):
    used = sum(r.shape[0] for r in rows_list)
    filler = jnp.zeros((128 - used, 128), F32)
    return jnp.concatenate(rows_list + [filler], axis=0).T


def widen(cols, base, heads):
    low = lanes_of((cols.shape[0], 128)) < SSM_DIM
    return jnp.concatenate(
        [
            jnp.where(low, cols[:, base + 2 * p : base + 2 * p + 1],
                      cols[:, base + 2 * p + 1 : base + 2 * p + 2])
            for p in range(heads // 2)
        ],
        axis=1,
    )


def conv_rows(ref, taps, first, rows):
    total = taps[CONV : CONV + 1, :] + taps[0:1, :] * ref[pl.ds(first, rows), :]
    for j in range(1, CONV):
        total = total + taps[j : j + 1, :] * ref[pl.ds(first + j, rows), :]
    return total


def quarter_at(i, z, nt):
    near = jnp.where(z < nt - 1, z + 1, z - 1)
    far = jnp.where(z < nt - 1, lax.rem(z + 3, nt), lax.rem(z + 1, nt))
    order = jnp.where(i == 0, lax.rem(z + 2, nt), far)
    return jnp.where(i == 2, near, jnp.where(i == 3, z, order))


class FeedGather:
    def __init__(self, step, nt, hid, dwn, hid_f, dwn_f, hid_z, dwn_z, lsem, sems):
        self.step, self.nt = step, nt
        d = lax.axis_index("dp")
        z = lax.axis_index("tensor")
        self.d, self.z = d, z
        self.cube = CubeGather(
            [(hid, lambda s: hid_f.at[s, z]), (dwn, lambda s: dwn_f.at[s, z])], (0,), sems[0], sems[1], d, z
        )
        self.chains = [
            ChainGather(hid, hid_z, sems[2], sems[3], d, z, nt),
            ChainGather(dwn, dwn_z, sems[4], sems[5], d, z, nt),
        ]
        self.own = lambda: [
            pltpu.make_async_copy(hid, hid_f.at[d, z], lsem.at[0]),
            pltpu.make_async_copy(dwn, dwn_f.at[d, z], lsem.at[1]),
        ]

    def at(self, step, act):
        pl.when(self.step == step)(act)

    def begin(self):
        def act():
            greet([(p, self.z) for p in cube_peers(self.d)] + other_quarters(self.d, self.z, self.nt))
            for chain in self.chains:
                chain.start()
            for i in range(2):
                self.cube.start(i)
            for copy in self.own():
                copy.start()

        self.at(0, act)
    def middle(self):
        def near():
            for chain in self.chains:
                chain.hop(1)
            for i in range(2):
                self.cube.near(i)

        def far():
            for chain in self.chains:
                chain.hop(2)
            for i in range(2):
                self.cube.far(i)

        self.at(1, near)
        self.at(2, far)

    def end(self):
        def act():
            for chain in self.chains:
                chain.hop(3)
            self.cube.finish()
            for copy in self.own():
                copy.wait()
            for chain in self.chains:
                chain.drain()

        self.at(3, act)


def forward_kernel(heads, nt, feed, *refs):
    if feed:
        beside = FeedGather(
            pl.program_id(0), nt, *refs[14:16], *refs[29:33], refs[38], refs[39:45]
        )
        refs = refs[:14] + refs[16:29] + refs[33:38]
        beside.begin()
        forward_step(heads, beside.middle, *refs)
        beside.end()
    else:
        forward_step(heads, lambda: None, *refs)


def forward_step(
    heads, middle, kvh, tok, gain, wq, win, stp, wsh, cosine, sine, tapx, tapb, decay, bias, skip,
    a1_o, q_o, k_o, v_o, lse_o, o_o, x_o, z_o, b_o, y_o, t_o, s_o, sq_o,
    keys, vals, xs, bs, state,
):
    step = pl.program_id(0)
    rows = tok.shape[0]
    second = kvh[0] == 1

    @pl.when(step == 0)
    def _():
        xs[0:8, :] = jnp.zeros((8, xs.shape[1]), F32)
        bs[0:8, :] = jnp.zeros((8, bs.shape[1]), F32)
        state[...] = jnp.zeros(state.shape, F32)

    t = tok[...].astype(F32)
    r = lax.rsqrt(jnp.mean(t * t, axis=1, keepdims=True) + epsilon)
    a1 = (t * r * gain[...]).astype(BF16)
    a1_o[...] = a1
    q = turn(dot_nn(a1, wq[...]), cosine[...], sine[...]).astype(BF16)
    q_o[...] = q
    s = dot_nn(a1, wsh[...])
    low = lanes_of((rows, 128)) < HEAD_SIZE
    k = turn(s[:, :128], cosine[...], sine[...])
    v = s[:, 128:256]
    pick_own = low != second
    k2 = jnp.where(pick_own, k, pltpu.roll(k, 64, 1)).astype(BF16)
    v2 = jnp.where(pick_own, v, pltpu.roll(v, 64, 1))
    k_o[...] = k2
    v_o[...] = v2.astype(BF16)
    place = pl.ds(pl.multiple_of(step * rows, rows), rows)
    keys[place, :] = k2
    vals[:, place] = v2.T.astype(BF16)

    scale = HEAD_SIZE**-0.5

    def attend(blocks):
        n = blocks * rows
        shape = (rows, rows)
        allowed = lax.broadcasted_iota(jnp.int32, shape, 0) <= lanes_of(shape)
        parts = []
        for h in range(2):
            qh = jnp.where(low == (h == 0), q, jnp.zeros_like(q))
            sc = dot_nt(keys[0:n, :], qh) * scale
            last = jnp.where(allowed, sc[n - rows :, :], neg_large)
            sc = jnp.concatenate([sc[: n - rows, :], last], axis=0) if blocks > 1 else last
            top = jnp.max(sc, axis=0, keepdims=True)
            e = jnp.exp(sc - top)
            total = jnp.sum(e, axis=0, keepdims=True)
            lse_o[h : h + 1, :] = top + jnp.log(total)
            parts.append(dot_nn(vals[:, 0:n], e.astype(BF16)) / total)
        sub = lax.broadcasted_iota(jnp.int32, parts[0].shape, 0)
        o_o[...] = jnp.where(sub < HEAD_SIZE, parts[0], parts[1]).T.astype(BF16)

    for i in range(keys.shape[0] // rows):
        pl.when(step == i)(partial(attend, i + 1))

    middle()
    zr = dot_nn(a1, win[0])
    z_o[...] = zr
    xr = dot_nn(a1, win[1])
    x_o[...] = xr
    br = s[:, 256:]
    b_o[...] = br
    xs[8 : 8 + rows, :] = xr
    bs[8 : 8 + rows, :] = br
    u = conv_rows(xs, tapx, 5, rows)
    x = u * sigmoid(u)
    u = conv_rows(bs, tapb, 5, rows)
    bc = (u * sigmoid(u)).astype(BF16)
    xs[0:8, :] = xs[rows : rows + 8, :]
    bs[0:8, :] = bs[rows : rows + 8, :]
    tr = dot_nt(stp[...], a1)
    t_o[...] = tr
    n_state = bc.shape[1] // 2
    tri_shape = (block_len, block_len)
    lower = lax.broadcasted_iota(jnp.int32, tri_shape, 0) >= lanes_of(tri_shape)
    half = lanes_of(tri_shape) < SSM_DIM
    for c in range(rows // block_len):
        part = slice(c * block_len, (c + 1) * block_len)
        dt = softplus(tr[:, part] + bias[...])
        cum = running_sum(dt * decay[...])
        end = cum[:, block_len - 1 :]
        cols = stack_columns([cum, jnp.exp(cum), dt * jnp.exp(end - cum)])
        xc = x[part]
        x_low = xc.astype(BF16)
        b_low = bc[part, :n_state]
        c_low = bc[part, n_state:]
        cross = dot_nt(c_low, b_low)
        grow = widen(cols, 8, heads)
        y = dot_nn(c_low, state[...].astype(BF16)) * grow + skip[...] * xc
        inner = []
        for p in range(heads // 2):
            mats = []
            for h in (2 * p, 2 * p + 1):
                gap = jnp.where(lower, cols[:, h : h + 1] - cum[h : h + 1, :], neg_large)
                mats.append((cross * jnp.exp(gap) * dt[h : h + 1, :]).astype(BF16))
            xp = x_low[:, 128 * p : 128 * p + 128]
            zero = jnp.zeros_like(xp)
            both = jnp.concatenate([jnp.where(half, xp, zero), jnp.where(half, zero, xp)], axis=0)
            inner.append(dot_nn(jnp.concatenate(mats, axis=1), both))
        y = y + jnp.concatenate(inner, axis=1)
        y_o[part, :] = y
        s_o[c] = state[...]
        carried = (xc * widen(cols, 16, heads)).astype(BF16)
        state[...] = grow[block_len - 1 :, :] * state[...] + dot_tn(b_low, carried)
        zc = zr[part]
        w = y * (zc * sigmoid(zc))
        total = jnp.sum(w * w, axis=1, keepdims=True)
        sq_o[:, part] = jnp.broadcast_to(total, (block_len, 128)).T[0:8, :]


def mixers_forward(
    heads, nt, kvh, tok, gain, wq, win, stp, wsh, cosine, sine, tapx, tapb, decay, bias, skip, feed=()
):
    total, width = tok.shape
    rows = 256
    inner = heads * SSM_DIM
    pair = wsh.shape[1] - 256
    state = pair // 2
    chunks = rows // block_len

    def whole(v):
        return pl.BlockSpec(v.shape, lambda i: (0,) * v.ndim)

    def tall(n):
        return pl.BlockSpec((rows, n), lambda i: (i, 0))

    wide = pl.BlockSpec((8, rows), lambda i: (0, i))
    sds = jax.ShapeDtypeStruct
    more_in, more_out, more_shape, more_scratch, extra = [], [], [], [], {}
    if feed:
        nd = 8
        dma = pltpu.SemaphoreType.DMA
        more_in = [whole(v) for v in feed]
        more_out = [pl.BlockSpec(memory_space=pl.ANY)] * 4
        more_shape = [sds((nd, nt) + v.shape, BF16) for v in feed] + [sds((nt,) + v.shape, BF16) for v in feed]
        more_scratch = [dma((2,)), dma((2, 7)), dma((2, 7))] + [dma((2, nt - 1))] * 4
        extra = dict(collective_id=6, has_side_effects=True)
    return pl.pallas_call(
        partial(forward_kernel, heads, nt, bool(feed)),
        grid=(total // rows,),
        in_specs=[pl.BlockSpec(memory_space=pltpu.SMEM), tall(width), whole(gain), whole(wq), whole(win),
                  whole(stp), whole(wsh), tall(128), tall(128), whole(tapx), whole(tapb),
                  whole(decay), whole(bias), whole(skip)] + more_in,
        out_specs=[tall(width), tall(128), tall(128), tall(128), wide, tall(128), tall(inner),
                   tall(inner), tall(pair), tall(inner), wide,
                   pl.BlockSpec((chunks, state, inner), lambda i: (i, 0, 0)), wide] + more_out,
        out_shape=[sds((total, width), BF16), sds((total, 128), BF16), sds((total, 128), BF16),
                   sds((total, 128), BF16), sds((8, total), F32), sds((total, 128), BF16),
                   sds((total, inner), F32), sds((total, inner), F32), sds((total, pair), F32),
                   sds((total, inner), F32), sds((8, total), F32),
                   sds((total // block_len, state, inner), F32), sds((8, total), F32)] + more_shape,
        scratch_shapes=[pltpu.VMEM((total, 128), BF16), pltpu.VMEM((128, total), BF16),
                        pltpu.VMEM((rows + 8, inner), F32), pltpu.VMEM((rows + 8, pair), F32),
                        pltpu.VMEM((state, inner), F32)] + more_scratch,
        compiler_params=pltpu.CompilerParams(vmem_limit_bytes=VMEM_LIMIT, **extra),
        cost_estimate=pl.CostEstimate(flops=int(5e9), bytes_accessed=int(15e6), transcendentals=int(4e6)),
        name="mixers_forward",
    )(kvh, tok, gain, wq, win, stp, wsh, cosine, sine, tapx, tapb, decay, bias, skip, *feed)


def attend_back(step, kvh, q, k2, v2, lse, do, cosine, sine, cos_all, sin_all, dq_o, dkv_o, dk, dv):
    rows = q.shape[0]
    steps = k2.shape[0] // rows
    scale = HEAD_SIZE**-0.5
    low = lanes_of((rows, 128)) < HEAD_SIZE

    @pl.when(step == 0)
    def _():
        dk[...] = jnp.zeros(dk.shape, F32)
        dv[...] = jnp.zeros(dv.shape, F32)

    def back(blocks):
        n = blocks * rows
        shape = (rows, rows)
        allowed = lax.broadcasted_iota(jnp.int32, shape, 0) <= lanes_of(shape)
        qs, dos, ps, dss, dqs = [], [], [], [], []
        for h in range(2):
            mine = low == (h == 0)
            qh = jnp.where(mine, q[...], jnp.zeros_like(q[...]))
            doh = jnp.where(mine, do[...], jnp.zeros_like(do[...]))
            sc = dot_nt(k2[0:n, :], qh) * scale - lse[h : h + 1, :]
            last = jnp.where(allowed, sc[n - rows :, :], neg_large)
            sc = jnp.concatenate([sc[: n - rows, :], last], axis=0) if blocks > 1 else last
            p = jnp.exp(sc)
            dp = dot_nt(v2[0:n, :], doh)
            centre = jnp.sum(p * dp, axis=0, keepdims=True)
            ds = (p * (dp - centre)).astype(BF16)
            qs.append(qh)
            dos.append(doh)
            ps.append(p.astype(BF16))
            dss.append(ds)
            dqs.append(dot_tn(ds, k2[0:n, :]) * scale)
        dk[0:n, :] += dot_nn(jnp.concatenate(dss, axis=1), jnp.concatenate(qs, axis=0)) * scale
        dv[0:n, :] += dot_nn(jnp.concatenate(ps, axis=1), jnp.concatenate(dos, axis=0))
        dq_o[...] = turn(jnp.where(low, dqs[0], dqs[1]), cosine[...], -sine[...]).astype(BF16)

    for i in range(steps):
        pl.when(step == 2 * (steps - 1 - i))(partial(back, i + 1))

    @pl.when(step == 2 * steps - 1)
    def _():
        own = (lanes_of(dk.shape) < HEAD_SIZE) != (kvh[0] == 1)
        g = dk[...]
        g = turn(g + pltpu.roll(g, 64, 1), cos_all[...], -sin_all[...])
        dkv_o[:, 0:128] = jnp.where(own, g, 0.0).astype(BF16)
        g = dv[...]
        g = g + pltpu.roll(g, 64, 1)
        dkv_o[:, 128:256] = jnp.where(own, g, 0.0).astype(BF16)


def back_kernel(heads, channels, nt, feed, *refs):
    step = pl.program_id(0)
    if feed:
        d = lax.axis_index("dp")
        z = lax.axis_index("tensor")
        sums, raw, refs = refs[0], refs[1], refs[2:]
        feed_o, refs = refs[37], refs[:37] + refs[38:]
        parts, chain_boxes, box = refs[44], refs[45:49], refs[49:57]
        (dot_sum, dot_land, d_send, d_recv), refs = refs[57:61], refs[:44]
        peers = cube_peers(d)
        square = SquareScatter(
            lambda i, j: (2 * i + j,), raw, box[:6], box[6], box[7], peers, dp_bits(d), z
        )
        chain = ChainScatter(parts, *chain_boxes, d, z, nt)
        dots = Exchange(refs[20], dot_land, d_send, d_recv, d, z, nt)

        @pl.when(step == 0)
        def _():
            greet([(p, z) for p in peers[1:]] + other_quarters(d, z, nt))
            for k in range(nt - 2):
                parts[quarter_at(k, z, nt)] = sums[k]
            parts[z] = jnp.zeros(parts.shape[1:], BF16)
            dots.start()
            chain.step(0)
            square.start()

        pl.when(step == 3)(lambda: chain.step(1))
        pl.when(step == 3)(square.middle)

        @pl.when(step == 5)
        def _():
            square.finish(parts.at[quarter_at(nt - 2, z, nt)])
            chain.step(2)

    attend_back(step, *refs[:10], *refs[27:29], *refs[37:39])
    if feed:

        @pl.when(step == 0)
        def _():
            dots.wait()
            dot_sum[...] = dots.total()

        at = pl.ds(pl.multiple_of((pl.num_programs(0) - 1 - step) * block_len, block_len), block_len)
        refs = refs[:20] + (dot_sum.at[:, at],) + refs[21:]
    scan_back(heads, channels, step, *refs[10:27], *refs[29:37], *refs[39:44])
    if feed:

        @pl.when(step == pl.num_programs(0) - 1)
        def _():
            chain.finish(feed_o)
            chain.drain()
            square.drain()


def scan_back(
    heads, channels, step, dm, y, zr, xr, xp, br, bp, trow, states, rsum, dots, gain, tapx, tapb, decay,
    bias, skip,
    dz_o, dx_o, db_o, dt_o, gx_o, gb_o, gm_o, gh_o,
    xs, bs, dxs, dbs, dstate,
):
    last_step = pl.num_programs(0) - 1
    first = step == last_step
    rows = block_len
    inner = heads * SSM_DIM
    n_state = br.shape[1] // 2

    @pl.when(step == 0)
    def _():
        dxs[rows : rows + 8, :] = jnp.zeros((8, inner), F32)
        dbs[rows : rows + 8, :] = jnp.zeros((8, 2 * n_state), F32)
        dstate[...] = jnp.zeros(dstate.shape, F32)
        gx_o[...] = jnp.zeros(gx_o.shape, F32)
        gb_o[...] = jnp.zeros(gb_o.shape, F32)
        gm_o[...] = jnp.zeros(gm_o.shape, F32)
        gh_o[...] = jnp.zeros(gh_o.shape, F32)

    xs[0:8, :] = jnp.where(first, 0.0, xp[...])
    bs[0:8, :] = jnp.where(first, 0.0, bp[...])
    xs[8 : 8 + rows, :] = xr[...]
    bs[8 : 8 + rows, :] = br[...]
    ux = conv_rows(xs, tapx, 5, rows)
    sx = sigmoid(ux)
    x = ux * sx
    ub = conv_rows(bs, tapb, 5, rows)
    sb = sigmoid(ub)
    bc = (ub * sb).astype(BF16)
    b_low, c_low = bc[:, :n_state], bc[:, n_state:]

    pre = trow[...] + bias[...]
    dt = softplus(pre)
    cum = running_sum(dt * decay[...])
    end = cum[:, rows - 1 :]
    fade = jnp.exp(end - cum)
    inv = lax.rsqrt(rsum[...] / channels + epsilon)
    cols = stack_columns(
        [cum, jnp.exp(cum), dt * fade, dt, inv, inv * inv * inv * dots[...] / channels]
    )
    r = cols[:, 32:33]
    kk = cols[:, 40:41]
    z = zr[...]
    sz = sigmoid(z)
    silu_z = z * sz
    yv = y[...]
    w = yv * silu_z
    dmv = dm[...]
    dw = r * gain[...] * dmv - w * kk
    gm_o[0:1, :] += jnp.sum(dmv * w * r, axis=0, keepdims=True)
    dy = dw * silu_z
    dz_o[...] = (dw * yv * sz * (1.0 + z * (1.0 - sz))).astype(BF16)
    gm_o[1:2, :] += jnp.sum(dy * x, axis=0, keepdims=True)

    grow = widen(cols, 8, heads)
    tail = widen(cols, 16, heads)
    dt_wide = widen(cols, 24, heads)
    x_low = x.astype(BF16)
    dy_low = dy.astype(BF16)
    state = states[0]
    state_low = state.astype(BF16)
    ds = dstate[...]
    ds_low = ds.astype(BF16)
    cross = dot_nt(b_low, c_low)
    shape = (rows, rows)
    upper = lax.broadcasted_iota(jnp.int32, shape, 0) <= lanes_of(shape)
    half = lanes_of(shape) < SSM_DIM
    lane = lanes_of(shape)
    dcross = jnp.zeros(shape, F32)
    col_sums = jnp.zeros(shape, F32)
    row_sums = []
    mids = []
    for p in range(heads // 2):
        span = slice(128 * p, 128 * p + 128)
        xpair, dypair = x_low[:, span], dy_low[:, span]
        zero = jnp.zeros_like(xpair)
        dys = (jnp.where(half, dypair, zero), jnp.where(half, zero, dypair))
        mats = []
        for k in range(2):
            h = 2 * p + k
            gap = jnp.where(upper, cum[h : h + 1, :] - cols[:, h : h + 1], neg_large)
            faded = jnp.exp(gap)
            mats.append((cross * faded).astype(BF16))
            t = dot_nt(xpair, dys[k]) * faded
            dt_col = cols[:, 24 + h : 25 + h]
            td = t * dt_col
            dcross = dcross + td
            row_sums.append(jnp.sum(td * cross, axis=0, keepdims=True))
            col = jnp.sum(t * cross, axis=1, keepdims=True)
            col_sums = jnp.where(lane == h, col, col_sums)
        mids.append(dot_nn(jnp.concatenate(mats, axis=1), jnp.concatenate(dys, axis=0)))
    mid = jnp.concatenate(mids, axis=1)
    row_sums = jnp.concatenate(row_sums + [jnp.zeros((8 - heads, rows), F32)], axis=0)
    col_sums = col_sums.T[0:8, :]

    dye = dy * grow
    dye_low = dye.astype(BF16)
    xd = x * tail
    xd_low = xd.astype(BF16)
    from_b = dot_nn(b_low, ds_low)
    through = dot_nn(c_low, state_low)
    dcross_low = dcross.astype(BF16)
    db = dot_nn(dcross_low, c_low) + dot_nt(xd_low, ds_low)
    dc = dot_tn(dcross_low, b_low) + dot_nt(dye_low, state_low)

    head_of = lax.broadcasted_iota(jnp.int32, (8, inner), 0)
    chan = lanes_of((8, inner)) // SSM_DIM
    ones = jnp.where(head_of == chan, 1.0, 0.0).astype(BF16)

    def by_head(v):
        high = v.astype(BF16)
        rest = (v - high.astype(F32)).astype(BF16)
        return dot_nt(ones, high) + dot_nt(ones, rest)

    grown = by_head(dye * through)
    ended = by_head(x * from_b)
    kept = jnp.sum(ds * state, axis=0, keepdims=True) * grow[rows - 1 :, :]
    kept = jnp.where(head_of == chan, kept, 0.0).sum(axis=1, keepdims=True)
    pulled = dt * fade * ended
    lane8 = lanes_of((8, rows))
    at_end = kept + jnp.sum(pulled, axis=1, keepdims=True)
    dcum = row_sums - dt * col_sums + grown - pulled + jnp.where(lane8 == rows - 1, at_end, 0.0)
    da = running_sum_back(dcum)
    ddt = col_sums + fade * ended + decay[...] * da
    dpre = ddt * sigmoid(pre)
    dt_o[...] = dpre
    gh_o[0:8, :] += da * dt * decay[...]
    gh_o[8:16, :] += dpre

    dstate[...] = grow[rows - 1 :, :] * ds + dot_tn(c_low, dye_low)
    dx = skip[...] * dy + dt_wide * mid + tail * from_b
    dux = dx * sx * (1.0 + ux * (1.0 - sx))
    dub = jnp.concatenate([db, dc], axis=1) * sb * (1.0 + ub * (1.0 - sb))
    for taps, src, d, buf, acc, out in (
        (tapx, xs, dux, dxs, gx_o, dx_o),
        (tapb, bs, dub, dbs, gb_o, db_o),
    ):
        buf[0:rows, :] = d
        total = taps[CONV - 1 : CONV, :] * d
        for j in range(CONV - 1):
            total = total + taps[j : j + 1, :] * buf[pl.ds(CONV - 1 - j, rows), :]
        out[...] = total.astype(BF16)
        for j in range(CONV):
            acc[j : j + 1, :] += jnp.sum(d * src[pl.ds(5 + j, rows), :], axis=0, keepdims=True)
        acc[CONV : CONV + 1, :] += jnp.sum(d, axis=0, keepdims=True)
        buf[rows : rows + 8, :] = d[0:8, :]


def mixers_back(
    heads, channels, nt, kvh, q, k2, v2, lse, do, cosine, sine, dm, y, zr, xr, br, trow, states, rsum, dots,
    gain, tapx, tapb, decay, bias, skip, feed=None,
):
    total, inner = y.shape
    pair = br.shape[1]
    rows = block_len
    steps = total // rows
    per = rows // 8
    q_rows = 2 * rows

    def whole(v):
        return pl.BlockSpec(v.shape, lambda i: (0,) * v.ndim)

    def tall(n):
        return pl.BlockSpec((rows, n), lambda i: (steps - 1 - i, 0))

    def before(n):
        return pl.BlockSpec((8, n), lambda i: (jnp.maximum((steps - 1 - i) * per - 1, 0), 0))

    wide = pl.BlockSpec((8, rows), lambda i: (0, steps - 1 - i))
    ask = pl.BlockSpec((q_rows, 128), lambda i: (steps // 2 - 1 - i // 2, 0))
    sds = jax.ShapeDtypeStruct

    def fixed(*shape):
        return pl.BlockSpec(shape, lambda i: (0,) * len(shape))

    in_specs = [pl.BlockSpec(memory_space=pltpu.SMEM), ask, whole(k2), whole(v2),
                pl.BlockSpec((8, q_rows), lambda i: (0, steps // 2 - 1 - i // 2)), ask, ask, ask, whole(cosine), whole(sine),
                tall(inner), tall(inner), tall(inner), tall(inner), before(inner), tall(pair),
                before(pair), wide, pl.BlockSpec((1, pair // 2, inner), lambda i: (steps - 1 - i, 0, 0)),
                wide, wide, whole(gain), whole(tapx), whole(tapb), whole(decay), whole(bias), whole(skip)]
    out_specs = [ask, fixed(total, 256), tall(inner), tall(inner), tall(pair), wide, fixed(8, inner),
                 fixed(8, pair), fixed(8, inner), fixed(16, rows)]
    out_shape = [sds((total, 128), BF16), sds((total, 256), BF16), sds((total, inner), BF16),
                 sds((total, inner), BF16), sds((total, pair), BF16), sds((8, total), F32),
                 sds((8, inner), F32), sds((8, pair), F32), sds((8, inner), F32), sds((16, rows), F32)]
    scratch = [pltpu.VMEM((total, 128), F32), pltpu.VMEM((total, 128), F32),
               pltpu.VMEM((rows + 8, inner), F32), pltpu.VMEM((rows + 8, pair), F32),
               pltpu.VMEM((rows + 8, inner), F32), pltpu.VMEM((rows + 8, pair), F32),
               pltpu.VMEM((pair // 2, inner), F32)]
    args = [kvh, q, k2, v2, lse, do, cosine, sine, cosine, sine, dm, y, zr, xr, xr, br, br, trow, states,
            rsum, dots, gain, tapx, tapb, decay, bias, skip]
    extra = {}
    if feed is not None:
        piece = feed[0].shape[1:]
        dma = pltpu.SemaphoreType.DMA
        in_specs[20] = whole(dots)
        args = list(feed) + args
        in_specs = [whole(v) for v in feed] + in_specs
        out_specs = out_specs + [fixed(*piece)]
        out_shape = out_shape + [sds(piece, F32)]
        scratch = scratch + [pltpu.VMEM((nt,) + piece, BF16)] + chain_scratch(nt, *piece)
        scratch = scratch + square_scratch(*piece)
        scratch = scratch + [pltpu.VMEM(dots.shape, F32), pltpu.VMEM((nt - 1,) + dots.shape, F32),
                             dma((nt - 1,)), dma((nt - 1,))]
        extra = dict(collective_id=5, has_side_effects=True)
    return pl.pallas_call(
        partial(back_kernel, heads, channels, nt, feed is not None),
        grid=(steps,),
        in_specs=in_specs,
        out_specs=out_specs,
        out_shape=out_shape,
        scratch_shapes=scratch,
        compiler_params=pltpu.CompilerParams(vmem_limit_bytes=VMEM_LIMIT, **extra),
        cost_estimate=pl.CostEstimate(flops=int(6e9), bytes_accessed=int(18e6), transcendentals=int(7e6)),
        name="mixers_back",
    )(*args)


def whole_spec(v):
    return pl.BlockSpec(v.shape, lambda i: (0,) * v.ndim)


def feed_open(hid, gain, a2, a2t, acc, dacc):
    v = hid[...]
    f = lax.rsqrt(jnp.mean(v * v, axis=1, keepdims=True) + epsilon)
    low = (v * f * gain[...]).astype(BF16)
    a2[...] = low
    a2t[...] = low.T
    acc[...] = jnp.zeros(acc.shape, F32)
    dacc[...] = jnp.zeros(dacc.shape, F32)


def feed_tile(a2, cot, whid, wdown, acc, dacc):
    width = a2.shape[1]
    units = whid.shape[4]
    w_gate = whid[:, 0, 0].reshape(width, units)
    w_up = whid[:, 0, 1].reshape(width, units)
    w_down = jnp.concatenate([wdown[k, 0] for k in range(width // 128)], axis=1)
    g = dot_nn(a2[...], w_gate)
    u = dot_nn(a2[...], w_up)
    s = sigmoid(g)
    f_low = (g * s * u).astype(BF16)
    acc[...] += dot_nn(f_low, w_down)
    df = dot_nt(cot[...], w_down)
    du = (df * g * s).astype(BF16)
    dg = (df * u * s * (1.0 + g * (1.0 - s))).astype(BF16)
    dacc[...] += dot_nt(dg, w_gate) + dot_nt(du, w_up)
    return f_low, dg, du


def feed_close(hid, gain, cot, acc, dacc, out_o, dh_o, gg_o):
    v = hid[...]
    out_o[...] = (v + acc[...]).astype(BF16)
    f = lax.rsqrt(jnp.mean(v * v, axis=1, keepdims=True) + epsilon)
    dy = dacc[...]
    gg_o[...] = jnp.sum(dy * v * f, axis=0, keepdims=True)
    gdy = dy * gain[...]
    lean = jnp.sum(gdy * v, axis=1, keepdims=True) * (f * f * f / v.shape[1])
    dh = cot[...].astype(F32) + (f * gdy - v * lean)
    dh_o[...] = dh
    return dh.astype(BF16)


def feed_grads(a2t, cot, f_low, dg, du):
    blocks = a2t.shape[0] // 128
    values = []
    for grad in (dg, du):
        full = dot_nn(a2t[...], grad).astype(BF16)
        for cb in range(grad.shape[1] // 128):
            values.append(full[:, 128 * cb : 128 * cb + 128].reshape(blocks, 128, 128))
    full = dot_tn(f_low, cot[...]).astype(BF16)
    values.append(jnp.stack([full[:, 128 * k : 128 * k + 128] for k in range(blocks)]))
    return values


def piece_rows(part, units, quarter_units):
    rows = [
        (k * quarter_units + part * units + cb * 128, 128) for k in range(2) for cb in range(units // 128)
    ]
    return rows + [(2 * quarter_units + part * units, units)]


def feed_kernel(hid, gain, cot, whid, wdown, out_o, dh_o, dmix_o, gg_o, piece_o, a2, a2t, acc, dacc):
    step = pl.program_id(0)
    pl.when(step == 0)(lambda: feed_open(hid, gain, a2, a2t, acc, dacc))
    values = feed_grads(a2t, cot, *feed_tile(a2, cot, whid, wdown, acc, dacc))
    units = whid.shape[4]
    quarter_units = piece_o.shape[2] // 3
    tiles_per = quarter_units // units
    rows = piece_rows(lax.rem(step, tiles_per), units, quarter_units)
    for value, (row, n) in zip(values, rows):
        piece_o[:, step // tiles_per, pl.ds(pl.multiple_of(row, 128), n), :] = value

    @pl.when(step == pl.num_programs(0) - 1)
    def _():
        dmix_o[...] = feed_close(hid, gain, cot, acc, dacc, out_o, dh_o, gg_o)


def feed_forward(hid, gain, cot, whid, wdown):
    rows, width = hid.shape
    blocks, nt, _, depth, units = whid.shape
    tile = 256
    per = units // tile
    hid_spec = pl.BlockSpec((blocks, 1, 2, depth, tile), lambda i: (0, i // per, 0, 0, lax.rem(i, per)))
    down_spec = pl.BlockSpec((blocks, 1, tile, 128), lambda i: (0, i // per, lax.rem(i, per), 0))
    sds = jax.ShapeDtypeStruct
    piece = (blocks, nt, 3 * units, 128)

    def fixed(*shape):
        return pl.BlockSpec(shape, lambda i: (0,) * len(shape))

    return pl.pallas_call(
        feed_kernel,
        grid=(nt * per,),
        in_specs=[fixed(rows, width), fixed(1, width), fixed(rows, width), hid_spec, down_spec],
        out_specs=[fixed(rows, width), fixed(rows, width), fixed(rows, width), fixed(1, width),
                   fixed(*piece)],
        out_shape=[sds((rows, width), BF16), sds((rows, width), F32), sds((rows, width), BF16),
                   sds((1, width), F32), sds(piece, BF16)],
        scratch_shapes=[pltpu.VMEM((rows, width), BF16), pltpu.VMEM((width, rows), BF16),
                        pltpu.VMEM((rows, width), F32), pltpu.VMEM((rows, width), F32)],
        compiler_params=pltpu.CompilerParams(vmem_limit_bytes=VMEM_LIMIT),
        name="feed_forward",
    )(hid, gain, cot, whid, wdown)


def row_columns(rows_list, rows):
    return jnp.concatenate(
        [stack_columns([r[:, c : c + 128] for r in rows_list]) for c in range(0, rows, 128)], axis=0
    )


def down_rows(at, dq, dz, dx, dkv, db, drow, wq, win, stp, wsh):
    total = dot_nt(dq[at, :], wq[...]) + dot_nt(dz[at, :], win[0]) + dot_nt(dx[at, :], win[1])
    total = total + dot_nt(dkv[at, :], wsh[:, 0:256]) + dot_nt(db[at, :], wsh[:, 256:])
    return total + dot_tn(drow[:, at].astype(BF16), stp[...])


def down_kernel(dq, dz, dx, dkv, db, drow, wq, win, stp, wsh, part_o):
    every = slice(None)
    part_o[...] = down_rows(every, dq, dz, dx, dkv, db, drow, wq, win, stp, wsh).astype(BF16)


def down_parts(dq, dz, dx, dkv, db, drow, wq, win, stp, wsh):
    total, inner = dz.shape
    width = wq.shape[0]
    rows = 256

    def tall(v):
        return pl.BlockSpec((rows, v.shape[1]), lambda i: (i, 0))

    wide = pl.BlockSpec((8, rows), lambda i: (0, i))
    return pl.pallas_call(
        down_kernel,
        grid=(total // rows,),
        in_specs=[tall(dq), tall(dz), tall(dx), tall(dkv), tall(db), wide, whole_spec(wq), whole_spec(win),
                  whole_spec(stp), whole_spec(wsh)],
        out_specs=pl.BlockSpec((rows, width), lambda i: (i, 0)),
        out_shape=jax.ShapeDtypeStruct((total, width), BF16),
        compiler_params=pltpu.CompilerParams(vmem_limit_bytes=VMEM_LIMIT),
        cost_estimate=pl.CostEstimate(flops=int(3e9), bytes_accessed=int(8e6), transcendentals=0),
        name="down_parts",
    )(dq, dz, dx, dkv, db, drow, wq, win, stp, wsh)


def weight_columns(a, g, dq, dz, dx, dkv, db, ot, mt, put, put_shared):
    at = a.T
    inner = dz.shape[1]

    def by_rows(values, first):
        for j in range(values.shape[1] // 128):
            for k in range(2):
                put(k, first + 128 * j, values[128 * k : 128 * (k + 1), 128 * j : 128 * (j + 1)])

    def by_lanes(values, first):
        for k in range(2):
            put(k, first, values[:, 128 * k : 128 * (k + 1)])

    by_rows(dot_nn(at, dq[...]).astype(BF16), 0)
    by_lanes(dot_nn(ot[...], g).astype(BF16), 128)
    by_rows(dot_nn(at, dz[...]).astype(BF16), 256)
    by_rows(dot_nn(at, dx[...]).astype(BF16), 256 + inner)
    by_lanes(dot_nn(mt[...], g).astype(BF16), 256 + 2 * inner)
    for first, values in ((0, dot_nn(at, dkv[...]).astype(BF16)), (256, dot_nn(at, db[...]).astype(BF16))):
        for k in range(2):
            put_shared(k, first, values[128 * k : 128 * (k + 1)])


def weight_kernel(a1, dq, dz, dx, dkv, db, drow, o, m, dmix, piece_o, shared_o, step_o, ot, mt):
    @pl.when(pl.program_id(0) == 0)
    def _():
        ot[...] = o[...].T
        mt[...] = m[...].T

    step_o[...] = dot_nn(drow[...].astype(BF16), a1[...])

    def put(k, first, values):
        piece_o[k, first : first + values.shape[0], :] = values

    def put_shared(k, first, values):
        shared_o[k, :, first : first + values.shape[1]] = values

    weight_columns(a1[...], dmix[...], dq, dz, dx, dkv, db, ot, mt, put, put_shared)


def weight_pieces(a1, dq, dz, dx, dkv, db, drow, o, m, dmix):
    total, width = a1.shape
    inner = dz.shape[1]
    n = 256 + 3 * inner
    shared = 256 + db.shape[1]
    cols = pl.BlockSpec((total, 256), lambda i: (0, i))
    sds = jax.ShapeDtypeStruct
    args = (dq, dz, dx, dkv, db, drow, o, m)
    return pl.pallas_call(
        weight_kernel,
        grid=(width // 256,),
        in_specs=[cols] + [whole_spec(v) for v in args] + [cols],
        out_specs=[pl.BlockSpec((2, n, 128), lambda i: (i, 0, 0)),
                   pl.BlockSpec((2, 128, shared), lambda i: (i, 0, 0)),
                   pl.BlockSpec((8, 256), lambda i: (0, i))],
        out_shape=[sds((width // 128, n, 128), BF16), sds((width // 128, 128, shared), BF16),
                   sds((8, width), F32)],
        scratch_shapes=[pltpu.VMEM((128, total), BF16), pltpu.VMEM((inner, total), BF16)],
        compiler_params=pltpu.CompilerParams(vmem_limit_bytes=VMEM_LIMIT),
        cost_estimate=pl.CostEstimate(flops=int(4e9), bytes_accessed=int(12e6), transcendentals=0),
        name="weight_pieces",
    )(a1, *args, dmix)


class Exchange:
    def __init__(self, own, landed, send, recv, d, z, nt):
        self.own, self.landed, self.z, self.nt = own, landed, z, nt
        self.copies = [
            remote_copy(own, landed.at[k - 1], send.at[k - 1], recv.at[k - 1], peer)
            for k, peer in enumerate(other_quarters(d, z, nt), 1)
        ]

    def start(self):
        for copy in self.copies:
            copy.start()

    def wait(self):
        for copy in self.copies:
            copy.wait()

    def total(self):
        total = None
        for q in range(self.nt):
            value = jnp.where(self.z == q, self.own[...].astype(F32), 0.0)
            for k in range(1, self.nt):
                value = value + jnp.where(
                    lax.rem(self.z - k + self.nt, self.nt) == q, self.landed[k - 1].astype(F32), 0.0
                )
            total = value if total is None else total + value
        return total


class ChainScatter:
    def __init__(self, parts, bufs, landed, send, recv, d, z, nt):
        self.parts, self.bufs, self.landed = parts, bufs, landed
        self.send, self.recv = send, recv
        self.d, self.z, self.nt = d, z, nt

    def active(self, way, t):
        z, nt = self.z, self.nt
        if way == 0:
            return (z <= t) & (z < nt - 1)
        return (nt - 1 - z <= t) & (z > 0)

    def copy(self, way, t):
        dev = (self.d, self.z + 1 if way == 0 else self.z - 1)
        return remote_copy(
            self.bufs.at[way, t], self.landed.at[way, t], self.send.at[way, t], self.recv.at[way, t], dev
        )

    def arrives(self, way, t):
        z, nt = self.z, self.nt
        if way == 0:
            return (z >= 1) & (z - 1 <= t)
        return (z < nt - 1) & (nt - 2 - z <= t)

    def step(self, t):
        z, nt = self.z, self.nt
        for way in range(2):
            q = nt - 1 - t + z if way == 0 else t - (nt - 1) + z

            def run():
                value = self.parts[q]
                if t > 0:
                    came = self.arrives(way, t - 1)

                    @pl.when(came)
                    def _():
                        self.copy(way, t - 1).wait_recv()
                        total = value.astype(F32) + self.landed[way, t - 1].astype(F32)
                        self.bufs[way, t] = total.astype(BF16)

                    @pl.when(jnp.logical_not(came))
                    def _():
                        self.bufs[way, t] = value
                else:
                    self.bufs[way, t] = value
                self.copy(way, t).start()

            pl.when(self.active(way, t))(run)

    def finish(self, out):
        out[...] = self.parts[self.z].astype(F32)
        t = self.nt - 2
        for way in range(2):

            @pl.when(self.arrives(way, t))
            def _():
                self.copy(way, t).wait_recv()
                out[...] += self.landed[way, t].astype(F32)

    def drain(self):
        for way in range(2):
            for t in range(self.nt - 1):
                pl.when(self.active(way, t))(self.copy(way, t).wait_send)


def chain_scratch(nt, rows, width):
    dma = pltpu.SemaphoreType.DMA
    return [
        pltpu.VMEM((2, nt - 1, rows, width), BF16),
        pltpu.VMEM((2, nt - 1, rows, width), BF16),
        dma((2, nt - 1)),
        dma((2, nt - 1)),
    ]


def mix_scatter_kernel(channels, nt, feed, *refs):
    (o, y_in, gate_in, sq, gain, watt, wmam, tok), refs = refs[:8], refs[8:]
    if feed:
        (hid_z, dwn_z), refs = refs[2:4], refs[4:]
        (m_o, sq_o, hid_o, hid_f, dwn_f), refs = refs[:5], refs[5:]
        (lsem, f_send, f_recv), refs = refs[:3], refs[3:]
    else:
        (m_o, sq_o, hid_o), refs = refs[:3], refs[3:]
    (y, z_in, in_sem, sq_land, sq_send, sq_recv, parts, bufs, landed, c_send, c_recv) = refs
    d = lax.axis_index("dp")
    z = lax.axis_index("tensor")
    rows = tok.shape[0]

    def rows_of(q):
        return pl.ds(pl.multiple_of(q * rows, rows), rows)

    def load(q):
        at = rows_of(q)
        return [
            pltpu.make_async_copy(y_in.at[at], y.at[at], in_sem.at[0, q]),
            pltpu.make_async_copy(gate_in.at[at], z_in.at[at], in_sem.at[1, q]),
        ]

    first = jnp.where(z < nt // 2, nt - 1, 0)
    for k in range(nt):
        for copy in load(lax.rem(first + k, nt)):
            copy.start()
    peers = [(p, z) for p in cube_peers(d)] if feed else []
    greet(peers + other_quarters(d, z, nt))
    squares = Exchange(sq, sq_land, sq_send, sq_recv, d, z, nt)
    squares.start()
    n = 2 * nt - 1
    if feed:
        items = []
        for k in range(1, nt):
            q = lax.rem(z - k + nt, nt)
            items.append((hid_z.at[q], lambda s, q=q: hid_f.at[s, q]))
            if k < nt - 1:
                items.append((dwn_z.at[q], lambda s, q=q: dwn_f.at[s, q]))
        half = dwn_z.shape[1] // 2
        for first_row in (0, half):
            at = pl.ds(first_row, half)
            items.append((dwn_z.at[q, at], lambda s, q=q, at=at: dwn_f.at[s, q, at]))
        cube = CubeGather(items, (0, 2, 5), f_send, f_recv, d, z)
        for i in range(n):
            cube.start(i)
        locals_ = []
        for i, (src, dst) in enumerate([(src, at(d)) for src, at in items]):
            locals_.append(pltpu.make_async_copy(src, dst, lsem.at[i]))
            locals_[-1].start()
    chain = ChainScatter(parts, bufs, landed, c_send, c_recv, d, z, nt)
    squares.wait()
    sq_o[...] = squares.total()

    def part(q):
        at = rows_of(q)
        for copy in load(q):
            copy.wait()
        total = sq_o[:, at]
        r = row_columns([lax.rsqrt(total / channels + epsilon)], rows)[:, 0:1]
        zv = z_in[at, :]
        m = (y[at, :] * (zv * sigmoid(zv)) * r * gain[...]).astype(BF16)
        m_o[at, :] = m
        parts[q] = (dot_nn(o[at, :], watt[...]) + dot_nn(m, wmam[...])).astype(BF16)

    part(first)
    chain.step(0)

    def rest(i, carry):
        part(lax.rem(first + 1 + i, nt))
        return carry

    lax.fori_loop(0, nt - 1, rest, 0)
    for t in range(1, nt - 1):
        chain.step(t)
        if feed and t == 1:
            for i in range(n):
                cube.near(i)
    if feed:
        for i in range(n):
            cube.far(i)
    chain.finish(hid_o)
    hid_o[...] += tok[...].astype(F32)
    chain.drain()
    if feed:
        cube.finish()
        for copy in locals_:
            copy.wait()


def mix_scatter(channels, nt, o, y, zr, sq, gain, watt, wmam, tok, feed=()):
    total, inner = y.shape
    rows, width = tok.shape
    dma = pltpu.SemaphoreType.DMA
    sds = jax.ShapeDtypeStruct
    vmem = pl.BlockSpec(memory_space=pltpu.VMEM)
    anywhere = pl.BlockSpec(memory_space=pl.ANY)
    outs = [sds((total, inner), BF16), sds((8, total), F32), sds((rows, width), F32)]
    scratch = []
    n = 2 * nt - 1
    if feed:
        for v in feed[:2]:
            outs.append(sds(v.shape, BF16))
        scratch = [dma((n,)), dma((n, 7)), dma((n, 7))]
    return pl.pallas_call(
        partial(mix_scatter_kernel, channels, nt, bool(feed)),
        in_specs=[vmem, anywhere, anywhere] + [vmem] * 5 + [anywhere] * len(feed[:2]) + [vmem] * len(feed[2:]),
        out_specs=[vmem] * 3 + [anywhere] * (len(outs) - 3),
        out_shape=outs,
        input_output_aliases={8: 3, 9: 4} if feed else {},
        scratch_shapes=scratch + [pltpu.VMEM((total, inner), F32), pltpu.VMEM((total, inner), F32),
                                  dma((2, nt)), pltpu.VMEM((nt - 1, 8, total), F32), dma((nt - 1,)), dma((nt - 1,)),
                        pltpu.VMEM((nt, rows, width), BF16)] + chain_scratch(nt, rows, width),
        compiler_params=pltpu.CompilerParams(
            vmem_limit_bytes=VMEM_LIMIT, collective_id=1, has_side_effects=True
        ),
        cost_estimate=pl.CostEstimate(flops=int(1e9), bytes_accessed=int(130e6), transcendentals=int(4e5)),
        name="mix_scatter",
    )(o, y, zr, sq, gain, watt, wmam, tok, *feed)


class ChainGather:
    def __init__(self, own, slots, send, recv, d, z, nt):
        self.own, self.slots, self.send, self.recv = own, slots, send, recv
        self.d, self.z, self.nt = d, z, nt

    def copy(self, way, dist):
        dev = (self.d, self.z + 1 if way == 0 else self.z - 1)
        slot = self.z - dist if way == 0 else self.z + dist
        src = self.own if dist == 0 else self.slots.at[slot]
        return remote_copy(src, self.slots.at[slot], self.send.at[way, dist], self.recv.at[way, dist], dev)

    def landing(self, way, dist):
        slot = self.z - dist if way == 0 else self.z + dist
        return remote_copy(
            self.slots.at[slot], self.slots.at[slot], self.send.at[way, dist - 1],
            self.recv.at[way, dist - 1], (self.d, self.z),
        )

    def has(self, way, dist):
        return self.z >= dist if way == 0 else self.z + dist < self.nt

    def goes_on(self, way):
        return self.z < self.nt - 1 if way == 0 else self.z > 0

    def start(self):
        for way in range(2):
            pl.when(self.goes_on(way))(self.copy(way, 0).start)

    def hop(self, dist):
        for way in range(2):
            pl.when(self.has(way, dist))(self.landing(way, dist).wait_recv)
            if dist < self.nt - 1:
                pl.when(self.has(way, dist) & self.goes_on(way))(self.copy(way, dist).start)

    def drain(self):
        for way in range(2):
            pl.when(self.goes_on(way))(self.copy(way, 0).wait_send)
            for dist in range(1, self.nt - 1):
                pl.when(self.has(way, dist) & self.goes_on(way))(self.copy(way, dist).wait_send)


class Unmix:
    def __init__(self, y, z_in, gain, watt, wmam, g_o, do_o, dm_o, dots, rows):
        self.ins = (y, z_in, gain, watt, wmam)
        self.outs = (g_o, do_o, dm_o, dots)
        self.rows = rows

    def __call__(self, q, g):
        y, z_in, gain, watt, wmam = self.ins
        g_o, do_o, dm_o, dots_o = self.outs
        rows = self.rows
        at = pl.ds(pl.multiple_of(q * rows, rows), rows)
        if g_o is not None:
            g_o[at, :] = g
        do_o[at, :] = dot_nt(g, watt[...]).astype(BF16)
        dm = dot_nt(g, wmam[...])
        dm_o[at, :] = dm
        zv = z_in[at, :]
        dots = jnp.sum(dm * gain[...] * (y[at, :] * (zv * sigmoid(zv))), axis=1, keepdims=True)
        turned = [jnp.broadcast_to(dots[c : c + 128], (128, 128)).T[0:8, :] for c in range(0, rows, 128)]
        dots_o[:, at] = jnp.concatenate(turned, axis=1)

    def around(self, z, dist, nt, slots, after=lambda q: None):
        def side(way, carry):
            q = jnp.where(way == 0, z - dist, z + dist)

            @pl.when((q >= 0) & (q < nt))
            def _():
                self(q, slots[q])
                after(q)

            return carry

        lax.fori_loop(0, 2, side, 0)


def unmix_gather_kernel(nt, *refs):
    (dmix, y, z_in, gain, watt, wmam), refs = refs[:6], refs[6:]
    (g_o, do_o, dm_o, dot_o), refs = refs[:4], refs[4:]
    (slots, g_send, g_recv, dot_own, dot_land, d_send, d_recv) = refs
    d = lax.axis_index("dp")
    z = lax.axis_index("tensor")
    greet(other_quarters(d, z, nt))
    chain = ChainGather(dmix, slots, g_send, g_recv, d, z, nt)
    chain.start()
    work = Unmix(y, z_in, gain, watt, wmam, g_o, do_o, dm_o, dot_own, dmix.shape[0])
    work(z, dmix[...])
    for dist in range(1, nt):
        chain.hop(dist)
        work.around(z, dist, nt, slots)
    dots = Exchange(dot_own, dot_land, d_send, d_recv, d, z, nt)
    dots.start()
    chain.drain()
    dots.wait()
    dot_o[...] = dots.total()


def unmix_shapes(total, width, inner):
    sds = jax.ShapeDtypeStruct
    return [sds((total, width), BF16), sds((total, 128), BF16), sds((total, inner), F32),
            sds((8, total), F32)]


def unmix_scratch(nt, rows, width, total):
    dma = pltpu.SemaphoreType.DMA
    return [pltpu.VMEM((nt, rows, width), BF16), dma((2, nt - 1)), dma((2, nt - 1)),
            pltpu.VMEM((8, total), F32), pltpu.VMEM((nt - 1, 8, total), F32), dma((nt - 1,)), dma((nt - 1,))]


def unmix_gather(nt, dmix, y, zr, gain, watt, wmam):
    total, inner = y.shape
    rows, width = dmix.shape
    vmem = pl.BlockSpec(memory_space=pltpu.VMEM)
    return pl.pallas_call(
        partial(unmix_gather_kernel, nt),
        in_specs=[vmem] * 6,
        out_specs=[vmem] * 4,
        out_shape=unmix_shapes(total, width, inner),
        scratch_shapes=unmix_scratch(nt, rows, width, total),
        compiler_params=pltpu.CompilerParams(
            vmem_limit_bytes=VMEM_LIMIT, collective_id=2, has_side_effects=True
        ),
        name="unmix_gather",
    )(dmix, y, zr, gain, watt, wmam)


BOXES = 4


def feed_unmix_kernel(nt, *refs):
    (hid, gain, cot, whid, wdown, y_in, gate_in, mgain, watt_in, wmam_in), refs = refs[:10], refs[10:]
    (out_o, dh_o, gg_o, g_o, do_o, dm_o, dot_o, own_o, raw_o, sum_o), refs = refs[:10], refs[10:]
    (y, z_in, watt, wmam, out, dh, dm, in_sem, out_sem, g_sem, dm_sem), refs = refs[:11], refs[11:]
    (a2, a2t, acc, dacc, fs, dgs, dus, dmix, piece, sent, came, b_send, b_recv), refs = refs[:13], refs[13:]
    boxes, refs = refs[: 8 * (nt - 2)], refs[8 * (nt - 2) :]
    (slots, g_send, g_recv) = refs
    step = pl.program_id(0)
    tiles = pl.num_programs(0) // 2
    d = lax.axis_index("dp")
    z = lax.axis_index("tensor")
    core = lax.rem(d, 2)
    bits = dp_bits(d)
    peers = cube_peers(d)
    chain = ChainGather(dmix, slots, g_send, g_recv, d, z, nt)
    cubes = []
    for k in range(1, nt - 1):
        q = quarter_at(k - 1, z, nt)
        box = boxes[8 * k - 8 : 8 * k]
        cubes.append(
            SquareScatter(lambda i, j, q=q: (2 * i + j, q), piece, box[:6], box[6], box[7], peers, bits, z)
        )

    rows = hid.shape[0]
    late = [
        pltpu.make_async_copy(src, dst, in_sem.at[i])
        for i, (src, dst) in enumerate(((y_in, y), (gate_in, z_in), (watt_in, watt), (wmam_in, wmam)))
    ]

    def rows_of(q):
        return pl.ds(pl.multiple_of(q * rows, rows), rows)

    def store_g(q):
        return pltpu.make_async_copy(slots.at[q], g_o.at[rows_of(q)], g_sem.at[q])

    def store_dm(q):
        return pltpu.make_async_copy(dm.at[rows_of(q)], dm_o.at[rows_of(q)], dm_sem.at[q])

    ready = [
        pltpu.make_async_copy(src, dst, out_sem.at[i])
        for i, (src, dst) in enumerate(
            (
                (out, out_o),
                (dh, dh_o),
                (dmix, g_o.at[rows_of(z)]),
                (piece.at[:, z], own_o),
                (piece.at[:, quarter_at(2, z, nt)], raw_o),
            )
        )
    ]

    @pl.when(step == 0)
    def _():
        for copy in late:
            copy.start()
        greet([(p, z) for p in peers] + other_quarters(d, z, nt))
        feed_open(hid, gain, a2, a2t, acc, dacc)

    @pl.when(step < tiles)
    def _():
        fs[step], dgs[step], dus[step] = feed_tile(a2, cot, whid, wdown, acc, dacc)

    @pl.when(step == tiles - 1)
    def _():
        dmix[...] = feed_close(hid, gain, cot, acc, dacc, out, dh, gg_o)
        chain.start()
        for copy in ready[:3]:
            copy.start()

    units = whid.shape[4]
    quarter_units = piece.shape[2] // 3
    tiles_per = quarter_units // units

    def swap(turn_):
        box = lax.rem(turn_, BOXES)
        return remote_copy(
            sent.at[box], came.at[box], b_send.at[box], b_recv.at[box], (peers[0], z)
        )

    def places(turn_):
        quarter = quarter_at(turn_ // tiles_per, z, nt)
        part = lax.rem(turn_, tiles_per)
        return quarter, part, piece_rows(part, units, quarter_units)

    def take(turn_):
        swap(turn_).wait_recv()
        quarter, _, rows = places(turn_)
        box = lax.rem(turn_, BOXES)
        first = 0
        for row, n in rows:
            at = pl.ds(pl.multiple_of(row, 128), n)
            piece[:, quarter, at, :] = add_refs(
                piece[:, quarter, at, :], came[box, :, first : first + n, :]
            ).astype(BF16)
            first += n

    @pl.when(step >= tiles)
    def _():
        turn_ = step - tiles
        quarter, part, rows = places(turn_)
        tile = quarter * tiles_per + part
        box = lax.rem(turn_, BOXES)
        pl.when(turn_ >= BOXES)(lambda: swap(turn_ - BOXES).wait_send())
        first = 0
        for value, (row, n) in zip(feed_grads(a2t, cot, fs[tile], dgs[tile], dus[tile]), rows):
            at = pl.ds(pl.multiple_of(row, 128), n)
            value = value.reshape(value.shape[0] // 2, 2, n, 128)
            even, odd = value[:, 0], value[:, 1]
            piece[:, quarter, at, :] = jnp.where(core == 0, even, odd)
            sent[box, :, first : first + n, :] = jnp.where(core == 0, odd, even)
            first += n
        swap(turn_).start()
        pl.when(turn_ == tiles - 1)(lambda: chain.hop(1))
        pl.when(turn_ >= 1)(lambda: take(turn_ - 1))
        for k in range(1, nt - 1):
            pl.when(turn_ == k * tiles_per)(cubes[k - 1].start)

    @pl.when(step == 2 * tiles - 1)
    def _():
        take(tiles - 1)
        for i in range(BOXES):
            swap(tiles - BOXES + i).wait_send()
        for copy in ready[3:]:
            copy.start()
        for copy in late:
            copy.wait()
        work = Unmix(y, z_in, mgain, watt, wmam, None, do_o, dm, dot_o, rows)
        work(z, dmix[...])
        store_dm(z).start()

        def after(q):
            store_g(q).start()
            store_dm(q).start()

        for dist in range(1, nt):
            if dist > 1:
                chain.hop(dist)
            work.around(z, dist, nt, slots, after)
            if dist == 1:
                cubes[0].middle()
            if dist < nt - 2:
                cubes[dist].middle()
        for k, cube in enumerate(cubes):
            cube.finish(sum_o.at[k])
        chain.drain()
        for cube in cubes:
            cube.drain()
        for copy in ready:
            copy.wait()
        for q in range(nt):
            store_dm(q).wait()
            pl.when(z != q)(store_g(q).wait)


def feed_unmix(nt, hid, gain, cot, whid, wdown, y, zr, mgain, watt, wmam):
    rows, width = hid.shape
    total, inner = y.shape
    blocks, _, _, depth, units = whid.shape
    tile = 256
    per = units // tile
    tiles = nt * per
    kept = blocks // 2
    n = 3 * units
    dma = pltpu.SemaphoreType.DMA
    sds = jax.ShapeDtypeStruct

    def fixed(v):
        return pl.BlockSpec(v.shape, lambda i: (0,) * len(v.shape), pipeline_mode=pl.Buffered(1))

    def at_tile(i):
        return jnp.minimum(i, tiles - 1)

    hid_spec = pl.BlockSpec(
        (blocks, 1, 2, depth, tile), lambda i: (0, at_tile(i) // per, 0, 0, lax.rem(at_tile(i), per))
    )
    down_spec = pl.BlockSpec(
        (blocks, 1, tile, 128), lambda i: (0, at_tile(i) // per, lax.rem(at_tile(i), per), 0)
    )
    out_shape = [sds((rows, width), BF16), sds((rows, width), F32), sds((1, width), F32)]
    out_shape += unmix_shapes(total, width, inner)
    out_shape += [sds((kept, n, 128), BF16), sds((kept, n, 128), BF16), sds((nt - 2, n, 128), BF16)]
    anywhere = pl.BlockSpec(memory_space=pl.ANY)
    late = [pltpu.VMEM(v.shape, v.dtype) for v in (y, zr, watt, wmam) + tuple(out_shape[:2])]
    late += [pltpu.VMEM((total, inner), F32), dma((4,)), dma((5,)), dma((nt,)), dma((nt,))]
    box = pltpu.VMEM((BOXES, kept, 3 * tile, 128), BF16)
    kept_tile = pltpu.VMEM((tiles, rows, tile), BF16)
    scratch = [pltpu.VMEM((rows, width), BF16), pltpu.VMEM((width, rows), BF16),
               pltpu.VMEM((rows, width), F32), pltpu.VMEM((rows, width), F32), kept_tile, kept_tile, kept_tile,
               pltpu.VMEM((rows, width), BF16), pltpu.VMEM((kept, nt, n, 128), BF16), box, box, dma((BOXES,)),
               dma((BOXES,))]
    for _ in range(nt - 2):
        scratch += square_scratch(n, 128)
    return pl.pallas_call(
        partial(feed_unmix_kernel, nt),
        grid=(2 * tiles,),
        in_specs=[fixed(hid), fixed(gain), fixed(cot), hid_spec, down_spec, anywhere, anywhere, fixed(mgain),
                  anywhere, anywhere],
        out_specs=[anywhere if i in (0, 1, 3, 5, 7, 8) else fixed(v) for i, v in enumerate(out_shape)],
        out_shape=out_shape,
        scratch_shapes=late + scratch + unmix_scratch(nt, rows, width, total)[:3],
        compiler_params=pltpu.CompilerParams(
            vmem_limit_bytes=60 * 1024 * 1024, collective_id=4, has_side_effects=True
        ),
        cost_estimate=pl.CostEstimate(flops=int(1e10), bytes_accessed=int(150e6), transcendentals=int(9e5)),
        name="feed_unmix",
    )(hid, gain, cot, whid, wdown, y, zr, mgain, watt, wmam)


def add_refs(left, right):
    return left.astype(F32) + right.astype(F32)


class SquareScatter:
    def __init__(self, place, held, bufs, send, recv, peers, bits, z):
        (self.r1, self.r2, self.ob, self.tb, self.r3, self.r4) = bufs
        self.place, self.held = place, held
        n = held.shape[-2]
        half = n // 2
        self.lo, self.hi = pl.ds(0, half), pl.ds(half, n - half)
        self.half = half
        _, self.x, self.y = bits
        x, y = self.x, self.y
        _, d_x, d_y = peers
        self.copies = []
        for i in range(2):
            self.copies.append(
                remote_copy(held.at[place(i, 1 - x) + (self.lo,)], self.r1.at[i], send.at[i], recv.at[i],
                            (d_x, z))
            )
        for j in range(2):
            self.copies.append(
                remote_copy(held.at[place(1 - y, j) + (self.hi,)], self.r2.at[j], send.at[2 + j],
                            recv.at[2 + j], (d_y, z))
            )
        self.copies.append(remote_copy(self.ob.at[1 - y], self.r3, send.at[4], recv.at[4], (d_y, z)))
        self.copies.append(remote_copy(self.tb.at[1 - x], self.r4, send.at[5], recv.at[5], (d_x, z)))

    def start(self):
        for copy in self.copies[:4]:
            copy.start()

    def middle(self):
        for i in range(2):
            self.copies[i].wait_recv()
            self.ob[i] = add_refs(self.held[self.place(i, self.x) + (self.lo,)], self.r1[i]).astype(BF16)
        self.copies[4].start()
        for j in range(2):
            self.copies[2 + j].wait_recv()
            self.tb[j] = add_refs(self.held[self.place(self.y, j) + (self.hi,)], self.r2[j]).astype(BF16)
        self.copies[5].start()

    def finish(self, out):
        self.copies[4].wait_recv()
        out[0 : self.half] = add_refs(self.ob[self.y], self.r3[...]).astype(out.dtype)
        self.copies[5].wait_recv()
        out[self.half :] = add_refs(self.tb[self.x], self.r4[...]).astype(out.dtype)

    def drain(self):
        for copy in self.copies:
            copy.wait_send()


def square_scratch(n, lanes):
    dma = pltpu.SemaphoreType.DMA
    half = n // 2
    return [
        pltpu.VMEM((2, half, lanes), BF16),
        pltpu.VMEM((2, n - half, lanes), BF16),
        pltpu.VMEM((2, half, lanes), BF16),
        pltpu.VMEM((2, n - half, lanes), BF16),
        pltpu.VMEM((half, lanes), BF16),
        pltpu.VMEM((n - half, lanes), BF16),
        dma((6,)),
        dma((6,)),
    ]


class CubeScatter:
    def __init__(self, pieces, bufs, peers, bits, z):
        (self.rc, self.held, self.send, self.recv) = bufs[:4]
        self.p = pieces
        self.core = bits[0]
        self.peer = (peers[0], z)
        self.square = SquareScatter(
            lambda i, j: (2 * i + j,), self.held, bufs[4:10], bufs[10], bufs[11], peers, bits, z
        )

    def swap(self, i):
        return remote_copy(
            self.p.at[i, 1 - self.core], self.rc.at[i], self.send.at[i], self.recv.at[i], self.peer
        )

    def middle(self):
        for i in range(4):
            self.swap(i).wait_recv()
            self.held[i] = add_refs(self.p[i, self.core], self.rc[i]).astype(BF16)
        self.square.start()

    def last(self):
        self.square.middle()

    def finish(self, out):
        self.square.finish(out)

    def drain(self):
        for i in range(4):
            self.swap(i).wait_send()
        self.square.drain()


def cube_scratch(n, lanes):
    dma = pltpu.SemaphoreType.DMA
    return [
        pltpu.VMEM((4, n, lanes), BF16),
        pltpu.VMEM((4, n, lanes), BF16),
        dma((4,)),
        dma((4,)),
    ] + square_scratch(n, lanes)


class CubeTotal:
    def __init__(self, held, landed, send, recv, peers, z):
        self.held, self.landed = held, landed
        self.copies = [
            remote_copy(held.at[i], landed.at[i], send.at[i], recv.at[i], (peer, z))
            for i, peer in enumerate(peers)
        ]

    def start(self, i):
        self.copies[i].start()

    def take(self, i):
        self.copies[i].wait_recv()
        self.held[i + 1] = self.held[i] + self.landed[i]

    def drain(self):
        for copy in self.copies:
            copy.wait_send()


def norm_back(dy, v, gain, dh):
    f = lax.rsqrt(jnp.mean(v * v, axis=1, keepdims=True) + epsilon)
    gdy = dy * gain
    lean = jnp.sum(gdy * v, axis=1, keepdims=True) * (f * f * f / v.shape[1])
    return dh + (f * gdy - v * lean)


SMALL_ALL = 32
SMALL_ROWS = 160


def tail_kernel(
    nt, tok_in, gain, dh_in, a1_in, dmix_in, o_in, m_in, dq, dz, dx, dkv, db, drow, wq, win, stp, wsh,
    gg, gtb, gtx, grows, gheads, own_in, rest_in,
    gt_o, mixed_o, fed_o, sh_o, small_o,
    feed_own, a1, o, m, dmix, feed_rest, tok, dh, lsem,
    da, gone, parts, pieces, shared, ot, mt, bufs, landed, c_send, c_recv, *rest,
):
    cube_a, rest = rest[:12], rest[12:]
    cube_b, rest = rest[:12], rest[12:]
    square_c, rest = rest[:8], rest[8:]
    (sh_sum, sh_land, sh_send, sh_recv) = rest[:4]
    (sm_held, sm_land, sm_send, sm_recv, all_own, all_land, all_send, all_recv) = rest[4:]
    d = lax.axis_index("dp")
    z = lax.axis_index("tensor")
    bits = dp_bits(d)
    peers = cube_peers(d)
    rows = tok.shape[0]
    late = [
        pltpu.make_async_copy(src, dst, lsem.at[i])
        for i, (src, dst) in enumerate(
            [(own_in, feed_own), (a1_in, a1), (o_in, o), (m_in, m), (dmix_in, dmix), (rest_in, feed_rest),
             (tok_in, tok), (dh_in, dh)]
        )
    ]
    for copy in late:
        copy.start()
    greet([(p, z) for p in peers] + other_quarters(d, z, nt))
    three = SquareScatter(
        lambda i, j: (i, j), feed_own, square_c[:6], square_c[6], square_c[7], peers, bits, z
    )
    chain = ChainScatter(parts, bufs, landed, c_send, c_recv, d, z, nt)

    def part(q):
        at = pl.ds(pl.multiple_of(q * rows, rows), rows)
        parts[q] = down_rows(at, dq, dz, dx, dkv, db, drow, wq, win, stp, wsh).astype(BF16)

    first = jnp.where(z < nt // 2, nt - 1, 0)
    part(first)
    chain.step(0)

    def others(i, carry):
        part(lax.rem(first + 1 + i, nt))
        return carry

    late[0].wait()
    three.start()
    lax.fori_loop(0, nt - 1, others, 0)
    for copy in late[1:5]:
        copy.wait()
    gone[...] = jnp.zeros(gone.shape, F32)

    def gain_sums(q, carry):
        at = pl.ds(pl.multiple_of(q * rows, rows), rows)
        gone[...] += jnp.sum(parts[q].astype(F32) * a1[at, :].astype(F32), axis=0, keepdims=True)
        return carry

    lax.fori_loop(0, nt, gain_sums, 0)
    gone[...] = gone[...] / gain[...]
    sums = CubeTotal(sm_held, sm_land, sm_send, sm_recv, peers, z)
    for k in range(8):
        sm_held[0, k : k + 1, :] = gg[:, 128 * k : 128 * k + 128]
        sm_held[0, 24 + k : 25 + k, :] = gone[:, 128 * k : 128 * k + 128]
    for first_row, ref in ((8, gtb), (SMALL_ALL, gtx), (56, grows)):
        for k in range(ref.shape[1] // 128):
            sm_held[0, first_row + 8 * k : first_row + 8 * k + 8, :] = ref[:, 128 * k : 128 * k + 128]
    sm_held[0, 80:96, :] = gheads[...]
    steps = dot_nn(drow[...].astype(BF16), a1[...])
    for k in range(8):
        sm_held[0, 96 + 8 * k : 104 + 8 * k, :] = steps[:, 128 * k : 128 * k + 128]
    sums.start(0)
    ot[...] = o[...].T
    mt[...] = m[...].T

    def columns(i, carry):
        at = pl.ds(pl.multiple_of(i * 256, 256), 256)

        def put(k, first, values):
            pieces[i, k, first : first + values.shape[0], :] = values

        def put_shared(k, first, values):
            shared[i, k, :, first : first + values.shape[1]] = values

        weight_columns(a1[:, at], dmix[:, at], dq, dz, dx, dkv, db, ot, mt, put, put_shared)
        two.swap(i).start()
        one.swap(i).start()
        return carry

    one = CubeScatter(pieces, cube_a, peers, bits, z)
    two = CubeScatter(shared, cube_b, peers, bits, z)
    lax.fori_loop(0, 1, columns, 0)
    chain.step(1)
    three.middle()
    sums.take(0)
    sums.start(1)
    lax.fori_loop(1, 4, columns, 0)
    sums.take(1)
    sums.start(2)
    two.middle()
    one.middle()
    for t in range(2, nt - 1):
        chain.step(t)
    two.last()
    one.last()
    sums.take(2)
    all_own[...] = sm_held[3, 0:SMALL_ALL, :]
    over_all = Exchange(all_own, all_land, all_send, all_recv, d, z, nt)
    over_all.start()
    three.finish(fed_o)
    for copy in late[5:]:
        copy.wait()
    fed_o[...] += feed_rest[...]
    two.finish(sh_sum)
    per = sh_sum.shape[0] // nt
    copies = []
    for k in range(1, nt):
        q = lax.rem(z + k, nt)
        at = pl.ds(pl.multiple_of(q * per, per), per)
        copies.append(
            remote_copy(sh_sum.at[at], sh_land.at[k - 1], sh_send.at[k - 1], sh_recv.at[k - 1], (d, q))
        )
        copies[-1].start()
    one.finish(mixed_o)
    small_o[...] = sm_held[3]
    over_all.wait()
    small_o[0:SMALL_ALL, :] = over_all.total()
    for copy in copies:
        copy.wait()
    total = sh_sum[pl.ds(pl.multiple_of(z * per, per), per), :].astype(F32)
    for k in range(nt - 1):
        total = total + sh_land[k].astype(F32)
    sh_o[...] = total
    chain.finish(da)
    gt_o[...] = norm_back(da[...], tok[...].astype(F32), gain[...], dh[...]).astype(BF16)
    for thing in (chain, one, two, three, sums):
        thing.drain()


def tail(nt, *args):
    tok, a1, dz = args[0], args[3], args[8]
    feed_own = args[-2]
    rows, width = tok.shape
    total = a1.shape[0]
    inner = dz.shape[1]
    n, lanes = 256 + 3 * inner, 128
    s_rows, s_lanes = 128, args[16].shape[1]
    f_rows = feed_own.shape[2]
    late = (len(args) - 2, 3, 5, 6, 4, len(args) - 1, 0, 2)
    dma = pltpu.SemaphoreType.DMA
    sds = jax.ShapeDtypeStruct
    vmem = pl.BlockSpec(memory_space=pltpu.VMEM)
    return pl.pallas_call(
        partial(tail_kernel, nt),
        in_specs=[pl.BlockSpec(memory_space=pl.ANY) if i in late else vmem for i in range(len(args))],
        out_specs=[vmem] * 5,
        out_shape=[sds((rows, width), BF16), sds((n, lanes), F32), sds((f_rows, 128), F32),
                   sds((s_rows // nt, s_lanes), F32), sds((SMALL_ROWS, 128), F32)],
        scratch_shapes=[pltpu.VMEM(args[i].shape, args[i].dtype) for i in late] + [dma((len(late),))]
        + [pltpu.VMEM((rows, width), F32), pltpu.VMEM((1, width), F32), pltpu.VMEM((nt, rows, width), BF16),
                        pltpu.VMEM((4, 2, n, lanes), BF16), pltpu.VMEM((4, 2, s_rows, s_lanes), BF16),
                        pltpu.VMEM((128, total), BF16), pltpu.VMEM((inner, total), BF16)]
        + chain_scratch(nt, rows, width)
        + cube_scratch(n, lanes) + cube_scratch(s_rows, s_lanes) + square_scratch(f_rows, 128)
        + [pltpu.VMEM((s_rows, s_lanes), BF16), pltpu.VMEM((nt - 1, s_rows // nt, s_lanes), BF16),
           dma((nt - 1,)), dma((nt - 1,)),
           pltpu.VMEM((4, SMALL_ROWS, 128), F32), pltpu.VMEM((3, SMALL_ROWS, 128), F32), dma((3,)), dma((3,)),
           pltpu.VMEM((SMALL_ALL, 128), F32), pltpu.VMEM((nt - 1, SMALL_ALL, 128), F32), dma((nt - 1,)),
           dma((nt - 1,))],
        compiler_params=pltpu.CompilerParams(
            vmem_limit_bytes=VMEM_LIMIT, collective_id=3, has_side_effects=True
        ),
        cost_estimate=pl.CostEstimate(flops=int(7e9), bytes_accessed=int(150e6), transcendentals=0),
        name="tail",
    )(*args)


def finish_kernel(
    heads, place, mixed, fed, small, *refs
):
    (que_o, att_o, inn_o, mam_o, hid_o, dwn_o, norms_o, taps_o, chan_o, gain_o, step_o) = refs[-17:-6]
    heads_o = refs[-6:-3]
    for src, dst in zip(refs[:3], refs[-3:]):
        dst[...] = src[...]
    d, p = place[0], place[1]
    block = que_o.shape[0]
    inner = mam_o.shape[0]
    first = 0
    for j in range(que_o.shape[1] // 128):
        que_o[:, 128 * j : 128 * j + 128] = mixed[first : first + block]
        first += block
    att_o[...] = mixed[first : first + att_o.shape[0]]
    first += att_o.shape[0]
    for i in range(2):
        for j in range(inner // 128):
            inn_o[i, :, 128 * j : 128 * j + 128] = mixed[first : first + block]
            first += block
    mam_o[...] = mixed[first : first + inner]
    first = 0
    for i in range(2):
        for j in range(hid_o.shape[2] // 128):
            hid_o[i, :, 128 * j : 128 * j + 128] = fed[first : first + block]
            first += block
    dwn_o[...] = fed[first:]

    def lanes_from(values, lane):
        return pltpu.roll(values, lax.rem(128 - lane, 128), 1)

    width = norms_o.shape[1]
    per = 128 // width
    for i, base in enumerate((24, 0)):
        row = jnp.broadcast_to(small[pl.ds(base + p // per, 1), :], (8, 128))
        row = lanes_from(row, lax.rem(p, per) * width)
        norms_o[i : i + 1, :] = row[0:1, 0:width]
    width = taps_o.shape[1]
    per = 128 // width
    row = small[pl.ds(pl.multiple_of(8 + 8 * (p // per), 8), 8), :]
    taps_o[...] = lanes_from(row, lax.rem(p, per) * width)[0 : CONV + 1, 0:width]
    width = gain_o.shape[1]
    sums = jnp.zeros((8, 128), F32)
    lane = lanes_of(sums.shape)
    sub = lax.broadcasted_iota(jnp.int32, sums.shape, 0)
    for b in range(heads // 2):
        rows = lanes_from(small[SMALL_ALL + 8 * b : SMALL_ALL + 8 * b + 8, :], d * width)
        raw = small[56 + 8 * b : 64 + 8 * b, :]
        gains = lanes_from(raw, d * width)
        for k in range(2):
            h = 2 * b + k
            at = slice(64 * k, 64 * k + width)
            chan_o[:, h, :] = rows[0 : CONV + 1, at]
            gain_o[h : h + 1, :] = gains[0:1, at]
            skip = jnp.sum(jnp.where(lane // SSM_DIM == k, raw[1:2, :], 0.0), axis=1, keepdims=True)
            sums = jnp.where((sub == h) & (lane == 2), skip, sums)
    for k in range(2):
        total = jnp.sum(small[80 + 8 * k : 88 + 8 * k, :], axis=1, keepdims=True)
        sums = jnp.where(lane == k, total, sums)
    sums = jnp.concatenate([sums, jnp.zeros((120, 128), F32)], axis=0).T
    for k in range(3):
        heads_o[k][...] = sums[k : k + 1, 0:heads]
    steps = small[pl.ds(pl.multiple_of(96 + 8 * d, 8), 8), :]
    step_o[...] = steps[0:heads, :]


def finish(heads, place, mixed, fed, small, shapes, passed):
    vmem = pl.BlockSpec(memory_space=pltpu.VMEM)
    sds = jax.ShapeDtypeStruct
    return pl.pallas_call(
        partial(finish_kernel, heads),
        in_specs=[pl.BlockSpec(memory_space=pltpu.SMEM)] + [vmem] * 6,
        out_specs=[vmem] * (len(shapes) + 6),
        out_shape=[sds(s, F32) for s in shapes] + [sds((1, heads), F32)] * 3
        + [sds(v.shape, v.dtype) for v in passed],
        compiler_params=pltpu.CompilerParams(vmem_limit_bytes=VMEM_LIMIT),
        name="finish",
    )(place, mixed, fed, small, *passed)


def rope_wide(length):
    half = HEAD_SIZE // 2
    inverse = rope_base ** (-np.arange(half) * (2.0 / HEAD_SIZE))
    angles = np.arange(length)[:, None] * inverse[None, :]
    c, s = np.cos(angles), np.sin(angles)
    return (
        jnp.asarray(np.concatenate([c, c, c, c], axis=1), F32),
        jnp.asarray(np.concatenate([-s, s, -s, s], axis=1), F32),
    )


def to_blocks(full, axis, nt):
    if axis == 1:
        two, width, cols = full.shape
        return full.reshape(2, 8, width // 8, nt, cols // nt).transpose(1, 3, 0, 2, 4)
    rows, width = full.shape
    return full.reshape(nt, rows // nt, 8, width // 8).transpose(2, 0, 1, 3)


def per_device(
    nd,
    nt,
    tokens,
    query_proj,
    attend_out,
    inner_proj,
    step_proj,
    mamba_out,
    hidden_proj,
    down_proj,
    channel_taps,
    mixer_gain,
    decay_log,
    step_bias,
    skip_weight,
    shared_proj,
    norm_gains,
    shared_taps,
    cotangent,
):
    tensor_index = lax.axis_index("tensor")
    d = lax.axis_index("dp")
    local_rows, width = tokens.shape
    group_rows = local_rows * nt
    heads = step_proj.shape[1]
    inner = heads * SSM_DIM
    channels = inner * nt
    units = down_proj.shape[0]
    feed = ()
    if nd == 8:
        small = pack_small(channel_taps, mixer_gain, norm_gains, shared_taps, step_proj.T)
        (tok_full, full_query, full_attend, full_inner, full_mamba, sha, sma) = gather_start(
            tokens, query_proj, attend_out, inner_proj, mamba_out, shared_proj, small, nd, nt
        )
        scal = jnp.stack([decay_log, step_bias, skip_weight]).astype(F32)
        where = tensor_index.astype(jnp.int32).reshape(1)
        (
            gain_first, gain_second, gain_mix, taps_x, taps_b, step_rows, decay, bias, skip,
        ) = unpack_small(heads, where, scal, sma, width)
        full_shared = sha.reshape(width, -1)
        feed = (hidden_proj, down_proj)
    else:
        small_parts = [channel_taps, mixer_gain, norm_gains, shared_taps, step_proj.T]
        flat = jnp.concatenate([p.reshape(-1) for p in small_parts])
        small_len = -(-flat.shape[0] // 2048) * 2048
        small = jnp.pad(flat, (0, small_len - flat.shape[0])).reshape(-1, 128)
        (tok_full, full_query, full_attend, full_inner, full_mamba, sha, sma) = gather_start(
            tokens, query_proj, attend_out, inner_proj, mamba_out, shared_proj, small, nd, nt
        )
        full_hidden = lax.all_gather(hidden_proj, "tensor", axis=2, tiled=True)
        full_hidden = to_blocks(lax.all_gather(full_hidden, "dp", axis=1, tiled=True), 1, nt)
        full_down = lax.all_gather(down_proj, "tensor", axis=0, tiled=True)
        full_down = to_blocks(lax.all_gather(full_down, "dp", axis=1, tiled=True), 0, nt)

        full_shared = sha.reshape(width, -1)
        sma = sma.reshape(nd, nt, small_len)

        def small_piece(index):
            start = sum(p.size for p in small_parts[:index])
            part = small_parts[index]
            return sma[:, :, start : start + part.size].reshape((nd, nt) + part.shape)

        taps_x = pick(small_piece(0), tensor_index, 1).transpose(1, 2, 0, 3).reshape(CONV + 1, inner)
        gain_mix = pick(small_piece(1), tensor_index, 1).transpose(1, 0, 2).reshape(1, inner)
        full_norms = small_piece(2).transpose(2, 0, 1, 3).reshape(2, width).astype(F32)
        taps_b = small_piece(3).transpose(2, 0, 1, 3).reshape(CONV + 1, -1)
        step_rows = pick(small_piece(4), tensor_index, 1).transpose(1, 0, 2).reshape(heads, width)
        step_rows = jnp.pad(step_rows, ((0, 8 - heads), (0, 0)))
        taps_x = jnp.pad(taps_x.astype(F32), ((0, 7 - CONV), (0, 0)))
        taps_b = jnp.pad(taps_b.astype(F32), ((0, 7 - CONV), (0, 0)))
        gain_mix = gain_mix.astype(F32)
        gain_first = full_norms[0:1]
        gain_second = full_norms[1:2]

        def head_rows(values):
            return jnp.pad(jnp.broadcast_to(values[:, None], (heads, 128)), ((0, 8 - heads), (0, 0)))

        decay = head_rows(-jnp.exp(decay_log.astype(F32)))
        bias = head_rows(step_bias.astype(F32))
        skip = jnp.repeat(skip_weight.astype(F32), SSM_DIM)[None, :]
    q_heads = query_proj.shape[1] // HEAD_SIZE
    kv_head = (tensor_index * q_heads // (QHEADS // KVHEADS)).astype(jnp.int32).reshape(1)
    cosine, sine = rope_wide(group_rows)

    (a1, q, k2, v2, lse, o, xr, zr, br, y, trow, states, squares, *feed) = mixers_forward(
        heads, nt, kv_head, tok_full.reshape(group_rows, width), gain_first, full_query, full_inner, step_rows,
        full_shared, cosine, sine, taps_x, taps_b, decay, bias, skip, feed,
    )
    mixed = mix_scatter(
        channels, nt, o, y, zr, squares, gain_mix, full_attend, full_mamba, tokens, tuple(feed)
    )
    m, squares, hidden = mixed[:3]
    if nd == 8:
        full_hidden, full_down = mixed[3:]
    if nd == 8:
        layer_out, dh, grad_gain_two, grad_mix, do, dm, dots, feed_own, feed_raw, feed_sums = feed_unmix(
            nt, hidden, gain_second, cotangent, full_hidden, full_down, y, zr, gain_mix, full_attend, full_mamba
        )
        feed_own = feed_own.reshape((2, 2) + feed_own.shape[1:])
    else:
        layer_out, dh, dmix, grad_gain_two, feed_pieces = feed_forward(
            hidden, gain_second, cotangent, full_hidden, full_down
        )
        grad_mix, do, dm, dots = unmix_gather(nt, dmix, y, zr, gain_mix, full_attend, full_mamba)
        hid_full = feed_pieces[:, :, : 2 * units].reshape(8, nt, 2, units // 128, width // 8, 128)
        hid_full = hid_full.transpose(2, 0, 4, 1, 3, 5).reshape(2, nd, width // nd, nt, units)
        hid_sum = cube_scatter(hid_full.transpose(1, 3, 0, 2, 4), nd, BF16)
        down_full = feed_pieces[:, :, 2 * units :].transpose(1, 2, 0, 3)
        down_full = down_full.reshape(nt, units, nd, width // nd)
        down_sum = cube_scatter(down_full.transpose(2, 0, 1, 3), nd, BF16)
        gradient_hidden = chain_scatter(hid_sum, nt)
        gradient_down = chain_scatter(down_sum, nt)

    back = mixers_back(
        heads, channels, nt, kv_head, q, k2, v2, lse, do, cosine, sine, dm, y, zr, xr, br, trow, states,
        squares, dots, gain_mix, taps_x, taps_b, decay, bias, skip,
        (feed_sums, feed_raw) if nd == 8 else None,
    )
    dq, dkv, dz, dx, db, drow, grad_tx, grad_tb, grad_rows, grad_heads = back[:10]
    if nd == 8:
        sums = tail(
            nt, tokens, gain_first, dh, a1, grad_mix, o, m, dq, dz, dx, dkv, db, drow, full_query, full_inner,
            step_rows, full_shared, grad_gain_two, grad_tb, grad_tx, grad_rows, grad_heads, feed_own, back[10],
        )
        gradient_tokens, mixed, fed, gradient_shared, small_sums = sums
        place = jnp.stack([d, d * nt + tensor_index]).astype(jnp.int32)
        shapes = [
            query_proj.shape, attend_out.shape, inner_proj.shape, mamba_out.shape, hidden_proj.shape,
            down_proj.shape, norm_gains.shape, shared_taps.shape, channel_taps.shape, mixer_gain.shape,
            step_proj.T.shape,
        ]
        (
            gradient_query,
            gradient_attend,
            gradient_inner,
            gradient_mamba,
            gradient_hidden,
            gradient_down,
            gradient_norms,
            gradient_taps,
            gradient_channel,
            gradient_mixer,
            gradient_step,
            gradient_decay,
            gradient_bias,
            gradient_skip,
            layer_out,
            gradient_tokens,
            gradient_shared,
        ) = finish(
            heads, place, mixed, fed, small_sums, shapes, (layer_out, gradient_tokens, gradient_shared)
        )
        return (
            layer_out,
            gradient_tokens,
            gradient_query,
            gradient_attend,
            gradient_inner,
            gradient_step.T,
            gradient_mamba,
            gradient_hidden,
            gradient_down,
            gradient_channel,
            gradient_mixer,
            gradient_decay.reshape(heads),
            gradient_bias.reshape(heads),
            gradient_skip.reshape(heads),
            gradient_shared,
            gradient_norms,
            gradient_taps,
        )

    part_one = down_parts(dq, dz, dx, dkv, db, drow, full_query, full_inner, step_rows, full_shared)
    pieces, shared_pieces, grad_step = weight_pieces(a1, dq, dz, dx, dkv, db, drow, o, m, grad_mix)
    block = width // nd
    q_cols = query_proj.shape[1]
    cuts = [0, q_cols, q_cols + attend_out.shape[0]]
    cuts += [cuts[2] + inner, cuts[2] + 2 * inner, cuts[2] + 3 * inner]

    def from_rows(values):
        return values.reshape(8, -1, 128, 128).transpose(0, 2, 1, 3).reshape(width, -1)

    def from_lanes(values):
        return values.transpose(1, 0, 2).reshape(-1, width)

    n_tap = CONV + 1
    over_all = jnp.concatenate([grad_gain_two.reshape(-1), grad_tb[:n_tap].reshape(-1)])
    over_dp = jnp.concatenate(
        [
            grad_tx[:n_tap].reshape(-1),
            grad_rows[0],
            grad_rows[1].reshape(heads, SSM_DIM).sum(axis=1),
            grad_heads[:heads].sum(axis=1),
            grad_heads[8 : 8 + heads].sum(axis=1),
            grad_step[:heads].reshape(-1),
        ]
    )

    def in_rows(values):
        return jnp.pad(values, (0, -values.shape[0] % 1024)).reshape(-1, 128)

    rows_all = in_rows(over_all)
    n_all = rows_all.shape[0]
    small_sums = jnp.concatenate([rows_all, in_rows(over_dp)], axis=0)
    parts = part_one.reshape(nt, local_rows, width)
    token_f32 = tokens.astype(F32)
    _, norm_one_back = jax.vjp(norm_apply, token_f32, gain_first[0])
    grad_from_one, grad_gain_one = norm_one_back(chain_scatter(parts, nt))
    gradient_tokens = (dh + grad_from_one).astype(BF16)
    got = [pieces[:, cuts[i] : cuts[i + 1]] for i in range(5)]

    def over_rows(values):
        return cube_scatter(from_rows(values).reshape(nd, block, -1), nd)

    def over_lanes(values):
        return cube_scatter(from_lanes(values).reshape(-1, nd, block).transpose(1, 0, 2), nd)

    gradient_query = over_rows(got[0])
    gradient_attend = over_lanes(got[1])
    gradient_inner = jnp.stack([over_rows(got[2]), over_rows(got[3])])
    gradient_mamba = over_lanes(got[4])
    shared_cut = shared_pieces.reshape(nd, nt, width // (nd * nt), -1)
    gradient_shared = chain_scatter(cube_scatter(shared_cut, nd, BF16), nt)
    small_sums = lax.psum(small_sums, "dp")
    small_sums = jnp.concatenate(
        [lax.psum(small_sums[:n_all], "tensor"), small_sums[n_all:]], axis=0
    )
    grad_gain_one = lax.psum(grad_gain_one, ("dp", "tensor")).reshape(1, width)
    over_all = small_sums[:n_all].reshape(-1)
    over_dp = small_sums[n_all:].reshape(-1)
    place = d * nt + tensor_index
    norm_w = width // (nd * nt)
    both_norms = jnp.concatenate([grad_gain_one, over_all[:width].reshape(1, width)], axis=0)
    gradient_norms = lax.dynamic_slice_in_dim(both_norms, place * norm_w, norm_w, 1)
    tap_w = shared_taps.shape[1]
    tap_all = over_all[width : width + n_tap * taps_b.shape[1]].reshape(n_tap, -1)
    gradient_taps = lax.dynamic_slice_in_dim(tap_all, place * tap_w, tap_w, 1)
    part = mixer_gain.shape[1]
    n_taps = n_tap * inner
    chan = over_dp[:n_taps].reshape(n_tap, heads, SSM_DIM)
    gain = over_dp[n_taps : n_taps + inner].reshape(heads, SSM_DIM)
    gradient_channel = lax.dynamic_slice_in_dim(chan, d * part, part, 2)
    gradient_mixer = lax.dynamic_slice_in_dim(gain, d * part, part, 1)
    rest = over_dp[n_taps + inner :]
    gradient_skip = rest[:heads]
    gradient_decay = rest[heads : 2 * heads]
    gradient_bias = rest[2 * heads : 3 * heads]
    step_all = rest[3 * heads : 3 * heads + heads * width].reshape(heads, width)
    gradient_step = lax.dynamic_slice_in_dim(step_all, d * block, block, 1).T
    return (
        layer_out,
        gradient_tokens,
        gradient_query,
        gradient_attend,
        gradient_inner,
        gradient_step,
        gradient_mamba,
        gradient_hidden,
        gradient_down,
        gradient_channel,
        gradient_mixer,
        gradient_decay,
        gradient_bias,
        gradient_skip,
        gradient_shared,
        gradient_norms,
        gradient_taps,
    )


def solution(mesh):
    placed = (
        P(("dp", "tensor"), None),
        P("dp", "tensor"),
        P("tensor", "dp"),
        P(None, "dp", "tensor"),
        P("dp", "tensor"),
        P("tensor", "dp"),
        P(None, "dp", "tensor"),
        P("tensor", "dp"),
        P(None, "tensor", "dp"),
        P("tensor", "dp"),
        P("tensor"),
        P("tensor"),
        P("tensor"),
        P(("dp", "tensor"), None),
        P(None, ("dp", "tensor")),
        P(None, ("dp", "tensor")),
        P(("dp", "tensor"), None),
    )
    return jax.shard_map(
        partial(per_device, mesh.shape["dp"], mesh.shape["tensor"]),
        mesh=mesh,
        in_specs=placed,
        out_specs=(
            P(("dp", "tensor"), None),
            P(("dp", "tensor"), None),
            P("dp", "tensor"),
            P("tensor", "dp"),
            P(None, "dp", "tensor"),
            P("dp", "tensor"),
            P("tensor", "dp"),
            P(None, "dp", "tensor"),
            P("tensor", "dp"),
            P(None, "tensor", "dp"),
            P("tensor", "dp"),
            P("tensor"),
            P("tensor"),
            P("tensor"),
            P(("dp", "tensor"), None),
            P(None, ("dp", "tensor")),
            P(None, ("dp", "tensor")),
        ),
        check_vma=False,
    )
```

```python
from functools import partial

import numpy as np
import jax
import jax.numpy as jnp
from jax import lax
from jax.experimental import pallas as pl
from jax.experimental.pallas import tpu as pltpu
from jax.sharding import PartitionSpec as P

MESH = pl.DeviceIdType.MESH

QHEADS = 8
KVHEADS = 2
HEAD_SIZE = 64
SSM_DIM = 64
CONV = 4


epsilon = 1e-05
rope_base = 100000000000.0
neg_large = -1e30
block_len = 128


def norm_apply(values, gain):
    factor = lax.rsqrt(jnp.mean(values * values, axis=-1, keepdims=True) + epsilon)
    return values * factor * gain


def dp_bits(index):
    core = lax.rem(index, 2)
    xbit = lax.rem(index // 2, 2)
    ybit = lax.rem(index // 4, 2)
    return core, xbit, ybit


def remote_copy(src, dst, send, recv, dev):
    return pltpu.make_async_remote_copy(
        src_ref=src, dst_ref=dst, send_sem=send, recv_sem=recv, device_id=dev, device_id_type=MESH
    )


def greet(peers):
    barrier = pltpu.get_barrier_semaphore()
    for peer in peers:
        pl.semaphore_signal(barrier, inc=1, device_id=peer, device_id_type=MESH)
    pl.semaphore_wait(barrier, len(peers))


def other_quarters(d, z, nt):
    return [(d, lax.rem(z + k, nt)) for k in range(1, nt)]


def cube_peers(d):
    core, xbit, ybit = dp_bits(d)
    return d + 1 - 2 * core, d + 2 - 4 * xbit, d + 4 - 8 * ybit


class CubeGather:
    def __init__(self, items, via_y, send, recv, d, z):
        self.items, self.via_y, self.send, self.recv = items, via_y, send, recv
        self.d, self.z = d, z
        self.d_core, self.d_x, self.d_y = cube_peers(d)
        self.d_xy = self.d_x + self.d_y - d
        self.sent = []

    def push(self, i, j, src, dst, peer):
        def make():
            return remote_copy(src(), dst(), self.send.at[i, j], self.recv.at[i, j], (peer, self.z))

        make().start()
        self.sent.append(make)

    def landed(self, i, j, slot):
        at = self.items[i][1]
        remote_copy(
            at(slot), at(slot), self.send.at[i, j], self.recv.at[i, j], (self.d_core, self.z)
        ).wait_recv()

    def start(self, i):
        src, at = self.items[i]
        for j, peer in enumerate((self.d_x, self.d_y, self.d_core)):
            self.push(i, j, lambda: src, lambda: at(self.d), peer)

    def near(self, i):
        d_x, d_y, d_core = self.d_x, self.d_y, self.d_core
        self.landed(i, 0, d_x)
        if i in self.via_y:
            self.hand_on(i, 3, d_x, d_y)
        self.hand_on(i, 4, d_x, d_core)
        self.landed(i, 1, d_y)
        if i not in self.via_y:
            self.hand_on(i, 3, d_y, d_x)
        self.hand_on(i, 5, d_y, d_core)

    def hand_on(self, i, j, slot, peer):
        at = self.items[i][1]
        self.push(i, j, lambda: at(slot), lambda: at(slot), peer)

    def far(self, i):
        self.landed(i, 3, self.d_xy)
        self.hand_on(i, 6, self.d_xy, self.d_core)

    def finish(self):
        for i in range(len(self.items)):
            self.landed(i, 2, self.d_core)
            for j in (4, 5, 6):
                self.landed(i, j, self.d_core)
        for make in self.sent:
            make().wait_send()


def gather_kernel(nt, *refs):
    (tok, que, att, inn, mam, sha, sma) = refs[:7]
    (tok_f, que_f, att_f, inn_f, mam_f, sha_f, sma_f) = refs[7:14]
    (lsem, zs_send, zs_recv, t_send, t_recv, d_send, d_recv) = refs[14:]
    d = lax.axis_index("dp")
    z = lax.axis_index("tensor")
    greet([(p, z) for p in cube_peers(d)] + other_quarters(d, z, nt))

    small = []
    for i, (src, dst) in enumerate(((sha, sha_f), (sma, sma_f))):
        for k, peer in enumerate(other_quarters(d, z, nt)):
            small.append(remote_copy(src, dst.at[d, z], zs_send.at[i, k], zs_recv.at[i, k], peer))
            small[-1].start()
    q_rows = que.shape[0]
    cols = att.shape[1]
    i_rows = inn.shape[1]
    items = [
        (inn, lambda s: inn_f.at[:, pl.ds(s * i_rows, i_rows)]),
        (que, lambda s: que_f.at[pl.ds(s * q_rows, q_rows)]),
        (att, lambda s: att_f.at[:, pl.ds(pl.multiple_of(s * cols, cols), cols)]),
        (mam, lambda s: mam_f.at[:, pl.ds(pl.multiple_of(s * cols, cols), cols)]),
        (sha_f.at[d], lambda s: sha_f.at[s]),
        (sma_f.at[d], lambda s: sma_f.at[s]),
    ]
    cube = CubeGather(items, (0, 5), d_send, d_recv, d, z)
    locals_ = []
    for i, (src, dst) in enumerate(
        [(sha, sha_f.at[d, z]), (sma, sma_f.at[d, z]), (tok, tok_f.at[z])]
        + [(src, at(d)) for src, at in items[:4]]
    ):
        copy = pltpu.make_async_copy(src, dst, lsem.at[i])
        copy.start()
        locals_.append(copy)
    for i in range(4):
        cube.start(i)
    chain = ChainGather(tok, tok_f, t_send, t_recv, d, z, nt)
    chain.start()
    locals_[0].wait()
    locals_[1].wait()
    for copy in small:
        copy.wait()
    cube.start(4)
    cube.start(5)
    for i in range(4):
        cube.near(i)
    chain.hop(1)
    for i in (4, 5):
        cube.near(i)
    for i in range(6):
        cube.far(i)
    for dist in range(2, nt):
        chain.hop(dist)
    cube.finish()
    for copy in locals_[2:]:
        copy.wait()
    chain.drain()


def gather_start(tok, que, att, inn, mam, sha, sma, nd, nt):
    if nd != 8:
        shared = lax.all_gather(sha, ("dp", "tensor"), axis=0)
        small = lax.all_gather(sma, ("dp", "tensor"), axis=0)
        return (
            lax.all_gather(tok, "tensor", axis=0),
            lax.all_gather(que, "dp", axis=0, tiled=True),
            lax.all_gather(att, "dp", axis=1, tiled=True),
            lax.all_gather(inn, "dp", axis=1, tiled=True),
            lax.all_gather(mam, "dp", axis=1, tiled=True),
            shared.reshape((nd, nt) + sha.shape),
            small.reshape((nd, nt) + sma.shape),
        )
    bf = jnp.bfloat16
    outs = (
        (nt,) + tok.shape,
        (nd * que.shape[0], que.shape[1]),
        (att.shape[0], nd * att.shape[1]),
        (2, nd * inn.shape[1], inn.shape[2]),
        (mam.shape[0], nd * mam.shape[1]),
        (nd, nt) + sha.shape,
        (nd, nt) + sma.shape,
    )
    anywhere = pl.BlockSpec(memory_space=pl.ANY)
    dma = pltpu.SemaphoreType.DMA
    return pl.pallas_call(
        partial(gather_kernel, nt),
        out_shape=[jax.ShapeDtypeStruct(s, bf) for s in outs],
        in_specs=[pl.BlockSpec(memory_space=pltpu.VMEM)] * 7,
        out_specs=[anywhere] * 7,
        scratch_shapes=[
            dma((7,)), dma((2, nt)), dma((2, nt)), dma((2, nt)), dma((2, nt)),
            dma((6, 7)), dma((6, 7)),
        ],
        compiler_params=pltpu.CompilerParams(collective_id=0, has_side_effects=True),
        name="gather_start",
    )(tok, que, att, inn, mam, sha, sma)


def pack_kernel(taps, gain, norms, staps, step, out, rows):
    heads = step.shape[0]
    f32 = jnp.float32
    rows[...] = jnp.zeros(rows.shape, f32)
    rows[0:2, 0:32] = norms[...].astype(f32)
    rows[0 : CONV + 1, 32:40] = staps[...].astype(f32)
    rows[0:heads, 40:48] = gain[...].astype(f32)
    for j in range(CONV + 1):
        rows[0:heads, 48 + 8 * j : 56 + 8 * j] = taps[j].astype(f32)
    rows[8 : 8 + heads, :] = step[...].astype(f32)
    out[...] = rows[...].astype(jnp.bfloat16)


def pack_small(taps, gain, norms, staps, step):
    vmem = pl.BlockSpec(memory_space=pltpu.VMEM)
    return pl.pallas_call(
        pack_kernel,
        in_specs=[vmem] * 5,
        out_specs=vmem,
        out_shape=jax.ShapeDtypeStruct((16, 128), jnp.bfloat16),
        scratch_shapes=[pltpu.VMEM((16, 128), jnp.float32)],
        name="pack_small",
    )(taps, gain, norms, staps, step)


def unpack_kernel(
    heads, scal, packed, first_o, second_o, gain_o, tapx_o, tapb_o, step_o, decay_o, bias_o, skip_o
):
    z = lax.axis_index("tensor")
    f32 = jnp.float32
    nd, nt = packed.shape[:2]
    tiles = [[packed[k, q].astype(f32) for q in range(nt)] for k in range(nd)]
    for k in range(nd):
        both = jnp.concatenate([tiles[k][q][0:8, 0:32] for q in range(nt)], axis=1)
        first_o[:, 128 * k : 128 * k + 128] = both[0:1]
        second_o[:, 128 * k : 128 * k + 128] = both[1:2]
        step_o[:, 128 * k : 128 * k + 128] = packed[k, z].astype(f32)[8:16, :].astype(jnp.bfloat16)
    half = nd // 2
    for k in range(2):
        tapb_o[:, 128 * k : 128 * k + 128] = jnp.concatenate(
            [tiles[half * k + i][q][0:8, 32:40] for i in range(half) for q in range(nt)], axis=1
        )
    own = [packed[k, z].astype(f32) for k in range(nd)]

    def by_head(lane):
        wide = jnp.concatenate([own[k][0:8, lane : lane + 8] for k in range(nd)], axis=1)
        return jnp.concatenate([wide[h : h + 1, :] for h in range(heads)], axis=1)

    gain_o[...] = by_head(40)
    tapx_o[...] = jnp.zeros(tapx_o.shape, f32)
    tapb_o[CONV + 1 :, :] = jnp.zeros((7 - CONV, tapb_o.shape[1]), f32)
    for j in range(CONV + 1):
        tapx_o[j : j + 1, :] = by_head(48 + 8 * j)
    sub = lax.broadcasted_iota(jnp.int32, (8, 128), 0)
    decay = jnp.zeros((8, 128), f32)
    bias = jnp.zeros((8, 128), f32)
    for h in range(heads):
        decay = jnp.where(sub == h, scal[0, h], decay)
        bias = jnp.where(sub == h, scal[1, h], bias)
        skip_o[:, SSM_DIM * h : SSM_DIM * (h + 1)] = jnp.full((1, SSM_DIM), scal[2, h], f32)
    decay_o[...] = jnp.where(sub < heads, -jnp.exp(decay), 0.0)
    bias_o[...] = bias


def unpack_small(heads, scal, packed, width):
    inner = heads * SSM_DIM
    vmem = pl.BlockSpec(memory_space=pltpu.VMEM)
    smem = pl.BlockSpec(memory_space=pltpu.SMEM)
    sds = jax.ShapeDtypeStruct
    f32 = jnp.float32
    shapes = [(1, width), (1, width), (1, inner), (8, inner), (8, 256)]
    return pl.pallas_call(
        partial(unpack_kernel, heads),
        in_specs=[smem, vmem],
        out_specs=[vmem] * 9,
        out_shape=[sds(s, f32) for s in shapes]
        + [sds((8, width), jnp.bfloat16), sds((8, 128), f32), sds((8, 128), f32), sds((1, inner), f32)],
        name="unpack_small",
    )(scal, packed)


def pick(values, index, axis=0):
    return lax.dynamic_index_in_dim(values, index, axis, keepdims=False)


def add_low(left, right):
    return (left.astype(jnp.float32) + right.astype(jnp.float32)).astype(jnp.bfloat16)


def chain_scatter(parts, nt):
    z = lax.axis_index("tensor")
    right = left = None
    for t in range(nt - 1):
        to_right = pick(parts, jnp.clip(nt - 1 - t + z, 0, nt - 1))
        to_left = pick(parts, jnp.clip(t - (nt - 1) + z, 0, nt - 1))
        if t > 0:
            to_right = add_low(to_right, right)
            to_left = add_low(to_left, left)
        right = lax.ppermute(to_right, "tensor", [(i, i + 1) for i in range(t + 1)])
        left = lax.ppermute(
            to_left, "tensor", [(nt - 1 - i, nt - 2 - i) for i in range(t + 1)]
        )
    f32 = jnp.float32
    return pick(parts, z).astype(f32) + right.astype(f32) + left.astype(f32)


def cube_scatter(parts, nd, last=jnp.float32):
    return lax.psum_scatter(parts, "dp", scatter_dimension=0, tiled=False).astype(last)


F32, BF16 = jnp.float32, jnp.bfloat16
VMEM_LIMIT = 56 * 1024 * 1024


def dot_nn(a, b):
    return lax.dot_general(a, b, (((1,), (0,)), ((), ())), preferred_element_type=F32)


def dot_nt(a, b):
    return lax.dot_general(a, b, (((1,), (1,)), ((), ())), preferred_element_type=F32)


def dot_tn(a, b):
    return lax.dot_general(a, b, (((0,), (0,)), ((), ())), preferred_element_type=F32)


def sigmoid(v):
    return 1.0 / (1.0 + jnp.exp(-v))


def second_head():
    return lax.axis_index("tensor") * 2 // (QHEADS // KVHEADS) == 1


def lanes_of(shape):
    return lax.broadcasted_iota(jnp.int32, shape, len(shape) - 1)


def turn(values, cosine, sine):
    lane = lanes_of(values.shape)
    other = jnp.where(
        lax.rem(lane, HEAD_SIZE) < HEAD_SIZE // 2,
        pltpu.roll(values, 128 - HEAD_SIZE // 2, 1),
        pltpu.roll(values, HEAD_SIZE // 2, 1),
    )
    return values * cosine + other * sine


def softplus(v):
    return jnp.maximum(v, 0.0) + jnp.log1p(jnp.exp(-jnp.abs(v)))


def running_sum(rows):
    lane = lanes_of(rows.shape)
    step = 1
    while step < rows.shape[1]:
        rows = rows + jnp.where(lane >= step, pltpu.roll(rows, step, 1), 0.0)
        step *= 2
    return rows


def running_sum_back(rows):
    lane = lanes_of(rows.shape)
    width = rows.shape[1]
    step = 1
    while step < width:
        rows = rows + jnp.where(lane < width - step, pltpu.roll(rows, width - step, 1), 0.0)
        step *= 2
    return rows


def stack_columns(rows_list):
    used = sum(r.shape[0] for r in rows_list)
    filler = jnp.zeros((128 - used, 128), F32)
    return jnp.concatenate(rows_list + [filler], axis=0).T


def widen(cols, base, heads):
    low = lanes_of((cols.shape[0], 128)) < SSM_DIM
    return jnp.concatenate(
        [
            jnp.where(low, cols[:, base + 2 * p : base + 2 * p + 1],
                      cols[:, base + 2 * p + 1 : base + 2 * p + 2])
            for p in range(heads // 2)
        ],
        axis=1,
    )


def conv_rows(ref, taps, first, rows):
    total = taps[CONV : CONV + 1, :] + taps[0:1, :] * ref[pl.ds(first, rows), :]
    for j in range(1, CONV):
        total = total + taps[j : j + 1, :] * ref[pl.ds(first + j, rows), :]
    return total


def quarter_at(i, z, nt):
    near = jnp.where(z < nt - 1, z + 1, z - 1)
    far = jnp.where(z < nt - 1, lax.rem(z + 3, nt), lax.rem(z + 1, nt))
    order = jnp.where(i == 0, lax.rem(z + 2, nt), far)
    return jnp.where(i == 2, near, jnp.where(i == 3, z, order))


class FeedGather:
    def __init__(self, step, nt, hid, dwn, hid_f, dwn_f, hid_z, dwn_z, lsem, sems):
        self.step, self.nt = step, nt
        d = lax.axis_index("dp")
        z = lax.axis_index("tensor")
        self.d, self.z = d, z
        self.cube = CubeGather(
            [(hid, lambda s: hid_f.at[s, z]), (dwn, lambda s: dwn_f.at[s, z])], (0,), sems[0], sems[1], d, z
        )
        self.chains = [
            ChainGather(hid, hid_z, sems[2], sems[3], d, z, nt),
            ChainGather(dwn, dwn_z, sems[4], sems[5], d, z, nt),
        ]
        self.own = lambda: [
            pltpu.make_async_copy(hid, hid_f.at[d, z], lsem.at[0]),
            pltpu.make_async_copy(dwn, dwn_f.at[d, z], lsem.at[1]),
        ]

    def at(self, step, act):
        pl.when(self.step == step)(act)

    def begin(self):
        def act():
            greet([(p, self.z) for p in cube_peers(self.d)] + other_quarters(self.d, self.z, self.nt))
            for chain in self.chains:
                chain.start()
            for i in range(2):
                self.cube.start(i)
            for copy in self.own():
                copy.start()

        self.at(0, act)
        def first():
            for chain in self.chains:
                chain.hop(1)

        self.at(1, first)

    def middle(self):
        def near():
            for i in range(2):
                self.cube.near(i)

        def far():
            for chain in self.chains:
                chain.hop(2)
            for i in range(2):
                self.cube.far(i)

        self.at(1, near)
        self.at(2, far)

    def end(self):
        def act():
            for chain in self.chains:
                chain.hop(3)
            self.cube.finish()
            for copy in self.own():
                copy.wait()
            for chain in self.chains:
                chain.drain()

        self.at(3, act)


def forward_kernel(heads, nt, feed, *refs):
    if feed:
        beside = FeedGather(
            pl.program_id(0), nt, *refs[13:15], *refs[28:32], refs[37], refs[38:44]
        )
        refs = refs[:13] + refs[15:28] + refs[32:37]
        beside.begin()
        forward_step(heads, beside.middle, *refs)
        beside.end()
    else:
        forward_step(heads, lambda: None, *refs)


def forward_step(
    heads, middle, tok, gain, wq, win, stp, wsh, cosine, sine, tapx, tapb, decay, bias, skip,
    a1_o, q_o, k_o, v_o, lse_o, o_o, x_o, z_o, b_o, y_o, t_o, s_o, sq_o,
    keys, vals, xs, bs, state,
):
    step = pl.program_id(0)
    rows = tok.shape[0]
    second = second_head()

    @pl.when(step == 0)
    def _():
        xs[0:8, :] = jnp.zeros((8, xs.shape[1]), F32)
        bs[0:8, :] = jnp.zeros((8, bs.shape[1]), F32)
        state[...] = jnp.zeros(state.shape, F32)

    t = tok[...].astype(F32)
    r = lax.rsqrt(jnp.mean(t * t, axis=1, keepdims=True) + epsilon)
    a1 = (t * r * gain[...]).astype(BF16)
    a1_o[...] = a1
    q = turn(dot_nn(a1, wq[...]), cosine[...], sine[...]).astype(BF16)
    q_o[...] = q
    s = dot_nn(a1, wsh[...])
    low = lanes_of((rows, 128)) < HEAD_SIZE
    k = turn(s[:, :128], cosine[...], sine[...])
    v = s[:, 128:256]
    pick_own = low != second
    k2 = jnp.where(pick_own, k, pltpu.roll(k, 64, 1)).astype(BF16)
    v2 = jnp.where(pick_own, v, pltpu.roll(v, 64, 1))
    k_o[...] = k2
    v_o[...] = v2.astype(BF16)
    place = pl.ds(pl.multiple_of(step * rows, rows), rows)
    keys[place, :] = k2
    vals[:, place] = v2.T.astype(BF16)

    scale = HEAD_SIZE**-0.5

    def attend(blocks):
        n = blocks * rows
        shape = (rows, rows)
        allowed = lax.broadcasted_iota(jnp.int32, shape, 0) <= lanes_of(shape)
        parts = []
        for h in range(2):
            qh = jnp.where(low == (h == 0), q, jnp.zeros_like(q))
            sc = dot_nt(keys[0:n, :], qh) * scale
            last = jnp.where(allowed, sc[n - rows :, :], neg_large)
            sc = jnp.concatenate([sc[: n - rows, :], last], axis=0) if blocks > 1 else last
            top = jnp.max(sc, axis=0, keepdims=True)
            e = jnp.exp(sc - top)
            total = jnp.sum(e, axis=0, keepdims=True)
            lse_o[h : h + 1, :] = top + jnp.log(total)
            parts.append(dot_nn(vals[:, 0:n], e.astype(BF16)) / total)
        sub = lax.broadcasted_iota(jnp.int32, parts[0].shape, 0)
        o_o[...] = jnp.where(sub < HEAD_SIZE, parts[0], parts[1]).T.astype(BF16)

    for i in range(keys.shape[0] // rows):
        pl.when(step == i)(partial(attend, i + 1))

    middle()
    zr = dot_nn(a1, win[0])
    z_o[...] = zr
    xr = dot_nn(a1, win[1])
    x_o[...] = xr
    br = s[:, 256:]
    b_o[...] = br
    xs[8 : 8 + rows, :] = xr
    bs[8 : 8 + rows, :] = br
    u = conv_rows(xs, tapx, 5, rows)
    x = u * sigmoid(u)
    u = conv_rows(bs, tapb, 5, rows)
    bc = (u * sigmoid(u)).astype(BF16)
    xs[0:8, :] = xs[rows : rows + 8, :]
    bs[0:8, :] = bs[rows : rows + 8, :]
    tr = dot_nt(stp[...], a1)
    t_o[...] = tr
    n_state = bc.shape[1] // 2
    tri_shape = (block_len, block_len)
    lower = lax.broadcasted_iota(jnp.int32, tri_shape, 0) >= lanes_of(tri_shape)
    half = lanes_of(tri_shape) < SSM_DIM
    for c in range(rows // block_len):
        part = slice(c * block_len, (c + 1) * block_len)
        dt = softplus(tr[:, part] + bias[...])
        cum = running_sum(dt * decay[...])
        end = cum[:, block_len - 1 :]
        cols = stack_columns([cum, jnp.exp(cum), dt * jnp.exp(end - cum)])
        xc = x[part]
        x_low = xc.astype(BF16)
        b_low = bc[part, :n_state]
        c_low = bc[part, n_state:]
        cross = dot_nt(c_low, b_low)
        grow = widen(cols, 8, heads)
        y = dot_nn(c_low, state[...].astype(BF16)) * grow + skip[...] * xc
        inner = []
        for p in range(heads // 2):
            mats = []
            for h in (2 * p, 2 * p + 1):
                gap = jnp.where(lower, cols[:, h : h + 1] - cum[h : h + 1, :], neg_large)
                mats.append((cross * jnp.exp(gap) * dt[h : h + 1, :]).astype(BF16))
            xp = x_low[:, 128 * p : 128 * p + 128]
            zero = jnp.zeros_like(xp)
            both = jnp.concatenate([jnp.where(half, xp, zero), jnp.where(half, zero, xp)], axis=0)
            inner.append(dot_nn(jnp.concatenate(mats, axis=1), both))
        y = y + jnp.concatenate(inner, axis=1)
        y_o[part, :] = y
        s_o[c] = state[...]
        carried = (xc * widen(cols, 16, heads)).astype(BF16)
        state[...] = grow[block_len - 1 :, :] * state[...] + dot_tn(b_low, carried)
        zc = zr[part]
        w = y * (zc * sigmoid(zc))
        total = jnp.sum(w * w, axis=1, keepdims=True)
        sq_o[:, part] = jnp.broadcast_to(total, (block_len, 128)).T[0:8, :]


def mixers_forward(
    heads, nt, tok, gain, wq, win, stp, wsh, cosine, sine, tapx, tapb, decay, bias, skip, feed=()
):
    total, width = tok.shape
    rows = 256
    inner = heads * SSM_DIM
    pair = wsh.shape[1] - 256
    state = pair // 2
    chunks = rows // block_len

    def whole(v):
        return pl.BlockSpec(v.shape, lambda i: (0,) * v.ndim)

    def tall(n):
        return pl.BlockSpec((rows, n), lambda i: (i, 0))

    wide = pl.BlockSpec((8, rows), lambda i: (0, i))
    sds = jax.ShapeDtypeStruct
    more_in, more_out, more_shape, more_scratch, extra = [], [], [], [], {}
    if feed:
        nd = 8
        dma = pltpu.SemaphoreType.DMA
        more_in = [whole(v) for v in feed]
        more_out = [pl.BlockSpec(memory_space=pl.ANY)] * 4
        more_shape = [sds((nd, nt) + v.shape, BF16) for v in feed] + [sds((nt,) + v.shape, BF16) for v in feed]
        more_scratch = [dma((2,)), dma((2, 7)), dma((2, 7))] + [dma((2, nt - 1))] * 4
        extra = dict(collective_id=6, has_side_effects=True)
    return pl.pallas_call(
        partial(forward_kernel, heads, nt, bool(feed)),
        grid=(total // rows,),
        in_specs=[tall(width), whole(gain), whole(wq), whole(win),
                  whole(stp), whole(wsh), tall(128), tall(128), whole(tapx), whole(tapb),
                  whole(decay), whole(bias), whole(skip)] + more_in,
        out_specs=[tall(width), tall(128), tall(128), tall(128), wide, tall(128), tall(inner),
                   tall(inner), tall(pair), tall(inner), wide,
                   pl.BlockSpec((chunks, state, inner), lambda i: (i, 0, 0)), wide] + more_out,
        out_shape=[sds((total, width), BF16), sds((total, 128), BF16), sds((total, 128), BF16),
                   sds((total, 128), BF16), sds((8, total), F32), sds((total, 128), BF16),
                   sds((total, inner), F32), sds((total, inner), F32), sds((total, pair), F32),
                   sds((total, inner), F32), sds((8, total), F32),
                   sds((total // block_len, state, inner), F32), sds((8, total), F32)] + more_shape,
        scratch_shapes=[pltpu.VMEM((total, 128), BF16), pltpu.VMEM((128, total), BF16),
                        pltpu.VMEM((rows + 8, inner), F32), pltpu.VMEM((rows + 8, pair), F32),
                        pltpu.VMEM((state, inner), F32)] + more_scratch,
        compiler_params=pltpu.CompilerParams(vmem_limit_bytes=VMEM_LIMIT, **extra),
        cost_estimate=pl.CostEstimate(flops=int(5e9), bytes_accessed=int(15e6), transcendentals=int(4e6)),
        name="mixers_forward",
    )(tok, gain, wq, win, stp, wsh, cosine, sine, tapx, tapb, decay, bias, skip, *feed)


def attend_back(step, q, k2, v2, lse, do, cosine, sine, cos_all, sin_all, dq_o, dkv_o, dk, dv):
    rows = q.shape[0]
    steps = k2.shape[0] // rows
    scale = HEAD_SIZE**-0.5
    low = lanes_of((rows, 128)) < HEAD_SIZE

    @pl.when(step == 0)
    def _():
        dk[...] = jnp.zeros(dk.shape, F32)
        dv[...] = jnp.zeros(dv.shape, F32)

    def back(blocks):
        n = blocks * rows
        shape = (rows, rows)
        allowed = lax.broadcasted_iota(jnp.int32, shape, 0) <= lanes_of(shape)
        qs, dos, ps, dss, dqs = [], [], [], [], []
        for h in range(2):
            mine = low == (h == 0)
            qh = jnp.where(mine, q[...], jnp.zeros_like(q[...]))
            doh = jnp.where(mine, do[...], jnp.zeros_like(do[...]))
            sc = dot_nt(k2[0:n, :], qh) * scale - lse[h : h + 1, :]
            last = jnp.where(allowed, sc[n - rows :, :], neg_large)
            sc = jnp.concatenate([sc[: n - rows, :], last], axis=0) if blocks > 1 else last
            p = jnp.exp(sc)
            dp = dot_nt(v2[0:n, :], doh)
            centre = jnp.sum(p * dp, axis=0, keepdims=True)
            ds = (p * (dp - centre)).astype(BF16)
            qs.append(qh)
            dos.append(doh)
            ps.append(p.astype(BF16))
            dss.append(ds)
            dqs.append(dot_tn(ds, k2[0:n, :]) * scale)
        dk[0:n, :] += dot_nn(jnp.concatenate(dss, axis=1), jnp.concatenate(qs, axis=0)) * scale
        dv[0:n, :] += dot_nn(jnp.concatenate(ps, axis=1), jnp.concatenate(dos, axis=0))
        dq_o[...] = turn(jnp.where(low, dqs[0], dqs[1]), cosine[...], -sine[...]).astype(BF16)

    for i in range(steps):
        pl.when(step == 2 * (steps - 1 - i))(partial(back, i + 1))

    @pl.when(step == 2 * steps - 1)
    def _():
        own = (lanes_of(dk.shape) < HEAD_SIZE) != second_head()
        g = dk[...]
        g = turn(g + pltpu.roll(g, 64, 1), cos_all[...], -sin_all[...])
        dkv_o[:, 0:128] = jnp.where(own, g, 0.0).astype(BF16)
        g = dv[...]
        g = g + pltpu.roll(g, 64, 1)
        dkv_o[:, 128:256] = jnp.where(own, g, 0.0).astype(BF16)


def back_kernel(heads, channels, nt, feed, *refs):
    step = pl.program_id(0)
    if feed:
        d = lax.axis_index("dp")
        z = lax.axis_index("tensor")
        sums, raw, refs = refs[0], refs[1], refs[2:]
        feed_o, refs = refs[36], refs[:36] + refs[37:]
        parts, chain_boxes, box = refs[43], refs[44:48], refs[48:56]
        (dot_sum, dot_land, d_send, d_recv), refs = refs[56:60], refs[:43]
        peers = cube_peers(d)
        square = SquareScatter(
            lambda i, j: (2 * i + j,), raw, box[:6], box[6], box[7], peers, dp_bits(d), z
        )
        chain = ChainScatter(parts, *chain_boxes, d, z, nt)
        dots = Exchange(refs[19], dot_land, d_send, d_recv, d, z, nt)

        @pl.when(step == 0)
        def _():
            greet([(p, z) for p in peers[1:]] + other_quarters(d, z, nt))
            for k in range(nt - 2):
                parts[quarter_at(k, z, nt)] = sums[k]
            parts[z] = jnp.zeros(parts.shape[1:], BF16)
            dots.start()
            chain.step(0)
            square.start()

        pl.when(step == 3)(lambda: chain.step(1))
        pl.when(step == 3)(square.middle)

        @pl.when(step == 5)
        def _():
            square.finish(parts.at[quarter_at(nt - 2, z, nt)])
            chain.step(2)

    attend_back(step, *refs[:9], *refs[26:28], *refs[36:38])
    if feed:

        @pl.when(step == 0)
        def _():
            dots.wait()
            dot_sum[...] = dots.total()

        at = pl.ds(pl.multiple_of((pl.num_programs(0) - 1 - step) * block_len, block_len), block_len)
        refs = refs[:19] + (dot_sum.at[:, at],) + refs[20:]
    scan_back(heads, channels, step, *refs[9:26], *refs[28:36], *refs[38:43])
    if feed:

        @pl.when(step == pl.num_programs(0) - 1)
        def _():
            chain.finish(feed_o)
            chain.drain()
            square.drain()


def scan_back(
    heads, channels, step, dm, y, zr, xr, xp, br, bp, trow, states, rsum, dots, gain, tapx, tapb, decay,
    bias, skip,
    dz_o, dx_o, db_o, dt_o, gx_o, gb_o, gm_o, gh_o,
    xs, bs, dxs, dbs, dstate,
):
    last_step = pl.num_programs(0) - 1
    first = step == last_step
    rows = block_len
    inner = heads * SSM_DIM
    n_state = br.shape[1] // 2

    @pl.when(step == 0)
    def _():
        dxs[rows : rows + 8, :] = jnp.zeros((8, inner), F32)
        dbs[rows : rows + 8, :] = jnp.zeros((8, 2 * n_state), F32)
        dstate[...] = jnp.zeros(dstate.shape, F32)
        gx_o[...] = jnp.zeros(gx_o.shape, F32)
        gb_o[...] = jnp.zeros(gb_o.shape, F32)
        gm_o[...] = jnp.zeros(gm_o.shape, F32)
        gh_o[...] = jnp.zeros(gh_o.shape, F32)

    xs[0:8, :] = jnp.where(first, 0.0, xp[...])
    bs[0:8, :] = jnp.where(first, 0.0, bp[...])
    xs[8 : 8 + rows, :] = xr[...]
    bs[8 : 8 + rows, :] = br[...]
    ux = conv_rows(xs, tapx, 5, rows)
    sx = sigmoid(ux)
    x = ux * sx
    ub = conv_rows(bs, tapb, 5, rows)
    sb = sigmoid(ub)
    bc = (ub * sb).astype(BF16)
    b_low, c_low = bc[:, :n_state], bc[:, n_state:]

    pre = trow[...] + bias[...]
    dt = softplus(pre)
    cum = running_sum(dt * decay[...])
    end = cum[:, rows - 1 :]
    fade = jnp.exp(end - cum)
    inv = lax.rsqrt(rsum[...] / channels + epsilon)
    cols = stack_columns(
        [cum, jnp.exp(cum), dt * fade, dt, inv, inv * inv * inv * dots[...] / channels]
    )
    r = cols[:, 32:33]
    kk = cols[:, 40:41]
    z = zr[...]
    sz = sigmoid(z)
    silu_z = z * sz
    yv = y[...]
    w = yv * silu_z
    dmv = dm[...]
    dw = r * gain[...] * dmv - w * kk
    gm_o[0:1, :] += jnp.sum(dmv * w * r, axis=0, keepdims=True)
    dy = dw * silu_z
    dz_o[...] = (dw * yv * sz * (1.0 + z * (1.0 - sz))).astype(BF16)
    gm_o[1:2, :] += jnp.sum(dy * x, axis=0, keepdims=True)

    grow = widen(cols, 8, heads)
    tail = widen(cols, 16, heads)
    dt_wide = widen(cols, 24, heads)
    x_low = x.astype(BF16)
    dy_low = dy.astype(BF16)
    state = states[0]
    state_low = state.astype(BF16)
    ds = dstate[...]
    ds_low = ds.astype(BF16)
    cross = dot_nt(b_low, c_low)
    shape = (rows, rows)
    upper = lax.broadcasted_iota(jnp.int32, shape, 0) <= lanes_of(shape)
    half = lanes_of(shape) < SSM_DIM
    lane = lanes_of(shape)
    dcross = jnp.zeros(shape, F32)
    col_sums = jnp.zeros(shape, F32)
    row_sums = []
    mids = []
    for p in range(heads // 2):
        span = slice(128 * p, 128 * p + 128)
        xpair, dypair = x_low[:, span], dy_low[:, span]
        zero = jnp.zeros_like(xpair)
        dys = (jnp.where(half, dypair, zero), jnp.where(half, zero, dypair))
        mats = []
        for k in range(2):
            h = 2 * p + k
            gap = jnp.where(upper, cum[h : h + 1, :] - cols[:, h : h + 1], neg_large)
            faded = jnp.exp(gap)
            mats.append((cross * faded).astype(BF16))
            t = dot_nt(xpair, dys[k]) * faded
            dt_col = cols[:, 24 + h : 25 + h]
            td = t * dt_col
            dcross = dcross + td
            row_sums.append(jnp.sum(td * cross, axis=0, keepdims=True))
            col = jnp.sum(t * cross, axis=1, keepdims=True)
            col_sums = jnp.where(lane == h, col, col_sums)
        mids.append(dot_nn(jnp.concatenate(mats, axis=1), jnp.concatenate(dys, axis=0)))
    mid = jnp.concatenate(mids, axis=1)
    row_sums = jnp.concatenate(row_sums + [jnp.zeros((8 - heads, rows), F32)], axis=0)
    col_sums = col_sums.T[0:8, :]

    dye = dy * grow
    dye_low = dye.astype(BF16)
    xd = x * tail
    xd_low = xd.astype(BF16)
    from_b = dot_nn(b_low, ds_low)
    through = dot_nn(c_low, state_low)
    dcross_low = dcross.astype(BF16)
    db = dot_nn(dcross_low, c_low) + dot_nt(xd_low, ds_low)
    dc = dot_tn(dcross_low, b_low) + dot_nt(dye_low, state_low)

    head_of = lax.broadcasted_iota(jnp.int32, (8, inner), 0)
    chan = lanes_of((8, inner)) // SSM_DIM
    ones = jnp.where(head_of == chan, 1.0, 0.0).astype(BF16)

    def by_head(v):
        high = v.astype(BF16)
        rest = (v - high.astype(F32)).astype(BF16)
        return dot_nt(ones, high) + dot_nt(ones, rest)

    grown = by_head(dye * through)
    ended = by_head(x * from_b)
    kept = jnp.sum(ds * state, axis=0, keepdims=True) * grow[rows - 1 :, :]
    kept = jnp.where(head_of == chan, kept, 0.0).sum(axis=1, keepdims=True)
    pulled = dt * fade * ended
    lane8 = lanes_of((8, rows))
    at_end = kept + jnp.sum(pulled, axis=1, keepdims=True)
    dcum = row_sums - dt * col_sums + grown - pulled + jnp.where(lane8 == rows - 1, at_end, 0.0)
    da = running_sum_back(dcum)
    ddt = col_sums + fade * ended + decay[...] * da
    dpre = ddt * sigmoid(pre)
    dt_o[...] = dpre
    gh_o[0:8, :] += da * dt * decay[...]
    gh_o[8:16, :] += dpre

    dstate[...] = grow[rows - 1 :, :] * ds + dot_tn(c_low, dye_low)
    dx = skip[...] * dy + dt_wide * mid + tail * from_b
    dux = dx * sx * (1.0 + ux * (1.0 - sx))
    dub = jnp.concatenate([db, dc], axis=1) * sb * (1.0 + ub * (1.0 - sb))
    for taps, src, d, buf, acc, out in (
        (tapx, xs, dux, dxs, gx_o, dx_o),
        (tapb, bs, dub, dbs, gb_o, db_o),
    ):
        buf[0:rows, :] = d
        total = taps[CONV - 1 : CONV, :] * d
        for j in range(CONV - 1):
            total = total + taps[j : j + 1, :] * buf[pl.ds(CONV - 1 - j, rows), :]
        out[...] = total.astype(BF16)
        for j in range(CONV):
            acc[j : j + 1, :] += jnp.sum(d * src[pl.ds(5 + j, rows), :], axis=0, keepdims=True)
        acc[CONV : CONV + 1, :] += jnp.sum(d, axis=0, keepdims=True)
        buf[rows : rows + 8, :] = d[0:8, :]


def mixers_back(
    heads, channels, nt, q, k2, v2, lse, do, cosine, sine, dm, y, zr, xr, br, trow, states, rsum, dots,
    gain, tapx, tapb, decay, bias, skip, feed=None,
):
    total, inner = y.shape
    pair = br.shape[1]
    rows = block_len
    steps = total // rows
    per = rows // 8
    q_rows = 2 * rows

    def whole(v):
        return pl.BlockSpec(v.shape, lambda i: (0,) * v.ndim)

    def tall(n):
        return pl.BlockSpec((rows, n), lambda i: (steps - 1 - i, 0))

    def before(n):
        return pl.BlockSpec((8, n), lambda i: (jnp.maximum((steps - 1 - i) * per - 1, 0), 0))

    wide = pl.BlockSpec((8, rows), lambda i: (0, steps - 1 - i))
    ask = pl.BlockSpec((q_rows, 128), lambda i: (steps // 2 - 1 - i // 2, 0))
    sds = jax.ShapeDtypeStruct

    def fixed(*shape):
        return pl.BlockSpec(shape, lambda i: (0,) * len(shape))

    in_specs = [ask, whole(k2), whole(v2),
                pl.BlockSpec((8, q_rows), lambda i: (0, steps // 2 - 1 - i // 2)), ask, ask, ask, whole(cosine), whole(sine),
                tall(inner), tall(inner), tall(inner), tall(inner), before(inner), tall(pair),
                before(pair), wide, pl.BlockSpec((1, pair // 2, inner), lambda i: (steps - 1 - i, 0, 0)),
                wide, wide, whole(gain), whole(tapx), whole(tapb), whole(decay), whole(bias), whole(skip)]
    out_specs = [ask, fixed(total, 256), tall(inner), tall(inner), tall(pair), wide, fixed(8, inner),
                 fixed(8, pair), fixed(8, inner), fixed(16, rows)]
    out_shape = [sds((total, 128), BF16), sds((total, 256), BF16), sds((total, inner), BF16),
                 sds((total, inner), BF16), sds((total, pair), BF16), sds((8, total), F32),
                 sds((8, inner), F32), sds((8, pair), F32), sds((8, inner), F32), sds((16, rows), F32)]
    scratch = [pltpu.VMEM((total, 128), F32), pltpu.VMEM((total, 128), F32),
               pltpu.VMEM((rows + 8, inner), F32), pltpu.VMEM((rows + 8, pair), F32),
               pltpu.VMEM((rows + 8, inner), F32), pltpu.VMEM((rows + 8, pair), F32),
               pltpu.VMEM((pair // 2, inner), F32)]
    args = [q, k2, v2, lse, do, cosine, sine, cosine, sine, dm, y, zr, xr, xr, br, br, trow, states,
            rsum, dots, gain, tapx, tapb, decay, bias, skip]
    extra = {}
    if feed is not None:
        piece = feed[0].shape[1:]
        dma = pltpu.SemaphoreType.DMA
        in_specs[19] = whole(dots)
        args = list(feed) + args
        in_specs = [whole(v) for v in feed] + in_specs
        out_specs = out_specs + [fixed(*piece)]
        out_shape = out_shape + [sds(piece, F32)]
        scratch = scratch + [pltpu.VMEM((nt,) + piece, BF16)] + chain_scratch(nt, *piece)
        scratch = scratch + square_scratch(*piece)
        scratch = scratch + [pltpu.VMEM(dots.shape, F32), pltpu.VMEM((nt - 1,) + dots.shape, F32),
                             dma((nt - 1,)), dma((nt - 1,))]
        extra = dict(collective_id=5, has_side_effects=True)
    return pl.pallas_call(
        partial(back_kernel, heads, channels, nt, feed is not None),
        grid=(steps,),
        in_specs=in_specs,
        out_specs=out_specs,
        out_shape=out_shape,
        scratch_shapes=scratch,
        compiler_params=pltpu.CompilerParams(vmem_limit_bytes=VMEM_LIMIT, **extra),
        cost_estimate=pl.CostEstimate(flops=int(6e9), bytes_accessed=int(18e6), transcendentals=int(7e6)),
        name="mixers_back",
    )(*args)


def whole_spec(v):
    return pl.BlockSpec(v.shape, lambda i: (0,) * v.ndim)


def feed_open(hid, gain, a2, a2t, acc, dacc):
    v = hid[...]
    f = lax.rsqrt(jnp.mean(v * v, axis=1, keepdims=True) + epsilon)
    low = (v * f * gain[...]).astype(BF16)
    a2[...] = low
    a2t[...] = low.T
    acc[...] = jnp.zeros(acc.shape, F32)
    dacc[...] = jnp.zeros(dacc.shape, F32)


def feed_tile(a2, cot, whid, wdown, acc, dacc):
    width = a2.shape[1]
    units = whid.shape[4]
    w_gate = whid[:, 0, 0].reshape(width, units)
    w_up = whid[:, 0, 1].reshape(width, units)
    w_down = jnp.concatenate([wdown[k, 0] for k in range(width // 128)], axis=1)
    g = dot_nn(a2[...], w_gate)
    u = dot_nn(a2[...], w_up)
    s = sigmoid(g)
    f_low = (g * s * u).astype(BF16)
    acc[...] += dot_nn(f_low, w_down)
    df = dot_nt(cot[...], w_down)
    du = (df * g * s).astype(BF16)
    dg = (df * u * s * (1.0 + g * (1.0 - s))).astype(BF16)
    dacc[...] += dot_nt(dg, w_gate) + dot_nt(du, w_up)
    return f_low, dg, du


def feed_close(hid, gain, cot, acc, dacc, out_o, dh_o, gg_o):
    v = hid[...]
    out_o[...] = (v + acc[...]).astype(BF16)
    f = lax.rsqrt(jnp.mean(v * v, axis=1, keepdims=True) + epsilon)
    dy = dacc[...]
    gg_o[...] = jnp.sum(dy * v * f, axis=0, keepdims=True)
    gdy = dy * gain[...]
    lean = jnp.sum(gdy * v, axis=1, keepdims=True) * (f * f * f / v.shape[1])
    dh = cot[...].astype(F32) + (f * gdy - v * lean)
    dh_o[...] = dh
    return dh.astype(BF16)


def feed_grads(a2t, cot, f_low, dg, du):
    blocks = a2t.shape[0] // 128
    values = []
    for grad in (dg, du):
        full = dot_nn(a2t[...], grad).astype(BF16)
        for cb in range(grad.shape[1] // 128):
            values.append(full[:, 128 * cb : 128 * cb + 128].reshape(blocks, 128, 128))
    full = dot_tn(f_low, cot[...]).astype(BF16)
    values.append(jnp.stack([full[:, 128 * k : 128 * k + 128] for k in range(blocks)]))
    return values


def piece_rows(part, units, quarter_units):
    rows = [
        (k * quarter_units + part * units + cb * 128, 128) for k in range(2) for cb in range(units // 128)
    ]
    return rows + [(2 * quarter_units + part * units, units)]


def feed_kernel(hid, gain, cot, whid, wdown, out_o, dh_o, dmix_o, gg_o, piece_o, a2, a2t, acc, dacc):
    step = pl.program_id(0)
    pl.when(step == 0)(lambda: feed_open(hid, gain, a2, a2t, acc, dacc))
    values = feed_grads(a2t, cot, *feed_tile(a2, cot, whid, wdown, acc, dacc))
    units = whid.shape[4]
    quarter_units = piece_o.shape[2] // 3
    tiles_per = quarter_units // units
    rows = piece_rows(lax.rem(step, tiles_per), units, quarter_units)
    for value, (row, n) in zip(values, rows):
        piece_o[:, step // tiles_per, pl.ds(pl.multiple_of(row, 128), n), :] = value

    @pl.when(step == pl.num_programs(0) - 1)
    def _():
        dmix_o[...] = feed_close(hid, gain, cot, acc, dacc, out_o, dh_o, gg_o)


def feed_forward(hid, gain, cot, whid, wdown):
    rows, width = hid.shape
    blocks, nt, _, depth, units = whid.shape
    tile = 256
    per = units // tile
    hid_spec = pl.BlockSpec((blocks, 1, 2, depth, tile), lambda i: (0, i // per, 0, 0, lax.rem(i, per)))
    down_spec = pl.BlockSpec((blocks, 1, tile, 128), lambda i: (0, i // per, lax.rem(i, per), 0))
    sds = jax.ShapeDtypeStruct
    piece = (blocks, nt, 3 * units, 128)

    def fixed(*shape):
        return pl.BlockSpec(shape, lambda i: (0,) * len(shape))

    return pl.pallas_call(
        feed_kernel,
        grid=(nt * per,),
        in_specs=[fixed(rows, width), fixed(1, width), fixed(rows, width), hid_spec, down_spec],
        out_specs=[fixed(rows, width), fixed(rows, width), fixed(rows, width), fixed(1, width),
                   fixed(*piece)],
        out_shape=[sds((rows, width), BF16), sds((rows, width), F32), sds((rows, width), BF16),
                   sds((1, width), F32), sds(piece, BF16)],
        scratch_shapes=[pltpu.VMEM((rows, width), BF16), pltpu.VMEM((width, rows), BF16),
                        pltpu.VMEM((rows, width), F32), pltpu.VMEM((rows, width), F32)],
        compiler_params=pltpu.CompilerParams(vmem_limit_bytes=VMEM_LIMIT),
        name="feed_forward",
    )(hid, gain, cot, whid, wdown)


def row_columns(rows_list, rows):
    return jnp.concatenate(
        [stack_columns([r[:, c : c + 128] for r in rows_list]) for c in range(0, rows, 128)], axis=0
    )


def down_rows(at, dq, dz, dx, dkv, db, drow, wq, win, stp, wsh):
    total = dot_nt(dq[at, :], wq[...]) + dot_nt(dz[at, :], win[0]) + dot_nt(dx[at, :], win[1])
    total = total + dot_nt(dkv[at, :], wsh[:, 0:256]) + dot_nt(db[at, :], wsh[:, 256:])
    return total + dot_tn(drow[:, at].astype(BF16), stp[...])


def down_kernel(dq, dz, dx, dkv, db, drow, wq, win, stp, wsh, part_o):
    every = slice(None)
    part_o[...] = down_rows(every, dq, dz, dx, dkv, db, drow, wq, win, stp, wsh).astype(BF16)


def down_parts(dq, dz, dx, dkv, db, drow, wq, win, stp, wsh):
    total, inner = dz.shape
    width = wq.shape[0]
    rows = 256

    def tall(v):
        return pl.BlockSpec((rows, v.shape[1]), lambda i: (i, 0))

    wide = pl.BlockSpec((8, rows), lambda i: (0, i))
    return pl.pallas_call(
        down_kernel,
        grid=(total // rows,),
        in_specs=[tall(dq), tall(dz), tall(dx), tall(dkv), tall(db), wide, whole_spec(wq), whole_spec(win),
                  whole_spec(stp), whole_spec(wsh)],
        out_specs=pl.BlockSpec((rows, width), lambda i: (i, 0)),
        out_shape=jax.ShapeDtypeStruct((total, width), BF16),
        compiler_params=pltpu.CompilerParams(vmem_limit_bytes=VMEM_LIMIT),
        cost_estimate=pl.CostEstimate(flops=int(3e9), bytes_accessed=int(8e6), transcendentals=0),
        name="down_parts",
    )(dq, dz, dx, dkv, db, drow, wq, win, stp, wsh)


def weight_columns(a, g, dq, dz, dx, dkv, db, ot, mt, put, put_shared):
    at = a.T
    inner = dz.shape[1]

    def by_rows(values, first):
        for j in range(values.shape[1] // 128):
            for k in range(2):
                put(k, first + 128 * j, values[128 * k : 128 * (k + 1), 128 * j : 128 * (j + 1)])

    def by_lanes(values, first):
        for k in range(2):
            put(k, first, values[:, 128 * k : 128 * (k + 1)])

    by_rows(dot_nn(at, dq[...]).astype(BF16), 0)
    by_lanes(dot_nn(ot[...], g).astype(BF16), 128)
    by_rows(dot_nn(at, dz[...]).astype(BF16), 256)
    by_rows(dot_nn(at, dx[...]).astype(BF16), 256 + inner)
    by_lanes(dot_nn(mt[...], g).astype(BF16), 256 + 2 * inner)
    for first, values in ((0, dot_nn(at, dkv[...]).astype(BF16)), (256, dot_nn(at, db[...]).astype(BF16))):
        for k in range(2):
            put_shared(k, first, values[128 * k : 128 * (k + 1)])


def weight_kernel(a1, dq, dz, dx, dkv, db, drow, o, m, dmix, piece_o, shared_o, step_o, ot, mt):
    @pl.when(pl.program_id(0) == 0)
    def _():
        ot[...] = o[...].T
        mt[...] = m[...].T

    step_o[...] = dot_nn(drow[...].astype(BF16), a1[...])

    def put(k, first, values):
        piece_o[k, first : first + values.shape[0], :] = values

    def put_shared(k, first, values):
        shared_o[k, :, first : first + values.shape[1]] = values

    weight_columns(a1[...], dmix[...], dq, dz, dx, dkv, db, ot, mt, put, put_shared)


def weight_pieces(a1, dq, dz, dx, dkv, db, drow, o, m, dmix):
    total, width = a1.shape
    inner = dz.shape[1]
    n = 256 + 3 * inner
    shared = 256 + db.shape[1]
    cols = pl.BlockSpec((total, 256), lambda i: (0, i))
    sds = jax.ShapeDtypeStruct
    args = (dq, dz, dx, dkv, db, drow, o, m)
    return pl.pallas_call(
        weight_kernel,
        grid=(width // 256,),
        in_specs=[cols] + [whole_spec(v) for v in args] + [cols],
        out_specs=[pl.BlockSpec((2, n, 128), lambda i: (i, 0, 0)),
                   pl.BlockSpec((2, 128, shared), lambda i: (i, 0, 0)),
                   pl.BlockSpec((8, 256), lambda i: (0, i))],
        out_shape=[sds((width // 128, n, 128), BF16), sds((width // 128, 128, shared), BF16),
                   sds((8, width), F32)],
        scratch_shapes=[pltpu.VMEM((128, total), BF16), pltpu.VMEM((inner, total), BF16)],
        compiler_params=pltpu.CompilerParams(vmem_limit_bytes=VMEM_LIMIT),
        cost_estimate=pl.CostEstimate(flops=int(4e9), bytes_accessed=int(12e6), transcendentals=0),
        name="weight_pieces",
    )(a1, *args, dmix)


class Exchange:
    def __init__(self, own, landed, send, recv, d, z, nt):
        self.own, self.landed, self.z, self.nt = own, landed, z, nt
        self.copies = [
            remote_copy(own, landed.at[k - 1], send.at[k - 1], recv.at[k - 1], peer)
            for k, peer in enumerate(other_quarters(d, z, nt), 1)
        ]

    def start(self):
        for copy in self.copies:
            copy.start()

    def wait(self):
        for copy in self.copies:
            copy.wait()

    def total(self):
        total = None
        for q in range(self.nt):
            value = jnp.where(self.z == q, self.own[...].astype(F32), 0.0)
            for k in range(1, self.nt):
                value = value + jnp.where(
                    lax.rem(self.z - k + self.nt, self.nt) == q, self.landed[k - 1].astype(F32), 0.0
                )
            total = value if total is None else total + value
        return total


class ChainScatter:
    def __init__(self, parts, bufs, landed, send, recv, d, z, nt):
        self.parts, self.bufs, self.landed = parts, bufs, landed
        self.send, self.recv = send, recv
        self.d, self.z, self.nt = d, z, nt

    def active(self, way, t):
        z, nt = self.z, self.nt
        if way == 0:
            return (z <= t) & (z < nt - 1)
        return (nt - 1 - z <= t) & (z > 0)

    def copy(self, way, t):
        dev = (self.d, self.z + 1 if way == 0 else self.z - 1)
        return remote_copy(
            self.bufs.at[way, t], self.landed.at[way, t], self.send.at[way, t], self.recv.at[way, t], dev
        )

    def arrives(self, way, t):
        z, nt = self.z, self.nt
        if way == 0:
            return (z >= 1) & (z - 1 <= t)
        return (z < nt - 1) & (nt - 2 - z <= t)

    def step(self, t):
        z, nt = self.z, self.nt
        for way in range(2):
            q = nt - 1 - t + z if way == 0 else t - (nt - 1) + z

            def run():
                value = self.parts[q]
                if t > 0:
                    came = self.arrives(way, t - 1)

                    @pl.when(came)
                    def _():
                        self.copy(way, t - 1).wait_recv()
                        total = value.astype(F32) + self.landed[way, t - 1].astype(F32)
                        self.bufs[way, t] = total.astype(BF16)

                    @pl.when(jnp.logical_not(came))
                    def _():
                        self.bufs[way, t] = value
                else:
                    self.bufs[way, t] = value
                self.copy(way, t).start()

            pl.when(self.active(way, t))(run)

    def finish(self, out):
        out[...] = self.parts[self.z].astype(F32)
        t = self.nt - 2
        for way in range(2):

            @pl.when(self.arrives(way, t))
            def _():
                self.copy(way, t).wait_recv()
                out[...] += self.landed[way, t].astype(F32)

    def drain(self):
        for way in range(2):
            for t in range(self.nt - 1):
                pl.when(self.active(way, t))(self.copy(way, t).wait_send)


def chain_scratch(nt, rows, width):
    dma = pltpu.SemaphoreType.DMA
    return [
        pltpu.VMEM((2, nt - 1, rows, width), BF16),
        pltpu.VMEM((2, nt - 1, rows, width), BF16),
        dma((2, nt - 1)),
        dma((2, nt - 1)),
    ]


def mix_scatter_kernel(channels, nt, feed, *refs):
    (o_in, y_in, gate_in, sq, gain, watt_in, wmam_in, tok_in), refs = refs[:8], refs[8:]
    if feed:
        (hid_z, dwn_z), refs = refs[2:4], refs[4:]
        (m_o, sq_o, hid_o, hid_f, dwn_f), refs = refs[:5], refs[5:]
        (lsem, f_send, f_recv), refs = refs[:3], refs[3:]
    else:
        (m_o, sq_o, hid_o), refs = refs[:3], refs[3:]
    (y, z_in, in_sem, o, watt, wmam, tok, late_sem, sq_land, sq_send, sq_recv, parts, bufs, landed, c_send, c_recv) = refs
    d = lax.axis_index("dp")
    z = lax.axis_index("tensor")
    rows = tok.shape[0]
    late = [
        pltpu.make_async_copy(src, dst, late_sem.at[i])
        for i, (src, dst) in enumerate(((o_in, o), (watt_in, watt), (wmam_in, wmam), (tok_in, tok)))
    ]
    for copy in late:
        copy.start()

    def rows_of(q):
        return pl.ds(pl.multiple_of(q * rows, rows), rows)

    def load(q):
        at = rows_of(q)
        return [
            pltpu.make_async_copy(y_in.at[at], y.at[at], in_sem.at[0, q]),
            pltpu.make_async_copy(gate_in.at[at], z_in.at[at], in_sem.at[1, q]),
        ]

    first = jnp.where(z < nt // 2, nt - 1, 0)
    for k in range(nt):
        for copy in load(lax.rem(first + k, nt)):
            copy.start()
    peers = [(p, z) for p in cube_peers(d)] if feed else []
    greet(peers + other_quarters(d, z, nt))
    squares = Exchange(sq, sq_land, sq_send, sq_recv, d, z, nt)
    squares.start()
    n = 2 * nt - 1
    if feed:
        items = []
        for k in range(1, nt):
            q = lax.rem(z - k + nt, nt)
            items.append((hid_z.at[q], lambda s, q=q: hid_f.at[s, q]))
            if k < nt - 1:
                items.append((dwn_z.at[q], lambda s, q=q: dwn_f.at[s, q]))
        half = dwn_z.shape[1] // 2
        for first_row in (0, half):
            at = pl.ds(first_row, half)
            items.append((dwn_z.at[q, at], lambda s, q=q, at=at: dwn_f.at[s, q, at]))
        cube = CubeGather(items, (0, 2, 5), f_send, f_recv, d, z)
        for i in range(n):
            cube.start(i)
        locals_ = []
        for i, (src, dst) in enumerate([(src, at(d)) for src, at in items]):
            locals_.append(pltpu.make_async_copy(src, dst, lsem.at[i]))
            locals_[-1].start()
    chain = ChainScatter(parts, bufs, landed, c_send, c_recv, d, z, nt)
    squares.wait()
    sq_o[...] = squares.total()

    def part(q):
        at = rows_of(q)
        for copy in load(q):
            copy.wait()
        total = sq_o[:, at]
        r = row_columns([lax.rsqrt(total / channels + epsilon)], rows)[:, 0:1]
        zv = z_in[at, :]
        m = (y[at, :] * (zv * sigmoid(zv)) * r * gain[...]).astype(BF16)
        m_o[at, :] = m
        parts[q] = (dot_nn(o[at, :], watt[...]) + dot_nn(m, wmam[...])).astype(BF16)

    for copy in late:
        copy.wait()
    part(first)
    chain.step(0)

    def rest(i, carry):
        part(lax.rem(first + 1 + i, nt))
        return carry

    lax.fori_loop(0, nt - 1, rest, 0)
    for t in range(1, nt - 1):
        chain.step(t)
        if feed and t == 1:
            for i in range(n):
                cube.near(i)
    if feed:
        for i in range(n):
            cube.far(i)
    chain.finish(hid_o)
    hid_o[...] += tok[...].astype(F32)
    chain.drain()
    if feed:
        cube.finish()
        for copy in locals_:
            copy.wait()


def mix_scatter(channels, nt, o, y, zr, sq, gain, watt, wmam, tok, feed=()):
    total, inner = y.shape
    rows, width = tok.shape
    dma = pltpu.SemaphoreType.DMA
    sds = jax.ShapeDtypeStruct
    vmem = pl.BlockSpec(memory_space=pltpu.VMEM)
    anywhere = pl.BlockSpec(memory_space=pl.ANY)
    outs = [sds((total, inner), BF16), sds((8, total), F32), sds((rows, width), F32)]
    scratch = []
    n = 2 * nt - 1
    if feed:
        for v in feed[:2]:
            outs.append(sds(v.shape, BF16))
        scratch = [dma((n,)), dma((n, 7)), dma((n, 7))]
    return pl.pallas_call(
        partial(mix_scatter_kernel, channels, nt, bool(feed)),
        in_specs=[anywhere] * 3 + [vmem] * 2 + [anywhere] * 3 + [anywhere] * len(feed[:2]) + [vmem] * len(feed[2:]),
        out_specs=[vmem] * 3 + [anywhere] * (len(outs) - 3),
        out_shape=outs,
        input_output_aliases={8: 3, 9: 4} if feed else {},
        scratch_shapes=scratch + [pltpu.VMEM((total, inner), F32), pltpu.VMEM((total, inner), F32),
                                  dma((2, nt))]
        + [pltpu.VMEM(v.shape, v.dtype) for v in (o, watt, wmam, tok)]
        + [dma((4,)), pltpu.VMEM((nt - 1, 8, total), F32), dma((nt - 1,)), dma((nt - 1,)),
                        pltpu.VMEM((nt, rows, width), BF16)] + chain_scratch(nt, rows, width),
        compiler_params=pltpu.CompilerParams(
            vmem_limit_bytes=VMEM_LIMIT, collective_id=1, has_side_effects=True
        ),
        cost_estimate=pl.CostEstimate(flops=int(1e9), bytes_accessed=int(130e6), transcendentals=int(4e5)),
        name="mix_scatter",
    )(o, y, zr, sq, gain, watt, wmam, tok, *feed)


class ChainGather:
    def __init__(self, own, slots, send, recv, d, z, nt):
        self.own, self.slots, self.send, self.recv = own, slots, send, recv
        self.d, self.z, self.nt = d, z, nt

    def copy(self, way, dist):
        dev = (self.d, self.z + 1 if way == 0 else self.z - 1)
        slot = self.z - dist if way == 0 else self.z + dist
        src = self.own if dist == 0 else self.slots.at[slot]
        return remote_copy(src, self.slots.at[slot], self.send.at[way, dist], self.recv.at[way, dist], dev)

    def landing(self, way, dist):
        slot = self.z - dist if way == 0 else self.z + dist
        return remote_copy(
            self.slots.at[slot], self.slots.at[slot], self.send.at[way, dist - 1],
            self.recv.at[way, dist - 1], (self.d, self.z),
        )

    def has(self, way, dist):
        return self.z >= dist if way == 0 else self.z + dist < self.nt

    def goes_on(self, way):
        return self.z < self.nt - 1 if way == 0 else self.z > 0

    def start(self):
        for way in range(2):
            pl.when(self.goes_on(way))(self.copy(way, 0).start)

    def hop(self, dist):
        for way in range(2):
            pl.when(self.has(way, dist))(self.landing(way, dist).wait_recv)
            if dist < self.nt - 1:
                pl.when(self.has(way, dist) & self.goes_on(way))(self.copy(way, dist).start)

    def drain(self):
        for way in range(2):
            pl.when(self.goes_on(way))(self.copy(way, 0).wait_send)
            for dist in range(1, self.nt - 1):
                pl.when(self.has(way, dist) & self.goes_on(way))(self.copy(way, dist).wait_send)


class Unmix:
    def __init__(self, y, z_in, gain, watt, wmam, g_o, do_o, dm_o, dots, rows):
        self.ins = (y, z_in, gain, watt, wmam)
        self.outs = (g_o, do_o, dm_o, dots)
        self.rows = rows

    def __call__(self, q, g):
        y, z_in, gain, watt, wmam = self.ins
        g_o, do_o, dm_o, dots_o = self.outs
        rows = self.rows
        at = pl.ds(pl.multiple_of(q * rows, rows), rows)
        if g_o is not None:
            g_o[at, :] = g
        do_o[at, :] = dot_nt(g, watt[...]).astype(BF16)
        dm = dot_nt(g, wmam[...])
        dm_o[at, :] = dm
        zv = z_in[at, :]
        dots = jnp.sum(dm * gain[...] * (y[at, :] * (zv * sigmoid(zv))), axis=1, keepdims=True)
        turned = [jnp.broadcast_to(dots[c : c + 128], (128, 128)).T[0:8, :] for c in range(0, rows, 128)]
        dots_o[:, at] = jnp.concatenate(turned, axis=1)

    def around(self, z, dist, nt, slots, after=lambda q: None):
        def side(way, carry):
            q = jnp.where(way == 0, z - dist, z + dist)

            @pl.when((q >= 0) & (q < nt))
            def _():
                self(q, slots[q])
                after(q)

            return carry

        lax.fori_loop(0, 2, side, 0)


def unmix_gather_kernel(nt, *refs):
    (dmix, y, z_in, gain, watt, wmam), refs = refs[:6], refs[6:]
    (g_o, do_o, dm_o, dot_o), refs = refs[:4], refs[4:]
    (slots, g_send, g_recv, dot_own, dot_land, d_send, d_recv) = refs
    d = lax.axis_index("dp")
    z = lax.axis_index("tensor")
    greet(other_quarters(d, z, nt))
    chain = ChainGather(dmix, slots, g_send, g_recv, d, z, nt)
    chain.start()
    work = Unmix(y, z_in, gain, watt, wmam, g_o, do_o, dm_o, dot_own, dmix.shape[0])
    work(z, dmix[...])
    for dist in range(1, nt):
        chain.hop(dist)
        work.around(z, dist, nt, slots)
    dots = Exchange(dot_own, dot_land, d_send, d_recv, d, z, nt)
    dots.start()
    chain.drain()
    dots.wait()
    dot_o[...] = dots.total()


def unmix_shapes(total, width, inner):
    sds = jax.ShapeDtypeStruct
    return [sds((total, width), BF16), sds((total, 128), BF16), sds((total, inner), F32),
            sds((8, total), F32)]


def unmix_scratch(nt, rows, width, total):
    dma = pltpu.SemaphoreType.DMA
    return [pltpu.VMEM((nt, rows, width), BF16), dma((2, nt - 1)), dma((2, nt - 1)),
            pltpu.VMEM((8, total), F32), pltpu.VMEM((nt - 1, 8, total), F32), dma((nt - 1,)), dma((nt - 1,))]


def unmix_gather(nt, dmix, y, zr, gain, watt, wmam):
    total, inner = y.shape
    rows, width = dmix.shape
    vmem = pl.BlockSpec(memory_space=pltpu.VMEM)
    return pl.pallas_call(
        partial(unmix_gather_kernel, nt),
        in_specs=[vmem] * 6,
        out_specs=[vmem] * 4,
        out_shape=unmix_shapes(total, width, inner),
        scratch_shapes=unmix_scratch(nt, rows, width, total),
        compiler_params=pltpu.CompilerParams(
            vmem_limit_bytes=VMEM_LIMIT, collective_id=2, has_side_effects=True
        ),
        name="unmix_gather",
    )(dmix, y, zr, gain, watt, wmam)


BOXES = 4


def feed_unmix_kernel(nt, *refs):
    (hid, gain, cot, whid, wdown, y_in, gate_in, mgain, watt_in, wmam_in), refs = refs[:10], refs[10:]
    (out_o, dh_o, gg_o, g_o, do_o, dm_o, dot_o, own_o, raw_o, sum_o), refs = refs[:10], refs[10:]
    (y, z_in, watt, wmam, out, dh, dm, in_sem, out_sem, g_sem, dm_sem), refs = refs[:11], refs[11:]
    (a2, a2t, acc, dacc, fs, dgs, dus, dmix, piece, sent, came, b_send, b_recv), refs = refs[:13], refs[13:]
    boxes, refs = refs[: 8 * (nt - 2)], refs[8 * (nt - 2) :]
    (slots, g_send, g_recv) = refs
    step = pl.program_id(0)
    tiles = pl.num_programs(0) // 2
    d = lax.axis_index("dp")
    z = lax.axis_index("tensor")
    core = lax.rem(d, 2)
    bits = dp_bits(d)
    peers = cube_peers(d)
    chain = ChainGather(dmix, slots, g_send, g_recv, d, z, nt)
    cubes = []
    for k in range(1, nt - 1):
        q = quarter_at(k - 1, z, nt)
        box = boxes[8 * k - 8 : 8 * k]
        cubes.append(
            SquareScatter(lambda i, j, q=q: (2 * i + j, q), piece, box[:6], box[6], box[7], peers, bits, z)
        )

    rows = hid.shape[0]
    late = [
        pltpu.make_async_copy(src, dst, in_sem.at[i])
        for i, (src, dst) in enumerate(((y_in, y), (gate_in, z_in), (watt_in, watt), (wmam_in, wmam)))
    ]

    def rows_of(q):
        return pl.ds(pl.multiple_of(q * rows, rows), rows)

    def store_g(q):
        return pltpu.make_async_copy(slots.at[q], g_o.at[rows_of(q)], g_sem.at[q])

    def store_dm(q):
        return pltpu.make_async_copy(dm.at[rows_of(q)], dm_o.at[rows_of(q)], dm_sem.at[q])

    ready = [
        pltpu.make_async_copy(src, dst, out_sem.at[i])
        for i, (src, dst) in enumerate(
            (
                (out, out_o),
                (dh, dh_o),
                (dmix, g_o.at[rows_of(z)]),
                (piece.at[:, z], own_o),
                (piece.at[:, quarter_at(2, z, nt)], raw_o),
            )
        )
    ]

    @pl.when(step == 0)
    def _():
        for copy in late:
            copy.start()
        greet([(p, z) for p in peers] + other_quarters(d, z, nt))
        feed_open(hid, gain, a2, a2t, acc, dacc)

    @pl.when(step < tiles)
    def _():
        fs[step], dgs[step], dus[step] = feed_tile(a2, cot, whid, wdown, acc, dacc)

    @pl.when(step == tiles - 1)
    def _():
        dmix[...] = feed_close(hid, gain, cot, acc, dacc, out, dh, gg_o)
        chain.start()
        for copy in ready[:3]:
            copy.start()

    units = whid.shape[4]
    quarter_units = piece.shape[2] // 3
    tiles_per = quarter_units // units

    def swap(turn_):
        box = lax.rem(turn_, BOXES)
        return remote_copy(
            sent.at[box], came.at[box], b_send.at[box], b_recv.at[box], (peers[0], z)
        )

    def places(turn_):
        quarter = quarter_at(turn_ // tiles_per, z, nt)
        part = lax.rem(turn_, tiles_per)
        return quarter, part, piece_rows(part, units, quarter_units)

    def take(turn_):
        swap(turn_).wait_recv()
        quarter, _, rows = places(turn_)
        box = lax.rem(turn_, BOXES)
        first = 0
        for row, n in rows:
            at = pl.ds(pl.multiple_of(row, 128), n)
            piece[:, quarter, at, :] = add_refs(
                piece[:, quarter, at, :], came[box, :, first : first + n, :]
            ).astype(BF16)
            first += n

    @pl.when(step >= tiles)
    def _():
        turn_ = step - tiles
        quarter, part, rows = places(turn_)
        tile = quarter * tiles_per + part
        box = lax.rem(turn_, BOXES)
        pl.when(turn_ >= BOXES)(lambda: swap(turn_ - BOXES).wait_send())
        first = 0
        for value, (row, n) in zip(feed_grads(a2t, cot, fs[tile], dgs[tile], dus[tile]), rows):
            at = pl.ds(pl.multiple_of(row, 128), n)
            value = value.reshape(value.shape[0] // 2, 2, n, 128)
            even, odd = value[:, 0], value[:, 1]
            piece[:, quarter, at, :] = jnp.where(core == 0, even, odd)
            sent[box, :, first : first + n, :] = jnp.where(core == 0, odd, even)
            first += n
        swap(turn_).start()
        pl.when(turn_ == tiles - 1)(lambda: chain.hop(1))
        pl.when(turn_ >= 1)(lambda: take(turn_ - 1))
        for k in range(1, nt - 1):
            pl.when(turn_ == k * tiles_per)(cubes[k - 1].start)

    @pl.when(step == 2 * tiles - 1)
    def _():
        take(tiles - 1)
        for i in range(BOXES):
            swap(tiles - BOXES + i).wait_send()
        for copy in ready[3:]:
            copy.start()
        for copy in late:
            copy.wait()
        work = Unmix(y, z_in, mgain, watt, wmam, None, do_o, dm, dot_o, rows)
        work(z, dmix[...])
        store_dm(z).start()

        def after(q):
            store_g(q).start()
            store_dm(q).start()

        for dist in range(1, nt):
            if dist > 1:
                chain.hop(dist)
            work.around(z, dist, nt, slots, after)
            if dist == 1:
                cubes[0].middle()
            if dist < nt - 2:
                cubes[dist].middle()
        for k, cube in enumerate(cubes):
            cube.finish(sum_o.at[k])
        chain.drain()
        for cube in cubes:
            cube.drain()
        for copy in ready:
            copy.wait()
        for q in range(nt):
            store_dm(q).wait()
            pl.when(z != q)(store_g(q).wait)


def feed_unmix(nt, hid, gain, cot, whid, wdown, y, zr, mgain, watt, wmam):
    rows, width = hid.shape
    total, inner = y.shape
    blocks, _, _, depth, units = whid.shape
    tile = 256
    per = units // tile
    tiles = nt * per
    kept = blocks // 2
    n = 3 * units
    dma = pltpu.SemaphoreType.DMA
    sds = jax.ShapeDtypeStruct

    def fixed(v):
        return pl.BlockSpec(v.shape, lambda i: (0,) * len(v.shape), pipeline_mode=pl.Buffered(1))

    def at_tile(i):
        return jnp.minimum(i, tiles - 1)

    hid_spec = pl.BlockSpec(
        (blocks, 1, 2, depth, tile), lambda i: (0, at_tile(i) // per, 0, 0, lax.rem(at_tile(i), per))
    )
    down_spec = pl.BlockSpec(
        (blocks, 1, tile, 128), lambda i: (0, at_tile(i) // per, lax.rem(at_tile(i), per), 0)
    )
    out_shape = [sds((rows, width), BF16), sds((rows, width), F32), sds((1, width), F32)]
    out_shape += unmix_shapes(total, width, inner)
    out_shape += [sds((kept, n, 128), BF16), sds((kept, n, 128), BF16), sds((nt - 2, n, 128), BF16)]
    anywhere = pl.BlockSpec(memory_space=pl.ANY)
    late = [pltpu.VMEM(v.shape, v.dtype) for v in (y, zr, watt, wmam) + tuple(out_shape[:2])]
    late += [pltpu.VMEM((total, inner), F32), dma((4,)), dma((5,)), dma((nt,)), dma((nt,))]
    box = pltpu.VMEM((BOXES, kept, 3 * tile, 128), BF16)
    kept_tile = pltpu.VMEM((tiles, rows, tile), BF16)
    scratch = [pltpu.VMEM((rows, width), BF16), pltpu.VMEM((width, rows), BF16),
               pltpu.VMEM((rows, width), F32), pltpu.VMEM((rows, width), F32), kept_tile, kept_tile, kept_tile,
               pltpu.VMEM((rows, width), BF16), pltpu.VMEM((kept, nt, n, 128), BF16), box, box, dma((BOXES,)),
               dma((BOXES,))]
    for _ in range(nt - 2):
        scratch += square_scratch(n, 128)
    return pl.pallas_call(
        partial(feed_unmix_kernel, nt),
        grid=(2 * tiles,),
        in_specs=[fixed(hid), fixed(gain), fixed(cot), hid_spec, down_spec, anywhere, anywhere, fixed(mgain),
                  anywhere, anywhere],
        out_specs=[anywhere if i in (0, 1, 3, 5, 7, 8) else fixed(v) for i, v in enumerate(out_shape)],
        out_shape=out_shape,
        scratch_shapes=late + scratch + unmix_scratch(nt, rows, width, total)[:3],
        compiler_params=pltpu.CompilerParams(
            vmem_limit_bytes=60 * 1024 * 1024, collective_id=4, has_side_effects=True
        ),
        cost_estimate=pl.CostEstimate(flops=int(1e10), bytes_accessed=int(150e6), transcendentals=int(9e5)),
        name="feed_unmix",
    )(hid, gain, cot, whid, wdown, y, zr, mgain, watt, wmam)


def add_refs(left, right):
    return left.astype(F32) + right.astype(F32)


class SquareScatter:
    def __init__(self, place, held, bufs, send, recv, peers, bits, z):
        (self.r1, self.r2, self.ob, self.tb, self.r3, self.r4) = bufs
        self.place, self.held = place, held
        n = held.shape[-2]
        half = n // 2
        self.lo, self.hi = pl.ds(0, half), pl.ds(half, n - half)
        self.half = half
        _, self.x, self.y = bits
        x, y = self.x, self.y
        _, d_x, d_y = peers
        self.copies = []
        for i in range(2):
            self.copies.append(
                remote_copy(held.at[place(i, 1 - x) + (self.lo,)], self.r1.at[i], send.at[i], recv.at[i],
                            (d_x, z))
            )
        for j in range(2):
            self.copies.append(
                remote_copy(held.at[place(1 - y, j) + (self.hi,)], self.r2.at[j], send.at[2 + j],
                            recv.at[2 + j], (d_y, z))
            )
        self.copies.append(remote_copy(self.ob.at[1 - y], self.r3, send.at[4], recv.at[4], (d_y, z)))
        self.copies.append(remote_copy(self.tb.at[1 - x], self.r4, send.at[5], recv.at[5], (d_x, z)))

    def start(self):
        for copy in self.copies[:4]:
            copy.start()

    def middle(self):
        for i in range(2):
            self.copies[i].wait_recv()
            self.ob[i] = add_refs(self.held[self.place(i, self.x) + (self.lo,)], self.r1[i]).astype(BF16)
        self.copies[4].start()
        for j in range(2):
            self.copies[2 + j].wait_recv()
            self.tb[j] = add_refs(self.held[self.place(self.y, j) + (self.hi,)], self.r2[j]).astype(BF16)
        self.copies[5].start()

    def finish(self, out):
        self.copies[4].wait_recv()
        out[0 : self.half] = add_refs(self.ob[self.y], self.r3[...]).astype(out.dtype)
        self.copies[5].wait_recv()
        out[self.half :] = add_refs(self.tb[self.x], self.r4[...]).astype(out.dtype)

    def drain(self):
        for copy in self.copies:
            copy.wait_send()


def square_scratch(n, lanes):
    dma = pltpu.SemaphoreType.DMA
    half = n // 2
    return [
        pltpu.VMEM((2, half, lanes), BF16),
        pltpu.VMEM((2, n - half, lanes), BF16),
        pltpu.VMEM((2, half, lanes), BF16),
        pltpu.VMEM((2, n - half, lanes), BF16),
        pltpu.VMEM((half, lanes), BF16),
        pltpu.VMEM((n - half, lanes), BF16),
        dma((6,)),
        dma((6,)),
    ]


class CubeScatter:
    def __init__(self, pieces, bufs, peers, bits, z):
        (self.rc, self.held, self.send, self.recv) = bufs[:4]
        self.p = pieces
        self.core = bits[0]
        self.peer = (peers[0], z)
        self.square = SquareScatter(
            lambda i, j: (2 * i + j,), self.held, bufs[4:10], bufs[10], bufs[11], peers, bits, z
        )

    def swap(self, i):
        return remote_copy(
            self.p.at[i, 1 - self.core], self.rc.at[i], self.send.at[i], self.recv.at[i], self.peer
        )

    def middle(self):
        for i in range(4):
            self.swap(i).wait_recv()
            self.held[i] = add_refs(self.p[i, self.core], self.rc[i]).astype(BF16)
        self.square.start()

    def last(self):
        self.square.middle()

    def finish(self, out):
        self.square.finish(out)

    def drain(self):
        for i in range(4):
            self.swap(i).wait_send()
        self.square.drain()


def cube_scratch(n, lanes):
    dma = pltpu.SemaphoreType.DMA
    return [
        pltpu.VMEM((4, n, lanes), BF16),
        pltpu.VMEM((4, n, lanes), BF16),
        dma((4,)),
        dma((4,)),
    ] + square_scratch(n, lanes)


class CubeTotal:
    def __init__(self, held, landed, send, recv, peers, z):
        self.held, self.landed = held, landed
        self.copies = [
            remote_copy(held.at[i], landed.at[i], send.at[i], recv.at[i], (peer, z))
            for i, peer in enumerate(peers)
        ]

    def start(self, i):
        self.copies[i].start()

    def take(self, i):
        self.copies[i].wait_recv()
        self.held[i + 1] = self.held[i] + self.landed[i]

    def drain(self):
        for copy in self.copies:
            copy.wait_send()


def norm_back(dy, v, gain, dh):
    f = lax.rsqrt(jnp.mean(v * v, axis=1, keepdims=True) + epsilon)
    gdy = dy * gain
    lean = jnp.sum(gdy * v, axis=1, keepdims=True) * (f * f * f / v.shape[1])
    return dh + (f * gdy - v * lean)


SMALL_ALL = 32
SMALL_ROWS = 160


def tail_kernel(
    nt, tok_in, gain, dh_in, a1_in, dmix_in, o_in, m_in, dq, dz, dx, dkv, db, drow, wq, win, stp, wsh,
    gg, gtb, gtx, grows, gheads, own_in, rest_in,
    gt_o, mixed_o, fed_o, sh_o, small_o,
    feed_own, a1, o, m, dmix, feed_rest, tok, dh, lsem,
    da, gone, parts, pieces, shared, ot, mt, bufs, landed, c_send, c_recv, *rest,
):
    cube_a, rest = rest[:12], rest[12:]
    cube_b, rest = rest[:12], rest[12:]
    square_c, rest = rest[:8], rest[8:]
    (sh_sum, sh_land, sh_send, sh_recv) = rest[:4]
    (sm_held, sm_land, sm_send, sm_recv, all_own, all_land, all_send, all_recv) = rest[4:]
    d = lax.axis_index("dp")
    z = lax.axis_index("tensor")
    bits = dp_bits(d)
    peers = cube_peers(d)
    rows = tok.shape[0]
    late = [
        pltpu.make_async_copy(src, dst, lsem.at[i])
        for i, (src, dst) in enumerate(
            [(own_in, feed_own), (a1_in, a1), (o_in, o), (m_in, m), (dmix_in, dmix), (rest_in, feed_rest),
             (tok_in, tok), (dh_in, dh)]
        )
    ]
    for copy in late:
        copy.start()
    greet([(p, z) for p in peers] + other_quarters(d, z, nt))
    three = SquareScatter(
        lambda i, j: (i, j), feed_own, square_c[:6], square_c[6], square_c[7], peers, bits, z
    )
    chain = ChainScatter(parts, bufs, landed, c_send, c_recv, d, z, nt)

    def part(q):
        at = pl.ds(pl.multiple_of(q * rows, rows), rows)
        parts[q] = down_rows(at, dq, dz, dx, dkv, db, drow, wq, win, stp, wsh).astype(BF16)

    first = jnp.where(z < nt // 2, nt - 1, 0)
    part(first)
    chain.step(0)

    def others(i, carry):
        part(lax.rem(first + 1 + i, nt))
        return carry

    late[0].wait()
    three.start()
    lax.fori_loop(0, nt - 1, others, 0)
    for copy in late[1:5]:
        copy.wait()
    gone[...] = jnp.zeros(gone.shape, F32)

    def gain_sums(q, carry):
        at = pl.ds(pl.multiple_of(q * rows, rows), rows)
        gone[...] += jnp.sum(parts[q].astype(F32) * a1[at, :].astype(F32), axis=0, keepdims=True)
        return carry

    lax.fori_loop(0, nt, gain_sums, 0)
    gone[...] = gone[...] / gain[...]
    sums = CubeTotal(sm_held, sm_land, sm_send, sm_recv, peers, z)
    for k in range(8):
        sm_held[0, k : k + 1, :] = gg[:, 128 * k : 128 * k + 128]
        sm_held[0, 24 + k : 25 + k, :] = gone[:, 128 * k : 128 * k + 128]
    for first_row, ref in ((8, gtb), (SMALL_ALL, gtx), (56, grows)):
        for k in range(ref.shape[1] // 128):
            sm_held[0, first_row + 8 * k : first_row + 8 * k + 8, :] = ref[:, 128 * k : 128 * k + 128]
    sm_held[0, 80:96, :] = gheads[...]
    steps = dot_nn(drow[...].astype(BF16), a1[...])
    for k in range(8):
        sm_held[0, 96 + 8 * k : 104 + 8 * k, :] = steps[:, 128 * k : 128 * k + 128]
    sums.start(0)
    ot[...] = o[...].T
    mt[...] = m[...].T

    def columns(i, carry):
        at = pl.ds(pl.multiple_of(i * 256, 256), 256)

        def put(k, first, values):
            pieces[i, k, first : first + values.shape[0], :] = values

        def put_shared(k, first, values):
            shared[i, k, :, first : first + values.shape[1]] = values

        weight_columns(a1[:, at], dmix[:, at], dq, dz, dx, dkv, db, ot, mt, put, put_shared)
        two.swap(i).start()
        one.swap(i).start()
        return carry

    one = CubeScatter(pieces, cube_a, peers, bits, z)
    two = CubeScatter(shared, cube_b, peers, bits, z)
    lax.fori_loop(0, 1, columns, 0)
    chain.step(1)
    three.middle()
    sums.take(0)
    sums.start(1)
    lax.fori_loop(1, 4, columns, 0)
    sums.take(1)
    sums.start(2)
    two.middle()
    one.middle()
    for t in range(2, nt - 1):
        chain.step(t)
    two.last()
    one.last()
    sums.take(2)
    all_own[...] = sm_held[3, 0:SMALL_ALL, :]
    over_all = Exchange(all_own, all_land, all_send, all_recv, d, z, nt)
    over_all.start()
    three.finish(fed_o)
    for copy in late[5:]:
        copy.wait()
    fed_o[...] += feed_rest[...]
    two.finish(sh_sum)
    per = sh_sum.shape[0] // nt
    copies = []
    for k in range(1, nt):
        q = lax.rem(z + k, nt)
        at = pl.ds(pl.multiple_of(q * per, per), per)
        copies.append(
            remote_copy(sh_sum.at[at], sh_land.at[k - 1], sh_send.at[k - 1], sh_recv.at[k - 1], (d, q))
        )
        copies[-1].start()
    one.finish(mixed_o)
    small_o[...] = sm_held[3]
    over_all.wait()
    small_o[0:SMALL_ALL, :] = over_all.total()
    for copy in copies:
        copy.wait()
    total = sh_sum[pl.ds(pl.multiple_of(z * per, per), per), :].astype(F32)
    for k in range(nt - 1):
        total = total + sh_land[k].astype(F32)
    sh_o[...] = total
    chain.finish(da)
    gt_o[...] = norm_back(da[...], tok[...].astype(F32), gain[...], dh[...]).astype(BF16)
    for thing in (chain, one, two, three, sums):
        thing.drain()


def tail(nt, *args):
    tok, a1, dz = args[0], args[3], args[8]
    feed_own = args[-2]
    rows, width = tok.shape
    total = a1.shape[0]
    inner = dz.shape[1]
    n, lanes = 256 + 3 * inner, 128
    s_rows, s_lanes = 128, args[16].shape[1]
    f_rows = feed_own.shape[2]
    late = (len(args) - 2, 3, 5, 6, 4, len(args) - 1, 0, 2)
    dma = pltpu.SemaphoreType.DMA
    sds = jax.ShapeDtypeStruct
    vmem = pl.BlockSpec(memory_space=pltpu.VMEM)
    return pl.pallas_call(
        partial(tail_kernel, nt),
        in_specs=[pl.BlockSpec(memory_space=pl.ANY) if i in late else vmem for i in range(len(args))],
        out_specs=[vmem] * 5,
        out_shape=[sds((rows, width), BF16), sds((n, lanes), F32), sds((f_rows, 128), F32),
                   sds((s_rows // nt, s_lanes), F32), sds((SMALL_ROWS, 128), F32)],
        scratch_shapes=[pltpu.VMEM(args[i].shape, args[i].dtype) for i in late] + [dma((len(late),))]
        + [pltpu.VMEM((rows, width), F32), pltpu.VMEM((1, width), F32), pltpu.VMEM((nt, rows, width), BF16),
                        pltpu.VMEM((4, 2, n, lanes), BF16), pltpu.VMEM((4, 2, s_rows, s_lanes), BF16),
                        pltpu.VMEM((128, total), BF16), pltpu.VMEM((inner, total), BF16)]
        + chain_scratch(nt, rows, width)
        + cube_scratch(n, lanes) + cube_scratch(s_rows, s_lanes) + square_scratch(f_rows, 128)
        + [pltpu.VMEM((s_rows, s_lanes), BF16), pltpu.VMEM((nt - 1, s_rows // nt, s_lanes), BF16),
           dma((nt - 1,)), dma((nt - 1,)),
           pltpu.VMEM((4, SMALL_ROWS, 128), F32), pltpu.VMEM((3, SMALL_ROWS, 128), F32), dma((3,)), dma((3,)),
           pltpu.VMEM((SMALL_ALL, 128), F32), pltpu.VMEM((nt - 1, SMALL_ALL, 128), F32), dma((nt - 1,)),
           dma((nt - 1,))],
        compiler_params=pltpu.CompilerParams(
            vmem_limit_bytes=VMEM_LIMIT, collective_id=3, has_side_effects=True
        ),
        cost_estimate=pl.CostEstimate(flops=int(7e9), bytes_accessed=int(150e6), transcendentals=0),
        name="tail",
    )(*args)


def finish_kernel(
    heads, nt, mixed, fed, small, *refs
):
    (que_o, att_o, inn_o, mam_o, hid_o, dwn_o, norms_o, taps_o, chan_o, gain_o, step_o) = refs[-17:-6]
    heads_o = refs[-6:-3]
    for src, dst in zip(refs[:3], refs[-3:]):
        dst[...] = src[...]
    d = lax.axis_index("dp")
    p = d * nt + lax.axis_index("tensor")
    block = que_o.shape[0]
    inner = mam_o.shape[0]
    first = 0
    for j in range(que_o.shape[1] // 128):
        que_o[:, 128 * j : 128 * j + 128] = mixed[first : first + block]
        first += block
    att_o[...] = mixed[first : first + att_o.shape[0]]
    first += att_o.shape[0]
    for i in range(2):
        for j in range(inner // 128):
            inn_o[i, :, 128 * j : 128 * j + 128] = mixed[first : first + block]
            first += block
    mam_o[...] = mixed[first : first + inner]
    first = 0
    for i in range(2):
        for j in range(hid_o.shape[2] // 128):
            hid_o[i, :, 128 * j : 128 * j + 128] = fed[first : first + block]
            first += block
    dwn_o[...] = fed[first:]

    def lanes_from(values, lane):
        return pltpu.roll(values, lax.rem(128 - lane, 128), 1)

    width = norms_o.shape[1]
    per = 128 // width
    for i, base in enumerate((24, 0)):
        row = jnp.broadcast_to(small[pl.ds(base + p // per, 1), :], (8, 128))
        row = lanes_from(row, lax.rem(p, per) * width)
        norms_o[i : i + 1, :] = row[0:1, 0:width]
    width = taps_o.shape[1]
    per = 128 // width
    row = small[pl.ds(pl.multiple_of(8 + 8 * (p // per), 8), 8), :]
    taps_o[...] = lanes_from(row, lax.rem(p, per) * width)[0 : CONV + 1, 0:width]
    width = gain_o.shape[1]
    sums = jnp.zeros((8, 128), F32)
    lane = lanes_of(sums.shape)
    sub = lax.broadcasted_iota(jnp.int32, sums.shape, 0)
    for b in range(heads // 2):
        rows = lanes_from(small[SMALL_ALL + 8 * b : SMALL_ALL + 8 * b + 8, :], d * width)
        raw = small[56 + 8 * b : 64 + 8 * b, :]
        gains = lanes_from(raw, d * width)
        for k in range(2):
            h = 2 * b + k
            at = slice(64 * k, 64 * k + width)
            chan_o[:, h, :] = rows[0 : CONV + 1, at]
            gain_o[h : h + 1, :] = gains[0:1, at]
            skip = jnp.sum(jnp.where(lane // SSM_DIM == k, raw[1:2, :], 0.0), axis=1, keepdims=True)
            sums = jnp.where((sub == h) & (lane == 2), skip, sums)
    for k in range(2):
        total = jnp.sum(small[80 + 8 * k : 88 + 8 * k, :], axis=1, keepdims=True)
        sums = jnp.where(lane == k, total, sums)
    sums = jnp.concatenate([sums, jnp.zeros((120, 128), F32)], axis=0).T
    for k in range(3):
        heads_o[k][...] = sums[k : k + 1, 0:heads]
    steps = small[pl.ds(pl.multiple_of(96 + 8 * d, 8), 8), :]
    step_o[...] = steps[0:heads, :]


def finish(heads, nt, mixed, fed, small, shapes, passed):
    vmem = pl.BlockSpec(memory_space=pltpu.VMEM)
    sds = jax.ShapeDtypeStruct
    return pl.pallas_call(
        partial(finish_kernel, heads, nt),
        in_specs=[vmem] * 6,
        out_specs=[vmem] * (len(shapes) + 6),
        out_shape=[sds(s, F32) for s in shapes] + [sds((1, heads), F32)] * 3
        + [sds(v.shape, v.dtype) for v in passed],
        compiler_params=pltpu.CompilerParams(vmem_limit_bytes=VMEM_LIMIT),
        name="finish",
    )(mixed, fed, small, *passed)


def rope_wide(length):
    half = HEAD_SIZE // 2
    inverse = rope_base ** (-np.arange(half) * (2.0 / HEAD_SIZE))
    angles = np.arange(length)[:, None] * inverse[None, :]
    c, s = np.cos(angles), np.sin(angles)
    return (
        jnp.asarray(np.concatenate([c, c, c, c], axis=1), F32),
        jnp.asarray(np.concatenate([-s, s, -s, s], axis=1), F32),
    )


def to_blocks(full, axis, nt):
    if axis == 1:
        two, width, cols = full.shape
        return full.reshape(2, 8, width // 8, nt, cols // nt).transpose(1, 3, 0, 2, 4)
    rows, width = full.shape
    return full.reshape(nt, rows // nt, 8, width // 8).transpose(2, 0, 1, 3)


def per_device(
    nd,
    nt,
    tokens,
    query_proj,
    attend_out,
    inner_proj,
    step_proj,
    mamba_out,
    hidden_proj,
    down_proj,
    channel_taps,
    mixer_gain,
    decay_log,
    step_bias,
    skip_weight,
    shared_proj,
    norm_gains,
    shared_taps,
    cotangent,
):
    tensor_index = lax.axis_index("tensor")
    d = lax.axis_index("dp")
    local_rows, width = tokens.shape
    group_rows = local_rows * nt
    heads = step_proj.shape[1]
    inner = heads * SSM_DIM
    channels = inner * nt
    units = down_proj.shape[0]
    feed = ()
    if nd == 8:
        small = pack_small(channel_taps, mixer_gain, norm_gains, shared_taps, step_proj.T)
        (tok_full, full_query, full_attend, full_inner, full_mamba, sha, sma) = gather_start(
            tokens, query_proj, attend_out, inner_proj, mamba_out, shared_proj, small, nd, nt
        )
        scal = jnp.stack([decay_log, step_bias, skip_weight]).astype(F32)
        (
            gain_first, gain_second, gain_mix, taps_x, taps_b, step_rows, decay, bias, skip,
        ) = unpack_small(heads, scal, sma, width)
        full_shared = sha.reshape(width, -1)
        feed = (hidden_proj, down_proj)
    else:
        small_parts = [channel_taps, mixer_gain, norm_gains, shared_taps, step_proj.T]
        flat = jnp.concatenate([p.reshape(-1) for p in small_parts])
        small_len = -(-flat.shape[0] // 2048) * 2048
        small = jnp.pad(flat, (0, small_len - flat.shape[0])).reshape(-1, 128)
        (tok_full, full_query, full_attend, full_inner, full_mamba, sha, sma) = gather_start(
            tokens, query_proj, attend_out, inner_proj, mamba_out, shared_proj, small, nd, nt
        )
        full_hidden = lax.all_gather(hidden_proj, "tensor", axis=2, tiled=True)
        full_hidden = to_blocks(lax.all_gather(full_hidden, "dp", axis=1, tiled=True), 1, nt)
        full_down = lax.all_gather(down_proj, "tensor", axis=0, tiled=True)
        full_down = to_blocks(lax.all_gather(full_down, "dp", axis=1, tiled=True), 0, nt)

        full_shared = sha.reshape(width, -1)
        sma = sma.reshape(nd, nt, small_len)

        def small_piece(index):
            start = sum(p.size for p in small_parts[:index])
            part = small_parts[index]
            return sma[:, :, start : start + part.size].reshape((nd, nt) + part.shape)

        taps_x = pick(small_piece(0), tensor_index, 1).transpose(1, 2, 0, 3).reshape(CONV + 1, inner)
        gain_mix = pick(small_piece(1), tensor_index, 1).transpose(1, 0, 2).reshape(1, inner)
        full_norms = small_piece(2).transpose(2, 0, 1, 3).reshape(2, width).astype(F32)
        taps_b = small_piece(3).transpose(2, 0, 1, 3).reshape(CONV + 1, -1)
        step_rows = pick(small_piece(4), tensor_index, 1).transpose(1, 0, 2).reshape(heads, width)
        step_rows = jnp.pad(step_rows, ((0, 8 - heads), (0, 0)))
        taps_x = jnp.pad(taps_x.astype(F32), ((0, 7 - CONV), (0, 0)))
        taps_b = jnp.pad(taps_b.astype(F32), ((0, 7 - CONV), (0, 0)))
        gain_mix = gain_mix.astype(F32)
        gain_first = full_norms[0:1]
        gain_second = full_norms[1:2]

        def head_rows(values):
            return jnp.pad(jnp.broadcast_to(values[:, None], (heads, 128)), ((0, 8 - heads), (0, 0)))

        decay = head_rows(-jnp.exp(decay_log.astype(F32)))
        bias = head_rows(step_bias.astype(F32))
        skip = jnp.repeat(skip_weight.astype(F32), SSM_DIM)[None, :]
    cosine, sine = rope_wide(group_rows)

    (a1, q, k2, v2, lse, o, xr, zr, br, y, trow, states, squares, *feed) = mixers_forward(
        heads, nt, tok_full.reshape(group_rows, width), gain_first, full_query, full_inner, step_rows,
        full_shared, cosine, sine, taps_x, taps_b, decay, bias, skip, feed,
    )
    mixed = mix_scatter(
        channels, nt, o, y, zr, squares, gain_mix, full_attend, full_mamba, tokens, tuple(feed)
    )
    m, squares, hidden = mixed[:3]
    if nd == 8:
        full_hidden, full_down = mixed[3:]
    if nd == 8:
        layer_out, dh, grad_gain_two, grad_mix, do, dm, dots, feed_own, feed_raw, feed_sums = feed_unmix(
            nt, hidden, gain_second, cotangent, full_hidden, full_down, y, zr, gain_mix, full_attend, full_mamba
        )
        feed_own = feed_own.reshape((2, 2) + feed_own.shape[1:])
    else:
        layer_out, dh, dmix, grad_gain_two, feed_pieces = feed_forward(
            hidden, gain_second, cotangent, full_hidden, full_down
        )
        grad_mix, do, dm, dots = unmix_gather(nt, dmix, y, zr, gain_mix, full_attend, full_mamba)
        hid_full = feed_pieces[:, :, : 2 * units].reshape(8, nt, 2, units // 128, width // 8, 128)
        hid_full = hid_full.transpose(2, 0, 4, 1, 3, 5).reshape(2, nd, width // nd, nt, units)
        hid_sum = cube_scatter(hid_full.transpose(1, 3, 0, 2, 4), nd, BF16)
        down_full = feed_pieces[:, :, 2 * units :].transpose(1, 2, 0, 3)
        down_full = down_full.reshape(nt, units, nd, width // nd)
        down_sum = cube_scatter(down_full.transpose(2, 0, 1, 3), nd, BF16)
        gradient_hidden = chain_scatter(hid_sum, nt)
        gradient_down = chain_scatter(down_sum, nt)

    back = mixers_back(
        heads, channels, nt, q, k2, v2, lse, do, cosine, sine, dm, y, zr, xr, br, trow, states,
        squares, dots, gain_mix, taps_x, taps_b, decay, bias, skip,
        (feed_sums, feed_raw) if nd == 8 else None,
    )
    dq, dkv, dz, dx, db, drow, grad_tx, grad_tb, grad_rows, grad_heads = back[:10]
    if nd == 8:
        sums = tail(
            nt, tokens, gain_first, dh, a1, grad_mix, o, m, dq, dz, dx, dkv, db, drow, full_query, full_inner,
            step_rows, full_shared, grad_gain_two, grad_tb, grad_tx, grad_rows, grad_heads, feed_own, back[10],
        )
        gradient_tokens, mixed, fed, gradient_shared, small_sums = sums
        shapes = [
            query_proj.shape, attend_out.shape, inner_proj.shape, mamba_out.shape, hidden_proj.shape,
            down_proj.shape, norm_gains.shape, shared_taps.shape, channel_taps.shape, mixer_gain.shape,
            step_proj.T.shape,
        ]
        (
            gradient_query,
            gradient_attend,
            gradient_inner,
            gradient_mamba,
            gradient_hidden,
            gradient_down,
            gradient_norms,
            gradient_taps,
            gradient_channel,
            gradient_mixer,
            gradient_step,
            gradient_decay,
            gradient_bias,
            gradient_skip,
            layer_out,
            gradient_tokens,
            gradient_shared,
        ) = finish(
            heads, nt, mixed, fed, small_sums, shapes, (layer_out, gradient_tokens, gradient_shared)
        )
        return (
            layer_out,
            gradient_tokens,
            gradient_query,
            gradient_attend,
            gradient_inner,
            gradient_step.T,
            gradient_mamba,
            gradient_hidden,
            gradient_down,
            gradient_channel,
            gradient_mixer,
            gradient_decay.reshape(heads),
            gradient_bias.reshape(heads),
            gradient_skip.reshape(heads),
            gradient_shared,
            gradient_norms,
            gradient_taps,
        )

    part_one = down_parts(dq, dz, dx, dkv, db, drow, full_query, full_inner, step_rows, full_shared)
    pieces, shared_pieces, grad_step = weight_pieces(a1, dq, dz, dx, dkv, db, drow, o, m, grad_mix)
    block = width // nd
    q_cols = query_proj.shape[1]
    cuts = [0, q_cols, q_cols + attend_out.shape[0]]
    cuts += [cuts[2] + inner, cuts[2] + 2 * inner, cuts[2] + 3 * inner]

    def from_rows(values):
        return values.reshape(8, -1, 128, 128).transpose(0, 2, 1, 3).reshape(width, -1)

    def from_lanes(values):
        return values.transpose(1, 0, 2).reshape(-1, width)

    n_tap = CONV + 1
    over_all = jnp.concatenate([grad_gain_two.reshape(-1), grad_tb[:n_tap].reshape(-1)])
    over_dp = jnp.concatenate(
        [
            grad_tx[:n_tap].reshape(-1),
            grad_rows[0],
            grad_rows[1].reshape(heads, SSM_DIM).sum(axis=1),
            grad_heads[:heads].sum(axis=1),
            grad_heads[8 : 8 + heads].sum(axis=1),
            grad_step[:heads].reshape(-1),
        ]
    )

    def in_rows(values):
        return jnp.pad(values, (0, -values.shape[0] % 1024)).reshape(-1, 128)

    rows_all = in_rows(over_all)
    n_all = rows_all.shape[0]
    small_sums = jnp.concatenate([rows_all, in_rows(over_dp)], axis=0)
    parts = part_one.reshape(nt, local_rows, width)
    token_f32 = tokens.astype(F32)
    _, norm_one_back = jax.vjp(norm_apply, token_f32, gain_first[0])
    grad_from_one, grad_gain_one = norm_one_back(chain_scatter(parts, nt))
    gradient_tokens = (dh + grad_from_one).astype(BF16)
    got = [pieces[:, cuts[i] : cuts[i + 1]] for i in range(5)]

    def over_rows(values):
        return cube_scatter(from_rows(values).reshape(nd, block, -1), nd)

    def over_lanes(values):
        return cube_scatter(from_lanes(values).reshape(-1, nd, block).transpose(1, 0, 2), nd)

    gradient_query = over_rows(got[0])
    gradient_attend = over_lanes(got[1])
    gradient_inner = jnp.stack([over_rows(got[2]), over_rows(got[3])])
    gradient_mamba = over_lanes(got[4])
    shared_cut = shared_pieces.reshape(nd, nt, width // (nd * nt), -1)
    gradient_shared = chain_scatter(cube_scatter(shared_cut, nd, BF16), nt)
    small_sums = lax.psum(small_sums, "dp")
    small_sums = jnp.concatenate(
        [lax.psum(small_sums[:n_all], "tensor"), small_sums[n_all:]], axis=0
    )
    grad_gain_one = lax.psum(grad_gain_one, ("dp", "tensor")).reshape(1, width)
    over_all = small_sums[:n_all].reshape(-1)
    over_dp = small_sums[n_all:].reshape(-1)
    place = d * nt + tensor_index
    norm_w = width // (nd * nt)
    both_norms = jnp.concatenate([grad_gain_one, over_all[:width].reshape(1, width)], axis=0)
    gradient_norms = lax.dynamic_slice_in_dim(both_norms, place * norm_w, norm_w, 1)
    tap_w = shared_taps.shape[1]
    tap_all = over_all[width : width + n_tap * taps_b.shape[1]].reshape(n_tap, -1)
    gradient_taps = lax.dynamic_slice_in_dim(tap_all, place * tap_w, tap_w, 1)
    part = mixer_gain.shape[1]
    n_taps = n_tap * inner
    chan = over_dp[:n_taps].reshape(n_tap, heads, SSM_DIM)
    gain = over_dp[n_taps : n_taps + inner].reshape(heads, SSM_DIM)
    gradient_channel = lax.dynamic_slice_in_dim(chan, d * part, part, 2)
    gradient_mixer = lax.dynamic_slice_in_dim(gain, d * part, part, 1)
    rest = over_dp[n_taps + inner :]
    gradient_skip = rest[:heads]
    gradient_decay = rest[heads : 2 * heads]
    gradient_bias = rest[2 * heads : 3 * heads]
    step_all = rest[3 * heads : 3 * heads + heads * width].reshape(heads, width)
    gradient_step = lax.dynamic_slice_in_dim(step_all, d * block, block, 1).T
    return (
        layer_out,
        gradient_tokens,
        gradient_query,
        gradient_attend,
        gradient_inner,
        gradient_step,
        gradient_mamba,
        gradient_hidden,
        gradient_down,
        gradient_channel,
        gradient_mixer,
        gradient_decay,
        gradient_bias,
        gradient_skip,
        gradient_shared,
        gradient_norms,
        gradient_taps,
    )


def solution(mesh):
    placed = (
        P(("dp", "tensor"), None),
        P("dp", "tensor"),
        P("tensor", "dp"),
        P(None, "dp", "tensor"),
        P("dp", "tensor"),
        P("tensor", "dp"),
        P(None, "dp", "tensor"),
        P("tensor", "dp"),
        P(None, "tensor", "dp"),
        P("tensor", "dp"),
        P("tensor"),
        P("tensor"),
        P("tensor"),
        P(("dp", "tensor"), None),
        P(None, ("dp", "tensor")),
        P(None, ("dp", "tensor")),
        P(("dp", "tensor"), None),
    )
    return jax.shard_map(
        partial(per_device, mesh.shape["dp"], mesh.shape["tensor"]),
        mesh=mesh,
        in_specs=placed,
        out_specs=(
            P(("dp", "tensor"), None),
            P(("dp", "tensor"), None),
            P("dp", "tensor"),
            P("tensor", "dp"),
            P(None, "dp", "tensor"),
            P("dp", "tensor"),
            P("tensor", "dp"),
            P(None, "dp", "tensor"),
            P("tensor", "dp"),
            P(None, "tensor", "dp"),
            P("tensor", "dp"),
            P("tensor"),
            P("tensor"),
            P("tensor"),
            P(("dp", "tensor"), None),
            P(None, ("dp", "tensor")),
            P(None, ("dp", "tensor")),
        ),
        check_vma=False,
    )
```
